32 devices in a mesh: dp: 4 (over y, x), row: 2 (over core), col: 4 (over z).
Axes of the slice: x: 2, y: 2, z: 4, core: 2. Of those that a mesh axis runs over, the one named last changes fastest.
Arguments:
- tokens: bfloat16 [6144, 1536], P(('dp', 'row', 'col')), may hold values from -6 to 6
- cotangent: bfloat16 [6144, 1536], P(('dp', 'row', 'col')), may hold values from -6 to 6
- routes: int32 [6144, 8], P(('dp', 'row', 'col')), may hold values from 0 to 39, all different within a row; in each aligned block of 192 rows (0 to 191, 192 to 383, ...) at most 64 rows name the same one
- lengths: int32 [4, 4], P('dp'), may hold values from 1 to 1376, 1536 in all within a row
- gain_attn: bfloat16 [1536], replicated, may hold values from 0.5 to 1.5
- w_query: bfloat16 [1536, 1536], P(None, ('row', 'col')), may hold values from -0.21875 to 0.21875
- w_key: bfloat16 [1536, 512], P(None, ('row', 'col')), may hold values from -0.21875 to 0.21875
- w_value: bfloat16 [1536, 512], P(None, ('row', 'col')), may hold values from -0.15625 to 0.15625
- w_out: bfloat16 [1536, 1536], P(None, ('row', 'col')), may hold values from -0.875 to 0.875
- gain_moe: bfloat16 [1536], replicated, may hold values from 0.5 to 1.5
- w_router: bfloat16 [1536, 40], replicated, may hold values from -0.078125 to 0.078125
- w_gate: bfloat16 [40, 1536, 512], P(('row', 'col')), may hold values from -0.15625 to 0.15625
- w_up: bfloat16 [40, 1536, 512], P(('row', 'col')), may hold values from -0.15625 to 0.15625
- w_down: bfloat16 [40, 1536, 512], P(('row', 'col')), may hold values from -1 to 1
Outputs:
- mixed: bfloat16 [6144, 1536], P(('dp', 'row', 'col'))
- tokens_grad: float32 [6144, 1536], P(('dp', 'row', 'col'))
- gain_attn_grad: float32 [1536], replicated
- w_query_grad: float32 [1536, 1536], P('dp', ('row', 'col'))
- w_key_grad: float32 [1536, 512], P('dp', ('row', 'col'))
- w_value_grad: float32 [1536, 512], P('dp', ('row', 'col'))
- w_out_grad: float32 [1536, 1536], P('dp', ('row', 'col'))
- gain_moe_grad: float32 [1536], replicated
- w_router_grad: float32 [1536, 40], replicated
- w_gate_grad: float32 [40, 1536, 512], P(('row', 'col'), 'dp')
- w_up_grad: float32 [40, 1536, 512], P(('row', 'col'), 'dp')
- w_down_grad: float32 [40, 1536, 512], P(('row', 'col'), 'dp')
The draws below stay inside these ranges and needn't reach their ends.
Inputs may be any that keep to these rules, and one draw needn't show every extreme that they name: `lengths`: each row sums to 1536 and holds one document of exactly 1376 tokens. `routes`: each token names 8 different experts; among the 192 rows of one device no expert is named by more than 64 rows, and in some device's rows one expert is named by exactly 64.
All inputs are finite; a program needn't handle non-finite values.
Results may differ from the reference program's by a relative error of at most 0.02.
The reference program's roundings to bfloat16 on the way count: a program that leaves them out, or rounds other values in their place, can miss the bound.
Values may be sent and summed in bfloat16 or wider, within the bound.
No kernel may reach another device: no remote copies, remote signals or barrier semaphores. Data moves between devices by JAX's collectives and lax.ppermute only.
A program may use at most 256 MiB of HBM per device.

```python
import math
from functools import partial
import jax
import jax.numpy as jnp
import numpy as np
from jax import lax

D = 1536
HEADS = 24
KEY_HEADS = 8
HEAD_DIM = 64
EXPERTS = 40
HIDDEN_SIZE = 512
TOP = 8
TOK_DEV = 192
DOCUMENTS = 4
QUERY_BLOCK = 768
GROUP = 1536
TOKENS = 6144
LONGEST = 1376
CAPACITY = 64
N_DP = 4


def raised(values, rng, source, target, shards_of, factor):
    def block_of(dim):
        return (jnp.arange(values.shape[dim]) // (values.shape[dim] // shards_of)).reshape((-1,) + (1,) * (values.ndim - 1 - dim))

    one_side = jax.random.permutation(rng, shards_of)[block_of(target)]
    other_side = (block_of(target) + shards_of // 2) % shards_of
    return jnp.where((block_of(source) == one_side) | (block_of(source) == other_side), factor * values, values)


def levels(rng, dims, pieces, least, high):
    loudness = 1.0
    for dim, parts in pieces:
        steps = jax.random.uniform(jax.random.fold_in(jax.random.fold_in(rng, 6), dim), (parts,), jnp.float32, least / len(pieces), high / len(pieces))
        loudness = loudness * jnp.repeat(jnp.exp(steps), dims[dim] // parts).reshape((-1,) + (1,) * (len(dims) - 1 - dim))
    return loudness


def split_up(number_of, total, limit, lean):
    portions = [(1 << 20) // math.isqrt(standing ** lean) + 1 for standing in range(2, number_of + 1)]
    rest, holding = total - limit - (number_of - 1), [1] * (number_of - 1)
    while rest > 0:
        candidates = [i for i in range(number_of - 1) if holding[i] < limit]
        whole, budget = sum([portions[i] for i in candidates]), rest
        for i in candidates:
            addition = min(limit - holding[i], max(1, budget * portions[i] // whole), rest)
            holding[i] = holding[i] + addition
            rest = rest - addition
    return np.array([limit] + holding)


def ragged_sizes(stream_key, amount, total, limit, skew):
    if amount == 2:
        one = jax.random.randint(stream_key, (), max(1, total - limit), min(limit, total - 1) + 1)
        return jnp.stack([one, total - one])
    tallies = jnp.asarray(split_up(amount, total, limit, skew), jnp.int32)
    couples = (amount - 1) // 2
    source_of, sink = tallies[1:1 + 2 * couples:2], tallies[2:2 + 2 * couples:2]
    margin = jnp.minimum(source_of - 1, limit - sink)
    shifted = jax.random.randint(jax.random.fold_in(stream_key, 1), (couples,), 0, 1 << 20) % (margin + 1)
    tallies = tallies.at[1:1 + 2 * couples:2].set(source_of - shifted).at[2:2 + 2 * couples:2].set(sink + shifted)
    return tallies[jax.random.permutation(jax.random.fold_in(stream_key, 2), amount)]


def shared_out(rng, own, number, rows, amount, top, most, skew):
    ranking = jax.random.permutation(rng, amount)
    crowded, common = load_shares(amount, rows * top, most, skew, True), load_shares(amount, rows * top, most, skew, False)
    places = jnp.arange(amount)

    def named(sizes, offset_by):
        used = int((sizes > 0).sum())
        fixed = max(1, used // 4)
        passed = fixed + (places - fixed + offset_by * (used - fixed)) % max(1, amount - fixed)
        return jnp.zeros((amount,), jnp.int32).at[ranking[jnp.where(places < fixed, places, passed)]].set(jnp.asarray(sizes, jnp.int32))

    sizes = jnp.where(number % 4 == 0, named(crowded, number // 4), named(common, number - number // 4 - 1))
    mixed = jax.random.permutation(jax.random.fold_in(own, 3), amount)
    donor, sink = mixed[0:amount // 2 * 2:2], mixed[1:amount // 2 * 2:2]
    slack = jnp.minimum(sizes[donor] - 1, most - sizes[sink]) // 2
    slack = jnp.where((donor == ranking[0]) | (sink == ranking[0]) | (sizes[sink] == 0), 0, jnp.maximum(slack, 0))
    passed = jax.random.randint(jax.random.fold_in(own, 4), (amount // 2,), 0, 1 << 20) % (slack + 1)
    sizes = sizes.at[donor].add(-passed).at[sink].add(passed)
    members = jnp.searchsorted(jnp.cumsum(sizes), jnp.arange(rows * top), side="right").astype(jnp.int32)
    table = members.reshape(top, rows).T
    table = table[jax.random.permutation(jax.random.fold_in(own, 1), rows)]
    offset_by = jax.random.randint(jax.random.fold_in(own, 2), (rows, 1), 0, top)
    return jnp.take_along_axis(table, (jnp.arange(top)[None, :] + offset_by) % top, axis=1)


def load_shares(number_of, total, bound, slope, full):
    portions = [(1 << 20) // math.isqrt(standing ** slope) + 1 for standing in range(1, number_of + 1)]
    largest = bound if full else min(bound, max(-(-total // number_of), total * portions[0] // sum(portions)))
    least = 1 if total - largest >= number_of - 1 else 0
    given, rest = [largest] + [least] * (number_of - 1), total - largest - least * (number_of - 1)
    while rest > 0:
        free = [i for i in range(1, number_of) if given[i] < largest] or [i for i in range(1, number_of) if given[i] < bound]
        pool, budget = sum([portions[i] for i in free]), rest
        for i in free:
            extra = min(bound - given[i], max(1, budget * portions[i] // pool), rest)
            given[i] = given[i] + extra
            rest = rest - extra
    return np.array(given)


def bell_draw(own_key, shape, spread, bound, split=(), kind=jnp.bfloat16):
    factor_of = levels(own_key, shape, split, -0.22, 0.18) if split else 1.0
    drawn = jax.random.normal(own_key, shape, jnp.float32) * spread * factor_of
    return jnp.minimum(jnp.maximum(drawn, -bound), bound).astype(kind)


def gaussian_with(rng, extent, spread, limit, split, heavy, kind=jnp.bfloat16):
    values = spread * jax.random.normal(rng, extent, jnp.float32)
    if split:
        values = values * levels(rng, extent, split, -0.22, 0.18)
    return jnp.clip(raised(values, jax.random.fold_in(rng, 3), *heavy), -limit, limit).astype(kind)


def setup_inputs(seed: int = 0) -> dict:
    key_of = jax.random.split(jax.random.key(seed), 15)
    tokens = bell_draw(key_of[0], (TOKENS, D), 1.0, 6.0, ((0, 32),))
    cotangent = gaussian_with(key_of[1], (TOKENS, D), 1.0, 6.0, ((0, 32),), (0, 1, 32, 2.75))
    routes_keys = jax.random.split(jax.random.fold_in(key_of[2], 1), TOKENS // TOK_DEV)
    routes_turns = jax.random.permutation(jax.random.fold_in(key_of[2], 3), TOKENS // TOK_DEV)
    routes = jax.vmap(lambda own, number: shared_out(jax.random.fold_in(key_of[2], 2), own, number, TOK_DEV, EXPERTS, TOP, CAPACITY, 1))(routes_keys, routes_turns).reshape((TOKENS, TOP))
    lengths = jax.vmap(lambda own: ragged_sizes(own, DOCUMENTS, GROUP, LONGEST, 2))(jax.random.split(key_of[3], N_DP)).reshape((N_DP, DOCUMENTS)).astype(jnp.int32)
    gain_attn = jnp.clip(1.0 + 0.1 * jax.random.normal(key_of[4], (D,), jnp.float32), 0.5, 1.5).astype(jnp.bfloat16)
    w_query = bell_draw(key_of[5], (D, HEADS * HEAD_DIM), (D // 2) ** -0.5, 0.21875, ((1, 8),))
    w_key = bell_draw(key_of[6], (D, KEY_HEADS * HEAD_DIM), (D // 2) ** -0.5, 0.21875, ((1, 8),))
    w_value = bell_draw(key_of[7], (D, KEY_HEADS * HEAD_DIM), D ** -0.5, 0.15625, ((1, 8),))
    w_out = bell_draw(key_of[8], (D, HEADS * HEAD_DIM), (HEADS * HEAD_DIM // 32) ** -0.5, 0.875, ((1, 8),))
    gain_moe = jnp.clip(1.0 + 0.1 * jax.random.normal(key_of[9], (D,), jnp.float32), 0.5, 1.5).astype(jnp.bfloat16)
    w_router = bell_draw(key_of[10], (D, EXPERTS), (4 * D) ** -0.5, 0.078125)
    w_gate = bell_draw(key_of[11], (EXPERTS, D, HIDDEN_SIZE), D ** -0.5, 0.15625, ((0, 8),))
    w_up = bell_draw(key_of[12], (EXPERTS, D, HIDDEN_SIZE), D ** -0.5, 0.15625, ((0, 8),))
    w_down = bell_draw(key_of[13], (EXPERTS, D, HIDDEN_SIZE), (HIDDEN_SIZE // 16) ** -0.5, 1.0, ((0, 8),))
    return dict(tokens=tokens, cotangent=cotangent, routes=routes, lengths=lengths, gain_attn=gain_attn, w_query=w_query, w_key=w_key, w_value=w_value, w_out=w_out, gain_moe=gain_moe, w_router=w_router, w_gate=w_gate, w_up=w_up, w_down=w_down)


@jax.custom_vjp
def low(v):
    return lax.optimization_barrier(v.astype(jnp.bfloat16)).astype(jnp.float32)

@jax.custom_vjp
def low_back(v):
    return v

def low_keep(v):
    return (low(v), None)

def low_pass(kept, grad):
    return (grad,)

def back_keep(v):
    return (v, None)

def back_low(kept, grad):
    return (low(grad),)
low.defvjp(low_keep, low_pass)
low_back.defvjp(back_keep, back_low)
epsilon = 1e-06
rope_base = 10000.0
masked_score = -1e+30
highest = lax.Precision.HIGHEST

def rms_scale(values, gain):
    inverse = lax.rsqrt(lax.optimization_barrier(jnp.mean(values * values, axis=-1, keepdims=True)) + epsilon)
    return values * inverse * gain

def doc_layout(lengths, total):
    ends = jnp.cumsum(lengths).astype(jnp.int32)
    starts = (ends - lengths).astype(jnp.int32)
    place = jnp.arange(total, dtype=jnp.int32)
    segment = lax.optimization_barrier(jnp.sum((place[:, None] >= ends[None, :]).astype(jnp.int32), axis=1)).astype(jnp.int32)
    member = segment[:, None] == jnp.arange(lengths.shape[0], dtype=jnp.int32)[None, :]
    offset = lax.optimization_barrier(jnp.sum(jnp.where(member, starts[None, :], 0), axis=1)).astype(jnp.int32)
    return (segment, (place - offset).astype(jnp.int32))

def rope_tables(place, width):
    half = width // 2
    freq = rope_base ** (-2.0 * jnp.arange(half, dtype=jnp.float32) / width)
    angle = place.astype(jnp.float32)[:, None] * freq[None, :]
    angle = jnp.concatenate([angle, angle], axis=1)
    return (jnp.cos(angle), jnp.sin(angle))

def rotate(values, cosine, sine):
    half = values.shape[-1] // 2
    turned = jnp.concatenate([-values[..., half:], values[..., :half]], axis=-1)
    return values * cosine[:, None, :] + turned * sine[:, None, :]

def attend_block(item, keys, values, segment, place):
    queries, query_segment, query_place = item
    scale = 1.0 / math.sqrt(HEAD_DIM)
    scores = jnp.einsum('qgrd,kgd->grqk', queries, keys, precision=highest) * scale
    scores = low_back(scores)
    allowed = (query_segment[:, None] == segment[None, :]) & (query_place[:, None] >= place[None, :])
    scores = jnp.where(allowed[None, None], scores, masked_score)
    probs = jax.nn.softmax(scores, axis=-1)
    return jnp.einsum('grqk,kgd->qgrd', low(probs), values, precision=highest)

def attend_group(queries, keys, values, lengths):
    segment, place = doc_layout(lengths, GROUP)
    cosine, sine = rope_tables(place, HEAD_DIM)
    ratio = HEADS // KEY_HEADS
    turned_q = low(rotate(queries.reshape(GROUP, HEADS, HEAD_DIM), cosine, sine))
    turned_k = low(rotate(keys.reshape(GROUP, KEY_HEADS, HEAD_DIM), cosine, sine))
    shaped_v = values.reshape(GROUP, KEY_HEADS, HEAD_DIM)
    blocks = GROUP // QUERY_BLOCK
    items = (turned_q.reshape(blocks, QUERY_BLOCK, KEY_HEADS, ratio, HEAD_DIM), segment.reshape(blocks, QUERY_BLOCK), place.reshape(blocks, QUERY_BLOCK))
    stepper = jax.checkpoint(attend_block)

    def one_block(item):
        return stepper(item, turned_k, shaped_v, segment, place)
    outputs = lax.map(one_block, items)
    return outputs.reshape(GROUP, HEADS * HEAD_DIM)

def slot_tables(routes):
    blocks = routes.shape[0] // TOK_DEV
    flat = routes.reshape(blocks, TOK_DEV * TOP)
    chosen = (flat[:, :, None] == jnp.arange(EXPERTS, dtype=jnp.int32)[None, None, :]).astype(jnp.int32)
    rank = lax.optimization_barrier(jnp.sum((jnp.cumsum(chosen, axis=1) - chosen) * chosen, axis=2)).astype(jnp.int32)
    target = (flat * CAPACITY + rank).astype(jnp.int32)
    route_ids = jnp.arange(blocks * TOK_DEV * TOP, dtype=jnp.int32).reshape(blocks, TOK_DEV * TOP)
    owners = jnp.broadcast_to(jnp.arange(blocks, dtype=jnp.int32)[:, None], flat.shape)
    source = jnp.zeros((blocks, EXPERTS * CAPACITY), jnp.int32).at[owners, target].set(route_ids)
    live = jnp.zeros((blocks, EXPERTS * CAPACITY), jnp.float32).at[owners, target].set(1.0)
    source = source.reshape(blocks, EXPERTS, CAPACITY).transpose(1, 0, 2).reshape(EXPERTS, blocks * CAPACITY)
    live = live.reshape(blocks, EXPERTS, CAPACITY).transpose(1, 0, 2).reshape(EXPERTS, blocks * CAPACITY)
    return (source, live)

def expert_step(normed, gates_flat, carry, item):
    gate_w, up_w, down_w, source, live = item
    token = (source // TOP).astype(jnp.int32)
    inputs = low_back(normed[token] * live[:, None])
    gate_pre = low_back(jnp.dot(inputs, gate_w, precision=highest))
    up_pre = low_back(jnp.dot(inputs, up_w, precision=highest))
    active = low(jax.nn.silu(gate_pre) * up_pre)
    result = low(low_back(jnp.einsum('cf,df->cd', active, down_w, precision=highest)))
    weight = gates_flat[source] * live
    return (carry.at[token].add(result * weight[:, None]), None)

def block(tokens, gain_attn, w_query, w_key, w_value, w_out, gain_moe, w_router, w_gate, w_up, w_down, routes, lengths):
    normed = low(rms_scale(tokens, gain_attn))
    queries = low_back(jnp.dot(normed, w_query, precision=highest))
    keys = low_back(jnp.dot(normed, w_key, precision=highest))
    values = low(low_back(jnp.dot(normed, w_value, precision=highest)))
    groups = lengths.shape[0]
    group_step = jax.checkpoint(attend_group)

    def one_group(item):
        return group_step(item[0], item[1], item[2], item[3])
    attended = lax.map(one_group, (queries.reshape(groups, GROUP, HEADS * HEAD_DIM), keys.reshape(groups, GROUP, KEY_HEADS * HEAD_DIM), values.reshape(groups, GROUP, KEY_HEADS * HEAD_DIM), lengths))
    attended = low(low_back(attended.reshape(groups * GROUP, HEADS * HEAD_DIM)))
    branch = low_back(jnp.einsum('tk,dk->td', attended, w_out, precision=highest))
    middle = tokens + branch
    normed_two = low(rms_scale(middle, gain_moe))
    logits = jnp.dot(normed_two, w_router, precision=highest)
    gates = jax.nn.softmax(jnp.take_along_axis(logits, routes, axis=1), axis=-1)
    source, live = slot_tables(routes)
    stepper = jax.checkpoint(partial(expert_step, normed_two, gates.reshape(-1)))
    mixture, unused = lax.scan(stepper, jnp.zeros_like(middle), (w_gate, w_up, w_down, source, live))
    return middle + mixture

def reference(tokens, cotangent, routes, lengths, gain_attn, w_query, w_key, w_value, w_out, gain_moe, w_router, w_gate, w_up, w_down):
    floats = tuple((item.astype(jnp.float32) for item in (tokens, gain_attn, w_query, w_key, w_value, w_out, gain_moe, w_router, w_gate, w_up, w_down)))

    def forward(*given):
        return block(*given, routes, lengths)
    mixed, pullback = jax.vjp(forward, *floats)
    grads = pullback(cotangent.astype(jnp.float32))
    return (mixed.astype(jnp.bfloat16), grads[0], grads[1], grads[2], grads[3], grads[4], grads[5], grads[6], grads[7], grads[8], grads[9], grads[10])
```

```python
import math

import jax
import jax.numpy as jnp
from jax import lax
from jax.experimental import pallas as pl
from jax.experimental.pallas import tpu as pltpu
from jax.sharding import PartitionSpec as P

HEAD_DIM = 64
EXPERTS = 40
TOP = 8
CAPACITY = 64
LANES = 128
QUERY_BLOCK = 256
ROUTE_ROWS = 16

epsilon = 1e-06
rope_base = 10000.0
masked_score = -1e30
f32 = jnp.float32
bf16 = jnp.bfloat16
VMEM_LIMIT = 56 * 1024 * 1024

NT = (((1,), (1,)), ((), ()))
TN = (((0,), (0,)), ((), ()))


def dot(a, b):
    return jnp.dot(a, b, preferred_element_type=f32)


def dot_nt(a, b):
    return lax.dot_general(a, b, NT, preferred_element_type=f32)


def dot_tn(a, b):
    return lax.dot_general(a, b, TN, preferred_element_type=f32)


def lane_of(shape):
    return lax.broadcasted_iota(jnp.int32, shape, len(shape) - 1)


def call(kernel, grid, prefetch, in_specs, out_specs, out_shape, scratch=(), flops=0, bytes_accessed=0):
    return pl.pallas_call(
        kernel,
        grid_spec=pltpu.PrefetchScalarGridSpec(
            num_scalar_prefetch=prefetch,
            grid=grid,
            in_specs=in_specs,
            out_specs=out_specs,
            scratch_shapes=list(scratch),
        ),
        out_shape=out_shape,
        compiler_params=pltpu.CompilerParams(
            vmem_limit_bytes=VMEM_LIMIT, dimension_semantics=("arbitrary",) * len(grid)
        ),
        cost_estimate=pl.CostEstimate(
            flops=int(flops), bytes_accessed=int(bytes_accessed), transcendentals=0
        ),
    )


def whole(shape):
    zeros = (0,) * len(shape)
    return pl.BlockSpec(shape, lambda *_: zeros)


def struct(shape, dtype):
    return jax.ShapeDtypeStruct(shape, dtype)


def turn_within_heads(values, sign):
    lane = lane_of(values.shape) % HEAD_DIM
    ahead = pltpu.roll(values, LANES - HEAD_DIM // 2, 1)
    behind = pltpu.roll(values, HEAD_DIM // 2, 1)
    return jnp.where(lane < HEAD_DIM // 2, -sign * ahead, sign * behind)


def project_kernel(
    place_ref, mine_ref, other_ref, gain_ref, w_ref, cos_ref, sin_ref,
    query_ref, key_ref, value_ref, normed_ref, tokens_ref, half
):
    step = pl.program_id(0)
    resid = jnp.where(step < half, mine_ref[0].astype(f32), other_ref[0].astype(f32))
    inverse = lax.rsqrt(jnp.mean(resid * resid, axis=1, keepdims=True) + epsilon)
    normed = (resid * inverse * gain_ref[...]).astype(bf16)
    raw = dot_nt(normed, w_ref[...])
    cosine, sine = cos_ref[...], sin_ref[...]

    def rot(values):
        return (values * cosine + turn_within_heads(values, 1.0) * sine).astype(bf16).astype(f32)

    first = rot(raw[:, :LANES])
    second = rot(raw[:, LANES : 2 * LANES])
    low = lane_of(first.shape) < HEAD_DIM
    scale = 1.0 / math.sqrt(HEAD_DIM)
    query_ref[0] = jnp.where(low, first * scale, 0.0).astype(bf16)
    query_ref[1] = jnp.where(low, 0.0, first * scale).astype(bf16)
    query_ref[2] = jnp.where(low, second * scale, 0.0).astype(bf16)
    key_ref[...] = jnp.where(low, pltpu.roll(second, HEAD_DIM, 1), second).astype(bf16)
    value_ref[...] = raw[:, 2 * LANES :].astype(bf16)
    normed_ref[...] = normed
    tokens_ref[...] = resid.astype(bf16)


def project(place, mine, other, gain, w_stack, cosine, sine):
    half, rows, width = mine.shape
    total = 2 * half * rows

    def where(step, place_ref):
        row = place_ref[0]
        return jnp.where(step < half, row * half + step, (1 - row) * half + step - half)

    def rows_of(step, place_ref):
        return (where(step, place_ref), 0)

    return call(
        lambda *refs: project_kernel(*refs, half),
        (2 * half,),
        1,
        [
            pl.BlockSpec((1, rows, width), lambda j, p: (jnp.minimum(j, half - 1), 0, 0)),
            pl.BlockSpec((1, rows, width), lambda j, p: (jnp.maximum(j - half, 0), 0, 0)),
            whole((1, width)),
            whole(w_stack.shape),
            pl.BlockSpec((rows, LANES), rows_of),
            pl.BlockSpec((rows, LANES), rows_of),
        ],
        [
            pl.BlockSpec((3, rows, LANES), lambda j, p: (0, where(j, p), 0)),
            pl.BlockSpec((rows, LANES), rows_of),
            pl.BlockSpec((rows, LANES), rows_of),
            pl.BlockSpec((rows, width), rows_of),
            pl.BlockSpec((rows, width), rows_of),
        ],
        [
            struct((3, total, LANES), bf16),
            struct((total, LANES), bf16),
            struct((total, LANES), bf16),
            struct((total, width), bf16),
            struct((total, width), bf16),
        ],
        flops=2 * total * width * w_stack.shape[0],
        bytes_accessed=6 * total * width,
    )(place, mine, other, gain, w_stack, cosine, sine)


def attend_kernel(query_ref, key_ref, value_ref, start_ref, packed_ref, plain_ref, total_ref, out_ref):
    blocks = query_ref.shape[1] // QUERY_BLOCK
    block = pl.program_id(0)
    for index in range(blocks):

        @pl.when(block == index)
        def _(index=index):
            rows = pl.ds(index * QUERY_BLOCK, QUERY_BLOCK)
            span = (index + 1) * QUERY_BLOCK
            row = index * QUERY_BLOCK + lax.broadcasted_iota(jnp.int32, (QUERY_BLOCK, span), 0)
            column = lane_of((QUERY_BLOCK, span))
            allowed = (column <= row) & (column >= start_ref[rows, :])

            def head(number, carry):
                scores = dot_nt(query_ref[number, rows, :], key_ref[0:span, :])
                scores = jnp.where(allowed, scores, masked_score)
                peak = jnp.max(scores, axis=1, keepdims=True)
                weights = jnp.exp(scores - peak)
                summed = jnp.sum(weights, axis=1, keepdims=True)
                probs = (weights * (1.0 / summed)).astype(bf16)
                out_ref[number] = dot(probs, value_ref[0:span, :])
                total = jnp.broadcast_to(peak + jnp.log(summed), (QUERY_BLOCK, LANES))
                total_ref[number, :, rows] = jnp.transpose(total)[0:8, :]
                return carry

            lax.fori_loop(0, 3, head, 0)
            low = lane_of((QUERY_BLOCK, LANES)) < HEAD_DIM
            one, two, three = out_ref[0], out_ref[1], out_ref[2]
            pair = jnp.where(low, one, two).astype(bf16)
            plain_ref[rows, 0:LANES] = pair
            plain_ref[rows, LANES : 2 * LANES] = jnp.where(low, three, 0.0).astype(bf16)
            if index < blocks // 2:
                packed_ref[rows, 0:LANES] = pair
                packed_ref[rows, LANES : 2 * LANES] = three.astype(bf16)
            else:
                back = pl.ds((index - blocks // 2) * QUERY_BLOCK, QUERY_BLOCK)
                before = packed_ref[back, LANES : 2 * LANES].astype(f32)
                packed_ref[back, LANES : 2 * LANES] = jnp.where(low, before, one).astype(bf16)
                packed_ref[back, 2 * LANES : 3 * LANES] = jnp.where(low, two, three).astype(bf16)


def attend(query, key, value, start):
    total = key.shape[0]
    return call(
        attend_kernel,
        (total // QUERY_BLOCK,),
        0,
        [whole(query.shape), whole(key.shape), whole(value.shape), whole(start.shape)],
        [whole((total // 2, 3 * LANES)), whole((total, 2 * LANES)), whole((3, 8, total))],
        [
            struct((total // 2, 3 * LANES), bf16),
            struct((total, 2 * LANES), bf16),
            struct((3, 8, total), f32),
        ],
        scratch=[pltpu.VMEM((3, QUERY_BLOCK, LANES), f32)],
        flops=8 * 3 * total * total * LANES,
        bytes_accessed=8 * total * LANES * 2,
    )(query, key, value, start)


def attend_back_kernel(
    query_ref, key_ref, value_ref, grad_ref, total_ref, start_ref, cos_ref, sin_ref,
    out_ref, query_grad_ref, key_grad_ref, value_grad_ref
):
    blocks = query_ref.shape[1] // QUERY_BLOCK
    block = pl.program_id(0)
    scale = 1.0 / math.sqrt(HEAD_DIM)

    @pl.when(block == 0)
    def _():
        key_grad_ref[...] = jnp.zeros_like(key_grad_ref)
        value_grad_ref[...] = jnp.zeros_like(value_grad_ref)

    def back(values, cosine, sine):
        return values * cosine + turn_within_heads(values * sine, -1.0)

    for index in range(blocks):

        @pl.when(block == index)
        def _(index=index):
            rows = pl.ds(index * QUERY_BLOCK, QUERY_BLOCK)
            span = (index + 1) * QUERY_BLOCK
            row = index * QUERY_BLOCK + lane_of((span, QUERY_BLOCK))
            column = lax.broadcasted_iota(jnp.int32, (span, QUERY_BLOCK), 0)
            allowed = (column <= row) & (column >= start_ref[0:1, rows])
            low = lane_of((QUERY_BLOCK, LANES)) < HEAD_DIM

            def head(number, carry):
                query = query_ref[number, rows, :]
                tile = pl.multiple_of((number // 2) * LANES, LANES)
                upstream = grad_ref[rows, pl.ds(tile, LANES)].astype(f32)
                keep = low == (number != 1)
                upstream = jnp.where(keep, upstream, 0.0).astype(bf16)
                scores = dot_nt(key_ref[0:span, :], query)
                probs = jnp.exp(scores - total_ref[number, 0:1, rows])
                probs = jnp.where(allowed, probs, 0.0)
                prob_grad = dot_nt(value_ref[0:span, :], upstream)
                row_dot = jnp.sum(probs * prob_grad, axis=0, keepdims=True)
                score_grad = (probs * (prob_grad - row_dot)).astype(bf16)
                key_grad_ref[0:span, :] += dot(score_grad, query)
                value_grad_ref[0:span, :] += dot(probs.astype(bf16), upstream)
                query_grad_ref[number] = dot_tn(score_grad, key_ref[0:span, :]) * scale
                return carry

            lax.fori_loop(0, 3, head, 0)
            cosine, sine = cos_ref[rows, :], sin_ref[rows, :]
            pair = jnp.where(low, query_grad_ref[0], query_grad_ref[1])
            out_ref[rows, 0:LANES] = back(pair, cosine, sine).astype(bf16)
            out_ref[rows, LANES : 2 * LANES] = back(query_grad_ref[2], cosine, sine).astype(bf16)

    @pl.when(block == blocks - 1)
    def _():
        low = lane_of(key_grad_ref.shape) < HEAD_DIM
        key_grad = key_grad_ref[...]
        key_grad = key_grad + pltpu.roll(key_grad, HEAD_DIM, 1)
        key_grad = back(key_grad, cos_ref[...], sin_ref[...])
        before = out_ref[:, LANES : 2 * LANES].astype(f32)
        out_ref[:, LANES : 2 * LANES] = jnp.where(low, before, key_grad).astype(bf16)
        value_grad = value_grad_ref[...]
        value_grad = value_grad + pltpu.roll(value_grad, HEAD_DIM, 1)
        out_ref[:, 2 * LANES : 3 * LANES] = jnp.where(low, value_grad, 0.0).astype(bf16)


def attend_back(query, key, value, grad, totals, start, cosine, sine):
    total = key.shape[0]
    args = (query, key, value, grad, totals, start, cosine, sine)
    return call(
        attend_back_kernel,
        (total // QUERY_BLOCK,),
        0,
        [whole(item.shape) for item in args],
        whole((total, 3 * LANES)),
        struct((total, 3 * LANES), bf16),
        scratch=[
            pltpu.VMEM((3, QUERY_BLOCK, LANES), f32),
            pltpu.VMEM((total, LANES), f32),
            pltpu.VMEM((total, LANES), f32),
        ],
        flops=16 * 3 * total * total * LANES,
        bytes_accessed=14 * total * LANES * 2,
    )(*args)


def branch_operand(ref):
    members = ref.shape[0]
    low = lane_of((ref.shape[1], LANES)) < HEAD_DIM
    pairs, thirds = [], []
    for member in range(members):
        one = ref[member, :, 0:LANES]
        mid = ref[member, :, LANES : 2 * LANES].astype(f32)
        end = ref[member, :, 2 * LANES : 3 * LANES].astype(f32)
        mid_turned = pltpu.roll(mid, HEAD_DIM, 1)
        end_turned = pltpu.roll(end, HEAD_DIM, 1)
        late = jnp.where(low, mid_turned, end_turned).astype(bf16)
        pairs.append(jnp.concatenate([one, late], axis=0))
        thirds.append((mid, end_turned))
    for member in range(0, members, 2):
        tops = []
        for which in range(2):
            left, right = thirds[member][which], thirds[member + 1][which]
            tops.append(jnp.where(low, left, pltpu.roll(right, HEAD_DIM, 1)).astype(bf16))
        pairs.append(jnp.concatenate(tops, axis=0))
    return jnp.concatenate(pairs, axis=1)


def middle_kernel(
    place_ref, att_mine_ref, att_other_ref, w_out_ref, tok_a_ref, tok_b_ref, cot_mine_ref, cot_other_ref,
    gain_ref, w_router_ref, after_ref,
    x_ref, g_ref, slot_gate_ref, rank_ref, middle_ref, gates_own_ref, gates_ref, ranks_ref
):
    step = pl.program_id(0)
    row, member = place_ref[0], place_ref[2]
    cols = pl.num_programs(0)
    rows = tok_a_ref.shape[0]
    local_experts = x_ref.shape[0]
    branch = dot(branch_operand(att_mine_ref), w_out_ref[row])
    branch = branch + dot(branch_operand(att_other_ref), w_out_ref[1 - row])
    for half in range(2):
        tok_ref = (tok_a_ref, tok_b_ref)[half]
        middle = tok_ref[...].astype(f32) + branch[half * rows : (half + 1) * rows]
        inverse = lax.rsqrt(jnp.mean(middle * middle, axis=1, keepdims=True) + epsilon)
        normed = (middle * inverse * gain_ref[...]).astype(bf16)
        is_mine = row == half
        cot = jnp.where(is_mine, cot_mine_ref[0].astype(f32), cot_other_ref[0].astype(f32))
        logits = dot_nt(w_router_ref[...], normed)
        padded = logits.shape[0]
        slot = lax.broadcasted_iota(jnp.int32, (padded, rows), 0)
        expert = (slot // 8) * local_experts + slot % 8
        expert = jnp.where(slot % 8 < local_experts, expert, -1).astype(f32)
        named = expert == cot[rows : rows + 1, 0:rows]
        for k in range(1, TOP):
            named = named | (expert == cot[rows + k : rows + k + 1, 0:rows])
        peak = jnp.max(jnp.where(named, logits, masked_score), axis=0, keepdims=True)
        weights = jnp.where(named, jnp.exp(logits - peak), 0.0)
        gates = weights / jnp.sum(weights, axis=0, keepdims=True)
        gates_ref[...] = gates
        ranks_ref[...] = jnp.where(named, dot(named.astype(f32).astype(bf16), after_ref[...]), -1.0)
        here = pl.ds(pl.multiple_of(member * 8, 8), 8)
        gate, rank = gates_ref[here, :], ranks_ref[here, :]
        rank_ref[half, 0] = rank
        chosen, slot_gates = [], []
        place = lax.broadcasted_iota(jnp.int32, (CAPACITY, rows), 0).astype(f32)
        for j in range(local_experts):
            hit = place == rank[j : j + 1, :]
            slot_gates.append(jnp.sum(jnp.where(hit, gate[j : j + 1, :], 0.0), axis=1, keepdims=True))
            chosen.append(jnp.where(hit, 1.0, 0.0).astype(bf16))
        chosen = jnp.concatenate(chosen, axis=0)
        slot_gate = jnp.concatenate(slot_gates, axis=0)
        picked = dot(chosen, normed).astype(bf16)
        grads = (dot(chosen, cot[0:rows].astype(bf16)) * slot_gate).astype(bf16)
        spread = jnp.broadcast_to(slot_gate, (slot_gate.shape[0], LANES))
        for j in range(local_experts):
            part = slice(j * CAPACITY, (j + 1) * CAPACITY)
            x_ref[j, half, 0] = picked[part]
            g_ref[j, half, 0] = grads[part]
            slot_gate_ref[j, half, 0] = spread[part]

        @pl.when(member == half * cols + step)
        def _(middle=middle, gates=gates):
            middle_ref[...] = middle
            gates_own_ref[...] = gates


def middle_and_dispatch(place, att_mine, att_other, w_out, tokens, cot_mine, cot_other, gain, w_router, local_experts):
    half = att_mine.shape[0]
    width = tokens.shape[1]
    rows = tokens.shape[0] // (2 * half)
    padded = w_router.shape[0]
    after = (jnp.arange(rows)[:, None] < jnp.arange(rows)[None, :]).astype(bf16)
    att_spec = pl.BlockSpec((half, rows, 3 * LANES), lambda i, p: (0, i, 0))
    cot_spec = pl.BlockSpec((1,) + cot_mine.shape[1:], lambda i, p: (i, 0, 0))
    slot_shape = (local_experts, 2, half, CAPACITY)
    return call(
        middle_kernel,
        (half,),
        1,
        [
            att_spec,
            att_spec,
            whole(w_out.shape),
            pl.BlockSpec((rows, width), lambda i, p: (i, 0)),
            pl.BlockSpec((rows, width), lambda i, p: (i + half, 0)),
            cot_spec,
            cot_spec,
            whole((1, width)),
            whole(w_router.shape),
            whole((rows, rows)),
        ],
        [
            pl.BlockSpec((local_experts, 2, 1, CAPACITY, width), lambda i, p: (0, 0, i, 0, 0)),
            pl.BlockSpec((local_experts, 2, 1, CAPACITY, width), lambda i, p: (0, 0, i, 0, 0)),
            pl.BlockSpec((local_experts, 2, 1, CAPACITY, LANES), lambda i, p: (0, 0, i, 0, 0)),
            pl.BlockSpec((2, 1, 8, rows), lambda i, p: (0, i, 0, 0)),
            whole((rows, width)),
            whole((padded, rows)),
        ],
        [
            struct(slot_shape + (width,), bf16),
            struct(slot_shape + (width,), bf16),
            struct(slot_shape + (LANES,), f32),
            struct((2, half, 8, rows), f32),
            struct((rows, width), f32),
            struct((padded, rows), f32),
        ],
        scratch=[pltpu.VMEM((padded, rows), f32), pltpu.VMEM((padded, rows), f32)],
        flops=2 * 2 * half * rows * width * (width + 2 * local_experts * CAPACITY),
        bytes_accessed=2 * 2 * half * rows * width * 5,
    )(place, att_mine, att_other, w_out, tokens, tokens, cot_mine, cot_other, gain, w_router, after)


def expert_kernel(
    x_ref, g_ref, gate_ref, w_gate_ref, w_up_ref, w_down_ref,
    back_ref, forth_ref, dots_ref, gate_grad_ref, up_grad_ref, down_grad_ref,
    active_ref, gate_low_ref, up_low_ref
):
    slots, width = x_ref.shape[1], x_ref.shape[2]
    chunk = 256

    def rows_step(index, carry):
        rows = pl.ds(pl.multiple_of(index * chunk, chunk), chunk)
        x, g = x_ref[0, rows, :], g_ref[0, rows, :]
        gate_pre = dot(x, w_gate_ref[0])
        up_pre = dot(x, w_up_ref[0])
        active_grad = dot(g, w_down_ref[0])
        sig = 1.0 / (1.0 + jnp.exp(-gate_pre))
        silu = gate_pre * sig
        active = (silu * up_pre).astype(bf16)
        gate_low = (active_grad * up_pre * sig * (1.0 + gate_pre * (1.0 - sig))).astype(bf16)
        up_low = (active_grad * silu).astype(bf16)
        active_ref[rows, :] = active
        gate_low_ref[rows, :] = gate_low
        up_low_ref[rows, :] = up_low
        dots = jnp.sum(active.astype(f32) * active_grad, axis=1, keepdims=True)
        dots_ref[0, rows, :] = jnp.broadcast_to(dots, (chunk, LANES))
        back = dot_nt(gate_low, w_gate_ref[0]) + dot_nt(up_low, w_up_ref[0])
        back_ref[0, rows, :] = back.astype(bf16)
        produced = dot_nt(active, w_down_ref[0]).astype(bf16).astype(f32)
        forth_ref[0, rows, :] = (produced * gate_ref[0, rows, 0:1]).astype(bf16)
        return carry

    lax.fori_loop(0, slots // chunk, rows_step, 0)

    def width_step(index, carry):
        cols = pl.ds(pl.multiple_of(index * chunk, chunk), chunk)
        x, g = x_ref[0, :, cols], g_ref[0, :, cols]
        gate_grad_ref[0, cols, :] = dot_tn(x, gate_low_ref[...]).astype(bf16)
        up_grad_ref[0, cols, :] = dot_tn(x, up_low_ref[...]).astype(bf16)
        down_grad_ref[0, cols, :] = dot_tn(g, active_ref[...]).astype(bf16)
        return carry

    lax.fori_loop(0, width // chunk, width_step, 0)


def run_experts(x, g, slot_gate, w_gate, w_up, w_down, first, count):
    slots, width = x.shape[1], x.shape[2]
    hidden = w_gate.shape[2]
    row_in = pl.BlockSpec((1, slots, width), lambda e: (e + first, 0, 0))
    row_out = pl.BlockSpec((1, slots, width), lambda e: (e, 0, 0))
    weight_in = pl.BlockSpec((1, width, hidden), lambda e: (e + first, 0, 0))
    weight_out = pl.BlockSpec((1, width, hidden), lambda e: (e, 0, 0))
    return call(
        expert_kernel,
        (count,),
        0,
        [
            row_in,
            row_in,
            pl.BlockSpec((1, slots, LANES), lambda e: (e + first, 0, 0)),
            weight_in,
            weight_in,
            weight_in,
        ],
        [
            row_out,
            row_out,
            pl.BlockSpec((1, slots, LANES), lambda e: (e, 0, 0)),
            weight_out,
            weight_out,
            weight_out,
        ],
        [
            struct((count, slots, width), bf16),
            struct((count, slots, width), bf16),
            struct((count, slots, LANES), f32),
            struct((count, width, hidden), bf16),
            struct((count, width, hidden), bf16),
            struct((count, width, hidden), bf16),
        ],
        scratch=[pltpu.VMEM((slots, hidden), bf16)] * 3,
        flops=2 * 9 * count * slots * width * hidden,
        bytes_accessed=2 * count * (4 * slots * width + 6 * width * hidden),
    )(x, g, slot_gate, w_gate, w_up, w_down)


def combine_kernel(place_ref, rank_ref, *refs, pieces, with_dots):
    step = pl.program_id(0)
    half = pl.num_programs(0) // 2
    parts = refs[:pieces]
    rest = refs[pieces:]
    rows = rank_ref.shape[2]
    place = lax.broadcasted_iota(jnp.int32, (CAPACITY, rows), 0).astype(f32)
    rank = rank_ref[0]
    local_experts = sum(part.shape[0] for part in parts)
    hits = [place == rank[j : j + 1, :] for j in range(local_experts)]
    chosen = jnp.concatenate([jnp.where(hit, 1.0, 0.0).astype(bf16) for hit in hits], axis=0)
    gathered = jnp.concatenate([part[j, 0] for part in parts for j in range(part.shape[0])], axis=0)
    summed = dot_tn(chosen, gathered).astype(bf16)
    if with_dots:
        dots, rest = rest[:pieces], rest[pieces:]
        column = [part[j, 0][:, 0:1] for part in dots for j in range(part.shape[0])]
        scattered = [
            jnp.sum(jnp.where(hit, value, 0.0), axis=0, keepdims=True) for hit, value in zip(hits, column)
        ]
        scattered.append(jnp.zeros((8 - local_experts, rows), f32))
        rest[2][0] = jnp.concatenate(scattered, axis=0)
    other_ref, mine_ref = rest[0], rest[1]

    @pl.when(step < half)
    def _():
        other_ref[0] = summed

    @pl.when(step >= half)
    def _():
        mine_ref[0] = summed


def combine(place, rank, parts, dots=None):
    half = rank.shape[0] // 2
    rows = rank.shape[2]
    width = parts[0].shape[-1]

    def where(step, place_ref):
        row = place_ref[0]
        return jnp.where(step < half, (1 - row) * half + step, row * half + step - half)

    def slots_of(array):
        return pl.BlockSpec((array.shape[0], 1) + array.shape[2:], lambda j, p: (0, where(j, p), 0, 0))

    parts = [part.reshape(part.shape[0], 2 * half, CAPACITY, width) for part in parts]
    inputs = list(parts)
    out_specs = [
        pl.BlockSpec((1, rows, width), lambda j, p: (jnp.minimum(j, half - 1), 0, 0)),
        pl.BlockSpec((1, rows, width), lambda j, p: (jnp.maximum(j - half, 0), 0, 0)),
    ]
    out_shape = [struct((half, rows, width), bf16), struct((half, rows, width), bf16)]
    if dots is not None:
        inputs += [item.reshape(item.shape[0], 2 * half, CAPACITY, LANES) for item in dots]
        out_specs.append(pl.BlockSpec((1, 8, rows), lambda j, p: (where(j, p), 0, 0)))
        out_shape.append(struct((2 * half, 8, rows), f32))
    return call(
        lambda *refs: combine_kernel(*refs, pieces=len(parts), with_dots=dots is not None),
        (2 * half,),
        1,
        [pl.BlockSpec((1, 8, rows), lambda j, p: (where(j, p), 0, 0))] + [slots_of(item) for item in inputs],
        out_specs,
        out_shape,
        flops=2 * 2 * half * rows * width * 320,
        bytes_accessed=2 * 2 * half * (rows + 320) * width,
    )(place, rank, *inputs)


def split_dot(dimension_numbers, values, exact):
    upper = values.astype(bf16)
    lower = (values - upper.astype(f32)).astype(bf16)
    return lax.dot_general(
        upper, exact, dimension_numbers, preferred_element_type=f32
    ) + lax.dot_general(lower, exact, dimension_numbers, preferred_element_type=f32)


def middle_back_kernel(
    sums_ref, dots_ref, gates_ref, middle_ref, cot_ref, gain_ref, w_router_ref, w_out_ref,
    grad_ref, branch_ref, attended_ref, small_ref
):
    dots, gates = dots_ref[...], gates_ref[...]
    logit_grad = dots - gates * jnp.sum(dots, axis=0, keepdims=True)
    middle = middle_ref[...]
    inverse = lax.rsqrt(jnp.mean(middle * middle, axis=1, keepdims=True) + epsilon)
    unit = middle * inverse
    gain = gain_ref[...]
    normed = (unit * gain).astype(bf16)
    grad = sums_ref[0].astype(f32)
    for index in range(1, sums_ref.shape[0]):
        grad = grad + sums_ref[index].astype(f32)
    grad = grad + split_dot(TN, logit_grad, w_router_ref[...])
    padded = logit_grad.shape[0]
    small_ref[0:padded, :] = split_dot((((1,), (0,)), ((), ())), logit_grad, normed)
    gain_grad = jnp.sum(grad * unit, axis=0, keepdims=True)
    small_ref[padded : padded + 8, :] = jnp.broadcast_to(gain_grad, (8, gain_grad.shape[1]))
    scaled = grad * gain
    middle_grad = cot_ref[...].astype(f32) + inverse * (
        scaled - unit * jnp.mean(scaled * unit, axis=1, keepdims=True)
    )
    grad_ref[...] = middle_grad
    branch_grad = middle_grad.astype(bf16)
    branch_ref[...] = branch_grad
    low = lane_of((branch_grad.shape[0], LANES)) < HEAD_DIM
    members = sums_ref.shape[0]
    for row in range(2):
        product = dot_nt(branch_grad, w_out_ref[row])
        for col in range(members):
            third = product[:, (members + col // 2) * LANES : (members + col // 2 + 1) * LANES]
            if col % 2:
                third = pltpu.roll(third, HEAD_DIM, 1)
            third = jnp.where(low, third, 0.0)
            attended_ref[row * members + col, :, 0:LANES] = product[:, col * LANES : (col + 1) * LANES].astype(bf16)
            attended_ref[row * members + col, :, LANES : 2 * LANES] = third.astype(bf16)


def middle_back(sums, dots, gates, middle, cotangent, gain, w_router, w_out):
    rows, width = middle.shape
    padded = gates.shape[0]
    members = 2 * sums.shape[0]
    args = (sums, dots, gates, middle, cotangent, gain, w_router, w_out)
    return call(
        middle_back_kernel,
        (1,),
        0,
        [whole(item.shape) for item in args],
        [
            whole((rows, width)),
            whole((rows, width)),
            whole((members, rows, 2 * LANES)),
            whole((padded + 8, width)),
        ],
        [
            struct((rows, width), f32),
            struct((rows, width), bf16),
            struct((members, rows, 2 * LANES), bf16),
            struct((padded + 8, width), f32),
        ],
        flops=2 * rows * width * width,
        bytes_accessed=2 * width * width + 16 * rows * width,
    )(*args)


def input_grad_kernel(place_ref, grads_ref, w_ref, tok_ref, other_ref, mine_ref, gain_grad_ref):
    step = pl.program_id(0)
    half = pl.num_programs(0) // 2
    product = dot(grads_ref[...], w_ref[...])
    resid = tok_ref[...].astype(f32)
    inverse = lax.rsqrt(jnp.mean(resid * resid, axis=1, keepdims=True) + epsilon)
    part = jnp.sum(product * (resid * inverse), axis=0, keepdims=True)

    @pl.when(step == 0)
    def _():
        gain_grad_ref[...] = jnp.zeros_like(gain_grad_ref)

    gain_grad_ref[...] += jnp.broadcast_to(part, gain_grad_ref.shape)

    @pl.when(step < half)
    def _():
        other_ref[0] = product.astype(bf16)

    @pl.when(step >= half)
    def _():
        mine_ref[0] = product.astype(bf16)


def input_grad(place, grads, w_stack, tokens, half):
    rows, width = tokens.shape[0] // (2 * half), tokens.shape[1]

    def where(step, place_ref):
        row = place_ref[0]
        return jnp.where(step < half, (1 - row) * half + step, row * half + step - half)

    return call(
        input_grad_kernel,
        (2 * half,),
        1,
        [
            pl.BlockSpec((rows, 3 * LANES), lambda j, p: (where(j, p), 0)),
            whole(w_stack.shape),
            pl.BlockSpec((rows, width), lambda j, p: (where(j, p), 0)),
        ],
        [
            pl.BlockSpec((1, rows, width), lambda j, p: (jnp.minimum(j, half - 1), 0, 0)),
            pl.BlockSpec((1, rows, width), lambda j, p: (jnp.maximum(j - half, 0), 0, 0)),
            whole((8, width)),
        ],
        [
            struct((half, rows, width), bf16),
            struct((half, rows, width), bf16),
            struct((8, width), f32),
        ],
        flops=2 * tokens.shape[0] * width * 3 * LANES,
        bytes_accessed=4 * tokens.shape[0] * width,
    )(place, grads, w_stack, tokens)


SWAP = [(0, 1), (1, 0)]


def gather_group(block, cols):
    mine = lax.all_to_all(
        jnp.broadcast_to(block[None], (cols,) + block.shape), "col", 0, 0, tiled=True
    )
    return mine, lax.ppermute(mine, "row", SWAP)


def scatter_group(other, mine):
    arrived = lax.ppermute(other, "row", SWAP)
    summed = (mine.astype(f32) + arrived.astype(f32)).astype(bf16)
    return lax.all_to_all(summed, "col", 0, 0, tiled=True)


def flip(value, axis, bit, size):
    return lax.ppermute(value, axis, [(i, i ^ (1 << bit)) for i in range(size)])


def bits_of(size):
    return size.bit_length() - 1


def sum_everywhere(value, sizes):
    for axis in ("row", "dp", "col"):
        for bit in range(bits_of(sizes[axis])):
            value = value + flip(value, axis, bit, sizes[axis])
    return value


def reduce_over_dp(value, size, turned):
    count = bits_of(size)
    index = lax.axis_index("dp")
    value = value.reshape(value.shape[:1] + (2,) * count + value.shape[2:])
    axes = list(range(count - 1, -1, -1))
    order = list(range(count))
    if turned:
        order = order[::-1]
    current = value
    for bit in order:
        axis = 1 + axes.index(bit)
        axes.remove(bit)
        own = (index >> bit) & 1
        keep = lax.dynamic_index_in_dim(current, own, axis, keepdims=False)
        send = lax.dynamic_index_in_dim(current, 1 - own, axis, keepdims=False).astype(bf16)
        current = keep.astype(f32) + flip(send, "dp", bit, size).astype(f32)
    return current


def layer(sizes):
    n_dp, n_row, n_col = sizes["dp"], sizes["row"], sizes["col"]
    members = n_row * n_col
    assert n_row == 2 and n_dp & (n_dp - 1) == 0 and n_col == 4

    def local(
        tokens, cotangent, routes, lengths, gain_attn, w_query, w_key, w_value, w_out,
        gain_moe, w_router, w_gate, w_up, w_down,
    ):
        rows, width = tokens.shape
        group = rows * members
        local_experts = w_gate.shape[0]
        row, col = lax.axis_index("row"), lax.axis_index("col")
        place = jnp.stack([row, col, row * n_col + col]).astype(jnp.int32)
        gain_one = gain_attn.astype(f32)[None]
        gain_two = gain_moe.astype(f32)[None]

        tok_mine, tok_other = gather_group(tokens, n_col)
        route_rows = jnp.zeros((ROUTE_ROWS, width), bf16)
        route_rows = lax.dynamic_update_slice(route_rows, routes.T.astype(bf16), (0, 0))
        cot_mine, cot_other = gather_group(jnp.concatenate([cotangent, route_rows], axis=0), n_col)
        w_out_mine, w_out_other = gather_group(w_out.T, n_col)

        def by_row(mine, other):
            first = jnp.where(row == 0, mine, other)
            second = jnp.where(row == 0, other, mine)
            return jnp.stack([first, second])

        w_out_all = by_row(w_out_mine, w_out_other)
        w_out_all = jnp.concatenate(
            [
                w_out_all[:, :, :LANES].reshape(2, n_col * LANES, width),
                w_out_all[:, :, LANES:].reshape(2, n_col * HEAD_DIM, width),
            ],
            axis=1,
        )
        w_stack = jnp.concatenate([w_query.T, w_key.T, w_value.T, w_value.T], axis=0)

        ends = jnp.cumsum(lengths[0])
        starts = ends - lengths[0]
        position = jnp.arange(group, dtype=jnp.int32)
        segment = jnp.sum((position[:, None] >= ends[None, :]).astype(jnp.int32), axis=1)
        member = segment[:, None] == jnp.arange(starts.shape[0], dtype=jnp.int32)[None, :]
        start = jnp.sum(jnp.where(member, starts[None, :], 0), axis=1).astype(jnp.int32)
        frequency = rope_base ** (-2.0 * jnp.arange(HEAD_DIM // 2, dtype=f32) / HEAD_DIM)
        angle = (position - start).astype(f32)[:, None] * frequency[None, :]
        cosine = jnp.tile(jnp.cos(angle), (1, 4))
        sine = jnp.tile(jnp.sin(angle), (1, 4))

        query, key, value, normed_one, tok_all = project(
            place, tok_mine, tok_other, gain_one, w_stack, cosine, sine
        )
        packed, attended, totals = attend(query, key, value, start[:, None])
        att_mine, att_other = gather_group(packed, n_col)

        w_router_rows = w_router.T.reshape(members, local_experts, width)
        w_router_rows = jnp.pad(w_router_rows, ((0, 0), (0, 8 - local_experts), (0, 0)))
        w_router_rows = w_router_rows.reshape(members * 8, width)
        x, g, slot_gate, rank, middle, gates = middle_and_dispatch(
            place, att_mine, att_other, w_out_all, tok_all, cot_mine, cot_other, gain_two,
            w_router_rows, local_experts,
        )
        slots = members * CAPACITY
        x = x.reshape(local_experts, slots, width)
        g = g.reshape(local_experts, slots, width)
        slot_gate = slot_gate.reshape(local_experts, slots, LANES)
        rank = rank.reshape(members, 8, rows)

        cuts = [0, 2, local_experts]
        runs = [
            run_experts(x, g, slot_gate, w_gate, w_up, w_down, first, last - first)
            for first, last in zip(cuts[:-1], cuts[1:])
        ]
        back_other, back_mine, dots = combine(
            place, rank, [run[0] for run in runs], [run[2] for run in runs]
        )
        dots = lax.all_to_all(dots, ("row", "col"), 0, 0, tiled=True).reshape(members * 8, rows)
        back = scatter_group(back_other, back_mine)

        expert_grads = []
        turned = False
        for run in runs:
            grads = []
            for item in run[3:]:
                cut = item.reshape(item.shape[0], n_dp, item.shape[1] // n_dp, item.shape[2])
                grads.append(reduce_over_dp(cut, n_dp, turned))
                turned = not turned
            expert_grads.append(grads)
        w_gate_grad, w_up_grad, w_down_grad = [
            jnp.concatenate([grads[which] for grads in expert_grads], axis=0) for which in range(3)
        ]

        forth_other, forth_mine = combine(place, rank, [run[1] for run in runs])
        forth = scatter_group(forth_other, forth_mine)
        mixed = (middle + jnp.sum(forth.astype(f32), axis=0)).astype(bf16)

        middle_grad, branch_grad, attended_grad, small = middle_back(
            back, dots, gates, middle, cotangent, gain_two, w_router_rows, w_out_all
        )
        attended_grad = lax.all_to_all(attended_grad, ("row", "col"), 0, 0, tiled=True)
        small = sum_everywhere(small, sizes)
        w_router_grad = small[: members * 8].reshape(members, 8, width)[:, :local_experts]
        w_router_grad = w_router_grad.reshape(members * local_experts, width).T
        gain_moe_grad = small[members * 8]
        branch_mine, branch_other = gather_group(branch_grad, n_col)
        branch_all = by_row(branch_mine, branch_other).reshape(group, width)

        start_row = jnp.broadcast_to(start[None, :], (8, group))
        projected_grad = attend_back(
            query, key, value, attended_grad.reshape(group, 2 * LANES), totals, start_row, cosine, sine
        )
        in_other, in_mine, gain_part = input_grad(place, projected_grad, w_stack, tok_all, n_col)
        gain_attn_grad = sum_everywhere(gain_part, sizes)[0]
        in_sums = scatter_group(in_other, in_mine)
        w_in_part = dot_tn(normed_one, projected_grad)
        w_out_part = dot_tn(branch_all, attended)
        local_q, local_k = w_query.shape[1], w_key.shape[1]
        w_part = jnp.concatenate(
            [w_in_part[:, : local_q + 2 * local_k], w_out_part[:, :local_q]], axis=1
        ).astype(bf16)
        w_part = w_part.reshape(1, n_dp, width // n_dp, w_part.shape[1])
        w_sum = reduce_over_dp(w_part, n_dp, False)[0]
        cut = local_q + local_k
        w_query_grad = w_sum[:, :local_q]
        w_key_grad = w_sum[:, local_q:cut]
        w_value_grad = w_sum[:, cut : cut + local_k]
        w_out_grad = w_sum[:, cut + local_k :]

        normed_grad = jnp.sum(in_sums.astype(f32), axis=0)
        resid = tokens.astype(f32)
        inverse = lax.rsqrt(jnp.mean(resid * resid, axis=1, keepdims=True) + epsilon)
        unit = resid * inverse
        scaled = normed_grad * gain_one
        tokens_grad = middle_grad + inverse * (
            scaled - unit * jnp.mean(scaled * unit, axis=1, keepdims=True)
        )
        return (
            mixed, tokens_grad, gain_attn_grad, w_query_grad, w_key_grad, w_value_grad, w_out_grad,
            gain_moe_grad, w_router_grad, w_gate_grad, w_up_grad, w_down_grad,
        )

    return local


def solution(mesh):
    return jax.shard_map(
        layer(dict(mesh.shape)),
        mesh=mesh,
        in_specs=(
            P(("dp", "row", "col"), None),
            P(("dp", "row", "col"), None),
            P(("dp", "row", "col"), None),
            P("dp", None),
            P(),
            P(None, ("row", "col")),
            P(None, ("row", "col")),
            P(None, ("row", "col")),
            P(None, ("row", "col")),
            P(),
            P(),
            P(("row", "col"), None, None),
            P(("row", "col"), None, None),
            P(("row", "col"), None, None),
        ),
        out_specs=(
            P(("dp", "row", "col"), None),
            P(("dp", "row", "col"), None),
            P(),
            P("dp", ("row", "col")),
            P("dp", ("row", "col")),
            P("dp", ("row", "col")),
            P("dp", ("row", "col")),
            P(),
            P(),
            P(("row", "col"), "dp", None),
            P(("row", "col"), "dp", None),
            P(("row", "col"), "dp", None),
        ),
        check_vma=False,
    )
```

```python
import math

import jax
import jax.numpy as jnp
from jax import lax
from jax.experimental import pallas as pl
from jax.experimental.pallas import tpu as pltpu
from jax.sharding import PartitionSpec as P

HEAD_DIM = 64
EXPERTS = 40
TOP = 8
CAPACITY = 64
COLS = 4
LANES = 128
QUERY_BLOCK = 256
ROUTE_ROWS = 16

epsilon = 1e-06
rope_base = 10000.0
masked_score = -1e30
f32 = jnp.float32
bf16 = jnp.bfloat16
VMEM_LIMIT = 56 * 1024 * 1024

NT = (((1,), (1,)), ((), ()))
TN = (((0,), (0,)), ((), ()))


def dot(a, b):
    return jnp.dot(a, b, preferred_element_type=f32)


def dot_nt(a, b):
    return lax.dot_general(a, b, NT, preferred_element_type=f32)


def dot_tn(a, b):
    return lax.dot_general(a, b, TN, preferred_element_type=f32)


def lane_of(shape):
    return lax.broadcasted_iota(jnp.int32, shape, len(shape) - 1)


def call(
    kernel, grid, prefetch, in_specs, out_specs, out_shape, scratch=(), flops=0, bytes_accessed=0, aliases=None
):
    return pl.pallas_call(
        kernel,
        grid_spec=pltpu.PrefetchScalarGridSpec(
            num_scalar_prefetch=prefetch,
            grid=grid,
            in_specs=in_specs,
            out_specs=out_specs,
            scratch_shapes=list(scratch),
        ),
        out_shape=out_shape,
        input_output_aliases=aliases or {},
        compiler_params=pltpu.CompilerParams(
            vmem_limit_bytes=VMEM_LIMIT, dimension_semantics=("arbitrary",) * len(grid)
        ),
        cost_estimate=pl.CostEstimate(
            flops=int(flops), bytes_accessed=int(bytes_accessed), transcendentals=0
        ),
    )


def whole(shape):
    zeros = (0,) * len(shape)
    return pl.BlockSpec(shape, lambda *_: zeros)


def struct(shape, dtype):
    return jax.ShapeDtypeStruct(shape, dtype)


RING = (0, 2, 3, 1)


def member_of(step, place_ref):
    row, col = place_ref[0], place_ref[1]
    turn = lax.rem(step, COLS)
    offset = jnp.where(turn == 0, RING[0], jnp.where(turn == 1, RING[1], jnp.where(turn == 2, RING[2], RING[3])))
    line = jnp.where(step < COLS, row, 1 - row)
    return line * COLS + lax.rem(col + offset, COLS)


def fetch(step, place_ref, refs, store):
    col = place_ref[1]
    for index in range(2 * COLS):
        own, two, before, later, relayed = refs[5 * (index // COLS) : 5 * (index // COLS) + 5]

        @pl.when(step == index)
        def _(index=index, own=own, two=two, before=before, later=later, relayed=relayed):
            if index % COLS == 0:
                store(own)
            elif index % COLS == 1:
                store(two)
            else:
                near, edge = (before, 0) if index % COLS == 2 else (later, COLS - 1)

                @pl.when(col == edge)
                def _():
                    store(relayed)

                @pl.when(col != edge)
                def _():
                    store(near)


def turn_within_heads(values, sign):
    lane = lane_of(values.shape) % HEAD_DIM
    ahead = pltpu.roll(values, LANES - HEAD_DIM // 2, 1)
    behind = pltpu.roll(values, HEAD_DIM // 2, 1)
    return jnp.where(lane < HEAD_DIM // 2, -sign * ahead, sign * behind)


def project_kernel(place_ref, *refs):
    pieces, (gain_ref, w_ref, cos_ref, sin_ref) = refs[:10], refs[10:14]
    query_ref, key_ref, value_ref, normed_ref, tokens_ref, block_ref, all_ref = refs[14:]
    step = pl.program_id(0)

    def store(ref):
        block_ref[...] = ref[...]

    fetch(step, place_ref, pieces, store)
    resid = block_ref[...].astype(f32)
    rows = resid.shape[0]
    inverse = lax.rsqrt(jnp.mean(resid * resid, axis=1, keepdims=True) + epsilon)
    normed = (resid * inverse * gain_ref[...]).astype(bf16)
    normed_ref[...] = normed
    tokens_ref[...] = block_ref[...]
    all_ref[pl.ds(pl.multiple_of(member_of(step, place_ref) * rows, rows), rows), :] = normed

    @pl.when(step == pl.num_programs(0) - 1)
    def _():
        scale = 1.0 / math.sqrt(HEAD_DIM)
        chunk = 512
        low = lane_of((chunk, LANES)) < HEAD_DIM

        def body(index, carry):
            part = pl.ds(pl.multiple_of(index * chunk, chunk), chunk)
            raw = dot_nt(all_ref[part, :], w_ref[...])
            cosine, sine = cos_ref[part, :], sin_ref[part, :]

            def rot(values):
                return (values * cosine + turn_within_heads(values, 1.0) * sine).astype(bf16).astype(f32)

            first = rot(raw[:, :LANES])
            second = rot(raw[:, LANES : 2 * LANES])
            query_ref[0, part, :] = jnp.where(low, first * scale, 0.0).astype(bf16)
            query_ref[1, part, :] = jnp.where(low, 0.0, first * scale).astype(bf16)
            query_ref[2, part, :] = jnp.where(low, second * scale, 0.0).astype(bf16)
            key_ref[part, :] = jnp.where(low, pltpu.roll(second, HEAD_DIM, 1), second).astype(bf16)
            value_ref[part, :] = raw[:, 2 * LANES :].astype(bf16)
            return carry

        lax.fori_loop(0, all_ref.shape[0] // chunk, body, 0)


def project(place, pieces, gain, w_stack, cosine, sine):
    rows, width = pieces[0].shape
    total = 2 * COLS * rows
    by_member = pl.BlockSpec((rows, width), lambda j, p: (member_of(j, p), 0))
    return call(
        project_kernel,
        (2 * COLS,),
        1,
        [whole((rows, width))] * 10
        + [whole((1, width)), whole(w_stack.shape), whole((total, LANES)), whole((total, LANES))],
        [whole((3, total, LANES)), whole((total, LANES)), whole((total, LANES)), by_member, by_member],
        [
            struct((3, total, LANES), bf16),
            struct((total, LANES), bf16),
            struct((total, LANES), bf16),
            struct((total, width), bf16),
            struct((total, width), bf16),
        ],
        scratch=[pltpu.VMEM((rows, width), bf16), pltpu.VMEM((total, width), bf16)],
        flops=2 * total * width * w_stack.shape[0],
        bytes_accessed=6 * total * width,
    )(place, *pieces, gain, w_stack, cosine, sine)


def attend_kernel(
    query_ref, key_ref, value_ref, start_ref, packed_ref, plain_ref, total_ref, out_ref, *, half
):
    blocks = pl.num_programs(0)
    block = pl.program_id(0)
    count = plain_ref.shape[0] // QUERY_BLOCK
    for index in range(count):

        @pl.when(block == index)
        def _(index=index):
            first = (half * count + index) * QUERY_BLOCK
            rows = pl.ds(first, QUERY_BLOCK)
            here = pl.ds(index * QUERY_BLOCK, QUERY_BLOCK)
            span = first + QUERY_BLOCK
            row = first + lax.broadcasted_iota(jnp.int32, (QUERY_BLOCK, span), 0)
            column = lane_of((QUERY_BLOCK, span))
            allowed = (column <= row) & (column >= start_ref[rows, :])

            def head(number, carry):
                scores = dot_nt(query_ref[number, rows, :], key_ref[0:span, :])
                scores = jnp.where(allowed, scores, masked_score)
                peak = jnp.max(scores, axis=1, keepdims=True)
                weights = jnp.exp(scores - peak)
                summed = jnp.sum(weights, axis=1, keepdims=True)
                probs = (weights * (1.0 / summed)).astype(bf16)
                out_ref[number, here, :] = dot(probs, value_ref[0:span, :])
                total = jnp.broadcast_to(peak + jnp.log(summed), (QUERY_BLOCK, LANES))
                total_ref[number, :, here] = jnp.transpose(total)[0:8, :]
                return carry

            lax.fori_loop(0, 3, head, 0)

    @pl.when(block == blocks - 1)
    def _():
        total = plain_ref.shape[0]
        low = lane_of((total, LANES)) < HEAD_DIM
        plain_ref[:, 0:LANES] = jnp.where(low, out_ref[0], out_ref[1]).astype(bf16)
        plain_ref[:, LANES : 2 * LANES] = jnp.where(low, out_ref[2], 0.0).astype(bf16)
        mid = total // 2
        low = lane_of((mid, LANES)) < HEAD_DIM
        packed_ref[:, 0:LANES] = jnp.where(low, out_ref[0, :mid], out_ref[1, :mid]).astype(bf16)
        packed_ref[:, LANES : 2 * LANES] = jnp.where(low, out_ref[2, :mid], out_ref[0, mid:]).astype(bf16)
        packed_ref[:, 2 * LANES :] = jnp.where(low, out_ref[1, mid:], out_ref[2, mid:]).astype(bf16)


def attend(query, key, value, start, half):
    total = key.shape[0] // 2
    return call(
        lambda *refs: attend_kernel(*refs, half=half),
        (total // QUERY_BLOCK,),
        0,
        [whole(query.shape), whole(key.shape), whole(value.shape), whole(start.shape)],
        [whole((total // 2, 3 * LANES)), whole((total, 2 * LANES)), whole((3, 8, total))],
        [
            struct((total // 2, 3 * LANES), bf16),
            struct((total, 2 * LANES), bf16),
            struct((3, 8, total), f32),
        ],
        scratch=[pltpu.VMEM((3, total, LANES), f32)],
        flops=8 * 3 * total * total * LANES * (1 + 2 * half),
        bytes_accessed=16 * total * LANES * 2,
    )(query, key, value, start)


def attend_back_kernel(place_ref, *refs):
    grads = refs[:8]
    query_ref, key_ref, value_ref, total_a_ref, total_b_ref, start_ref, cos_ref, sin_ref = refs[8:16]
    out_ref, grad_ref, query_grad_ref, key_grad_ref, value_grad_ref = refs[16:]
    blocks = pl.num_programs(0)
    block = pl.program_id(0)
    scale = 1.0 / math.sqrt(HEAD_DIM)

    @pl.when(block == 0)
    def _():
        key_grad_ref[...] = jnp.zeros_like(key_grad_ref)
        value_grad_ref[...] = jnp.zeros_like(value_grad_ref)
        row, col = place_ref[0], place_ref[1]
        rows = grads[0].shape[0]
        for index, ref in enumerate(grads):
            line = row if index < COLS else 1 - row
            member = line * COLS + lax.rem(col + COLS - index % COLS, COLS)
            grad_ref[pl.ds(pl.multiple_of(member * rows, rows), rows), :] = ref[...]

    def back(values, cosine, sine):
        return values * cosine + turn_within_heads(values * sine, -1.0)

    for index in range(out_ref.shape[0] // QUERY_BLOCK):

        @pl.when(block == index)
        def _(index=index):
            first = index * QUERY_BLOCK
            rows = pl.ds(first, QUERY_BLOCK)
            span = first + QUERY_BLOCK
            half = total_a_ref.shape[2]
            total_ref, here = (total_a_ref, rows) if first < half else (total_b_ref, pl.ds(first - half, QUERY_BLOCK))
            row = first + lane_of((span, QUERY_BLOCK))
            column = lax.broadcasted_iota(jnp.int32, (span, QUERY_BLOCK), 0)
            allowed = (column <= row) & (column >= start_ref[0:1, rows])
            low = lane_of((QUERY_BLOCK, LANES)) < HEAD_DIM

            def head(number, carry):
                query = query_ref[number, rows, :]
                tile = pl.multiple_of((number // 2) * LANES, LANES)
                upstream = grad_ref[rows, pl.ds(tile, LANES)].astype(f32)
                keep = low == (number != 1)
                upstream = jnp.where(keep, upstream, 0.0).astype(bf16)
                scores = dot_nt(key_ref[0:span, :], query)
                probs = jnp.exp(scores - total_ref[number, 0:1, here])
                probs = jnp.where(allowed, probs, 0.0)
                prob_grad = dot_nt(value_ref[0:span, :], upstream)
                row_dot = jnp.sum(probs * prob_grad, axis=0, keepdims=True)
                score_grad = (probs * (prob_grad - row_dot)).astype(bf16)
                key_grad_ref[0:span, :] += dot(score_grad, query)
                value_grad_ref[0:span, :] += dot(probs.astype(bf16), upstream)
                query_grad_ref[number] = dot_tn(score_grad, key_ref[0:span, :]) * scale
                return carry

            lax.fori_loop(0, 3, head, 0)
            cosine, sine = cos_ref[rows, :], sin_ref[rows, :]
            pair = jnp.where(low, query_grad_ref[0], query_grad_ref[1])
            out_ref[rows, 0:LANES] = back(pair, cosine, sine).astype(bf16)
            out_ref[rows, LANES : 2 * LANES] = back(query_grad_ref[2], cosine, sine).astype(bf16)

    @pl.when(block == blocks - 1)
    def _():
        low = lane_of(key_grad_ref.shape) < HEAD_DIM
        key_grad = key_grad_ref[...]
        key_grad = key_grad + pltpu.roll(key_grad, HEAD_DIM, 1)
        key_grad = back(key_grad, cos_ref[...], sin_ref[...])
        before = out_ref[:, LANES : 2 * LANES].astype(f32)
        out_ref[:, LANES : 2 * LANES] = jnp.where(low, before, key_grad).astype(bf16)
        value_grad = value_grad_ref[...]
        value_grad = value_grad + pltpu.roll(value_grad, HEAD_DIM, 1)
        out_ref[:, 2 * LANES : 3 * LANES] = jnp.where(low, 0.0, value_grad).astype(bf16)


def attend_back(place, grads, query, key, value, total_a, total_b, start, cosine, sine):
    total = key.shape[0]
    args = (query, key, value, total_a, total_b, start, cosine, sine)
    return call(
        attend_back_kernel,
        (total // QUERY_BLOCK,),
        1,
        [whole(item.shape) for item in tuple(grads) + args],
        whole((total, 3 * LANES)),
        struct((total, 3 * LANES), bf16),
        scratch=[
            pltpu.VMEM((total, 2 * LANES), bf16),
            pltpu.VMEM((3, QUERY_BLOCK, LANES), f32),
            pltpu.VMEM((total, LANES), f32),
            pltpu.VMEM((total, LANES), f32),
        ],
        flops=16 * 3 * total * total * LANES,
        bytes_accessed=14 * total * LANES * 2,
    )(place, *grads, *args)


def middle_kernel(place_ref, *refs, half):
    pieces, (w_out_ref, tok_ref, routes_ref, gain_ref, w_router_ref, after_ref) = refs[:10], refs[10:16]
    x_ref, slot_gate_ref, rank_ref, gate_ref, middle_ref, gates_own_ref = refs[16:22]
    left_ref, mid_ref, gates_ref, ranks_ref = refs[22:]
    col, member = place_ref[1], place_ref[2]
    rows = after_ref.shape[0]
    part = pieces[0].shape[0]
    blocks = tok_ref.shape[0] // rows
    local_experts = x_ref.shape[0]
    low = lane_of((part, LANES)) < HEAD_DIM

    thirds = []
    for index in range(2 * COLS):
        own, two, before, later, relayed = pieces[5 * (index // COLS) : 5 * (index // COLS) + 5]

        def tile(number):
            lanes = slice(number * LANES, (number + 1) * LANES)
            if index % COLS == 0:
                return own[:, lanes].astype(f32)
            if index % COLS == 1:
                return two[:, lanes].astype(f32)
            near, edge = (before, 0) if index % COLS == 2 else (later, COLS - 1)
            return jnp.where(col == edge, relayed[:, lanes].astype(f32), near[:, lanes].astype(f32))

        one, mid, end = tile(0), tile(1), tile(2)
        mid_turned, end_turned = pltpu.roll(mid, HEAD_DIM, 1), pltpu.roll(end, HEAD_DIM, 1)
        lanes = slice(index * LANES, (index + 1) * LANES)
        left_ref[0:part, lanes] = one.astype(bf16)
        left_ref[part:, lanes] = jnp.where(low, mid_turned, end_turned).astype(bf16)
        thirds.append((mid, end_turned))
        if index % 2:
            lanes = slice((2 * COLS + index // 2) * LANES, (2 * COLS + index // 2 + 1) * LANES)
            for which in range(2):
                right = pltpu.roll(thirds[index][which], HEAD_DIM, 1)
                joined = jnp.where(low, thirds[index - 1][which], right).astype(bf16)
                left_ref[which * part : (which + 1) * part, lanes] = joined

    order = [member_of(jnp.int32(index), place_ref) for index in range(2 * COLS)]
    chunk = 256

    def columns(index, carry):
        cols = pl.ds(pl.multiple_of(index * chunk, chunk), chunk)
        right = [w_out_ref[source, 0:LANES, cols] for source in order]
        right += [w_out_ref[source, LANES:, cols] for source in order]
        branch = dot(left_ref[...], jnp.concatenate(right, axis=0))
        mid_ref[:, cols] = tok_ref[:, cols].astype(f32) + branch
        return carry

    lax.fori_loop(0, tok_ref.shape[1] // chunk, columns, 0)

    def block(index, carry):
        here = pl.ds(pl.multiple_of(index * rows, rows), rows)
        middle = mid_ref[here, :]
        inverse = lax.rsqrt(jnp.mean(middle * middle, axis=1, keepdims=True) + epsilon)
        normed = (middle * inverse * gain_ref[...]).astype(bf16)
        logits = dot_nt(w_router_ref[...], normed)
        padded = logits.shape[0]
        slot = lax.broadcasted_iota(jnp.int32, (padded, rows), 0)
        expert = (slot // 8) * local_experts + slot % 8
        expert = jnp.where(slot % 8 < local_experts, expert, -1).astype(f32)
        routes = routes_ref[index].astype(f32)
        named = expert == routes[0:1, 0:rows]
        for k in range(1, TOP):
            named = named | (expert == routes[k : k + 1, 0:rows])
        peak = jnp.max(jnp.where(named, logits, masked_score), axis=0, keepdims=True)
        weights = jnp.where(named, jnp.exp(logits - peak), 0.0)
        gates = weights / jnp.sum(weights, axis=0, keepdims=True)
        gates_ref[...] = gates
        ranks_ref[...] = jnp.where(named, dot(named.astype(f32).astype(bf16), after_ref[...]), -1.0)
        mine = pl.ds(pl.multiple_of(member * 8, 8), 8)
        gate, rank = gates_ref[mine, :], ranks_ref[mine, :]
        rank_ref[index] = rank
        gate_ref[index] = gate
        chosen, slot_gates = [], []
        place = lax.broadcasted_iota(jnp.int32, (CAPACITY, rows), 0).astype(f32)
        for j in range(local_experts):
            hit = place == rank[j : j + 1, :]
            slot_gates.append(jnp.sum(jnp.where(hit, gate[j : j + 1, :], 0.0), axis=1, keepdims=True))
            chosen.append(jnp.where(hit, 1.0, 0.0).astype(bf16))
        picked = dot(jnp.concatenate(chosen, axis=0), normed).astype(bf16)
        spread = jnp.broadcast_to(jnp.concatenate(slot_gates, axis=0), (local_experts * CAPACITY, LANES))
        for j in range(local_experts):
            x_ref[j, index] = picked[j * CAPACITY : (j + 1) * CAPACITY]
            slot_gate_ref[j, index] = spread[j * CAPACITY : (j + 1) * CAPACITY]

        @pl.when(member == half * COLS + index)
        def _():
            middle_ref[...] = middle
            gates_own_ref[...] = gates

        return carry

    lax.fori_loop(0, blocks, block, 0)


def middle_and_dispatch(place, pieces, w_out, tokens, routes, gain, w_router, local_experts, half):
    width = tokens.shape[1]
    total = tokens.shape[0] // 2
    rows = total // COLS
    padded = w_router.shape[0]
    after = (jnp.arange(rows)[:, None] < jnp.arange(rows)[None, :]).astype(bf16)
    slot_shape = (local_experts, COLS, CAPACITY)
    return call(
        lambda *refs: middle_kernel(*refs, half=half),
        (1,),
        1,
        [whole(pieces[0].shape)] * 10
        + [
            whole(w_out.shape),
            pl.BlockSpec((total, width), lambda i, p: (half, 0)),
            pl.BlockSpec((COLS,) + routes.shape[1:], lambda i, p: (half, 0, 0)),
            whole((1, width)),
            whole(w_router.shape),
            whole((rows, rows)),
        ],
        [
            whole(slot_shape + (width,)),
            whole(slot_shape + (LANES,)),
            whole((COLS, 8, rows)),
            whole((COLS, 8, rows)),
            whole((rows, width)),
            whole((padded, rows)),
        ],
        [
            struct(slot_shape + (width,), bf16),
            struct(slot_shape + (LANES,), f32),
            struct((COLS, 8, rows), f32),
            struct((COLS, 8, rows), f32),
            struct((rows, width), f32),
            struct((padded, rows), f32),
        ],
        scratch=[
            pltpu.VMEM((total, width), bf16),
            pltpu.VMEM((total, width), f32),
            pltpu.VMEM((padded, rows), f32),
            pltpu.VMEM((padded, rows), f32),
        ],
        flops=2 * total * width * (width + local_experts * CAPACITY),
        bytes_accessed=10 * total * width,
    )(place, *pieces, w_out, tokens, routes, gain, w_router, after)


def hits_of(rank, local_experts):
    place = lax.broadcasted_iota(jnp.int32, (CAPACITY, rank.shape[1]), 0).astype(f32)
    return [place == rank[j : j + 1, :] for j in range(local_experts)]


def chosen_of(hits):
    return jnp.concatenate([jnp.where(hit, 1.0, 0.0).astype(bf16) for hit in hits], axis=0)


def grad_dispatch_kernel(place_ref, *refs):
    pieces, (rank_ref, gate_ref, g_ref, block_ref) = refs[:10], refs[10:]
    local_experts = g_ref.shape[0]

    def store(ref):
        block_ref[...] = ref[...]

    fetch(pl.program_id(0), place_ref, pieces, store)
    gate = gate_ref[0]
    hits = hits_of(rank_ref[0], local_experts)
    slot_gate = [
        jnp.sum(jnp.where(hit, gate[j : j + 1, :], 0.0), axis=1, keepdims=True) for j, hit in enumerate(hits)
    ]
    grads = (dot(chosen_of(hits), block_ref[...]) * jnp.concatenate(slot_gate, axis=0)).astype(bf16)
    for j in range(local_experts):
        g_ref[j, 0] = grads[j * CAPACITY : (j + 1) * CAPACITY]


def grad_dispatch(place, pieces, rank, gate, local_experts):
    rows, width = pieces[0].shape
    small = pl.BlockSpec((1, 8, rows), lambda j, p: (member_of(j, p), 0, 0))
    return call(
        grad_dispatch_kernel,
        (2 * COLS,),
        1,
        [whole((rows, width))] * 10 + [small, small],
        pl.BlockSpec((local_experts, 1, CAPACITY, width), lambda j, p: (0, member_of(j, p), 0, 0)),
        struct((local_experts, 2 * COLS, CAPACITY, width), bf16),
        scratch=[pltpu.VMEM((rows, width), bf16)],
        flops=2 * 2 * COLS * rows * width * local_experts * CAPACITY,
        bytes_accessed=2 * 2 * COLS * (rows + local_experts * CAPACITY) * width,
    )(place, *pieces, rank, gate)


def expert_kernel(
    x_ref, gate_ref, w_gate_ref, w_up_ref, w_down_ref, forth_ref, active_ref, factor_ref, silu_ref
):
    width, hidden = w_gate_ref.shape[1], w_gate_ref.shape[2]
    chunk = 256
    for first in range(0, hidden, chunk):
        cols = slice(first, first + chunk)
        gate_pre = dot(x_ref[0], w_gate_ref[0, :, cols])
        up_pre = dot(x_ref[0], w_up_ref[0, :, cols])
        sig = 1.0 / (1.0 + jnp.exp(-gate_pre))
        silu = gate_pre * sig
        silu_ref[0, :, cols] = silu
        factor_ref[0, :, cols] = up_pre * sig * (1.0 + gate_pre * (1.0 - sig))
        active_ref[0, :, cols] = (silu * up_pre).astype(bf16)

    def columns(index, carry):
        cols = pl.ds(pl.multiple_of(index * chunk, chunk), chunk)
        produced = dot_nt(active_ref[0], w_down_ref[0, cols, :]).astype(bf16).astype(f32)
        forth_ref[0, :, cols] = (produced * gate_ref[0, :, 0:1]).astype(bf16)
        return carry

    lax.fori_loop(0, width // chunk, columns, 0)


def run_experts(x, slot_gate, w_gate, w_up, w_down):
    count, slots, width = x.shape
    hidden = w_gate.shape[2]

    def per_expert(*shape):
        return pl.BlockSpec((1,) + shape, lambda e: (e, 0, 0))

    return call(
        expert_kernel,
        (count,),
        0,
        [per_expert(slots, width), per_expert(slots, LANES)] + [per_expert(width, hidden)] * 3,
        [per_expert(slots, width)] + [per_expert(slots, hidden)] * 3,
        [
            struct((count, slots, width), bf16),
            struct((count, slots, hidden), bf16),
            struct((count, slots, hidden), f32),
            struct((count, slots, hidden), f32),
        ],
        flops=2 * 3 * count * slots * width * hidden,
        bytes_accessed=2 * count * (2 * slots * width + 3 * width * hidden + 5 * slots * hidden),
    )(x, slot_gate, w_gate, w_up, w_down)


def expert_back_kernel(place_ref, *refs, fast):
    (x_a_ref, x_b_ref, g_ref, act_a_ref, act_b_ref, fac_a_ref, fac_b_ref, silu_a_ref, silu_b_ref) = refs[:9]
    w_gate_ref, w_up_ref, w_down_ref, back_ref, dots_ref = refs[9:14]
    grads, (gate_low_ref, up_low_ref) = refs[14:-2], refs[-2:]
    slots, width = g_ref.shape[1], g_ref.shape[2]
    hidden = w_gate_ref.shape[2]
    chunk = 256
    dots = jnp.zeros((slots, 1), f32)
    for first in range(0, hidden, chunk):
        cols = slice(first, first + chunk)
        active_grad = dot(g_ref[0], w_down_ref[0, :, cols])
        factor = jnp.concatenate([fac_a_ref[0, :, cols], fac_b_ref[0, :, cols]], axis=0)
        silu = jnp.concatenate([silu_a_ref[0, :, cols], silu_b_ref[0, :, cols]], axis=0)
        active = jnp.concatenate([act_a_ref[0, :, cols], act_b_ref[0, :, cols]], axis=0)
        gate_low_ref[:, cols] = (active_grad * factor).astype(bf16)
        up_low_ref[:, cols] = (active_grad * silu).astype(bf16)
        dots = dots + jnp.sum(active.astype(f32) * active_grad, axis=1, keepdims=True)
    dots_ref[0] = jnp.broadcast_to(dots, (slots, LANES))

    def columns(index, carry):
        cols = pl.ds(pl.multiple_of(index * chunk, chunk), chunk)
        back = dot_nt(gate_low_ref[...], w_gate_ref[0, cols, :]) + dot_nt(up_low_ref[...], w_up_ref[0, cols, :])
        back_ref[0, :, cols] = back.astype(bf16)
        return carry

    lax.fori_loop(0, width // chunk, columns, 0)

    def products(cols):
        x = jnp.concatenate([x_a_ref[0, :, cols], x_b_ref[0, :, cols]], axis=0)
        active = jnp.concatenate([act_a_ref[0], act_b_ref[0]], axis=0)
        yield 0, dot_tn(x, gate_low_ref[...]).astype(bf16)
        yield 1, dot_tn(x, up_low_ref[...]).astype(bf16)
        yield 2, dot_tn(g_ref[0, :, cols], active).astype(bf16)

    if fast:
        write_shards(place_ref, grads, products, width)
    else:

        def whole_columns(index, carry):
            cols = pl.ds(pl.multiple_of(index * chunk, chunk), chunk)
            for which, product in products(cols):
                grads[which][0, cols, :] = product
            return carry

        lax.fori_loop(0, width // chunk, whole_columns, 0)


def write_shards(place_ref, outs, products, width):
    send_a, keep_a, send_b, keep_b = outs
    x_bit, y_bit = place_ref[3], place_ref[4]
    shard = width // 4
    for dy in range(2):
        for dx in range(2):
            x, y = x_bit ^ dx, y_bit ^ dy
            cols = pl.ds(pl.multiple_of((y * 2 + x) * shard, shard), shard)
            for which, product in products(cols):
                side = product.shape[1] // 2
                (send_a if dx else keep_a)[0, which, y] = product[:, :side]
                (send_b if dy else keep_b)[0, which, x] = product[:, side:]


def run_experts_back(place, xs, g, acts, factors, silus, w_gate, w_up, w_down, first, count, fast):
    slots, width = g.shape[1], g.shape[2]
    hidden = w_gate.shape[2]
    part = slots // 2

    def taken(*shape):
        return pl.BlockSpec((1,) + shape, lambda e, p: (e + first, 0, 0))

    def given(*shape):
        zeros = (0,) * len(shape)
        return pl.BlockSpec((1,) + shape, lambda e, p: (e,) + zeros)

    if fast:
        grad_shapes = [(3, 2, width // 4, hidden // 2)] * 4
    else:
        grad_shapes = [(width, hidden)] * 3
    return call(
        lambda *refs: expert_back_kernel(*refs, fast=fast),
        (count,),
        1,
        [taken(part, width)] * 2
        + [taken(slots, width)]
        + [taken(part, hidden)] * 6
        + [taken(width, hidden)] * 3,
        [given(slots, width), given(slots, LANES)] + [given(*shape) for shape in grad_shapes],
        [struct((count, slots, width), bf16), struct((count, slots, LANES), f32)]
        + [struct((count,) + shape, bf16) for shape in grad_shapes],
        scratch=[pltpu.VMEM((slots, hidden), bf16)] * 2,
        flops=2 * 6 * count * slots * width * hidden,
        bytes_accessed=2 * count * (3 * slots * width + 6 * width * hidden + 5 * slots * hidden),
    )(place, *xs, g, *acts, *factors, *silus, w_gate, w_up, w_down)


def combine_half_kernel(rank_ref, slots_ref, out_ref):
    local_experts = slots_ref.shape[0]
    rows = jnp.concatenate([slots_ref[j, 0] for j in range(local_experts)], axis=0)
    out_ref[0] = dot_tn(chosen_of(hits_of(rank_ref[0], local_experts)), rows).astype(bf16)


def combine_half(rank, slots):
    rows, width = rank.shape[2], slots.shape[-1]
    local_experts = slots.shape[0]
    slots = slots.reshape(local_experts, COLS, CAPACITY, width)
    return call(
        combine_half_kernel,
        (COLS,),
        0,
        [
            pl.BlockSpec((1, 8, rows), lambda j: (j, 0, 0)),
            pl.BlockSpec((local_experts, 1, CAPACITY, width), lambda j: (0, j, 0, 0)),
        ],
        pl.BlockSpec((1, rows, width), lambda j: (j, 0, 0)),
        struct((COLS, rows, width), bf16),
        flops=2 * COLS * rows * width * 320,
        bytes_accessed=2 * COLS * (rows + 320) * width,
    )(rank, slots)


def combine_kernel(place_ref, rank_ref, *refs, pieces, mine):
    step = pl.program_id(0)
    parts, dots, rest = refs[:pieces], refs[pieces : 2 * pieces], refs[2 * pieces :]
    local_experts = sum(part.shape[0] for part in parts)
    hits = hits_of(rank_ref[0], local_experts)
    gathered = jnp.concatenate([part[j, 0] for part in parts for j in range(part.shape[0])], axis=0)
    summed = dot_tn(chosen_of(hits), gathered)
    column = [part[j, 0][:, 0:1] for part in dots for j in range(part.shape[0])]
    scattered = [
        jnp.sum(jnp.where(hit, value, 0.0), axis=0, keepdims=True) for hit, value in zip(hits, column)
    ]
    scattered.append(jnp.zeros((8 - local_experts, rank_ref.shape[2]), f32))
    if mine:
        arrived_ref, outs, dots_ref = rest[0], rest[1:-1], rest[-1]
        summed = (summed + arrived_ref[0].astype(f32)).astype(bf16)
        for index in range(COLS):

            @pl.when(step == index)
            def _(index=index):
                outs[index][...] = summed
    else:
        out_ref, dots_ref = rest
        out_ref[0] = summed.astype(bf16)
    dots_ref[0] = jnp.concatenate(scattered, axis=0)


def combine(place, rank, parts, dots, arrived=None):
    mine = arrived is not None
    rows, width = rank.shape[2], parts[0].shape[-1]

    def chip(step, p):
        return lax.rem(p[1] + step, COLS) if mine else step

    def member(step, p):
        return (p[0] if mine else 1 - p[0]) * COLS + chip(step, p)

    def slots_of(array):
        return pl.BlockSpec((array.shape[0], 1) + array.shape[2:], lambda j, p: (0, member(j, p), 0, 0))

    inputs = [part.reshape(part.shape[0], 2 * COLS, CAPACITY, part.shape[-1]) for part in list(parts) + list(dots)]
    in_specs = [pl.BlockSpec((1, 8, rows), lambda j, p: (member(j, p), 0, 0))] + [slots_of(item) for item in inputs]
    by_chip = pl.BlockSpec((1, rows, width), lambda j, p: (chip(j, p), 0, 0))
    if mine:
        inputs.append(arrived)
        in_specs.append(by_chip)
        out_specs, out_shape = [whole((rows, width))] * COLS, [struct((rows, width), bf16)] * COLS
    else:
        out_specs, out_shape = [by_chip], [struct((COLS, rows, width), bf16)]
    return call(
        lambda *refs: combine_kernel(*refs, pieces=len(parts), mine=mine),
        (COLS,),
        1,
        in_specs,
        out_specs + [pl.BlockSpec((1, 8, rows), lambda j, p: (chip(j, p), 0, 0))],
        out_shape + [struct((COLS, 8, rows), f32)],
        flops=2 * COLS * rows * width * 320,
        bytes_accessed=2 * COLS * (rows + 320) * width,
    )(place, rank, *inputs)


def add_cores_kernel(place_ref, a_ref, b_ref, from_b_ref, from_a_ref, *outs):
    step = pl.program_id(0)
    first = a_ref[0].astype(f32) + from_b_ref[0].astype(f32)
    second = b_ref[0].astype(f32) + from_a_ref[0].astype(f32)
    summed = jnp.where(place_ref[0] == 0, first, second).astype(bf16)
    for index in range(COLS):

        @pl.when(step == index)
        def _(index=index):
            outs[index][...] = summed


def add_cores(place, a, b, arrived_a, arrived_b):
    rows, width = a.shape[1], a.shape[2]
    spec = pl.BlockSpec((1, rows, width), lambda j, p: (lax.rem(p[1] + j, COLS), 0, 0))
    return call(
        add_cores_kernel,
        (COLS,),
        1,
        [spec] * 4,
        [whole((rows, width))] * COLS,
        [struct((rows, width), bf16)] * COLS,
        flops=COLS * rows * width * 3,
        bytes_accessed=2 * COLS * rows * width * 5,
    )(place, a, b, arrived_a, arrived_b)


def split_dot(dimension_numbers, values, exact):
    upper = values.astype(bf16)
    lower = (values - upper.astype(f32)).astype(bf16)
    return lax.dot_general(
        upper, exact, dimension_numbers, preferred_element_type=f32
    ) + lax.dot_general(lower, exact, dimension_numbers, preferred_element_type=f32)


def middle_back_kernel(place_ref, *refs):
    sums = refs[:COLS]
    (dots_ref, gates_a_ref, gates_b_ref, middle_a_ref, middle_b_ref, cot_ref, gain_ref, w_router_ref, w_out_ref) = refs[
        COLS : COLS + 9
    ]
    grad_ref, branch_ref, small_ref = refs[COLS + 9 : COLS + 12]
    attended = refs[COLS + 12 :]
    row, col = place_ref[0], place_ref[1]
    dots = dots_ref[...]
    gates = jnp.where(row == 0, gates_a_ref[...], gates_b_ref[...])
    logit_grad = dots - gates * jnp.sum(dots, axis=0, keepdims=True)
    middle = jnp.where(row == 0, middle_a_ref[...], middle_b_ref[...])
    inverse = lax.rsqrt(jnp.mean(middle * middle, axis=1, keepdims=True) + epsilon)
    unit = middle * inverse
    gain = gain_ref[...]
    normed = (unit * gain).astype(bf16)
    grad = sums[0][...].astype(f32)
    for ref in sums[1:]:
        grad = grad + ref[...].astype(f32)
    grad = grad + split_dot(TN, logit_grad, w_router_ref[...])
    small_ref[...] = split_dot((((1,), (0,)), ((), ())), logit_grad, normed)
    small_ref[7:8, :] = jnp.sum(grad * unit, axis=0, keepdims=True)
    scaled = grad * gain
    middle_grad = cot_ref[...].astype(f32) + inverse * (
        scaled - unit * jnp.mean(scaled * unit, axis=1, keepdims=True)
    )
    grad_ref[...] = middle_grad
    branch_grad = middle_grad.astype(bf16)
    branch_ref[...] = branch_grad
    for index, ref in enumerate(attended):
        line = row if index < COLS else 1 - row
        product = dot_nt(branch_grad, w_out_ref[line * COLS + lax.rem(col + index % COLS, COLS)])
        ref[:, 0:LANES] = product[:, 0:LANES].astype(bf16)
        ref[:, LANES : LANES + HEAD_DIM] = product[:, LANES:].astype(bf16)
        ref[:, LANES + HEAD_DIM :] = jnp.zeros((product.shape[0], HEAD_DIM), bf16)


def middle_back(place, sums, dots, gates, middles, cotangent, gain, w_router, w_out):
    rows, width = cotangent.shape
    args = tuple(sums) + (dots,) + tuple(gates) + tuple(middles) + (cotangent, gain, w_router, w_out)
    return call(
        middle_back_kernel,
        (1,),
        1,
        [whole(item.shape) for item in args],
        [whole((rows, width)), whole((rows, width)), whole(w_router.shape)] + [whole((rows, 2 * LANES))] * 2 * COLS,
        [struct((rows, width), f32), struct((rows, width), bf16), struct(w_router.shape, f32)]
        + [struct((rows, 2 * LANES), bf16)] * 2 * COLS,
        flops=2 * rows * width * width,
        bytes_accessed=2 * width * width + 16 * rows * width,
    )(place, *args)


def input_grad_kernel(place_ref, grads_ref, w_ref, tok_ref, *rest, mine):
    step = pl.program_id(0)
    product = dot(grads_ref[...], w_ref[...])
    resid = tok_ref[...].astype(f32)
    inverse = lax.rsqrt(jnp.mean(resid * resid, axis=1, keepdims=True) + epsilon)
    part = jnp.sum(product * (resid * inverse), axis=0, keepdims=True)
    gain_grad_ref = rest[-1]

    @pl.when(step == 0)
    def _():
        gain_grad_ref[...] = jnp.zeros_like(gain_grad_ref)

    gain_grad_ref[...] += jnp.broadcast_to(part, gain_grad_ref.shape)
    if mine:
        arrived_ref, outs = rest[0], rest[1:-1]
        summed = (product + arrived_ref[0].astype(f32)).astype(bf16)
        for index in range(COLS):

            @pl.when(step == index)
            def _(index=index):
                outs[index][...] = summed
    else:
        rest[0][0] = product.astype(bf16)


def input_grad(place, grads, w_stack, tokens, arrived=None):
    mine = arrived is not None
    rows, width = tokens.shape[0] // (2 * COLS), tokens.shape[1]

    def chip(step, p):
        return lax.rem(p[1] + step, COLS) if mine else step

    def member(step, p):
        return (p[0] if mine else 1 - p[0]) * COLS + chip(step, p)

    by_chip = pl.BlockSpec((1, rows, width), lambda j, p: (chip(j, p), 0, 0))
    inputs = [grads, w_stack, tokens]
    in_specs = [
        pl.BlockSpec((rows, 3 * LANES), lambda j, p: (member(j, p), 0)),
        whole(w_stack.shape),
        pl.BlockSpec((rows, width), lambda j, p: (member(j, p), 0)),
    ]
    if mine:
        inputs.append(arrived)
        in_specs.append(by_chip)
        out_specs, out_shape = [whole((rows, width))] * COLS, [struct((rows, width), bf16)] * COLS
    else:
        out_specs, out_shape = [by_chip], [struct((COLS, rows, width), bf16)]
    return call(
        lambda *refs: input_grad_kernel(*refs, mine=mine),
        (COLS,),
        1,
        in_specs,
        out_specs + [whole((8, width))],
        out_shape + [struct((8, width), f32)],
        flops=tokens.shape[0] * width * 3 * LANES,
        bytes_accessed=2 * tokens.shape[0] * width,
    )(place, *inputs)


def attention_weights_kernel(place_ref, *refs, fast):
    pieces, (normed_ref, projected_ref, att_a_ref, att_b_ref) = refs[:10], refs[10:14]
    outs, (block_ref, one_ref, two_ref) = refs[14:-3], refs[-3:]
    step = pl.program_id(0)
    rows = block_ref.shape[0]

    def store(ref):
        block_ref[...] = ref[...]

    fetch(step, place_ref, pieces, store)

    @pl.when(step == 0)
    def _():
        one_ref[...] = jnp.zeros_like(one_ref)
        two_ref[...] = jnp.zeros_like(two_ref)

    first_half = member_of(step, place_ref) < COLS
    attended = jnp.where(first_half, att_a_ref[...].astype(f32), att_b_ref[...].astype(f32)).astype(bf16)
    normed, projected = normed_ref[...], projected_ref[...]
    one_ref[...] += dot_tn(normed, projected[:, : 2 * LANES])
    two_ref[...] += dot_tn(block_ref[...], attended)
    two_ref[:, LANES:] += dot_tn(normed, projected[:, 2 * LANES :])

    @pl.when(step == pl.num_programs(0) - 1)
    def _():
        if fast:

            def products(cols):
                yield 0, jnp.concatenate([one_ref[cols, :], two_ref[cols, :]], axis=1).astype(bf16)

            write_shards(place_ref, outs, products, one_ref.shape[0])
        else:
            outs[0][:, 0 : 2 * LANES] = one_ref[...].astype(bf16)
            outs[0][:, 2 * LANES :] = two_ref[...].astype(bf16)


def attention_weights(place, pieces, normed, projected, att_a, att_b, fast):
    rows, width = pieces[0].shape

    def by_member(lanes):
        return pl.BlockSpec((rows, lanes), lambda j, p: (member_of(j, p), 0))

    def in_half(half):
        return pl.BlockSpec(
            (rows, 2 * LANES), lambda j, p: (jnp.clip(member_of(j, p) - half * COLS, 0, COLS - 1), 0)
        )

    if fast:
        shapes = [(1, 1, 2, width // 4, 2 * LANES)] * 4
    else:
        shapes = [(width, 4 * LANES)]
    return call(
        lambda *refs: attention_weights_kernel(*refs, fast=fast),
        (2 * COLS,),
        1,
        [whole((rows, width))] * 10 + [by_member(width), by_member(3 * LANES), in_half(0), in_half(1)],
        [whole(shape) for shape in shapes],
        [struct(shape, bf16) for shape in shapes],
        scratch=[
            pltpu.VMEM((rows, width), bf16),
            pltpu.VMEM((width, 2 * LANES), f32),
            pltpu.VMEM((width, 2 * LANES), f32),
        ],
        flops=2 * 2 * COLS * rows * width * 5 * LANES,
        bytes_accessed=4 * 2 * COLS * rows * width,
    )(place, *pieces, normed, projected, att_a, att_b)


def first_sum_kernel(place_ref, keep_a_ref, got_a_ref, keep_b_ref, got_b_ref, send_a_ref, held_a_ref, send_b_ref, held_b_ref):
    x_bit, y_bit = place_ref[3], place_ref[4]
    for bit, keep, got, send, held in (
        (y_bit, keep_a_ref, got_a_ref, send_a_ref, held_a_ref),
        (x_bit, keep_b_ref, got_b_ref, send_b_ref, held_b_ref),
    ):
        held[0, 0] = keep[0, 0, bit].astype(f32) + got[0, 0, bit].astype(f32)
        send[0, 0] = (keep[0, 0, 1 - bit].astype(f32) + got[0, 0, 1 - bit].astype(f32)).astype(bf16)


def first_sum(place, keep_a, got_a, keep_b, got_b):
    count, kinds, _, rows, cols = keep_a.shape
    taken = pl.BlockSpec((1, 1, 2, rows, cols), lambda e, k, p: (e, k, 0, 0, 0))
    given = pl.BlockSpec((1, 1, rows, cols), lambda e, k, p: (e, k, 0, 0))
    shape = (count, kinds, rows, cols)
    return call(
        first_sum_kernel,
        (count, kinds),
        1,
        [taken] * 4,
        [given] * 4,
        [struct(shape, bf16), struct(shape, f32), struct(shape, bf16), struct(shape, f32)],
        flops=4 * keep_a.size,
        bytes_accessed=14 * keep_a.size,
    )(place, keep_a, got_a, keep_b, got_b)


def last_sum_kernel(held_a_ref, got_a_ref, held_b_ref, got_b_ref, *rest):
    outs = rest[-3:]
    side = held_a_ref.shape[3]
    for which, out in enumerate(outs):
        out[0, :, :side] = held_a_ref[0, which] + got_a_ref[0, which].astype(f32)
        out[0, :, side:] = held_b_ref[0, which] + got_b_ref[0, which].astype(f32)


def last_sum(held_a, got_a, held_b, got_b, first, total, before):
    count, kinds, rows, cols = held_a.shape
    taken = pl.BlockSpec((1, kinds, rows, cols), lambda e: (e, 0, 0, 0))
    given = pl.BlockSpec((1, rows, 2 * cols), lambda e: (e + first, 0, 0))
    extra = list(before) if before else []
    return call(
        last_sum_kernel,
        (count,),
        0,
        [taken] * 4 + [pl.BlockSpec(memory_space=pl.ANY)] * len(extra),
        [given] * 3,
        [struct((total, rows, 2 * cols), f32)] * 3,
        flops=2 * held_a.size,
        bytes_accessed=20 * held_a.size,
        aliases={4 + i: i for i in range(len(extra))},
    )(held_a, got_a, held_b, got_b, *extra)


SWAP = [(0, 1), (1, 0)]


def after(value, *events):
    return lax.optimization_barrier((value,) + events)[0]


def line_pieces(block):
    two = lax.ppermute(block, "col", [(i, (i + 2) % COLS) for i in range(COLS)])
    before = lax.ppermute(block, "col", [(i, i + 1) for i in range(COLS - 1)])
    later = lax.ppermute(block, "col", [(i + 1, i) for i in range(COLS - 1)])
    relayed = lax.ppermute(two, "col", [(2, 3), (1, 0)])
    return [block, two, before, later, relayed]


def gather_group(block):
    mine = line_pieces(block)
    return mine + [lax.ppermute(piece, "row", SWAP) for piece in mine]


def scatter_line(blocks):
    return [blocks[0]] + [
        lax.ppermute(blocks[d], "col", [(i, (i + d) % COLS) for i in range(COLS)]) for d in range(1, COLS)
    ]


def flip(value, axis, bit, size):
    return lax.ppermute(value, axis, [(i, i ^ (1 << bit)) for i in range(size)])


def bits_of(size):
    return size.bit_length() - 1


def own_bit(axis, bit):
    return (lax.axis_index(axis) >> bit) & 1


def joined(mine, got, own):
    return jnp.where(own == 0, jnp.concatenate([mine, got]), jnp.concatenate([got, mine]))


def cube_gather(value, axis, size):
    value = value[None]
    for bit in range(bits_of(size)):
        value = joined(value, flip(value, axis, bit, size), own_bit(axis, bit))
    return value


def sum_group_then(value, sizes):
    for axis, bit in (("row", 0), ("col", 0), ("col", 1)):
        pair = value.reshape((2, value.shape[0] // 2) + value.shape[1:])
        own = own_bit(axis, bit)
        keep = lax.dynamic_index_in_dim(pair, own, 0, keepdims=False)
        send = lax.dynamic_index_in_dim(pair, 1 - own, 0, keepdims=False)
        value = keep + flip(send, axis, bit, sizes[axis])
    return value


def sum_dp(value, sizes):
    for bit in range(bits_of(sizes["dp"])):
        value = value + flip(value, "dp", bit, sizes["dp"])
    return value


def gather_rows_back(value, sizes):
    for axis, bit in (("col", 1), ("col", 0), ("row", 0)):
        value = joined(value, flip(value, axis, bit, sizes[axis]), own_bit(axis, bit))
    return value


def reduce_over_dp(value, size):
    count = bits_of(size)
    value = value.reshape(value.shape[:1] + (2,) * count + value.shape[2:])
    current = value
    for bit in range(count - 1, -1, -1):
        own = own_bit("dp", bit)
        keep = lax.dynamic_index_in_dim(current, own, 1, keepdims=False)
        send = lax.dynamic_index_in_dim(current, 1 - own, 1, keepdims=False).astype(bf16)
        current = keep.astype(f32) + flip(send, "dp", bit, size).astype(f32)
    return current


def layer(sizes):
    n_dp, n_row, n_col = sizes["dp"], sizes["row"], sizes["col"]
    members = n_row * n_col
    fast = n_dp == 4
    assert n_row == 2 and n_col == COLS and n_dp & (n_dp - 1) == 0

    def local(
        tokens, cotangent, routes, lengths, gain_attn, w_query, w_key, w_value, w_out,
        gain_moe, w_router, w_gate, w_up, w_down,
    ):
        rows, width = tokens.shape
        group = rows * members
        local_experts = w_gate.shape[0]
        row, col, dp = lax.axis_index("row"), lax.axis_index("col"), lax.axis_index("dp")
        place = jnp.stack([row, col, row * n_col + col, dp & 1, (dp >> 1) & 1]).astype(jnp.int32)
        gain_one = gain_attn.astype(f32)[None]
        gain_two = gain_moe.astype(f32)[None]

        tok_pieces = gather_group(tokens)
        share = rows // n_dp
        w_out_share = lax.dynamic_slice(w_out.T, (dp * share, 0), (share, width))
        w_out_all = cube_gather(w_out_share, "col", n_col)
        w_out_all = cube_gather(w_out_all, "dp", n_dp)
        w_out_all = cube_gather(w_out_all, "row", n_row)
        w_out_all = jnp.transpose(w_out_all, (0, 2, 1, 3, 4)).reshape(members, rows, width)
        route_rows = jnp.zeros((ROUTE_ROWS, 2 * LANES), bf16)
        route_rows = lax.dynamic_update_slice(route_rows, routes.T.astype(bf16), (0, 0))
        route_rows = cube_gather(cube_gather(route_rows, "col", n_col), "row", n_row)
        route_rows = route_rows.reshape(members, ROUTE_ROWS, 2 * LANES)
        cot_pieces = gather_group(after(cotangent, tok_pieces[1]))
        w_stack = jnp.concatenate([w_query.T, w_key.T, w_value.T, w_value.T], axis=0)

        ends = jnp.cumsum(lengths[0])
        starts = ends - lengths[0]
        position = jnp.arange(group, dtype=jnp.int32)
        segment = jnp.sum((position[:, None] >= ends[None, :]).astype(jnp.int32), axis=1)
        member = segment[:, None] == jnp.arange(starts.shape[0], dtype=jnp.int32)[None, :]
        start = jnp.sum(jnp.where(member, starts[None, :], 0), axis=1).astype(jnp.int32)
        frequency = rope_base ** (-2.0 * jnp.arange(HEAD_DIM // 2, dtype=f32) / HEAD_DIM)
        angle = (position - start).astype(f32)[:, None] * frequency[None, :]
        cosine = jnp.tile(jnp.cos(angle), (1, 4))
        sine = jnp.tile(jnp.sin(angle), (1, 4))

        query, key, value, normed_one, tok_all = project(place, tok_pieces, gain_one, w_stack, cosine, sine)
        w_router_rows = w_router.T.reshape(members, local_experts, width)
        w_router_rows = jnp.pad(w_router_rows, ((0, 0), (0, 8 - local_experts), (0, 0)))
        w_router_rows = w_router_rows.reshape(members * 8, width)
        halves = []
        for half in range(2):
            packed, attended, totals = attend(query, key, value, start[:, None], half)
            halves.append((gather_group(packed), attended, totals))

        slots = COLS * CAPACITY
        forward = []
        for half in range(2):
            x, slot_gate, rank, gate, middle, gates = middle_and_dispatch(
                place, halves[half][0], w_out_all, tok_all, route_rows, gain_two, w_router_rows, local_experts, half
            )
            x = x.reshape(local_experts, slots, width)
            slot_gate = slot_gate.reshape(local_experts, slots, LANES)
            forth, active, factor, silu = run_experts(x, slot_gate, w_gate, w_up, w_down)
            forward.append(
                dict(x=x, rank=rank, gate=gate, middle=middle, gates=gates, forth=forth, active=active, factor=factor, silu=silu)
            )

        def both(name):
            return [part[name] for part in forward]

        rank = jnp.concatenate(both("rank"), axis=0)
        g = grad_dispatch(place, cot_pieces, rank, jnp.concatenate(both("gate"), axis=0), local_experts)
        forth_a, forth_b = [combine_half(part["rank"], part["forth"]) for part in forward]
        forth_sums = add_cores(
            place, forth_a, forth_b,
            lax.ppermute(forth_a, "row", [(1, 0)]), lax.ppermute(forth_b, "row", [(0, 1)]),
        )
        forth_sums = scatter_line([after(forth_sums[0], g)] + list(forth_sums[1:]))

        g = g.reshape(local_experts, members * CAPACITY, width)
        cuts = [0, 1, 3, local_experts]
        runs = [
            run_experts_back(
                place, both("x"), g, both("active"), both("factor"), both("silu"), w_gate, w_up, w_down,
                first, last - first, fast,
            )
            for first, last in zip(cuts[:-1], cuts[1:])
        ]
        back_parts, dot_parts = [run[0] for run in runs], [run[1] for run in runs]
        back_other, dots_other = combine(place, rank, back_parts, dot_parts)
        arrived = lax.ppermute(back_other, "row", SWAP)
        *back_sums, dots_mine = combine(place, rank, back_parts, dot_parts, arrived)
        back_sums_sent = back_sums[1]
        back_sums = scatter_line(back_sums)
        dots = jnp.where(
            row == 0, jnp.concatenate([dots_mine, dots_other]), jnp.concatenate([dots_other, dots_mine])
        )
        dots = lax.all_to_all(dots, ("row", "col"), 0, 0, tiled=True).reshape(members * 8, rows)

        middle_grad, branch_grad, small, *attended_grad = middle_back(
            place, back_sums, dots, both("gates"), both("middle"), cotangent, gain_two, w_router_rows, w_out_all
        )
        pairs = [(r * n_col + c, r, c) for r in range(n_row) for c in range(n_col)]
        attended_got = [attended_grad[0]]
        for index in range(1, members):
            dr, dc = index // n_col, index % n_col
            moves = [(i, (r ^ dr) * n_col + (c + dc) % n_col) for i, r, c in pairs]
            attended_got.append(lax.ppermute(attended_grad[index], ("row", "col"), moves))
        branch_pieces = gather_group(after(branch_grad, attended_got[2]))
        small = sum_group_then(small, sizes)

        def start_sum(run, event):
            send_a, keep_a, send_b, keep_b = run
            got_a, got_b = flip(send_a, "dp", 0, n_dp), flip(send_b, "dp", 1, n_dp)
            keep_a, keep_b = after((keep_a, keep_b), event)
            send_a, held_a, send_b, held_b = first_sum(place, keep_a, got_a, keep_b, got_b)
            return held_a, flip(send_a, "dp", 1, n_dp), held_b, flip(send_b, "dp", 0, n_dp)

        started = []
        if fast:
            events = [back_sums_sent, branch_grad, branch_grad]
            started = [start_sum(run[2:], event) for run, event in zip(runs, events)]

        start_row = jnp.broadcast_to(start[None, :], (8, group))
        projected_grad = attend_back(
            place, attended_got, query, key, value, halves[0][2], halves[1][2], start_row, cosine, sine
        )
        in_other, gain_other = input_grad(place, projected_grad, w_stack, tok_all)
        arrived = lax.ppermute(in_other, "row", SWAP)
        *in_sums, gain_mine = input_grad(place, projected_grad, w_stack, tok_all, arrived)
        in_sums = scatter_line(in_sums)
        gain_part = (gain_other + gain_mine)[0].reshape(8, width // 8)
        gain_attn_grad = sum_group_then(gain_part, sizes)
        w_parts = attention_weights(
            place, branch_pieces, normed_one, projected_grad, halves[0][1], halves[1][1], fast
        )
        if fast:
            w_started = start_sum(w_parts, projected_grad)
        else:
            cut = w_parts[0].reshape(1, n_dp, width // n_dp, w_parts[0].shape[1])
            w_sum = reduce_over_dp(cut, n_dp)[0]

        mixed = middle_sum(row, both("middle"), after(forth_sums, projected_grad))

        small = gather_rows_back(sum_dp(after(small, projected_grad), sizes), sizes)
        w_router_grad = small.reshape(members, 8, width)[:, :local_experts]
        w_router_grad = w_router_grad.reshape(members * local_experts, width).T
        gain_moe_grad = small[7]
        gain_attn_grad = gather_rows_back(sum_dp(gain_attn_grad, sizes), sizes).reshape(width)

        normed_grad = sum(item.astype(f32) for item in in_sums)
        resid = tokens.astype(f32)
        inverse = lax.rsqrt(jnp.mean(resid * resid, axis=1, keepdims=True) + epsilon)
        unit = resid * inverse
        scaled = normed_grad * gain_one
        tokens_grad = middle_grad + inverse * (
            scaled - unit * jnp.mean(scaled * unit, axis=1, keepdims=True)
        )

        if fast:
            expert_grads = None
            for item, first, event in zip(started, cuts, (projected_grad, projected_grad, in_sums[0])):
                held = after((item[0], item[2]), event)
                expert_grads = last_sum(held[0], item[1], held[1], item[3], first, local_experts, expert_grads)
            held_a, got_a, held_b, got_b = [item[0, 0] for item in w_started]
            left = held_a + got_a.astype(f32)
            right = held_b + got_b.astype(f32)
            w_sum = jnp.concatenate([left, right], axis=1)
        else:
            expert_grads = []
            for which in range(3):
                parts = [run[2 + which] for run in runs]
                parts = [part.reshape(part.shape[0], n_dp, width // n_dp, part.shape[2]) for part in parts]
                expert_grads.append(jnp.concatenate([reduce_over_dp(part, n_dp) for part in parts], axis=0))
        w_gate_grad, w_up_grad, w_down_grad = expert_grads
        local_q, local_k = w_query.shape[1], w_key.shape[1]
        cut = local_q + local_k
        return (
            mixed, tokens_grad, gain_attn_grad, w_sum[:, :local_q], w_sum[:, local_q:cut],
            w_sum[:, cut + local_q :], w_sum[:, cut : cut + local_q],
            gain_moe_grad, w_router_grad, w_gate_grad, w_up_grad, w_down_grad,
        )

    return local


def middle_sum(row, middles, sums):
    middle = jnp.where(row == 0, middles[0], middles[1])
    return (middle + sum(item.astype(f32) for item in sums)).astype(bf16)


def solution(mesh):
    return jax.shard_map(
        layer(dict(mesh.shape)),
        mesh=mesh,
        in_specs=(
            P(("dp", "row", "col"), None),
            P(("dp", "row", "col"), None),
            P(("dp", "row", "col"), None),
            P("dp", None),
            P(),
            P(None, ("row", "col")),
            P(None, ("row", "col")),
            P(None, ("row", "col")),
            P(None, ("row", "col")),
            P(),
            P(),
            P(("row", "col"), None, None),
            P(("row", "col"), None, None),
            P(("row", "col"), None, None),
        ),
        out_specs=(
            P(("dp", "row", "col"), None),
            P(("dp", "row", "col"), None),
            P(),
            P("dp", ("row", "col")),
            P("dp", ("row", "col")),
            P("dp", ("row", "col")),
            P("dp", ("row", "col")),
            P(),
            P(),
            P(("row", "col"), "dp", None),
            P(("row", "col"), "dp", None),
            P(("row", "col"), "dp", None),
        ),
        check_vma=False,
    )
```

```python
import math

import jax
import jax.numpy as jnp
from jax import lax
from jax.experimental import pallas as pl
from jax.experimental.pallas import tpu as pltpu
from jax.sharding import PartitionSpec as P

HEAD_DIM = 64
EXPERTS = 40
TOP = 8
CAPACITY = 64
COLS = 4
LANES = 128
QUERY_BLOCK = 256
ROUTE_ROWS = 16

epsilon = 1e-06
rope_base = 10000.0
masked_score = -1e30
f32 = jnp.float32
bf16 = jnp.bfloat16
COST = 0.05
VMEM_LIMIT = 56 * 1024 * 1024

NT = (((1,), (1,)), ((), ()))
TN = (((0,), (0,)), ((), ()))


def dot(a, b):
    return jnp.dot(a, b, preferred_element_type=f32)


def dot_nt(a, b):
    return lax.dot_general(a, b, NT, preferred_element_type=f32)


def dot_tn(a, b):
    return lax.dot_general(a, b, TN, preferred_element_type=f32)


def lane_of(shape):
    return lax.broadcasted_iota(jnp.int32, shape, len(shape) - 1)


def call(
    kernel, grid, prefetch, in_specs, out_specs, out_shape, scratch=(), flops=0, bytes_accessed=0, aliases=None
):
    return pl.pallas_call(
        kernel,
        grid_spec=pltpu.PrefetchScalarGridSpec(
            num_scalar_prefetch=prefetch,
            grid=grid,
            in_specs=in_specs,
            out_specs=out_specs,
            scratch_shapes=list(scratch),
        ),
        out_shape=out_shape,
        input_output_aliases=aliases or {},
        compiler_params=pltpu.CompilerParams(
            vmem_limit_bytes=VMEM_LIMIT, dimension_semantics=("arbitrary",) * len(grid)
        ),
        cost_estimate=pl.CostEstimate(
            flops=int(flops * COST), bytes_accessed=int(bytes_accessed * COST), transcendentals=0
        ),
    )


def whole(shape):
    zeros = (0,) * len(shape)
    return pl.BlockSpec(shape, lambda *_: zeros)


def struct(shape, dtype):
    return jax.ShapeDtypeStruct(shape, dtype)


def turn_within_heads(values, sign):
    lane = lane_of(values.shape) % HEAD_DIM
    ahead = pltpu.roll(values, LANES - HEAD_DIM // 2, 1)
    behind = pltpu.roll(values, HEAD_DIM // 2, 1)
    return jnp.where(lane < HEAD_DIM // 2, -sign * ahead, sign * behind)


def project_kernel(
    tok_ref, gain_ref, w_ref, cos_ref, sin_ref, query_ref, key_ref, value_ref, normed_ref
):
    resid = tok_ref[...].astype(f32)
    inverse = lax.rsqrt(jnp.mean(resid * resid, axis=1, keepdims=True) + epsilon)
    normed = (resid * inverse * gain_ref[...]).astype(bf16)
    normed_ref[...] = normed
    raw = dot_nt(normed, w_ref[...])
    cosine, sine = cos_ref[...], sin_ref[...]

    def rot(values):
        return (values * cosine + turn_within_heads(values, 1.0) * sine).astype(bf16).astype(f32)

    first = rot(raw[:, :LANES])
    second = rot(raw[:, LANES : 2 * LANES])
    low = lane_of(first.shape) < HEAD_DIM
    scale = 1.0 / math.sqrt(HEAD_DIM)
    query_ref[0] = jnp.where(low, first * scale, 0.0).astype(bf16)
    query_ref[1] = jnp.where(low, 0.0, first * scale).astype(bf16)
    query_ref[2] = jnp.where(low, second * scale, 0.0).astype(bf16)
    key_ref[...] = jnp.where(low, pltpu.roll(second, HEAD_DIM, 1), second).astype(bf16)
    value_ref[...] = raw[:, 2 * LANES :].astype(bf16)


def project(tokens, gain, w_stack, cosine, sine):
    total, width = tokens.shape
    rows = 512
    lanes = pl.BlockSpec((rows, LANES), lambda j: (j, 0))
    wide = pl.BlockSpec((rows, width), lambda j: (j, 0))
    return call(
        project_kernel,
        (total // rows,),
        0,
        [wide, whole((1, width)), whole(w_stack.shape), lanes, lanes],
        [pl.BlockSpec((3, rows, LANES), lambda j: (0, j, 0)), lanes, lanes, wide],
        [
            struct((3, total, LANES), bf16),
            struct((total, LANES), bf16),
            struct((total, LANES), bf16),
            struct((total, width), bf16),
        ],
        flops=2 * total * width * w_stack.shape[0],
        bytes_accessed=6 * total * width,
    )(tokens, gain, w_stack, cosine, sine)


def attend_kernel(query_ref, key_ref, value_ref, start_ref, packed_ref, plain_ref, total_ref, out_ref):
    blocks = query_ref.shape[1] // QUERY_BLOCK
    block = pl.program_id(0)
    for index in range(blocks):

        @pl.when(block == index)
        def _(index=index):
            rows = pl.ds(index * QUERY_BLOCK, QUERY_BLOCK)
            span = (index + 1) * QUERY_BLOCK
            row = index * QUERY_BLOCK + lax.broadcasted_iota(jnp.int32, (QUERY_BLOCK, span), 0)
            column = lane_of((QUERY_BLOCK, span))
            allowed = (column <= row) & (column >= start_ref[rows, :])

            def head(number, carry):
                scores = dot_nt(query_ref[number, rows, :], key_ref[0:span, :])
                scores = jnp.where(allowed, scores, masked_score)
                peak = jnp.max(scores, axis=1, keepdims=True)
                weights = jnp.exp(scores - peak)
                summed = jnp.sum(weights, axis=1, keepdims=True)
                probs = (weights * (1.0 / summed)).astype(bf16)
                out_ref[number] = dot(probs, value_ref[0:span, :])
                total = jnp.broadcast_to(peak + jnp.log(summed), (QUERY_BLOCK, LANES))
                total_ref[number, :, rows] = jnp.transpose(total)[0:8, :]
                return carry

            lax.fori_loop(0, 3, head, 0)
            low = lane_of((QUERY_BLOCK, LANES)) < HEAD_DIM
            one, two, three = out_ref[0], out_ref[1], out_ref[2]
            pair = jnp.where(low, one, two).astype(bf16)
            plain_ref[rows, 0:LANES] = pair
            plain_ref[rows, LANES : 2 * LANES] = jnp.where(low, three, 0.0).astype(bf16)
            if index < blocks // 2:
                packed_ref[rows, 0:LANES] = pair
                packed_ref[rows, LANES : 2 * LANES] = three.astype(bf16)
            else:
                back = pl.ds((index - blocks // 2) * QUERY_BLOCK, QUERY_BLOCK)
                before = packed_ref[back, LANES : 2 * LANES].astype(f32)
                packed_ref[back, LANES : 2 * LANES] = jnp.where(low, before, one).astype(bf16)
                packed_ref[back, 2 * LANES : 3 * LANES] = jnp.where(low, two, three).astype(bf16)


def attend(query, key, value, start):
    total = key.shape[0]
    return call(
        attend_kernel,
        (total // QUERY_BLOCK,),
        0,
        [whole(query.shape), whole(key.shape), whole(value.shape), whole(start.shape)],
        [whole((total // 2, 3 * LANES)), whole((total, 2 * LANES)), whole((3, 8, total))],
        [
            struct((total // 2, 3 * LANES), bf16),
            struct((total, 2 * LANES), bf16),
            struct((3, 8, total), f32),
        ],
        scratch=[pltpu.VMEM((3, QUERY_BLOCK, LANES), f32)],
        flops=8 * 3 * total * total * LANES,
        bytes_accessed=8 * total * LANES * 2,
    )(query, key, value, start)


def attend_back_kernel(
    query_ref, key_ref, value_ref, grad_ref, total_ref, start_ref, cos_ref, sin_ref,
    out_ref, query_grad_ref, key_grad_ref, value_grad_ref
):
    blocks = query_ref.shape[1] // QUERY_BLOCK
    block = pl.program_id(0)
    scale = 1.0 / math.sqrt(HEAD_DIM)

    @pl.when(block == 0)
    def _():
        key_grad_ref[...] = jnp.zeros_like(key_grad_ref)
        value_grad_ref[...] = jnp.zeros_like(value_grad_ref)

    def back(values, cosine, sine):
        return values * cosine + turn_within_heads(values * sine, -1.0)

    for index in range(blocks):

        @pl.when(block == index)
        def _(index=index):
            rows = pl.ds(index * QUERY_BLOCK, QUERY_BLOCK)
            span = (index + 1) * QUERY_BLOCK
            row = index * QUERY_BLOCK + lane_of((span, QUERY_BLOCK))
            column = lax.broadcasted_iota(jnp.int32, (span, QUERY_BLOCK), 0)
            allowed = (column <= row) & (column >= start_ref[0:1, rows])
            low = lane_of((QUERY_BLOCK, LANES)) < HEAD_DIM

            def head(number, carry):
                query = query_ref[number, rows, :]
                tile = pl.multiple_of((number // 2) * LANES, LANES)
                upstream = grad_ref[rows, pl.ds(tile, LANES)].astype(f32)
                keep = low == (number != 1)
                upstream = jnp.where(keep, upstream, 0.0).astype(bf16)
                scores = dot_nt(key_ref[0:span, :], query)
                probs = jnp.exp(scores - total_ref[number, 0:1, rows])
                probs = jnp.where(allowed, probs, 0.0)
                prob_grad = dot_nt(value_ref[0:span, :], upstream)
                row_dot = jnp.sum(probs * prob_grad, axis=0, keepdims=True)
                score_grad = (probs * (prob_grad - row_dot)).astype(bf16)
                key_grad_ref[0:span, :] += dot(score_grad, query)
                value_grad_ref[0:span, :] += dot(probs.astype(bf16), upstream)
                query_grad_ref[number] = dot_tn(score_grad, key_ref[0:span, :]) * scale
                return carry

            lax.fori_loop(0, 3, head, 0)
            cosine, sine = cos_ref[rows, :], sin_ref[rows, :]
            pair = jnp.where(low, query_grad_ref[0], query_grad_ref[1])
            out_ref[rows, 0:LANES] = back(pair, cosine, sine).astype(bf16)
            out_ref[rows, LANES : 2 * LANES] = back(query_grad_ref[2], cosine, sine).astype(bf16)

    @pl.when(block == blocks - 1)
    def _():
        low = lane_of(key_grad_ref.shape) < HEAD_DIM
        key_grad = key_grad_ref[...]
        key_grad = key_grad + pltpu.roll(key_grad, HEAD_DIM, 1)
        key_grad = back(key_grad, cos_ref[...], sin_ref[...])
        before = out_ref[:, LANES : 2 * LANES].astype(f32)
        out_ref[:, LANES : 2 * LANES] = jnp.where(low, before, key_grad).astype(bf16)
        value_grad = value_grad_ref[...]
        value_grad = value_grad + pltpu.roll(value_grad, HEAD_DIM, 1)
        out_ref[:, 2 * LANES : 3 * LANES] = jnp.where(low, 0.0, value_grad).astype(bf16)


def attend_back(query, key, value, grad, totals, start, cosine, sine):
    total = key.shape[0]
    args = (query, key, value, grad, totals, start, cosine, sine)
    return call(
        attend_back_kernel,
        (total // QUERY_BLOCK,),
        0,
        [whole(item.shape) for item in args],
        whole((total, 3 * LANES)),
        struct((total, 3 * LANES), bf16),
        scratch=[
            pltpu.VMEM((3, QUERY_BLOCK, LANES), f32),
            pltpu.VMEM((total, LANES), f32),
            pltpu.VMEM((total, LANES), f32),
        ],
        flops=16 * 3 * total * total * LANES,
        bytes_accessed=14 * total * LANES * 2,
    )(*args)


def branch_operand(refs):
    rows = refs.shape[1]
    low = lane_of((rows, LANES)) < HEAD_DIM
    pairs, thirds = [], []
    for member in range(refs.shape[0]):
        one = refs[member, :, 0:LANES]
        mid = refs[member, :, LANES : 2 * LANES].astype(f32)
        end = refs[member, :, 2 * LANES : 3 * LANES].astype(f32)
        mid_turned = pltpu.roll(mid, HEAD_DIM, 1)
        end_turned = pltpu.roll(end, HEAD_DIM, 1)
        late = jnp.where(low, mid_turned, end_turned).astype(bf16)
        pairs.append(jnp.concatenate([one, late], axis=0))
        thirds.append((mid, end_turned))
    for member in range(0, refs.shape[0], 2):
        tops = []
        for which in range(2):
            left, right = thirds[member][which], thirds[member + 1][which]
            tops.append(jnp.where(low, left, pltpu.roll(right, HEAD_DIM, 1)).astype(bf16))
        pairs.append(jnp.concatenate(tops, axis=0))
    return jnp.concatenate(pairs, axis=1)


def hits_of(rank, local_experts):
    place = lax.broadcasted_iota(jnp.int32, (CAPACITY, rank.shape[1]), 0).astype(f32)
    return [place == rank[j : j + 1, :] for j in range(local_experts)]


def chosen_of(hits):
    return jnp.concatenate([jnp.where(hit, 1.0, 0.0).astype(bf16) for hit in hits], axis=0)


def middle_kernel(
    place_ref, att_ref, w_out_ref, tok_a_ref, tok_b_ref, cot_a_ref, cot_b_ref, routes_a_ref, routes_b_ref,
    gain_ref, w_router_ref, after_ref,
    x_ref, g_ref, slot_gate_ref, rank_ref, middle_ref, gates_own_ref, gates_ref, ranks_ref
):
    step = pl.program_id(0)
    member = place_ref[2]
    cols = pl.num_programs(0)
    rows = tok_a_ref.shape[0]
    local_experts = x_ref.shape[0]
    members = w_out_ref.shape[0]
    right = [w_out_ref[source, 0:LANES] for source in range(members)]
    right += [w_out_ref[source, LANES:] for source in range(members)]
    branch = dot(branch_operand(att_ref), jnp.concatenate(right, axis=0))
    for half in range(2):
        tok_ref, cot_ref, routes_ref = (
            (tok_a_ref, cot_a_ref, routes_a_ref), (tok_b_ref, cot_b_ref, routes_b_ref)
        )[half]
        middle = tok_ref[...].astype(f32) + branch[half * rows : (half + 1) * rows]
        inverse = lax.rsqrt(jnp.mean(middle * middle, axis=1, keepdims=True) + epsilon)
        normed = (middle * inverse * gain_ref[...]).astype(bf16)
        logits = dot_nt(w_router_ref[...], normed)
        padded = logits.shape[0]
        slot = lax.broadcasted_iota(jnp.int32, (padded, rows), 0)
        expert = (slot // 8) * local_experts + slot % 8
        expert = jnp.where(slot % 8 < local_experts, expert, -1).astype(f32)
        routes = routes_ref[0].astype(f32)
        named = expert == routes[0:1, 0:rows]
        for k in range(1, TOP):
            named = named | (expert == routes[k : k + 1, 0:rows])
        peak = jnp.max(jnp.where(named, logits, masked_score), axis=0, keepdims=True)
        weights = jnp.where(named, jnp.exp(logits - peak), 0.0)
        gates = weights / jnp.sum(weights, axis=0, keepdims=True)
        gates_ref[...] = gates
        ranks_ref[...] = jnp.where(named, dot(named.astype(f32).astype(bf16), after_ref[...]), -1.0)
        here = pl.ds(pl.multiple_of(member * 8, 8), 8)
        gate, rank = gates_ref[here, :], ranks_ref[here, :]
        rank_ref[half, 0] = rank
        hits = hits_of(rank, local_experts)
        slot_gate = jnp.concatenate(
            [jnp.sum(jnp.where(hit, gate[j : j + 1, :], 0.0), axis=1, keepdims=True) for j, hit in enumerate(hits)],
            axis=0,
        )
        chosen = chosen_of(hits)
        picked = dot(chosen, normed).astype(bf16)
        grads = (dot(chosen, cot_ref[...]) * slot_gate).astype(bf16)
        spread = jnp.broadcast_to(slot_gate, (slot_gate.shape[0], LANES))
        for j in range(local_experts):
            part = slice(j * CAPACITY, (j + 1) * CAPACITY)
            x_ref[j, half, 0] = picked[part]
            g_ref[j, half, 0] = grads[part]
            slot_gate_ref[j, half, 0] = spread[part]

        @pl.when(member == half * cols + step)
        def _(middle=middle, gates=gates):
            middle_ref[...] = middle
            gates_own_ref[...] = gates


def middle_and_dispatch(place, att, w_out, tokens, cotangents, routes, gain, w_router, local_experts):
    width = tokens.shape[1]
    half = COLS
    rows = tokens.shape[0] // (2 * half)
    padded = w_router.shape[0]
    after = (jnp.arange(rows)[:, None] < jnp.arange(rows)[None, :]).astype(bf16)
    slot_shape = (local_experts, 2, half, CAPACITY)
    early = pl.BlockSpec((rows, width), lambda i, p: (i, 0))
    late = pl.BlockSpec((rows, width), lambda i, p: (i + half, 0))
    routes_shape = (1,) + routes.shape[1:]
    return call(
        middle_kernel,
        (half,),
        1,
        [
            pl.BlockSpec((att.shape[0], rows, 3 * LANES), lambda i, p: (0, i, 0)),
            whole(w_out.shape),
            early,
            late,
            early,
            late,
            pl.BlockSpec(routes_shape, lambda i, p: (i, 0, 0)),
            pl.BlockSpec(routes_shape, lambda i, p: (i + half, 0, 0)),
            whole((1, width)),
            whole(w_router.shape),
            whole((rows, rows)),
        ],
        [
            pl.BlockSpec((local_experts, 2, 1, CAPACITY, width), lambda i, p: (0, 0, i, 0, 0)),
            pl.BlockSpec((local_experts, 2, 1, CAPACITY, width), lambda i, p: (0, 0, i, 0, 0)),
            pl.BlockSpec((local_experts, 2, 1, CAPACITY, LANES), lambda i, p: (0, 0, i, 0, 0)),
            pl.BlockSpec((2, 1, 8, rows), lambda i, p: (0, i, 0, 0)),
            whole((rows, width)),
            whole((padded, rows)),
        ],
        [
            struct(slot_shape + (width,), bf16),
            struct(slot_shape + (width,), bf16),
            struct(slot_shape + (LANES,), f32),
            struct((2, half, 8, rows), f32),
            struct((rows, width), f32),
            struct((padded, rows), f32),
        ],
        scratch=[pltpu.VMEM((padded, rows), f32), pltpu.VMEM((padded, rows), f32)],
        flops=2 * 2 * half * rows * width * (width + 2 * local_experts * CAPACITY),
        bytes_accessed=2 * 2 * half * rows * width * 5,
    )(place, att, w_out, tokens, tokens, cotangents, cotangents, routes, routes, gain, w_router, after)


def expert_kernel(
    x_ref, gate_ref, w_gate_ref, w_up_ref, w_down_ref, forth_ref, active_ref, factor_ref, silu_ref
):
    width, hidden = w_gate_ref.shape[1], w_gate_ref.shape[2]
    chunk = 256
    for first in range(0, hidden, chunk):
        cols = slice(first, first + chunk)
        gate_pre = dot(x_ref[0], w_gate_ref[0, :, cols])
        up_pre = dot(x_ref[0], w_up_ref[0, :, cols])
        sig = 1.0 / (1.0 + jnp.exp(-gate_pre))
        silu = gate_pre * sig
        silu_ref[0, :, cols] = silu
        factor_ref[0, :, cols] = up_pre * sig * (1.0 + gate_pre * (1.0 - sig))
        active_ref[0, :, cols] = (silu * up_pre).astype(bf16)

    def columns(index, carry):
        cols = pl.ds(pl.multiple_of(index * chunk, chunk), chunk)
        produced = dot_nt(active_ref[0], w_down_ref[0, cols, :]).astype(bf16).astype(f32)
        forth_ref[0, :, cols] = (produced * gate_ref[0, :, 0:1]).astype(bf16)
        return carry

    lax.fori_loop(0, width // chunk, columns, 0)


def run_experts(x, slot_gate, w_gate, w_up, w_down):
    count, slots, width = x.shape
    hidden = w_gate.shape[2]

    def per_expert(*shape):
        return pl.BlockSpec((1,) + shape, lambda e: (e, 0, 0))

    return call(
        expert_kernel,
        (count,),
        0,
        [per_expert(slots, width), per_expert(slots, LANES)] + [per_expert(width, hidden)] * 3,
        [per_expert(slots, width)] + [per_expert(slots, hidden)] * 3,
        [
            struct((count, slots, width), bf16),
            struct((count, slots, hidden), bf16),
            struct((count, slots, hidden), f32),
            struct((count, slots, hidden), f32),
        ],
        flops=2 * 3 * count * slots * width * hidden,
        bytes_accessed=2 * count * (2 * slots * width + 3 * width * hidden + 5 * slots * hidden),
    )(x, slot_gate, w_gate, w_up, w_down)


def expert_back_kernel(place_ref, *refs, fast):
    x_ref, g_ref, active_ref, factor_ref, silu_ref = refs[:5]
    w_gate_ref, w_up_ref, w_down_ref, back_ref, dots_ref = refs[5:10]
    grads, (gate_low_ref, up_low_ref) = refs[10:-2], refs[-2:]
    slots, width = g_ref.shape[1], g_ref.shape[2]
    hidden = w_gate_ref.shape[2]
    chunk = 256
    dots = jnp.zeros((slots, 1), f32)
    for first in range(0, hidden, chunk):
        cols = slice(first, first + chunk)
        active_grad = dot(g_ref[0], w_down_ref[0, :, cols])
        gate_low_ref[:, cols] = (active_grad * factor_ref[0, :, cols]).astype(bf16)
        up_low_ref[:, cols] = (active_grad * silu_ref[0, :, cols]).astype(bf16)
        dots = dots + jnp.sum(active_ref[0, :, cols].astype(f32) * active_grad, axis=1, keepdims=True)
    dots_ref[0] = jnp.broadcast_to(dots, (slots, LANES))

    def columns(index, carry):
        cols = pl.ds(pl.multiple_of(index * chunk, chunk), chunk)
        back = dot_nt(gate_low_ref[...], w_gate_ref[0, cols, :]) + dot_nt(up_low_ref[...], w_up_ref[0, cols, :])
        back_ref[0, :, cols] = back.astype(bf16)
        return carry

    lax.fori_loop(0, width // chunk, columns, 0)

    def products(cols):
        x = x_ref[0, :, cols]
        yield 0, dot_tn(x, gate_low_ref[...]).astype(bf16)
        yield 1, dot_tn(x, up_low_ref[...]).astype(bf16)
        yield 2, dot_tn(g_ref[0, :, cols], active_ref[0]).astype(bf16)

    if fast:
        write_shards(place_ref, grads, products, width)
    else:

        def whole_columns(index, carry):
            cols = pl.ds(pl.multiple_of(index * chunk, chunk), chunk)
            for which, product in products(cols):
                grads[which][0, cols, :] = product
            return carry

        lax.fori_loop(0, width // chunk, whole_columns, 0)


def write_shards(place_ref, outs, products, width):
    send_a, keep_a, send_b, keep_b = outs
    x_bit, y_bit = place_ref[3], place_ref[4]
    shard = width // 4
    for dy in range(2):
        for dx in range(2):
            x, y = x_bit ^ dx, y_bit ^ dy
            cols = pl.ds(pl.multiple_of((y * 2 + x) * shard, shard), shard)
            for which, product in products(cols):
                side = product.shape[1] // 2
                (send_a if dx else keep_a)[0, which, y] = product[:, :side]
                (send_b if dy else keep_b)[0, which, x] = product[:, side:]


def run_experts_back(place, x, g, active, factor, silu, w_gate, w_up, w_down, first, count, fast):
    slots, width = g.shape[1], g.shape[2]
    hidden = w_gate.shape[2]

    def taken(*shape):
        return pl.BlockSpec((1,) + shape, lambda e, p: (e + first, 0, 0))

    def given(*shape):
        zeros = (0,) * len(shape)
        return pl.BlockSpec((1,) + shape, lambda e, p: (e,) + zeros)

    if fast:
        grad_shapes = [(3, 2, width // 4, hidden // 2)] * 4
    else:
        grad_shapes = [(width, hidden)] * 3
    return call(
        lambda *refs: expert_back_kernel(*refs, fast=fast),
        (count,),
        1,
        [taken(slots, width)] * 2 + [taken(slots, hidden)] * 3 + [taken(width, hidden)] * 3,
        [given(slots, width), given(slots, LANES)] + [given(*shape) for shape in grad_shapes],
        [struct((count, slots, width), bf16), struct((count, slots, LANES), f32)]
        + [struct((count,) + shape, bf16) for shape in grad_shapes],
        scratch=[pltpu.VMEM((slots, hidden), bf16)] * 2,
        flops=2 * 6 * count * slots * width * hidden,
        bytes_accessed=2 * count * (3 * slots * width + 6 * width * hidden + 5 * slots * hidden),
    )(place, x, g, active, factor, silu, w_gate, w_up, w_down)


def combine_kernel(place_ref, rank_ref, *refs, pieces, with_dots, mine):
    parts, rest = refs[:pieces], refs[pieces:]
    local_experts = sum(part.shape[0] for part in parts)
    hits = hits_of(rank_ref[0], local_experts)
    gathered = jnp.concatenate([part[j, 0] for part in parts for j in range(part.shape[0])], axis=0)
    summed = dot_tn(chosen_of(hits), gathered)
    if with_dots:
        dots, rest = rest[:pieces], rest[pieces:]
        column = [part[j, 0][:, 0:1] for part in dots for j in range(part.shape[0])]
        scattered = [
            jnp.sum(jnp.where(hit, value, 0.0), axis=0, keepdims=True) for hit, value in zip(hits, column)
        ]
        scattered.append(jnp.zeros((8 - local_experts, rank_ref.shape[2]), f32))
        rest[-1][0] = jnp.concatenate(scattered, axis=0)
    if mine:
        summed = summed + rest[0][0].astype(f32)
        rest = rest[1:]
    rest[0][0] = summed.astype(bf16)


def combine(place, rank, parts, dots=None, arrived=None):
    mine = arrived is not None
    rows, width = rank.shape[2], parts[0].shape[-1]

    def member(step, p):
        return (p[0] if mine else 1 - p[0]) * COLS + step

    def slots_of(array):
        return pl.BlockSpec((array.shape[0], 1) + array.shape[2:], lambda j, p: (0, member(j, p), 0, 0))

    inputs = [
        part.reshape(part.shape[0], 2 * COLS, CAPACITY, part.shape[-1]) for part in list(parts) + list(dots or [])
    ]
    in_specs = [pl.BlockSpec((1, 8, rows), lambda j, p: (member(j, p), 0, 0))] + [slots_of(item) for item in inputs]
    by_chip = pl.BlockSpec((1, rows, width), lambda j, p: (j, 0, 0))
    if mine:
        inputs.append(arrived)
        in_specs.append(by_chip)
    out_specs, out_shape = [by_chip], [struct((COLS, rows, width), bf16)]
    if dots:
        out_specs.append(pl.BlockSpec((1, 8, rows), lambda j, p: (j, 0, 0)))
        out_shape.append(struct((COLS, 8, rows), f32))
    return call(
        lambda *refs: combine_kernel(*refs, pieces=len(parts), with_dots=bool(dots), mine=mine),
        (COLS,),
        1,
        in_specs,
        out_specs,
        out_shape,
        flops=2 * COLS * rows * width * 320,
        bytes_accessed=2 * COLS * (rows + 320) * width,
    )(place, rank, *inputs)


def split_dot(dimension_numbers, values, exact):
    upper = values.astype(bf16)
    lower = (values - upper.astype(f32)).astype(bf16)
    return lax.dot_general(
        upper, exact, dimension_numbers, preferred_element_type=f32
    ) + lax.dot_general(lower, exact, dimension_numbers, preferred_element_type=f32)


def middle_back_kernel(
    sums_ref, dots_ref, gates_ref, middle_ref, cot_ref, gain_ref, w_router_ref, w_out_ref,
    grad_ref, branch_ref, attended_ref, small_ref
):
    dots, gates = dots_ref[...], gates_ref[...]
    logit_grad = dots - gates * jnp.sum(dots, axis=0, keepdims=True)
    middle = middle_ref[...]
    inverse = lax.rsqrt(jnp.mean(middle * middle, axis=1, keepdims=True) + epsilon)
    unit = middle * inverse
    gain = gain_ref[...]
    normed = (unit * gain).astype(bf16)
    grad = sums_ref[0].astype(f32)
    for index in range(1, sums_ref.shape[0]):
        grad = grad + sums_ref[index].astype(f32)
    grad = grad + split_dot(TN, logit_grad, w_router_ref[...])
    small_ref[...] = split_dot((((1,), (0,)), ((), ())), logit_grad, normed)
    small_ref[7:8, :] = jnp.sum(grad * unit, axis=0, keepdims=True)
    scaled = grad * gain
    middle_grad = cot_ref[...].astype(f32) + inverse * (
        scaled - unit * jnp.mean(scaled * unit, axis=1, keepdims=True)
    )
    grad_ref[...] = middle_grad
    branch_grad = middle_grad.astype(bf16)
    branch_ref[...] = branch_grad
    for member in range(w_out_ref.shape[0]):
        product = dot_nt(branch_grad, w_out_ref[member])
        attended_ref[member, :, 0:LANES] = product[:, 0:LANES].astype(bf16)
        attended_ref[member, :, LANES : LANES + HEAD_DIM] = product[:, LANES:].astype(bf16)
        attended_ref[member, :, LANES + HEAD_DIM :] = jnp.zeros((product.shape[0], HEAD_DIM), bf16)


def middle_back(sums, dots, gates, middle, cotangent, gain, w_router, w_out):
    rows, width = middle.shape
    members = w_out.shape[0]
    args = (sums, dots, gates, middle, cotangent, gain, w_router, w_out)
    return call(
        middle_back_kernel,
        (1,),
        0,
        [whole(item.shape) for item in args],
        [
            whole((rows, width)),
            whole((rows, width)),
            whole((members, rows, 2 * LANES)),
            whole(w_router.shape),
        ],
        [
            struct((rows, width), f32),
            struct((rows, width), bf16),
            struct((members, rows, 2 * LANES), bf16),
            struct(w_router.shape, f32),
        ],
        flops=2 * rows * width * width,
        bytes_accessed=2 * width * width + 16 * rows * width,
    )(*args)


def input_grad_kernel(grads_ref, w_ref, tok_ref, middle_grad_ref, gain_ref, out_ref, sum_ref):
    step = pl.program_id(0)

    @pl.when(step == 0)
    def _():
        sum_ref[...] = jnp.zeros_like(sum_ref)

    right = jnp.concatenate([w_ref[0], w_ref[0, 4 * HEAD_DIM :]], axis=0)
    sum_ref[...] += dot(grads_ref[0], right)

    @pl.when(step == pl.num_programs(0) - 1)
    def _():
        resid = tok_ref[...].astype(f32)
        inverse = lax.rsqrt(jnp.mean(resid * resid, axis=1, keepdims=True) + epsilon)
        unit = resid * inverse
        scaled = sum_ref[...] * gain_ref[...]
        out_ref[...] = middle_grad_ref[...] + inverse * (
            scaled - unit * jnp.mean(scaled * unit, axis=1, keepdims=True)
        )


def input_grad(grads, w_all, tokens, middle_grad, gain):
    rows, width = tokens.shape
    members, lanes = grads.shape[0], grads.shape[2]
    return call(
        input_grad_kernel,
        (members,),
        0,
        [
            pl.BlockSpec((1, rows, lanes), lambda m: (m, 0, 0)),
            pl.BlockSpec((1,) + w_all.shape[1:], lambda m: (m, 0, 0)),
            whole((rows, width)),
            whole((rows, width)),
            whole((1, width)),
        ],
        whole((rows, width)),
        struct((rows, width), f32),
        scratch=[pltpu.VMEM((rows, width), f32)],
        flops=2 * members * rows * width * lanes,
        bytes_accessed=2 * members * width * lanes,
    )(grads, w_all, tokens, middle_grad, gain)


def own_weights_kernel(normed_ref, projected_ref, w_ref, gain_ref, out_ref, gain_grad_ref, sum_ref):
    step = pl.program_id(0)

    @pl.when(step == 0)
    def _():
        sum_ref[...] = jnp.zeros_like(sum_ref)

    sum_ref[...] += dot_tn(normed_ref[...], projected_ref[...])

    @pl.when(step == pl.num_programs(0) - 1)
    def _():
        total = sum_ref[...]
        out_ref[...] = total.astype(bf16)
        by_weight = jnp.sum(total * w_ref[...].astype(f32), axis=1, keepdims=True)
        gain_grad_ref[...] = jnp.broadcast_to(by_weight / gain_ref[...], gain_grad_ref.shape)


def own_weights(normed, projected, w_natural, gain):
    total, width = normed.shape
    lanes = projected.shape[1]
    rows = 512
    return call(
        own_weights_kernel,
        (total // rows,),
        0,
        [
            pl.BlockSpec((rows, width), lambda j: (j, 0)),
            pl.BlockSpec((rows, lanes), lambda j: (j, 0)),
            whole((width, lanes)),
            whole((width, 1)),
        ],
        [whole((width, lanes)), whole((width, 8))],
        [struct((width, lanes), bf16), struct((width, 8), f32)],
        scratch=[pltpu.VMEM((width, lanes), f32)],
        flops=2 * total * width * lanes,
        bytes_accessed=2 * total * width,
    )(normed, projected, w_natural, gain)


def out_weights_kernel(place_ref, branch_ref, att_ref, own_ref, *refs, fast):
    outs, sum_ref = refs[:-1], refs[-1]
    step = pl.program_id(0)

    @pl.when(step == 0)
    def _():
        sum_ref[...] = jnp.zeros_like(sum_ref)

    sum_ref[...] += dot_tn(branch_ref[...], att_ref[...])

    @pl.when(step == pl.num_programs(0) - 1)
    def _():
        def products(cols):
            own = own_ref[cols, 0 : 2 * LANES]
            out_one = sum_ref[cols, 0:LANES].astype(bf16)
            out_two = sum_ref[cols, LANES:]
            low = lane_of(out_two.shape) < HEAD_DIM
            tail = jnp.where(low, out_two, own_ref[cols, 2 * LANES :].astype(f32)).astype(bf16)
            yield 0, jnp.concatenate([own, out_one, tail], axis=1)

        if fast:
            write_shards(place_ref, outs, products, own_ref.shape[0])
        else:
            outs[0][...] = next(products(slice(0, own_ref.shape[0])))[1]


def out_weights(place, branch, attended, own, fast):
    total, width = branch.shape
    rows = 512
    if fast:
        shapes = [(1, 1, 2, width // 4, 2 * LANES)] * 4
    else:
        shapes = [(width, 4 * LANES)]
    return call(
        lambda *refs: out_weights_kernel(*refs, fast=fast),
        (total // rows,),
        1,
        [
            pl.BlockSpec((rows, width), lambda j, p: (j, 0)),
            pl.BlockSpec((rows, 2 * LANES), lambda j, p: (j, 0)),
            whole(own.shape),
        ],
        [whole(shape) for shape in shapes],
        [struct(shape, bf16) for shape in shapes],
        scratch=[pltpu.VMEM((width, 2 * LANES), f32)],
        flops=2 * total * width * 2 * LANES,
        bytes_accessed=2 * total * width,
    )(place, branch, attended, own)


def first_sum_kernel(place_ref, keep_a_ref, got_a_ref, keep_b_ref, got_b_ref, send_a_ref, held_a_ref, send_b_ref, held_b_ref):
    x_bit, y_bit = place_ref[3], place_ref[4]
    for bit, keep, got, send, held in (
        (y_bit, keep_a_ref, got_a_ref, send_a_ref, held_a_ref),
        (x_bit, keep_b_ref, got_b_ref, send_b_ref, held_b_ref),
    ):
        held[0, 0] = keep[0, 0, bit].astype(f32) + got[0, 0, bit].astype(f32)
        send[0, 0] = (keep[0, 0, 1 - bit].astype(f32) + got[0, 0, 1 - bit].astype(f32)).astype(bf16)


def first_sum(place, keep_a, got_a, keep_b, got_b):
    count, kinds, _, rows, cols = keep_a.shape
    taken = pl.BlockSpec((1, 1, 2, rows, cols), lambda e, k, p: (e, k, 0, 0, 0))
    given = pl.BlockSpec((1, 1, rows, cols), lambda e, k, p: (e, k, 0, 0))
    shape = (count, kinds, rows, cols)
    return call(
        first_sum_kernel,
        (count, kinds),
        1,
        [taken] * 4,
        [given] * 4,
        [struct(shape, bf16), struct(shape, f32), struct(shape, bf16), struct(shape, f32)],
        flops=4 * keep_a.size,
        bytes_accessed=14 * keep_a.size,
    )(place, keep_a, got_a, keep_b, got_b)


def last_sum_kernel(held_a_ref, got_a_ref, held_b_ref, got_b_ref, *rest):
    outs = rest[-3:]
    side = held_a_ref.shape[3]
    for which, out in enumerate(outs):
        out[0, :, :side] = held_a_ref[0, which] + got_a_ref[0, which].astype(f32)
        out[0, :, side:] = held_b_ref[0, which] + got_b_ref[0, which].astype(f32)


def last_sum(held_a, got_a, held_b, got_b, first, total, before):
    count, kinds, rows, cols = held_a.shape
    taken = pl.BlockSpec((1, kinds, rows, cols), lambda e: (e, 0, 0, 0))
    given = pl.BlockSpec((1, rows, 2 * cols), lambda e: (e + first, 0, 0))
    extra = list(before) if before else []
    return call(
        last_sum_kernel,
        (count,),
        0,
        [taken] * 4 + [pl.BlockSpec(memory_space=pl.ANY)] * len(extra),
        [given] * 3,
        [struct((total, rows, 2 * cols), f32)] * 3,
        flops=2 * held_a.size,
        bytes_accessed=20 * held_a.size,
        aliases={4 + i: i for i in range(len(extra))},
    )(held_a, got_a, held_b, got_b, *extra)


SWAP = [(0, 1), (1, 0)]


def after(value, *events):
    return lax.optimization_barrier((value,) + events)[0]


def gather_group(block):
    return lax.all_gather(block, ("row", "col"), axis=0, tiled=True)


def flip(value, axis, bit, size):
    return lax.ppermute(value, axis, [(i, i ^ (1 << bit)) for i in range(size)])


def bits_of(size):
    return size.bit_length() - 1


def own_bit(axis, bit):
    return (lax.axis_index(axis) >> bit) & 1


def joined(mine, got, own):
    return jnp.where(own == 0, jnp.concatenate([mine, got]), jnp.concatenate([got, mine]))


def cube_gather(value, axis, size):
    value = value[None]
    for bit in range(bits_of(size)):
        value = joined(value, flip(value, axis, bit, size), own_bit(axis, bit))
    return value


def sum_group_then(value, sizes):
    for axis, bit in (("row", 0), ("col", 0), ("col", 1)):
        pair = value.reshape((2, value.shape[0] // 2) + value.shape[1:])
        own = own_bit(axis, bit)
        keep = lax.dynamic_index_in_dim(pair, own, 0, keepdims=False)
        send = lax.dynamic_index_in_dim(pair, 1 - own, 0, keepdims=False)
        value = keep + flip(send, axis, bit, sizes[axis])
    return value


def sum_dp(value, sizes):
    for bit in range(bits_of(sizes["dp"])):
        value = value + flip(value, "dp", bit, sizes["dp"])
    return value


def gather_rows_back(value, sizes):
    for axis, bit in (("col", 1), ("col", 0), ("row", 0)):
        value = joined(value, flip(value, axis, bit, sizes[axis]), own_bit(axis, bit))
    return value


def reduce_over_dp(value, size):
    count = bits_of(size)
    value = value.reshape(value.shape[:1] + (2,) * count + value.shape[2:])
    current = value
    for bit in range(count - 1, -1, -1):
        own = own_bit("dp", bit)
        keep = lax.dynamic_index_in_dim(current, own, 1, keepdims=False)
        send = lax.dynamic_index_in_dim(current, 1 - own, 1, keepdims=False).astype(bf16)
        current = keep.astype(f32) + flip(send, "dp", bit, size).astype(f32)
    return current


def layer(sizes):
    n_dp, n_row, n_col = sizes["dp"], sizes["row"], sizes["col"]
    members = n_row * n_col
    fast = n_dp == 4
    assert n_row == 2 and n_col == COLS and n_dp & (n_dp - 1) == 0

    def local(
        tokens, cotangent, routes, lengths, gain_attn, w_query, w_key, w_value, w_out,
        gain_moe, w_router, w_gate, w_up, w_down,
    ):
        rows, width = tokens.shape
        group = rows * members
        local_experts = w_gate.shape[0]
        row, col, dp = lax.axis_index("row"), lax.axis_index("col"), lax.axis_index("dp")
        place = jnp.stack([row, col, row * n_col + col, dp & 1, (dp >> 1) & 1]).astype(jnp.int32)
        gain_one = gain_attn.astype(f32)[None]
        gain_two = gain_moe.astype(f32)[None]

        tok_all = gather_group(tokens)
        share = rows // n_dp
        w_out_share = lax.dynamic_slice(w_out.T, (dp * share, 0), (share, width))
        w_out_all = cube_gather(w_out_share, "col", n_col)
        w_out_all = cube_gather(w_out_all, "dp", n_dp)
        w_out_all = cube_gather(w_out_all, "row", n_row)
        w_out_all = jnp.transpose(w_out_all, (0, 2, 1, 3, 4)).reshape(members, rows, width)
        route_rows = jnp.zeros((ROUTE_ROWS, 2 * LANES), bf16)
        route_rows = lax.dynamic_update_slice(route_rows, routes.T.astype(bf16), (0, 0))
        route_rows = cube_gather(cube_gather(route_rows, "col", n_col), "row", n_row)
        route_rows = route_rows.reshape(members, ROUTE_ROWS, 2 * LANES)
        cot_all = gather_group(after(cotangent, tok_all))
        w_rows = jnp.concatenate([w_query.T, w_key.T, w_value.T], axis=0)
        w_stack = jnp.concatenate([w_rows, w_value.T], axis=0)
        w_natural = jnp.concatenate([w_query, w_key, w_value, w_value], axis=1)

        ends = jnp.cumsum(lengths[0])
        starts = ends - lengths[0]
        position = jnp.arange(group, dtype=jnp.int32)
        segment = jnp.sum((position[:, None] >= ends[None, :]).astype(jnp.int32), axis=1)
        member = segment[:, None] == jnp.arange(starts.shape[0], dtype=jnp.int32)[None, :]
        start = jnp.sum(jnp.where(member, starts[None, :], 0), axis=1).astype(jnp.int32)
        frequency = rope_base ** (-2.0 * jnp.arange(HEAD_DIM // 2, dtype=f32) / HEAD_DIM)
        angle = (position - start).astype(f32)[:, None] * frequency[None, :]
        cosine = jnp.tile(jnp.cos(angle), (1, 4))
        sine = jnp.tile(jnp.sin(angle), (1, 4))

        query, key, value, normed_one = project(tok_all, gain_one, w_stack, cosine, sine)
        w_router_rows = w_router.T.reshape(members, local_experts, width)
        w_router_rows = jnp.pad(w_router_rows, ((0, 0), (0, 8 - local_experts), (0, 0)))
        w_router_rows = w_router_rows.reshape(members * 8, width)
        packed, attended, totals = attend(query, key, value, start[:, None])
        att_all = gather_group(packed).reshape((members,) + packed.shape)
        w_rows_all = gather_group(after(w_rows, att_all)).reshape((members,) + w_rows.shape)

        x, g, slot_gate, rank, middle, gates = middle_and_dispatch(
            place, att_all, w_out_all, tok_all, cot_all, route_rows, gain_two, w_router_rows, local_experts
        )
        slots = members * CAPACITY
        x = x.reshape(local_experts, slots, width)
        g = g.reshape(local_experts, slots, width)
        slot_gate = slot_gate.reshape(local_experts, slots, LANES)
        rank = rank.reshape(members, 8, rows)
        forth, active, factor, silu = run_experts(x, slot_gate, w_gate, w_up, w_down)
        (forth_other,) = combine(place, rank, [forth])
        cuts = [0, 2, local_experts]
        runs = [
            run_experts_back(place, x, g, active, factor, silu, w_gate, w_up, w_down, first, last - first, fast)
            for first, last in zip(cuts[:-1], cuts[1:])
        ]
        (forth_mine,) = combine(place, rank, [forth], arrived=lax.ppermute(forth_other, "row", SWAP))
        forth_sums = lax.all_to_all(forth_mine, "col", 0, 0, tiled=True)
        back_parts, dot_parts = [run[0] for run in runs], [run[1] for run in runs]
        back_other, dots_other = combine(place, rank, back_parts, dot_parts)
        back_mine, dots_mine = combine(
            place, rank, back_parts, dot_parts, arrived=lax.ppermute(back_other, "row", SWAP)
        )
        dots = jnp.where(
            row == 0, jnp.concatenate([dots_mine, dots_other]), jnp.concatenate([dots_other, dots_mine])
        )
        dots = lax.all_to_all(dots, ("row", "col"), 0, 0, tiled=True).reshape(members * 8, rows)
        back_sums = lax.all_to_all(back_mine, "col", 0, 0, tiled=True)

        middle_grad, branch_grad, attended_grad, small = middle_back(
            back_sums, dots, gates, middle, cotangent, gain_two, w_router_rows, w_out_all
        )
        attended_grad = lax.all_to_all(attended_grad, ("row", "col"), 0, 0, tiled=True)
        branch_all = gather_group(branch_grad)
        small = sum_group_then(small, sizes)

        def start_sum(run):
            send_a, keep_a, send_b, keep_b = run
            got_a, got_b = flip(send_a, "dp", 0, n_dp), flip(send_b, "dp", 1, n_dp)
            send_a, held_a, send_b, held_b = first_sum(place, keep_a, got_a, keep_b, got_b)
            return held_a, flip(send_a, "dp", 1, n_dp), held_b, flip(send_b, "dp", 0, n_dp)

        started = [start_sum(run[2:]) for run in runs] if fast else []

        start_row = jnp.broadcast_to(start[None, :], (8, group))
        attended_grad = attended_grad.reshape(group, 2 * LANES)
        if fast:
            attended_grad = after(attended_grad, started[0][0])
        projected_grad = attend_back(query, key, value, attended_grad, totals, start_row, cosine, sine)
        own_grads, gain_part = own_weights(normed_one, projected_grad, w_natural, gain_attn.astype(f32)[:, None])
        projected_all = lax.all_to_all(
            projected_grad.reshape(members, rows, 3 * LANES), ("row", "col"), 0, 0, tiled=True
        )
        gain_attn_grad = sum_group_then(gain_part[:, 0].reshape(8, width // 8), sizes)
        w_parts = out_weights(place, branch_all, attended, own_grads, fast)
        if fast:
            w_started = start_sum(w_parts)
        else:
            cut = w_parts[0].reshape(1, n_dp, width // n_dp, w_parts[0].shape[1])
            w_sum = reduce_over_dp(cut, n_dp)[0]

        mixed = (middle + jnp.sum(after(forth_sums, projected_grad).astype(f32), axis=0)).astype(bf16)

        small = gather_rows_back(sum_dp(small, sizes), sizes)
        w_router_grad = small.reshape(members, 8, width)[:, :local_experts]
        w_router_grad = w_router_grad.reshape(members * local_experts, width).T
        gain_moe_grad = small[7]
        gain_attn_grad = gather_rows_back(sum_dp(gain_attn_grad, sizes), sizes).reshape(width)

        tokens_grad = input_grad(projected_all, w_rows_all, tokens, middle_grad, gain_one)

        if fast:
            expert_grads = None
            for (held_a, got_a, held_b, got_b), first in zip(started, cuts):
                expert_grads = last_sum(held_a, got_a, held_b, got_b, first, local_experts, expert_grads)
            held_a, got_a, held_b, got_b = [item[0, 0] for item in w_started]
            left = held_a + got_a.astype(f32)
            right = held_b + got_b.astype(f32)
            w_sum = jnp.concatenate([left, right], axis=1)
        else:
            expert_grads = []
            for which in range(3):
                parts = [run[2 + which] for run in runs]
                parts = [part.reshape(part.shape[0], n_dp, width // n_dp, part.shape[2]) for part in parts]
                expert_grads.append(jnp.concatenate([reduce_over_dp(part, n_dp) for part in parts], axis=0))
        w_gate_grad, w_up_grad, w_down_grad = expert_grads
        local_q, local_k = w_query.shape[1], w_key.shape[1]
        cut = local_q + local_k
        return (
            mixed, tokens_grad, gain_attn_grad, w_sum[:, :local_q], w_sum[:, local_q:cut],
            w_sum[:, cut + local_q :], w_sum[:, cut : cut + local_q],
            gain_moe_grad, w_router_grad, w_gate_grad, w_up_grad, w_down_grad,
        )

    return local


def solution(mesh):
    return jax.shard_map(
        layer(dict(mesh.shape)),
        mesh=mesh,
        in_specs=(
            P(("dp", "row", "col"), None),
            P(("dp", "row", "col"), None),
            P(("dp", "row", "col"), None),
            P("dp", None),
            P(),
            P(None, ("row", "col")),
            P(None, ("row", "col")),
            P(None, ("row", "col")),
            P(None, ("row", "col")),
            P(),
            P(),
            P(("row", "col"), None, None),
            P(("row", "col"), None, None),
            P(("row", "col"), None, None),
        ),
        out_specs=(
            P(("dp", "row", "col"), None),
            P(("dp", "row", "col"), None),
            P(),
            P("dp", ("row", "col")),
            P("dp", ("row", "col")),
            P("dp", ("row", "col")),
            P("dp", ("row", "col")),
            P(),
            P(),
            P(("row", "col"), "dp", None),
            P(("row", "col"), "dp", None),
            P(("row", "col"), "dp", None),
        ),
        check_vma=False,
    )
```

```python
import math

import jax
import jax.numpy as jnp
from jax import lax
from jax.experimental import pallas as pl
from jax.experimental.pallas import tpu as pltpu
from jax.sharding import PartitionSpec as P

HEAD_DIM = 64
EXPERTS = 40
TOP = 8
CAPACITY = 64
COLS = 4
LANES = 128
QUERY_BLOCK = 256
ROUTE_ROWS = 16
DOT_ROWS = 16

epsilon = 1e-06
rope_base = 10000.0
masked_score = -1e30
f32 = jnp.float32
bf16 = jnp.bfloat16
VMEM_LIMIT = 56 * 1024 * 1024

NT = (((1,), (1,)), ((), ()))
TN = (((0,), (0,)), ((), ()))


def dot(a, b):
    return jnp.dot(a, b, preferred_element_type=f32)


def dot_nt(a, b):
    return lax.dot_general(a, b, NT, preferred_element_type=f32)


def dot_tn(a, b):
    return lax.dot_general(a, b, TN, preferred_element_type=f32)


def lane_of(shape):
    return lax.broadcasted_iota(jnp.int32, shape, len(shape) - 1)


def call(
    kernel, grid, prefetch, in_specs, out_specs, out_shape, scratch=(), us=1.0, aliases=None
):
    return pl.pallas_call(
        kernel,
        grid_spec=pltpu.PrefetchScalarGridSpec(
            num_scalar_prefetch=prefetch,
            grid=grid,
            in_specs=in_specs,
            out_specs=out_specs,
            scratch_shapes=list(scratch),
        ),
        out_shape=out_shape,
        input_output_aliases=aliases or {},
        compiler_params=pltpu.CompilerParams(
            vmem_limit_bytes=VMEM_LIMIT, dimension_semantics=("arbitrary",) * len(grid)
        ),
        cost_estimate=pl.CostEstimate(
            flops=int(us * 1.1e9), bytes_accessed=int(us * 3.6e6), transcendentals=0
        ),
    )


def whole(shape):
    zeros = (0,) * len(shape)
    return pl.BlockSpec(shape, lambda *_: zeros)


def struct(shape, dtype):
    return jax.ShapeDtypeStruct(shape, dtype)


def turn_within_heads(values, sign):
    lane = lane_of(values.shape) % HEAD_DIM
    ahead = pltpu.roll(values, LANES - HEAD_DIM // 2, 1)
    behind = pltpu.roll(values, HEAD_DIM // 2, 1)
    return jnp.where(lane < HEAD_DIM // 2, -sign * ahead, sign * behind)


def project_kernel(
    tok_ref, gain_ref, w_ref, cos_ref, sin_ref, query_ref, key_ref, value_ref, normed_ref
):
    resid = tok_ref[...].astype(f32)
    inverse = lax.rsqrt(jnp.mean(resid * resid, axis=1, keepdims=True) + epsilon)
    normed = (resid * inverse * gain_ref[...]).astype(bf16)
    normed_ref[...] = normed
    raw = dot_nt(normed, w_ref[...])
    cosine, sine = cos_ref[...], sin_ref[...]

    def rot(values):
        return (values * cosine + turn_within_heads(values, 1.0) * sine).astype(bf16).astype(f32)

    first = rot(raw[:, :LANES])
    second = rot(raw[:, LANES : 2 * LANES])
    low = lane_of(first.shape) < HEAD_DIM
    scale = 1.0 / math.sqrt(HEAD_DIM)
    query_ref[0] = jnp.where(low, first * scale, 0.0).astype(bf16)
    query_ref[1] = jnp.where(low, 0.0, first * scale).astype(bf16)
    query_ref[2] = jnp.where(low, second * scale, 0.0).astype(bf16)
    key_ref[...] = jnp.where(low, pltpu.roll(second, HEAD_DIM, 1), second).astype(bf16)
    value_ref[...] = raw[:, 2 * LANES :].astype(bf16)


def project(tokens, gain, w_stack, cosine, sine):
    total, width = tokens.shape
    rows = 512
    lanes = pl.BlockSpec((rows, LANES), lambda j: (j, 0))
    wide = pl.BlockSpec((rows, width), lambda j: (j, 0))
    return call(
        project_kernel,
        (total // rows,),
        0,
        [wide, whole((1, width)), whole(w_stack.shape), lanes, lanes],
        [pl.BlockSpec((3, rows, LANES), lambda j: (0, j, 0)), lanes, lanes, wide],
        [
            struct((3, total, LANES), bf16),
            struct((total, LANES), bf16),
            struct((total, LANES), bf16),
            struct((total, width), bf16),
        ],
        us=9,
    )(tokens, gain, w_stack, cosine, sine)


def attend_kernel(query_ref, key_ref, value_ref, start_ref, packed_ref, plain_ref, total_ref, out_ref):
    blocks = query_ref.shape[1] // QUERY_BLOCK
    block = pl.program_id(0)
    for index in range(blocks):

        @pl.when(block == index)
        def _(index=index):
            rows = pl.ds(index * QUERY_BLOCK, QUERY_BLOCK)
            span = (index + 1) * QUERY_BLOCK
            row = index * QUERY_BLOCK + lax.broadcasted_iota(jnp.int32, (QUERY_BLOCK, span), 0)
            column = lane_of((QUERY_BLOCK, span))
            allowed = (column <= row) & (column >= start_ref[rows, :])

            def head(number, carry):
                scores = dot_nt(query_ref[number, rows, :], key_ref[0:span, :])
                scores = jnp.where(allowed, scores, masked_score)
                peak = jnp.max(scores, axis=1, keepdims=True)
                weights = jnp.exp(scores - peak)
                summed = jnp.sum(weights, axis=1, keepdims=True)
                probs = (weights * (1.0 / summed)).astype(bf16)
                out_ref[number] = dot(probs, value_ref[0:span, :])
                total = jnp.broadcast_to(peak + jnp.log(summed), (QUERY_BLOCK, LANES))
                total_ref[number, :, rows] = jnp.transpose(total)[0:8, :]
                return carry

            lax.fori_loop(0, 3, head, 0)
            low = lane_of((QUERY_BLOCK, LANES)) < HEAD_DIM
            one, two, three = out_ref[0], out_ref[1], out_ref[2]
            pair = jnp.where(low, one, two).astype(bf16)
            plain_ref[rows, 0:LANES] = pair
            plain_ref[rows, LANES : 2 * LANES] = jnp.where(low, three, 0.0).astype(bf16)
            if index < blocks // 2:
                packed_ref[rows, 0:LANES] = pair
                packed_ref[rows, LANES : 2 * LANES] = three.astype(bf16)
            else:
                back = pl.ds((index - blocks // 2) * QUERY_BLOCK, QUERY_BLOCK)
                before = packed_ref[back, LANES : 2 * LANES].astype(f32)
                packed_ref[back, LANES : 2 * LANES] = jnp.where(low, before, one).astype(bf16)
                packed_ref[back, 2 * LANES : 3 * LANES] = jnp.where(low, two, three).astype(bf16)


def attend(query, key, value, start):
    total = key.shape[0]
    return call(
        attend_kernel,
        (total // QUERY_BLOCK,),
        0,
        [whole(query.shape), whole(key.shape), whole(value.shape), whole(start.shape)],
        [whole((total // 2, 3 * LANES)), whole((total, 2 * LANES)), whole((3, 8, total))],
        [
            struct((total // 2, 3 * LANES), bf16),
            struct((total, 2 * LANES), bf16),
            struct((3, 8, total), f32),
        ],
        scratch=[pltpu.VMEM((3, QUERY_BLOCK, LANES), f32)],
        us=18,
    )(query, key, value, start)


def attend_back_kernel(
    query_ref, key_ref, value_ref, grad_ref, total_ref, start_ref, cos_ref, sin_ref,
    out_ref, query_grad_ref, key_grad_ref, value_grad_ref
):
    blocks = query_ref.shape[1] // QUERY_BLOCK
    block = pl.program_id(0)
    scale = 1.0 / math.sqrt(HEAD_DIM)

    @pl.when(block == 0)
    def _():
        key_grad_ref[...] = jnp.zeros_like(key_grad_ref)
        value_grad_ref[...] = jnp.zeros_like(value_grad_ref)

    def back(values, cosine, sine):
        return values * cosine + turn_within_heads(values * sine, -1.0)

    for index in range(blocks):

        @pl.when(block == index)
        def _(index=index):
            rows = pl.ds(index * QUERY_BLOCK, QUERY_BLOCK)
            span = (index + 1) * QUERY_BLOCK
            row = index * QUERY_BLOCK + lane_of((span, QUERY_BLOCK))
            column = lax.broadcasted_iota(jnp.int32, (span, QUERY_BLOCK), 0)
            allowed = (column <= row) & (column >= start_ref[0:1, rows])
            low = lane_of((QUERY_BLOCK, LANES)) < HEAD_DIM

            def head(number, carry):
                query = query_ref[number, rows, :]
                tile = pl.multiple_of((number // 2) * LANES, LANES)
                upstream = grad_ref[rows, pl.ds(tile, LANES)].astype(f32)
                keep = low == (number != 1)
                upstream = jnp.where(keep, upstream, 0.0).astype(bf16)
                scores = dot_nt(key_ref[0:span, :], query)
                probs = jnp.exp(scores - total_ref[number, 0:1, rows])
                probs = jnp.where(allowed, probs, 0.0)
                prob_grad = dot_nt(value_ref[0:span, :], upstream)
                row_dot = jnp.sum(probs * prob_grad, axis=0, keepdims=True)
                score_grad = (probs * (prob_grad - row_dot)).astype(bf16)
                key_grad_ref[0:span, :] += dot(score_grad, query)
                value_grad_ref[0:span, :] += dot(probs.astype(bf16), upstream)
                query_grad_ref[number] = dot_tn(score_grad, key_ref[0:span, :]) * scale
                return carry

            lax.fori_loop(0, 3, head, 0)
            cosine, sine = cos_ref[rows, :], sin_ref[rows, :]
            pair = jnp.where(low, query_grad_ref[0], query_grad_ref[1])
            out_ref[rows, 0:LANES] = back(pair, cosine, sine).astype(bf16)
            out_ref[rows, LANES : 2 * LANES] = back(query_grad_ref[2], cosine, sine).astype(bf16)

    @pl.when(block == blocks - 1)
    def _():
        low = lane_of(key_grad_ref.shape) < HEAD_DIM
        key_grad = key_grad_ref[...]
        key_grad = key_grad + pltpu.roll(key_grad, HEAD_DIM, 1)
        key_grad = back(key_grad, cos_ref[...], sin_ref[...])
        before = out_ref[:, LANES : 2 * LANES].astype(f32)
        out_ref[:, LANES : 2 * LANES] = jnp.where(low, before, key_grad).astype(bf16)
        value_grad = value_grad_ref[...]
        value_grad = value_grad + pltpu.roll(value_grad, HEAD_DIM, 1)
        out_ref[:, 2 * LANES : 3 * LANES] = jnp.where(low, 0.0, value_grad).astype(bf16)


def attend_back(query, key, value, grad, totals, start, cosine, sine):
    total = key.shape[0]
    args = (query, key, value, grad, totals, start, cosine, sine)
    return call(
        attend_back_kernel,
        (total // QUERY_BLOCK,),
        0,
        [whole(item.shape) for item in args],
        whole((total, 3 * LANES)),
        struct((total, 3 * LANES), bf16),
        scratch=[
            pltpu.VMEM((3, QUERY_BLOCK, LANES), f32),
            pltpu.VMEM((total, LANES), f32),
            pltpu.VMEM((total, LANES), f32),
        ],
        us=25,
    )(*args)


def branch_operand(refs):
    rows = refs.shape[1]
    low = lane_of((rows, LANES)) < HEAD_DIM
    pairs, thirds = [], []
    for member in range(refs.shape[0]):
        one = refs[member, :, 0:LANES]
        mid = refs[member, :, LANES : 2 * LANES].astype(f32)
        end = refs[member, :, 2 * LANES : 3 * LANES].astype(f32)
        mid_turned = pltpu.roll(mid, HEAD_DIM, 1)
        end_turned = pltpu.roll(end, HEAD_DIM, 1)
        late = jnp.where(low, mid_turned, end_turned).astype(bf16)
        pairs.append(jnp.concatenate([one, late], axis=0))
        thirds.append((mid, end_turned))
    for member in range(0, refs.shape[0], 2):
        tops = []
        for which in range(2):
            left, right = thirds[member][which], thirds[member + 1][which]
            tops.append(jnp.where(low, left, pltpu.roll(right, HEAD_DIM, 1)).astype(bf16))
        pairs.append(jnp.concatenate(tops, axis=0))
    return jnp.concatenate(pairs, axis=1)


def hits_of(rank, local_experts):
    place = lax.broadcasted_iota(jnp.int32, (CAPACITY, rank.shape[1]), 0).astype(f32)
    return [place == rank[j : j + 1, :] for j in range(local_experts)]


def chosen_of(hits):
    return jnp.concatenate([jnp.where(hit, 1.0, 0.0).astype(bf16) for hit in hits], axis=0)


def middle_kernel(
    place_ref, att_ref, w_out_ref, tok_a_ref, tok_b_ref, cot_a_ref, cot_b_ref, routes_a_ref, routes_b_ref,
    gain_ref, w_router_ref, after_ref,
    x_ref, g_ref, slot_gate_ref, rank_ref, middle_ref, gates_own_ref, gates_ref, ranks_ref
):
    step = pl.program_id(0)
    member = place_ref[2]
    cols = pl.num_programs(0)
    rows = tok_a_ref.shape[0]
    local_experts = x_ref.shape[0]
    members = w_out_ref.shape[0]
    right = [w_out_ref[source, 0:LANES] for source in range(members)]
    right += [w_out_ref[source, LANES:] for source in range(members)]
    branch = dot(branch_operand(att_ref), jnp.concatenate(right, axis=0))
    for half in range(2):
        tok_ref, cot_ref, routes_ref = (
            (tok_a_ref, cot_a_ref, routes_a_ref), (tok_b_ref, cot_b_ref, routes_b_ref)
        )[half]
        middle = tok_ref[...].astype(f32) + branch[half * rows : (half + 1) * rows]
        inverse = lax.rsqrt(jnp.mean(middle * middle, axis=1, keepdims=True) + epsilon)
        normed = (middle * inverse * gain_ref[...]).astype(bf16)
        logits = dot_nt(w_router_ref[...], normed)
        padded = logits.shape[0]
        slot = lax.broadcasted_iota(jnp.int32, (padded, rows), 0)
        expert = (slot // 8) * local_experts + slot % 8
        expert = jnp.where(slot % 8 < local_experts, expert, -1).astype(f32)
        routes = routes_ref[0].astype(f32)
        named = expert == routes[0:1, 0:rows]
        for k in range(1, TOP):
            named = named | (expert == routes[k : k + 1, 0:rows])
        peak = jnp.max(jnp.where(named, logits, masked_score), axis=0, keepdims=True)
        weights = jnp.where(named, jnp.exp(logits - peak), 0.0)
        gates = weights / jnp.sum(weights, axis=0, keepdims=True)
        gates_ref[...] = gates
        ranks_ref[...] = jnp.where(named, dot(named.astype(f32).astype(bf16), after_ref[...]), -1.0)
        here = pl.ds(pl.multiple_of(member * 8, 8), 8)
        gate, rank = gates_ref[here, :], ranks_ref[here, :]
        rank_ref[half, 0] = rank
        hits = hits_of(rank, local_experts)
        slot_gate = jnp.concatenate(
            [jnp.sum(jnp.where(hit, gate[j : j + 1, :], 0.0), axis=1, keepdims=True) for j, hit in enumerate(hits)],
            axis=0,
        )
        chosen = chosen_of(hits)
        picked = dot(chosen, normed).astype(bf16)
        grads = (dot(chosen, cot_ref[...]) * slot_gate).astype(bf16)
        spread = jnp.broadcast_to(slot_gate, (slot_gate.shape[0], LANES))
        for j in range(local_experts):
            part = slice(j * CAPACITY, (j + 1) * CAPACITY)
            x_ref[j, half, 0] = picked[part]
            g_ref[j, half, 0] = grads[part]
            slot_gate_ref[j, half, 0] = spread[part]

        @pl.when(member == half * cols + step)
        def _(middle=middle, gates=gates):
            middle_ref[...] = middle
            gates_own_ref[...] = gates


def middle_and_dispatch(place, att, w_out, tokens, cotangents, routes, gain, w_router, local_experts):
    width = tokens.shape[1]
    half = COLS
    rows = tokens.shape[0] // (2 * half)
    padded = w_router.shape[0]
    after = (jnp.arange(rows)[:, None] < jnp.arange(rows)[None, :]).astype(bf16)
    slot_shape = (local_experts, 2, half, CAPACITY)
    early = pl.BlockSpec((rows, width), lambda i, p: (i, 0))
    late = pl.BlockSpec((rows, width), lambda i, p: (i + half, 0))
    routes_shape = (1,) + routes.shape[1:]
    return call(
        middle_kernel,
        (half,),
        1,
        [
            pl.BlockSpec((att.shape[0], rows, 3 * LANES), lambda i, p: (0, i, 0)),
            whole(w_out.shape),
            early,
            late,
            early,
            late,
            pl.BlockSpec(routes_shape, lambda i, p: (i, 0, 0)),
            pl.BlockSpec(routes_shape, lambda i, p: (i + half, 0, 0)),
            whole((1, width)),
            whole(w_router.shape),
            whole((rows, rows)),
        ],
        [
            pl.BlockSpec((local_experts, 2, 1, CAPACITY, width), lambda i, p: (0, 0, i, 0, 0)),
            pl.BlockSpec((local_experts, 2, 1, CAPACITY, width), lambda i, p: (0, 0, i, 0, 0)),
            pl.BlockSpec((local_experts, 2, 1, CAPACITY, LANES), lambda i, p: (0, 0, i, 0, 0)),
            pl.BlockSpec((2, 1, 8, rows), lambda i, p: (0, i, 0, 0)),
            whole((rows, width)),
            whole((padded, rows)),
        ],
        [
            struct(slot_shape + (width,), bf16),
            struct(slot_shape + (width,), bf16),
            struct(slot_shape + (LANES,), f32),
            struct((2, half, 8, rows), f32),
            struct((rows, width), f32),
            struct((padded, rows), f32),
        ],
        scratch=[pltpu.VMEM((padded, rows), f32), pltpu.VMEM((padded, rows), f32)],
        us=23,
    )(place, att, w_out, tokens, tokens, cotangents, cotangents, routes, routes, gain, w_router, after)


def expert_kernel(
    x_ref, gate_ref, w_gate_ref, w_up_ref, w_down_ref, forth_ref, active_ref, factor_ref, silu_ref
):
    gate_pre = dot(x_ref[0], w_gate_ref[0])
    up_pre = dot(x_ref[0], w_up_ref[0])
    sig = 1.0 / (1.0 + jnp.exp(-gate_pre))
    silu = gate_pre * sig
    silu_ref[0] = silu
    factor_ref[0] = up_pre * sig * (1.0 + gate_pre * (1.0 - sig))
    active_ref[0] = (silu * up_pre).astype(bf16)
    produced = dot_nt(active_ref[0], w_down_ref[0]).astype(bf16).astype(f32)
    forth_ref[0] = (produced * gate_ref[0, :, 0:1]).astype(bf16)


def run_experts(x, slot_gate, w_gate, w_up, w_down):
    count, slots, width = x.shape
    hidden = w_gate.shape[2]

    def per_expert(*shape):
        return pl.BlockSpec((1,) + shape, lambda e: (e, 0, 0))

    return call(
        expert_kernel,
        (count,),
        0,
        [per_expert(slots, width), per_expert(slots, LANES)] + [per_expert(width, hidden)] * 3,
        [per_expert(slots, width)] + [per_expert(slots, hidden)] * 3,
        [
            struct((count, slots, width), bf16),
            struct((count, slots, hidden), bf16),
            struct((count, slots, hidden), f32),
            struct((count, slots, hidden), f32),
        ],
        us=25,
    )(x, slot_gate, w_gate, w_up, w_down)


def expert_back_kernel(place_ref, *refs, fast):
    x_ref, g_ref, active_ref, factor_ref, silu_ref = refs[:5]
    w_gate_ref, w_up_ref, w_down_ref, back_ref, dots_ref = refs[5:10]
    grads, (gate_low_ref, up_low_ref) = refs[10:-2], refs[-2:]
    slots, width = g_ref.shape[1], g_ref.shape[2]
    chunk = 256
    active_grad = dot(g_ref[0], w_down_ref[0])
    gate_low_ref[...] = (active_grad * factor_ref[0]).astype(bf16)
    up_low_ref[...] = (active_grad * silu_ref[0]).astype(bf16)
    dots = jnp.sum(active_ref[0].astype(f32) * active_grad, axis=1, keepdims=True)
    dots_ref[0] = jnp.broadcast_to(dots, (slots, LANES))
    back_ref[0] = (dot_nt(gate_low_ref[...], w_gate_ref[0]) + dot_nt(up_low_ref[...], w_up_ref[0])).astype(bf16)

    def products(cols):
        x = x_ref[0, :, cols]
        yield 0, dot_tn(x, gate_low_ref[...]).astype(bf16)
        yield 1, dot_tn(x, up_low_ref[...]).astype(bf16)
        yield 2, dot_tn(g_ref[0, :, cols], active_ref[0]).astype(bf16)

    if fast:
        write_shards(place_ref, grads, products, width)
    else:

        def whole_columns(index, carry):
            cols = pl.ds(pl.multiple_of(index * chunk, chunk), chunk)
            for which, product in products(cols):
                grads[which][0, cols, :] = product
            return carry

        lax.fori_loop(0, width // chunk, whole_columns, 0)


def write_shards(place_ref, outs, products, width):
    send_a, keep_a, send_b, keep_b = outs
    x_bit, y_bit = place_ref[3], place_ref[4]
    shard = width // 4
    for dy in range(2):
        for dx in range(2):
            x, y = x_bit ^ dx, y_bit ^ dy
            cols = pl.ds(pl.multiple_of((y * 2 + x) * shard, shard), shard)
            for which, product in products(cols):
                side = product.shape[1] // 2
                (send_a if dx else keep_a)[0, which, y] = product[:, :side]
                (send_b if dy else keep_b)[0, which, x] = product[:, side:]


def run_experts_back(place, x, g, active, factor, silu, w_gate, w_up, w_down, first, count, fast):
    slots, width = g.shape[1], g.shape[2]
    hidden = w_gate.shape[2]

    def taken(*shape):
        return pl.BlockSpec((1,) + shape, lambda e, p: (e + first, 0, 0))

    def given(*shape):
        zeros = (0,) * len(shape)
        return pl.BlockSpec((1,) + shape, lambda e, p: (e,) + zeros)

    if fast:
        grad_shapes = [(3, 2, width // 4, hidden // 2)] * 4
    else:
        grad_shapes = [(width, hidden)] * 3
    return call(
        lambda *refs: expert_back_kernel(*refs, fast=fast),
        (count,),
        1,
        [taken(slots, width)] * 2 + [taken(slots, hidden)] * 3 + [taken(width, hidden)] * 3,
        [given(slots, width), given(slots, LANES)] + [given(*shape) for shape in grad_shapes],
        [struct((count, slots, width), bf16), struct((count, slots, LANES), f32)]
        + [struct((count,) + shape, bf16) for shape in grad_shapes],
        scratch=[pltpu.VMEM((slots, hidden), bf16)] * 2,
        us=10 * count,
    )(place, x, g, active, factor, silu, w_gate, w_up, w_down)


DOT_LANES = 2 * LANES


def combine_kernel(place_ref, rank_ref, *refs, pieces, with_dots, mine):
    parts, rest = refs[:pieces], refs[pieces:]
    rows = rank_ref.shape[2]
    local_experts = sum(part.shape[0] for part in parts)
    hits = hits_of(rank_ref[0], local_experts)
    gathered = jnp.concatenate([part[j, 0] for part in parts for j in range(part.shape[0])], axis=0)
    summed = dot_tn(chosen_of(hits), gathered)
    out_ref = rest[-1]
    if mine:
        arrived_ref = rest[-2]
        summed = summed + arrived_ref[0, 0:rows, :].astype(f32)
    out_ref[0, 0:rows, :] = summed.astype(bf16)
    if with_dots:
        column = [part[j, 0][:, 0:1] for part in rest[:pieces] for j in range(part.shape[0])]
        scattered = [
            jnp.sum(jnp.where(hit, value, 0.0), axis=0, keepdims=True) for hit, value in zip(hits, column)
        ]
        scattered.append(jnp.zeros((DOT_ROWS - local_experts, rows), f32))
        scattered = jnp.concatenate(scattered, axis=0)
        upper = scattered.astype(bf16)
        out_ref[0, rows:, :] = jnp.zeros((DOT_ROWS, out_ref.shape[2]), bf16)
        out_ref[0, rows:, 0:rows] = upper
        out_ref[0, rows:, DOT_LANES : DOT_LANES + rows] = (scattered - upper.astype(f32)).astype(bf16)
        if mine:
            out_ref[0, rows:, 2 * DOT_LANES : 4 * DOT_LANES] = arrived_ref[0, rows:, 0 : 2 * DOT_LANES]


def combine(place, rank, parts, dots=None, arrived=None):
    mine = arrived is not None
    rows, width = rank.shape[2], parts[0].shape[-1]
    out_rows = rows + (DOT_ROWS if dots else 0)

    def member(step, p):
        return (p[0] if mine else 1 - p[0]) * COLS + step

    def slots_of(array):
        return pl.BlockSpec((array.shape[0], 1) + array.shape[2:], lambda j, p: (0, member(j, p), 0, 0))

    inputs = [
        part.reshape(part.shape[0], 2 * COLS, CAPACITY, part.shape[-1]) for part in list(parts) + list(dots or [])
    ]
    in_specs = [pl.BlockSpec((1, 8, rows), lambda j, p: (member(j, p), 0, 0))] + [slots_of(item) for item in inputs]
    by_chip = pl.BlockSpec((1, out_rows, width), lambda j, p: (j, 0, 0))
    if mine:
        inputs.append(arrived)
        in_specs.append(by_chip)
    return call(
        lambda *refs: combine_kernel(*refs, pieces=len(parts), with_dots=bool(dots), mine=mine),
        (COLS,),
        1,
        in_specs,
        by_chip,
        struct((COLS, out_rows, width), bf16),
        us=6,
    )(place, rank, *inputs)


def split_dot(dimension_numbers, values, exact):
    upper = values.astype(bf16)
    lower = (values - upper.astype(f32)).astype(bf16)
    return lax.dot_general(
        upper, exact, dimension_numbers, preferred_element_type=f32
    ) + lax.dot_general(lower, exact, dimension_numbers, preferred_element_type=f32)


def middle_back_kernel(
    place_ref, sums_ref, gates_ref, middle_ref, cot_ref, gain_ref, w_router_ref, w_out_ref,
    grad_ref, branch_ref, attended_ref, small_ref
):
    rows = middle_ref.shape[0]
    tail = sums_ref[:, rows : rows + 8, 0 : 4 * DOT_LANES].astype(f32)
    mine = tail[:, :, 0:rows] + tail[:, :, DOT_LANES : DOT_LANES + rows]
    other = tail[:, :, 2 * DOT_LANES : 2 * DOT_LANES + rows] + tail[:, :, 3 * DOT_LANES : 3 * DOT_LANES + rows]
    first_row = place_ref[0] == 0
    dots = jnp.concatenate([jnp.where(first_row, mine, other), jnp.where(first_row, other, mine)], axis=0)
    dots = dots.reshape(dots.shape[0] * 8, rows)
    gates = gates_ref[...]
    logit_grad = dots - gates * jnp.sum(dots, axis=0, keepdims=True)
    middle = middle_ref[...]
    inverse = lax.rsqrt(jnp.mean(middle * middle, axis=1, keepdims=True) + epsilon)
    unit = middle * inverse
    gain = gain_ref[...]
    normed = (unit * gain).astype(bf16)
    grad = sums_ref[0, 0:rows].astype(f32)
    for index in range(1, sums_ref.shape[0]):
        grad = grad + sums_ref[index, 0:rows].astype(f32)
    grad = grad + split_dot(TN, logit_grad, w_router_ref[...])
    small_ref[...] = split_dot((((1,), (0,)), ((), ())), logit_grad, normed)
    small_ref[7:8, :] = jnp.sum(grad * unit, axis=0, keepdims=True)
    scaled = grad * gain
    middle_grad = cot_ref[...].astype(f32) + inverse * (
        scaled - unit * jnp.mean(scaled * unit, axis=1, keepdims=True)
    )
    grad_ref[...] = middle_grad
    branch_grad = middle_grad.astype(bf16)
    branch_ref[...] = branch_grad
    for member in range(w_out_ref.shape[0]):
        product = dot_nt(branch_grad, w_out_ref[member])
        attended_ref[member, :, 0:LANES] = product[:, 0:LANES].astype(bf16)
        attended_ref[member, :, LANES : LANES + HEAD_DIM] = product[:, LANES:].astype(bf16)
        attended_ref[member, :, LANES + HEAD_DIM :] = jnp.zeros((product.shape[0], HEAD_DIM), bf16)


def middle_back(place, sums, gates, middle, cotangent, gain, w_router, w_out):
    rows, width = middle.shape
    members = w_out.shape[0]
    args = (sums, gates, middle, cotangent, gain, w_router, w_out)
    return call(
        middle_back_kernel,
        (1,),
        1,
        [whole(item.shape) for item in args],
        [
            whole((rows, width)),
            whole((rows, width)),
            whole((members, rows, 2 * LANES)),
            whole(w_router.shape),
        ],
        [
            struct((rows, width), f32),
            struct((rows, width), bf16),
            struct((members, rows, 2 * LANES), bf16),
            struct(w_router.shape, f32),
        ],
        us=7,
    )(place, *args)


def input_grad_kernel(grads_ref, w_query_ref, w_pair_ref, tok_ref, middle_grad_ref, gain_ref, out_ref, sum_ref):
    step = pl.program_id(0)

    @pl.when(step == 0)
    def _():
        sum_ref[...] = jnp.zeros_like(sum_ref)

    right = jnp.concatenate([w_query_ref[0], w_pair_ref[0], w_pair_ref[0, HEAD_DIM:]], axis=0)
    sum_ref[...] += dot(grads_ref[0], right)

    @pl.when(step == pl.num_programs(0) - 1)
    def _():
        resid = tok_ref[...].astype(f32)
        inverse = lax.rsqrt(jnp.mean(resid * resid, axis=1, keepdims=True) + epsilon)
        unit = resid * inverse
        scaled = sum_ref[...] * gain_ref[...]
        out_ref[...] = middle_grad_ref[...] + inverse * (
            scaled - unit * jnp.mean(scaled * unit, axis=1, keepdims=True)
        )


def input_grad(grads, w_query, w_pair, tokens, middle_grad, gain):
    rows, width = tokens.shape
    members, lanes = grads.shape[0], grads.shape[2]
    return call(
        input_grad_kernel,
        (members,),
        0,
        [
            pl.BlockSpec((1, rows, lanes), lambda m: (m, 0, 0)),
            pl.BlockSpec((1,) + w_query.shape[1:], lambda m: (m, 0, 0)),
            pl.BlockSpec((1,) + w_pair.shape[1:], lambda m: (m, 0, 0)),
            whole((rows, width)),
            whole((rows, width)),
            whole((1, width)),
        ],
        whole((rows, width)),
        struct((rows, width), f32),
        scratch=[pltpu.VMEM((rows, width), f32)],
        us=10,
    )(grads, w_query, w_pair, tokens, middle_grad, gain)


def own_weights_kernel(normed_ref, projected_ref, w_ref, gain_ref, out_ref, gain_grad_ref, sum_ref):
    step = pl.program_id(0)

    @pl.when(step == 0)
    def _():
        sum_ref[...] = jnp.zeros_like(sum_ref)

    sum_ref[...] += dot_tn(normed_ref[...], projected_ref[...])

    @pl.when(step == pl.num_programs(0) - 1)
    def _():
        total = sum_ref[...]
        out_ref[...] = total.astype(bf16)
        by_weight = jnp.sum(total * w_ref[...].astype(f32), axis=1, keepdims=True)
        gain_grad_ref[...] = jnp.broadcast_to(by_weight / gain_ref[...], gain_grad_ref.shape)


def own_weights(normed, projected, w_natural, gain):
    total, width = normed.shape
    lanes = projected.shape[1]
    rows = 512
    return call(
        own_weights_kernel,
        (total // rows,),
        0,
        [
            pl.BlockSpec((rows, width), lambda j: (j, 0)),
            pl.BlockSpec((rows, lanes), lambda j: (j, 0)),
            whole((width, lanes)),
            whole((width, 1)),
        ],
        [whole((width, lanes)), whole((width, 8))],
        [struct((width, lanes), bf16), struct((width, 8), f32)],
        scratch=[pltpu.VMEM((width, lanes), f32)],
        us=8,
    )(normed, projected, w_natural, gain)


def out_weights_kernel(place_ref, branch_ref, att_ref, own_ref, *refs, fast):
    outs, sum_ref = refs[:-1], refs[-1]
    step = pl.program_id(0)

    @pl.when(step == 0)
    def _():
        sum_ref[...] = jnp.zeros_like(sum_ref)

    sum_ref[...] += dot_tn(branch_ref[...], att_ref[...])

    @pl.when(step == pl.num_programs(0) - 1)
    def _():
        def products(cols):
            own = own_ref[cols, 0 : 2 * LANES]
            out_one = sum_ref[cols, 0:LANES].astype(bf16)
            out_two = sum_ref[cols, LANES:]
            low = lane_of(out_two.shape) < HEAD_DIM
            tail = jnp.where(low, out_two, own_ref[cols, 2 * LANES :].astype(f32)).astype(bf16)
            yield 0, jnp.concatenate([own, out_one, tail], axis=1)

        if fast:
            write_shards(place_ref, outs, products, own_ref.shape[0])
        else:
            outs[0][...] = next(products(slice(0, own_ref.shape[0])))[1]


def out_weights(place, branch, attended, own, fast):
    total, width = branch.shape
    rows = 512
    if fast:
        shapes = [(1, 1, 2, width // 4, 2 * LANES)] * 4
    else:
        shapes = [(width, 4 * LANES)]
    return call(
        lambda *refs: out_weights_kernel(*refs, fast=fast),
        (total // rows,),
        1,
        [
            pl.BlockSpec((rows, width), lambda j, p: (j, 0)),
            pl.BlockSpec((rows, 2 * LANES), lambda j, p: (j, 0)),
            whole(own.shape),
        ],
        [whole(shape) for shape in shapes],
        [struct(shape, bf16) for shape in shapes],
        scratch=[pltpu.VMEM((width, 2 * LANES), f32)],
        us=7,
    )(place, branch, attended, own)


def first_sum_kernel(place_ref, keep_a_ref, got_a_ref, keep_b_ref, got_b_ref, send_a_ref, held_a_ref, send_b_ref, held_b_ref):
    x_bit, y_bit = place_ref[3], place_ref[4]
    for bit, keep, got, send, held in (
        (y_bit, keep_a_ref, got_a_ref, send_a_ref, held_a_ref),
        (x_bit, keep_b_ref, got_b_ref, send_b_ref, held_b_ref),
    ):
        held[0, 0] = keep[0, 0, bit].astype(f32) + got[0, 0, bit].astype(f32)
        send[0, 0] = (keep[0, 0, 1 - bit].astype(f32) + got[0, 0, 1 - bit].astype(f32)).astype(bf16)


def first_sum(place, keep_a, got_a, keep_b, got_b):
    count, kinds, _, rows, cols = keep_a.shape
    taken = pl.BlockSpec((1, 1, 2, rows, cols), lambda e, k, p: (e, k, 0, 0, 0))
    given = pl.BlockSpec((1, 1, rows, cols), lambda e, k, p: (e, k, 0, 0))
    shape = (count, kinds, rows, cols)
    return call(
        first_sum_kernel,
        (count, kinds),
        1,
        [taken] * 4,
        [given] * 4,
        [struct(shape, bf16), struct(shape, f32), struct(shape, bf16), struct(shape, f32)],
        us=4 * count,
    )(place, keep_a, got_a, keep_b, got_b)


def last_sum_kernel(held_a_ref, got_a_ref, held_b_ref, got_b_ref, *rest):
    outs = rest[-3:]
    side = held_a_ref.shape[3]
    for which, out in enumerate(outs):
        out[0, :, :side] = held_a_ref[0, which] + got_a_ref[0, which].astype(f32)
        out[0, :, side:] = held_b_ref[0, which] + got_b_ref[0, which].astype(f32)


def last_sum(held_a, got_a, held_b, got_b, first, total, before):
    count, kinds, rows, cols = held_a.shape
    taken = pl.BlockSpec((1, kinds, rows, cols), lambda e: (e, 0, 0, 0))
    given = pl.BlockSpec((1, rows, 2 * cols), lambda e: (e + first, 0, 0))
    extra = list(before) if before else []
    return call(
        last_sum_kernel,
        (count,),
        0,
        [taken] * 4 + [pl.BlockSpec(memory_space=pl.ANY)] * len(extra),
        [given] * 3,
        [struct((total, rows, 2 * cols), f32)] * 3,
        us=2.5 * count,
        aliases={4 + i: i for i in range(len(extra))},
    )(held_a, got_a, held_b, got_b, *extra)


SWAP = [(0, 1), (1, 0)]


def after(value, *events):
    return lax.optimization_barrier((value,) + events)[0]


def gather_group(block):
    return lax.all_gather(block, ("row", "col"), axis=0, tiled=True)


def flip(value, axis, bit, size):
    return lax.ppermute(value, axis, [(i, i ^ (1 << bit)) for i in range(size)])


def bits_of(size):
    return size.bit_length() - 1


def own_bit(axis, bit):
    return (lax.axis_index(axis) >> bit) & 1


def joined(mine, got, own):
    return jnp.where(own == 0, jnp.concatenate([mine, got]), jnp.concatenate([got, mine]))


def cube_gather(value, axis, size):
    value = value[None]
    for bit in range(bits_of(size)):
        value = joined(value, flip(value, axis, bit, size), own_bit(axis, bit))
    return value


def sum_group_then(value, sizes):
    for axis, bit in (("row", 0), ("col", 0), ("col", 1)):
        pair = value.reshape((2, value.shape[0] // 2) + value.shape[1:])
        own = own_bit(axis, bit)
        keep = lax.dynamic_index_in_dim(pair, own, 0, keepdims=False)
        send = lax.dynamic_index_in_dim(pair, 1 - own, 0, keepdims=False)
        value = keep + flip(send, axis, bit, sizes[axis])
    return value


def sum_group(value, sizes):
    for axis, bit in (("row", 0), ("col", 0), ("col", 1)):
        value = value + flip(value, axis, bit, sizes[axis])
    return value


def sum_dp(value, sizes):
    for bit in range(bits_of(sizes["dp"])):
        value = value + flip(value, "dp", bit, sizes["dp"])
    return value


def gather_rows_back(value, sizes):
    for axis, bit in (("col", 1), ("col", 0), ("row", 0)):
        value = joined(value, flip(value, axis, bit, sizes[axis]), own_bit(axis, bit))
    return value


def reduce_over_dp(value, size):
    count = bits_of(size)
    value = value.reshape(value.shape[:1] + (2,) * count + value.shape[2:])
    current = value
    for bit in range(count - 1, -1, -1):
        own = own_bit("dp", bit)
        keep = lax.dynamic_index_in_dim(current, own, 1, keepdims=False)
        send = lax.dynamic_index_in_dim(current, 1 - own, 1, keepdims=False).astype(bf16)
        current = keep.astype(f32) + flip(send, "dp", bit, size).astype(f32)
    return current


def start_move(run, size):
    return flip(run[0], "dp", 0, size), flip(run[2], "dp", 1, size)


def first_half(place, run, got, size, event):
    keep_a, keep_b = after((run[1], run[3]), event)
    send_a, held_a, send_b, held_b = first_sum(place, keep_a, got[0], keep_b, got[1])
    return held_a, flip(send_a, "dp", 1, size), held_b, flip(send_b, "dp", 0, size)


def layer(sizes):
    n_dp, n_row, n_col = sizes["dp"], sizes["row"], sizes["col"]
    members = n_row * n_col
    fast = n_dp == 4
    assert n_row == 2 and n_col == COLS and n_dp & (n_dp - 1) == 0

    def local(
        tokens, cotangent, routes, lengths, gain_attn, w_query, w_key, w_value, w_out,
        gain_moe, w_router, w_gate, w_up, w_down,
    ):
        rows, width = tokens.shape
        group = rows * members
        local_experts = w_gate.shape[0]
        row, col, dp = lax.axis_index("row"), lax.axis_index("col"), lax.axis_index("dp")
        place = jnp.stack([row, col, row * n_col + col, dp & 1, (dp >> 1) & 1]).astype(jnp.int32)
        gain_one = gain_attn.astype(f32)[None]
        gain_two = gain_moe.astype(f32)[None]

        tok_all = gather_group(tokens)
        share = rows // n_dp
        w_out_share = lax.dynamic_slice(w_out.T, (dp * share, 0), (share, width))
        w_out_all = cube_gather(w_out_share, "col", n_col)
        w_out_all = cube_gather(w_out_all, "dp", n_dp)
        w_out_all = cube_gather(w_out_all, "row", n_row)
        w_out_all = jnp.transpose(w_out_all, (0, 2, 1, 3, 4)).reshape(members, rows, width)
        route_rows = jnp.zeros((ROUTE_ROWS, 2 * LANES), bf16)
        route_rows = lax.dynamic_update_slice(route_rows, routes.T.astype(bf16), (0, 0))
        route_rows = cube_gather(cube_gather(route_rows, "col", n_col), "row", n_row)
        route_rows = route_rows.reshape(members, ROUTE_ROWS, 2 * LANES)
        cot_all = gather_group(after(cotangent, tok_all))
        w_pair = jnp.concatenate([w_key.T, w_value.T], axis=0)
        w_stack = jnp.concatenate([w_query.T, w_pair, w_value.T], axis=0)
        w_natural = jnp.concatenate([w_query, w_key, w_value, w_value], axis=1)

        ends = jnp.cumsum(lengths[0])
        starts = ends - lengths[0]
        position = jnp.arange(group, dtype=jnp.int32)
        segment = jnp.sum((position[:, None] >= ends[None, :]).astype(jnp.int32), axis=1)
        member = segment[:, None] == jnp.arange(starts.shape[0], dtype=jnp.int32)[None, :]
        start = jnp.sum(jnp.where(member, starts[None, :], 0), axis=1).astype(jnp.int32)
        frequency = rope_base ** (-2.0 * jnp.arange(HEAD_DIM // 2, dtype=f32) / HEAD_DIM)
        angle = (position - start).astype(f32)[:, None] * frequency[None, :]
        cosine = jnp.tile(jnp.cos(angle), (1, 4))
        sine = jnp.tile(jnp.sin(angle), (1, 4))

        query, key, value, normed_one = project(tok_all, after(gain_one, w_out_all, route_rows), w_stack, cosine, sine)
        w_router_rows = w_router.T.reshape(members, local_experts, width)
        w_router_rows = jnp.pad(w_router_rows, ((0, 0), (0, 8 - local_experts), (0, 0)))
        w_router_rows = w_router_rows.reshape(members * 8, width)
        packed, attended, totals = attend(query, key, value, start[:, None])
        att_all = gather_group(after(packed, cot_all)).reshape((members,) + packed.shape)
        w_query_all = gather_group(after(w_query.T, att_all)).reshape(members, w_query.shape[1], width)
        w_pair_all = gather_group(after(w_pair, w_query_all)).reshape((members,) + w_pair.shape)

        x, g, slot_gate, rank, middle, gates = middle_and_dispatch(
            place, att_all, w_out_all, tok_all, cot_all, route_rows, gain_two, w_router_rows, local_experts
        )
        slots = members * CAPACITY
        x = x.reshape(local_experts, slots, width)
        g = g.reshape(local_experts, slots, width)
        slot_gate = slot_gate.reshape(local_experts, slots, LANES)
        rank = rank.reshape(members, 8, rows)
        forth, active, factor, silu = run_experts(x, slot_gate, w_gate, w_up, w_down)
        forth_other = combine(place, rank, [forth])
        arrived = lax.ppermute(forth_other, "row", SWAP)
        cuts = [0, 2, local_experts]

        def backward(which, x):
            first, last = cuts[which], cuts[which + 1]
            return run_experts_back(place, x, g, active, factor, silu, w_gate, w_up, w_down, first, last - first, fast)

        runs = [backward(0, after(x, forth_other, w_query_all))]
        forth_mine = combine(place, rank, [forth], arrived=after(arrived, runs[0][1]))
        forth_sums = lax.all_to_all(forth_mine, "col", 0, 0, tiled=True)
        runs.append(backward(1, after(x, forth_mine, w_pair_all)))
        moved = [start_move(run[2:], n_dp) for run in runs] if fast else []
        back_parts, dot_parts = [run[0] for run in runs], [run[1] for run in runs]
        back_other = combine(place, rank, back_parts, dot_parts)
        arrived = lax.ppermute(back_other, "row", SWAP)
        if fast:
            arrived = after(arrived, *moved[0])
        back_mine = combine(place, rank, back_parts, dot_parts, arrived)
        back_mine = after(back_mine, forth_sums)
        back_sums = lax.all_to_all(back_mine, "col", 0, 0, tiled=True)
        started, gate_middle = [], []
        if fast:
            started.append(first_half(place, runs[0][2:], moved[0], n_dp, back_mine))
            gate_middle += [started[0][0], *moved[1]]

        middle_grad, branch_grad, attended_grad, small = middle_back(
            place, back_sums, gates, middle, cotangent, after(gain_two, *gate_middle), w_router_rows, w_out_all
        )
        if fast:
            started.append(first_half(place, runs[1][2:], moved[1], n_dp, branch_grad))
        attended_grad = lax.all_to_all(attended_grad, ("row", "col"), 0, 0, tiled=True)
        branch_all = gather_group(branch_grad)
        small = gather_rows_back(sum_group_then(small, sizes), sizes)

        start_row = jnp.broadcast_to(start[None, :], (8, group))
        attended_grad = attended_grad.reshape(group, 2 * LANES)
        if fast:
            attended_grad = after(attended_grad, started[1][0])
        projected_grad = attend_back(query, key, value, attended_grad, totals, start_row, cosine, sine)
        own_grads, gain_part = own_weights(after(normed_one, branch_all), projected_grad, w_natural, gain_attn.astype(f32)[:, None])
        projected_all = lax.all_to_all(
            projected_grad.reshape(members, rows, 3 * LANES), ("row", "col"), 0, 0, tiled=True
        )
        gain_attn_grad = sum_group(gain_part[:, 0].reshape(8, width // 8), sizes)
        w_parts = out_weights(place, branch_all, attended, own_grads, fast)
        if fast:
            w_started = first_half(place, w_parts, start_move(w_parts, n_dp), n_dp, w_parts[1])
        else:
            cut = w_parts[0].reshape(1, n_dp, width // n_dp, w_parts[0].shape[1])
            w_sum = reduce_over_dp(cut, n_dp)[0]

        mixed = (middle + jnp.sum(after(forth_sums, projected_grad).astype(f32), axis=0)).astype(bf16)

        used = small.reshape(members, 8, width)[:, : local_experts].reshape(members * local_experts, width)
        both = jnp.concatenate([used, small[7:8], gain_attn_grad.reshape(1, width)], axis=0)
        both = sum_dp(after(both, w_parts[0]), sizes)
        w_router_grad = both[: members * local_experts].T
        gain_moe_grad, gain_attn_grad = both[members * local_experts], both[members * local_experts + 1]

        expert_grads = None
        gate_last = [small]
        if fast:
            held = after((started[0][0], started[0][2]), projected_grad)
            expert_grads = last_sum(held[0], started[0][1], held[1], started[0][3], cuts[0], local_experts, None)
            gate_last.append(expert_grads[0])
        tokens_grad = input_grad(
            projected_all, w_query_all, w_pair_all, tokens, middle_grad, after(gain_one, *gate_last)
        )

        if fast:
            held_a, got_a, held_b, got_b = started[1]
            expert_grads = last_sum(held_a, got_a, held_b, got_b, cuts[1], local_experts, expert_grads)
            held_a, got_a, held_b, got_b = [item[0, 0] for item in w_started]
            left = held_a + got_a.astype(f32)
            right = held_b + got_b.astype(f32)
            w_sum = jnp.concatenate([left, right], axis=1)
        else:
            expert_grads = []
            for which in range(3):
                parts = [run[2 + which] for run in runs]
                parts = [part.reshape(part.shape[0], n_dp, width // n_dp, part.shape[2]) for part in parts]
                expert_grads.append(jnp.concatenate([reduce_over_dp(part, n_dp) for part in parts], axis=0))
        w_gate_grad, w_up_grad, w_down_grad = expert_grads
        local_q, local_k = w_query.shape[1], w_key.shape[1]
        cut = local_q + local_k
        return (
            mixed, tokens_grad, gain_attn_grad, w_sum[:, :local_q], w_sum[:, local_q:cut],
            w_sum[:, cut + local_q :], w_sum[:, cut : cut + local_q],
            gain_moe_grad, w_router_grad, w_gate_grad, w_up_grad, w_down_grad,
        )

    return local


def solution(mesh):
    return jax.shard_map(
        layer(dict(mesh.shape)),
        mesh=mesh,
        in_specs=(
            P(("dp", "row", "col"), None),
            P(("dp", "row", "col"), None),
            P(("dp", "row", "col"), None),
            P("dp", None),
            P(),
            P(None, ("row", "col")),
            P(None, ("row", "col")),
            P(None, ("row", "col")),
            P(None, ("row", "col")),
            P(),
            P(),
            P(("row", "col"), None, None),
            P(("row", "col"), None, None),
            P(("row", "col"), None, None),
        ),
        out_specs=(
            P(("dp", "row", "col"), None),
            P(("dp", "row", "col"), None),
            P(),
            P("dp", ("row", "col")),
            P("dp", ("row", "col")),
            P("dp", ("row", "col")),
            P("dp", ("row", "col")),
            P(),
            P(),
            P(("row", "col"), "dp", None),
            P(("row", "col"), "dp", None),
            P(("row", "col"), "dp", None),
        ),
        check_vma=False,
    )
```

```python
import math

import jax
import jax.numpy as jnp
from jax import lax
from jax.experimental import pallas as pl
from jax.experimental.pallas import tpu as pltpu
from jax.sharding import PartitionSpec as P

HEAD_DIM = 64
EXPERTS = 40
TOP = 8
CAPACITY = 64
COLS = 4
LANES = 128
QUERY_BLOCK = 256
ROUTE_ROWS = 16
DOT_ROWS = 16

epsilon = 1e-06
rope_base = 10000.0
masked_score = -1e30
f32 = jnp.float32
bf16 = jnp.bfloat16
VMEM_LIMIT = 56 * 1024 * 1024

NT = (((1,), (1,)), ((), ()))
TN = (((0,), (0,)), ((), ()))


def dot(a, b):
    return jnp.dot(a, b, preferred_element_type=f32)


def dot_nt(a, b):
    return lax.dot_general(a, b, NT, preferred_element_type=f32)


def dot_tn(a, b):
    return lax.dot_general(a, b, TN, preferred_element_type=f32)


def lane_of(shape):
    return lax.broadcasted_iota(jnp.int32, shape, len(shape) - 1)


def call(
    kernel, grid, prefetch, in_specs, out_specs, out_shape, scratch=(), us=1.0, aliases=None
):
    return pl.pallas_call(
        kernel,
        grid_spec=pltpu.PrefetchScalarGridSpec(
            num_scalar_prefetch=prefetch,
            grid=grid,
            in_specs=in_specs,
            out_specs=out_specs,
            scratch_shapes=list(scratch),
        ),
        out_shape=out_shape,
        input_output_aliases=aliases or {},
        compiler_params=pltpu.CompilerParams(
            vmem_limit_bytes=VMEM_LIMIT, dimension_semantics=("arbitrary",) * len(grid)
        ),
        cost_estimate=pl.CostEstimate(
            flops=int(us * 1.1e9), bytes_accessed=int(us * 3.6e6), transcendentals=0
        ),
    )


def whole(shape):
    zeros = (0,) * len(shape)
    return pl.BlockSpec(shape, lambda *_: zeros)


def struct(shape, dtype):
    return jax.ShapeDtypeStruct(shape, dtype)


def turn_within_heads(values, sign):
    lane = lane_of(values.shape) % HEAD_DIM
    ahead = pltpu.roll(values, LANES - HEAD_DIM // 2, 1)
    behind = pltpu.roll(values, HEAD_DIM // 2, 1)
    return jnp.where(lane < HEAD_DIM // 2, -sign * ahead, sign * behind)


def project_kernel(
    tok_ref, gain_ref, w_ref, cos_ref, sin_ref, query_ref, key_ref, value_ref, normed_ref
):
    resid = tok_ref[...].astype(f32)
    inverse = lax.rsqrt(jnp.mean(resid * resid, axis=1, keepdims=True) + epsilon)
    normed = (resid * inverse * gain_ref[...]).astype(bf16)
    normed_ref[...] = normed
    raw = dot_nt(normed, w_ref[...])
    cosine, sine = cos_ref[...], sin_ref[...]

    def rot(values):
        return (values * cosine + turn_within_heads(values, 1.0) * sine).astype(bf16).astype(f32)

    first = rot(raw[:, :LANES])
    second = rot(raw[:, LANES : 2 * LANES])
    low = lane_of(first.shape) < HEAD_DIM
    scale = 1.0 / math.sqrt(HEAD_DIM)
    query_ref[0] = jnp.where(low, first * scale, 0.0).astype(bf16)
    query_ref[1] = jnp.where(low, 0.0, first * scale).astype(bf16)
    query_ref[2] = jnp.where(low, second * scale, 0.0).astype(bf16)
    key_ref[...] = jnp.where(low, pltpu.roll(second, HEAD_DIM, 1), second).astype(bf16)
    value_ref[...] = raw[:, 2 * LANES :].astype(bf16)


def project(tokens, gain, w_stack, cosine, sine):
    total, width = tokens.shape
    rows = 512
    lanes = pl.BlockSpec((rows, LANES), lambda j: (j, 0))
    wide = pl.BlockSpec((rows, width), lambda j: (j, 0))
    return call(
        project_kernel,
        (total // rows,),
        0,
        [wide, whole((1, width)), whole(w_stack.shape), lanes, lanes],
        [pl.BlockSpec((3, rows, LANES), lambda j: (0, j, 0)), lanes, lanes, wide],
        [
            struct((3, total, LANES), bf16),
            struct((total, LANES), bf16),
            struct((total, LANES), bf16),
            struct((total, width), bf16),
        ],
        us=9,
    )(tokens, gain, w_stack, cosine, sine)


def attend_kernel(query_ref, key_ref, value_ref, start_ref, packed_ref, plain_ref, total_ref, out_ref):
    blocks = query_ref.shape[1] // QUERY_BLOCK
    block = pl.program_id(0)
    for index in range(blocks):

        @pl.when(block == index)
        def _(index=index):
            rows = pl.ds(index * QUERY_BLOCK, QUERY_BLOCK)
            span = (index + 1) * QUERY_BLOCK
            row = index * QUERY_BLOCK + lax.broadcasted_iota(jnp.int32, (QUERY_BLOCK, span), 0)
            column = lane_of((QUERY_BLOCK, span))
            allowed = (column <= row) & (column >= start_ref[rows, :])

            def head(number, carry):
                scores = dot_nt(query_ref[number, rows, :], key_ref[0:span, :])
                scores = jnp.where(allowed, scores, masked_score)
                peak = jnp.max(scores, axis=1, keepdims=True)
                weights = jnp.exp(scores - peak)
                summed = jnp.sum(weights, axis=1, keepdims=True)
                probs = (weights * (1.0 / summed)).astype(bf16)
                out_ref[number] = dot(probs, value_ref[0:span, :])
                total = jnp.broadcast_to(peak + jnp.log(summed), (QUERY_BLOCK, LANES))
                total_ref[number, :, rows] = jnp.transpose(total)[0:8, :]
                return carry

            lax.fori_loop(0, 3, head, 0)
            low = lane_of((QUERY_BLOCK, LANES)) < HEAD_DIM
            one, two, three = out_ref[0], out_ref[1], out_ref[2]
            pair = jnp.where(low, one, two).astype(bf16)
            plain_ref[rows, 0:LANES] = pair
            plain_ref[rows, LANES : 2 * LANES] = jnp.where(low, three, 0.0).astype(bf16)
            if index < blocks // 2:
                packed_ref[rows, 0:LANES] = pair
                packed_ref[rows, LANES : 2 * LANES] = three.astype(bf16)
            else:
                back = pl.ds((index - blocks // 2) * QUERY_BLOCK, QUERY_BLOCK)
                before = packed_ref[back, LANES : 2 * LANES].astype(f32)
                packed_ref[back, LANES : 2 * LANES] = jnp.where(low, before, one).astype(bf16)
                packed_ref[back, 2 * LANES : 3 * LANES] = jnp.where(low, two, three).astype(bf16)


def attend(query, key, value, start):
    total = key.shape[0]
    return call(
        attend_kernel,
        (total // QUERY_BLOCK,),
        0,
        [whole(query.shape), whole(key.shape), whole(value.shape), whole(start.shape)],
        [whole((total // 2, 3 * LANES)), whole((total, 2 * LANES)), whole((3, 8, total))],
        [
            struct((total // 2, 3 * LANES), bf16),
            struct((total, 2 * LANES), bf16),
            struct((3, 8, total), f32),
        ],
        scratch=[pltpu.VMEM((3, QUERY_BLOCK, LANES), f32)],
        us=18,
    )(query, key, value, start)


def attend_back_kernel(
    query_ref, key_ref, value_ref, grad_ref, total_ref, start_ref, cos_ref, sin_ref,
    out_ref, query_grad_ref, key_grad_ref, value_grad_ref
):
    blocks = query_ref.shape[1] // QUERY_BLOCK
    block = pl.program_id(0)
    scale = 1.0 / math.sqrt(HEAD_DIM)

    @pl.when(block == 0)
    def _():
        key_grad_ref[...] = jnp.zeros_like(key_grad_ref)
        value_grad_ref[...] = jnp.zeros_like(value_grad_ref)

    def back(values, cosine, sine):
        return values * cosine + turn_within_heads(values * sine, -1.0)

    for index in range(blocks):

        @pl.when(block == index)
        def _(index=index):
            rows = pl.ds(index * QUERY_BLOCK, QUERY_BLOCK)
            span = (index + 1) * QUERY_BLOCK
            row = index * QUERY_BLOCK + lane_of((span, QUERY_BLOCK))
            column = lax.broadcasted_iota(jnp.int32, (span, QUERY_BLOCK), 0)
            allowed = (column <= row) & (column >= start_ref[0:1, rows])
            low = lane_of((QUERY_BLOCK, LANES)) < HEAD_DIM

            def head(number, carry):
                query = query_ref[number, rows, :]
                tile = pl.multiple_of((number // 2) * LANES, LANES)
                upstream = grad_ref[rows, pl.ds(tile, LANES)].astype(f32)
                keep = low == (number != 1)
                upstream = jnp.where(keep, upstream, 0.0).astype(bf16)
                scores = dot_nt(key_ref[0:span, :], query)
                probs = jnp.exp(scores - total_ref[number, 0:1, rows])
                probs = jnp.where(allowed, probs, 0.0)
                prob_grad = dot_nt(value_ref[0:span, :], upstream)
                row_dot = jnp.sum(probs * prob_grad, axis=0, keepdims=True)
                score_grad = (probs * (prob_grad - row_dot)).astype(bf16)
                key_grad_ref[0:span, :] += dot(score_grad, query)
                value_grad_ref[0:span, :] += dot(probs.astype(bf16), upstream)
                query_grad_ref[number] = dot_tn(score_grad, key_ref[0:span, :]) * scale
                return carry

            lax.fori_loop(0, 3, head, 0)
            cosine, sine = cos_ref[rows, :], sin_ref[rows, :]
            pair = jnp.where(low, query_grad_ref[0], query_grad_ref[1])
            out_ref[rows, 0:LANES] = back(pair, cosine, sine).astype(bf16)
            out_ref[rows, LANES : 2 * LANES] = back(query_grad_ref[2], cosine, sine).astype(bf16)

    @pl.when(block == blocks - 1)
    def _():
        low = lane_of(key_grad_ref.shape) < HEAD_DIM
        key_grad = key_grad_ref[...]
        key_grad = key_grad + pltpu.roll(key_grad, HEAD_DIM, 1)
        key_grad = back(key_grad, cos_ref[...], sin_ref[...])
        before = out_ref[:, LANES : 2 * LANES].astype(f32)
        out_ref[:, LANES : 2 * LANES] = jnp.where(low, before, key_grad).astype(bf16)
        value_grad = value_grad_ref[...]
        value_grad = value_grad + pltpu.roll(value_grad, HEAD_DIM, 1)
        out_ref[:, 2 * LANES : 3 * LANES] = jnp.where(low, 0.0, value_grad).astype(bf16)


def attend_back(query, key, value, grad, totals, start, cosine, sine):
    total = key.shape[0]
    args = (query, key, value, grad, totals, start, cosine, sine)
    return call(
        attend_back_kernel,
        (total // QUERY_BLOCK,),
        0,
        [whole(item.shape) for item in args],
        whole((total, 3 * LANES)),
        struct((total, 3 * LANES), bf16),
        scratch=[
            pltpu.VMEM((3, QUERY_BLOCK, LANES), f32),
            pltpu.VMEM((total, LANES), f32),
            pltpu.VMEM((total, LANES), f32),
        ],
        us=0,
    )(*args)


def branch_operand(refs):
    rows = refs.shape[1]
    low = lane_of((rows, LANES)) < HEAD_DIM
    pairs, thirds = [], []
    for member in range(refs.shape[0]):
        one = refs[member, :, 0:LANES]
        mid = refs[member, :, LANES : 2 * LANES].astype(f32)
        end = refs[member, :, 2 * LANES : 3 * LANES].astype(f32)
        mid_turned = pltpu.roll(mid, HEAD_DIM, 1)
        end_turned = pltpu.roll(end, HEAD_DIM, 1)
        late = jnp.where(low, mid_turned, end_turned).astype(bf16)
        pairs.append(jnp.concatenate([one, late], axis=0))
        thirds.append((mid, end_turned))
    for member in range(0, refs.shape[0], 2):
        tops = []
        for which in range(2):
            left, right = thirds[member][which], thirds[member + 1][which]
            tops.append(jnp.where(low, left, pltpu.roll(right, HEAD_DIM, 1)).astype(bf16))
        pairs.append(jnp.concatenate(tops, axis=0))
    return jnp.concatenate(pairs, axis=1)


def hits_of(rank, local_experts):
    place = lax.broadcasted_iota(jnp.int32, (CAPACITY, rank.shape[1]), 0).astype(f32)
    return [place == rank[j : j + 1, :] for j in range(local_experts)]


def chosen_of(hits):
    return jnp.concatenate([jnp.where(hit, 1.0, 0.0).astype(bf16) for hit in hits], axis=0)


def middle_kernel(
    place_ref, att_ref, w_out_ref, tok_a_ref, tok_b_ref, routes_a_ref, routes_b_ref,
    gain_ref, w_router_ref, after_ref,
    x_ref, slot_gate_ref, rank_ref, gate_ref, middle_ref, gates_own_ref, gates_ref, ranks_ref
):
    step = pl.program_id(0)
    member = place_ref[2]
    cols = pl.num_programs(0)
    rows = tok_a_ref.shape[0]
    local_experts = x_ref.shape[0]
    members = w_out_ref.shape[0]
    right = [w_out_ref[source, 0:LANES] for source in range(members)]
    right += [w_out_ref[source, LANES:] for source in range(members)]
    branch = dot(branch_operand(att_ref), jnp.concatenate(right, axis=0))
    for half in range(2):
        tok_ref, routes_ref = ((tok_a_ref, routes_a_ref), (tok_b_ref, routes_b_ref))[half]
        middle = tok_ref[...].astype(f32) + branch[half * rows : (half + 1) * rows]
        inverse = lax.rsqrt(jnp.mean(middle * middle, axis=1, keepdims=True) + epsilon)
        normed = (middle * inverse * gain_ref[...]).astype(bf16)
        logits = dot_nt(w_router_ref[...], normed)
        padded = logits.shape[0]
        slot = lax.broadcasted_iota(jnp.int32, (padded, rows), 0)
        expert = (slot // 8) * local_experts + slot % 8
        expert = jnp.where(slot % 8 < local_experts, expert, -1).astype(f32)
        routes = routes_ref[0].astype(f32)
        named = expert == routes[0:1, 0:rows]
        for k in range(1, TOP):
            named = named | (expert == routes[k : k + 1, 0:rows])
        peak = jnp.max(jnp.where(named, logits, masked_score), axis=0, keepdims=True)
        weights = jnp.where(named, jnp.exp(logits - peak), 0.0)
        gates = weights / jnp.sum(weights, axis=0, keepdims=True)
        gates_ref[...] = gates
        ranks_ref[...] = jnp.where(named, dot(named.astype(f32).astype(bf16), after_ref[...]), -1.0)
        here = pl.ds(pl.multiple_of(member * 8, 8), 8)
        gate, rank = gates_ref[here, :], ranks_ref[here, :]
        rank_ref[half, 0] = rank
        gate_ref[half, 0] = gate
        hits = hits_of(rank, local_experts)
        slot_gate = jnp.concatenate(
            [jnp.sum(jnp.where(hit, gate[j : j + 1, :], 0.0), axis=1, keepdims=True) for j, hit in enumerate(hits)],
            axis=0,
        )
        chosen = chosen_of(hits)
        picked = dot(chosen, normed).astype(bf16)
        spread = jnp.broadcast_to(slot_gate, (slot_gate.shape[0], LANES))
        for j in range(local_experts):
            part = slice(j * CAPACITY, (j + 1) * CAPACITY)
            x_ref[j, half, 0] = picked[part]
            slot_gate_ref[j, half, 0] = spread[part]

        @pl.when(member == half * cols + step)
        def _(middle=middle, gates=gates):
            middle_ref[...] = middle
            gates_own_ref[...] = gates


def middle_and_dispatch(place, att, w_out, tokens, routes, gain, w_router, local_experts):
    width = tokens.shape[1]
    half = COLS
    rows = tokens.shape[0] // (2 * half)
    padded = w_router.shape[0]
    after = (jnp.arange(rows)[:, None] < jnp.arange(rows)[None, :]).astype(bf16)
    slot_shape = (local_experts, 2, half, CAPACITY)
    early = pl.BlockSpec((rows, width), lambda i, p: (i, 0))
    late = pl.BlockSpec((rows, width), lambda i, p: (i + half, 0))
    routes_shape = (1,) + routes.shape[1:]
    return call(
        middle_kernel,
        (half,),
        1,
        [
            pl.BlockSpec((att.shape[0], rows, 3 * LANES), lambda i, p: (0, i, 0)),
            whole(w_out.shape),
            early,
            late,
            pl.BlockSpec(routes_shape, lambda i, p: (i, 0, 0)),
            pl.BlockSpec(routes_shape, lambda i, p: (i + half, 0, 0)),
            whole((1, width)),
            whole(w_router.shape),
            whole((rows, rows)),
        ],
        [
            pl.BlockSpec((local_experts, 2, 1, CAPACITY, width), lambda i, p: (0, 0, i, 0, 0)),
            pl.BlockSpec((local_experts, 2, 1, CAPACITY, LANES), lambda i, p: (0, 0, i, 0, 0)),
            pl.BlockSpec((2, 1, 8, rows), lambda i, p: (0, i, 0, 0)),
            pl.BlockSpec((2, 1, 8, rows), lambda i, p: (0, i, 0, 0)),
            whole((rows, width)),
            whole((padded, rows)),
        ],
        [
            struct(slot_shape + (width,), bf16),
            struct(slot_shape + (LANES,), f32),
            struct((2, half, 8, rows), f32),
            struct((2, half, 8, rows), f32),
            struct((rows, width), f32),
            struct((padded, rows), f32),
        ],
        scratch=[pltpu.VMEM((padded, rows), f32), pltpu.VMEM((padded, rows), f32)],
        us=20,
    )(place, att, w_out, tokens, tokens, routes, routes, gain, w_router, after)


def grad_dispatch_kernel(rank_ref, gate_ref, cot_ref, g_ref):
    local_experts = g_ref.shape[0]
    rows = cot_ref.shape[0] // 2
    for half in range(2):
        hits = hits_of(rank_ref[half], local_experts)
        gate = gate_ref[half]
        slot_gate = jnp.concatenate(
            [jnp.sum(jnp.where(hit, gate[j : j + 1, :], 0.0), axis=1, keepdims=True) for j, hit in enumerate(hits)],
            axis=0,
        )
        grads = (dot(chosen_of(hits), cot_ref[half * rows : (half + 1) * rows, :]) * slot_gate).astype(bf16)
        for j in range(local_experts):
            g_ref[j, half] = grads[j * CAPACITY : (j + 1) * CAPACITY]


def grad_dispatch(rank, gate, cotangents, local_experts):
    members, _, rows = rank.shape
    width = cotangents.shape[1]
    small = pl.BlockSpec((2, 8, rows), lambda j: (j, 0, 0))
    return call(
        grad_dispatch_kernel,
        (members // 2,),
        0,
        [small, small, pl.BlockSpec((2 * rows, width), lambda j: (j, 0))],
        pl.BlockSpec((local_experts, 2, CAPACITY, width), lambda j: (0, j, 0, 0)),
        struct((local_experts, members, CAPACITY, width), bf16),
        us=7,
    )(rank, gate, cotangents)


def expert_kernel(
    x_ref, gate_ref, w_gate_ref, w_up_ref, w_down_ref, forth_ref, active_ref, factor_ref, silu_ref
):
    gate_pre = dot(x_ref[0], w_gate_ref[0])
    up_pre = dot(x_ref[0], w_up_ref[0])
    sig = 1.0 / (1.0 + jnp.exp(-gate_pre))
    silu = gate_pre * sig
    silu_ref[0] = silu
    factor_ref[0] = up_pre * sig * (1.0 + gate_pre * (1.0 - sig))
    active_ref[0] = (silu * up_pre).astype(bf16)
    produced = dot_nt(active_ref[0], w_down_ref[0]).astype(bf16).astype(f32)
    forth_ref[0] = (produced * gate_ref[0, :, 0:1]).astype(bf16)


def run_experts(x, slot_gate, w_gate, w_up, w_down):
    count, slots, width = x.shape
    hidden = w_gate.shape[2]

    def per_expert(*shape):
        return pl.BlockSpec((1,) + shape, lambda e: (e, 0, 0))

    return call(
        expert_kernel,
        (count,),
        0,
        [per_expert(slots, width), per_expert(slots, LANES)] + [per_expert(width, hidden)] * 3,
        [per_expert(slots, width)] + [per_expert(slots, hidden)] * 3,
        [
            struct((count, slots, width), bf16),
            struct((count, slots, hidden), bf16),
            struct((count, slots, hidden), f32),
            struct((count, slots, hidden), f32),
        ],
        us=25,
    )(x, slot_gate, w_gate, w_up, w_down)


def expert_back_kernel(place_ref, *refs, fast):
    x_ref, g_ref, active_ref, factor_ref, silu_ref = refs[:5]
    w_gate_ref, w_up_ref, w_down_ref, back_ref, dots_ref = refs[5:10]
    grads, (gate_low_ref, up_low_ref) = refs[10:-2], refs[-2:]
    slots, width = g_ref.shape[1], g_ref.shape[2]
    chunk = 256
    active_grad = dot(g_ref[0], w_down_ref[0])
    gate_low_ref[...] = (active_grad * factor_ref[0]).astype(bf16)
    up_low_ref[...] = (active_grad * silu_ref[0]).astype(bf16)
    dots = jnp.sum(active_ref[0].astype(f32) * active_grad, axis=1, keepdims=True)
    dots_ref[0] = jnp.broadcast_to(dots, (slots, LANES))
    back_ref[0] = (dot_nt(gate_low_ref[...], w_gate_ref[0]) + dot_nt(up_low_ref[...], w_up_ref[0])).astype(bf16)

    def products(cols):
        x = x_ref[0, :, cols]
        yield 0, dot_tn(x, gate_low_ref[...]).astype(bf16)
        yield 1, dot_tn(x, up_low_ref[...]).astype(bf16)
        yield 2, dot_tn(g_ref[0, :, cols], active_ref[0]).astype(bf16)

    if fast:
        write_shards(place_ref, grads, products, width)
    else:

        def whole_columns(index, carry):
            cols = pl.ds(pl.multiple_of(index * chunk, chunk), chunk)
            for which, product in products(cols):
                grads[which][0, cols, :] = product
            return carry

        lax.fori_loop(0, width // chunk, whole_columns, 0)


def write_shards(place_ref, outs, products, width):
    send_a, keep_a, send_b, keep_b = outs
    x_bit, y_bit = place_ref[3], place_ref[4]
    shard = width // 4
    for dy in range(2):
        for dx in range(2):
            x, y = x_bit ^ dx, y_bit ^ dy
            cols = pl.ds(pl.multiple_of((y * 2 + x) * shard, shard), shard)
            for which, product in products(cols):
                side = product.shape[1] // 2
                (send_a if dx else keep_a)[0, which, y] = product[:, :side]
                (send_b if dy else keep_b)[0, which, x] = product[:, side:]


def run_experts_back(place, x, g, active, factor, silu, w_gate, w_up, w_down, first, count, fast):
    slots, width = g.shape[1], g.shape[2]
    hidden = w_gate.shape[2]

    def taken(*shape):
        return pl.BlockSpec((1,) + shape, lambda e, p: (e + first, 0, 0))

    def given(*shape):
        zeros = (0,) * len(shape)
        return pl.BlockSpec((1,) + shape, lambda e, p: (e,) + zeros)

    if fast:
        grad_shapes = [(3, 2, width // 4, hidden // 2)] * 4
    else:
        grad_shapes = [(width, hidden)] * 3
    return call(
        lambda *refs: expert_back_kernel(*refs, fast=fast),
        (count,),
        1,
        [taken(slots, width)] * 2 + [taken(slots, hidden)] * 3 + [taken(width, hidden)] * 3,
        [given(slots, width), given(slots, LANES)] + [given(*shape) for shape in grad_shapes],
        [struct((count, slots, width), bf16), struct((count, slots, LANES), f32)]
        + [struct((count,) + shape, bf16) for shape in grad_shapes],
        scratch=[pltpu.VMEM((slots, hidden), bf16)] * 2,
        us=10 * count,
    )(place, x, g, active, factor, silu, w_gate, w_up, w_down)


DOT_LANES = 2 * LANES


def combine_kernel(place_ref, rank_ref, *refs, pieces, with_dots, mine):
    parts, rest = refs[:pieces], refs[pieces:]
    rows = rank_ref.shape[2]
    local_experts = sum(part.shape[0] for part in parts)
    hits = hits_of(rank_ref[0], local_experts)
    gathered = jnp.concatenate([part[j, 0] for part in parts for j in range(part.shape[0])], axis=0)
    summed = dot_tn(chosen_of(hits), gathered)
    out_ref = rest[-1]
    if mine:
        arrived_ref = rest[-2]
        summed = summed + arrived_ref[0, 0:rows, :].astype(f32)
    out_ref[0, 0:rows, :] = summed.astype(bf16)
    if with_dots:
        column = [part[j, 0][:, 0:1] for part in rest[:pieces] for j in range(part.shape[0])]
        scattered = [
            jnp.sum(jnp.where(hit, value, 0.0), axis=0, keepdims=True) for hit, value in zip(hits, column)
        ]
        scattered.append(jnp.zeros((DOT_ROWS - local_experts, rows), f32))
        scattered = jnp.concatenate(scattered, axis=0)
        upper = scattered.astype(bf16)
        out_ref[0, rows:, :] = jnp.zeros((DOT_ROWS, out_ref.shape[2]), bf16)
        out_ref[0, rows:, 0:rows] = upper
        out_ref[0, rows:, DOT_LANES : DOT_LANES + rows] = (scattered - upper.astype(f32)).astype(bf16)
        if mine:
            out_ref[0, rows:, 2 * DOT_LANES : 4 * DOT_LANES] = arrived_ref[0, rows:, 0 : 2 * DOT_LANES]


def combine(place, rank, parts, dots=None, arrived=None):
    mine = arrived is not None
    rows, width = rank.shape[2], parts[0].shape[-1]
    out_rows = rows + (DOT_ROWS if dots else 0)

    def member(step, p):
        return (p[0] if mine else 1 - p[0]) * COLS + step

    def slots_of(array):
        return pl.BlockSpec((array.shape[0], 1) + array.shape[2:], lambda j, p: (0, member(j, p), 0, 0))

    inputs = [
        part.reshape(part.shape[0], 2 * COLS, CAPACITY, part.shape[-1]) for part in list(parts) + list(dots or [])
    ]
    in_specs = [pl.BlockSpec((1, 8, rows), lambda j, p: (member(j, p), 0, 0))] + [slots_of(item) for item in inputs]
    by_chip = pl.BlockSpec((1, out_rows, width), lambda j, p: (j, 0, 0))
    if mine:
        inputs.append(arrived)
        in_specs.append(by_chip)
    return call(
        lambda *refs: combine_kernel(*refs, pieces=len(parts), with_dots=bool(dots), mine=mine),
        (COLS,),
        1,
        in_specs,
        by_chip,
        struct((COLS, out_rows, width), bf16),
        us=6,
    )(place, rank, *inputs)


def split_dot(dimension_numbers, values, exact):
    upper = values.astype(bf16)
    lower = (values - upper.astype(f32)).astype(bf16)
    return lax.dot_general(
        upper, exact, dimension_numbers, preferred_element_type=f32
    ) + lax.dot_general(lower, exact, dimension_numbers, preferred_element_type=f32)


def middle_back_kernel(
    place_ref, sums_ref, gates_ref, middle_ref, cot_ref, gain_ref, w_router_ref, w_out_ref,
    grad_ref, branch_ref, attended_ref, small_ref
):
    rows = middle_ref.shape[0]
    tail = sums_ref[:, rows : rows + 8, 0 : 4 * DOT_LANES].astype(f32)
    mine = tail[:, :, 0:rows] + tail[:, :, DOT_LANES : DOT_LANES + rows]
    other = tail[:, :, 2 * DOT_LANES : 2 * DOT_LANES + rows] + tail[:, :, 3 * DOT_LANES : 3 * DOT_LANES + rows]
    first_row = place_ref[0] == 0
    dots = jnp.concatenate([jnp.where(first_row, mine, other), jnp.where(first_row, other, mine)], axis=0)
    dots = dots.reshape(dots.shape[0] * 8, rows)
    gates = gates_ref[...]
    logit_grad = dots - gates * jnp.sum(dots, axis=0, keepdims=True)
    middle = middle_ref[...]
    inverse = lax.rsqrt(jnp.mean(middle * middle, axis=1, keepdims=True) + epsilon)
    unit = middle * inverse
    gain = gain_ref[...]
    normed = (unit * gain).astype(bf16)
    grad = sums_ref[0, 0:rows].astype(f32)
    for index in range(1, sums_ref.shape[0]):
        grad = grad + sums_ref[index, 0:rows].astype(f32)
    grad = grad + split_dot(TN, logit_grad, w_router_ref[...])
    small_ref[...] = split_dot((((1,), (0,)), ((), ())), logit_grad, normed)
    small_ref[7:8, :] = jnp.sum(grad * unit, axis=0, keepdims=True)
    scaled = grad * gain
    middle_grad = cot_ref[...].astype(f32) + inverse * (
        scaled - unit * jnp.mean(scaled * unit, axis=1, keepdims=True)
    )
    grad_ref[...] = middle_grad
    branch_grad = middle_grad.astype(bf16)
    branch_ref[...] = branch_grad
    for member in range(w_out_ref.shape[0]):
        product = dot_nt(branch_grad, w_out_ref[member])
        attended_ref[member, :, 0:LANES] = product[:, 0:LANES].astype(bf16)
        attended_ref[member, :, LANES : LANES + HEAD_DIM] = product[:, LANES:].astype(bf16)
        attended_ref[member, :, LANES + HEAD_DIM :] = jnp.zeros((product.shape[0], HEAD_DIM), bf16)


def middle_back(place, sums, gates, middle, cotangent, gain, w_router, w_out):
    rows, width = middle.shape
    members = w_out.shape[0]
    args = (sums, gates, middle, cotangent, gain, w_router, w_out)
    return call(
        middle_back_kernel,
        (1,),
        1,
        [whole(item.shape) for item in args],
        [
            whole((rows, width)),
            whole((rows, width)),
            whole((members, rows, 2 * LANES)),
            whole(w_router.shape),
        ],
        [
            struct((rows, width), f32),
            struct((rows, width), bf16),
            struct((members, rows, 2 * LANES), bf16),
            struct(w_router.shape, f32),
        ],
        us=7,
    )(place, *args)


def input_grad_kernel(place_ref, grads_ref, w_ref, *rest):
    product = dot(grads_ref[...], w_ref[...])
    if len(rest) == 2:
        product = product + rest[0][0].astype(f32)
    rest[-1][0] = product.astype(bf16)


def input_grad(place, grads, w_stack, arrived=None):
    mine = arrived is not None
    total, lanes = grads.shape
    rows, width = total // (2 * COLS), w_stack.shape[1]

    def member(step, p):
        return (p[0] if mine else 1 - p[0]) * COLS + step

    by_chip = pl.BlockSpec((1, rows, width), lambda j, p: (j, 0, 0))
    return call(
        input_grad_kernel,
        (COLS,),
        1,
        [pl.BlockSpec((rows, lanes), lambda j, p: (member(j, p), 0)), whole(w_stack.shape)] + [by_chip] * mine,
        by_chip,
        struct((COLS, rows, width), bf16),
        us=5,
    )(place, grads, w_stack, *([arrived] if mine else []))


def own_weights_kernel(normed_ref, projected_ref, w_ref, gain_ref, out_ref, gain_grad_ref, sum_ref):
    step = pl.program_id(0)

    @pl.when(step == 0)
    def _():
        sum_ref[...] = jnp.zeros_like(sum_ref)

    sum_ref[...] += dot_tn(normed_ref[...], projected_ref[...])

    @pl.when(step == pl.num_programs(0) - 1)
    def _():
        total = sum_ref[...]
        out_ref[...] = total.astype(bf16)
        by_weight = jnp.sum(total * w_ref[...].astype(f32), axis=1, keepdims=True)
        gain_grad_ref[...] = jnp.broadcast_to(by_weight / gain_ref[...], gain_grad_ref.shape)


def own_weights(normed, projected, w_natural, gain):
    total, width = normed.shape
    lanes = projected.shape[1]
    rows = 512
    return call(
        own_weights_kernel,
        (total // rows,),
        0,
        [
            pl.BlockSpec((rows, width), lambda j: (j, 0)),
            pl.BlockSpec((rows, lanes), lambda j: (j, 0)),
            whole((width, lanes)),
            whole((width, 1)),
        ],
        [whole((width, lanes)), whole((width, 8))],
        [struct((width, lanes), bf16), struct((width, 8), f32)],
        scratch=[pltpu.VMEM((width, lanes), f32)],
        us=8,
    )(normed, projected, w_natural, gain)


def out_weights_kernel(place_ref, branch_ref, att_ref, own_ref, *refs, fast):
    outs, sum_ref = refs[:-1], refs[-1]
    step = pl.program_id(0)

    @pl.when(step == 0)
    def _():
        sum_ref[...] = jnp.zeros_like(sum_ref)

    sum_ref[...] += dot_tn(branch_ref[...], att_ref[...])

    @pl.when(step == pl.num_programs(0) - 1)
    def _():
        def products(cols):
            own = own_ref[cols, 0 : 2 * LANES]
            out_one = sum_ref[cols, 0:LANES].astype(bf16)
            out_two = sum_ref[cols, LANES:]
            low = lane_of(out_two.shape) < HEAD_DIM
            tail = jnp.where(low, out_two, own_ref[cols, 2 * LANES :].astype(f32)).astype(bf16)
            yield 0, jnp.concatenate([own, out_one, tail], axis=1)

        if fast:
            write_shards(place_ref, outs, products, own_ref.shape[0])
        else:
            outs[0][...] = next(products(slice(0, own_ref.shape[0])))[1]


def out_weights(place, branch, attended, own, fast):
    total, width = branch.shape
    rows = 512
    if fast:
        shapes = [(1, 1, 2, width // 4, 2 * LANES)] * 4
    else:
        shapes = [(width, 4 * LANES)]
    return call(
        lambda *refs: out_weights_kernel(*refs, fast=fast),
        (total // rows,),
        1,
        [
            pl.BlockSpec((rows, width), lambda j, p: (j, 0)),
            pl.BlockSpec((rows, 2 * LANES), lambda j, p: (j, 0)),
            whole(own.shape),
        ],
        [whole(shape) for shape in shapes],
        [struct(shape, bf16) for shape in shapes],
        scratch=[pltpu.VMEM((width, 2 * LANES), f32)],
        us=7,
    )(place, branch, attended, own)


def first_sum_kernel(place_ref, keep_a_ref, got_a_ref, keep_b_ref, got_b_ref, send_a_ref, held_a_ref, send_b_ref, held_b_ref):
    x_bit, y_bit = place_ref[3], place_ref[4]
    for bit, keep, got, send, held in (
        (y_bit, keep_a_ref, got_a_ref, send_a_ref, held_a_ref),
        (x_bit, keep_b_ref, got_b_ref, send_b_ref, held_b_ref),
    ):
        held[0, 0] = keep[0, 0, bit].astype(f32) + got[0, 0, bit].astype(f32)
        send[0, 0] = (keep[0, 0, 1 - bit].astype(f32) + got[0, 0, 1 - bit].astype(f32)).astype(bf16)


def first_sum(place, keep_a, got_a, keep_b, got_b):
    count, kinds, _, rows, cols = keep_a.shape
    taken = pl.BlockSpec((1, 1, 2, rows, cols), lambda e, k, p: (e, k, 0, 0, 0))
    given = pl.BlockSpec((1, 1, rows, cols), lambda e, k, p: (e, k, 0, 0))
    shape = (count, kinds, rows, cols)
    return call(
        first_sum_kernel,
        (count, kinds),
        1,
        [taken] * 4,
        [given] * 4,
        [struct(shape, bf16), struct(shape, f32), struct(shape, bf16), struct(shape, f32)],
        us=4 * count,
    )(place, keep_a, got_a, keep_b, got_b)


def last_sum_kernel(held_a_ref, got_a_ref, held_b_ref, got_b_ref, *rest):
    outs = rest[-3:]
    side = held_a_ref.shape[3]
    for which, out in enumerate(outs):
        out[0, :, :side] = held_a_ref[0, which] + got_a_ref[0, which].astype(f32)
        out[0, :, side:] = held_b_ref[0, which] + got_b_ref[0, which].astype(f32)


def last_sum(held_a, got_a, held_b, got_b, first, total, before):
    count, kinds, rows, cols = held_a.shape
    taken = pl.BlockSpec((1, kinds, rows, cols), lambda e: (e, 0, 0, 0))
    given = pl.BlockSpec((1, rows, 2 * cols), lambda e: (e + first, 0, 0))
    extra = list(before) if before else []
    return call(
        last_sum_kernel,
        (count,),
        0,
        [taken] * 4 + [pl.BlockSpec(memory_space=pl.ANY)] * len(extra),
        [given] * 3,
        [struct((total, rows, 2 * cols), f32)] * 3,
        us=2.5 * count,
        aliases={4 + i: i for i in range(len(extra))},
    )(held_a, got_a, held_b, got_b, *extra)


SWAP = [(0, 1), (1, 0)]


def after(value, *events):
    return lax.optimization_barrier((value,) + events)[0]


def gather_group(block):
    return lax.all_gather(block, ("row", "col"), axis=0, tiled=True)


def flip(value, axis, bit, size):
    return lax.ppermute(value, axis, [(i, i ^ (1 << bit)) for i in range(size)])


def bits_of(size):
    return size.bit_length() - 1


def own_bit(axis, bit):
    return (lax.axis_index(axis) >> bit) & 1


def joined(mine, got, own):
    return jnp.where(own == 0, jnp.concatenate([mine, got]), jnp.concatenate([got, mine]))


def cube_gather(value, axis, size):
    value = value[None]
    for bit in range(bits_of(size)):
        value = joined(value, flip(value, axis, bit, size), own_bit(axis, bit))
    return value


def sum_group_then(value, sizes):
    for axis, bit in (("row", 0), ("col", 0), ("col", 1)):
        pair = value.reshape((2, value.shape[0] // 2) + value.shape[1:])
        own = own_bit(axis, bit)
        keep = lax.dynamic_index_in_dim(pair, own, 0, keepdims=False)
        send = lax.dynamic_index_in_dim(pair, 1 - own, 0, keepdims=False)
        value = keep + flip(send, axis, bit, sizes[axis])
    return value


def sum_group(value, sizes):
    for axis, bit in (("row", 0), ("col", 0), ("col", 1)):
        value = value + flip(value, axis, bit, sizes[axis])
    return value


def sum_dp(value, sizes):
    for bit in range(bits_of(sizes["dp"])):
        value = value + flip(value, "dp", bit, sizes["dp"])
    return value


def gather_rows_back(value, sizes):
    for axis, bit in (("col", 1), ("col", 0), ("row", 0)):
        value = joined(value, flip(value, axis, bit, sizes[axis]), own_bit(axis, bit))
    return value


def reduce_over_dp(value, size):
    count = bits_of(size)
    value = value.reshape(value.shape[:1] + (2,) * count + value.shape[2:])
    current = value
    for bit in range(count - 1, -1, -1):
        own = own_bit("dp", bit)
        keep = lax.dynamic_index_in_dim(current, own, 1, keepdims=False)
        send = lax.dynamic_index_in_dim(current, 1 - own, 1, keepdims=False).astype(bf16)
        current = keep.astype(f32) + flip(send, "dp", bit, size).astype(f32)
    return current


def start_move(run, size):
    return flip(run[0], "dp", 0, size), flip(run[2], "dp", 1, size)


def first_half(place, run, got, size, event):
    keep_a, keep_b = after((run[1], run[3]), event)
    send_a, held_a, send_b, held_b = first_sum(place, keep_a, got[0], keep_b, got[1])
    return held_a, flip(send_a, "dp", 1, size), held_b, flip(send_b, "dp", 0, size)


def layer(sizes):
    n_dp, n_row, n_col = sizes["dp"], sizes["row"], sizes["col"]
    members = n_row * n_col
    fast = n_dp == 4
    assert n_row == 2 and n_col == COLS and n_dp & (n_dp - 1) == 0

    def local(
        tokens, cotangent, routes, lengths, gain_attn, w_query, w_key, w_value, w_out,
        gain_moe, w_router, w_gate, w_up, w_down,
    ):
        rows, width = tokens.shape
        group = rows * members
        local_experts = w_gate.shape[0]
        row, col, dp = lax.axis_index("row"), lax.axis_index("col"), lax.axis_index("dp")
        place = jnp.stack([row, col, row * n_col + col, dp & 1, (dp >> 1) & 1]).astype(jnp.int32)
        gain_one = gain_attn.astype(f32)[None]
        gain_two = gain_moe.astype(f32)[None]

        tok_all = gather_group(tokens)
        share = rows // n_dp
        w_out_share = lax.dynamic_slice(w_out.T, (dp * share, 0), (share, width))
        w_out_all = cube_gather(w_out_share, "col", n_col)
        w_out_all = cube_gather(w_out_all, "dp", n_dp)
        w_out_all = cube_gather(w_out_all, "row", n_row)
        w_out_all = jnp.transpose(w_out_all, (0, 2, 1, 3, 4)).reshape(members, rows, width)
        route_rows = jnp.zeros((ROUTE_ROWS, 2 * LANES), bf16)
        route_rows = lax.dynamic_update_slice(route_rows, routes.T.astype(bf16), (0, 0))
        route_rows = cube_gather(cube_gather(route_rows, "col", n_col), "row", n_row)
        route_rows = route_rows.reshape(members, ROUTE_ROWS, 2 * LANES)
        w_stack = jnp.concatenate([w_query.T, w_key.T, w_value.T, w_value.T], axis=0)
        w_natural = jnp.concatenate([w_query, w_key, w_value, w_value], axis=1)

        ends = jnp.cumsum(lengths[0])
        starts = ends - lengths[0]
        position = jnp.arange(group, dtype=jnp.int32)
        segment = jnp.sum((position[:, None] >= ends[None, :]).astype(jnp.int32), axis=1)
        member = segment[:, None] == jnp.arange(starts.shape[0], dtype=jnp.int32)[None, :]
        start = jnp.sum(jnp.where(member, starts[None, :], 0), axis=1).astype(jnp.int32)
        frequency = rope_base ** (-2.0 * jnp.arange(HEAD_DIM // 2, dtype=f32) / HEAD_DIM)
        angle = (position - start).astype(f32)[:, None] * frequency[None, :]
        cosine = jnp.tile(jnp.cos(angle), (1, 4))
        sine = jnp.tile(jnp.sin(angle), (1, 4))

        query, key, value, normed_one = project(tok_all, after(gain_one, w_out_all, route_rows), w_stack, cosine, sine)
        w_router_rows = w_router.T.reshape(members, local_experts, width)
        w_router_rows = jnp.pad(w_router_rows, ((0, 0), (0, 8 - local_experts), (0, 0)))
        w_router_rows = w_router_rows.reshape(members * 8, width)
        packed, attended, totals = attend(query, key, value, start[:, None])
        att_flat = gather_group(packed)
        att_all = att_flat.reshape((members,) + packed.shape)
        cot_all = gather_group(after(cotangent, att_flat))
        x, slot_gate, rank, gate, middle, gates = middle_and_dispatch(
            place, att_all, w_out_all, tok_all, route_rows, gain_two, w_router_rows, local_experts
        )
        slots = members * CAPACITY
        x = x.reshape(local_experts, slots, width)
        slot_gate = slot_gate.reshape(local_experts, slots, LANES)
        rank, gate = rank.reshape(members, 8, rows), gate.reshape(members, 8, rows)
        forth, active, factor, silu = run_experts(x, slot_gate, w_gate, w_up, w_down)
        forth_other = combine(place, rank, [forth])
        arrived = lax.ppermute(forth_other, "row", SWAP)
        g = grad_dispatch(after(rank, forth_other), gate, cot_all, local_experts)
        g = g.reshape(local_experts, slots, width)
        cuts = [0, 1, 3, local_experts]

        def backward(which, x):
            first, last = cuts[which], cuts[which + 1]
            return run_experts_back(place, x, g, active, factor, silu, w_gate, w_up, w_down, first, last - first, fast)

        runs = [backward(0, x)]
        forth_mine = combine(place, rank, [forth], arrived=after(arrived, runs[0][1]))
        forth_sums = lax.all_to_all(forth_mine, "col", 0, 0, tiled=True)
        runs.append(backward(1, after(x, forth_mine)))
        runs.append(backward(2, after(x, runs[1][1])))
        moved = [start_move(run[2:], n_dp) for run in runs] if fast else []
        back_parts, dot_parts = [run[0] for run in runs], [run[1] for run in runs]
        back_other = combine(place, after(rank, *moved[0]) if fast else rank, back_parts, dot_parts)
        arrived = lax.ppermute(back_other, "row", SWAP)
        back_mine = combine(place, rank, back_parts, dot_parts, arrived)
        back_mine = after(back_mine, forth_sums)
        back_sums = lax.all_to_all(back_mine, "col", 0, 0, tiled=True)
        started, gate_middle = [], []
        if fast:
            started.append(first_half(place, runs[0][2:], moved[0], n_dp, back_mine))
            gate_middle += [started[0][0], *moved[1]]

        middle_grad, branch_grad, attended_grad, small = middle_back(
            place, back_sums, gates, middle, cotangent, after(gain_two, *gate_middle), w_router_rows, w_out_all
        )
        if fast:
            started.append(first_half(place, runs[1][2:], moved[1], n_dp, branch_grad))
        attended_grad = lax.all_to_all(attended_grad, ("row", "col"), 0, 0, tiled=True)
        branch_all = gather_group(branch_grad)

        start_row = jnp.broadcast_to(start[None, :], (8, group))
        attended_grad = attended_grad.reshape(group, 2 * LANES)
        if fast:
            attended_grad = after(attended_grad, started[1][0])
        projected_grad = attend_back(query, key, value, attended_grad, totals, start_row, cosine, sine)
        in_other = input_grad(place, projected_grad, w_stack)
        arrived = lax.ppermute(in_other, "row", SWAP)
        if fast:
            started.append(first_half(place, runs[2][2:], moved[2], n_dp, in_other))
        in_mine = input_grad(place, projected_grad, w_stack, arrived)
        in_sums = lax.all_to_all(in_mine, "col", 0, 0, tiled=True)
        small = gather_rows_back(sum_group_then(after(small, in_mine), sizes), sizes)
        own_grads, gain_part = own_weights(
            after(normed_one, in_mine, branch_all), projected_grad, w_natural, gain_attn.astype(f32)[:, None]
        )
        gain_attn_grad = sum_group(gain_part[:, 0].reshape(8, width // 8), sizes)
        w_parts = out_weights(place, branch_all, attended, own_grads, fast)
        if fast:
            w_started = first_half(place, w_parts, start_move(w_parts, n_dp), n_dp, w_parts[1])
        else:
            cut = w_parts[0].reshape(1, n_dp, width // n_dp, w_parts[0].shape[1])
            w_sum = reduce_over_dp(cut, n_dp)[0]

        mixed = (middle + jnp.sum(after(forth_sums, projected_grad).astype(f32), axis=0)).astype(bf16)

        used = small.reshape(members, 8, width)[:, : local_experts].reshape(members * local_experts, width)
        both = jnp.concatenate([used, small[7:8], gain_attn_grad.reshape(1, width)], axis=0)
        both = sum_dp(after(both, w_parts[0]), sizes)
        w_router_grad = both[: members * local_experts].T
        gain_moe_grad, gain_attn_grad = both[members * local_experts], both[members * local_experts + 1]

        normed_grad = jnp.sum(in_sums.astype(f32), axis=0)
        resid = tokens.astype(f32)
        inverse = lax.rsqrt(jnp.mean(resid * resid, axis=1, keepdims=True) + epsilon)
        unit = resid * inverse
        scaled = normed_grad * gain_one
        tokens_grad = middle_grad + inverse * (
            scaled - unit * jnp.mean(scaled * unit, axis=1, keepdims=True)
        )

        if fast:
            expert_grads = None
            for which, event in enumerate((in_mine, own_grads, w_parts[0])):
                held_a, got_a, held_b, got_b = started[which]
                held_a, held_b = after((held_a, held_b), event)
                expert_grads = last_sum(held_a, got_a, held_b, got_b, cuts[which], local_experts, expert_grads)
            held_a, got_a, held_b, got_b = [item[0, 0] for item in w_started]
            left = held_a + got_a.astype(f32)
            right = held_b + got_b.astype(f32)
            w_sum = jnp.concatenate([left, right], axis=1)
        else:
            expert_grads = []
            for which in range(3):
                parts = [run[2 + which] for run in runs]
                parts = [part.reshape(part.shape[0], n_dp, width // n_dp, part.shape[2]) for part in parts]
                expert_grads.append(jnp.concatenate([reduce_over_dp(part, n_dp) for part in parts], axis=0))
        w_gate_grad, w_up_grad, w_down_grad = expert_grads
        local_q, local_k = w_query.shape[1], w_key.shape[1]
        cut = local_q + local_k
        return (
            mixed, tokens_grad, gain_attn_grad, w_sum[:, :local_q], w_sum[:, local_q:cut],
            w_sum[:, cut + local_q :], w_sum[:, cut : cut + local_q],
            gain_moe_grad, w_router_grad, w_gate_grad, w_up_grad, w_down_grad,
        )

    return local


def solution(mesh):
    return jax.shard_map(
        layer(dict(mesh.shape)),
        mesh=mesh,
        in_specs=(
            P(("dp", "row", "col"), None),
            P(("dp", "row", "col"), None),
            P(("dp", "row", "col"), None),
            P("dp", None),
            P(),
            P(None, ("row", "col")),
            P(None, ("row", "col")),
            P(None, ("row", "col")),
            P(None, ("row", "col")),
            P(),
            P(),
            P(("row", "col"), None, None),
            P(("row", "col"), None, None),
            P(("row", "col"), None, None),
        ),
        out_specs=(
            P(("dp", "row", "col"), None),
            P(("dp", "row", "col"), None),
            P(),
            P("dp", ("row", "col")),
            P("dp", ("row", "col")),
            P("dp", ("row", "col")),
            P("dp", ("row", "col")),
            P(),
            P(),
            P(("row", "col"), "dp", None),
            P(("row", "col"), "dp", None),
            P(("row", "col"), "dp", None),
        ),
        check_vma=False,
    )
```

```python
import math

import jax
import jax.numpy as jnp
from jax import lax
from jax.experimental import pallas as pl
from jax.experimental.pallas import tpu as pltpu
from jax.sharding import PartitionSpec as P

HEAD_DIM = 64
EXPERTS = 40
TOP = 8
CAPACITY = 64
COLS = 4
LANES = 128
QUERY_BLOCK = 256
ROUTE_ROWS = 16
DOT_ROWS = 16

epsilon = 1e-06
rope_base = 10000.0
masked_score = -1e30
f32 = jnp.float32
bf16 = jnp.bfloat16
VMEM_LIMIT = 56 * 1024 * 1024

NT = (((1,), (1,)), ((), ()))
TN = (((0,), (0,)), ((), ()))


def dot(a, b):
    return jnp.dot(a, b, preferred_element_type=f32)


def dot_nt(a, b):
    return lax.dot_general(a, b, NT, preferred_element_type=f32)


def dot_tn(a, b):
    return lax.dot_general(a, b, TN, preferred_element_type=f32)


def lane_of(shape):
    return lax.broadcasted_iota(jnp.int32, shape, len(shape) - 1)


def call(
    kernel, grid, prefetch, in_specs, out_specs, out_shape, scratch=(), us=1.0, aliases=None
):
    return pl.pallas_call(
        kernel,
        grid_spec=pltpu.PrefetchScalarGridSpec(
            num_scalar_prefetch=prefetch,
            grid=grid,
            in_specs=in_specs,
            out_specs=out_specs,
            scratch_shapes=list(scratch),
        ),
        out_shape=out_shape,
        input_output_aliases=aliases or {},
        compiler_params=pltpu.CompilerParams(
            vmem_limit_bytes=VMEM_LIMIT, dimension_semantics=("arbitrary",) * len(grid)
        ),
        cost_estimate=pl.CostEstimate(
            flops=int(us * 1.1e9), bytes_accessed=int(us * 3.6e6), transcendentals=0
        ),
    )


def whole(shape):
    zeros = (0,) * len(shape)
    return pl.BlockSpec(shape, lambda *_: zeros)


def struct(shape, dtype):
    return jax.ShapeDtypeStruct(shape, dtype)


def turn_within_heads(values, sign):
    lane = lane_of(values.shape) % HEAD_DIM
    ahead = pltpu.roll(values, LANES - HEAD_DIM // 2, 1)
    behind = pltpu.roll(values, HEAD_DIM // 2, 1)
    return jnp.where(lane < HEAD_DIM // 2, -sign * ahead, sign * behind)


def project_kernel(
    tok_ref, gain_ref, w_ref, cos_ref, sin_ref, query_ref, key_ref, value_ref, normed_ref
):
    resid = tok_ref[...].astype(f32)
    inverse = lax.rsqrt(jnp.mean(resid * resid, axis=1, keepdims=True) + epsilon)
    normed = (resid * inverse * gain_ref[...]).astype(bf16)
    normed_ref[...] = normed
    raw = dot_nt(normed, w_ref[...])
    cosine, sine = cos_ref[...], sin_ref[...]

    def rot(values):
        return (values * cosine + turn_within_heads(values, 1.0) * sine).astype(bf16).astype(f32)

    first = rot(raw[:, :LANES])
    second = rot(raw[:, LANES : 2 * LANES])
    low = lane_of(first.shape) < HEAD_DIM
    scale = 1.0 / math.sqrt(HEAD_DIM)
    query_ref[0] = jnp.where(low, first * scale, 0.0).astype(bf16)
    query_ref[1] = jnp.where(low, 0.0, first * scale).astype(bf16)
    query_ref[2] = jnp.where(low, second * scale, 0.0).astype(bf16)
    key_ref[...] = jnp.where(low, pltpu.roll(second, HEAD_DIM, 1), second).astype(bf16)
    value_ref[...] = raw[:, 2 * LANES :].astype(bf16)


def project(tokens, gain, w_stack, cosine, sine):
    total, width = tokens.shape
    rows = 512
    lanes = pl.BlockSpec((rows, LANES), lambda j: (j, 0))
    wide = pl.BlockSpec((rows, width), lambda j: (j, 0))
    return call(
        project_kernel,
        (total // rows,),
        0,
        [wide, whole((1, width)), whole(w_stack.shape), lanes, lanes],
        [pl.BlockSpec((3, rows, LANES), lambda j: (0, j, 0)), lanes, lanes, wide],
        [
            struct((3, total, LANES), bf16),
            struct((total, LANES), bf16),
            struct((total, LANES), bf16),
            struct((total, width), bf16),
        ],
        us=9,
    )(tokens, gain, w_stack, cosine, sine)


def attend_kernel(query_ref, key_ref, value_ref, start_ref, packed_ref, plain_ref, total_ref, out_ref):
    blocks = query_ref.shape[1] // QUERY_BLOCK
    block = pl.program_id(0)
    for index in range(blocks):

        @pl.when(block == index)
        def _(index=index):
            rows = pl.ds(index * QUERY_BLOCK, QUERY_BLOCK)
            span = (index + 1) * QUERY_BLOCK
            row = index * QUERY_BLOCK + lax.broadcasted_iota(jnp.int32, (QUERY_BLOCK, span), 0)
            column = lane_of((QUERY_BLOCK, span))
            allowed = (column <= row) & (column >= start_ref[rows, :])

            def head(number, carry):
                scores = dot_nt(query_ref[number, rows, :], key_ref[0:span, :])
                scores = jnp.where(allowed, scores, masked_score)
                peak = jnp.max(scores, axis=1, keepdims=True)
                weights = jnp.exp(scores - peak)
                summed = jnp.sum(weights, axis=1, keepdims=True)
                probs = (weights * (1.0 / summed)).astype(bf16)
                out_ref[number] = dot(probs, value_ref[0:span, :])
                total = jnp.broadcast_to(peak + jnp.log(summed), (QUERY_BLOCK, LANES))
                total_ref[number, :, rows] = jnp.transpose(total)[0:8, :]
                return carry

            lax.fori_loop(0, 3, head, 0)
            low = lane_of((QUERY_BLOCK, LANES)) < HEAD_DIM
            one, two, three = out_ref[0], out_ref[1], out_ref[2]
            pair = jnp.where(low, one, two).astype(bf16)
            plain_ref[rows, 0:LANES] = pair
            plain_ref[rows, LANES : 2 * LANES] = jnp.where(low, three, 0.0).astype(bf16)
            if index < blocks // 2:
                packed_ref[rows, 0:LANES] = pair
                packed_ref[rows, LANES : 2 * LANES] = three.astype(bf16)
            else:
                back = pl.ds((index - blocks // 2) * QUERY_BLOCK, QUERY_BLOCK)
                before = packed_ref[back, LANES : 2 * LANES].astype(f32)
                packed_ref[back, LANES : 2 * LANES] = jnp.where(low, before, one).astype(bf16)
                packed_ref[back, 2 * LANES : 3 * LANES] = jnp.where(low, two, three).astype(bf16)


def attend(query, key, value, start):
    total = key.shape[0]
    return call(
        attend_kernel,
        (total // QUERY_BLOCK,),
        0,
        [whole(query.shape), whole(key.shape), whole(value.shape), whole(start.shape)],
        [whole((total // 2, 3 * LANES)), whole((total, 2 * LANES)), whole((3, 8, total))],
        [
            struct((total // 2, 3 * LANES), bf16),
            struct((total, 2 * LANES), bf16),
            struct((3, 8, total), f32),
        ],
        scratch=[pltpu.VMEM((3, QUERY_BLOCK, LANES), f32)],
        us=18,
    )(query, key, value, start)


def attend_back_kernel(
    query_ref, key_ref, value_ref, grad_ref, total_ref, start_ref, cos_ref, sin_ref,
    out_ref, query_grad_ref, key_grad_ref, value_grad_ref
):
    blocks = query_ref.shape[1] // QUERY_BLOCK
    block = pl.program_id(0)
    scale = 1.0 / math.sqrt(HEAD_DIM)

    @pl.when(block == 0)
    def _():
        key_grad_ref[...] = jnp.zeros_like(key_grad_ref)
        value_grad_ref[...] = jnp.zeros_like(value_grad_ref)

    def back(values, cosine, sine):
        return values * cosine + turn_within_heads(values * sine, -1.0)

    for index in range(blocks):

        @pl.when(block == index)
        def _(index=index):
            rows = pl.ds(index * QUERY_BLOCK, QUERY_BLOCK)
            span = (index + 1) * QUERY_BLOCK
            row = index * QUERY_BLOCK + lane_of((span, QUERY_BLOCK))
            column = lax.broadcasted_iota(jnp.int32, (span, QUERY_BLOCK), 0)
            allowed = (column <= row) & (column >= start_ref[0:1, rows])
            low = lane_of((QUERY_BLOCK, LANES)) < HEAD_DIM

            def head(number, carry):
                query = query_ref[number, rows, :]
                tile = pl.multiple_of((number // 2) * LANES, LANES)
                upstream = grad_ref[rows, pl.ds(tile, LANES)].astype(f32)
                keep = low == (number != 1)
                upstream = jnp.where(keep, upstream, 0.0).astype(bf16)
                scores = dot_nt(key_ref[0:span, :], query)
                probs = jnp.exp(scores - total_ref[number, 0:1, rows])
                probs = jnp.where(allowed, probs, 0.0)
                prob_grad = dot_nt(value_ref[0:span, :], upstream)
                row_dot = jnp.sum(probs * prob_grad, axis=0, keepdims=True)
                score_grad = (probs * (prob_grad - row_dot)).astype(bf16)
                key_grad_ref[0:span, :] += dot(score_grad, query)
                value_grad_ref[0:span, :] += dot(probs.astype(bf16), upstream)
                query_grad_ref[number] = dot_tn(score_grad, key_ref[0:span, :]) * scale
                return carry

            lax.fori_loop(0, 3, head, 0)
            cosine, sine = cos_ref[rows, :], sin_ref[rows, :]
            pair = jnp.where(low, query_grad_ref[0], query_grad_ref[1])
            out_ref[rows, 0:LANES] = back(pair, cosine, sine).astype(bf16)
            out_ref[rows, LANES : 2 * LANES] = back(query_grad_ref[2], cosine, sine).astype(bf16)

    @pl.when(block == blocks - 1)
    def _():
        low = lane_of(key_grad_ref.shape) < HEAD_DIM
        key_grad = key_grad_ref[...]
        key_grad = key_grad + pltpu.roll(key_grad, HEAD_DIM, 1)
        key_grad = back(key_grad, cos_ref[...], sin_ref[...])
        before = out_ref[:, LANES : 2 * LANES].astype(f32)
        out_ref[:, LANES : 2 * LANES] = jnp.where(low, before, key_grad).astype(bf16)
        value_grad = value_grad_ref[...]
        value_grad = value_grad + pltpu.roll(value_grad, HEAD_DIM, 1)
        out_ref[:, 2 * LANES : 3 * LANES] = jnp.where(low, 0.0, value_grad).astype(bf16)


def attend_back(query, key, value, grad, totals, start, cosine, sine):
    total = key.shape[0]
    args = (query, key, value, grad, totals, start, cosine, sine)
    return call(
        attend_back_kernel,
        (total // QUERY_BLOCK,),
        0,
        [whole(item.shape) for item in args],
        whole((total, 3 * LANES)),
        struct((total, 3 * LANES), bf16),
        scratch=[
            pltpu.VMEM((3, QUERY_BLOCK, LANES), f32),
            pltpu.VMEM((total, LANES), f32),
            pltpu.VMEM((total, LANES), f32),
        ],
        us=0,
    )(*args)


def branch_operand(refs):
    rows = refs.shape[1]
    low = lane_of((rows, LANES)) < HEAD_DIM
    pairs, thirds = [], []
    for member in range(refs.shape[0]):
        one = refs[member, :, 0:LANES]
        mid = refs[member, :, LANES : 2 * LANES].astype(f32)
        end = refs[member, :, 2 * LANES : 3 * LANES].astype(f32)
        mid_turned = pltpu.roll(mid, HEAD_DIM, 1)
        end_turned = pltpu.roll(end, HEAD_DIM, 1)
        late = jnp.where(low, mid_turned, end_turned).astype(bf16)
        pairs.append(jnp.concatenate([one, late], axis=0))
        thirds.append((mid, end_turned))
    for member in range(0, refs.shape[0], 2):
        tops = []
        for which in range(2):
            left, right = thirds[member][which], thirds[member + 1][which]
            tops.append(jnp.where(low, left, pltpu.roll(right, HEAD_DIM, 1)).astype(bf16))
        pairs.append(jnp.concatenate(tops, axis=0))
    return jnp.concatenate(pairs, axis=1)


def hits_of(rank, local_experts):
    place = lax.broadcasted_iota(jnp.int32, (CAPACITY, rank.shape[1]), 0).astype(f32)
    return [place == rank[j : j + 1, :] for j in range(local_experts)]


def chosen_of(hits):
    return jnp.concatenate([jnp.where(hit, 1.0, 0.0).astype(bf16) for hit in hits], axis=0)


def middle_kernel(
    place_ref, att_ref, w_out_ref, tok_a_ref, tok_b_ref, routes_a_ref, routes_b_ref,
    gain_ref, w_router_ref, after_ref,
    x_ref, slot_gate_ref, rank_ref, gate_ref, middle_ref, gates_own_ref, gates_ref, ranks_ref
):
    step = pl.program_id(0)
    member = place_ref[2]
    cols = pl.num_programs(0)
    rows = tok_a_ref.shape[0]
    local_experts = x_ref.shape[0]
    members = w_out_ref.shape[0]
    right = [w_out_ref[source, 0:LANES] for source in range(members)]
    right += [w_out_ref[source, LANES:] for source in range(members)]
    branch = dot(branch_operand(att_ref), jnp.concatenate(right, axis=0))
    for half in range(2):
        tok_ref, routes_ref = ((tok_a_ref, routes_a_ref), (tok_b_ref, routes_b_ref))[half]
        middle = tok_ref[...].astype(f32) + branch[half * rows : (half + 1) * rows]
        inverse = lax.rsqrt(jnp.mean(middle * middle, axis=1, keepdims=True) + epsilon)
        normed = (middle * inverse * gain_ref[...]).astype(bf16)
        logits = dot_nt(w_router_ref[...], normed)
        padded = logits.shape[0]
        slot = lax.broadcasted_iota(jnp.int32, (padded, rows), 0)
        expert = (slot // 8) * local_experts + slot % 8
        expert = jnp.where(slot % 8 < local_experts, expert, -1).astype(f32)
        routes = routes_ref[0].astype(f32)
        named = expert == routes[0:1, 0:rows]
        for k in range(1, TOP):
            named = named | (expert == routes[k : k + 1, 0:rows])
        peak = jnp.max(jnp.where(named, logits, masked_score), axis=0, keepdims=True)
        weights = jnp.where(named, jnp.exp(logits - peak), 0.0)
        gates = weights / jnp.sum(weights, axis=0, keepdims=True)
        gates_ref[...] = gates
        ranks_ref[...] = jnp.where(named, dot(named.astype(f32).astype(bf16), after_ref[...]), -1.0)
        here = pl.ds(pl.multiple_of(member * 8, 8), 8)
        gate, rank = gates_ref[here, :], ranks_ref[here, :]
        rank_ref[half, 0] = rank
        gate_ref[half, 0] = gate
        hits = hits_of(rank, local_experts)
        slot_gate = jnp.concatenate(
            [jnp.sum(jnp.where(hit, gate[j : j + 1, :], 0.0), axis=1, keepdims=True) for j, hit in enumerate(hits)],
            axis=0,
        )
        chosen = chosen_of(hits)
        picked = dot(chosen, normed).astype(bf16)
        spread = jnp.broadcast_to(slot_gate, (slot_gate.shape[0], LANES))
        for j in range(local_experts):
            part = slice(j * CAPACITY, (j + 1) * CAPACITY)
            x_ref[j, half, 0] = picked[part]
            slot_gate_ref[j, half, 0] = spread[part]

        @pl.when(member == half * cols + step)
        def _(middle=middle, gates=gates):
            middle_ref[...] = middle
            gates_own_ref[...] = gates


def middle_and_dispatch(place, att, w_out, tokens, routes, gain, w_router, local_experts):
    width = tokens.shape[1]
    half = COLS
    rows = tokens.shape[0] // (2 * half)
    padded = w_router.shape[0]
    after = (jnp.arange(rows)[:, None] < jnp.arange(rows)[None, :]).astype(bf16)
    slot_shape = (local_experts, 2, half, CAPACITY)
    early = pl.BlockSpec((rows, width), lambda i, p: (i, 0))
    late = pl.BlockSpec((rows, width), lambda i, p: (i + half, 0))
    routes_shape = (1,) + routes.shape[1:]
    return call(
        middle_kernel,
        (half,),
        1,
        [
            pl.BlockSpec((att.shape[0], rows, 3 * LANES), lambda i, p: (0, i, 0)),
            whole(w_out.shape),
            early,
            late,
            pl.BlockSpec(routes_shape, lambda i, p: (i, 0, 0)),
            pl.BlockSpec(routes_shape, lambda i, p: (i + half, 0, 0)),
            whole((1, width)),
            whole(w_router.shape),
            whole((rows, rows)),
        ],
        [
            pl.BlockSpec((local_experts, 2, 1, CAPACITY, width), lambda i, p: (0, 0, i, 0, 0)),
            pl.BlockSpec((local_experts, 2, 1, CAPACITY, LANES), lambda i, p: (0, 0, i, 0, 0)),
            pl.BlockSpec((2, 1, 8, rows), lambda i, p: (0, i, 0, 0)),
            pl.BlockSpec((2, 1, 8, rows), lambda i, p: (0, i, 0, 0)),
            whole((rows, width)),
            whole((padded, rows)),
        ],
        [
            struct(slot_shape + (width,), bf16),
            struct(slot_shape + (LANES,), f32),
            struct((2, half, 8, rows), f32),
            struct((2, half, 8, rows), f32),
            struct((rows, width), f32),
            struct((padded, rows), f32),
        ],
        scratch=[pltpu.VMEM((padded, rows), f32), pltpu.VMEM((padded, rows), f32)],
        us=20,
    )(place, att, w_out, tokens, tokens, routes, routes, gain, w_router, after)


def grad_dispatch_kernel(rank_ref, gate_ref, cot_ref, g_ref):
    local_experts = g_ref.shape[0]
    rows = cot_ref.shape[0] // 2
    for half in range(2):
        hits = hits_of(rank_ref[half], local_experts)
        gate = gate_ref[half]
        slot_gate = jnp.concatenate(
            [jnp.sum(jnp.where(hit, gate[j : j + 1, :], 0.0), axis=1, keepdims=True) for j, hit in enumerate(hits)],
            axis=0,
        )
        grads = (dot(chosen_of(hits), cot_ref[half * rows : (half + 1) * rows, :]) * slot_gate).astype(bf16)
        for j in range(local_experts):
            g_ref[j, half] = grads[j * CAPACITY : (j + 1) * CAPACITY]


def grad_dispatch(rank, gate, cotangents, local_experts):
    members, _, rows = rank.shape
    width = cotangents.shape[1]
    small = pl.BlockSpec((2, 8, rows), lambda j: (j, 0, 0))
    return call(
        grad_dispatch_kernel,
        (members // 2,),
        0,
        [small, small, pl.BlockSpec((2 * rows, width), lambda j: (j, 0))],
        pl.BlockSpec((local_experts, 2, CAPACITY, width), lambda j: (0, j, 0, 0)),
        struct((local_experts, members, CAPACITY, width), bf16),
        us=7,
    )(rank, gate, cotangents)


def expert_kernel(
    x_ref, gate_ref, w_gate_ref, w_up_ref, w_down_ref, forth_ref, active_ref, factor_ref, silu_ref
):
    gate_pre = dot(x_ref[0], w_gate_ref[0])
    up_pre = dot(x_ref[0], w_up_ref[0])
    sig = 1.0 / (1.0 + jnp.exp(-gate_pre))
    silu = gate_pre * sig
    silu_ref[0] = silu
    factor_ref[0] = up_pre * sig * (1.0 + gate_pre * (1.0 - sig))
    active_ref[0] = (silu * up_pre).astype(bf16)
    produced = dot_nt(active_ref[0], w_down_ref[0]).astype(bf16).astype(f32)
    forth_ref[0] = (produced * gate_ref[0, :, 0:1]).astype(bf16)


def run_experts(x, slot_gate, w_gate, w_up, w_down):
    count, slots, width = x.shape
    hidden = w_gate.shape[2]

    def per_expert(*shape):
        return pl.BlockSpec((1,) + shape, lambda e: (e, 0, 0))

    return call(
        expert_kernel,
        (count,),
        0,
        [per_expert(slots, width), per_expert(slots, LANES)] + [per_expert(width, hidden)] * 3,
        [per_expert(slots, width)] + [per_expert(slots, hidden)] * 3,
        [
            struct((count, slots, width), bf16),
            struct((count, slots, hidden), bf16),
            struct((count, slots, hidden), f32),
            struct((count, slots, hidden), f32),
        ],
        us=25,
    )(x, slot_gate, w_gate, w_up, w_down)


def expert_back_kernel(place_ref, *refs, fast):
    x_ref, g_ref, active_ref, factor_ref, silu_ref = refs[:5]
    w_gate_ref, w_up_ref, w_down_ref, back_ref, dots_ref = refs[5:10]
    grads, (gate_low_ref, up_low_ref) = refs[10:-2], refs[-2:]
    slots, width = g_ref.shape[1], g_ref.shape[2]
    chunk = 256
    active_grad = dot(g_ref[0], w_down_ref[0])
    gate_low_ref[...] = (active_grad * factor_ref[0]).astype(bf16)
    up_low_ref[...] = (active_grad * silu_ref[0]).astype(bf16)
    dots = jnp.sum(active_ref[0].astype(f32) * active_grad, axis=1, keepdims=True)
    dots_ref[0] = jnp.broadcast_to(dots, (slots, LANES))
    back_ref[0] = (dot_nt(gate_low_ref[...], w_gate_ref[0]) + dot_nt(up_low_ref[...], w_up_ref[0])).astype(bf16)

    def products(cols):
        x = x_ref[0, :, cols]
        yield 0, dot_tn(x, gate_low_ref[...]).astype(bf16)
        yield 1, dot_tn(x, up_low_ref[...]).astype(bf16)
        yield 2, dot_tn(g_ref[0, :, cols], active_ref[0]).astype(bf16)

    if fast:
        write_shards(place_ref, grads, products, width)
    else:

        def whole_columns(index, carry):
            cols = pl.ds(pl.multiple_of(index * chunk, chunk), chunk)
            for which, product in products(cols):
                grads[which][0, cols, :] = product
            return carry

        lax.fori_loop(0, width // chunk, whole_columns, 0)


def write_shards(place_ref, outs, products, width):
    send_a, keep_a, send_b, keep_b = outs
    x_bit, y_bit = place_ref[3], place_ref[4]
    shard = width // 4
    for dy in range(2):
        for dx in range(2):
            x, y = x_bit ^ dx, y_bit ^ dy
            cols = pl.ds(pl.multiple_of((y * 2 + x) * shard, shard), shard)
            for which, product in products(cols):
                side = product.shape[1] // 2
                (send_a if dx else keep_a)[0, which, y] = product[:, :side]
                (send_b if dy else keep_b)[0, which, x] = product[:, side:]


def run_experts_back(place, x, g, active, factor, silu, w_gate, w_up, w_down, first, count, fast):
    slots, width = g.shape[1], g.shape[2]
    hidden = w_gate.shape[2]

    def taken(*shape):
        return pl.BlockSpec((1,) + shape, lambda e, p: (e + first, 0, 0))

    def given(*shape):
        zeros = (0,) * len(shape)
        return pl.BlockSpec((1,) + shape, lambda e, p: (e,) + zeros)

    if fast:
        grad_shapes = [(3, 2, width // 4, hidden // 2)] * 4
    else:
        grad_shapes = [(width, hidden)] * 3
    return call(
        lambda *refs: expert_back_kernel(*refs, fast=fast),
        (count,),
        1,
        [taken(slots, width)] * 2 + [taken(slots, hidden)] * 3 + [taken(width, hidden)] * 3,
        [given(slots, width), given(slots, LANES)] + [given(*shape) for shape in grad_shapes],
        [struct((count, slots, width), bf16), struct((count, slots, LANES), f32)]
        + [struct((count,) + shape, bf16) for shape in grad_shapes],
        scratch=[pltpu.VMEM((slots, hidden), bf16)] * 2,
        us=count,
    )(place, x, g, active, factor, silu, w_gate, w_up, w_down)


DOT_LANES = 2 * LANES


def combine_kernel(place_ref, rank_ref, *refs, pieces, with_dots, mine):
    parts, rest = refs[:pieces], refs[pieces:]
    rows = rank_ref.shape[2]
    local_experts = sum(part.shape[0] for part in parts)
    hits = hits_of(rank_ref[0], local_experts)
    gathered = jnp.concatenate([part[j, 0] for part in parts for j in range(part.shape[0])], axis=0)
    summed = dot_tn(chosen_of(hits), gathered)
    out_ref = rest[-1]
    if mine:
        arrived_ref = rest[-2]
        summed = summed + arrived_ref[0, 0:rows, :].astype(f32)
    out_ref[0, 0:rows, :] = summed.astype(bf16)
    if with_dots:
        column = [part[j, 0][:, 0:1] for part in rest[:pieces] for j in range(part.shape[0])]
        scattered = [
            jnp.sum(jnp.where(hit, value, 0.0), axis=0, keepdims=True) for hit, value in zip(hits, column)
        ]
        scattered.append(jnp.zeros((DOT_ROWS - local_experts, rows), f32))
        scattered = jnp.concatenate(scattered, axis=0)
        upper = scattered.astype(bf16)
        out_ref[0, rows:, :] = jnp.zeros((DOT_ROWS, out_ref.shape[2]), bf16)
        out_ref[0, rows:, 0:rows] = upper
        out_ref[0, rows:, DOT_LANES : DOT_LANES + rows] = (scattered - upper.astype(f32)).astype(bf16)
        if mine:
            out_ref[0, rows:, 2 * DOT_LANES : 4 * DOT_LANES] = arrived_ref[0, rows:, 0 : 2 * DOT_LANES]


def combine(place, rank, parts, dots=None, arrived=None):
    mine = arrived is not None
    rows, width = rank.shape[2], parts[0].shape[-1]
    out_rows = rows + (DOT_ROWS if dots else 0)

    def member(step, p):
        return (p[0] if mine else 1 - p[0]) * COLS + step

    def slots_of(array):
        return pl.BlockSpec((array.shape[0], 1) + array.shape[2:], lambda j, p: (0, member(j, p), 0, 0))

    inputs = [
        part.reshape(part.shape[0], 2 * COLS, CAPACITY, part.shape[-1]) for part in list(parts) + list(dots or [])
    ]
    in_specs = [pl.BlockSpec((1, 8, rows), lambda j, p: (member(j, p), 0, 0))] + [slots_of(item) for item in inputs]
    by_chip = pl.BlockSpec((1, out_rows, width), lambda j, p: (j, 0, 0))
    if mine:
        inputs.append(arrived)
        in_specs.append(by_chip)
    return call(
        lambda *refs: combine_kernel(*refs, pieces=len(parts), with_dots=bool(dots), mine=mine),
        (COLS,),
        1,
        in_specs,
        by_chip,
        struct((COLS, out_rows, width), bf16),
        us=0,
    )(place, rank, *inputs)


def split_dot(dimension_numbers, values, exact):
    upper = values.astype(bf16)
    lower = (values - upper.astype(f32)).astype(bf16)
    return lax.dot_general(
        upper, exact, dimension_numbers, preferred_element_type=f32
    ) + lax.dot_general(lower, exact, dimension_numbers, preferred_element_type=f32)


def middle_back_kernel(
    place_ref, sums_ref, gates_ref, middle_ref, cot_ref, gain_ref, w_router_ref, w_out_ref,
    grad_ref, branch_ref, attended_ref, small_ref
):
    rows = middle_ref.shape[0]
    tail = sums_ref[:, rows : rows + 8, 0 : 4 * DOT_LANES].astype(f32)
    mine = tail[:, :, 0:rows] + tail[:, :, DOT_LANES : DOT_LANES + rows]
    other = tail[:, :, 2 * DOT_LANES : 2 * DOT_LANES + rows] + tail[:, :, 3 * DOT_LANES : 3 * DOT_LANES + rows]
    first_row = place_ref[0] == 0
    dots = jnp.concatenate([jnp.where(first_row, mine, other), jnp.where(first_row, other, mine)], axis=0)
    dots = dots.reshape(dots.shape[0] * 8, rows)
    gates = gates_ref[...]
    logit_grad = dots - gates * jnp.sum(dots, axis=0, keepdims=True)
    middle = middle_ref[...]
    inverse = lax.rsqrt(jnp.mean(middle * middle, axis=1, keepdims=True) + epsilon)
    unit = middle * inverse
    gain = gain_ref[...]
    normed = (unit * gain).astype(bf16)
    grad = sums_ref[0, 0:rows].astype(f32)
    for index in range(1, sums_ref.shape[0]):
        grad = grad + sums_ref[index, 0:rows].astype(f32)
    grad = grad + split_dot(TN, logit_grad, w_router_ref[...])
    small_ref[...] = split_dot((((1,), (0,)), ((), ())), logit_grad, normed)
    small_ref[7:8, :] = jnp.sum(grad * unit, axis=0, keepdims=True)
    scaled = grad * gain
    middle_grad = cot_ref[...].astype(f32) + inverse * (
        scaled - unit * jnp.mean(scaled * unit, axis=1, keepdims=True)
    )
    grad_ref[...] = middle_grad
    branch_grad = middle_grad.astype(bf16)
    branch_ref[...] = branch_grad
    for member in range(w_out_ref.shape[0]):
        product = dot_nt(branch_grad, w_out_ref[member])
        attended_ref[member, :, 0:LANES] = product[:, 0:LANES].astype(bf16)
        attended_ref[member, :, LANES : LANES + HEAD_DIM] = product[:, LANES:].astype(bf16)
        attended_ref[member, :, LANES + HEAD_DIM :] = jnp.zeros((product.shape[0], HEAD_DIM), bf16)


def middle_back(place, sums, gates, middle, cotangent, gain, w_router, w_out):
    rows, width = middle.shape
    members = w_out.shape[0]
    args = (sums, gates, middle, cotangent, gain, w_router, w_out)
    return call(
        middle_back_kernel,
        (1,),
        1,
        [whole(item.shape) for item in args],
        [
            whole((rows, width)),
            whole((rows, width)),
            whole((members, rows, 2 * LANES)),
            whole(w_router.shape),
        ],
        [
            struct((rows, width), f32),
            struct((rows, width), bf16),
            struct((members, rows, 2 * LANES), bf16),
            struct(w_router.shape, f32),
        ],
        us=7,
    )(place, *args)


def input_grad_kernel(place_ref, grads_ref, w_ref, *rest):
    product = dot(grads_ref[...], w_ref[...])
    if len(rest) == 2:
        product = product + rest[0][0].astype(f32)
    rest[-1][0] = product.astype(bf16)


def input_grad(place, grads, w_stack, arrived=None):
    mine = arrived is not None
    total, lanes = grads.shape
    rows, width = total // (2 * COLS), w_stack.shape[1]

    def member(step, p):
        return (p[0] if mine else 1 - p[0]) * COLS + step

    by_chip = pl.BlockSpec((1, rows, width), lambda j, p: (j, 0, 0))
    return call(
        input_grad_kernel,
        (COLS,),
        1,
        [pl.BlockSpec((rows, lanes), lambda j, p: (member(j, p), 0)), whole(w_stack.shape)] + [by_chip] * mine,
        by_chip,
        struct((COLS, rows, width), bf16),
        us=0,
    )(place, grads, w_stack, *([arrived] if mine else []))


def own_weights_kernel(normed_ref, projected_ref, w_ref, gain_ref, out_ref, gain_grad_ref, sum_ref):
    step = pl.program_id(0)

    @pl.when(step == 0)
    def _():
        sum_ref[...] = jnp.zeros_like(sum_ref)

    sum_ref[...] += dot_tn(normed_ref[...], projected_ref[...])

    @pl.when(step == pl.num_programs(0) - 1)
    def _():
        total = sum_ref[...]
        out_ref[...] = total.astype(bf16)
        by_weight = jnp.sum(total * w_ref[...].astype(f32), axis=1, keepdims=True)
        gain_grad_ref[...] = jnp.broadcast_to(by_weight / gain_ref[...], gain_grad_ref.shape)


def own_weights(normed, projected, w_natural, gain):
    total, width = normed.shape
    lanes = projected.shape[1]
    rows = 512
    return call(
        own_weights_kernel,
        (total // rows,),
        0,
        [
            pl.BlockSpec((rows, width), lambda j: (j, 0)),
            pl.BlockSpec((rows, lanes), lambda j: (j, 0)),
            whole((width, lanes)),
            whole((width, 1)),
        ],
        [whole((width, lanes)), whole((width, 8))],
        [struct((width, lanes), bf16), struct((width, 8), f32)],
        scratch=[pltpu.VMEM((width, lanes), f32)],
        us=8,
    )(normed, projected, w_natural, gain)


def out_weights_kernel(place_ref, branch_ref, att_ref, own_ref, *refs, fast):
    outs, sum_ref = refs[:-1], refs[-1]
    step = pl.program_id(0)

    @pl.when(step == 0)
    def _():
        sum_ref[...] = jnp.zeros_like(sum_ref)

    sum_ref[...] += dot_tn(branch_ref[...], att_ref[...])

    @pl.when(step == pl.num_programs(0) - 1)
    def _():
        def products(cols):
            own = own_ref[cols, 0 : 2 * LANES]
            out_one = sum_ref[cols, 0:LANES].astype(bf16)
            out_two = sum_ref[cols, LANES:]
            low = lane_of(out_two.shape) < HEAD_DIM
            tail = jnp.where(low, out_two, own_ref[cols, 2 * LANES :].astype(f32)).astype(bf16)
            yield 0, jnp.concatenate([own, out_one, tail], axis=1)

        if fast:
            write_shards(place_ref, outs, products, own_ref.shape[0])
        else:
            outs[0][...] = next(products(slice(0, own_ref.shape[0])))[1]


def out_weights(place, branch, attended, own, fast):
    total, width = branch.shape
    rows = 512
    if fast:
        shapes = [(1, 1, 2, width // 4, 2 * LANES)] * 4
    else:
        shapes = [(width, 4 * LANES)]
    return call(
        lambda *refs: out_weights_kernel(*refs, fast=fast),
        (total // rows,),
        1,
        [
            pl.BlockSpec((rows, width), lambda j, p: (j, 0)),
            pl.BlockSpec((rows, 2 * LANES), lambda j, p: (j, 0)),
            whole(own.shape),
        ],
        [whole(shape) for shape in shapes],
        [struct(shape, bf16) for shape in shapes],
        scratch=[pltpu.VMEM((width, 2 * LANES), f32)],
        us=7,
    )(place, branch, attended, own)


def first_sum_kernel(place_ref, keep_a_ref, got_a_ref, keep_b_ref, got_b_ref, send_a_ref, held_a_ref, send_b_ref, held_b_ref):
    x_bit, y_bit = place_ref[3], place_ref[4]
    for bit, keep, got, send, held in (
        (y_bit, keep_a_ref, got_a_ref, send_a_ref, held_a_ref),
        (x_bit, keep_b_ref, got_b_ref, send_b_ref, held_b_ref),
    ):
        held[0, 0] = keep[0, 0, bit].astype(f32) + got[0, 0, bit].astype(f32)
        send[0, 0] = (keep[0, 0, 1 - bit].astype(f32) + got[0, 0, 1 - bit].astype(f32)).astype(bf16)


def first_sum(place, keep_a, got_a, keep_b, got_b):
    count, kinds, _, rows, cols = keep_a.shape
    taken = pl.BlockSpec((1, 1, 2, rows, cols), lambda e, k, p: (e, k, 0, 0, 0))
    given = pl.BlockSpec((1, 1, rows, cols), lambda e, k, p: (e, k, 0, 0))
    shape = (count, kinds, rows, cols)
    return call(
        first_sum_kernel,
        (count, kinds),
        1,
        [taken] * 4,
        [given] * 4,
        [struct(shape, bf16), struct(shape, f32), struct(shape, bf16), struct(shape, f32)],
        us=4 * count,
    )(place, keep_a, got_a, keep_b, got_b)


def last_sum_kernel(held_a_ref, got_a_ref, held_b_ref, got_b_ref, *rest):
    outs = rest[-3:]
    side = held_a_ref.shape[3]
    for which, out in enumerate(outs):
        out[0, :, :side] = held_a_ref[0, which] + got_a_ref[0, which].astype(f32)
        out[0, :, side:] = held_b_ref[0, which] + got_b_ref[0, which].astype(f32)


def last_sum(held_a, got_a, held_b, got_b, first, total, before):
    count, kinds, rows, cols = held_a.shape
    taken = pl.BlockSpec((1, kinds, rows, cols), lambda e: (e, 0, 0, 0))
    given = pl.BlockSpec((1, rows, 2 * cols), lambda e: (e + first, 0, 0))
    extra = list(before) if before else []
    return call(
        last_sum_kernel,
        (count,),
        0,
        [taken] * 4 + [pl.BlockSpec(memory_space=pl.ANY)] * len(extra),
        [given] * 3,
        [struct((total, rows, 2 * cols), f32)] * 3,
        us=2.5 * count,
        aliases={4 + i: i for i in range(len(extra))},
    )(held_a, got_a, held_b, got_b, *extra)


SWAP = [(0, 1), (1, 0)]


def after(value, *events):
    return lax.optimization_barrier((value,) + events)[0]


def gather_group(block):
    return lax.all_gather(block, ("row", "col"), axis=0, tiled=True)


def flip(value, axis, bit, size):
    return lax.ppermute(value, axis, [(i, i ^ (1 << bit)) for i in range(size)])


def bits_of(size):
    return size.bit_length() - 1


def own_bit(axis, bit):
    return (lax.axis_index(axis) >> bit) & 1


def joined(mine, got, own):
    return jnp.where(own == 0, jnp.concatenate([mine, got]), jnp.concatenate([got, mine]))


def cube_step(value, axis, bit, size):
    return joined(value, flip(value, axis, bit, size), own_bit(axis, bit))


def cube_gather(value, axis, size):
    value = value[None]
    for bit in range(bits_of(size)):
        value = cube_step(value, axis, bit, size)
    return value


def sum_dp(value, sizes):
    for bit in range(bits_of(sizes["dp"])):
        value = value + flip(value, "dp", bit, sizes["dp"])
    return value


def reduce_over_dp(value, size):
    count = bits_of(size)
    value = value.reshape(value.shape[:1] + (2,) * count + value.shape[2:])
    current = value
    for bit in range(count - 1, -1, -1):
        own = own_bit("dp", bit)
        keep = lax.dynamic_index_in_dim(current, own, 1, keepdims=False)
        send = lax.dynamic_index_in_dim(current, 1 - own, 1, keepdims=False).astype(bf16)
        current = keep.astype(f32) + flip(send, "dp", bit, size).astype(f32)
    return current


def start_move(run, size):
    return flip(run[0], "dp", 0, size), flip(run[2], "dp", 1, size)


def first_half(place, run, got, size, event):
    keep_a, keep_b = after((run[1], run[3]), event)
    send_a, held_a, send_b, held_b = first_sum(place, keep_a, got[0], keep_b, got[1])
    return held_a, flip(send_a, "dp", 1, size), held_b, flip(send_b, "dp", 0, size)


def layer(sizes):
    n_dp, n_row, n_col = sizes["dp"], sizes["row"], sizes["col"]
    members = n_row * n_col
    fast = n_dp == 4
    assert n_row == 2 and n_col == COLS and n_dp & (n_dp - 1) == 0

    def local(
        tokens, cotangent, routes, lengths, gain_attn, w_query, w_key, w_value, w_out,
        gain_moe, w_router, w_gate, w_up, w_down,
    ):
        rows, width = tokens.shape
        group = rows * members
        local_experts = w_gate.shape[0]
        row, col, dp = lax.axis_index("row"), lax.axis_index("col"), lax.axis_index("dp")
        place = jnp.stack([row, col, row * n_col + col, dp & 1, (dp >> 1) & 1]).astype(jnp.int32)
        gain_one = gain_attn.astype(f32)[None]
        gain_two = gain_moe.astype(f32)[None]

        tok_all = gather_group(tokens)
        share = rows // n_dp
        w_out_share = lax.dynamic_slice(w_out.T, (dp * share, 0), (share, width))
        route_row = routes.T.astype(bf16).reshape(1, TOP * rows)
        route_row = jnp.pad(route_row, ((0, 7), (0, width - TOP * rows)))
        shares = cube_gather(jnp.concatenate([w_out_share, route_row], axis=0), "col", n_col)
        route_rows = cube_gather(shares[:, share], "row", n_row)[:, :, : TOP * rows].reshape(members, TOP, rows)
        route_rows = jnp.pad(route_rows, ((0, 0), (0, ROUTE_ROWS - TOP), (0, 2 * LANES - rows)))
        w_out_part = cube_step(shares[None, :, :share], "dp", 0, n_dp)
        w_out_all = w_out_part
        for bit in range(1, bits_of(n_dp)):
            w_out_all = cube_step(w_out_all, "dp", bit, n_dp)
        w_out_all = cube_gather(w_out_all, "row", n_row)
        w_out_all = jnp.transpose(w_out_all, (0, 2, 1, 3, 4)).reshape(members, rows, width)
        w_stack = jnp.concatenate([w_query.T, w_key.T, w_value.T, w_value.T], axis=0)
        w_natural = jnp.concatenate([w_query, w_key, w_value, w_value], axis=1)

        ends = jnp.cumsum(lengths[0])
        starts = ends - lengths[0]
        position = jnp.arange(group, dtype=jnp.int32)
        segment = jnp.sum((position[:, None] >= ends[None, :]).astype(jnp.int32), axis=1)
        member = segment[:, None] == jnp.arange(starts.shape[0], dtype=jnp.int32)[None, :]
        start = jnp.sum(jnp.where(member, starts[None, :], 0), axis=1).astype(jnp.int32)
        frequency = rope_base ** (-2.0 * jnp.arange(HEAD_DIM // 2, dtype=f32) / HEAD_DIM)
        angle = (position - start).astype(f32)[:, None] * frequency[None, :]
        cosine = jnp.tile(jnp.cos(angle), (1, 4))
        sine = jnp.tile(jnp.sin(angle), (1, 4))

        query, key, value, normed_one = project(tok_all, after(gain_one, w_out_part, route_rows), w_stack, cosine, sine)
        w_router_rows = w_router.T.reshape(members, local_experts, width)
        w_router_rows = jnp.pad(w_router_rows, ((0, 0), (0, 8 - local_experts), (0, 0)))
        w_router_rows = w_router_rows.reshape(members * 8, width)
        packed, attended, totals = attend(query, key, value, start[:, None])
        att_flat = gather_group(packed)
        att_all = att_flat.reshape((members,) + packed.shape)
        cot_all = gather_group(after(cotangent, att_flat))
        x, slot_gate, rank, gate, middle, gates = middle_and_dispatch(
            place, att_all, w_out_all, tok_all, route_rows, gain_two, w_router_rows, local_experts
        )
        slots = members * CAPACITY
        x = x.reshape(local_experts, slots, width)
        slot_gate = slot_gate.reshape(local_experts, slots, LANES)
        rank, gate = rank.reshape(members, 8, rows), gate.reshape(members, 8, rows)
        forth, active, factor, silu = run_experts(x, slot_gate, w_gate, w_up, w_down)
        forth_other = combine(place, rank, [forth])
        arrived = lax.ppermute(forth_other, "row", SWAP)
        g = grad_dispatch(after(rank, forth_other), gate, cot_all, local_experts)
        g = g.reshape(local_experts, slots, width)
        cuts = [0, 1, 3, local_experts]

        def backward(which, x):
            first, last = cuts[which], cuts[which + 1]
            return run_experts_back(place, x, g, active, factor, silu, w_gate, w_up, w_down, first, last - first, fast)

        runs = [backward(0, x)]
        forth_mine = combine(place, rank, [forth], arrived=after(arrived, runs[0][1]))
        forth_sums = lax.all_to_all(forth_mine, "col", 0, 0, tiled=True)
        runs.append(backward(1, after(x, forth_mine)))
        runs.append(backward(2, after(x, runs[1][1])))
        moved = [start_move(run[2:], n_dp) for run in runs] if fast else []
        back_parts, dot_parts = [run[0] for run in runs], [run[1] for run in runs]
        back_other = combine(place, after(rank, *moved[0]) if fast else rank, back_parts, dot_parts)
        arrived = lax.ppermute(back_other, "row", SWAP)
        back_mine = combine(place, rank, back_parts, dot_parts, arrived)
        back_mine = after(back_mine, forth_sums)
        back_sums = lax.all_to_all(back_mine, "col", 0, 0, tiled=True)
        started, gate_middle = [], []
        if fast:
            started.append(first_half(place, runs[0][2:], moved[0], n_dp, back_mine))
            gate_middle += [started[0][0], *moved[1]]

        middle_grad, branch_grad, attended_grad, small = middle_back(
            place, back_sums, gates, middle, cotangent, after(gain_two, *gate_middle), w_router_rows, w_out_all
        )
        if fast:
            started.append(first_half(place, runs[1][2:], moved[1], n_dp, branch_grad))
        attended_grad = lax.all_to_all(attended_grad, ("row", "col"), 0, 0, tiled=True)
        branch_all = gather_group(branch_grad)

        start_row = jnp.broadcast_to(start[None, :], (8, group))
        attended_grad = attended_grad.reshape(group, 2 * LANES)
        if fast:
            attended_grad = after(attended_grad, started[1][0])
        projected_grad = attend_back(query, key, value, attended_grad, totals, start_row, cosine, sine)
        in_other = input_grad(place, projected_grad, after(w_stack, *moved[2]) if fast else w_stack)
        arrived = lax.ppermute(in_other, "row", SWAP)
        if fast:
            started.append(first_half(place, runs[2][2:], moved[2], n_dp, in_other))
        in_mine = input_grad(place, projected_grad, after(w_stack, branch_all), arrived)
        in_sums = lax.all_to_all(in_mine, "col", 0, 0, tiled=True)
        own_grads, gain_part = own_weights(
            after(normed_one, in_mine), projected_grad, w_natural, gain_attn.astype(f32)[:, None]
        )
        used = small.reshape(members, 8, width)[:, :local_experts].reshape(members * local_experts, width)
        sums = jnp.concatenate([used, small[7:8], gain_part[:, 0].reshape(1, width)], axis=0)
        sums = lax.psum(sums, ("row", "col"))
        w_parts = out_weights(place, branch_all, attended, own_grads, fast)
        if fast:
            w_started = first_half(place, w_parts, start_move(w_parts, n_dp), n_dp, w_parts[1])
        else:
            cut = w_parts[0].reshape(1, n_dp, width // n_dp, w_parts[0].shape[1])
            w_sum = reduce_over_dp(cut, n_dp)[0]

        mixed = (middle + jnp.sum(after(forth_sums, projected_grad).astype(f32), axis=0)).astype(bf16)

        both = sum_dp(after(sums, w_parts[0]), sizes)
        w_router_grad = both[: members * local_experts].T
        gain_moe_grad, gain_attn_grad = both[members * local_experts], both[members * local_experts + 1]

        normed_grad = jnp.sum(in_sums.astype(f32), axis=0)
        resid = tokens.astype(f32)
        inverse = lax.rsqrt(jnp.mean(resid * resid, axis=1, keepdims=True) + epsilon)
        unit = resid * inverse
        scaled = normed_grad * gain_one
        tokens_grad = middle_grad + inverse * (
            scaled - unit * jnp.mean(scaled * unit, axis=1, keepdims=True)
        )

        if fast:
            expert_grads = None
            for which, event in enumerate((in_mine, own_grads, w_parts[0])):
                held_a, got_a, held_b, got_b = started[which]
                held_a, held_b = after((held_a, held_b), event)
                expert_grads = last_sum(held_a, got_a, held_b, got_b, cuts[which], local_experts, expert_grads)
            held_a, got_a, held_b, got_b = [item[0, 0] for item in w_started]
            left = held_a + got_a.astype(f32)
            right = held_b + got_b.astype(f32)
            w_sum = jnp.concatenate([left, right], axis=1)
        else:
            expert_grads = []
            for which in range(3):
                parts = [run[2 + which] for run in runs]
                parts = [part.reshape(part.shape[0], n_dp, width // n_dp, part.shape[2]) for part in parts]
                expert_grads.append(jnp.concatenate([reduce_over_dp(part, n_dp) for part in parts], axis=0))
        w_gate_grad, w_up_grad, w_down_grad = expert_grads
        local_q, local_k = w_query.shape[1], w_key.shape[1]
        cut = local_q + local_k
        return (
            mixed, tokens_grad, gain_attn_grad, w_sum[:, :local_q], w_sum[:, local_q:cut],
            w_sum[:, cut + local_q :], w_sum[:, cut : cut + local_q],
            gain_moe_grad, w_router_grad, w_gate_grad, w_up_grad, w_down_grad,
        )

    return local


def solution(mesh):
    return jax.shard_map(
        layer(dict(mesh.shape)),
        mesh=mesh,
        in_specs=(
            P(("dp", "row", "col"), None),
            P(("dp", "row", "col"), None),
            P(("dp", "row", "col"), None),
            P("dp", None),
            P(),
            P(None, ("row", "col")),
            P(None, ("row", "col")),
            P(None, ("row", "col")),
            P(None, ("row", "col")),
            P(),
            P(),
            P(("row", "col"), None, None),
            P(("row", "col"), None, None),
            P(("row", "col"), None, None),
        ),
        out_specs=(
            P(("dp", "row", "col"), None),
            P(("dp", "row", "col"), None),
            P(),
            P("dp", ("row", "col")),
            P("dp", ("row", "col")),
            P("dp", ("row", "col")),
            P("dp", ("row", "col")),
            P(),
            P(),
            P(("row", "col"), "dp", None),
            P(("row", "col"), "dp", None),
            P(("row", "col"), "dp", None),
        ),
        check_vma=False,
    )
```

```python
import math

import jax
import jax.numpy as jnp
from jax import lax
from jax.experimental import pallas as pl
from jax.experimental.pallas import tpu as pltpu
from jax.sharding import PartitionSpec as P

HEAD_DIM = 64
EXPERTS = 40
TOP = 8
CAPACITY = 64
COLS = 4
LANES = 128
QUERY_BLOCK = 256
ROUTE_ROWS = 16
DOT_ROWS = 16

epsilon = 1e-06
rope_base = 10000.0
masked_score = -1e30
f32 = jnp.float32
bf16 = jnp.bfloat16
VMEM_LIMIT = 56 * 1024 * 1024

NT = (((1,), (1,)), ((), ()))
TN = (((0,), (0,)), ((), ()))


def dot(a, b):
    return jnp.dot(a, b, preferred_element_type=f32)


def dot_nt(a, b):
    return lax.dot_general(a, b, NT, preferred_element_type=f32)


def dot_tn(a, b):
    return lax.dot_general(a, b, TN, preferred_element_type=f32)


def lane_of(shape):
    return lax.broadcasted_iota(jnp.int32, shape, len(shape) - 1)


def call(
    kernel, grid, prefetch, in_specs, out_specs, out_shape, scratch=(), us=1.0, aliases=None
):
    return pl.pallas_call(
        kernel,
        grid_spec=pltpu.PrefetchScalarGridSpec(
            num_scalar_prefetch=prefetch,
            grid=grid,
            in_specs=in_specs,
            out_specs=out_specs,
            scratch_shapes=list(scratch),
        ),
        out_shape=out_shape,
        input_output_aliases=aliases or {},
        compiler_params=pltpu.CompilerParams(
            vmem_limit_bytes=VMEM_LIMIT, dimension_semantics=("arbitrary",) * len(grid)
        ),
        cost_estimate=pl.CostEstimate(
            flops=int(us * 1.1e9), bytes_accessed=int(us * 3.6e6), transcendentals=0
        ),
    )


def whole(shape):
    zeros = (0,) * len(shape)
    return pl.BlockSpec(shape, lambda *_: zeros)


def struct(shape, dtype):
    return jax.ShapeDtypeStruct(shape, dtype)


def turn_within_heads(values, sign):
    lane = lane_of(values.shape) % HEAD_DIM
    ahead = pltpu.roll(values, LANES - HEAD_DIM // 2, 1)
    behind = pltpu.roll(values, HEAD_DIM // 2, 1)
    return jnp.where(lane < HEAD_DIM // 2, -sign * ahead, sign * behind)


def project_kernel(
    tok_ref, gain_ref, w_ref, cos_ref, sin_ref, query_ref, key_ref, value_ref, normed_ref
):
    resid = tok_ref[...].astype(f32)
    inverse = lax.rsqrt(jnp.mean(resid * resid, axis=1, keepdims=True) + epsilon)
    normed = (resid * inverse * gain_ref[...]).astype(bf16)
    normed_ref[...] = normed
    raw = dot_nt(normed, w_ref[...])
    cosine, sine = cos_ref[...], sin_ref[...]

    def rot(values):
        return (values * cosine + turn_within_heads(values, 1.0) * sine).astype(bf16).astype(f32)

    first = rot(raw[:, :LANES])
    second = rot(raw[:, LANES : 2 * LANES])
    low = lane_of(first.shape) < HEAD_DIM
    scale = 1.0 / math.sqrt(HEAD_DIM)
    query_ref[0] = jnp.where(low, first * scale, 0.0).astype(bf16)
    query_ref[1] = jnp.where(low, 0.0, first * scale).astype(bf16)
    query_ref[2] = jnp.where(low, second * scale, 0.0).astype(bf16)
    key_ref[...] = jnp.where(low, pltpu.roll(second, HEAD_DIM, 1), second).astype(bf16)
    value_ref[...] = raw[:, 2 * LANES :].astype(bf16)


def project(tokens, gain, w_stack, cosine, sine):
    total, width = tokens.shape
    rows = 512
    lanes = pl.BlockSpec((rows, LANES), lambda j: (j, 0))
    wide = pl.BlockSpec((rows, width), lambda j: (j, 0))
    return call(
        project_kernel,
        (total // rows,),
        0,
        [wide, whole((1, width)), whole(w_stack.shape), lanes, lanes],
        [pl.BlockSpec((3, rows, LANES), lambda j: (0, j, 0)), lanes, lanes, wide],
        [
            struct((3, total, LANES), bf16),
            struct((total, LANES), bf16),
            struct((total, LANES), bf16),
            struct((total, width), bf16),
        ],
        us=9,
    )(tokens, gain, w_stack, cosine, sine)


def attend_kernel(query_ref, key_ref, value_ref, start_ref, packed_ref, plain_ref, total_ref, out_ref):
    blocks = query_ref.shape[1] // QUERY_BLOCK
    block = pl.program_id(0)
    for index in range(blocks):

        @pl.when(block == index)
        def _(index=index):
            rows = pl.ds(index * QUERY_BLOCK, QUERY_BLOCK)
            span = (index + 1) * QUERY_BLOCK
            row = index * QUERY_BLOCK + lax.broadcasted_iota(jnp.int32, (QUERY_BLOCK, span), 0)
            column = lane_of((QUERY_BLOCK, span))
            allowed = (column <= row) & (column >= start_ref[rows, :])

            def head(number, carry):
                scores = dot_nt(query_ref[number, rows, :], key_ref[0:span, :])
                scores = jnp.where(allowed, scores, masked_score)
                peak = jnp.max(scores, axis=1, keepdims=True)
                weights = jnp.exp(scores - peak)
                summed = jnp.sum(weights, axis=1, keepdims=True)
                probs = (weights * (1.0 / summed)).astype(bf16)
                out_ref[number] = dot(probs, value_ref[0:span, :])
                total = jnp.broadcast_to(peak + jnp.log(summed), (QUERY_BLOCK, LANES))
                total_ref[number, :, rows] = jnp.transpose(total)[0:8, :]
                return carry

            lax.fori_loop(0, 3, head, 0)
            low = lane_of((QUERY_BLOCK, LANES)) < HEAD_DIM
            one, two, three = out_ref[0], out_ref[1], out_ref[2]
            pair = jnp.where(low, one, two).astype(bf16)
            plain_ref[rows, 0:LANES] = pair
            plain_ref[rows, LANES : 2 * LANES] = jnp.where(low, three, 0.0).astype(bf16)
            if index < blocks // 2:
                packed_ref[rows, 0:LANES] = pair
                packed_ref[rows, LANES : 2 * LANES] = three.astype(bf16)
            else:
                back = pl.ds((index - blocks // 2) * QUERY_BLOCK, QUERY_BLOCK)
                before = packed_ref[back, LANES : 2 * LANES].astype(f32)
                packed_ref[back, LANES : 2 * LANES] = jnp.where(low, before, one).astype(bf16)
                packed_ref[back, 2 * LANES : 3 * LANES] = jnp.where(low, two, three).astype(bf16)


def attend(query, key, value, start):
    total = key.shape[0]
    return call(
        attend_kernel,
        (total // QUERY_BLOCK,),
        0,
        [whole(query.shape), whole(key.shape), whole(value.shape), whole(start.shape)],
        [whole((total // 2, 3 * LANES)), whole((total, 2 * LANES)), whole((3, 8, total))],
        [
            struct((total // 2, 3 * LANES), bf16),
            struct((total, 2 * LANES), bf16),
            struct((3, 8, total), f32),
        ],
        scratch=[pltpu.VMEM((3, QUERY_BLOCK, LANES), f32)],
        us=18,
    )(query, key, value, start)


def attend_back_kernel(
    query_ref, key_ref, value_ref, grad_ref, total_ref, start_ref, cos_ref, sin_ref,
    out_ref, query_grad_ref, key_grad_ref, value_grad_ref
):
    blocks = query_ref.shape[1] // QUERY_BLOCK
    block = pl.program_id(0)
    scale = 1.0 / math.sqrt(HEAD_DIM)

    @pl.when(block == 0)
    def _():
        key_grad_ref[...] = jnp.zeros_like(key_grad_ref)
        value_grad_ref[...] = jnp.zeros_like(value_grad_ref)

    def back(values, cosine, sine):
        return values * cosine + turn_within_heads(values * sine, -1.0)

    for index in range(blocks):

        @pl.when(block == index)
        def _(index=index):
            rows = pl.ds(index * QUERY_BLOCK, QUERY_BLOCK)
            span = (index + 1) * QUERY_BLOCK
            row = index * QUERY_BLOCK + lane_of((span, QUERY_BLOCK))
            column = lax.broadcasted_iota(jnp.int32, (span, QUERY_BLOCK), 0)
            allowed = (column <= row) & (column >= start_ref[0:1, rows])
            low = lane_of((QUERY_BLOCK, LANES)) < HEAD_DIM

            def head(number, carry):
                query = query_ref[number, rows, :]
                tile = pl.multiple_of((number // 2) * LANES, LANES)
                upstream = grad_ref[rows, pl.ds(tile, LANES)].astype(f32)
                keep = low == (number != 1)
                upstream = jnp.where(keep, upstream, 0.0).astype(bf16)
                scores = dot_nt(key_ref[0:span, :], query)
                probs = jnp.exp(scores - total_ref[number, 0:1, rows])
                probs = jnp.where(allowed, probs, 0.0)
                prob_grad = dot_nt(value_ref[0:span, :], upstream)
                row_dot = jnp.sum(probs * prob_grad, axis=0, keepdims=True)
                score_grad = (probs * (prob_grad - row_dot)).astype(bf16)
                key_grad_ref[0:span, :] += dot(score_grad, query)
                value_grad_ref[0:span, :] += dot(probs.astype(bf16), upstream)
                query_grad_ref[number] = dot_tn(score_grad, key_ref[0:span, :]) * scale
                return carry

            lax.fori_loop(0, 3, head, 0)
            cosine, sine = cos_ref[rows, :], sin_ref[rows, :]
            pair = jnp.where(low, query_grad_ref[0], query_grad_ref[1])
            out_ref[rows, 0:LANES] = back(pair, cosine, sine).astype(bf16)
            out_ref[rows, LANES : 2 * LANES] = back(query_grad_ref[2], cosine, sine).astype(bf16)

    @pl.when(block == blocks - 1)
    def _():
        low = lane_of(key_grad_ref.shape) < HEAD_DIM
        key_grad = key_grad_ref[...]
        key_grad = key_grad + pltpu.roll(key_grad, HEAD_DIM, 1)
        key_grad = back(key_grad, cos_ref[...], sin_ref[...])
        before = out_ref[:, LANES : 2 * LANES].astype(f32)
        out_ref[:, LANES : 2 * LANES] = jnp.where(low, before, key_grad).astype(bf16)
        value_grad = value_grad_ref[...]
        value_grad = value_grad + pltpu.roll(value_grad, HEAD_DIM, 1)
        out_ref[:, 2 * LANES : 3 * LANES] = jnp.where(low, 0.0, value_grad).astype(bf16)


def attend_back(query, key, value, grad, totals, start, cosine, sine):
    total = key.shape[0]
    args = (query, key, value, grad, totals, start, cosine, sine)
    return call(
        attend_back_kernel,
        (total // QUERY_BLOCK,),
        0,
        [whole(item.shape) for item in args],
        whole((total, 3 * LANES)),
        struct((total, 3 * LANES), bf16),
        scratch=[
            pltpu.VMEM((3, QUERY_BLOCK, LANES), f32),
            pltpu.VMEM((total, LANES), f32),
            pltpu.VMEM((total, LANES), f32),
        ],
        us=0,
    )(*args)


def branch_operand(refs):
    rows = refs.shape[2]
    low = lane_of((rows, LANES)) < HEAD_DIM
    pairs, thirds = [], []
    for member in range(refs.shape[1]):
        one = refs[0, member, :, 0:LANES]
        mid = refs[0, member, :, LANES : 2 * LANES].astype(f32)
        end = refs[0, member, :, 2 * LANES : 3 * LANES].astype(f32)
        mid_turned = pltpu.roll(mid, HEAD_DIM, 1)
        end_turned = pltpu.roll(end, HEAD_DIM, 1)
        late = jnp.where(low, mid_turned, end_turned).astype(bf16)
        pairs.append(jnp.concatenate([one, late], axis=0))
        thirds.append((mid, end_turned))
    for member in range(0, refs.shape[1], 2):
        tops = []
        for which in range(2):
            left, right = thirds[member][which], thirds[member + 1][which]
            tops.append(jnp.where(low, left, pltpu.roll(right, HEAD_DIM, 1)).astype(bf16))
        pairs.append(jnp.concatenate(tops, axis=0))
    return jnp.concatenate(pairs, axis=1)


def branch_weights(ref):
    right = [ref[source, 0:LANES] for source in range(ref.shape[0])]
    return jnp.concatenate(right + [ref[source, LANES:] for source in range(ref.shape[0])], axis=0)


def hits_of(rank, local_experts):
    place = lax.broadcasted_iota(jnp.int32, (CAPACITY, rank.shape[1]), 0).astype(f32)
    return [place == rank[j : j + 1, :] for j in range(local_experts)]


def chosen_of(hits):
    return jnp.concatenate([jnp.where(hit, 1.0, 0.0).astype(bf16) for hit in hits], axis=0)


def middle_kernel(
    place_ref, att_mine_ref, att_other_ref, w_mine_ref, w_other_ref, tok_a_ref, tok_b_ref, routes_a_ref, routes_b_ref,
    gain_ref, w_router_ref, after_ref,
    x_ref, slot_gate_ref, rank_ref, gate_ref, normed_ref, middle_ref, gates_own_ref, gates_ref, ranks_ref
):
    step = pl.program_id(0)
    member = place_ref[2]
    cols = pl.num_programs(0)
    rows = tok_a_ref.shape[0]
    local_experts = x_ref.shape[0]
    branch = dot(branch_operand(att_mine_ref), branch_weights(w_mine_ref))
    branch = branch + dot(branch_operand(att_other_ref), branch_weights(w_other_ref))
    for half in range(2):
        tok_ref, routes_ref = ((tok_a_ref, routes_a_ref), (tok_b_ref, routes_b_ref))[half]
        middle = tok_ref[...].astype(f32) + branch[half * rows : (half + 1) * rows]
        inverse = lax.rsqrt(jnp.mean(middle * middle, axis=1, keepdims=True) + epsilon)
        normed = (middle * inverse * gain_ref[...]).astype(bf16)
        normed_ref[half, 0] = normed
        logits = dot_nt(w_router_ref[...], normed)
        padded = logits.shape[0]
        slot = lax.broadcasted_iota(jnp.int32, (padded, rows), 0)
        expert = (slot // 8) * local_experts + slot % 8
        expert = jnp.where(slot % 8 < local_experts, expert, -1).astype(f32)
        routes = routes_ref[0].astype(f32)
        named = expert == routes[0:1, 0:rows]
        for k in range(1, TOP):
            named = named | (expert == routes[k : k + 1, 0:rows])
        peak = jnp.max(jnp.where(named, logits, masked_score), axis=0, keepdims=True)
        weights = jnp.where(named, jnp.exp(logits - peak), 0.0)
        gates = weights / jnp.sum(weights, axis=0, keepdims=True)
        gates_ref[...] = gates
        ranks_ref[...] = jnp.where(named, dot(named.astype(f32).astype(bf16), after_ref[...]), -1.0)
        here = pl.ds(pl.multiple_of(member * 8, 8), 8)
        gate, rank = gates_ref[here, :], ranks_ref[here, :]
        rank_ref[half, 0] = rank
        gate_ref[half, 0] = gate
        hits = hits_of(rank, local_experts)
        slot_gate = jnp.concatenate(
            [jnp.sum(jnp.where(hit, gate[j : j + 1, :], 0.0), axis=1, keepdims=True) for j, hit in enumerate(hits)],
            axis=0,
        )
        chosen = chosen_of(hits)
        picked = dot(chosen, normed).astype(bf16)
        spread = jnp.broadcast_to(slot_gate, (slot_gate.shape[0], LANES))
        for j in range(local_experts):
            part = slice(j * CAPACITY, (j + 1) * CAPACITY)
            x_ref[j, half, 0] = picked[part]
            slot_gate_ref[j, half, 0] = spread[part]

        @pl.when(member == half * cols + step)
        def _(middle=middle, gates=gates):
            middle_ref[...] = middle
            gates_own_ref[...] = gates


def middle_and_dispatch(place, att, w_mine, w_other, tokens, routes, gain, w_router, local_experts):
    width = tokens.shape[1]
    half = COLS
    rows = tokens.shape[0] // (2 * half)
    padded = w_router.shape[0]
    after = (jnp.arange(rows)[:, None] < jnp.arange(rows)[None, :]).astype(bf16)
    slot_shape = (local_experts, 2, half, CAPACITY)
    early = pl.BlockSpec((rows, width), lambda i, p: (i, 0))
    late = pl.BlockSpec((rows, width), lambda i, p: (i + half, 0))
    routes_shape = (1,) + routes.shape[1:]
    return call(
        middle_kernel,
        (half,),
        1,
        [
            pl.BlockSpec((1, half, rows, 3 * LANES), lambda i, p: (p[0], 0, i, 0)),
            pl.BlockSpec((1, half, rows, 3 * LANES), lambda i, p: (1 - p[0], 0, i, 0)),
            whole(w_mine.shape),
            whole(w_other.shape),
            early,
            late,
            pl.BlockSpec(routes_shape, lambda i, p: (i, 0, 0)),
            pl.BlockSpec(routes_shape, lambda i, p: (i + half, 0, 0)),
            whole((1, width)),
            whole(w_router.shape),
            whole((rows, rows)),
        ],
        [
            pl.BlockSpec((local_experts, 2, 1, CAPACITY, width), lambda i, p: (0, 0, i, 0, 0)),
            pl.BlockSpec((local_experts, 2, 1, CAPACITY, LANES), lambda i, p: (0, 0, i, 0, 0)),
            pl.BlockSpec((2, 1, 8, rows), lambda i, p: (0, i, 0, 0)),
            pl.BlockSpec((2, 1, 8, rows), lambda i, p: (0, i, 0, 0)),
            pl.BlockSpec((2, 1, rows, width), lambda i, p: (0, i, 0, 0)),
            whole((rows, width)),
            whole((padded, rows)),
        ],
        [
            struct(slot_shape + (width,), bf16),
            struct(slot_shape + (LANES,), f32),
            struct((2, half, 8, rows), f32),
            struct((2, half, 8, rows), f32),
            struct((2, half, rows, width), bf16),
            struct((rows, width), f32),
            struct((padded, rows), f32),
        ],
        scratch=[pltpu.VMEM((padded, rows), f32), pltpu.VMEM((padded, rows), f32)],
        us=2,
    )(place, att, att, w_mine, w_other, tokens, tokens, routes, routes, gain, w_router, after)


def grad_dispatch_kernel(rank_ref, gate_ref, cot_ref, g_ref):
    local_experts = g_ref.shape[0]
    rows = cot_ref.shape[0] // 2
    for half in range(2):
        hits = hits_of(rank_ref[half], local_experts)
        gate = gate_ref[half]
        slot_gate = jnp.concatenate(
            [jnp.sum(jnp.where(hit, gate[j : j + 1, :], 0.0), axis=1, keepdims=True) for j, hit in enumerate(hits)],
            axis=0,
        )
        grads = (dot(chosen_of(hits), cot_ref[half * rows : (half + 1) * rows, :]) * slot_gate).astype(bf16)
        for j in range(local_experts):
            g_ref[j, half] = grads[j * CAPACITY : (j + 1) * CAPACITY]


def grad_dispatch(rank, gate, cotangents, local_experts):
    members, _, rows = rank.shape
    width = cotangents.shape[1]
    small = pl.BlockSpec((2, 8, rows), lambda j: (j, 0, 0))
    return call(
        grad_dispatch_kernel,
        (members // 2,),
        0,
        [small, small, pl.BlockSpec((2 * rows, width), lambda j: (j, 0))],
        pl.BlockSpec((local_experts, 2, CAPACITY, width), lambda j: (0, j, 0, 0)),
        struct((local_experts, members, CAPACITY, width), bf16),
        us=7,
    )(rank, gate, cotangents)


def expert_kernel(
    x_ref, gate_ref, w_gate_ref, w_up_ref, w_down_ref, forth_ref, active_ref, factor_ref, silu_ref
):
    gate_pre = dot(x_ref[0], w_gate_ref[0])
    up_pre = dot(x_ref[0], w_up_ref[0])
    sig = 1.0 / (1.0 + jnp.exp(-gate_pre))
    silu = gate_pre * sig
    silu_ref[0] = silu
    factor_ref[0] = up_pre * sig * (1.0 + gate_pre * (1.0 - sig))
    active_ref[0] = (silu * up_pre).astype(bf16)
    produced = dot_nt(active_ref[0], w_down_ref[0]).astype(bf16).astype(f32)
    forth_ref[0] = (produced * gate_ref[0, :, 0:1]).astype(bf16)


def run_experts(x, slot_gate, w_gate, w_up, w_down):
    count, slots, width = x.shape
    hidden = w_gate.shape[2]

    def per_expert(*shape):
        return pl.BlockSpec((1,) + shape, lambda e: (e, 0, 0))

    return call(
        expert_kernel,
        (count,),
        0,
        [per_expert(slots, width), per_expert(slots, LANES)] + [per_expert(width, hidden)] * 3,
        [per_expert(slots, width)] + [per_expert(slots, hidden)] * 3,
        [
            struct((count, slots, width), bf16),
            struct((count, slots, hidden), bf16),
            struct((count, slots, hidden), f32),
            struct((count, slots, hidden), f32),
        ],
        us=2,
    )(x, slot_gate, w_gate, w_up, w_down)


def expert_back_kernel(place_ref, *refs, fast):
    x_ref, g_ref, active_ref, factor_ref, silu_ref = refs[:5]
    w_gate_ref, w_up_ref, w_down_ref, back_ref, dots_ref = refs[5:10]
    grads, (gate_low_ref, up_low_ref) = refs[10:-2], refs[-2:]
    slots, width = g_ref.shape[1], g_ref.shape[2]
    chunk = 256
    active_grad = dot(g_ref[0], w_down_ref[0])
    gate_low_ref[...] = (active_grad * factor_ref[0]).astype(bf16)
    up_low_ref[...] = (active_grad * silu_ref[0]).astype(bf16)
    dots = jnp.sum(active_ref[0].astype(f32) * active_grad, axis=1, keepdims=True)
    dots_ref[0] = jnp.broadcast_to(dots, (slots, LANES))
    back_ref[0] = (dot_nt(gate_low_ref[...], w_gate_ref[0]) + dot_nt(up_low_ref[...], w_up_ref[0])).astype(bf16)

    def products(cols):
        x = x_ref[0, :, cols]
        yield 0, dot_tn(x, gate_low_ref[...]).astype(bf16)
        yield 1, dot_tn(x, up_low_ref[...]).astype(bf16)
        yield 2, dot_tn(g_ref[0, :, cols], active_ref[0]).astype(bf16)

    if fast:
        write_shards(place_ref, grads, products, width)
    else:

        def whole_columns(index, carry):
            cols = pl.ds(pl.multiple_of(index * chunk, chunk), chunk)
            for which, product in products(cols):
                grads[which][0, cols, :] = product
            return carry

        lax.fori_loop(0, width // chunk, whole_columns, 0)


def write_shards(place_ref, outs, products, width):
    send_a, keep_a, send_b, keep_b = outs
    x_bit, y_bit = place_ref[3], place_ref[4]
    shard = width // 4
    for dy in range(2):
        for dx in range(2):
            x, y = x_bit ^ dx, y_bit ^ dy
            cols = pl.ds(pl.multiple_of((y * 2 + x) * shard, shard), shard)
            for which, product in products(cols):
                side = product.shape[1] // 2
                (send_a if dx else keep_a)[0, which, y] = product[:, :side]
                (send_b if dy else keep_b)[0, which, x] = product[:, side:]


def run_experts_back(place, x, g, active, factor, silu, w_gate, w_up, w_down, first, count, fast):
    slots, width = g.shape[1], g.shape[2]
    hidden = w_gate.shape[2]

    def taken(*shape):
        return pl.BlockSpec((1,) + shape, lambda e, p: (e + first, 0, 0))

    def given(*shape):
        zeros = (0,) * len(shape)
        return pl.BlockSpec((1,) + shape, lambda e, p: (e,) + zeros)

    if fast:
        grad_shapes = [(3, 2, width // 4, hidden // 2)] * 4
    else:
        grad_shapes = [(width, hidden)] * 3
    return call(
        lambda *refs: expert_back_kernel(*refs, fast=fast),
        (count,),
        1,
        [taken(slots, width)] * 2 + [taken(slots, hidden)] * 3 + [taken(width, hidden)] * 3,
        [given(slots, width), given(slots, LANES)] + [given(*shape) for shape in grad_shapes],
        [struct((count, slots, width), bf16), struct((count, slots, LANES), f32)]
        + [struct((count,) + shape, bf16) for shape in grad_shapes],
        scratch=[pltpu.VMEM((slots, hidden), bf16)] * 2,
        us=count,
    )(place, x, g, active, factor, silu, w_gate, w_up, w_down)


DOT_LANES = 2 * LANES


def combine_kernel(place_ref, rank_ref, *refs, pieces, with_dots, mine):
    parts, rest = refs[:pieces], refs[pieces:]
    rows = rank_ref.shape[2]
    local_experts = sum(part.shape[0] for part in parts)
    hits = hits_of(rank_ref[0], local_experts)
    gathered = jnp.concatenate([part[j, 0] for part in parts for j in range(part.shape[0])], axis=0)
    summed = dot_tn(chosen_of(hits), gathered)
    out_ref = rest[-1]
    if mine:
        arrived_ref = rest[-2]
        summed = summed + arrived_ref[0, 0:rows, :].astype(f32)
    out_ref[0, 0:rows, :] = summed.astype(bf16)
    if with_dots:
        column = [part[j, 0][:, 0:1] for part in rest[:pieces] for j in range(part.shape[0])]
        scattered = [
            jnp.sum(jnp.where(hit, value, 0.0), axis=0, keepdims=True) for hit, value in zip(hits, column)
        ]
        scattered.append(jnp.zeros((DOT_ROWS - local_experts, rows), f32))
        scattered = jnp.concatenate(scattered, axis=0)
        upper = scattered.astype(bf16)
        out_ref[0, rows:, :] = jnp.zeros((DOT_ROWS, out_ref.shape[2]), bf16)
        out_ref[0, rows:, 0:rows] = upper
        out_ref[0, rows:, DOT_LANES : DOT_LANES + rows] = (scattered - upper.astype(f32)).astype(bf16)
        if mine:
            out_ref[0, rows:, 2 * DOT_LANES : 4 * DOT_LANES] = arrived_ref[0, rows:, 0 : 2 * DOT_LANES]


def combine(place, rank, parts, dots=None, arrived=None):
    mine = arrived is not None
    rows, width = rank.shape[2], parts[0].shape[-1]
    out_rows = rows + (DOT_ROWS if dots else 0)

    def member(step, p):
        return (p[0] if mine else 1 - p[0]) * COLS + step

    def slots_of(array):
        return pl.BlockSpec((array.shape[0], 1) + array.shape[2:], lambda j, p: (0, member(j, p), 0, 0))

    inputs = [
        part.reshape(part.shape[0], 2 * COLS, CAPACITY, part.shape[-1]) for part in list(parts) + list(dots or [])
    ]
    in_specs = [pl.BlockSpec((1, 8, rows), lambda j, p: (member(j, p), 0, 0))] + [slots_of(item) for item in inputs]
    by_chip = pl.BlockSpec((1, out_rows, width), lambda j, p: (j, 0, 0))
    if mine:
        inputs.append(arrived)
        in_specs.append(by_chip)
    return call(
        lambda *refs: combine_kernel(*refs, pieces=len(parts), with_dots=bool(dots), mine=mine),
        (COLS,),
        1,
        in_specs,
        by_chip,
        struct((COLS, out_rows, width), bf16),
        us=0,
    )(place, rank, *inputs)


def split_dot(dimension_numbers, values, exact):
    upper = values.astype(bf16)
    lower = (values - upper.astype(f32)).astype(bf16)
    return lax.dot_general(
        upper, exact, dimension_numbers, preferred_element_type=f32
    ) + lax.dot_general(lower, exact, dimension_numbers, preferred_element_type=f32)


EXTRA_SLOTS = 6


def middle_back_kernel(
    place_ref, sums_ref, gates_ref, middle_ref, cot_ref, gain_ref, w_router_ref, w_mine_ref, w_other_ref,
    grad_ref, branch_ref, attended_ref, extra_ref
):
    rows = middle_ref.shape[0]
    tail = sums_ref[:, rows : rows + 8, 0 : 4 * DOT_LANES].astype(f32)
    mine = tail[:, :, 0:rows] + tail[:, :, DOT_LANES : DOT_LANES + rows]
    other = tail[:, :, 2 * DOT_LANES : 2 * DOT_LANES + rows] + tail[:, :, 3 * DOT_LANES : 3 * DOT_LANES + rows]
    first_row = place_ref[0] == 0
    dots = jnp.concatenate([jnp.where(first_row, mine, other), jnp.where(first_row, other, mine)], axis=0)
    dots = dots.reshape(dots.shape[0] * 8, rows)
    gates = gates_ref[...]
    logit_grad = dots - gates * jnp.sum(dots, axis=0, keepdims=True)
    middle = middle_ref[...]
    inverse = lax.rsqrt(jnp.mean(middle * middle, axis=1, keepdims=True) + epsilon)
    unit = middle * inverse
    gain = gain_ref[...]
    grad = sums_ref[0, 0:rows].astype(f32)
    for index in range(1, sums_ref.shape[0]):
        grad = grad + sums_ref[index, 0:rows].astype(f32)
    grad = grad + split_dot(TN, logit_grad, w_router_ref[...])
    gain_grad = jnp.sum(grad * unit, axis=0, keepdims=True)
    scaled = grad * gain
    middle_grad = cot_ref[...].astype(f32) + inverse * (
        scaled - unit * jnp.mean(scaled * unit, axis=1, keepdims=True)
    )
    grad_ref[...] = middle_grad
    branch_grad = middle_grad.astype(bf16)
    branch_ref[0:rows, :] = branch_grad
    extra_ref[...] = jnp.zeros_like(extra_ref)
    for index in range(logit_grad.shape[0] // 8):
        first, lane = index // EXTRA_SLOTS * 8, index % EXTRA_SLOTS * DOT_LANES
        extra_ref[first : first + 8, lane : lane + rows] = logit_grad[index * 8 : index * 8 + 8]
    upper = gain_grad.astype(bf16).astype(f32)
    extra_ref[13:14, :] = upper
    extra_ref[14:15, :] = gain_grad - upper
    branch_ref[rows:, :] = extra_ref[...].astype(bf16)
    for which, ref in enumerate((w_mine_ref, w_other_ref)):
        line = place_ref[0] if which == 0 else 1 - place_ref[0]
        for col in range(ref.shape[0]):
            product = dot_nt(branch_grad, ref[col])
            member = line * COLS + col
            attended_ref[member, :, 0:LANES] = product[:, 0:LANES].astype(bf16)
            attended_ref[member, :, LANES : LANES + HEAD_DIM] = product[:, LANES:].astype(bf16)
            attended_ref[member, :, LANES + HEAD_DIM :] = jnp.zeros((product.shape[0], HEAD_DIM), bf16)


def middle_back(place, sums, gates, middle, cotangent, gain, w_router, w_mine, w_other):
    rows, width = middle.shape
    members = 2 * COLS
    args = (sums, gates, middle, cotangent, gain, w_router, w_mine, w_other)
    return call(
        middle_back_kernel,
        (1,),
        1,
        [whole(item.shape) for item in args],
        [whole((rows, width)), whole((rows + DOT_ROWS, width)), whole((members, rows, 2 * LANES))],
        [
            struct((rows, width), f32),
            struct((rows + DOT_ROWS, width), bf16),
            struct((members, rows, 2 * LANES), bf16),
        ],
        scratch=[pltpu.VMEM((DOT_ROWS, width), f32)],
        us=7,
    )(place, *args)


def input_grad_kernel(
    place_ref, grads_ref, w_mine_ref, w_other_ref, tok_ref, middle_grad_ref, gain_ref, out_ref, sum_ref
):
    step = pl.program_id(0)

    @pl.when(step == 0)
    def _():
        sum_ref[...] = jnp.zeros_like(sum_ref)

    def add(ref):
        sum_ref[...] += dot(grads_ref[0], jnp.concatenate([ref[0], ref[0, 4 * HEAD_DIM :]], axis=0))

    @pl.when(step < COLS)
    def _():
        add(w_mine_ref)

    @pl.when(step >= COLS)
    def _():
        add(w_other_ref)

    @pl.when(step == pl.num_programs(0) - 1)
    def _():
        resid = tok_ref[...].astype(f32)
        inverse = lax.rsqrt(jnp.mean(resid * resid, axis=1, keepdims=True) + epsilon)
        unit = resid * inverse
        scaled = sum_ref[...] * gain_ref[...]
        out_ref[...] = middle_grad_ref[...] + inverse * (
            scaled - unit * jnp.mean(scaled * unit, axis=1, keepdims=True)
        )


def input_grad(place, grads, w_mine, w_other, tokens, middle_grad, gain):
    rows, width = tokens.shape
    members, lanes = grads.shape[0], grads.shape[2]
    w_shape = (1,) + w_mine.shape[1:]

    def member(step, p):
        line = jnp.where(step < COLS, p[0], 1 - p[0])
        return line * COLS + lax.rem(step, COLS)

    return call(
        input_grad_kernel,
        (members,),
        1,
        [
            pl.BlockSpec((1, rows, lanes), lambda m, p: (member(m, p), 0, 0)),
            pl.BlockSpec(w_shape, lambda m, p: (jnp.minimum(m, COLS - 1), 0, 0)),
            pl.BlockSpec(w_shape, lambda m, p: (jnp.maximum(m - COLS, 0), 0, 0)),
            whole((rows, width)),
            whole((rows, width)),
            whole((1, width)),
        ],
        whole((rows, width)),
        struct((rows, width), f32),
        scratch=[pltpu.VMEM((rows, width), f32)],
        us=10,
    )(place, grads, w_mine, w_other, tokens, middle_grad, gain)


def own_weights_kernel(normed_ref, projected_ref, w_ref, gain_ref, out_ref, gain_grad_ref, sum_ref):
    step = pl.program_id(0)

    @pl.when(step == 0)
    def _():
        sum_ref[...] = jnp.zeros_like(sum_ref)

    sum_ref[...] += dot_tn(normed_ref[...], projected_ref[...])

    @pl.when(step == pl.num_programs(0) - 1)
    def _():
        total = sum_ref[...]
        out_ref[...] = total.astype(bf16)
        by_weight = jnp.sum(total * w_ref[...].astype(f32), axis=1, keepdims=True)
        gain_grad_ref[...] = jnp.broadcast_to(by_weight / gain_ref[...], gain_grad_ref.shape)


def own_weights(normed, projected, w_natural, gain):
    total, width = normed.shape
    lanes = projected.shape[1]
    rows = 512
    return call(
        own_weights_kernel,
        (total // rows,),
        0,
        [
            pl.BlockSpec((rows, width), lambda j: (j, 0)),
            pl.BlockSpec((rows, lanes), lambda j: (j, 0)),
            whole((width, lanes)),
            whole((width, 1)),
        ],
        [whole((width, lanes)), whole((width, 8))],
        [struct((width, lanes), bf16), struct((width, 8), f32)],
        scratch=[pltpu.VMEM((width, lanes), f32)],
        us=8,
    )(normed, projected, w_natural, gain)


def out_weights_kernel(place_ref, branch_ref, att_ref, normed_ref, own_ref, *refs, fast, local_experts):
    outs, small_ref, (sum_ref, gain_sum_ref) = refs[:-3], refs[-3], refs[-2:]
    step = pl.program_id(0)
    rows = att_ref.shape[0] // 2
    block = rows + DOT_ROWS

    @pl.when(step == 0)
    def _():
        sum_ref[...] = jnp.zeros_like(sum_ref)
        small_ref[...] = jnp.zeros_like(small_ref)
        gain_sum_ref[...] = jnp.zeros_like(gain_sum_ref)

    branch = jnp.concatenate([branch_ref[0:rows, :], branch_ref[block : block + rows, :]], axis=0)
    sum_ref[...] += dot_tn(branch, att_ref[...])
    for which in range(2):
        tail = branch_ref[which * block + rows : (which + 1) * block, :].astype(f32)
        slots = []
        for index in range(small_ref.shape[0] // 8):
            first, lane = index // EXTRA_SLOTS * 8, index % EXTRA_SLOTS * DOT_LANES
            slots.append(tail[first : first + 8, lane : lane + rows])
        logit_grad = jnp.concatenate(slots, axis=0)
        real = lax.broadcasted_iota(jnp.int32, logit_grad.shape, 0) % 8 < local_experts
        logit_grad = jnp.where(real, logit_grad, 0.0).astype(bf16)
        small_ref[...] += dot(logit_grad, normed_ref[which * rows : (which + 1) * rows, :])
        gain_sum_ref[...] += tail[8:16, :]

    @pl.when(step == pl.num_programs(0) - 1)
    def _():
        small_ref[7:8, :] = gain_sum_ref[5:6, :] + gain_sum_ref[6:7, :]

        def products(cols):
            own = own_ref[cols, 0 : 2 * LANES]
            out_one = sum_ref[cols, 0:LANES].astype(bf16)
            out_two = sum_ref[cols, LANES:]
            low = lane_of(out_two.shape) < HEAD_DIM
            tail = jnp.where(low, out_two, own_ref[cols, 2 * LANES :].astype(f32)).astype(bf16)
            yield 0, jnp.concatenate([own, out_one, tail], axis=1)

        if fast:
            write_shards(place_ref, outs, products, own_ref.shape[0])
        else:
            outs[0][...] = next(products(slice(0, own_ref.shape[0])))[1]


def out_weights(place, branch, attended, normed, own, padded, local_experts, fast):
    total, width = normed.shape
    rows = total // COLS
    blocks = branch.shape[0] // COLS
    if fast:
        shapes = [(1, 1, 2, width // 4, 2 * LANES)] * 4
    else:
        shapes = [(width, 4 * LANES)]
    return call(
        lambda *refs: out_weights_kernel(*refs, fast=fast, local_experts=local_experts),
        (COLS,),
        1,
        [
            pl.BlockSpec((blocks, width), lambda j, p: (j, 0)),
            pl.BlockSpec((rows, 2 * LANES), lambda j, p: (j, 0)),
            pl.BlockSpec((rows, width), lambda j, p: (j, 0)),
            whole(own.shape),
        ],
        [whole(shape) for shape in shapes] + [whole((padded, width))],
        [struct(shape, bf16) for shape in shapes] + [struct((padded, width), f32)],
        scratch=[pltpu.VMEM((width, 2 * LANES), f32), pltpu.VMEM((8, width), f32)],
        us=7,
    )(place, branch, attended, normed, own)


def first_sum_kernel(place_ref, *refs, counts):
    outs = refs[4 * len(counts) :]
    x_bit, y_bit = place_ref[3], place_ref[4]
    expert = pl.program_id(0)
    first = 0
    for index, count in enumerate(counts):
        parts = refs[4 * index : 4 * index + 4]

        @pl.when((expert >= first) & (expert < first + count))
        def _(parts=parts):
            for side, bit in enumerate((y_bit, x_bit)):
                keep, got = parts[2 * side], parts[2 * side + 1]
                send, held = outs[2 * side], outs[2 * side + 1]
                held[0, 0] = keep[0, 0, bit].astype(f32) + got[0, 0, bit].astype(f32)
                send[0, 0] = (keep[0, 0, 1 - bit].astype(f32) + got[0, 0, 1 - bit].astype(f32)).astype(bf16)

        first += count


def first_sum(place, chunks):
    counts = [chunk[0].shape[0] for chunk in chunks]
    _, kinds, _, rows, cols = chunks[0][0].shape
    specs, first = [], 0
    for count in counts:

        def taken(e, k, p, first=first, count=count):
            inside = (e >= first) & (e < first + count)
            kind = jnp.where(inside, k, jnp.where(e < first, 0, kinds - 1))
            return (jnp.clip(e - first, 0, count - 1), kind, 0, 0, 0)

        specs += [pl.BlockSpec((1, 1, 2, rows, cols), taken)] * 4
        first += count
    given = pl.BlockSpec((1, 1, rows, cols), lambda e, k, p: (e, k, 0, 0))
    shape = (first, kinds, rows, cols)
    return call(
        lambda *refs: first_sum_kernel(*refs, counts=counts),
        (first, kinds),
        1,
        specs,
        [given] * 4,
        [struct(shape, bf16), struct(shape, f32), struct(shape, bf16), struct(shape, f32)],
        us=4 * first,
    )(place, *[item for chunk in chunks for item in chunk])


def last_sum_kernel(held_a_ref, got_a_ref, held_b_ref, got_b_ref, *rest):
    outs = rest[-3:]
    side = held_a_ref.shape[3]
    for which, out in enumerate(outs):
        out[0, :, :side] = held_a_ref[0, which] + got_a_ref[0, which].astype(f32)
        out[0, :, side:] = held_b_ref[0, which] + got_b_ref[0, which].astype(f32)


def last_sum(held_a, got_a, held_b, got_b, first, total, before):
    count, kinds, rows, cols = held_a.shape
    taken = pl.BlockSpec((1, kinds, rows, cols), lambda e: (e, 0, 0, 0))
    given = pl.BlockSpec((1, rows, 2 * cols), lambda e: (e + first, 0, 0))
    extra = list(before) if before else []
    return call(
        last_sum_kernel,
        (count,),
        0,
        [taken] * 4 + [pl.BlockSpec(memory_space=pl.ANY)] * len(extra),
        [given] * 3,
        [struct((total, rows, 2 * cols), f32)] * 3,
        us=2.5 * count,
        aliases={4 + i: i for i in range(len(extra))},
    )(held_a, got_a, held_b, got_b, *extra)


SWAP = [(0, 1), (1, 0)]


def after(value, *events):
    return lax.optimization_barrier((value,) + events)[0]


def gather_group(block):
    return lax.all_gather(block, ("row", "col"), axis=0, tiled=True)


def flip(value, axis, bit, size):
    return lax.ppermute(value, axis, [(i, i ^ (1 << bit)) for i in range(size)])


def bits_of(size):
    return size.bit_length() - 1


def own_bit(axis, bit):
    return (lax.axis_index(axis) >> bit) & 1


def joined(mine, got, own):
    return jnp.where(own == 0, jnp.concatenate([mine, got]), jnp.concatenate([got, mine]))


def cube_step(value, axis, bit, size):
    return joined(value, flip(value, axis, bit, size), own_bit(axis, bit))


def cube_gather(value, axis, size):
    value = value[None]
    for bit in range(bits_of(size)):
        value = cube_step(value, axis, bit, size)
    return value


def sum_group(value, sizes):
    for axis, bit in (("row", 0), ("col", 0), ("col", 1)):
        value = value + flip(value, axis, bit, sizes[axis])
    return value


def sum_dp(value, sizes):
    for bit in range(bits_of(sizes["dp"])):
        value = value + flip(value, "dp", bit, sizes["dp"])
    return value


def reduce_over_dp(value, size):
    count = bits_of(size)
    value = value.reshape(value.shape[:1] + (2,) * count + value.shape[2:])
    current = value
    for bit in range(count - 1, -1, -1):
        own = own_bit("dp", bit)
        keep = lax.dynamic_index_in_dim(current, own, 1, keepdims=False)
        send = lax.dynamic_index_in_dim(current, 1 - own, 1, keepdims=False).astype(bf16)
        current = keep.astype(f32) + flip(send, "dp", bit, size).astype(f32)
    return current


def start_move(run, size):
    return flip(run[0], "dp", 0, size), flip(run[2], "dp", 1, size)


def first_half(place, runs, gots, size, event):
    chunks = []
    for run, got in zip(runs, gots):
        keep_a, keep_b = after((run[1], run[3]), event)
        chunks.append((keep_a, got[0], keep_b, got[1]))
    send_a, held_a, send_b, held_b = first_sum(place, chunks)
    return held_a, flip(send_a, "dp", 1, size), held_b, flip(send_b, "dp", 0, size)


def layer(sizes):
    n_dp, n_row, n_col = sizes["dp"], sizes["row"], sizes["col"]
    members = n_row * n_col
    fast = n_dp == 4
    assert n_row == 2 and n_col == COLS and n_dp & (n_dp - 1) == 0

    def local(
        tokens, cotangent, routes, lengths, gain_attn, w_query, w_key, w_value, w_out,
        gain_moe, w_router, w_gate, w_up, w_down,
    ):
        rows, width = tokens.shape
        group = rows * members
        local_experts = w_gate.shape[0]
        row, col, dp = lax.axis_index("row"), lax.axis_index("col"), lax.axis_index("dp")
        place = jnp.stack([row, col, row * n_col + col, dp & 1, (dp >> 1) & 1]).astype(jnp.int32)
        gain_one = gain_attn.astype(f32)[None]
        gain_two = gain_moe.astype(f32)[None]

        tok_all = gather_group(tokens)
        w_in = jnp.concatenate([w_query.T, w_key.T, w_value.T], axis=0)
        out_share, in_share = rows // n_dp, w_in.shape[0] // n_dp
        shares = jnp.concatenate(
            [
                lax.dynamic_slice(w_out.T, (dp * out_share, 0), (out_share, width)),
                lax.dynamic_slice(w_in, (dp * in_share, 0), (in_share, width)),
                jnp.pad(routes.T.astype(bf16).reshape(1, TOP * rows), ((0, 7), (0, width - TOP * rows))),
            ],
            axis=0,
        )
        shares = cube_gather(after(shares, tok_all), "col", n_col)
        route_rows = shares[:, out_share + in_share]
        out_half = cube_step(shares[None, :, :out_share], "dp", 0, n_dp)
        in_half = cube_step(shares[None, :, out_share : out_share + in_share], "dp", 0, n_dp)

        def finish(value, event):
            value = after(value, event)
            for bit in range(1, bits_of(n_dp)):
                value = cube_step(value, "dp", bit, n_dp)
            value = jnp.transpose(value, (1, 0, 2, 3)).reshape(n_col, n_dp * value.shape[2], width)
            return value

        w_stack = jnp.concatenate([w_query.T, w_key.T, w_value.T, w_value.T], axis=0)
        w_natural = jnp.concatenate([w_query, w_key, w_value, w_value], axis=1)

        ends = jnp.cumsum(lengths[0])
        starts = ends - lengths[0]
        position = jnp.arange(group, dtype=jnp.int32)
        segment = jnp.sum((position[:, None] >= ends[None, :]).astype(jnp.int32), axis=1)
        member = segment[:, None] == jnp.arange(starts.shape[0], dtype=jnp.int32)[None, :]
        start = jnp.sum(jnp.where(member, starts[None, :], 0), axis=1).astype(jnp.int32)
        frequency = rope_base ** (-2.0 * jnp.arange(HEAD_DIM // 2, dtype=f32) / HEAD_DIM)
        angle = (position - start).astype(f32)[:, None] * frequency[None, :]
        cosine = jnp.tile(jnp.cos(angle), (1, 4))
        sine = jnp.tile(jnp.sin(angle), (1, 4))

        query, key, value, normed_one = project(tok_all, gain_one, w_stack, cosine, sine)
        w_router_rows = w_router.T.reshape(members, local_experts, width)
        w_router_rows = jnp.pad(w_router_rows, ((0, 0), (0, 8 - local_experts), (0, 0)))
        w_router_rows = w_router_rows.reshape(members * 8, width)
        packed, attended, totals = attend(query, key, value, start[:, None])
        att_flat = gather_group(after(packed, shares))
        att_all = att_flat.reshape((n_row, n_col) + packed.shape)
        w_out_mine = finish(out_half, packed)
        w_out_other = lax.ppermute(w_out_mine, "row", SWAP)
        w_in_mine = finish(in_half, w_out_mine)
        route_rows = cube_gather(route_rows, "row", n_row)[:, :, : TOP * rows].reshape(members, TOP, rows)
        route_rows = jnp.pad(route_rows, ((0, 0), (0, ROUTE_ROWS - TOP), (0, 2 * LANES - rows)))
        cot_all = gather_group(after(cotangent, att_flat))
        x, slot_gate, rank, gate, normed_two, middle, gates = middle_and_dispatch(
            place, att_all, w_out_mine, after(w_out_other, in_half), tok_all, route_rows, gain_two, w_router_rows, local_experts
        )
        slots = members * CAPACITY
        x = x.reshape(local_experts, slots, width)
        slot_gate = slot_gate.reshape(local_experts, slots, LANES)
        rank, gate = rank.reshape(members, 8, rows), gate.reshape(members, 8, rows)
        forth, active, factor, silu = run_experts(x, slot_gate, w_gate, w_up, w_down)
        forth_other = combine(place, after(rank, w_in_mine), [forth])
        w_in_other = lax.ppermute(w_in_mine, "row", SWAP)
        arrived = lax.ppermute(forth_other, "row", SWAP)
        g = grad_dispatch(after(rank, forth_other), gate, cot_all, local_experts)
        g = g.reshape(local_experts, slots, width)
        cuts = [0, 1, 3, local_experts]

        def backward(which, x):
            first, last = cuts[which], cuts[which + 1]
            return run_experts_back(place, x, g, active, factor, silu, w_gate, w_up, w_down, first, last - first, fast)

        runs = [backward(0, x)]
        forth_mine = combine(place, rank, [forth], arrived=after(arrived, runs[0][1]))
        forth_sums = lax.all_to_all(forth_mine, "col", 0, 0, tiled=True)
        runs.append(backward(1, after(x, forth_mine)))
        runs.append(backward(2, after(x, runs[1][1], w_in_other)))
        moved = [start_move(run[2:], n_dp) for run in runs] if fast else []
        back_parts, dot_parts = [run[0] for run in runs], [run[1] for run in runs]
        back_other = combine(place, after(rank, *moved[0]) if fast else rank, back_parts, dot_parts)
        arrived = lax.ppermute(back_other, "row", SWAP)
        back_mine = combine(place, rank, back_parts, dot_parts, arrived)
        back_mine = after(back_mine, forth_sums)
        back_sums = lax.all_to_all(back_mine, "col", 0, 0, tiled=True)

        middle_grad, branch_grad, attended_grad = middle_back(
            place, back_sums, gates, middle, cotangent, after(gain_two, *moved[1]) if fast else gain_two,
            w_router_rows, w_out_mine, w_out_other,
        )
        started = []
        if fast:
            started.append(first_half(place, [run[2:] for run in runs[:2]], moved[:2], n_dp, branch_grad))
        attended_grad = lax.all_to_all(attended_grad, ("row", "col"), 0, 0, tiled=True)
        branch_all = gather_group(branch_grad)

        start_row = jnp.broadcast_to(start[None, :], (8, group))
        attended_grad = attended_grad.reshape(group, 2 * LANES)
        if fast:
            attended_grad = after(attended_grad, started[0][0])
        projected_grad = attend_back(query, key, value, attended_grad, totals, start_row, cosine, sine)
        projected_all = lax.all_to_all(
            projected_grad.reshape(members, rows, 3 * LANES), ("row", "col"), 0, 0, tiled=True
        )
        own_grads, gain_part = own_weights(
            after(normed_one, *moved[2]) if fast else normed_one,
            projected_grad, w_natural, gain_attn.astype(f32)[:, None],
        )
        if fast:
            started.append(first_half(place, [runs[2][2:]], moved[2:], n_dp, own_grads))
        *w_parts, small = out_weights(
            place, branch_all, attended, normed_two.reshape(group, width), own_grads, members * 8, local_experts, fast
        )
        gain_attn_grad = sum_group(gain_part[:, 0].reshape(8, width // 8), sizes)
        if fast:
            w_started = first_half(place, [w_parts], [start_move(w_parts, n_dp)], n_dp, w_parts[1])
        else:
            cut = w_parts[0].reshape(1, n_dp, width // n_dp, w_parts[0].shape[1])
            w_sum = reduce_over_dp(cut, n_dp)[0]

        mixed = (middle + jnp.sum(after(forth_sums, projected_grad).astype(f32), axis=0)).astype(bf16)

        used = small.reshape(members, 8, width)[:, :local_experts].reshape(members * local_experts, width)
        both = jnp.concatenate([used, small[7:8], gain_attn_grad.reshape(1, width)], axis=0)
        both = sum_dp(both, sizes)
        w_router_grad = both[: members * local_experts].T
        gain_moe_grad, gain_attn_grad = both[members * local_experts], both[members * local_experts + 1]

        tokens_grad = input_grad(
            place, projected_all, w_in_mine, w_in_other, tokens, middle_grad, after(gain_one, w_parts[0])
        )

        if fast:
            expert_grads = None
            for item, first, event in zip(started, (0, cuts[2]), (own_grads, w_parts[0])):
                held_a, got_a, held_b, got_b = item
                held_a, held_b = after((held_a, held_b), event)
                expert_grads = last_sum(held_a, got_a, held_b, got_b, first, local_experts, expert_grads)
            held_a, got_a, held_b, got_b = [item[0, 0] for item in w_started]
            left = held_a + got_a.astype(f32)
            right = held_b + got_b.astype(f32)
            w_sum = jnp.concatenate([left, right], axis=1)
        else:
            expert_grads = []
            for which in range(3):
                parts = [run[2 + which] for run in runs]
                parts = [part.reshape(part.shape[0], n_dp, width // n_dp, part.shape[2]) for part in parts]
                expert_grads.append(jnp.concatenate([reduce_over_dp(part, n_dp) for part in parts], axis=0))
        w_gate_grad, w_up_grad, w_down_grad = expert_grads
        local_q, local_k = w_query.shape[1], w_key.shape[1]
        cut = local_q + local_k
        return (
            mixed, tokens_grad, gain_attn_grad, w_sum[:, :local_q], w_sum[:, local_q:cut],
            w_sum[:, cut + local_q :], w_sum[:, cut : cut + local_q],
            gain_moe_grad, w_router_grad, w_gate_grad, w_up_grad, w_down_grad,
        )

    return local


def solution(mesh):
    return jax.shard_map(
        layer(dict(mesh.shape)),
        mesh=mesh,
        in_specs=(
            P(("dp", "row", "col"), None),
            P(("dp", "row", "col"), None),
            P(("dp", "row", "col"), None),
            P("dp", None),
            P(),
            P(None, ("row", "col")),
            P(None, ("row", "col")),
            P(None, ("row", "col")),
            P(None, ("row", "col")),
            P(),
            P(),
            P(("row", "col"), None, None),
            P(("row", "col"), None, None),
            P(("row", "col"), None, None),
        ),
        out_specs=(
            P(("dp", "row", "col"), None),
            P(("dp", "row", "col"), None),
            P(),
            P("dp", ("row", "col")),
            P("dp", ("row", "col")),
            P("dp", ("row", "col")),
            P("dp", ("row", "col")),
            P(),
            P(),
            P(("row", "col"), "dp", None),
            P(("row", "col"), "dp", None),
            P(("row", "col"), "dp", None),
        ),
        check_vma=False,
    )
```

```python
import math

import jax
import jax.numpy as jnp
from jax import lax
from jax.experimental import pallas as pl
from jax.experimental.pallas import tpu as pltpu
from jax.sharding import PartitionSpec as P

HEAD_DIM = 64
EXPERTS = 40
TOP = 8
CAPACITY = 64
COLS = 4
LANES = 128
QUERY_BLOCK = 256
ROUTE_ROWS = 16
DOT_ROWS = 16

epsilon = 1e-06
rope_base = 10000.0
masked_score = -1e30
f32 = jnp.float32
bf16 = jnp.bfloat16
VMEM_LIMIT = 56 * 1024 * 1024

NT = (((1,), (1,)), ((), ()))
TN = (((0,), (0,)), ((), ()))


def dot(a, b):
    return jnp.dot(a, b, preferred_element_type=f32)


def dot_nt(a, b):
    return lax.dot_general(a, b, NT, preferred_element_type=f32)


def dot_tn(a, b):
    return lax.dot_general(a, b, TN, preferred_element_type=f32)


def lane_of(shape):
    return lax.broadcasted_iota(jnp.int32, shape, len(shape) - 1)


def call(
    kernel, grid, prefetch, in_specs, out_specs, out_shape, scratch=(), us=1.0, aliases=None
):
    return pl.pallas_call(
        kernel,
        grid_spec=pltpu.PrefetchScalarGridSpec(
            num_scalar_prefetch=prefetch,
            grid=grid,
            in_specs=in_specs,
            out_specs=out_specs,
            scratch_shapes=list(scratch),
        ),
        out_shape=out_shape,
        input_output_aliases=aliases or {},
        compiler_params=pltpu.CompilerParams(
            vmem_limit_bytes=VMEM_LIMIT, dimension_semantics=("arbitrary",) * len(grid)
        ),
        cost_estimate=pl.CostEstimate(
            flops=int(us * 1.1e9), bytes_accessed=int(us * 3.6e6), transcendentals=0
        ),
    )


def whole(shape):
    zeros = (0,) * len(shape)
    return pl.BlockSpec(shape, lambda *_: zeros)


def struct(shape, dtype):
    return jax.ShapeDtypeStruct(shape, dtype)


def turn_within_heads(values, sign):
    lane = lane_of(values.shape) % HEAD_DIM
    ahead = pltpu.roll(values, LANES - HEAD_DIM // 2, 1)
    behind = pltpu.roll(values, HEAD_DIM // 2, 1)
    return jnp.where(lane < HEAD_DIM // 2, -sign * ahead, sign * behind)


def project_kernel(
    tok_ref, gain_ref, w_ref, cos_ref, sin_ref, query_ref, key_ref, value_ref, normed_ref
):
    resid = tok_ref[...].astype(f32)
    inverse = lax.rsqrt(jnp.mean(resid * resid, axis=1, keepdims=True) + epsilon)
    normed = (resid * inverse * gain_ref[...]).astype(bf16)
    normed_ref[...] = normed
    raw = dot_nt(normed, w_ref[...])
    cosine, sine = cos_ref[...], sin_ref[...]

    def rot(values):
        return (values * cosine + turn_within_heads(values, 1.0) * sine).astype(bf16).astype(f32)

    first = rot(raw[:, :LANES])
    second = rot(raw[:, LANES : 2 * LANES])
    low = lane_of(first.shape) < HEAD_DIM
    scale = 1.0 / math.sqrt(HEAD_DIM)
    query_ref[0] = jnp.where(low, first * scale, 0.0).astype(bf16)
    query_ref[1] = jnp.where(low, 0.0, first * scale).astype(bf16)
    query_ref[2] = jnp.where(low, second * scale, 0.0).astype(bf16)
    key_ref[...] = jnp.where(low, pltpu.roll(second, HEAD_DIM, 1), second).astype(bf16)
    value_ref[...] = raw[:, 2 * LANES :].astype(bf16)


def project(tokens, gain, w_stack, cosine, sine):
    total, width = tokens.shape
    rows = 512
    lanes = pl.BlockSpec((rows, LANES), lambda j: (j, 0))
    wide = pl.BlockSpec((rows, width), lambda j: (j, 0))
    return call(
        project_kernel,
        (total // rows,),
        0,
        [wide, whole((1, width)), whole(w_stack.shape), lanes, lanes],
        [pl.BlockSpec((3, rows, LANES), lambda j: (0, j, 0)), lanes, lanes, wide],
        [
            struct((3, total, LANES), bf16),
            struct((total, LANES), bf16),
            struct((total, LANES), bf16),
            struct((total, width), bf16),
        ],
        us=0.5,
    )(tokens, gain, w_stack, cosine, sine)


def attend_kernel(query_ref, key_ref, value_ref, start_ref, packed_ref, plain_ref, total_ref, out_ref):
    blocks = query_ref.shape[1] // QUERY_BLOCK
    block = pl.program_id(0)
    for index in range(blocks):

        @pl.when(block == index)
        def _(index=index):
            rows = pl.ds(index * QUERY_BLOCK, QUERY_BLOCK)
            span = (index + 1) * QUERY_BLOCK
            row = index * QUERY_BLOCK + lax.broadcasted_iota(jnp.int32, (QUERY_BLOCK, span), 0)
            column = lane_of((QUERY_BLOCK, span))
            allowed = (column <= row) & (column >= start_ref[rows, :])

            def head(number, carry):
                scores = dot_nt(query_ref[number, rows, :], key_ref[0:span, :])
                scores = jnp.where(allowed, scores, masked_score)
                peak = jnp.max(scores, axis=1, keepdims=True)
                weights = jnp.exp(scores - peak)
                summed = jnp.sum(weights, axis=1, keepdims=True)
                probs = (weights * (1.0 / summed)).astype(bf16)
                out_ref[number] = dot(probs, value_ref[0:span, :])
                total = jnp.broadcast_to(peak + jnp.log(summed), (QUERY_BLOCK, LANES))
                total_ref[number, :, rows] = jnp.transpose(total)[0:8, :]
                return carry

            lax.fori_loop(0, 3, head, 0)
            low = lane_of((QUERY_BLOCK, LANES)) < HEAD_DIM
            one, two, three = out_ref[0], out_ref[1], out_ref[2]
            pair = jnp.where(low, one, two).astype(bf16)
            plain_ref[rows, 0:LANES] = pair
            plain_ref[rows, LANES : 2 * LANES] = jnp.where(low, three, 0.0).astype(bf16)
            if index < blocks // 2:
                packed_ref[rows, 0:LANES] = pair
                packed_ref[rows, LANES : 2 * LANES] = three.astype(bf16)
            else:
                back = pl.ds((index - blocks // 2) * QUERY_BLOCK, QUERY_BLOCK)
                before = packed_ref[back, LANES : 2 * LANES].astype(f32)
                packed_ref[back, LANES : 2 * LANES] = jnp.where(low, before, one).astype(bf16)
                packed_ref[back, 2 * LANES : 3 * LANES] = jnp.where(low, two, three).astype(bf16)


def attend(query, key, value, start):
    total = key.shape[0]
    return call(
        attend_kernel,
        (total // QUERY_BLOCK,),
        0,
        [whole(query.shape), whole(key.shape), whole(value.shape), whole(start.shape)],
        [whole((total // 2, 3 * LANES)), whole((total, 2 * LANES)), whole((3, 8, total))],
        [
            struct((total // 2, 3 * LANES), bf16),
            struct((total, 2 * LANES), bf16),
            struct((3, 8, total), f32),
        ],
        scratch=[pltpu.VMEM((3, QUERY_BLOCK, LANES), f32)],
        us=0.5,
    )(query, key, value, start)


def attend_back_kernel(
    query_ref, key_ref, value_ref, grad_ref, total_ref, start_ref, cos_ref, sin_ref,
    out_ref, query_grad_ref, key_grad_ref, value_grad_ref
):
    blocks = query_ref.shape[1] // QUERY_BLOCK
    block = pl.program_id(0)
    scale = 1.0 / math.sqrt(HEAD_DIM)

    @pl.when(block == 0)
    def _():
        key_grad_ref[...] = jnp.zeros_like(key_grad_ref)
        value_grad_ref[...] = jnp.zeros_like(value_grad_ref)

    def back(values, cosine, sine):
        return values * cosine + turn_within_heads(values * sine, -1.0)

    for index in range(blocks):

        @pl.when(block == index)
        def _(index=index):
            rows = pl.ds(index * QUERY_BLOCK, QUERY_BLOCK)
            span = (index + 1) * QUERY_BLOCK
            row = index * QUERY_BLOCK + lane_of((span, QUERY_BLOCK))
            column = lax.broadcasted_iota(jnp.int32, (span, QUERY_BLOCK), 0)
            allowed = (column <= row) & (column >= start_ref[0:1, rows])
            low = lane_of((QUERY_BLOCK, LANES)) < HEAD_DIM

            def head(number, carry):
                query = query_ref[number, rows, :]
                tile = pl.multiple_of((number // 2) * LANES, LANES)
                upstream = grad_ref[rows, pl.ds(tile, LANES)].astype(f32)
                keep = low == (number != 1)
                upstream = jnp.where(keep, upstream, 0.0).astype(bf16)
                scores = dot_nt(key_ref[0:span, :], query)
                probs = jnp.exp(scores - total_ref[number, 0:1, rows])
                probs = jnp.where(allowed, probs, 0.0)
                prob_grad = dot_nt(value_ref[0:span, :], upstream)
                row_dot = jnp.sum(probs * prob_grad, axis=0, keepdims=True)
                score_grad = (probs * (prob_grad - row_dot)).astype(bf16)
                key_grad_ref[0:span, :] += dot(score_grad, query)
                value_grad_ref[0:span, :] += dot(probs.astype(bf16), upstream)
                query_grad_ref[number] = dot_tn(score_grad, key_ref[0:span, :]) * scale
                return carry

            lax.fori_loop(0, 3, head, 0)
            cosine, sine = cos_ref[rows, :], sin_ref[rows, :]
            pair = jnp.where(low, query_grad_ref[0], query_grad_ref[1])
            out_ref[rows, 0:LANES] = back(pair, cosine, sine).astype(bf16)
            out_ref[rows, LANES : 2 * LANES] = back(query_grad_ref[2], cosine, sine).astype(bf16)

    @pl.when(block == blocks - 1)
    def _():
        low = lane_of(key_grad_ref.shape) < HEAD_DIM
        key_grad = key_grad_ref[...]
        key_grad = key_grad + pltpu.roll(key_grad, HEAD_DIM, 1)
        key_grad = back(key_grad, cos_ref[...], sin_ref[...])
        before = out_ref[:, LANES : 2 * LANES].astype(f32)
        out_ref[:, LANES : 2 * LANES] = jnp.where(low, before, key_grad).astype(bf16)
        value_grad = value_grad_ref[...]
        value_grad = value_grad + pltpu.roll(value_grad, HEAD_DIM, 1)
        out_ref[:, 2 * LANES : 3 * LANES] = jnp.where(low, 0.0, value_grad).astype(bf16)


def attend_back(query, key, value, grad, totals, start, cosine, sine):
    total = key.shape[0]
    args = (query, key, value, grad, totals, start, cosine, sine)
    return call(
        attend_back_kernel,
        (total // QUERY_BLOCK,),
        0,
        [whole(item.shape) for item in args],
        whole((total, 3 * LANES)),
        struct((total, 3 * LANES), bf16),
        scratch=[
            pltpu.VMEM((3, QUERY_BLOCK, LANES), f32),
            pltpu.VMEM((total, LANES), f32),
            pltpu.VMEM((total, LANES), f32),
        ],
        us=0.5,
    )(*args)


def branch_operand(refs):
    rows = refs.shape[2]
    low = lane_of((rows, LANES)) < HEAD_DIM
    pairs, thirds = [], []
    for member in range(refs.shape[1]):
        one = refs[0, member, :, 0:LANES]
        mid = refs[0, member, :, LANES : 2 * LANES].astype(f32)
        end = refs[0, member, :, 2 * LANES : 3 * LANES].astype(f32)
        mid_turned = pltpu.roll(mid, HEAD_DIM, 1)
        end_turned = pltpu.roll(end, HEAD_DIM, 1)
        late = jnp.where(low, mid_turned, end_turned).astype(bf16)
        pairs.append(jnp.concatenate([one, late], axis=0))
        thirds.append((mid, end_turned))
    for member in range(0, refs.shape[1], 2):
        tops = []
        for which in range(2):
            left, right = thirds[member][which], thirds[member + 1][which]
            tops.append(jnp.where(low, left, pltpu.roll(right, HEAD_DIM, 1)).astype(bf16))
        pairs.append(jnp.concatenate(tops, axis=0))
    return jnp.concatenate(pairs, axis=1)


def branch_weights(ref):
    right = [ref[source, 0:LANES] for source in range(ref.shape[0])]
    return jnp.concatenate(right + [ref[source, LANES:] for source in range(ref.shape[0])], axis=0)


def hits_of(rank, local_experts):
    place = lax.broadcasted_iota(jnp.int32, (CAPACITY, rank.shape[1]), 0).astype(f32)
    return [place == rank[j : j + 1, :] for j in range(local_experts)]


def chosen_of(hits):
    return jnp.concatenate([jnp.where(hit, 1.0, 0.0).astype(bf16) for hit in hits], axis=0)


def middle_kernel(
    place_ref, att_mine_ref, att_other_ref, w_mine_ref, w_other_ref, tok_a_ref, tok_b_ref, routes_a_ref, routes_b_ref,
    gain_ref, w_router_ref, after_ref,
    x_ref, slot_gate_ref, rank_ref, gate_ref, normed_ref, middle_ref, gates_own_ref, gates_ref, ranks_ref
):
    step = pl.program_id(0)
    member = place_ref[2]
    cols = pl.num_programs(0)
    rows = tok_a_ref.shape[0]
    local_experts = x_ref.shape[0]
    branch = dot(branch_operand(att_mine_ref), branch_weights(w_mine_ref))
    branch = branch + dot(branch_operand(att_other_ref), branch_weights(w_other_ref))
    for half in range(2):
        tok_ref, routes_ref = ((tok_a_ref, routes_a_ref), (tok_b_ref, routes_b_ref))[half]
        middle = tok_ref[...].astype(f32) + branch[half * rows : (half + 1) * rows]
        inverse = lax.rsqrt(jnp.mean(middle * middle, axis=1, keepdims=True) + epsilon)
        normed = (middle * inverse * gain_ref[...]).astype(bf16)
        normed_ref[half, 0] = normed
        logits = dot_nt(w_router_ref[...], normed)
        padded = logits.shape[0]
        slot = lax.broadcasted_iota(jnp.int32, (padded, rows), 0)
        expert = (slot // 8) * local_experts + slot % 8
        expert = jnp.where(slot % 8 < local_experts, expert, -1).astype(f32)
        routes = routes_ref[0].astype(f32)
        named = expert == routes[0:1, 0:rows]
        for k in range(1, TOP):
            named = named | (expert == routes[k : k + 1, 0:rows])
        peak = jnp.max(jnp.where(named, logits, masked_score), axis=0, keepdims=True)
        weights = jnp.where(named, jnp.exp(logits - peak), 0.0)
        gates = weights / jnp.sum(weights, axis=0, keepdims=True)
        gates_ref[...] = gates
        ranks_ref[...] = jnp.where(named, dot(named.astype(f32).astype(bf16), after_ref[...]), -1.0)
        here = pl.ds(pl.multiple_of(member * 8, 8), 8)
        gate, rank = gates_ref[here, :], ranks_ref[here, :]
        rank_ref[half, 0] = rank
        gate_ref[half, 0] = gate
        hits = hits_of(rank, local_experts)
        slot_gate = jnp.concatenate(
            [jnp.sum(jnp.where(hit, gate[j : j + 1, :], 0.0), axis=1, keepdims=True) for j, hit in enumerate(hits)],
            axis=0,
        )
        chosen = chosen_of(hits)
        picked = dot(chosen, normed).astype(bf16)
        spread = jnp.broadcast_to(slot_gate, (slot_gate.shape[0], LANES))
        for j in range(local_experts):
            part = slice(j * CAPACITY, (j + 1) * CAPACITY)
            x_ref[j, half, 0] = picked[part]
            slot_gate_ref[j, half, 0] = spread[part]

        @pl.when(member == half * cols + step)
        def _(middle=middle, gates=gates):
            middle_ref[...] = middle
            gates_own_ref[...] = gates


def middle_and_dispatch(place, att, w_mine, w_other, tokens, routes, gain, w_router, local_experts):
    width = tokens.shape[1]
    half = COLS
    rows = tokens.shape[0] // (2 * half)
    padded = w_router.shape[0]
    after = (jnp.arange(rows)[:, None] < jnp.arange(rows)[None, :]).astype(bf16)
    slot_shape = (local_experts, 2, half, CAPACITY)
    early = pl.BlockSpec((rows, width), lambda i, p: (i, 0))
    late = pl.BlockSpec((rows, width), lambda i, p: (i + half, 0))
    routes_shape = (1,) + routes.shape[1:]
    return call(
        middle_kernel,
        (half,),
        1,
        [
            pl.BlockSpec((1, half, rows, 3 * LANES), lambda i, p: (p[0], 0, i, 0)),
            pl.BlockSpec((1, half, rows, 3 * LANES), lambda i, p: (1 - p[0], 0, i, 0)),
            whole(w_mine.shape),
            whole(w_other.shape),
            early,
            late,
            pl.BlockSpec(routes_shape, lambda i, p: (i, 0, 0)),
            pl.BlockSpec(routes_shape, lambda i, p: (i + half, 0, 0)),
            whole((1, width)),
            whole(w_router.shape),
            whole((rows, rows)),
        ],
        [
            pl.BlockSpec((local_experts, 2, 1, CAPACITY, width), lambda i, p: (0, 0, i, 0, 0)),
            pl.BlockSpec((local_experts, 2, 1, CAPACITY, LANES), lambda i, p: (0, 0, i, 0, 0)),
            pl.BlockSpec((2, 1, 8, rows), lambda i, p: (0, i, 0, 0)),
            pl.BlockSpec((2, 1, 8, rows), lambda i, p: (0, i, 0, 0)),
            pl.BlockSpec((2, 1, rows, width), lambda i, p: (0, i, 0, 0)),
            whole((rows, width)),
            whole((padded, rows)),
        ],
        [
            struct(slot_shape + (width,), bf16),
            struct(slot_shape + (LANES,), f32),
            struct((2, half, 8, rows), f32),
            struct((2, half, 8, rows), f32),
            struct((2, half, rows, width), bf16),
            struct((rows, width), f32),
            struct((padded, rows), f32),
        ],
        scratch=[pltpu.VMEM((padded, rows), f32), pltpu.VMEM((padded, rows), f32)],
        us=0.5,
    )(place, att, att, w_mine, w_other, tokens, tokens, routes, routes, gain, w_router, after)


def grad_dispatch_kernel(rank_ref, gate_ref, cot_ref, g_ref):
    local_experts = g_ref.shape[0]
    rows = cot_ref.shape[0] // 2
    for half in range(2):
        hits = hits_of(rank_ref[half], local_experts)
        gate = gate_ref[half]
        slot_gate = jnp.concatenate(
            [jnp.sum(jnp.where(hit, gate[j : j + 1, :], 0.0), axis=1, keepdims=True) for j, hit in enumerate(hits)],
            axis=0,
        )
        grads = (dot(chosen_of(hits), cot_ref[half * rows : (half + 1) * rows, :]) * slot_gate).astype(bf16)
        for j in range(local_experts):
            g_ref[j, half] = grads[j * CAPACITY : (j + 1) * CAPACITY]


def grad_dispatch(rank, gate, cotangents, local_experts):
    members, _, rows = rank.shape
    width = cotangents.shape[1]
    small = pl.BlockSpec((2, 8, rows), lambda j: (j, 0, 0))
    return call(
        grad_dispatch_kernel,
        (members // 2,),
        0,
        [small, small, pl.BlockSpec((2 * rows, width), lambda j: (j, 0))],
        pl.BlockSpec((local_experts, 2, CAPACITY, width), lambda j: (0, j, 0, 0)),
        struct((local_experts, members, CAPACITY, width), bf16),
        us=0.5,
    )(rank, gate, cotangents)


def expert_kernel(
    x_ref, gate_ref, w_gate_ref, w_up_ref, w_down_ref, forth_ref, active_ref, factor_ref, silu_ref
):
    gate_pre = dot(x_ref[0], w_gate_ref[0])
    up_pre = dot(x_ref[0], w_up_ref[0])
    sig = 1.0 / (1.0 + jnp.exp(-gate_pre))
    silu = gate_pre * sig
    silu_ref[0] = silu
    factor_ref[0] = up_pre * sig * (1.0 + gate_pre * (1.0 - sig))
    active_ref[0] = (silu * up_pre).astype(bf16)
    produced = dot_nt(active_ref[0], w_down_ref[0]).astype(bf16).astype(f32)
    forth_ref[0] = (produced * gate_ref[0, :, 0:1]).astype(bf16)


def run_experts(x, slot_gate, w_gate, w_up, w_down):
    count, slots, width = x.shape
    hidden = w_gate.shape[2]

    def per_expert(*shape):
        return pl.BlockSpec((1,) + shape, lambda e: (e, 0, 0))

    return call(
        expert_kernel,
        (count,),
        0,
        [per_expert(slots, width), per_expert(slots, LANES)] + [per_expert(width, hidden)] * 3,
        [per_expert(slots, width)] + [per_expert(slots, hidden)] * 3,
        [
            struct((count, slots, width), bf16),
            struct((count, slots, hidden), bf16),
            struct((count, slots, hidden), f32),
            struct((count, slots, hidden), f32),
        ],
        us=0.5,
    )(x, slot_gate, w_gate, w_up, w_down)


def expert_back_kernel(place_ref, *refs, fast):
    x_ref, g_ref, active_ref, factor_ref, silu_ref = refs[:5]
    w_gate_ref, w_up_ref, w_down_ref, back_ref, dots_ref = refs[5:10]
    grads, (gate_low_ref, up_low_ref) = refs[10:-2], refs[-2:]
    slots, width = g_ref.shape[1], g_ref.shape[2]
    chunk = 256
    active_grad = dot(g_ref[0], w_down_ref[0])
    gate_low_ref[...] = (active_grad * factor_ref[0]).astype(bf16)
    up_low_ref[...] = (active_grad * silu_ref[0]).astype(bf16)
    dots = jnp.sum(active_ref[0].astype(f32) * active_grad, axis=1, keepdims=True)
    dots_ref[0] = jnp.broadcast_to(dots, (slots, LANES))
    back_ref[0] = (dot_nt(gate_low_ref[...], w_gate_ref[0]) + dot_nt(up_low_ref[...], w_up_ref[0])).astype(bf16)

    def products(cols):
        x = x_ref[0, :, cols]
        yield 0, dot_tn(x, gate_low_ref[...]).astype(bf16)
        yield 1, dot_tn(x, up_low_ref[...]).astype(bf16)
        yield 2, dot_tn(g_ref[0, :, cols], active_ref[0]).astype(bf16)

    if fast:
        write_shards(place_ref, grads, products, width)
    else:

        def whole_columns(index, carry):
            cols = pl.ds(pl.multiple_of(index * chunk, chunk), chunk)
            for which, product in products(cols):
                grads[which][0, cols, :] = product
            return carry

        lax.fori_loop(0, width // chunk, whole_columns, 0)


def write_shards(place_ref, outs, products, width):
    send_a, keep_a, send_b, keep_b = outs
    x_bit, y_bit = place_ref[3], place_ref[4]
    shard = width // 4
    for dy in range(2):
        for dx in range(2):
            x, y = x_bit ^ dx, y_bit ^ dy
            cols = pl.ds(pl.multiple_of((y * 2 + x) * shard, shard), shard)
            for which, product in products(cols):
                side = product.shape[1] // 2
                (send_a if dx else keep_a)[0, which, y] = product[:, :side]
                (send_b if dy else keep_b)[0, which, x] = product[:, side:]


def run_experts_back(place, x, g, active, factor, silu, w_gate, w_up, w_down, first, count, fast):
    slots, width = g.shape[1], g.shape[2]
    hidden = w_gate.shape[2]

    def taken(*shape):
        return pl.BlockSpec((1,) + shape, lambda e, p: (e + first, 0, 0))

    def given(*shape):
        zeros = (0,) * len(shape)
        return pl.BlockSpec((1,) + shape, lambda e, p: (e,) + zeros)

    if fast:
        grad_shapes = [(3, 2, width // 4, hidden // 2)] * 4
    else:
        grad_shapes = [(width, hidden)] * 3
    return call(
        lambda *refs: expert_back_kernel(*refs, fast=fast),
        (count,),
        1,
        [taken(slots, width)] * 2 + [taken(slots, hidden)] * 3 + [taken(width, hidden)] * 3,
        [given(slots, width), given(slots, LANES)] + [given(*shape) for shape in grad_shapes],
        [struct((count, slots, width), bf16), struct((count, slots, LANES), f32)]
        + [struct((count,) + shape, bf16) for shape in grad_shapes],
        scratch=[pltpu.VMEM((slots, hidden), bf16)] * 2,
        us=0.5,
    )(place, x, g, active, factor, silu, w_gate, w_up, w_down)


DOT_LANES = 2 * LANES


def combine_kernel(place_ref, rank_ref, *refs, pieces, with_dots, mine):
    parts, rest = refs[:pieces], refs[pieces:]
    rows = rank_ref.shape[2]
    local_experts = sum(part.shape[0] for part in parts)
    hits = hits_of(rank_ref[0], local_experts)
    gathered = jnp.concatenate([part[j, 0] for part in parts for j in range(part.shape[0])], axis=0)
    summed = dot_tn(chosen_of(hits), gathered)
    out_ref = rest[-1]
    if mine:
        arrived_ref = rest[-2]
        summed = summed + arrived_ref[0, 0:rows, :].astype(f32)
    out_ref[0, 0:rows, :] = summed.astype(bf16)
    if with_dots:
        column = [part[j, 0][:, 0:1] for part in rest[:pieces] for j in range(part.shape[0])]
        scattered = [
            jnp.sum(jnp.where(hit, value, 0.0), axis=0, keepdims=True) for hit, value in zip(hits, column)
        ]
        scattered.append(jnp.zeros((DOT_ROWS - local_experts, rows), f32))
        scattered = jnp.concatenate(scattered, axis=0)
        upper = scattered.astype(bf16)
        out_ref[0, rows:, :] = jnp.zeros((DOT_ROWS, out_ref.shape[2]), bf16)
        out_ref[0, rows:, 0:rows] = upper
        out_ref[0, rows:, DOT_LANES : DOT_LANES + rows] = (scattered - upper.astype(f32)).astype(bf16)
        if mine:
            out_ref[0, rows:, 2 * DOT_LANES : 4 * DOT_LANES] = arrived_ref[0, rows:, 0 : 2 * DOT_LANES]


def combine(place, rank, parts, dots=None, arrived=None):
    mine = arrived is not None
    rows, width = rank.shape[2], parts[0].shape[-1]
    out_rows = rows + (DOT_ROWS if dots else 0)

    def member(step, p):
        return (p[0] if mine else 1 - p[0]) * COLS + step

    def slots_of(array):
        return pl.BlockSpec((array.shape[0], 1) + array.shape[2:], lambda j, p: (0, member(j, p), 0, 0))

    inputs = [
        part.reshape(part.shape[0], 2 * COLS, CAPACITY, part.shape[-1]) for part in list(parts) + list(dots or [])
    ]
    in_specs = [pl.BlockSpec((1, 8, rows), lambda j, p: (member(j, p), 0, 0))] + [slots_of(item) for item in inputs]
    by_chip = pl.BlockSpec((1, out_rows, width), lambda j, p: (j, 0, 0))
    if mine:
        inputs.append(arrived)
        in_specs.append(by_chip)
    return call(
        lambda *refs: combine_kernel(*refs, pieces=len(parts), with_dots=bool(dots), mine=mine),
        (COLS,),
        1,
        in_specs,
        by_chip,
        struct((COLS, out_rows, width), bf16),
        us=0.5,
    )(place, rank, *inputs)


def split_dot(dimension_numbers, values, exact):
    upper = values.astype(bf16)
    lower = (values - upper.astype(f32)).astype(bf16)
    return lax.dot_general(
        upper, exact, dimension_numbers, preferred_element_type=f32
    ) + lax.dot_general(lower, exact, dimension_numbers, preferred_element_type=f32)


EXTRA_SLOTS = 6


def middle_back_kernel(
    place_ref, sums_ref, gates_ref, middle_ref, cot_ref, gain_ref, w_router_ref, w_mine_ref, w_other_ref,
    grad_ref, branch_ref, attended_ref, extra_ref
):
    rows = middle_ref.shape[0]
    tail = sums_ref[:, rows : rows + 8, 0 : 4 * DOT_LANES].astype(f32)
    mine = tail[:, :, 0:rows] + tail[:, :, DOT_LANES : DOT_LANES + rows]
    other = tail[:, :, 2 * DOT_LANES : 2 * DOT_LANES + rows] + tail[:, :, 3 * DOT_LANES : 3 * DOT_LANES + rows]
    first_row = place_ref[0] == 0
    dots = jnp.concatenate([jnp.where(first_row, mine, other), jnp.where(first_row, other, mine)], axis=0)
    dots = dots.reshape(dots.shape[0] * 8, rows)
    gates = gates_ref[...]
    logit_grad = dots - gates * jnp.sum(dots, axis=0, keepdims=True)
    middle = middle_ref[...]
    inverse = lax.rsqrt(jnp.mean(middle * middle, axis=1, keepdims=True) + epsilon)
    unit = middle * inverse
    gain = gain_ref[...]
    grad = sums_ref[0, 0:rows].astype(f32)
    for index in range(1, sums_ref.shape[0]):
        grad = grad + sums_ref[index, 0:rows].astype(f32)
    grad = grad + split_dot(TN, logit_grad, w_router_ref[...])
    gain_grad = jnp.sum(grad * unit, axis=0, keepdims=True)
    scaled = grad * gain
    middle_grad = cot_ref[...].astype(f32) + inverse * (
        scaled - unit * jnp.mean(scaled * unit, axis=1, keepdims=True)
    )
    grad_ref[...] = middle_grad
    branch_grad = middle_grad.astype(bf16)
    branch_ref[0:rows, :] = branch_grad
    extra_ref[...] = jnp.zeros_like(extra_ref)
    for index in range(logit_grad.shape[0] // 8):
        first, lane = index // EXTRA_SLOTS * 8, index % EXTRA_SLOTS * DOT_LANES
        extra_ref[first : first + 8, lane : lane + rows] = logit_grad[index * 8 : index * 8 + 8]
    upper = gain_grad.astype(bf16).astype(f32)
    extra_ref[13:14, :] = upper
    extra_ref[14:15, :] = gain_grad - upper
    branch_ref[rows:, :] = extra_ref[...].astype(bf16)
    for which, ref in enumerate((w_mine_ref, w_other_ref)):
        line = place_ref[0] if which == 0 else 1 - place_ref[0]
        for col in range(ref.shape[0]):
            product = dot_nt(branch_grad, ref[col])
            member = line * COLS + col
            attended_ref[member, :, 0:LANES] = product[:, 0:LANES].astype(bf16)
            attended_ref[member, :, LANES : LANES + HEAD_DIM] = product[:, LANES:].astype(bf16)
            attended_ref[member, :, LANES + HEAD_DIM :] = jnp.zeros((product.shape[0], HEAD_DIM), bf16)


def middle_back(place, sums, gates, middle, cotangent, gain, w_router, w_mine, w_other):
    rows, width = middle.shape
    members = 2 * COLS
    args = (sums, gates, middle, cotangent, gain, w_router, w_mine, w_other)
    return call(
        middle_back_kernel,
        (1,),
        1,
        [whole(item.shape) for item in args],
        [whole((rows, width)), whole((rows + DOT_ROWS, width)), whole((members, rows, 2 * LANES))],
        [
            struct((rows, width), f32),
            struct((rows + DOT_ROWS, width), bf16),
            struct((members, rows, 2 * LANES), bf16),
        ],
        scratch=[pltpu.VMEM((DOT_ROWS, width), f32)],
        us=0.5,
    )(place, *args)


def input_grad_kernel(
    place_ref, grads_ref, w_mine_ref, w_other_ref, tok_ref, middle_grad_ref, gain_ref, out_ref, sum_ref
):
    step = pl.program_id(0)

    @pl.when(step == 0)
    def _():
        sum_ref[...] = jnp.zeros_like(sum_ref)

    def add(ref):
        sum_ref[...] += dot(grads_ref[0], jnp.concatenate([ref[0], ref[0, 4 * HEAD_DIM :]], axis=0))

    @pl.when(step < COLS)
    def _():
        add(w_mine_ref)

    @pl.when(step >= COLS)
    def _():
        add(w_other_ref)

    @pl.when(step == pl.num_programs(0) - 1)
    def _():
        resid = tok_ref[...].astype(f32)
        inverse = lax.rsqrt(jnp.mean(resid * resid, axis=1, keepdims=True) + epsilon)
        unit = resid * inverse
        scaled = sum_ref[...] * gain_ref[...]
        out_ref[...] = middle_grad_ref[...] + inverse * (
            scaled - unit * jnp.mean(scaled * unit, axis=1, keepdims=True)
        )


def input_grad(place, grads, w_mine, w_other, tokens, middle_grad, gain):
    rows, width = tokens.shape
    members, lanes = grads.shape[0], grads.shape[2]
    w_shape = (1,) + w_mine.shape[1:]

    def member(step, p):
        line = jnp.where(step < COLS, p[0], 1 - p[0])
        return line * COLS + lax.rem(step, COLS)

    return call(
        input_grad_kernel,
        (members,),
        1,
        [
            pl.BlockSpec((1, rows, lanes), lambda m, p: (member(m, p), 0, 0)),
            pl.BlockSpec(w_shape, lambda m, p: (jnp.minimum(m, COLS - 1), 0, 0)),
            pl.BlockSpec(w_shape, lambda m, p: (jnp.maximum(m - COLS, 0), 0, 0)),
            whole((rows, width)),
            whole((rows, width)),
            whole((1, width)),
        ],
        whole((rows, width)),
        struct((rows, width), f32),
        scratch=[pltpu.VMEM((rows, width), f32)],
        us=0.5,
    )(place, grads, w_mine, w_other, tokens, middle_grad, gain)


def own_weights_kernel(normed_ref, projected_ref, w_ref, gain_ref, out_ref, gain_grad_ref, sum_ref):
    step = pl.program_id(0)

    @pl.when(step == 0)
    def _():
        sum_ref[...] = jnp.zeros_like(sum_ref)

    sum_ref[...] += dot_tn(normed_ref[...], projected_ref[...])

    @pl.when(step == pl.num_programs(0) - 1)
    def _():
        total = sum_ref[...]
        out_ref[...] = total.astype(bf16)
        by_weight = jnp.sum(total * w_ref[...].astype(f32), axis=1, keepdims=True)
        gain_grad_ref[...] = jnp.broadcast_to(by_weight / gain_ref[...], gain_grad_ref.shape)


def own_weights(normed, projected, w_natural, gain):
    total, width = normed.shape
    lanes = projected.shape[1]
    rows = 512
    return call(
        own_weights_kernel,
        (total // rows,),
        0,
        [
            pl.BlockSpec((rows, width), lambda j: (j, 0)),
            pl.BlockSpec((rows, lanes), lambda j: (j, 0)),
            whole((width, lanes)),
            whole((width, 1)),
        ],
        [whole((width, lanes)), whole((width, 8))],
        [struct((width, lanes), bf16), struct((width, 8), f32)],
        scratch=[pltpu.VMEM((width, lanes), f32)],
        us=0.5,
    )(normed, projected, w_natural, gain)


def out_weights_kernel(place_ref, branch_ref, att_ref, normed_ref, own_ref, *refs, fast, local_experts):
    outs, small_ref, (sum_ref, gain_sum_ref) = refs[:-3], refs[-3], refs[-2:]
    step = pl.program_id(0)
    rows = att_ref.shape[0] // 2
    block = rows + DOT_ROWS

    @pl.when(step == 0)
    def _():
        sum_ref[...] = jnp.zeros_like(sum_ref)
        small_ref[...] = jnp.zeros_like(small_ref)
        gain_sum_ref[...] = jnp.zeros_like(gain_sum_ref)

    branch = jnp.concatenate([branch_ref[0:rows, :], branch_ref[block : block + rows, :]], axis=0)
    sum_ref[...] += dot_tn(branch, att_ref[...])
    for which in range(2):
        tail = branch_ref[which * block + rows : (which + 1) * block, :].astype(f32)
        slots = []
        for index in range(small_ref.shape[0] // 8):
            first, lane = index // EXTRA_SLOTS * 8, index % EXTRA_SLOTS * DOT_LANES
            slots.append(tail[first : first + 8, lane : lane + rows])
        logit_grad = jnp.concatenate(slots, axis=0)
        real = lax.broadcasted_iota(jnp.int32, logit_grad.shape, 0) % 8 < local_experts
        logit_grad = jnp.where(real, logit_grad, 0.0).astype(bf16)
        small_ref[...] += dot(logit_grad, normed_ref[which * rows : (which + 1) * rows, :])
        gain_sum_ref[...] += tail[8:16, :]

    @pl.when(step == pl.num_programs(0) - 1)
    def _():
        small_ref[7:8, :] = gain_sum_ref[5:6, :] + gain_sum_ref[6:7, :]

        def products(cols):
            own = own_ref[cols, 0 : 2 * LANES]
            out_one = sum_ref[cols, 0:LANES].astype(bf16)
            out_two = sum_ref[cols, LANES:]
            low = lane_of(out_two.shape) < HEAD_DIM
            tail = jnp.where(low, out_two, own_ref[cols, 2 * LANES :].astype(f32)).astype(bf16)
            yield 0, jnp.concatenate([own, out_one, tail], axis=1)

        if fast:
            write_shards(place_ref, outs, products, own_ref.shape[0])
        else:
            outs[0][...] = next(products(slice(0, own_ref.shape[0])))[1]


def out_weights(place, branch, attended, normed, own, padded, local_experts, fast):
    total, width = normed.shape
    rows = total // COLS
    blocks = branch.shape[0] // COLS
    if fast:
        shapes = [(1, 1, 2, width // 4, 2 * LANES)] * 4
    else:
        shapes = [(width, 4 * LANES)]
    return call(
        lambda *refs: out_weights_kernel(*refs, fast=fast, local_experts=local_experts),
        (COLS,),
        1,
        [
            pl.BlockSpec((blocks, width), lambda j, p: (j, 0)),
            pl.BlockSpec((rows, 2 * LANES), lambda j, p: (j, 0)),
            pl.BlockSpec((rows, width), lambda j, p: (j, 0)),
            whole(own.shape),
        ],
        [whole(shape) for shape in shapes] + [whole((padded, width))],
        [struct(shape, bf16) for shape in shapes] + [struct((padded, width), f32)],
        scratch=[pltpu.VMEM((width, 2 * LANES), f32), pltpu.VMEM((8, width), f32)],
        us=0.5,
    )(place, branch, attended, normed, own)


def first_sum_kernel(place_ref, *refs, counts):
    outs = refs[4 * len(counts) :]
    x_bit, y_bit = place_ref[3], place_ref[4]
    expert = pl.program_id(0)
    first = 0
    for index, count in enumerate(counts):
        parts = refs[4 * index : 4 * index + 4]

        @pl.when((expert >= first) & (expert < first + count))
        def _(parts=parts):
            for side, bit in enumerate((y_bit, x_bit)):
                keep, got = parts[2 * side], parts[2 * side + 1]
                send, held = outs[2 * side], outs[2 * side + 1]
                held[0, 0] = keep[0, 0, bit].astype(f32) + got[0, 0, bit].astype(f32)
                send[0, 0] = (keep[0, 0, 1 - bit].astype(f32) + got[0, 0, 1 - bit].astype(f32)).astype(bf16)

        first += count


def first_sum(place, chunks):
    counts = [chunk[0].shape[0] for chunk in chunks]
    _, kinds, _, rows, cols = chunks[0][0].shape
    specs, first = [], 0
    for count in counts:

        def taken(e, k, p, first=first, count=count):
            inside = (e >= first) & (e < first + count)
            kind = jnp.where(inside, k, jnp.where(e < first, 0, kinds - 1))
            return (jnp.clip(e - first, 0, count - 1), kind, 0, 0, 0)

        specs += [pl.BlockSpec((1, 1, 2, rows, cols), taken)] * 4
        first += count
    given = pl.BlockSpec((1, 1, rows, cols), lambda e, k, p: (e, k, 0, 0))
    shape = (first, kinds, rows, cols)
    return call(
        lambda *refs: first_sum_kernel(*refs, counts=counts),
        (first, kinds),
        1,
        specs,
        [given] * 4,
        [struct(shape, bf16), struct(shape, f32), struct(shape, bf16), struct(shape, f32)],
        us=0.5,
    )(place, *[item for chunk in chunks for item in chunk])


def last_sum_kernel(held_a_ref, got_a_ref, held_b_ref, got_b_ref, *rest):
    outs = rest[-3:]
    side = held_a_ref.shape[3]
    for which, out in enumerate(outs):
        out[0, :, :side] = held_a_ref[0, which] + got_a_ref[0, which].astype(f32)
        out[0, :, side:] = held_b_ref[0, which] + got_b_ref[0, which].astype(f32)


def last_sum(held_a, got_a, held_b, got_b, first, total, before):
    count, kinds, rows, cols = held_a.shape
    taken = pl.BlockSpec((1, kinds, rows, cols), lambda e: (e, 0, 0, 0))
    given = pl.BlockSpec((1, rows, 2 * cols), lambda e: (e + first, 0, 0))
    extra = list(before) if before else []
    return call(
        last_sum_kernel,
        (count,),
        0,
        [taken] * 4 + [pl.BlockSpec(memory_space=pl.ANY)] * len(extra),
        [given] * 3,
        [struct((total, rows, 2 * cols), f32)] * 3,
        us=0.5,
        aliases={4 + i: i for i in range(len(extra))},
    )(held_a, got_a, held_b, got_b, *extra)


SWAP = [(0, 1), (1, 0)]


def after(value, *events):
    return lax.optimization_barrier((value,) + events)[0]


def gather_group(block):
    return lax.all_gather(block, ("row", "col"), axis=0, tiled=True)


def line_pieces(value):
    parts = [value]
    for distance in range(1, COLS):
        parts.insert(0, lax.ppermute(value, "col", [(i, (i + distance) % COLS) for i in range(COLS)]))
    return parts


def in_line_order(parts):
    parts = jnp.stack(parts + parts)
    return lax.dynamic_slice_in_dim(parts, COLS - 1 - lax.axis_index("col"), COLS, axis=0)


def flip(value, axis, bit, size):
    return lax.ppermute(value, axis, [(i, i ^ (1 << bit)) for i in range(size)])


def bits_of(size):
    return size.bit_length() - 1


def own_bit(axis, bit):
    return (lax.axis_index(axis) >> bit) & 1


def joined(mine, got, own):
    return jnp.where(own == 0, jnp.concatenate([mine, got]), jnp.concatenate([got, mine]))


def cube_step(value, axis, bit, size):
    return joined(value, flip(value, axis, bit, size), own_bit(axis, bit))


def cube_gather(value, axis, size):
    value = value[None]
    for bit in range(bits_of(size)):
        value = cube_step(value, axis, bit, size)
    return value


def sum_group(value, sizes):
    for axis, bit in (("row", 0), ("col", 0), ("col", 1)):
        value = value + flip(value, axis, bit, sizes[axis])
    return value


def sum_dp(value, sizes):
    for bit in range(bits_of(sizes["dp"])):
        value = value + flip(value, "dp", bit, sizes["dp"])
    return value


def reduce_over_dp(value, size):
    count = bits_of(size)
    value = value.reshape(value.shape[:1] + (2,) * count + value.shape[2:])
    current = value
    for bit in range(count - 1, -1, -1):
        own = own_bit("dp", bit)
        keep = lax.dynamic_index_in_dim(current, own, 1, keepdims=False)
        send = lax.dynamic_index_in_dim(current, 1 - own, 1, keepdims=False).astype(bf16)
        current = keep.astype(f32) + flip(send, "dp", bit, size).astype(f32)
    return current


def start_move(run, size):
    return flip(run[0], "dp", 0, size), flip(run[2], "dp", 1, size)


def first_half(place, runs, gots, size, event):
    chunks = []
    for run, got in zip(runs, gots):
        keep_a, keep_b = after((run[1], run[3]), event)
        chunks.append((keep_a, got[0], keep_b, got[1]))
    send_a, held_a, send_b, held_b = first_sum(place, chunks)
    return held_a, flip(send_a, "dp", 1, size), held_b, flip(send_b, "dp", 0, size)


def layer(sizes):
    n_dp, n_row, n_col = sizes["dp"], sizes["row"], sizes["col"]
    members = n_row * n_col
    fast = n_dp == 4
    assert n_row == 2 and n_col == COLS and n_dp & (n_dp - 1) == 0

    def local(
        tokens, cotangent, routes, lengths, gain_attn, w_query, w_key, w_value, w_out,
        gain_moe, w_router, w_gate, w_up, w_down,
    ):
        rows, width = tokens.shape
        group = rows * members
        local_experts = w_gate.shape[0]
        row, col, dp = lax.axis_index("row"), lax.axis_index("col"), lax.axis_index("dp")
        place = jnp.stack([row, col, row * n_col + col, dp & 1, (dp >> 1) & 1]).astype(jnp.int32)
        gain_one = gain_attn.astype(f32)[None]
        gain_two = gain_moe.astype(f32)[None]

        tok_all = gather_group(tokens)
        w_in = jnp.concatenate([w_query.T, w_key.T, w_value.T], axis=0)
        out_share, in_share = rows // n_dp, w_in.shape[0] // n_dp
        shares = jnp.concatenate(
            [
                lax.dynamic_slice(w_out.T, (dp * out_share, 0), (out_share, width)),
                lax.dynamic_slice(w_in, (dp * in_share, 0), (in_share, width)),
                jnp.pad(routes.T.astype(bf16).reshape(1, TOP * rows), ((0, 7), (0, width - TOP * rows))),
            ],
            axis=0,
        )
        shares = line_pieces(after(shares, tok_all))
        def finish(value, event):
            value = after(value, event)
            for bit in range(1, bits_of(n_dp)):
                value = cube_step(value, "dp", bit, n_dp)
            value = jnp.transpose(value, (1, 0, 2, 3)).reshape(n_col, n_dp * value.shape[2], width)
            return value

        w_stack = jnp.concatenate([w_query.T, w_key.T, w_value.T, w_value.T], axis=0)
        w_natural = jnp.concatenate([w_query, w_key, w_value, w_value], axis=1)

        ends = jnp.cumsum(lengths[0])
        starts = ends - lengths[0]
        position = jnp.arange(group, dtype=jnp.int32)
        segment = jnp.sum((position[:, None] >= ends[None, :]).astype(jnp.int32), axis=1)
        member = segment[:, None] == jnp.arange(starts.shape[0], dtype=jnp.int32)[None, :]
        start = jnp.sum(jnp.where(member, starts[None, :], 0), axis=1).astype(jnp.int32)
        frequency = rope_base ** (-2.0 * jnp.arange(HEAD_DIM // 2, dtype=f32) / HEAD_DIM)
        angle = (position - start).astype(f32)[:, None] * frequency[None, :]
        cosine = jnp.tile(jnp.cos(angle), (1, 4))
        sine = jnp.tile(jnp.sin(angle), (1, 4))

        query, key, value, normed_one = project(tok_all, gain_one, w_stack, cosine, sine)
        w_router_rows = w_router.T.reshape(members, local_experts, width)
        w_router_rows = jnp.pad(w_router_rows, ((0, 0), (0, 8 - local_experts), (0, 0)))
        w_router_rows = w_router_rows.reshape(members * 8, width)
        packed, attended, totals = attend(query, key, value, start[:, None])
        att_flat = gather_group(packed)
        att_all = att_flat.reshape((n_row, n_col) + packed.shape)
        shares = in_line_order(after(shares, packed))
        route_rows = shares[:, out_share + in_share]
        out_half = cube_step(shares[None, :, :out_share], "dp", 0, n_dp)
        in_half = cube_step(shares[None, :, out_share : out_share + in_share], "dp", 0, n_dp)
        w_out_mine = finish(out_half, packed)
        w_out_other = lax.ppermute(w_out_mine, "row", SWAP)
        w_in_mine = finish(in_half, w_out_mine)
        route_rows = cube_gather(route_rows, "row", n_row)[:, :, : TOP * rows].reshape(members, TOP, rows)
        route_rows = jnp.pad(route_rows, ((0, 0), (0, ROUTE_ROWS - TOP), (0, 2 * LANES - rows)))
        cot_all = gather_group(after(cotangent, w_out_other))
        x, slot_gate, rank, gate, normed_two, middle, gates = middle_and_dispatch(
            place, att_all, w_out_mine, after(w_out_other, in_half), tok_all, route_rows, gain_two, w_router_rows, local_experts
        )
        slots = members * CAPACITY
        x = x.reshape(local_experts, slots, width)
        slot_gate = slot_gate.reshape(local_experts, slots, LANES)
        rank, gate = rank.reshape(members, 8, rows), gate.reshape(members, 8, rows)
        forth, active, factor, silu = run_experts(x, slot_gate, w_gate, w_up, w_down)
        forth_other = combine(place, after(rank, w_in_mine), [forth])
        w_in_other = lax.ppermute(after(w_in_mine, forth_other), "row", SWAP)
        arrived = lax.ppermute(forth_other, "row", SWAP)
        g = grad_dispatch(after(rank, forth_other), gate, cot_all, local_experts)
        g = g.reshape(local_experts, slots, width)
        cuts = [0, 1, 3, local_experts]

        def backward(which, x):
            first, last = cuts[which], cuts[which + 1]
            return run_experts_back(place, x, g, active, factor, silu, w_gate, w_up, w_down, first, last - first, fast)

        runs = [backward(0, x)]
        forth_mine = combine(place, rank, [forth], arrived=after(arrived, runs[0][1]))
        forth_sums = lax.all_to_all(forth_mine, "col", 0, 0, tiled=True)
        runs.append(backward(1, after(x, forth_mine)))
        runs.append(backward(2, after(x, runs[1][1], w_in_other)))
        moved = [start_move(run[2:], n_dp) for run in runs] if fast else []
        back_parts, dot_parts = [run[0] for run in runs], [run[1] for run in runs]
        back_other = combine(place, after(rank, *moved[0]) if fast else rank, back_parts, dot_parts)
        arrived = lax.ppermute(back_other, "row", SWAP)
        back_mine = combine(place, rank, back_parts, dot_parts, arrived)
        back_mine = after(back_mine, forth_sums)
        back_sums = lax.all_to_all(back_mine, "col", 0, 0, tiled=True)

        middle_grad, branch_grad, attended_grad = middle_back(
            place, back_sums, gates, middle, cotangent, after(gain_two, *moved[1]) if fast else gain_two,
            w_router_rows, w_out_mine, w_out_other,
        )
        started = []
        if fast:
            started.append(first_half(place, [run[2:] for run in runs[:2]], moved[:2], n_dp, branch_grad))
        attended_grad = lax.all_to_all(attended_grad, ("row", "col"), 0, 0, tiled=True)
        branch_all = gather_group(branch_grad)

        start_row = jnp.broadcast_to(start[None, :], (8, group))
        attended_grad = attended_grad.reshape(group, 2 * LANES)
        if fast:
            attended_grad = after(attended_grad, started[0][0])
        projected_grad = attend_back(query, key, value, attended_grad, totals, start_row, cosine, sine)
        projected_all = lax.all_to_all(
            projected_grad.reshape(members, rows, 3 * LANES), ("row", "col"), 0, 0, tiled=True
        )
        own_grads, gain_part = own_weights(
            after(normed_one, *moved[2]) if fast else normed_one,
            projected_grad, w_natural, gain_attn.astype(f32)[:, None],
        )
        if fast:
            started.append(first_half(place, [runs[2][2:]], moved[2:], n_dp, own_grads))
        *w_parts, small = out_weights(
            place, branch_all, attended, normed_two.reshape(group, width), own_grads, members * 8, local_experts, fast
        )
        gain_attn_grad = sum_group(gain_part[:, 0].reshape(8, width // 8), sizes)
        if fast:
            w_started = first_half(place, [w_parts], [start_move(w_parts, n_dp)], n_dp, w_parts[1])
        else:
            cut = w_parts[0].reshape(1, n_dp, width // n_dp, w_parts[0].shape[1])
            w_sum = reduce_over_dp(cut, n_dp)[0]

        mixed = (middle + jnp.sum(after(forth_sums, projected_grad).astype(f32), axis=0)).astype(bf16)

        used = small.reshape(members, 8, width)[:, :local_experts].reshape(members * local_experts, width)
        both = jnp.concatenate([used, small[7:8], gain_attn_grad.reshape(1, width)], axis=0)
        both = sum_dp(both, sizes)
        w_router_grad = both[: members * local_experts].T
        gain_moe_grad, gain_attn_grad = both[members * local_experts], both[members * local_experts + 1]

        tokens_grad = input_grad(
            place, projected_all, w_in_mine, w_in_other, tokens, middle_grad, after(gain_one, w_parts[0])
        )

        if fast:
            expert_grads = None
            for item, first, event in zip(started, (0, cuts[2]), (own_grads, w_parts[0])):
                held_a, got_a, held_b, got_b = item
                held_a, held_b = after((held_a, held_b), event)
                expert_grads = last_sum(held_a, got_a, held_b, got_b, first, local_experts, expert_grads)
            held_a, got_a, held_b, got_b = [item[0, 0] for item in w_started]
            left = held_a + got_a.astype(f32)
            right = held_b + got_b.astype(f32)
            w_sum = jnp.concatenate([left, right], axis=1)
        else:
            expert_grads = []
            for which in range(3):
                parts = [run[2 + which] for run in runs]
                parts = [part.reshape(part.shape[0], n_dp, width // n_dp, part.shape[2]) for part in parts]
                expert_grads.append(jnp.concatenate([reduce_over_dp(part, n_dp) for part in parts], axis=0))
        w_gate_grad, w_up_grad, w_down_grad = expert_grads
        local_q, local_k = w_query.shape[1], w_key.shape[1]
        cut = local_q + local_k
        return (
            mixed, tokens_grad, gain_attn_grad, w_sum[:, :local_q], w_sum[:, local_q:cut],
            w_sum[:, cut + local_q :], w_sum[:, cut : cut + local_q],
            gain_moe_grad, w_router_grad, w_gate_grad, w_up_grad, w_down_grad,
        )

    return local


def solution(mesh):
    return jax.shard_map(
        layer(dict(mesh.shape)),
        mesh=mesh,
        in_specs=(
            P(("dp", "row", "col"), None),
            P(("dp", "row", "col"), None),
            P(("dp", "row", "col"), None),
            P("dp", None),
            P(),
            P(None, ("row", "col")),
            P(None, ("row", "col")),
            P(None, ("row", "col")),
            P(None, ("row", "col")),
            P(),
            P(),
            P(("row", "col"), None, None),
            P(("row", "col"), None, None),
            P(("row", "col"), None, None),
        ),
        out_specs=(
            P(("dp", "row", "col"), None),
            P(("dp", "row", "col"), None),
            P(),
            P("dp", ("row", "col")),
            P("dp", ("row", "col")),
            P("dp", ("row", "col")),
            P("dp", ("row", "col")),
            P(),
            P(),
            P(("row", "col"), "dp", None),
            P(("row", "col"), "dp", None),
            P(("row", "col"), "dp", None),
        ),
        check_vma=False,
    )
```

```python
import math

import jax
import jax.numpy as jnp
from jax import lax
from jax.experimental import pallas as pl
from jax.experimental.pallas import tpu as pltpu
from jax.sharding import PartitionSpec as P

HEAD_DIM = 64
EXPERTS = 40
TOP = 8
CAPACITY = 64
COLS = 4
LANES = 128
QUERY_BLOCK = 256
ROUTE_ROWS = 16
DOT_ROWS = 16

epsilon = 1e-06
rope_base = 10000.0
masked_score = -1e30
f32 = jnp.float32
bf16 = jnp.bfloat16
VMEM_LIMIT = 56 * 1024 * 1024

NT = (((1,), (1,)), ((), ()))
TN = (((0,), (0,)), ((), ()))


def dot(a, b):
    return jnp.dot(a, b, preferred_element_type=f32)


def dot_nt(a, b):
    return lax.dot_general(a, b, NT, preferred_element_type=f32)


def dot_tn(a, b):
    return lax.dot_general(a, b, TN, preferred_element_type=f32)


def lane_of(shape):
    return lax.broadcasted_iota(jnp.int32, shape, len(shape) - 1)


def call(
    kernel, grid, prefetch, in_specs, out_specs, out_shape, scratch=(), us=1.0, aliases=None
):
    return pl.pallas_call(
        kernel,
        grid_spec=pltpu.PrefetchScalarGridSpec(
            num_scalar_prefetch=prefetch,
            grid=grid,
            in_specs=in_specs,
            out_specs=out_specs,
            scratch_shapes=list(scratch),
        ),
        out_shape=out_shape,
        input_output_aliases=aliases or {},
        compiler_params=pltpu.CompilerParams(
            vmem_limit_bytes=VMEM_LIMIT, dimension_semantics=("arbitrary",) * len(grid)
        ),
        cost_estimate=pl.CostEstimate(
            flops=int(us * 1.1e9), bytes_accessed=int(us * 3.6e6), transcendentals=0
        ),
    )


def whole(shape):
    zeros = (0,) * len(shape)
    return pl.BlockSpec(shape, lambda *_: zeros)


def struct(shape, dtype):
    return jax.ShapeDtypeStruct(shape, dtype)


def turn_within_heads(values, sign):
    lane = lane_of(values.shape) % HEAD_DIM
    ahead = pltpu.roll(values, LANES - HEAD_DIM // 2, 1)
    behind = pltpu.roll(values, HEAD_DIM // 2, 1)
    return jnp.where(lane < HEAD_DIM // 2, -sign * ahead, sign * behind)


def project_kernel(
    tok_ref, gain_ref, w_ref, cos_ref, sin_ref, query_ref, key_ref, value_ref, normed_ref
):
    resid = tok_ref[...].astype(f32)
    inverse = lax.rsqrt(jnp.mean(resid * resid, axis=1, keepdims=True) + epsilon)
    normed = (resid * inverse * gain_ref[...]).astype(bf16)
    normed_ref[...] = normed
    raw = dot_nt(normed, w_ref[...])
    cosine, sine = cos_ref[...], sin_ref[...]

    def rot(values):
        return (values * cosine + turn_within_heads(values, 1.0) * sine).astype(bf16).astype(f32)

    first = rot(raw[:, :LANES])
    second = rot(raw[:, LANES : 2 * LANES])
    low = lane_of(first.shape) < HEAD_DIM
    scale = 1.0 / math.sqrt(HEAD_DIM)
    query_ref[0] = jnp.where(low, first * scale, 0.0).astype(bf16)
    query_ref[1] = jnp.where(low, 0.0, first * scale).astype(bf16)
    query_ref[2] = jnp.where(low, second * scale, 0.0).astype(bf16)
    key_ref[...] = jnp.where(low, pltpu.roll(second, HEAD_DIM, 1), second).astype(bf16)
    value_ref[...] = raw[:, 2 * LANES :].astype(bf16)


def project(tokens, gain, w_stack, cosine, sine):
    total, width = tokens.shape
    rows = 512
    lanes = pl.BlockSpec((rows, LANES), lambda j: (j, 0))
    wide = pl.BlockSpec((rows, width), lambda j: (j, 0))
    return call(
        project_kernel,
        (total // rows,),
        0,
        [wide, whole((1, width)), whole(w_stack.shape), lanes, lanes],
        [pl.BlockSpec((3, rows, LANES), lambda j: (0, j, 0)), lanes, lanes, wide],
        [
            struct((3, total, LANES), bf16),
            struct((total, LANES), bf16),
            struct((total, LANES), bf16),
            struct((total, width), bf16),
        ],
        us=0.5,
    )(tokens, gain, w_stack, cosine, sine)


def attend_kernel(query_ref, key_ref, value_ref, start_ref, packed_ref, plain_ref, total_ref, out_ref):
    blocks = query_ref.shape[1] // QUERY_BLOCK
    block = pl.program_id(0)
    for index in range(blocks):

        @pl.when(block == index)
        def _(index=index):
            rows = pl.ds(index * QUERY_BLOCK, QUERY_BLOCK)
            span = (index + 1) * QUERY_BLOCK
            row = index * QUERY_BLOCK + lax.broadcasted_iota(jnp.int32, (QUERY_BLOCK, span), 0)
            column = lane_of((QUERY_BLOCK, span))
            allowed = (column <= row) & (column >= start_ref[rows, :])

            def head(number, carry):
                scores = dot_nt(query_ref[number, rows, :], key_ref[0:span, :])
                scores = jnp.where(allowed, scores, masked_score)
                peak = jnp.max(scores, axis=1, keepdims=True)
                weights = jnp.exp(scores - peak)
                summed = jnp.sum(weights, axis=1, keepdims=True)
                probs = (weights * (1.0 / summed)).astype(bf16)
                out_ref[number] = dot(probs, value_ref[0:span, :])
                total = jnp.broadcast_to(peak + jnp.log(summed), (QUERY_BLOCK, LANES))
                total_ref[number, :, rows] = jnp.transpose(total)[0:8, :]
                return carry

            lax.fori_loop(0, 3, head, 0)
            low = lane_of((QUERY_BLOCK, LANES)) < HEAD_DIM
            one, two, three = out_ref[0], out_ref[1], out_ref[2]
            pair = jnp.where(low, one, two).astype(bf16)
            plain_ref[rows, 0:LANES] = pair
            plain_ref[rows, LANES : 2 * LANES] = jnp.where(low, three, 0.0).astype(bf16)
            if index < blocks // 2:
                packed_ref[rows, 0:LANES] = pair
                packed_ref[rows, LANES : 2 * LANES] = three.astype(bf16)
            else:
                back = pl.ds((index - blocks // 2) * QUERY_BLOCK, QUERY_BLOCK)
                before = packed_ref[back, LANES : 2 * LANES].astype(f32)
                packed_ref[back, LANES : 2 * LANES] = jnp.where(low, before, one).astype(bf16)
                packed_ref[back, 2 * LANES : 3 * LANES] = jnp.where(low, two, three).astype(bf16)


def attend(query, key, value, start):
    total = key.shape[0]
    return call(
        attend_kernel,
        (total // QUERY_BLOCK,),
        0,
        [whole(query.shape), whole(key.shape), whole(value.shape), whole(start.shape)],
        [whole((total // 2, 3 * LANES)), whole((total, 2 * LANES)), whole((3, 8, total))],
        [
            struct((total // 2, 3 * LANES), bf16),
            struct((total, 2 * LANES), bf16),
            struct((3, 8, total), f32),
        ],
        scratch=[pltpu.VMEM((3, QUERY_BLOCK, LANES), f32)],
        us=0.5,
    )(query, key, value, start)


def attend_back_kernel(
    query_ref, key_ref, value_ref, grad_ref, total_ref, start_ref, cos_ref, sin_ref,
    out_ref, query_grad_ref, key_grad_ref, value_grad_ref
):
    blocks = query_ref.shape[1] // QUERY_BLOCK
    block = pl.program_id(0)
    scale = 1.0 / math.sqrt(HEAD_DIM)

    @pl.when(block == 0)
    def _():
        key_grad_ref[...] = jnp.zeros_like(key_grad_ref)
        value_grad_ref[...] = jnp.zeros_like(value_grad_ref)

    def back(values, cosine, sine):
        return values * cosine + turn_within_heads(values * sine, -1.0)

    for index in range(blocks):

        @pl.when(block == index)
        def _(index=index):
            rows = pl.ds(index * QUERY_BLOCK, QUERY_BLOCK)
            span = (index + 1) * QUERY_BLOCK
            row = index * QUERY_BLOCK + lane_of((span, QUERY_BLOCK))
            column = lax.broadcasted_iota(jnp.int32, (span, QUERY_BLOCK), 0)
            allowed = (column <= row) & (column >= start_ref[0:1, rows])
            low = lane_of((QUERY_BLOCK, LANES)) < HEAD_DIM

            def head(number, carry):
                query = query_ref[number, rows, :]
                tile = pl.multiple_of((number // 2) * LANES, LANES)
                upstream = grad_ref[rows, pl.ds(tile, LANES)].astype(f32)
                keep = low == (number != 1)
                upstream = jnp.where(keep, upstream, 0.0).astype(bf16)
                scores = dot_nt(key_ref[0:span, :], query)
                probs = jnp.exp(scores - total_ref[number, 0:1, rows])
                probs = jnp.where(allowed, probs, 0.0)
                prob_grad = dot_nt(value_ref[0:span, :], upstream)
                row_dot = jnp.sum(probs * prob_grad, axis=0, keepdims=True)
                score_grad = (probs * (prob_grad - row_dot)).astype(bf16)
                key_grad_ref[0:span, :] += dot(score_grad, query)
                value_grad_ref[0:span, :] += dot(probs.astype(bf16), upstream)
                query_grad_ref[number] = dot_tn(score_grad, key_ref[0:span, :]) * scale
                return carry

            lax.fori_loop(0, 3, head, 0)
            cosine, sine = cos_ref[rows, :], sin_ref[rows, :]
            pair = jnp.where(low, query_grad_ref[0], query_grad_ref[1])
            out_ref[rows, 0:LANES] = back(pair, cosine, sine).astype(bf16)
            out_ref[rows, LANES : 2 * LANES] = back(query_grad_ref[2], cosine, sine).astype(bf16)

    @pl.when(block == blocks - 1)
    def _():
        low = lane_of(key_grad_ref.shape) < HEAD_DIM
        key_grad = key_grad_ref[...]
        key_grad = key_grad + pltpu.roll(key_grad, HEAD_DIM, 1)
        key_grad = back(key_grad, cos_ref[...], sin_ref[...])
        before = out_ref[:, LANES : 2 * LANES].astype(f32)
        out_ref[:, LANES : 2 * LANES] = jnp.where(low, before, key_grad).astype(bf16)
        value_grad = value_grad_ref[...]
        value_grad = value_grad + pltpu.roll(value_grad, HEAD_DIM, 1)
        out_ref[:, 2 * LANES : 3 * LANES] = jnp.where(low, 0.0, value_grad).astype(bf16)


def attend_back(query, key, value, grad, totals, start, cosine, sine):
    total = key.shape[0]
    args = (query, key, value, grad, totals, start, cosine, sine)
    return call(
        attend_back_kernel,
        (total // QUERY_BLOCK,),
        0,
        [whole(item.shape) for item in args],
        whole((total, 3 * LANES)),
        struct((total, 3 * LANES), bf16),
        scratch=[
            pltpu.VMEM((3, QUERY_BLOCK, LANES), f32),
            pltpu.VMEM((total, LANES), f32),
            pltpu.VMEM((total, LANES), f32),
        ],
        us=0.5,
    )(*args)


def branch_operand(refs):
    rows = refs.shape[2]
    low = lane_of((rows, LANES)) < HEAD_DIM
    pairs, thirds = [], []
    for member in range(refs.shape[1]):
        one = refs[0, member, :, 0:LANES]
        mid = refs[0, member, :, LANES : 2 * LANES].astype(f32)
        end = refs[0, member, :, 2 * LANES : 3 * LANES].astype(f32)
        mid_turned = pltpu.roll(mid, HEAD_DIM, 1)
        end_turned = pltpu.roll(end, HEAD_DIM, 1)
        late = jnp.where(low, mid_turned, end_turned).astype(bf16)
        pairs.append(jnp.concatenate([one, late], axis=0))
        thirds.append((mid, end_turned))
    for member in range(0, refs.shape[1], 2):
        tops = []
        for which in range(2):
            left, right = thirds[member][which], thirds[member + 1][which]
            tops.append(jnp.where(low, left, pltpu.roll(right, HEAD_DIM, 1)).astype(bf16))
        pairs.append(jnp.concatenate(tops, axis=0))
    return jnp.concatenate(pairs, axis=1)


def branch_weights(ref):
    right = [ref[source, 0:LANES] for source in range(ref.shape[0])]
    return jnp.concatenate(right + [ref[source, LANES:] for source in range(ref.shape[0])], axis=0)


def hits_of(rank, local_experts):
    place = lax.broadcasted_iota(jnp.int32, (CAPACITY, rank.shape[1]), 0).astype(f32)
    return [place == rank[j : j + 1, :] for j in range(local_experts)]


def chosen_of(hits):
    return jnp.concatenate([jnp.where(hit, 1.0, 0.0).astype(bf16) for hit in hits], axis=0)


def middle_kernel(
    place_ref, att_mine_ref, att_other_ref, w_mine_ref, w_other_ref, tok_a_ref, tok_b_ref, routes_a_ref, routes_b_ref,
    gain_ref, w_router_ref, after_ref,
    x_ref, slot_gate_ref, rank_ref, gate_ref, normed_ref, middle_ref, gates_own_ref, gates_ref, ranks_ref
):
    step = pl.program_id(0)
    member = place_ref[2]
    cols = pl.num_programs(0)
    rows = tok_a_ref.shape[0]
    local_experts = x_ref.shape[0]
    branch = dot(branch_operand(att_mine_ref), branch_weights(w_mine_ref))
    branch = branch + dot(branch_operand(att_other_ref), branch_weights(w_other_ref))
    for half in range(2):
        tok_ref, routes_ref = ((tok_a_ref, routes_a_ref), (tok_b_ref, routes_b_ref))[half]
        middle = tok_ref[...].astype(f32) + branch[half * rows : (half + 1) * rows]
        inverse = lax.rsqrt(jnp.mean(middle * middle, axis=1, keepdims=True) + epsilon)
        normed = (middle * inverse * gain_ref[...]).astype(bf16)
        normed_ref[half, 0] = normed
        logits = dot_nt(w_router_ref[...], normed)
        padded = logits.shape[0]
        slot = lax.broadcasted_iota(jnp.int32, (padded, rows), 0)
        expert = (slot // 8) * local_experts + slot % 8
        expert = jnp.where(slot % 8 < local_experts, expert, -1).astype(f32)
        routes = routes_ref[0].astype(f32)
        named = expert == routes[0:1, 0:rows]
        for k in range(1, TOP):
            named = named | (expert == routes[k : k + 1, 0:rows])
        peak = jnp.max(jnp.where(named, logits, masked_score), axis=0, keepdims=True)
        weights = jnp.where(named, jnp.exp(logits - peak), 0.0)
        gates = weights / jnp.sum(weights, axis=0, keepdims=True)
        gates_ref[...] = gates
        ranks_ref[...] = jnp.where(named, dot(named.astype(f32).astype(bf16), after_ref[...]), -1.0)
        here = pl.ds(pl.multiple_of(member * 8, 8), 8)
        gate, rank = gates_ref[here, :], ranks_ref[here, :]
        rank_ref[half, 0] = rank
        gate_ref[half, 0] = gate
        hits = hits_of(rank, local_experts)
        slot_gate = jnp.concatenate(
            [jnp.sum(jnp.where(hit, gate[j : j + 1, :], 0.0), axis=1, keepdims=True) for j, hit in enumerate(hits)],
            axis=0,
        )
        chosen = chosen_of(hits)
        picked = dot(chosen, normed).astype(bf16)
        spread = jnp.broadcast_to(slot_gate, (slot_gate.shape[0], LANES))
        for j in range(local_experts):
            part = slice(j * CAPACITY, (j + 1) * CAPACITY)
            x_ref[j, half, 0] = picked[part]
            slot_gate_ref[j, half, 0] = spread[part]

        @pl.when(member == half * cols + step)
        def _(middle=middle, gates=gates):
            middle_ref[...] = middle
            gates_own_ref[...] = gates


def middle_and_dispatch(place, att, w_mine, w_other, tokens, routes, gain, w_router, local_experts):
    width = tokens.shape[1]
    half = COLS
    rows = tokens.shape[0] // (2 * half)
    padded = w_router.shape[0]
    after = (jnp.arange(rows)[:, None] < jnp.arange(rows)[None, :]).astype(bf16)
    slot_shape = (local_experts, 2, half, CAPACITY)
    early = pl.BlockSpec((rows, width), lambda i, p: (i, 0))
    late = pl.BlockSpec((rows, width), lambda i, p: (i + half, 0))
    routes_shape = (1,) + routes.shape[1:]
    return call(
        middle_kernel,
        (half,),
        1,
        [
            pl.BlockSpec((1, half, rows, 3 * LANES), lambda i, p: (p[0], 0, i, 0)),
            pl.BlockSpec((1, half, rows, 3 * LANES), lambda i, p: (1 - p[0], 0, i, 0)),
            whole(w_mine.shape),
            whole(w_other.shape),
            early,
            late,
            pl.BlockSpec(routes_shape, lambda i, p: (i, 0, 0)),
            pl.BlockSpec(routes_shape, lambda i, p: (i + half, 0, 0)),
            whole((1, width)),
            whole(w_router.shape),
            whole((rows, rows)),
        ],
        [
            pl.BlockSpec((local_experts, 2, 1, CAPACITY, width), lambda i, p: (0, 0, i, 0, 0)),
            pl.BlockSpec((local_experts, 2, 1, CAPACITY, LANES), lambda i, p: (0, 0, i, 0, 0)),
            pl.BlockSpec((2, 1, 8, rows), lambda i, p: (0, i, 0, 0)),
            pl.BlockSpec((2, 1, 8, rows), lambda i, p: (0, i, 0, 0)),
            pl.BlockSpec((2, 1, rows, width), lambda i, p: (0, i, 0, 0)),
            whole((rows, width)),
            whole((padded, rows)),
        ],
        [
            struct(slot_shape + (width,), bf16),
            struct(slot_shape + (LANES,), f32),
            struct((2, half, 8, rows), f32),
            struct((2, half, 8, rows), f32),
            struct((2, half, rows, width), bf16),
            struct((rows, width), f32),
            struct((padded, rows), f32),
        ],
        scratch=[pltpu.VMEM((padded, rows), f32), pltpu.VMEM((padded, rows), f32)],
        us=0.5,
    )(place, att, att, w_mine, w_other, tokens, tokens, routes, routes, gain, w_router, after)


def grad_dispatch_kernel(rank_ref, gate_ref, cot_ref, g_ref):
    local_experts = g_ref.shape[0]
    rows = cot_ref.shape[0] // 2
    for half in range(2):
        hits = hits_of(rank_ref[half], local_experts)
        gate = gate_ref[half]
        slot_gate = jnp.concatenate(
            [jnp.sum(jnp.where(hit, gate[j : j + 1, :], 0.0), axis=1, keepdims=True) for j, hit in enumerate(hits)],
            axis=0,
        )
        grads = (dot(chosen_of(hits), cot_ref[half * rows : (half + 1) * rows, :]) * slot_gate).astype(bf16)
        for j in range(local_experts):
            g_ref[j, half] = grads[j * CAPACITY : (j + 1) * CAPACITY]


def grad_dispatch(rank, gate, cotangents, local_experts):
    members, _, rows = rank.shape
    width = cotangents.shape[1]
    small = pl.BlockSpec((2, 8, rows), lambda j: (j, 0, 0))
    return call(
        grad_dispatch_kernel,
        (members // 2,),
        0,
        [small, small, pl.BlockSpec((2 * rows, width), lambda j: (j, 0))],
        pl.BlockSpec((local_experts, 2, CAPACITY, width), lambda j: (0, j, 0, 0)),
        struct((local_experts, members, CAPACITY, width), bf16),
        us=0.5,
    )(rank, gate, cotangents)


def expert_kernel(
    x_ref, gate_ref, w_gate_ref, w_up_ref, w_down_ref, forth_ref, active_ref, factor_ref, silu_ref
):
    gate_pre = dot(x_ref[0], w_gate_ref[0])
    up_pre = dot(x_ref[0], w_up_ref[0])
    sig = 1.0 / (1.0 + jnp.exp(-gate_pre))
    silu = gate_pre * sig
    silu_ref[0] = silu
    factor_ref[0] = up_pre * sig * (1.0 + gate_pre * (1.0 - sig))
    active_ref[0] = (silu * up_pre).astype(bf16)
    produced = dot_nt(active_ref[0], w_down_ref[0]).astype(bf16).astype(f32)
    forth_ref[0] = (produced * gate_ref[0, :, 0:1]).astype(bf16)


def run_experts(x, slot_gate, w_gate, w_up, w_down):
    count, slots, width = x.shape
    hidden = w_gate.shape[2]

    def per_expert(*shape):
        return pl.BlockSpec((1,) + shape, lambda e: (e, 0, 0))

    return call(
        expert_kernel,
        (count,),
        0,
        [per_expert(slots, width), per_expert(slots, LANES)] + [per_expert(width, hidden)] * 3,
        [per_expert(slots, width)] + [per_expert(slots, hidden)] * 3,
        [
            struct((count, slots, width), bf16),
            struct((count, slots, hidden), bf16),
            struct((count, slots, hidden), f32),
            struct((count, slots, hidden), f32),
        ],
        us=0.5,
    )(x, slot_gate, w_gate, w_up, w_down)


def expert_back_kernel(place_ref, *refs, fast):
    x_ref, g_ref, active_ref, factor_ref, silu_ref = refs[:5]
    w_gate_ref, w_up_ref, w_down_ref, back_ref, dots_ref = refs[5:10]
    grads, (gate_low_ref, up_low_ref) = refs[10:-2], refs[-2:]
    slots, width = g_ref.shape[1], g_ref.shape[2]
    chunk = 256
    active_grad = dot(g_ref[0], w_down_ref[0])
    gate_low_ref[...] = (active_grad * factor_ref[0]).astype(bf16)
    up_low_ref[...] = (active_grad * silu_ref[0]).astype(bf16)
    dots = jnp.sum(active_ref[0].astype(f32) * active_grad, axis=1, keepdims=True)
    dots_ref[0] = jnp.broadcast_to(dots, (slots, LANES))
    back_ref[0] = (dot_nt(gate_low_ref[...], w_gate_ref[0]) + dot_nt(up_low_ref[...], w_up_ref[0])).astype(bf16)

    def products(cols):
        x = x_ref[0, :, cols]
        yield 0, dot_tn(x, gate_low_ref[...]).astype(bf16)
        yield 1, dot_tn(x, up_low_ref[...]).astype(bf16)
        yield 2, dot_tn(g_ref[0, :, cols], active_ref[0]).astype(bf16)

    if fast:
        write_shards(place_ref, grads, products, width)
    else:

        def whole_columns(index, carry):
            cols = pl.ds(pl.multiple_of(index * chunk, chunk), chunk)
            for which, product in products(cols):
                grads[which][0, cols, :] = product
            return carry

        lax.fori_loop(0, width // chunk, whole_columns, 0)


def write_shards(place_ref, outs, products, width):
    send_a, keep_a, send_b, keep_b = outs
    x_bit, y_bit = place_ref[3], place_ref[4]
    shard = width // 4
    for dy in range(2):
        for dx in range(2):
            x, y = x_bit ^ dx, y_bit ^ dy
            cols = pl.ds(pl.multiple_of((y * 2 + x) * shard, shard), shard)
            for which, product in products(cols):
                side = product.shape[1] // 2
                (send_a if dx else keep_a)[0, which, y] = product[:, :side]
                (send_b if dy else keep_b)[0, which, x] = product[:, side:]


def run_experts_back(place, x, g, active, factor, silu, w_gate, w_up, w_down, first, count, fast):
    slots, width = g.shape[1], g.shape[2]
    hidden = w_gate.shape[2]

    def taken(*shape):
        return pl.BlockSpec((1,) + shape, lambda e, p: (e + first, 0, 0))

    def given(*shape):
        zeros = (0,) * len(shape)
        return pl.BlockSpec((1,) + shape, lambda e, p: (e,) + zeros)

    if fast:
        grad_shapes = [(3, 2, width // 4, hidden // 2)] * 4
    else:
        grad_shapes = [(width, hidden)] * 3
    return call(
        lambda *refs: expert_back_kernel(*refs, fast=fast),
        (count,),
        1,
        [taken(slots, width)] * 2 + [taken(slots, hidden)] * 3 + [taken(width, hidden)] * 3,
        [given(slots, width), given(slots, LANES)] + [given(*shape) for shape in grad_shapes],
        [struct((count, slots, width), bf16), struct((count, slots, LANES), f32)]
        + [struct((count,) + shape, bf16) for shape in grad_shapes],
        scratch=[pltpu.VMEM((slots, hidden), bf16)] * 2,
        us=0.5,
    )(place, x, g, active, factor, silu, w_gate, w_up, w_down)


DOT_LANES = 2 * LANES


def combine_kernel(place_ref, rank_ref, *refs, pieces, with_dots, mine):
    parts, rest = refs[:pieces], refs[pieces:]
    rows = rank_ref.shape[2]
    local_experts = sum(part.shape[0] for part in parts)
    hits = hits_of(rank_ref[0], local_experts)
    gathered = jnp.concatenate([part[j, 0] for part in parts for j in range(part.shape[0])], axis=0)
    summed = dot_tn(chosen_of(hits), gathered)
    out_ref = rest[-1]
    if mine:
        arrived_ref = rest[-2]
        summed = summed + arrived_ref[0, 0:rows, :].astype(f32)
    out_ref[0, 0:rows, :] = summed.astype(bf16)
    if with_dots:
        column = [part[j, 0][:, 0:1] for part in rest[:pieces] for j in range(part.shape[0])]
        scattered = [
            jnp.sum(jnp.where(hit, value, 0.0), axis=0, keepdims=True) for hit, value in zip(hits, column)
        ]
        scattered.append(jnp.zeros((DOT_ROWS - local_experts, rows), f32))
        scattered = jnp.concatenate(scattered, axis=0)
        upper = scattered.astype(bf16)
        out_ref[0, rows:, :] = jnp.zeros((DOT_ROWS, out_ref.shape[2]), bf16)
        out_ref[0, rows:, 0:rows] = upper
        out_ref[0, rows:, DOT_LANES : DOT_LANES + rows] = (scattered - upper.astype(f32)).astype(bf16)
        if mine:
            out_ref[0, rows:, 2 * DOT_LANES : 4 * DOT_LANES] = arrived_ref[0, rows:, 0 : 2 * DOT_LANES]


def combine(place, rank, parts, dots=None, arrived=None):
    mine = arrived is not None
    rows, width = rank.shape[2], parts[0].shape[-1]
    out_rows = rows + (DOT_ROWS if dots else 0)

    def member(step, p):
        return (p[0] if mine else 1 - p[0]) * COLS + step

    def slots_of(array):
        return pl.BlockSpec((array.shape[0], 1) + array.shape[2:], lambda j, p: (0, member(j, p), 0, 0))

    inputs = [
        part.reshape(part.shape[0], 2 * COLS, CAPACITY, part.shape[-1]) for part in list(parts) + list(dots or [])
    ]
    in_specs = [pl.BlockSpec((1, 8, rows), lambda j, p: (member(j, p), 0, 0))] + [slots_of(item) for item in inputs]
    by_chip = pl.BlockSpec((1, out_rows, width), lambda j, p: (j, 0, 0))
    if mine:
        inputs.append(arrived)
        in_specs.append(by_chip)
    return call(
        lambda *refs: combine_kernel(*refs, pieces=len(parts), with_dots=bool(dots), mine=mine),
        (COLS,),
        1,
        in_specs,
        by_chip,
        struct((COLS, out_rows, width), bf16),
        us=0.5,
    )(place, rank, *inputs)


def split_dot(dimension_numbers, values, exact):
    upper = values.astype(bf16)
    lower = (values - upper.astype(f32)).astype(bf16)
    return lax.dot_general(
        upper, exact, dimension_numbers, preferred_element_type=f32
    ) + lax.dot_general(lower, exact, dimension_numbers, preferred_element_type=f32)


EXTRA_SLOTS = 6


def middle_back_kernel(
    place_ref, sums_ref, gates_ref, middle_ref, cot_ref, gain_ref, w_router_ref, w_mine_ref, w_other_ref,
    grad_ref, branch_ref, attended_ref, extra_ref
):
    rows = middle_ref.shape[0]
    tail = sums_ref[:, rows : rows + 8, 0 : 4 * DOT_LANES].astype(f32)
    mine = tail[:, :, 0:rows] + tail[:, :, DOT_LANES : DOT_LANES + rows]
    other = tail[:, :, 2 * DOT_LANES : 2 * DOT_LANES + rows] + tail[:, :, 3 * DOT_LANES : 3 * DOT_LANES + rows]
    first_row = place_ref[0] == 0
    dots = jnp.concatenate([jnp.where(first_row, mine, other), jnp.where(first_row, other, mine)], axis=0)
    dots = dots.reshape(dots.shape[0] * 8, rows)
    gates = gates_ref[...]
    logit_grad = dots - gates * jnp.sum(dots, axis=0, keepdims=True)
    middle = middle_ref[...]
    inverse = lax.rsqrt(jnp.mean(middle * middle, axis=1, keepdims=True) + epsilon)
    unit = middle * inverse
    gain = gain_ref[...]
    grad = sums_ref[0, 0:rows].astype(f32)
    for index in range(1, sums_ref.shape[0]):
        grad = grad + sums_ref[index, 0:rows].astype(f32)
    grad = grad + split_dot(TN, logit_grad, w_router_ref[...])
    gain_grad = jnp.sum(grad * unit, axis=0, keepdims=True)
    scaled = grad * gain
    middle_grad = cot_ref[...].astype(f32) + inverse * (
        scaled - unit * jnp.mean(scaled * unit, axis=1, keepdims=True)
    )
    grad_ref[...] = middle_grad
    branch_grad = middle_grad.astype(bf16)
    branch_ref[0:rows, :] = branch_grad
    extra_ref[...] = jnp.zeros_like(extra_ref)
    for index in range(logit_grad.shape[0] // 8):
        first, lane = index // EXTRA_SLOTS * 8, index % EXTRA_SLOTS * DOT_LANES
        extra_ref[first : first + 8, lane : lane + rows] = logit_grad[index * 8 : index * 8 + 8]
    upper = gain_grad.astype(bf16).astype(f32)
    extra_ref[13:14, :] = upper
    extra_ref[14:15, :] = gain_grad - upper
    branch_ref[rows:, :] = extra_ref[...].astype(bf16)
    for which, ref in enumerate((w_mine_ref, w_other_ref)):
        line = place_ref[0] if which == 0 else 1 - place_ref[0]
        for col in range(ref.shape[0]):
            product = dot_nt(branch_grad, ref[col])
            member = line * COLS + col
            attended_ref[member, :, 0:LANES] = product[:, 0:LANES].astype(bf16)
            attended_ref[member, :, LANES : LANES + HEAD_DIM] = product[:, LANES:].astype(bf16)
            attended_ref[member, :, LANES + HEAD_DIM :] = jnp.zeros((product.shape[0], HEAD_DIM), bf16)


def middle_back(place, sums, gates, middle, cotangent, gain, w_router, w_mine, w_other):
    rows, width = middle.shape
    members = 2 * COLS
    args = (sums, gates, middle, cotangent, gain, w_router, w_mine, w_other)
    return call(
        middle_back_kernel,
        (1,),
        1,
        [whole(item.shape) for item in args],
        [whole((rows, width)), whole((rows + DOT_ROWS, width)), whole((members, rows, 2 * LANES))],
        [
            struct((rows, width), f32),
            struct((rows + DOT_ROWS, width), bf16),
            struct((members, rows, 2 * LANES), bf16),
        ],
        scratch=[pltpu.VMEM((DOT_ROWS, width), f32)],
        us=0.5,
    )(place, *args)


def input_grad_kernel(
    place_ref, grads_ref, w_mine_ref, w_other_ref, tok_ref, middle_grad_ref, gain_ref, out_ref, sum_ref
):
    step = pl.program_id(0)

    @pl.when(step == 0)
    def _():
        sum_ref[...] = jnp.zeros_like(sum_ref)

    def add(ref):
        sum_ref[...] += dot(grads_ref[0], jnp.concatenate([ref[0], ref[0, 4 * HEAD_DIM :]], axis=0))

    @pl.when(step < COLS)
    def _():
        add(w_mine_ref)

    @pl.when(step >= COLS)
    def _():
        add(w_other_ref)

    @pl.when(step == pl.num_programs(0) - 1)
    def _():
        resid = tok_ref[...].astype(f32)
        inverse = lax.rsqrt(jnp.mean(resid * resid, axis=1, keepdims=True) + epsilon)
        unit = resid * inverse
        scaled = sum_ref[...] * gain_ref[...]
        out_ref[...] = middle_grad_ref[...] + inverse * (
            scaled - unit * jnp.mean(scaled * unit, axis=1, keepdims=True)
        )


def input_grad(place, grads, w_mine, w_other, tokens, middle_grad, gain):
    rows, width = tokens.shape
    members, lanes = grads.shape[0], grads.shape[2]
    w_shape = (1,) + w_mine.shape[1:]

    def member(step, p):
        line = jnp.where(step < COLS, p[0], 1 - p[0])
        return line * COLS + lax.rem(step, COLS)

    return call(
        input_grad_kernel,
        (members,),
        1,
        [
            pl.BlockSpec((1, rows, lanes), lambda m, p: (member(m, p), 0, 0)),
            pl.BlockSpec(w_shape, lambda m, p: (jnp.minimum(m, COLS - 1), 0, 0)),
            pl.BlockSpec(w_shape, lambda m, p: (jnp.maximum(m - COLS, 0), 0, 0)),
            whole((rows, width)),
            whole((rows, width)),
            whole((1, width)),
        ],
        whole((rows, width)),
        struct((rows, width), f32),
        scratch=[pltpu.VMEM((rows, width), f32)],
        us=0.5,
    )(place, grads, w_mine, w_other, tokens, middle_grad, gain)


def own_weights_kernel(normed_ref, projected_ref, w_ref, gain_ref, out_ref, gain_grad_ref, sum_ref):
    step = pl.program_id(0)

    @pl.when(step == 0)
    def _():
        sum_ref[...] = jnp.zeros_like(sum_ref)

    sum_ref[...] += dot_tn(normed_ref[...], projected_ref[...])

    @pl.when(step == pl.num_programs(0) - 1)
    def _():
        total = sum_ref[...]
        out_ref[...] = total.astype(bf16)
        by_weight = jnp.sum(total * w_ref[...].astype(f32), axis=1, keepdims=True)
        gain_grad_ref[...] = jnp.broadcast_to(by_weight / gain_ref[...], gain_grad_ref.shape)


def own_weights(normed, projected, w_natural, gain):
    total, width = normed.shape
    lanes = projected.shape[1]
    rows = 512
    return call(
        own_weights_kernel,
        (total // rows,),
        0,
        [
            pl.BlockSpec((rows, width), lambda j: (j, 0)),
            pl.BlockSpec((rows, lanes), lambda j: (j, 0)),
            whole((width, lanes)),
            whole((width, 1)),
        ],
        [whole((width, lanes)), whole((width, 8))],
        [struct((width, lanes), bf16), struct((width, 8), f32)],
        scratch=[pltpu.VMEM((width, lanes), f32)],
        us=0.5,
    )(normed, projected, w_natural, gain)


def out_weights_kernel(place_ref, branch_ref, att_ref, normed_ref, own_ref, *refs, fast, local_experts):
    outs, small_ref, (sum_ref, gain_sum_ref) = refs[:-3], refs[-3], refs[-2:]
    step = pl.program_id(0)
    rows = att_ref.shape[0] // 2
    block = rows + DOT_ROWS

    @pl.when(step == 0)
    def _():
        sum_ref[...] = jnp.zeros_like(sum_ref)
        small_ref[...] = jnp.zeros_like(small_ref)
        gain_sum_ref[...] = jnp.zeros_like(gain_sum_ref)

    branch = jnp.concatenate([branch_ref[0:rows, :], branch_ref[block : block + rows, :]], axis=0)
    sum_ref[...] += dot_tn(branch, att_ref[...])
    for which in range(2):
        tail = branch_ref[which * block + rows : (which + 1) * block, :].astype(f32)
        slots = []
        for index in range(small_ref.shape[0] // 8):
            first, lane = index // EXTRA_SLOTS * 8, index % EXTRA_SLOTS * DOT_LANES
            slots.append(tail[first : first + 8, lane : lane + rows])
        logit_grad = jnp.concatenate(slots, axis=0)
        real = lax.broadcasted_iota(jnp.int32, logit_grad.shape, 0) % 8 < local_experts
        logit_grad = jnp.where(real, logit_grad, 0.0).astype(bf16)
        small_ref[...] += dot(logit_grad, normed_ref[which * rows : (which + 1) * rows, :])
        gain_sum_ref[...] += tail[8:16, :]

    @pl.when(step == pl.num_programs(0) - 1)
    def _():
        small_ref[7:8, :] = gain_sum_ref[5:6, :] + gain_sum_ref[6:7, :]

        def products(cols):
            own = own_ref[cols, 0 : 2 * LANES]
            out_one = sum_ref[cols, 0:LANES].astype(bf16)
            out_two = sum_ref[cols, LANES:]
            low = lane_of(out_two.shape) < HEAD_DIM
            tail = jnp.where(low, out_two, own_ref[cols, 2 * LANES :].astype(f32)).astype(bf16)
            yield 0, jnp.concatenate([own, out_one, tail], axis=1)

        if fast:
            write_shards(place_ref, outs, products, own_ref.shape[0])
        else:
            outs[0][...] = next(products(slice(0, own_ref.shape[0])))[1]


def out_weights(place, branch, attended, normed, own, padded, local_experts, fast):
    total, width = normed.shape
    rows = total // COLS
    blocks = branch.shape[0] // COLS
    if fast:
        shapes = [(1, 1, 2, width // 4, 2 * LANES)] * 4
    else:
        shapes = [(width, 4 * LANES)]
    return call(
        lambda *refs: out_weights_kernel(*refs, fast=fast, local_experts=local_experts),
        (COLS,),
        1,
        [
            pl.BlockSpec((blocks, width), lambda j, p: (j, 0)),
            pl.BlockSpec((rows, 2 * LANES), lambda j, p: (j, 0)),
            pl.BlockSpec((rows, width), lambda j, p: (j, 0)),
            whole(own.shape),
        ],
        [whole(shape) for shape in shapes] + [whole((padded, width))],
        [struct(shape, bf16) for shape in shapes] + [struct((padded, width), f32)],
        scratch=[pltpu.VMEM((width, 2 * LANES), f32), pltpu.VMEM((8, width), f32)],
        us=0.5,
    )(place, branch, attended, normed, own)


def first_sum_kernel(place_ref, *refs, counts):
    outs = refs[4 * len(counts) :]
    x_bit, y_bit = place_ref[3], place_ref[4]
    expert = pl.program_id(0)
    first = 0
    for index, count in enumerate(counts):
        parts = refs[4 * index : 4 * index + 4]

        @pl.when((expert >= first) & (expert < first + count))
        def _(parts=parts):
            for side, bit in enumerate((y_bit, x_bit)):
                keep, got = parts[2 * side], parts[2 * side + 1]
                send, held = outs[2 * side], outs[2 * side + 1]
                held[0, 0] = keep[0, 0, bit].astype(f32) + got[0, 0, bit].astype(f32)
                send[0, 0] = (keep[0, 0, 1 - bit].astype(f32) + got[0, 0, 1 - bit].astype(f32)).astype(bf16)

        first += count


def first_sum(place, chunks):
    counts = [chunk[0].shape[0] for chunk in chunks]
    _, kinds, _, rows, cols = chunks[0][0].shape
    specs, first = [], 0
    for count in counts:

        def taken(e, k, p, first=first, count=count):
            inside = (e >= first) & (e < first + count)
            kind = jnp.where(inside, k, jnp.where(e < first, 0, kinds - 1))
            return (jnp.clip(e - first, 0, count - 1), kind, 0, 0, 0)

        specs += [pl.BlockSpec((1, 1, 2, rows, cols), taken)] * 4
        first += count
    given = pl.BlockSpec((1, 1, rows, cols), lambda e, k, p: (e, k, 0, 0))
    shape = (first, kinds, rows, cols)
    return call(
        lambda *refs: first_sum_kernel(*refs, counts=counts),
        (first, kinds),
        1,
        specs,
        [given] * 4,
        [struct(shape, bf16), struct(shape, f32), struct(shape, bf16), struct(shape, f32)],
        us=0.5,
    )(place, *[item for chunk in chunks for item in chunk])


def last_sum_kernel(held_a_ref, got_a_ref, held_b_ref, got_b_ref, *rest):
    outs = rest[-3:]
    side = held_a_ref.shape[3]
    for which, out in enumerate(outs):
        out[0, :, :side] = held_a_ref[0, which] + got_a_ref[0, which].astype(f32)
        out[0, :, side:] = held_b_ref[0, which] + got_b_ref[0, which].astype(f32)


def last_sum(held_a, got_a, held_b, got_b, first, total, before):
    count, kinds, rows, cols = held_a.shape
    taken = pl.BlockSpec((1, kinds, rows, cols), lambda e: (e, 0, 0, 0))
    given = pl.BlockSpec((1, rows, 2 * cols), lambda e: (e + first, 0, 0))
    extra = list(before) if before else []
    return call(
        last_sum_kernel,
        (count,),
        0,
        [taken] * 4 + [pl.BlockSpec(memory_space=pl.ANY)] * len(extra),
        [given] * 3,
        [struct((total, rows, 2 * cols), f32)] * 3,
        us=0.5,
        aliases={4 + i: i for i in range(len(extra))},
    )(held_a, got_a, held_b, got_b, *extra)


SWAP = [(0, 1), (1, 0)]


def after(value, *events):
    return lax.optimization_barrier((value,) + events)[0]


def gather_group(block):
    return lax.all_gather(block, ("row", "col"), axis=0, tiled=True)


def line_pieces(value):
    parts = [value]
    for distance in range(1, COLS):
        parts.insert(0, lax.ppermute(value, "col", [(i, (i + distance) % COLS) for i in range(COLS)]))
    return parts


def in_line_order(parts):
    parts = jnp.stack(parts + parts)
    return lax.dynamic_slice_in_dim(parts, COLS - 1 - lax.axis_index("col"), COLS, axis=0)


def flip(value, axis, bit, size):
    return lax.ppermute(value, axis, [(i, i ^ (1 << bit)) for i in range(size)])


def bits_of(size):
    return size.bit_length() - 1


def own_bit(axis, bit):
    return (lax.axis_index(axis) >> bit) & 1


def joined(mine, got, own):
    return jnp.where(own == 0, jnp.concatenate([mine, got]), jnp.concatenate([got, mine]))


def cube_step(value, axis, bit, size):
    return joined(value, flip(value, axis, bit, size), own_bit(axis, bit))


def lines_first(value):
    return jnp.transpose(value, (1, 0, 2, 3)).reshape(value.shape[1], value.shape[0] * value.shape[2], value.shape[3])


def cube_gather(value, axis, size):
    value = value[None]
    for bit in range(bits_of(size)):
        value = cube_step(value, axis, bit, size)
    return value


def sum_group(value, sizes):
    for axis, bit in (("row", 0), ("col", 0), ("col", 1)):
        value = value + flip(value, axis, bit, sizes[axis])
    return value


def sum_dp(value, sizes):
    for bit in range(bits_of(sizes["dp"])):
        value = value + flip(value, "dp", bit, sizes["dp"])
    return value


def reduce_over_dp(value, size):
    count = bits_of(size)
    value = value.reshape(value.shape[:1] + (2,) * count + value.shape[2:])
    current = value
    for bit in range(count - 1, -1, -1):
        own = own_bit("dp", bit)
        keep = lax.dynamic_index_in_dim(current, own, 1, keepdims=False)
        send = lax.dynamic_index_in_dim(current, 1 - own, 1, keepdims=False).astype(bf16)
        current = keep.astype(f32) + flip(send, "dp", bit, size).astype(f32)
    return current


def start_move(run, size):
    return flip(run[0], "dp", 0, size), flip(run[2], "dp", 1, size)


def first_half(place, runs, gots, size, event):
    chunks = []
    for run, got in zip(runs, gots):
        keep_a, keep_b = after((run[1], run[3]), event)
        chunks.append((keep_a, got[0], keep_b, got[1]))
    send_a, held_a, send_b, held_b = first_sum(place, chunks)
    return held_a, flip(send_a, "dp", 1, size), held_b, flip(send_b, "dp", 0, size)


def layer(sizes):
    n_dp, n_row, n_col = sizes["dp"], sizes["row"], sizes["col"]
    members = n_row * n_col
    fast = n_dp == 4
    assert n_row == 2 and n_col == COLS and n_dp & (n_dp - 1) == 0

    def local(
        tokens, cotangent, routes, lengths, gain_attn, w_query, w_key, w_value, w_out,
        gain_moe, w_router, w_gate, w_up, w_down,
    ):
        rows, width = tokens.shape
        group = rows * members
        local_experts = w_gate.shape[0]
        row, col, dp = lax.axis_index("row"), lax.axis_index("col"), lax.axis_index("dp")
        place = jnp.stack([row, col, row * n_col + col, dp & 1, (dp >> 1) & 1]).astype(jnp.int32)
        gain_one = gain_attn.astype(f32)[None]
        gain_two = gain_moe.astype(f32)[None]

        tok_all = gather_group(tokens)
        w_in = jnp.concatenate([w_query.T, w_key.T, w_value.T], axis=0)
        out_share, in_share = rows // n_dp, w_in.shape[0] // n_dp
        shares = jnp.concatenate(
            [
                lax.dynamic_slice(w_out.T, (dp * out_share, 0), (out_share, width)),
                lax.dynamic_slice(w_in, (dp * in_share, 0), (in_share, width)),
                jnp.pad(routes.T.astype(bf16).reshape(1, TOP * rows), ((0, 7), (0, width - TOP * rows))),
            ],
            axis=0,
        )
        shares = line_pieces(after(shares, tok_all))
        w_stack = jnp.concatenate([w_query.T, w_key.T, w_value.T, w_value.T], axis=0)
        w_natural = jnp.concatenate([w_query, w_key, w_value, w_value], axis=1)

        ends = jnp.cumsum(lengths[0])
        starts = ends - lengths[0]
        position = jnp.arange(group, dtype=jnp.int32)
        segment = jnp.sum((position[:, None] >= ends[None, :]).astype(jnp.int32), axis=1)
        member = segment[:, None] == jnp.arange(starts.shape[0], dtype=jnp.int32)[None, :]
        start = jnp.sum(jnp.where(member, starts[None, :], 0), axis=1).astype(jnp.int32)
        frequency = rope_base ** (-2.0 * jnp.arange(HEAD_DIM // 2, dtype=f32) / HEAD_DIM)
        angle = (position - start).astype(f32)[:, None] * frequency[None, :]
        cosine = jnp.tile(jnp.cos(angle), (1, 4))
        sine = jnp.tile(jnp.sin(angle), (1, 4))

        query, key, value, normed_one = project(tok_all, gain_one, w_stack, cosine, sine)
        w_router_rows = w_router.T.reshape(members, local_experts, width)
        w_router_rows = jnp.pad(w_router_rows, ((0, 0), (0, 8 - local_experts), (0, 0)))
        w_router_rows = w_router_rows.reshape(members * 8, width)
        packed, attended, totals = attend(query, key, value, start[:, None])
        att_flat = gather_group(packed)
        att_all = att_flat.reshape((n_row, n_col) + packed.shape)
        shares = in_line_order(after(shares, packed))
        route_rows = shares[:, out_share + in_share]
        w_out_mine, in_part = shares[None, :, :out_share], shares[None, :, out_share : out_share + in_share]
        for bit in range(bits_of(n_dp)):
            w_out_mine = cube_step(w_out_mine, "dp", bit, n_dp)
        in_part = cube_step(in_part, "dp", 0, n_dp)
        w_out_mine = lines_first(w_out_mine)
        w_out_other = lax.ppermute(after(w_out_mine, in_part), "row", SWAP)
        route_rows = cube_gather(route_rows, "row", n_row)[:, :, : TOP * rows].reshape(members, TOP, rows)
        route_rows = jnp.pad(route_rows, ((0, 0), (0, ROUTE_ROWS - TOP), (0, 2 * LANES - rows)))
        cot_all = gather_group(after(cotangent, w_out_other))
        x, slot_gate, rank, gate, normed_two, middle, gates = middle_and_dispatch(
            place, att_all, w_out_mine, w_out_other, tok_all, route_rows, gain_two, w_router_rows, local_experts
        )
        slots = members * CAPACITY
        x = x.reshape(local_experts, slots, width)
        slot_gate = slot_gate.reshape(local_experts, slots, LANES)
        rank, gate = rank.reshape(members, 8, rows), gate.reshape(members, 8, rows)
        forth, active, factor, silu = run_experts(x, slot_gate, w_gate, w_up, w_down)
        for bit in range(1, bits_of(n_dp) - 1):
            in_part = cube_step(in_part, "dp", bit, n_dp)
        last_bit = bits_of(n_dp) - 1
        in_got = after(flip(in_part, "dp", last_bit, n_dp), forth)
        forth_other = combine(place, after(rank, in_got), [forth])
        arrived = lax.ppermute(forth_other, "row", SWAP)
        g = grad_dispatch(after(rank, forth_other), gate, cot_all, local_experts)
        g = g.reshape(local_experts, slots, width)
        cuts = [0, 1, 3, local_experts]

        def backward(which, x):
            first, last = cuts[which], cuts[which + 1]
            return run_experts_back(place, x, g, active, factor, silu, w_gate, w_up, w_down, first, last - first, fast)

        runs = [backward(0, x)]
        forth_mine = combine(place, rank, [forth], arrived=after(arrived, runs[0][1]))
        forth_sums = lax.all_to_all(forth_mine, "col", 0, 0, tiled=True)
        runs.append(backward(1, after(x, forth_mine)))
        runs.append(backward(2, after(x, runs[1][1])))
        moved = [start_move(run[2:], n_dp) for run in runs] if fast else []
        back_parts, dot_parts = [run[0] for run in runs], [run[1] for run in runs]
        back_other = combine(place, after(rank, *moved[0]) if fast else rank, back_parts, dot_parts)
        arrived = lax.ppermute(back_other, "row", SWAP)
        back_mine = combine(place, rank, back_parts, dot_parts, arrived)
        back_mine = after(back_mine, forth_sums)
        back_sums = lax.all_to_all(back_mine, "col", 0, 0, tiled=True)

        w_in_mine = lines_first(joined(in_part, after(in_got, back_mine), own_bit("dp", last_bit)))
        w_in_other = lax.ppermute(w_in_mine, "row", SWAP)

        middle_grad, branch_grad, attended_grad = middle_back(
            place, back_sums, gates, middle, cotangent, after(gain_two, w_in_other, *(moved[1] if fast else ())),
            w_router_rows, w_out_mine, w_out_other,
        )
        started = []
        if fast:
            started.append(first_half(place, [run[2:] for run in runs[:2]], moved[:2], n_dp, branch_grad))
        attended_grad = lax.all_to_all(attended_grad, ("row", "col"), 0, 0, tiled=True)
        branch_all = gather_group(after(branch_grad, attended_grad))

        start_row = jnp.broadcast_to(start[None, :], (8, group))
        attended_grad = attended_grad.reshape(group, 2 * LANES)
        if fast:
            attended_grad = after(attended_grad, started[0][0])
        projected_grad = attend_back(query, key, value, attended_grad, totals, start_row, cosine, sine)
        projected_all = lax.all_to_all(
            projected_grad.reshape(members, rows, 3 * LANES), ("row", "col"), 0, 0, tiled=True
        )
        own_grads, gain_part = own_weights(
            after(normed_one, *moved[2]) if fast else normed_one,
            projected_grad, w_natural, gain_attn.astype(f32)[:, None],
        )
        if fast:
            started.append(first_half(place, [runs[2][2:]], moved[2:], n_dp, own_grads))
        *w_parts, small = out_weights(
            place, branch_all, attended, after(normed_two, *[item[0] for item in started]).reshape(group, width), own_grads, members * 8, local_experts, fast
        )
        gain_attn_grad = sum_group(after(gain_part, small)[:, 0].reshape(8, width // 8), sizes)
        if fast:
            w_started = first_half(place, [w_parts], [start_move(w_parts, n_dp)], n_dp, w_parts[1])
        else:
            cut = w_parts[0].reshape(1, n_dp, width // n_dp, w_parts[0].shape[1])
            w_sum = reduce_over_dp(cut, n_dp)[0]

        mixed = (middle + jnp.sum(after(forth_sums, projected_grad).astype(f32), axis=0)).astype(bf16)

        used = small.reshape(members, 8, width)[:, :local_experts].reshape(members * local_experts, width)
        both = jnp.concatenate([used, small[7:8], gain_attn_grad.reshape(1, width)], axis=0)
        both = sum_dp(both, sizes)
        w_router_grad = both[: members * local_experts].T
        gain_moe_grad, gain_attn_grad = both[members * local_experts], both[members * local_experts + 1]

        tokens_grad = input_grad(
            place, projected_all, w_in_mine, w_in_other, tokens, middle_grad, after(gain_one, w_parts[0])
        )

        if fast:
            expert_grads = None
            for item, first, event in zip(started, (0, cuts[2]), (own_grads, w_parts[0])):
                held_a, got_a, held_b, got_b = item
                held_a, held_b = after((held_a, held_b), event)
                expert_grads = last_sum(held_a, got_a, held_b, got_b, first, local_experts, expert_grads)
            held_a, got_a, held_b, got_b = [item[0, 0] for item in w_started]
            left = held_a + got_a.astype(f32)
            right = held_b + got_b.astype(f32)
            w_sum = jnp.concatenate([left, right], axis=1)
        else:
            expert_grads = []
            for which in range(3):
                parts = [run[2 + which] for run in runs]
                parts = [part.reshape(part.shape[0], n_dp, width // n_dp, part.shape[2]) for part in parts]
                expert_grads.append(jnp.concatenate([reduce_over_dp(part, n_dp) for part in parts], axis=0))
        w_gate_grad, w_up_grad, w_down_grad = expert_grads
        local_q, local_k = w_query.shape[1], w_key.shape[1]
        cut = local_q + local_k
        return (
            mixed, tokens_grad, gain_attn_grad, w_sum[:, :local_q], w_sum[:, local_q:cut],
            w_sum[:, cut + local_q :], w_sum[:, cut : cut + local_q],
            gain_moe_grad, w_router_grad, w_gate_grad, w_up_grad, w_down_grad,
        )

    return local


def solution(mesh):
    return jax.shard_map(
        layer(dict(mesh.shape)),
        mesh=mesh,
        in_specs=(
            P(("dp", "row", "col"), None),
            P(("dp", "row", "col"), None),
            P(("dp", "row", "col"), None),
            P("dp", None),
            P(),
            P(None, ("row", "col")),
            P(None, ("row", "col")),
            P(None, ("row", "col")),
            P(None, ("row", "col")),
            P(),
            P(),
            P(("row", "col"), None, None),
            P(("row", "col"), None, None),
            P(("row", "col"), None, None),
        ),
        out_specs=(
            P(("dp", "row", "col"), None),
            P(("dp", "row", "col"), None),
            P(),
            P("dp", ("row", "col")),
            P("dp", ("row", "col")),
            P("dp", ("row", "col")),
            P("dp", ("row", "col")),
            P(),
            P(),
            P(("row", "col"), "dp", None),
            P(("row", "col"), "dp", None),
            P(("row", "col"), "dp", None),
        ),
        check_vma=False,
    )
```

```python
import math

import jax
import jax.numpy as jnp
import numpy as np
from jax import lax
from jax.experimental import pallas as pl
from jax.experimental.pallas import tpu as pltpu
from jax.sharding import PartitionSpec as P

HEAD_DIM = 64
EXPERTS = 40
TOP = 8
CAPACITY = 64
COLS = 4
LANES = 128
QUERY_BLOCK = 256
DOT_ROWS = 16

epsilon = 1e-06
rope_base = 10000.0
masked_score = -1e30
f32 = jnp.float32
bf16 = jnp.bfloat16
VMEM_LIMIT = 56 * 1024 * 1024

NT = (((1,), (1,)), ((), ()))
TN = (((0,), (0,)), ((), ()))


def dot(a, b):
    return jnp.dot(a, b, preferred_element_type=f32)


def dot_nt(a, b):
    return lax.dot_general(a, b, NT, preferred_element_type=f32)


def dot_tn(a, b):
    return lax.dot_general(a, b, TN, preferred_element_type=f32)


def lane_of(shape):
    return lax.broadcasted_iota(jnp.int32, shape, len(shape) - 1)


def call(
    kernel, grid, prefetch, in_specs, out_specs, out_shape, scratch=(), us=1.0, aliases=None
):
    return pl.pallas_call(
        kernel,
        grid_spec=pltpu.PrefetchScalarGridSpec(
            num_scalar_prefetch=prefetch,
            grid=grid,
            in_specs=in_specs,
            out_specs=out_specs,
            scratch_shapes=list(scratch),
        ),
        out_shape=out_shape,
        input_output_aliases=aliases or {},
        compiler_params=pltpu.CompilerParams(
            vmem_limit_bytes=VMEM_LIMIT, dimension_semantics=("arbitrary",) * len(grid)
        ),
        cost_estimate=pl.CostEstimate(
            flops=int(us * 1.1e9), bytes_accessed=int(us * 3.6e6), transcendentals=0
        ),
    )


def whole(shape):
    zeros = (0,) * len(shape)
    return pl.BlockSpec(shape, lambda *_: zeros)


def struct(shape, dtype):
    return jax.ShapeDtypeStruct(shape, dtype)


def turn_within_heads(values, sign):
    lane = lane_of(values.shape) % HEAD_DIM
    ahead = pltpu.roll(values, LANES - HEAD_DIM // 2, 1)
    behind = pltpu.roll(values, HEAD_DIM // 2, 1)
    return jnp.where(lane < HEAD_DIM // 2, -sign * ahead, sign * behind)


def project_kernel(
    tok_ref, gain_ref, w_ref, cos_ref, sin_ref, query_ref, key_ref, value_ref, normed_ref
):
    resid = tok_ref[...].astype(f32)
    inverse = lax.rsqrt(jnp.mean(resid * resid, axis=1, keepdims=True) + epsilon)
    normed = (resid * inverse * gain_ref[...]).astype(bf16)
    normed_ref[...] = normed
    raw = dot_nt(normed, w_ref[...])
    cosine, sine = cos_ref[...], sin_ref[...]

    def rot(values):
        return (values * cosine + turn_within_heads(values, 1.0) * sine).astype(bf16).astype(f32)

    first = rot(raw[:, :LANES])
    second = rot(raw[:, LANES : 2 * LANES])
    low = lane_of(first.shape) < HEAD_DIM
    scale = 1.0 / math.sqrt(HEAD_DIM)
    query_ref[0] = jnp.where(low, first * scale, 0.0).astype(bf16)
    query_ref[1] = jnp.where(low, 0.0, first * scale).astype(bf16)
    query_ref[2] = jnp.where(low, second * scale, 0.0).astype(bf16)
    key_ref[...] = jnp.where(low, pltpu.roll(second, HEAD_DIM, 1), second).astype(bf16)
    value_ref[...] = raw[:, 2 * LANES :].astype(bf16)


def project(tokens, gain, w_stack, cosine, sine):
    total, width = tokens.shape
    rows = 512
    lanes = pl.BlockSpec((rows, LANES), lambda j: (j, 0))
    wide = pl.BlockSpec((rows, width), lambda j: (j, 0))
    return call(
        project_kernel,
        (total // rows,),
        0,
        [wide, whole((1, width)), whole(w_stack.shape), lanes, lanes],
        [pl.BlockSpec((3, rows, LANES), lambda j: (0, j, 0)), lanes, lanes, wide],
        [
            struct((3, total, LANES), bf16),
            struct((total, LANES), bf16),
            struct((total, LANES), bf16),
            struct((total, width), bf16),
        ],
        us=0.5,
    )(tokens, gain, w_stack, cosine, sine)


def attend_kernel(query_ref, key_ref, value_ref, start_ref, packed_ref, plain_ref, total_ref, out_ref):
    blocks = query_ref.shape[1] // QUERY_BLOCK
    block = pl.program_id(0)
    for index in range(blocks):

        @pl.when(block == index)
        def _(index=index):
            rows = pl.ds(index * QUERY_BLOCK, QUERY_BLOCK)
            span = (index + 1) * QUERY_BLOCK
            row = index * QUERY_BLOCK + lax.broadcasted_iota(jnp.int32, (QUERY_BLOCK, span), 0)
            column = lane_of((QUERY_BLOCK, span))
            allowed = (column <= row) & (column >= start_ref[rows, :])

            def head(number, carry):
                scores = dot_nt(query_ref[number, rows, :], key_ref[0:span, :])
                scores = jnp.where(allowed, scores, masked_score)
                peak = jnp.max(scores, axis=1, keepdims=True)
                weights = jnp.exp(scores - peak)
                summed = jnp.sum(weights, axis=1, keepdims=True)
                probs = (weights * (1.0 / summed)).astype(bf16)
                out_ref[number] = dot(probs, value_ref[0:span, :])
                total = jnp.broadcast_to(peak + jnp.log(summed), (QUERY_BLOCK, LANES))
                total_ref[number, :, rows] = jnp.transpose(total)[0:8, :]
                return carry

            lax.fori_loop(0, 3, head, 0)
            low = lane_of((QUERY_BLOCK, LANES)) < HEAD_DIM
            one, two, three = out_ref[0], out_ref[1], out_ref[2]
            pair = jnp.where(low, one, two).astype(bf16)
            plain_ref[rows, 0:LANES] = pair
            plain_ref[rows, LANES : 2 * LANES] = jnp.where(low, three, 0.0).astype(bf16)
            if index < blocks // 2:
                packed_ref[rows, 0:LANES] = pair
                packed_ref[rows, LANES : 2 * LANES] = three.astype(bf16)
            else:
                back = pl.ds((index - blocks // 2) * QUERY_BLOCK, QUERY_BLOCK)
                before = packed_ref[back, LANES : 2 * LANES].astype(f32)
                packed_ref[back, LANES : 2 * LANES] = jnp.where(low, before, one).astype(bf16)
                packed_ref[back, 2 * LANES : 3 * LANES] = jnp.where(low, two, three).astype(bf16)


def attend(query, key, value, start):
    total = key.shape[0]
    return call(
        attend_kernel,
        (total // QUERY_BLOCK,),
        0,
        [whole(query.shape), whole(key.shape), whole(value.shape), whole(start.shape)],
        [whole((total // 2, 3 * LANES)), whole((total, 2 * LANES)), whole((3, 8, total))],
        [
            struct((total // 2, 3 * LANES), bf16),
            struct((total, 2 * LANES), bf16),
            struct((3, 8, total), f32),
        ],
        scratch=[pltpu.VMEM((3, QUERY_BLOCK, LANES), f32)],
        us=0.5,
    )(query, key, value, start)


def attend_back_kernel(
    query_ref, key_ref, value_ref, grad_ref, total_ref, start_ref, cos_ref, sin_ref,
    out_ref, query_grad_ref, key_grad_ref, value_grad_ref
):
    blocks = query_ref.shape[1] // QUERY_BLOCK
    block = pl.program_id(0)
    scale = 1.0 / math.sqrt(HEAD_DIM)

    @pl.when(block == 0)
    def _():
        key_grad_ref[...] = jnp.zeros_like(key_grad_ref)
        value_grad_ref[...] = jnp.zeros_like(value_grad_ref)

    def back(values, cosine, sine):
        return values * cosine + turn_within_heads(values * sine, -1.0)

    for index in range(blocks):

        @pl.when(block == index)
        def _(index=index):
            rows = pl.ds(index * QUERY_BLOCK, QUERY_BLOCK)
            span = (index + 1) * QUERY_BLOCK
            row = index * QUERY_BLOCK + lane_of((span, QUERY_BLOCK))
            column = lax.broadcasted_iota(jnp.int32, (span, QUERY_BLOCK), 0)
            allowed = (column <= row) & (column >= start_ref[0:1, rows])
            low = lane_of((QUERY_BLOCK, LANES)) < HEAD_DIM

            def head(number, carry):
                query = query_ref[number, rows, :]
                tile = pl.multiple_of((number // 2) * LANES, LANES)
                upstream = grad_ref[rows, pl.ds(tile, LANES)].astype(f32)
                keep = low == (number != 1)
                upstream = jnp.where(keep, upstream, 0.0).astype(bf16)
                scores = dot_nt(key_ref[0:span, :], query)
                probs = jnp.exp(scores - total_ref[number, 0:1, rows])
                probs = jnp.where(allowed, probs, 0.0)
                prob_grad = dot_nt(value_ref[0:span, :], upstream)
                row_dot = jnp.sum(probs * prob_grad, axis=0, keepdims=True)
                score_grad = (probs * (prob_grad - row_dot)).astype(bf16)
                key_grad_ref[0:span, :] += dot(score_grad, query)
                value_grad_ref[0:span, :] += dot(probs.astype(bf16), upstream)
                query_grad_ref[number] = dot_tn(score_grad, key_ref[0:span, :]) * scale
                return carry

            lax.fori_loop(0, 3, head, 0)
            cosine, sine = cos_ref[rows, :], sin_ref[rows, :]
            pair = jnp.where(low, query_grad_ref[0], query_grad_ref[1])
            out_ref[rows, 0:LANES] = back(pair, cosine, sine).astype(bf16)
            out_ref[rows, LANES : 2 * LANES] = back(query_grad_ref[2], cosine, sine).astype(bf16)

    @pl.when(block == blocks - 1)
    def _():
        low = lane_of(key_grad_ref.shape) < HEAD_DIM
        key_grad = key_grad_ref[...]
        key_grad = key_grad + pltpu.roll(key_grad, HEAD_DIM, 1)
        key_grad = back(key_grad, cos_ref[...], sin_ref[...])
        before = out_ref[:, LANES : 2 * LANES].astype(f32)
        out_ref[:, LANES : 2 * LANES] = jnp.where(low, before, key_grad).astype(bf16)
        value_grad = value_grad_ref[...]
        value_grad = value_grad + pltpu.roll(value_grad, HEAD_DIM, 1)
        out_ref[:, 2 * LANES : 3 * LANES] = jnp.where(low, 0.0, value_grad).astype(bf16)


def attend_back(query, key, value, grad, totals, start, cosine, sine):
    total = key.shape[0]
    args = (query, key, value, grad, totals, start, cosine, sine)
    return call(
        attend_back_kernel,
        (total // QUERY_BLOCK,),
        0,
        [whole(item.shape) for item in args],
        whole((total, 3 * LANES)),
        struct((total, 3 * LANES), bf16),
        scratch=[
            pltpu.VMEM((3, QUERY_BLOCK, LANES), f32),
            pltpu.VMEM((total, LANES), f32),
            pltpu.VMEM((total, LANES), f32),
        ],
        us=0.5,
    )(*args)


def branch_operand(refs):
    rows = refs.shape[2]
    low = lane_of((rows, LANES)) < HEAD_DIM
    pairs, thirds = [], []
    for member in range(refs.shape[1]):
        one = refs[0, member, :, 0:LANES]
        mid = refs[0, member, :, LANES : 2 * LANES].astype(f32)
        end = refs[0, member, :, 2 * LANES : 3 * LANES].astype(f32)
        mid_turned = pltpu.roll(mid, HEAD_DIM, 1)
        end_turned = pltpu.roll(end, HEAD_DIM, 1)
        late = jnp.where(low, mid_turned, end_turned).astype(bf16)
        pairs.append(jnp.concatenate([one, late], axis=0))
        thirds.append((mid, end_turned))
    for member in range(0, refs.shape[1], 2):
        tops = []
        for which in range(2):
            left, right = thirds[member][which], thirds[member + 1][which]
            tops.append(jnp.where(low, left, pltpu.roll(right, HEAD_DIM, 1)).astype(bf16))
        pairs.append(jnp.concatenate(tops, axis=0))
    return jnp.concatenate(pairs, axis=1)


def branch_weights(ref):
    right = [ref[source, 0:LANES] for source in range(ref.shape[0])]
    return jnp.concatenate(right + [ref[source, LANES:] for source in range(ref.shape[0])], axis=0)


def hits_of(rank, local_experts):
    place = lax.broadcasted_iota(jnp.int32, (CAPACITY, rank.shape[1]), 0).astype(f32)
    return [place == rank[j : j + 1, :] for j in range(local_experts)]


def chosen_of(hits):
    return jnp.concatenate([jnp.where(hit, 1.0, 0.0).astype(bf16) for hit in hits], axis=0)


def middle_kernel(
    place_ref, att_mine_ref, att_other_ref, w_mine_ref, w_other_ref, tok_a_ref, tok_b_ref, routes_a_ref, routes_b_ref,
    gain_ref, w_router_ref, after_ref,
    x_ref, slot_gate_ref, rank_ref, gate_ref, normed_ref, middle_ref, gates_own_ref, gates_ref, ranks_ref
):
    step = pl.program_id(0)
    member = place_ref[2]
    cols = pl.num_programs(0)
    rows = tok_a_ref.shape[0]
    local_experts = x_ref.shape[0]
    branch = dot(branch_operand(att_mine_ref), branch_weights(w_mine_ref))
    branch = branch + dot(branch_operand(att_other_ref), branch_weights(w_other_ref))
    for half in range(2):
        tok_ref, routes_ref = ((tok_a_ref, routes_a_ref), (tok_b_ref, routes_b_ref))[half]
        middle = tok_ref[...].astype(f32) + branch[half * rows : (half + 1) * rows]
        inverse = lax.rsqrt(jnp.mean(middle * middle, axis=1, keepdims=True) + epsilon)
        normed = (middle * inverse * gain_ref[...]).astype(bf16)
        normed_ref[half, 0] = normed
        logits = dot_nt(w_router_ref[...], normed)
        padded = logits.shape[0]
        slot = lax.broadcasted_iota(jnp.int32, (padded, rows), 0)
        expert = (slot // 8) * local_experts + slot % 8
        expert = jnp.where(slot % 8 < local_experts, expert, -1).astype(f32)
        routes = routes_ref[0].astype(f32)
        named = expert == routes[0:1, 0:rows]
        for k in range(1, TOP):
            named = named | (expert == routes[k : k + 1, 0:rows])
        peak = jnp.max(jnp.where(named, logits, masked_score), axis=0, keepdims=True)
        weights = jnp.where(named, jnp.exp(logits - peak), 0.0)
        gates = weights / jnp.sum(weights, axis=0, keepdims=True)
        gates_ref[...] = gates
        ranks_ref[...] = jnp.where(named, dot(named.astype(f32).astype(bf16), after_ref[...]), -1.0)
        here = pl.ds(pl.multiple_of(member * 8, 8), 8)
        gate, rank = gates_ref[here, :], ranks_ref[here, :]
        rank_ref[half, 0] = rank
        gate_ref[half, 0] = gate
        hits = hits_of(rank, local_experts)
        slot_gate = jnp.concatenate(
            [jnp.sum(jnp.where(hit, gate[j : j + 1, :], 0.0), axis=1, keepdims=True) for j, hit in enumerate(hits)],
            axis=0,
        )
        chosen = chosen_of(hits)
        picked = dot(chosen, normed).astype(bf16)
        spread = jnp.broadcast_to(slot_gate, (slot_gate.shape[0], LANES))
        for j in range(local_experts):
            part = slice(j * CAPACITY, (j + 1) * CAPACITY)
            x_ref[j, half, 0] = picked[part]
            slot_gate_ref[j, half, 0] = spread[part]

        @pl.when(member == half * cols + step)
        def _(middle=middle, gates=gates):
            middle_ref[...] = middle
            gates_own_ref[...] = gates


def middle_and_dispatch(place, att, w_mine, w_other, tokens, routes, gain, w_router, local_experts):
    width = tokens.shape[1]
    half = COLS
    rows = tokens.shape[0] // (2 * half)
    padded = w_router.shape[0]
    after = jnp.asarray(np.triu(np.ones((rows, rows), np.float32), 1), bf16)
    slot_shape = (local_experts, 2, half, CAPACITY)
    early = pl.BlockSpec((rows, width), lambda i, p: (i, 0))
    late = pl.BlockSpec((rows, width), lambda i, p: (i + half, 0))
    routes_shape = (1,) + routes.shape[1:]
    return call(
        middle_kernel,
        (half,),
        1,
        [
            pl.BlockSpec((1, half, rows, 3 * LANES), lambda i, p: (p[0], 0, i, 0)),
            pl.BlockSpec((1, half, rows, 3 * LANES), lambda i, p: (1 - p[0], 0, i, 0)),
            whole(w_mine.shape),
            whole(w_other.shape),
            early,
            late,
            pl.BlockSpec(routes_shape, lambda i, p: (i, 0, 0)),
            pl.BlockSpec(routes_shape, lambda i, p: (i + half, 0, 0)),
            whole((1, width)),
            whole(w_router.shape),
            whole((rows, rows)),
        ],
        [
            pl.BlockSpec((local_experts, 2, 1, CAPACITY, width), lambda i, p: (0, 0, i, 0, 0)),
            pl.BlockSpec((local_experts, 2, 1, CAPACITY, LANES), lambda i, p: (0, 0, i, 0, 0)),
            pl.BlockSpec((2, 1, 8, rows), lambda i, p: (0, i, 0, 0)),
            pl.BlockSpec((2, 1, 8, rows), lambda i, p: (0, i, 0, 0)),
            pl.BlockSpec((2, 1, rows, width), lambda i, p: (0, i, 0, 0)),
            whole((rows, width)),
            whole((padded, rows)),
        ],
        [
            struct(slot_shape + (width,), bf16),
            struct(slot_shape + (LANES,), f32),
            struct((2, half, 8, rows), f32),
            struct((2, half, 8, rows), f32),
            struct((2, half, rows, width), bf16),
            struct((rows, width), f32),
            struct((padded, rows), f32),
        ],
        scratch=[pltpu.VMEM((padded, rows), f32), pltpu.VMEM((padded, rows), f32)],
        us=0.5,
    )(place, att, att, w_mine, w_other, tokens, tokens, routes, routes, gain, w_router, after)


def grad_dispatch_kernel(rank_ref, gate_ref, cot_ref, g_ref):
    local_experts = g_ref.shape[0]
    rows = cot_ref.shape[0] // 2
    for half in range(2):
        hits = hits_of(rank_ref[half], local_experts)
        gate = gate_ref[half]
        slot_gate = jnp.concatenate(
            [jnp.sum(jnp.where(hit, gate[j : j + 1, :], 0.0), axis=1, keepdims=True) for j, hit in enumerate(hits)],
            axis=0,
        )
        grads = (dot(chosen_of(hits), cot_ref[half * rows : (half + 1) * rows, :]) * slot_gate).astype(bf16)
        for j in range(local_experts):
            g_ref[j, half] = grads[j * CAPACITY : (j + 1) * CAPACITY]


def grad_dispatch(rank, gate, cotangents, local_experts):
    members, _, rows = rank.shape
    width = cotangents.shape[1]
    small = pl.BlockSpec((2, 8, rows), lambda j: (j, 0, 0))
    return call(
        grad_dispatch_kernel,
        (members // 2,),
        0,
        [small, small, pl.BlockSpec((2 * rows, width), lambda j: (j, 0))],
        pl.BlockSpec((local_experts, 2, CAPACITY, width), lambda j: (0, j, 0, 0)),
        struct((local_experts, members, CAPACITY, width), bf16),
        us=0.5,
    )(rank, gate, cotangents)


def expert_kernel(
    x_ref, gate_ref, w_gate_ref, w_up_ref, w_down_ref, forth_ref, active_ref, factor_ref, silu_ref
):
    gate_pre = dot(x_ref[0], w_gate_ref[0])
    up_pre = dot(x_ref[0], w_up_ref[0])
    sig = 1.0 / (1.0 + jnp.exp(-gate_pre))
    silu = gate_pre * sig
    silu_ref[0] = silu
    factor_ref[0] = up_pre * sig * (1.0 + gate_pre * (1.0 - sig))
    active_ref[0] = (silu * up_pre).astype(bf16)
    produced = dot_nt(active_ref[0], w_down_ref[0]).astype(bf16).astype(f32)
    forth_ref[0] = (produced * gate_ref[0, :, 0:1]).astype(bf16)


def run_experts(x, slot_gate, w_gate, w_up, w_down):
    count, slots, width = x.shape
    hidden = w_gate.shape[2]

    def per_expert(*shape):
        return pl.BlockSpec((1,) + shape, lambda e: (e, 0, 0))

    return call(
        expert_kernel,
        (count,),
        0,
        [per_expert(slots, width), per_expert(slots, LANES)] + [per_expert(width, hidden)] * 3,
        [per_expert(slots, width)] + [per_expert(slots, hidden)] * 3,
        [
            struct((count, slots, width), bf16),
            struct((count, slots, hidden), bf16),
            struct((count, slots, hidden), f32),
            struct((count, slots, hidden), f32),
        ],
        us=0.5,
    )(x, slot_gate, w_gate, w_up, w_down)


def expert_back_kernel(place_ref, *refs, fast):
    x_ref, g_ref, active_ref, factor_ref, silu_ref = refs[:5]
    w_gate_ref, w_up_ref, w_down_ref, back_ref, dots_ref = refs[5:10]
    grads, (gate_low_ref, up_low_ref) = refs[10:-2], refs[-2:]
    slots, width = g_ref.shape[1], g_ref.shape[2]
    chunk = 256
    active_grad = dot(g_ref[0], w_down_ref[0])
    gate_low_ref[...] = (active_grad * factor_ref[0]).astype(bf16)
    up_low_ref[...] = (active_grad * silu_ref[0]).astype(bf16)
    dots = jnp.sum(active_ref[0].astype(f32) * active_grad, axis=1, keepdims=True)
    dots_ref[0] = jnp.broadcast_to(dots, (slots, LANES))
    back_ref[0] = (dot_nt(gate_low_ref[...], w_gate_ref[0]) + dot_nt(up_low_ref[...], w_up_ref[0])).astype(bf16)

    def products(cols):
        x = x_ref[0, :, cols]
        yield 0, dot_tn(x, gate_low_ref[...]).astype(bf16)
        yield 1, dot_tn(x, up_low_ref[...]).astype(bf16)
        yield 2, dot_tn(g_ref[0, :, cols], active_ref[0]).astype(bf16)

    if fast:
        write_shards(place_ref, grads, products, width)
    else:

        def whole_columns(index, carry):
            cols = pl.ds(pl.multiple_of(index * chunk, chunk), chunk)
            for which, product in products(cols):
                grads[which][0, cols, :] = product
            return carry

        lax.fori_loop(0, width // chunk, whole_columns, 0)


def write_shards(place_ref, outs, products, width):
    send_a, keep_a, send_b, keep_b = outs
    x_bit, y_bit = place_ref[3], place_ref[4]
    shard = width // 4
    for dy in range(2):
        for dx in range(2):
            x, y = x_bit ^ dx, y_bit ^ dy
            cols = pl.ds(pl.multiple_of((y * 2 + x) * shard, shard), shard)
            for which, product in products(cols):
                side = product.shape[1] // 2
                (send_a if dx else keep_a)[0, which, y] = product[:, :side]
                (send_b if dy else keep_b)[0, which, x] = product[:, side:]


def run_experts_back(place, x, g, active, factor, silu, w_gate, w_up, w_down, first, count, fast):
    slots, width = g.shape[1], g.shape[2]
    hidden = w_gate.shape[2]

    def taken(*shape):
        return pl.BlockSpec((1,) + shape, lambda e, p: (e + first, 0, 0))

    def given(*shape):
        zeros = (0,) * len(shape)
        return pl.BlockSpec((1,) + shape, lambda e, p: (e,) + zeros)

    if fast:
        grad_shapes = [(3, 2, width // 4, hidden // 2)] * 4
    else:
        grad_shapes = [(width, hidden)] * 3
    return call(
        lambda *refs: expert_back_kernel(*refs, fast=fast),
        (count,),
        1,
        [taken(slots, width)] * 2 + [taken(slots, hidden)] * 3 + [taken(width, hidden)] * 3,
        [given(slots, width), given(slots, LANES)] + [given(*shape) for shape in grad_shapes],
        [struct((count, slots, width), bf16), struct((count, slots, LANES), f32)]
        + [struct((count,) + shape, bf16) for shape in grad_shapes],
        scratch=[pltpu.VMEM((slots, hidden), bf16)] * 2,
        us=0.5,
    )(place, x, g, active, factor, silu, w_gate, w_up, w_down)


DOT_LANES = 2 * LANES


def combine_kernel(place_ref, rank_ref, *refs, pieces, with_dots, mine):
    parts, rest = refs[:pieces], refs[pieces:]
    rows = rank_ref.shape[2]
    local_experts = sum(part.shape[0] for part in parts)
    hits = hits_of(rank_ref[0], local_experts)
    gathered = jnp.concatenate([part[j, 0] for part in parts for j in range(part.shape[0])], axis=0)
    summed = dot_tn(chosen_of(hits), gathered)
    out_ref = rest[-1]
    if mine:
        arrived_ref = rest[-2]
        summed = summed + arrived_ref[0, 0:rows, :].astype(f32)
    out_ref[0, 0:rows, :] = summed.astype(bf16)
    if with_dots:
        column = [part[j, 0][:, 0:1] for part in rest[:pieces] for j in range(part.shape[0])]
        scattered = [
            jnp.sum(jnp.where(hit, value, 0.0), axis=0, keepdims=True) for hit, value in zip(hits, column)
        ]
        scattered.append(jnp.zeros((DOT_ROWS - local_experts, rows), f32))
        scattered = jnp.concatenate(scattered, axis=0)
        upper = scattered.astype(bf16)
        out_ref[0, rows:, :] = jnp.zeros((DOT_ROWS, out_ref.shape[2]), bf16)
        out_ref[0, rows:, 0:rows] = upper
        out_ref[0, rows:, DOT_LANES : DOT_LANES + rows] = (scattered - upper.astype(f32)).astype(bf16)
        if mine:
            out_ref[0, rows:, 2 * DOT_LANES : 4 * DOT_LANES] = arrived_ref[0, rows:, 0 : 2 * DOT_LANES]


def combine(place, rank, parts, dots=None, arrived=None):
    mine = arrived is not None
    rows, width = rank.shape[2], parts[0].shape[-1]
    out_rows = rows + (DOT_ROWS if dots else 0)

    def member(step, p):
        return (p[0] if mine else 1 - p[0]) * COLS + step

    def slots_of(array):
        return pl.BlockSpec((array.shape[0], 1) + array.shape[2:], lambda j, p: (0, member(j, p), 0, 0))

    inputs = [
        part.reshape(part.shape[0], 2 * COLS, CAPACITY, part.shape[-1]) for part in list(parts) + list(dots or [])
    ]
    in_specs = [pl.BlockSpec((1, 8, rows), lambda j, p: (member(j, p), 0, 0))] + [slots_of(item) for item in inputs]
    by_chip = pl.BlockSpec((1, out_rows, width), lambda j, p: (j, 0, 0))
    if mine:
        inputs.append(arrived)
        in_specs.append(by_chip)
    return call(
        lambda *refs: combine_kernel(*refs, pieces=len(parts), with_dots=bool(dots), mine=mine),
        (COLS,),
        1,
        in_specs,
        by_chip,
        struct((COLS, out_rows, width), bf16),
        us=0.5,
    )(place, rank, *inputs)


def split_dot(dimension_numbers, values, exact):
    upper = values.astype(bf16)
    lower = (values - upper.astype(f32)).astype(bf16)
    return lax.dot_general(
        upper, exact, dimension_numbers, preferred_element_type=f32
    ) + lax.dot_general(lower, exact, dimension_numbers, preferred_element_type=f32)


EXTRA_SLOTS = 6


def middle_back_kernel(
    place_ref, sums_ref, gates_ref, middle_ref, cot_ref, gain_ref, w_router_ref, w_mine_ref, w_other_ref,
    grad_ref, branch_ref, attended_ref, extra_ref
):
    rows = middle_ref.shape[0]
    tail = sums_ref[:, rows : rows + 8, 0 : 4 * DOT_LANES].astype(f32)
    mine = tail[:, :, 0:rows] + tail[:, :, DOT_LANES : DOT_LANES + rows]
    other = tail[:, :, 2 * DOT_LANES : 2 * DOT_LANES + rows] + tail[:, :, 3 * DOT_LANES : 3 * DOT_LANES + rows]
    first_row = place_ref[0] == 0
    dots = jnp.concatenate([jnp.where(first_row, mine, other), jnp.where(first_row, other, mine)], axis=0)
    dots = dots.reshape(dots.shape[0] * 8, rows)
    gates = gates_ref[...]
    logit_grad = dots - gates * jnp.sum(dots, axis=0, keepdims=True)
    middle = middle_ref[...]
    inverse = lax.rsqrt(jnp.mean(middle * middle, axis=1, keepdims=True) + epsilon)
    unit = middle * inverse
    gain = gain_ref[...]
    grad = sums_ref[0, 0:rows].astype(f32)
    for index in range(1, sums_ref.shape[0]):
        grad = grad + sums_ref[index, 0:rows].astype(f32)
    grad = grad + split_dot(TN, logit_grad, w_router_ref[...])
    gain_grad = jnp.sum(grad * unit, axis=0, keepdims=True)
    scaled = grad * gain
    middle_grad = cot_ref[...].astype(f32) + inverse * (
        scaled - unit * jnp.mean(scaled * unit, axis=1, keepdims=True)
    )
    grad_ref[...] = middle_grad
    branch_grad = middle_grad.astype(bf16)
    branch_ref[0:rows, :] = branch_grad
    extra_ref[...] = jnp.zeros_like(extra_ref)
    for index in range(logit_grad.shape[0] // 8):
        first, lane = index // EXTRA_SLOTS * 8, index % EXTRA_SLOTS * DOT_LANES
        extra_ref[first : first + 8, lane : lane + rows] = logit_grad[index * 8 : index * 8 + 8]
    upper = gain_grad.astype(bf16).astype(f32)
    extra_ref[13:14, :] = upper
    extra_ref[14:15, :] = gain_grad - upper
    branch_ref[rows:, :] = extra_ref[...].astype(bf16)
    for which, ref in enumerate((w_mine_ref, w_other_ref)):
        line = place_ref[0] if which == 0 else 1 - place_ref[0]
        for col in range(ref.shape[0]):
            product = dot_nt(branch_grad, ref[col])
            member = line * COLS + col
            attended_ref[member, :, 0:LANES] = product[:, 0:LANES].astype(bf16)
            attended_ref[member, :, LANES : LANES + HEAD_DIM] = product[:, LANES:].astype(bf16)
            attended_ref[member, :, LANES + HEAD_DIM :] = jnp.zeros((product.shape[0], HEAD_DIM), bf16)


def middle_back(place, sums, gates, middle, cotangent, gain, w_router, w_mine, w_other):
    rows, width = middle.shape
    members = 2 * COLS
    args = (sums, gates, middle, cotangent, gain, w_router, w_mine, w_other)
    return call(
        middle_back_kernel,
        (1,),
        1,
        [whole(item.shape) for item in args],
        [whole((rows, width)), whole((rows + DOT_ROWS, width)), whole((members, rows, 2 * LANES))],
        [
            struct((rows, width), f32),
            struct((rows + DOT_ROWS, width), bf16),
            struct((members, rows, 2 * LANES), bf16),
        ],
        scratch=[pltpu.VMEM((DOT_ROWS, width), f32)],
        us=0.5,
    )(place, *args)


def input_grad_kernel(
    place_ref, grads_mine_ref, grads_other_ref, mine_a_ref, mine_b_ref, other_a_ref, other_b_ref,
    tok_ref, middle_grad_ref, gain_ref, out_ref, sum_ref
):
    step = pl.program_id(0)
    first = place_ref[4] == 0

    def weights(a_ref, b_ref):
        a = jnp.concatenate([a_ref[index, 0] for index in range(a_ref.shape[0])], axis=0)
        b = jnp.concatenate([b_ref[index, 0] for index in range(b_ref.shape[0])], axis=0)
        upper, lower = jnp.where(first, a, b), jnp.where(first, b, a)
        return jnp.concatenate([upper, lower, lower[lower.shape[0] - HEAD_DIM :]], axis=0)

    part = dot(grads_mine_ref[0], weights(mine_a_ref, mine_b_ref))
    part = part + dot(grads_other_ref[0], weights(other_a_ref, other_b_ref))

    @pl.when(step == 0)
    def _():
        sum_ref[...] = part

    @pl.when(step > 0)
    def _():
        sum_ref[...] += part

    @pl.when(step == pl.num_programs(0) - 1)
    def _():
        resid = tok_ref[...].astype(f32)
        inverse = lax.rsqrt(jnp.mean(resid * resid, axis=1, keepdims=True) + epsilon)
        unit = resid * inverse
        scaled = sum_ref[...] * gain_ref[...]
        out_ref[...] = middle_grad_ref[...] + inverse * (
            scaled - unit * jnp.mean(scaled * unit, axis=1, keepdims=True)
        )


def input_grad(place, grads, weights, tokens, middle_grad, gain):
    rows, width = tokens.shape
    lanes = grads.shape[2]
    w_shape = (weights[0].shape[0], 1) + weights[0].shape[2:]
    return call(
        input_grad_kernel,
        (COLS,),
        1,
        [
            pl.BlockSpec((1, rows, lanes), lambda c, p: (p[0] * COLS + c, 0, 0)),
            pl.BlockSpec((1, rows, lanes), lambda c, p: ((1 - p[0]) * COLS + c, 0, 0)),
        ]
        + [pl.BlockSpec(w_shape, lambda c, p: (0, c, 0, 0))] * 4
        + [whole((rows, width)), whole((rows, width)), whole((1, width))],
        whole((rows, width)),
        struct((rows, width), f32),
        scratch=[pltpu.VMEM((rows, width), f32)],
        us=0.5,
    )(place, grads, grads, *weights, tokens, middle_grad, gain)


def own_weights_kernel(normed_ref, projected_ref, w_ref, gain_ref, out_ref, gain_grad_ref, sum_ref):
    step = pl.program_id(0)

    @pl.when(step == 0)
    def _():
        sum_ref[...] = jnp.zeros_like(sum_ref)

    sum_ref[...] += dot_tn(normed_ref[...], projected_ref[...])

    @pl.when(step == pl.num_programs(0) - 1)
    def _():
        total = sum_ref[...]
        out_ref[...] = total.astype(bf16)
        by_weight = jnp.sum(total * w_ref[...].astype(f32), axis=1, keepdims=True)
        gain_grad_ref[...] = jnp.broadcast_to(by_weight / gain_ref[...], gain_grad_ref.shape)


def own_weights(normed, projected, w_natural, gain):
    total, width = normed.shape
    lanes = projected.shape[1]
    rows = 512
    return call(
        own_weights_kernel,
        (total // rows,),
        0,
        [
            pl.BlockSpec((rows, width), lambda j: (j, 0)),
            pl.BlockSpec((rows, lanes), lambda j: (j, 0)),
            whole((width, lanes)),
            whole((width, 1)),
        ],
        [whole((width, lanes)), whole((width, 8))],
        [struct((width, lanes), bf16), struct((width, 8), f32)],
        scratch=[pltpu.VMEM((width, lanes), f32)],
        us=0.5,
    )(normed, projected, w_natural, gain)


def out_weights_kernel(place_ref, branch_ref, att_ref, normed_ref, own_ref, *refs, fast, local_experts):
    outs, small_ref, (sum_ref, gain_sum_ref) = refs[:-3], refs[-3], refs[-2:]
    step = pl.program_id(0)
    rows = att_ref.shape[0] // 2
    block = rows + DOT_ROWS

    @pl.when(step == 0)
    def _():
        sum_ref[...] = jnp.zeros_like(sum_ref)
        small_ref[...] = jnp.zeros_like(small_ref)
        gain_sum_ref[...] = jnp.zeros_like(gain_sum_ref)

    branch = jnp.concatenate([branch_ref[0:rows, :], branch_ref[block : block + rows, :]], axis=0)
    sum_ref[...] += dot_tn(branch, att_ref[...])
    for which in range(2):
        tail = branch_ref[which * block + rows : (which + 1) * block, :].astype(f32)
        slots = []
        for index in range(small_ref.shape[0] // 8):
            first, lane = index // EXTRA_SLOTS * 8, index % EXTRA_SLOTS * DOT_LANES
            slots.append(tail[first : first + 8, lane : lane + rows])
        logit_grad = jnp.concatenate(slots, axis=0)
        real = lax.broadcasted_iota(jnp.int32, logit_grad.shape, 0) % 8 < local_experts
        logit_grad = jnp.where(real, logit_grad, 0.0).astype(bf16)
        small_ref[...] += dot(logit_grad, normed_ref[which * rows : (which + 1) * rows, :])
        gain_sum_ref[...] += tail[8:16, :]

    @pl.when(step == pl.num_programs(0) - 1)
    def _():
        small_ref[7:8, :] = gain_sum_ref[5:6, :] + gain_sum_ref[6:7, :]

        def products(cols):
            own = own_ref[cols, 0 : 2 * LANES]
            out_one = sum_ref[cols, 0:LANES].astype(bf16)
            out_two = sum_ref[cols, LANES:]
            low = lane_of(out_two.shape) < HEAD_DIM
            tail = jnp.where(low, out_two, own_ref[cols, 2 * LANES :].astype(f32)).astype(bf16)
            yield 0, jnp.concatenate([own, out_one, tail], axis=1)

        if fast:
            write_shards(place_ref, outs, products, own_ref.shape[0])
        else:
            outs[0][...] = next(products(slice(0, own_ref.shape[0])))[1]


def out_weights(place, branch, attended, normed, own, padded, local_experts, fast):
    total, width = normed.shape
    rows = total // COLS
    blocks = branch.shape[0] // COLS
    if fast:
        shapes = [(1, 1, 2, width // 4, 2 * LANES)] * 4
    else:
        shapes = [(width, 4 * LANES)]
    return call(
        lambda *refs: out_weights_kernel(*refs, fast=fast, local_experts=local_experts),
        (COLS,),
        1,
        [
            pl.BlockSpec((blocks, width), lambda j, p: (j, 0)),
            pl.BlockSpec((rows, 2 * LANES), lambda j, p: (j, 0)),
            pl.BlockSpec((rows, width), lambda j, p: (j, 0)),
            whole(own.shape),
        ],
        [whole(shape) for shape in shapes] + [whole((padded, width))],
        [struct(shape, bf16) for shape in shapes] + [struct((padded, width), f32)],
        scratch=[pltpu.VMEM((width, 2 * LANES), f32), pltpu.VMEM((8, width), f32)],
        us=0.5,
    )(place, branch, attended, normed, own)


def first_sum_kernel(place_ref, keep_a_ref, got_a_ref, keep_b_ref, got_b_ref, *rest):
    send_a_ref, held_a_ref, send_b_ref, held_b_ref = rest[-4:]
    x_bit, y_bit = place_ref[3], place_ref[4]
    for bit, keep, got, send, held in (
        (y_bit, keep_a_ref, got_a_ref, send_a_ref, held_a_ref),
        (x_bit, keep_b_ref, got_b_ref, send_b_ref, held_b_ref),
    ):
        for kind in range(keep.shape[1]):
            held[0, kind] = (keep[0, kind, bit].astype(f32) + got[0, kind, bit].astype(f32)).astype(bf16)
            send[0, kind] = (keep[0, kind, 1 - bit].astype(f32) + got[0, kind, 1 - bit].astype(f32)).astype(bf16)


def first_sum(place, chunk, first=0, total=None, before=None):
    count, kinds, _, rows, cols = chunk[0].shape
    taken = pl.BlockSpec((1, kinds, 2, rows, cols), lambda e, p: (e, 0, 0, 0, 0))
    given = pl.BlockSpec((1, kinds, rows, cols), lambda e, p: (e + first, 0, 0, 0))
    extra = list(before) if before else []
    return call(
        first_sum_kernel,
        (count,),
        1,
        [taken] * 4 + [pl.BlockSpec(memory_space=pl.ANY)] * len(extra),
        [given] * 4,
        [struct((total or count, kinds, rows, cols), bf16)] * 4,
        us=0.5,
        aliases={5 + i: i for i in range(len(extra))},
    )(place, *chunk, *extra)


def last_sum_kernel(held_a_ref, got_a_ref, held_b_ref, got_b_ref, *rest):
    outs = rest[-3:]
    side = held_a_ref.shape[3]
    for which, out in enumerate(outs):
        out[0, :, :side] = held_a_ref[0, which].astype(f32) + got_a_ref[0, which].astype(f32)
        out[0, :, side:] = held_b_ref[0, which].astype(f32) + got_b_ref[0, which].astype(f32)


def last_sum(held_a, got_a, held_b, got_b, first, total, before):
    count, kinds, rows, cols = held_a.shape
    taken = pl.BlockSpec((1, kinds, rows, cols), lambda e: (e, 0, 0, 0))
    given = pl.BlockSpec((1, rows, 2 * cols), lambda e: (e + first, 0, 0))
    extra = list(before) if before else []
    return call(
        last_sum_kernel,
        (count,),
        0,
        [taken] * 4 + [pl.BlockSpec(memory_space=pl.ANY)] * len(extra),
        [given] * 3,
        [struct((total, rows, 2 * cols), f32)] * 3,
        us=0.5,
        aliases={4 + i: i for i in range(len(extra))},
    )(held_a, got_a, held_b, got_b, *extra)


def last_weights_kernel(held_a_ref, got_a_ref, held_b_ref, got_b_ref, query_ref, key_ref, value_ref, out_ref):
    left = held_a_ref[0, 0].astype(f32) + got_a_ref[0, 0].astype(f32)
    right = held_b_ref[0, 0].astype(f32) + got_b_ref[0, 0].astype(f32)
    cut = query_ref.shape[1]
    query_ref[...] = left[:, :cut]
    key_ref[...] = left[:, cut:]
    out_ref[...] = right[:, :cut]
    value_ref[...] = right[:, cut:]


def last_weights(parts, widths):
    rows = parts[0].shape[2]
    shapes = [(rows, width) for width in widths]
    return call(
        last_weights_kernel,
        (1,),
        0,
        [whole(part.shape) for part in parts],
        [whole(shape) for shape in shapes],
        [struct(shape, f32) for shape in shapes],
        us=0.5,
    )(*parts)


SWAP = [(0, 1), (1, 0)]


def after(value, *events):
    return lax.optimization_barrier((value,) + events)[0]


def gather_group(block):
    return lax.all_gather(block, ("row", "col"), axis=0, tiled=True)


def line_pieces(value):
    parts = [value]
    for distance in range(1, COLS):
        parts.insert(0, lax.ppermute(value, "col", [(i, (i + distance) % COLS) for i in range(COLS)]))
    return parts


def in_line_order(parts):
    parts = jnp.stack(parts + parts)
    return lax.dynamic_slice_in_dim(parts, COLS - 1 - lax.axis_index("col"), COLS, axis=0)


def flip(value, axis, bit, size):
    return lax.ppermute(value, axis, [(i, i ^ (1 << bit)) for i in range(size)])


def bits_of(size):
    return size.bit_length() - 1


def own_bit(axis, bit):
    return (lax.axis_index(axis) >> bit) & 1


def joined(mine, got, own):
    return jnp.where(own == 0, jnp.concatenate([mine, got]), jnp.concatenate([got, mine]))


def cube_step(value, axis, bit, size):
    return joined(value, flip(value, axis, bit, size), own_bit(axis, bit))


def lines_first(value):
    return jnp.transpose(value, (1, 0, 2, 3)).reshape(value.shape[1], value.shape[0] * value.shape[2], value.shape[3])


def cube_gather(value, axis, size):
    value = value[None]
    for bit in range(bits_of(size)):
        value = cube_step(value, axis, bit, size)
    return value


def sum_group(value, sizes):
    for axis, bit in (("row", 0), ("col", 0), ("col", 1)):
        value = value + flip(value, axis, bit, sizes[axis])
    return value


def sum_dp(value, sizes):
    for bit in range(bits_of(sizes["dp"])):
        value = value + flip(value, "dp", bit, sizes["dp"])
    return value


def reduce_over_dp(value, size):
    count = bits_of(size)
    value = value.reshape(value.shape[:1] + (2,) * count + value.shape[2:])
    current = value
    for bit in range(count - 1, -1, -1):
        own = own_bit("dp", bit)
        keep = lax.dynamic_index_in_dim(current, own, 1, keepdims=False)
        send = lax.dynamic_index_in_dim(current, 1 - own, 1, keepdims=False).astype(bf16)
        current = keep.astype(f32) + flip(send, "dp", bit, size).astype(f32)
    return current


def start_move(run, size):
    return flip(run[0], "dp", 0, size), flip(run[2], "dp", 1, size)


def second_move(sums, size):
    send_a, held_a, send_b, held_b = sums
    return held_a, flip(send_a, "dp", 1, size), held_b, flip(send_b, "dp", 0, size)


def layer(sizes):
    n_dp, n_row, n_col = sizes["dp"], sizes["row"], sizes["col"]
    members = n_row * n_col
    fast = n_dp == 4
    assert n_row == 2 and n_col == COLS and n_dp & (n_dp - 1) == 0

    def local(
        tokens, cotangent, routes, lengths, gain_attn, w_query, w_key, w_value, w_out,
        gain_moe, w_router, w_gate, w_up, w_down,
    ):
        rows, width = tokens.shape
        group = rows * members
        local_experts = w_gate.shape[0]
        row, col, dp = lax.axis_index("row"), lax.axis_index("col"), lax.axis_index("dp")
        place = jnp.stack([row, col, row * n_col + col, dp & 1, (dp >> 1) & 1]).astype(jnp.int32)
        gain_one = gain_attn.astype(f32)[None]
        gain_two = gain_moe.astype(f32)[None]

        tok_all = gather_group(tokens)
        w_in = jnp.concatenate([w_query.T, w_key.T, w_value.T], axis=0)
        out_share, in_share = rows // n_dp, w_in.shape[0] // n_dp
        shares = jnp.concatenate(
            [
                lax.dynamic_slice(w_out.T, (dp * out_share, 0), (out_share, width)),
                lax.dynamic_slice(w_in, (dp * in_share, 0), (in_share, width)),
                jnp.pad(routes.T.astype(bf16).reshape(1, TOP * rows), ((0, 7), (0, width - TOP * rows))),
            ],
            axis=0,
        )
        w_stack = jnp.concatenate([w_query.T, w_key.T, w_value.T, w_value.T], axis=0)
        w_natural = jnp.concatenate([w_query, w_key, w_value, w_value], axis=1)

        ends = jnp.cumsum(lengths[0])
        starts = ends - lengths[0]
        position = jnp.arange(group, dtype=jnp.int32)
        segment = jnp.sum((position[:, None] >= ends[None, :]).astype(jnp.int32), axis=1)
        member = segment[:, None] == jnp.arange(starts.shape[0], dtype=jnp.int32)[None, :]
        start = jnp.sum(jnp.where(member, starts[None, :], 0), axis=1).astype(jnp.int32)
        frequency = rope_base ** (-2.0 * jnp.arange(HEAD_DIM // 2, dtype=f32) / HEAD_DIM)
        angle = (position - start).astype(f32)[:, None] * frequency[None, :]
        cosine = jnp.tile(jnp.cos(angle), (1, 4))
        sine = jnp.tile(jnp.sin(angle), (1, 4))

        w_router_rows = w_router.T.reshape(members, local_experts, width)
        w_router_rows = jnp.pad(w_router_rows, ((0, 0), (0, 8 - local_experts), (0, 0)))
        w_router_rows = w_router_rows.reshape(members * 8, width)
        start_row = jnp.broadcast_to(start[None, :], (8, group))
        start = start[:, None]
        gain_column = gain_attn.astype(f32)[:, None]
        ready = (place, gain_one, gain_two, w_stack, w_natural, cosine, sine, w_router_rows, start, start_row, gain_column)
        shares, place, gain_one, gain_two, w_stack, w_natural, cosine, sine, w_router_rows, start, start_row, gain_column = (
            lax.optimization_barrier((shares,) + ready)
        )
        shares = line_pieces(after(shares, tok_all, cosine))

        query, key, value, normed_one = project(tok_all, gain_one, w_stack, cosine, sine)
        packed, attended, totals = attend(query, key, value, start)
        att_flat = gather_group(packed)
        att_all = att_flat.reshape((n_row, n_col) + packed.shape)
        shares = in_line_order(after(shares, packed))
        route_rows = shares[:, out_share + in_share]
        w_out_mine, in_part = shares[None, :, :out_share], shares[None, :, out_share : out_share + in_share]
        for bit in range(bits_of(n_dp)):
            w_out_mine = cube_step(w_out_mine, "dp", bit, n_dp)
        in_part = cube_step(in_part, "dp", 0, n_dp)
        w_out_mine = lines_first(w_out_mine)
        w_out_other = lax.ppermute(after(w_out_mine, in_part), "row", SWAP)
        route_rows = cube_gather(route_rows, "row", n_row)[:, :, : TOP * rows].reshape(members, TOP, rows)
        cot_all = gather_group(after(cotangent, w_out_other))
        x, slot_gate, rank, gate, normed_two, middle, gates = middle_and_dispatch(
            place, att_all, w_out_mine, w_out_other, tok_all, route_rows, gain_two, w_router_rows, local_experts
        )
        slots = members * CAPACITY
        x = x.reshape(local_experts, slots, width)
        slot_gate = slot_gate.reshape(local_experts, slots, LANES)
        rank, gate = rank.reshape(members, 8, rows), gate.reshape(members, 8, rows)
        forth, active, factor, silu = run_experts(x, slot_gate, w_gate, w_up, w_down)
        for bit in range(1, bits_of(n_dp) - 1):
            in_part = cube_step(in_part, "dp", bit, n_dp)
        last_bit = bits_of(n_dp) - 1
        in_got = after(flip(in_part, "dp", last_bit, n_dp), forth)
        forth_other = combine(place, after(rank, in_got), [forth])
        arrived = lax.ppermute(forth_other, "row", SWAP)
        g = grad_dispatch(after(rank, forth_other), gate, cot_all, local_experts)
        g = g.reshape(local_experts, slots, width)
        cuts = [0, 1, 2, 4, local_experts]

        def backward(which, x):
            first, last = cuts[which], cuts[which + 1]
            return run_experts_back(place, x, g, active, factor, silu, w_gate, w_up, w_down, first, last - first, fast)

        runs = [backward(0, x)]
        forth_mine = combine(place, rank, [forth], arrived=after(arrived, runs[0][1]))
        forth_sums = lax.all_to_all(forth_mine, "col", 0, 0, tiled=True)
        runs.append(backward(1, after(x, forth_mine)))
        runs.append(backward(2, after(x, runs[1][1])))
        moved = [start_move(run[2:], n_dp) for run in runs] if fast else []
        runs.append(backward(3, after(x, runs[2][1], *(moved[0] if fast else ()))))
        if fast:
            moved.append(start_move(runs[3][2:], n_dp))
        back_parts, dot_parts = [run[0] for run in runs], [run[1] for run in runs]
        back_other = combine(place, after(rank, *moved[1]) if fast else rank, back_parts, dot_parts)
        arrived = lax.ppermute(back_other, "row", SWAP)
        back_mine = combine(place, rank, back_parts, dot_parts, arrived)
        back_mine = after(back_mine, forth_sums)
        back_sums = lax.all_to_all(back_mine, "col", 0, 0, tiled=True)

        if fast:
            w_in_parts = [in_part, in_got]
        else:
            own = own_bit("dp", last_bit)
            w_in_rows = lines_first(joined(in_part, in_got, own))[None]
            half = w_in_rows.shape[2] // 2
            upper, lower = w_in_rows[:, :, :half], w_in_rows[:, :, half:]
            w_in_parts = [jnp.where(place[4] == 0, upper, lower), jnp.where(place[4] == 0, lower, upper)]
        if fast:

            def chunk_of(which, event):
                keep_a, keep_b = after((runs[which][3], runs[which][5]), event)
                return keep_a, moved[which][0], keep_b, moved[which][1]

            sums = first_sum(place, chunk_of(0, back_mine), cuts[0], cuts[3])
            sums = first_sum(place, chunk_of(1, back_mine), cuts[1], cuts[3], sums)
            gate_middle = (sums[1],) + moved[2]
        else:
            gate_middle = ()
        w_in_parts += [lax.ppermute(after(part, back_mine), "row", SWAP) for part in w_in_parts]

        middle_grad, branch_grad, attended_grad = middle_back(
            place, back_sums, gates, middle, cotangent, after(gain_two, *w_in_parts[2:], *gate_middle),
            w_router_rows, w_out_mine, w_out_other,
        )
        if fast:
            sums = first_sum(place, chunk_of(2, branch_grad), cuts[2], cuts[3], sums)
            started = [second_move(sums, n_dp)]
        attended_grad = lax.all_to_all(attended_grad, ("row", "col"), 0, 0, tiled=True)
        if fast:
            attended_grad = after(attended_grad, sums[1])
        branch_all = gather_group(after(branch_grad, attended_grad))

        attended_grad = attended_grad.reshape(group, 2 * LANES)
        projected_grad = attend_back(query, key, value, attended_grad, totals, start_row, cosine, sine)
        projected_all = lax.all_to_all(
            projected_grad.reshape(members, rows, 3 * LANES), ("row", "col"), 0, 0, tiled=True
        )
        own_grads, gain_part = own_weights(
            after(normed_one, *moved[3]) if fast else normed_one,
            projected_grad, w_natural, gain_column,
        )
        if fast:
            started.append(second_move(first_sum(place, chunk_of(3, own_grads)), n_dp))
            normed_two = after(normed_two, started[1][0])
        gain_row = gain_part[:, 0].reshape(8, width // 8)
        gain_row = gain_row + flip(gain_row, "row", 0, n_row)
        *w_parts, small = out_weights(
            place, branch_all, attended, after(normed_two, gain_row).reshape(group, width), own_grads,
            members * 8, local_experts, fast,
        )
        gain_row = gain_row + flip(gain_row, "col", 0, n_col)
        expert_grads = None
        if fast:
            w_moved = start_move(w_parts, n_dp)
            held_a, got_a, held_b, got_b = started[0]
            held_a, held_b = after((held_a, held_b), gain_row, small)
            expert_grads = last_sum(held_a, got_a, held_b, got_b, 0, local_experts, None)
            gain_row = after(gain_row, expert_grads[0])
        else:
            cut = w_parts[0].reshape(1, n_dp, width // n_dp, w_parts[0].shape[1])
            w_sum = reduce_over_dp(cut, n_dp)[0]
        gain_attn_grad = gain_row + flip(gain_row, "col", 1, n_col)

        mixed = (middle + jnp.sum(after(forth_sums, projected_grad).astype(f32), axis=0)).astype(bf16)

        used = small.reshape(members, 8, width)[:, :local_experts].reshape(members * local_experts, width)
        both = jnp.concatenate([used, small[7:8], gain_attn_grad.reshape(1, width)], axis=0)
        both = sum_dp(both, sizes)
        w_router_grad = both[: members * local_experts].T
        gain_moe_grad, gain_attn_grad = both[members * local_experts], both[members * local_experts + 1]

        tokens_grad = input_grad(
            place, projected_all, w_in_parts, tokens, middle_grad, after(gain_one, w_parts[0], gain_attn_grad)
        )

        local_q, local_k = w_query.shape[1], w_key.shape[1]
        if fast:
            expert_grads = last_sum(*started[1], cuts[3], local_experts, expert_grads)
            w_sums = second_move(
                first_sum(place, (w_parts[1], w_moved[0], w_parts[3], w_moved[1])), n_dp
            )
            w_query_grad, w_key_grad, w_value_grad, w_out_grad = last_weights(
                w_sums, (local_q, local_k, local_k, local_q)
            )
        else:
            expert_grads = []
            for which in range(3):
                parts = [run[2 + which] for run in runs]
                parts = [part.reshape(part.shape[0], n_dp, width // n_dp, part.shape[2]) for part in parts]
                expert_grads.append(jnp.concatenate([reduce_over_dp(part, n_dp) for part in parts], axis=0))
            cut = local_q + local_k
            w_query_grad, w_key_grad = w_sum[:, :local_q], w_sum[:, local_q:cut]
            w_out_grad, w_value_grad = w_sum[:, cut : cut + local_q], w_sum[:, cut + local_q :]
        w_gate_grad, w_up_grad, w_down_grad = expert_grads
        return (
            mixed, tokens_grad, gain_attn_grad, w_query_grad, w_key_grad, w_value_grad, w_out_grad,
            gain_moe_grad, w_router_grad, w_gate_grad, w_up_grad, w_down_grad,
        )

    return local


def solution(mesh):
    return jax.shard_map(
        layer(dict(mesh.shape)),
        mesh=mesh,
        in_specs=(
            P(("dp", "row", "col"), None),
            P(("dp", "row", "col"), None),
            P(("dp", "row", "col"), None),
            P("dp", None),
            P(),
            P(None, ("row", "col")),
            P(None, ("row", "col")),
            P(None, ("row", "col")),
            P(None, ("row", "col")),
            P(),
            P(),
            P(("row", "col"), None, None),
            P(("row", "col"), None, None),
            P(("row", "col"), None, None),
        ),
        out_specs=(
            P(("dp", "row", "col"), None),
            P(("dp", "row", "col"), None),
            P(),
            P("dp", ("row", "col")),
            P("dp", ("row", "col")),
            P("dp", ("row", "col")),
            P("dp", ("row", "col")),
            P(),
            P(),
            P(("row", "col"), "dp", None),
            P(("row", "col"), "dp", None),
            P(("row", "col"), "dp", None),
        ),
        check_vma=False,
    )
```

```python
import math

import jax
import jax.numpy as jnp
import numpy as np
from jax import lax
from jax.experimental import pallas as pl
from jax.experimental.pallas import tpu as pltpu
from jax.sharding import PartitionSpec as P

HEAD_DIM = 64
EXPERTS = 40
TOP = 8
CAPACITY = 64
COLS = 4
LANES = 128
QUERY_BLOCK = 256
DOT_ROWS = 16

epsilon = 1e-06
rope_base = 10000.0
masked_score = -1e30
f32 = jnp.float32
bf16 = jnp.bfloat16
VMEM_LIMIT = 56 * 1024 * 1024

NT = (((1,), (1,)), ((), ()))
TN = (((0,), (0,)), ((), ()))


def dot(a, b):
    return jnp.dot(a, b, preferred_element_type=f32)


def dot_nt(a, b):
    return lax.dot_general(a, b, NT, preferred_element_type=f32)


def dot_tn(a, b):
    return lax.dot_general(a, b, TN, preferred_element_type=f32)


def lane_of(shape):
    return lax.broadcasted_iota(jnp.int32, shape, len(shape) - 1)


def call(
    kernel, grid, prefetch, in_specs, out_specs, out_shape, scratch=(), us=1.0, aliases=None
):
    return pl.pallas_call(
        kernel,
        grid_spec=pltpu.PrefetchScalarGridSpec(
            num_scalar_prefetch=prefetch,
            grid=grid,
            in_specs=in_specs,
            out_specs=out_specs,
            scratch_shapes=list(scratch),
        ),
        out_shape=out_shape,
        input_output_aliases=aliases or {},
        compiler_params=pltpu.CompilerParams(
            vmem_limit_bytes=VMEM_LIMIT, dimension_semantics=("arbitrary",) * len(grid)
        ),
        cost_estimate=pl.CostEstimate(
            flops=int(us * 1.1e9), bytes_accessed=int(us * 3.6e6), transcendentals=0
        ),
    )


def whole(shape):
    zeros = (0,) * len(shape)
    return pl.BlockSpec(shape, lambda *_: zeros)


def struct(shape, dtype):
    return jax.ShapeDtypeStruct(shape, dtype)


def turn_within_heads(values, sign):
    lane = lane_of(values.shape) % HEAD_DIM
    ahead = pltpu.roll(values, LANES - HEAD_DIM // 2, 1)
    behind = pltpu.roll(values, HEAD_DIM // 2, 1)
    return jnp.where(lane < HEAD_DIM // 2, -sign * ahead, sign * behind)


def project_kernel(
    tok_ref, gain_ref, w_ref, cos_ref, sin_ref, query_ref, key_ref, value_ref, normed_ref
):
    resid = tok_ref[...].astype(f32)
    inverse = lax.rsqrt(jnp.mean(resid * resid, axis=1, keepdims=True) + epsilon)
    normed = (resid * inverse * gain_ref[...]).astype(bf16)
    normed_ref[...] = normed
    raw = dot_nt(normed, w_ref[...])
    cosine, sine = cos_ref[...], sin_ref[...]

    def rot(values):
        return (values * cosine + turn_within_heads(values, 1.0) * sine).astype(bf16).astype(f32)

    first = rot(raw[:, :LANES])
    second = rot(raw[:, LANES : 2 * LANES])
    low = lane_of(first.shape) < HEAD_DIM
    scale = 1.0 / math.sqrt(HEAD_DIM)
    query_ref[0] = jnp.where(low, first * scale, 0.0).astype(bf16)
    query_ref[1] = jnp.where(low, 0.0, first * scale).astype(bf16)
    query_ref[2] = jnp.where(low, second * scale, 0.0).astype(bf16)
    key_ref[...] = jnp.where(low, pltpu.roll(second, HEAD_DIM, 1), second).astype(bf16)
    value_ref[...] = raw[:, 2 * LANES :].astype(bf16)


def project(tokens, gain, w_stack, cosine, sine):
    total, width = tokens.shape
    rows = 512
    lanes = pl.BlockSpec((rows, LANES), lambda j: (j, 0))
    wide = pl.BlockSpec((rows, width), lambda j: (j, 0))
    return call(
        project_kernel,
        (total // rows,),
        0,
        [wide, whole((1, width)), whole(w_stack.shape), lanes, lanes],
        [pl.BlockSpec((3, rows, LANES), lambda j: (0, j, 0)), lanes, lanes, wide],
        [
            struct((3, total, LANES), bf16),
            struct((total, LANES), bf16),
            struct((total, LANES), bf16),
            struct((total, width), bf16),
        ],
        us=0.5,
    )(tokens, gain, w_stack, cosine, sine)


def attend_kernel(query_ref, key_ref, value_ref, start_ref, packed_ref, plain_ref, total_ref, out_ref):
    blocks = query_ref.shape[1] // QUERY_BLOCK
    block = pl.program_id(0)
    for index in range(blocks):

        @pl.when(block == index)
        def _(index=index):
            rows = pl.ds(index * QUERY_BLOCK, QUERY_BLOCK)
            span = (index + 1) * QUERY_BLOCK
            row = index * QUERY_BLOCK + lax.broadcasted_iota(jnp.int32, (QUERY_BLOCK, span), 0)
            column = lane_of((QUERY_BLOCK, span))
            allowed = (column <= row) & (column >= start_ref[rows, :])

            def head(number, carry):
                scores = dot_nt(query_ref[number, rows, :], key_ref[0:span, :])
                scores = jnp.where(allowed, scores, masked_score)
                peak = jnp.max(scores, axis=1, keepdims=True)
                weights = jnp.exp(scores - peak)
                summed = jnp.sum(weights, axis=1, keepdims=True)
                probs = (weights * (1.0 / summed)).astype(bf16)
                out_ref[number] = dot(probs, value_ref[0:span, :])
                total = jnp.broadcast_to(peak + jnp.log(summed), (QUERY_BLOCK, LANES))
                total_ref[number, :, rows] = jnp.transpose(total)[0:8, :]
                return carry

            lax.fori_loop(0, 3, head, 0)
            low = lane_of((QUERY_BLOCK, LANES)) < HEAD_DIM
            one, two, three = out_ref[0], out_ref[1], out_ref[2]
            pair = jnp.where(low, one, two).astype(bf16)
            plain_ref[rows, 0:LANES] = pair
            plain_ref[rows, LANES : 2 * LANES] = jnp.where(low, three, 0.0).astype(bf16)
            if index < blocks // 2:
                packed_ref[rows, 0:LANES] = pair
                packed_ref[rows, LANES : 2 * LANES] = three.astype(bf16)
            else:
                back = pl.ds((index - blocks // 2) * QUERY_BLOCK, QUERY_BLOCK)
                before = packed_ref[back, LANES : 2 * LANES].astype(f32)
                packed_ref[back, LANES : 2 * LANES] = jnp.where(low, before, one).astype(bf16)
                packed_ref[back, 2 * LANES : 3 * LANES] = jnp.where(low, two, three).astype(bf16)


def attend(query, key, value, start):
    total = key.shape[0]
    return call(
        attend_kernel,
        (total // QUERY_BLOCK,),
        0,
        [whole(query.shape), whole(key.shape), whole(value.shape), whole(start.shape)],
        [whole((total // 2, 3 * LANES)), whole((total, 2 * LANES)), whole((3, 8, total))],
        [
            struct((total // 2, 3 * LANES), bf16),
            struct((total, 2 * LANES), bf16),
            struct((3, 8, total), f32),
        ],
        scratch=[pltpu.VMEM((3, QUERY_BLOCK, LANES), f32)],
        us=0.5,
    )(query, key, value, start)


def attend_back_kernel(
    query_ref, key_ref, value_ref, grad_ref, total_ref, start_ref, cos_ref, sin_ref,
    out_ref, query_grad_ref, key_grad_ref, value_grad_ref
):
    blocks = query_ref.shape[1] // QUERY_BLOCK
    block = pl.program_id(0)
    scale = 1.0 / math.sqrt(HEAD_DIM)

    @pl.when(block == 0)
    def _():
        key_grad_ref[...] = jnp.zeros_like(key_grad_ref)
        value_grad_ref[...] = jnp.zeros_like(value_grad_ref)

    def back(values, cosine, sine):
        return values * cosine + turn_within_heads(values * sine, -1.0)

    for index in range(blocks):

        @pl.when(block == index)
        def _(index=index):
            rows = pl.ds(index * QUERY_BLOCK, QUERY_BLOCK)
            span = (index + 1) * QUERY_BLOCK
            row = index * QUERY_BLOCK + lane_of((span, QUERY_BLOCK))
            column = lax.broadcasted_iota(jnp.int32, (span, QUERY_BLOCK), 0)
            allowed = (column <= row) & (column >= start_ref[0:1, rows])
            low = lane_of((QUERY_BLOCK, LANES)) < HEAD_DIM

            def head(number, carry):
                query = query_ref[number, rows, :]
                tile = pl.multiple_of((number // 2) * LANES, LANES)
                upstream = grad_ref[rows, pl.ds(tile, LANES)].astype(f32)
                keep = low == (number != 1)
                upstream = jnp.where(keep, upstream, 0.0).astype(bf16)
                scores = dot_nt(key_ref[0:span, :], query)
                probs = jnp.exp(scores - total_ref[number, 0:1, rows])
                probs = jnp.where(allowed, probs, 0.0)
                prob_grad = dot_nt(value_ref[0:span, :], upstream)
                row_dot = jnp.sum(probs * prob_grad, axis=0, keepdims=True)
                score_grad = (probs * (prob_grad - row_dot)).astype(bf16)
                key_grad_ref[0:span, :] += dot(score_grad, query)
                value_grad_ref[0:span, :] += dot(probs.astype(bf16), upstream)
                query_grad_ref[number] = dot_tn(score_grad, key_ref[0:span, :]) * scale
                return carry

            lax.fori_loop(0, 3, head, 0)
            cosine, sine = cos_ref[rows, :], sin_ref[rows, :]
            pair = jnp.where(low, query_grad_ref[0], query_grad_ref[1])
            out_ref[rows, 0:LANES] = back(pair, cosine, sine).astype(bf16)
            out_ref[rows, LANES : 2 * LANES] = back(query_grad_ref[2], cosine, sine).astype(bf16)

    @pl.when(block == blocks - 1)
    def _():
        low = lane_of(key_grad_ref.shape) < HEAD_DIM
        key_grad = key_grad_ref[...]
        key_grad = key_grad + pltpu.roll(key_grad, HEAD_DIM, 1)
        key_grad = back(key_grad, cos_ref[...], sin_ref[...])
        before = out_ref[:, LANES : 2 * LANES].astype(f32)
        out_ref[:, LANES : 2 * LANES] = jnp.where(low, before, key_grad).astype(bf16)
        value_grad = value_grad_ref[...]
        value_grad = value_grad + pltpu.roll(value_grad, HEAD_DIM, 1)
        out_ref[:, 2 * LANES : 3 * LANES] = jnp.where(low, 0.0, value_grad).astype(bf16)


def attend_back(query, key, value, grad, totals, start, cosine, sine):
    total = key.shape[0]
    args = (query, key, value, grad, totals, start, cosine, sine)
    return call(
        attend_back_kernel,
        (total // QUERY_BLOCK,),
        0,
        [whole(item.shape) for item in args],
        whole((total, 3 * LANES)),
        struct((total, 3 * LANES), bf16),
        scratch=[
            pltpu.VMEM((3, QUERY_BLOCK, LANES), f32),
            pltpu.VMEM((total, LANES), f32),
            pltpu.VMEM((total, LANES), f32),
        ],
        us=0.5,
    )(*args)


def branch_operand(refs):
    rows = refs.shape[2]
    low = lane_of((rows, LANES)) < HEAD_DIM
    pairs, thirds = [], []
    for member in range(refs.shape[1]):
        one = refs[0, member, :, 0:LANES]
        mid = refs[0, member, :, LANES : 2 * LANES].astype(f32)
        end = refs[0, member, :, 2 * LANES : 3 * LANES].astype(f32)
        mid_turned = pltpu.roll(mid, HEAD_DIM, 1)
        end_turned = pltpu.roll(end, HEAD_DIM, 1)
        late = jnp.where(low, mid_turned, end_turned).astype(bf16)
        pairs.append(jnp.concatenate([one, late], axis=0))
        thirds.append((mid, end_turned))
    for member in range(0, refs.shape[1], 2):
        tops = []
        for which in range(2):
            left, right = thirds[member][which], thirds[member + 1][which]
            tops.append(jnp.where(low, left, pltpu.roll(right, HEAD_DIM, 1)).astype(bf16))
        pairs.append(jnp.concatenate(tops, axis=0))
    return jnp.concatenate(pairs, axis=1)


def branch_weights(ref):
    right = [ref[source, 0:LANES] for source in range(ref.shape[0])]
    return jnp.concatenate(right + [ref[source, LANES:] for source in range(ref.shape[0])], axis=0)


def hits_of(rank, local_experts):
    place = lax.broadcasted_iota(jnp.int32, (CAPACITY, rank.shape[1]), 0).astype(f32)
    return [place == rank[j : j + 1, :] for j in range(local_experts)]


def chosen_of(hits):
    return jnp.concatenate([jnp.where(hit, 1.0, 0.0).astype(bf16) for hit in hits], axis=0)


def middle_kernel(
    place_ref, att_mine_ref, att_other_ref, w_mine_ref, w_other_ref, tok_a_ref, tok_b_ref, routes_a_ref, routes_b_ref,
    gain_ref, w_router_ref, after_ref,
    x_ref, slot_gate_ref, rank_ref, gate_ref, normed_ref, middle_ref, gates_own_ref, gates_ref, ranks_ref
):
    step = pl.program_id(0)
    member = place_ref[2]
    cols = pl.num_programs(0)
    rows = tok_a_ref.shape[0]
    local_experts = x_ref.shape[0]
    branch = dot(branch_operand(att_mine_ref), branch_weights(w_mine_ref))
    branch = branch + dot(branch_operand(att_other_ref), branch_weights(w_other_ref))
    for half in range(2):
        tok_ref, routes_ref = ((tok_a_ref, routes_a_ref), (tok_b_ref, routes_b_ref))[half]
        middle = tok_ref[...].astype(f32) + branch[half * rows : (half + 1) * rows]
        inverse = lax.rsqrt(jnp.mean(middle * middle, axis=1, keepdims=True) + epsilon)
        normed = (middle * inverse * gain_ref[...]).astype(bf16)
        normed_ref[half, 0] = normed
        logits = dot_nt(w_router_ref[...], normed)
        padded = logits.shape[0]
        slot = lax.broadcasted_iota(jnp.int32, (padded, rows), 0)
        expert = (slot // 8) * local_experts + slot % 8
        expert = jnp.where(slot % 8 < local_experts, expert, -1).astype(f32)
        routes = routes_ref[0].astype(f32)
        named = expert == routes[0:1, 0:rows]
        for k in range(1, TOP):
            named = named | (expert == routes[k : k + 1, 0:rows])
        peak = jnp.max(jnp.where(named, logits, masked_score), axis=0, keepdims=True)
        weights = jnp.where(named, jnp.exp(logits - peak), 0.0)
        gates = weights / jnp.sum(weights, axis=0, keepdims=True)
        gates_ref[...] = gates
        ranks_ref[...] = jnp.where(named, dot(named.astype(f32).astype(bf16), after_ref[...]), -1.0)
        here = pl.ds(pl.multiple_of(member * 8, 8), 8)
        gate, rank = gates_ref[here, :], ranks_ref[here, :]
        rank_ref[half, 0] = rank
        gate_ref[half, 0] = gate
        hits = hits_of(rank, local_experts)
        slot_gate = jnp.concatenate(
            [jnp.sum(jnp.where(hit, gate[j : j + 1, :], 0.0), axis=1, keepdims=True) for j, hit in enumerate(hits)],
            axis=0,
        )
        chosen = chosen_of(hits)
        picked = dot(chosen, normed).astype(bf16)
        spread = jnp.broadcast_to(slot_gate, (slot_gate.shape[0], LANES))
        for j in range(local_experts):
            part = slice(j * CAPACITY, (j + 1) * CAPACITY)
            x_ref[j, half, 0] = picked[part]
            slot_gate_ref[j, half, 0] = spread[part]

        @pl.when(member == half * cols + step)
        def _(middle=middle, gates=gates):
            middle_ref[...] = middle
            gates_own_ref[...] = gates


def middle_and_dispatch(place, att, w_mine, w_other, tokens, routes, gain, w_router, local_experts):
    width = tokens.shape[1]
    half = COLS
    rows = tokens.shape[0] // (2 * half)
    padded = w_router.shape[0]
    after = jnp.asarray(np.triu(np.ones((rows, rows), np.float32), 1), bf16)
    slot_shape = (local_experts, 2, half, CAPACITY)
    early = pl.BlockSpec((rows, width), lambda i, p: (i, 0))
    late = pl.BlockSpec((rows, width), lambda i, p: (i + half, 0))
    routes_shape = (1,) + routes.shape[1:]
    return call(
        middle_kernel,
        (half,),
        1,
        [
            pl.BlockSpec((1, half, rows, 3 * LANES), lambda i, p: (p[0], 0, i, 0)),
            pl.BlockSpec((1, half, rows, 3 * LANES), lambda i, p: (1 - p[0], 0, i, 0)),
            whole(w_mine.shape),
            whole(w_other.shape),
            early,
            late,
            pl.BlockSpec(routes_shape, lambda i, p: (i, 0, 0)),
            pl.BlockSpec(routes_shape, lambda i, p: (i + half, 0, 0)),
            whole((1, width)),
            whole(w_router.shape),
            whole((rows, rows)),
        ],
        [
            pl.BlockSpec((local_experts, 2, 1, CAPACITY, width), lambda i, p: (0, 0, i, 0, 0)),
            pl.BlockSpec((local_experts, 2, 1, CAPACITY, LANES), lambda i, p: (0, 0, i, 0, 0)),
            pl.BlockSpec((2, 1, 8, rows), lambda i, p: (0, i, 0, 0)),
            pl.BlockSpec((2, 1, 8, rows), lambda i, p: (0, i, 0, 0)),
            pl.BlockSpec((2, 1, rows, width), lambda i, p: (0, i, 0, 0)),
            whole((rows, width)),
            whole((padded, rows)),
        ],
        [
            struct(slot_shape + (width,), bf16),
            struct(slot_shape + (LANES,), f32),
            struct((2, half, 8, rows), f32),
            struct((2, half, 8, rows), f32),
            struct((2, half, rows, width), bf16),
            struct((rows, width), f32),
            struct((padded, rows), f32),
        ],
        scratch=[pltpu.VMEM((padded, rows), f32), pltpu.VMEM((padded, rows), f32)],
        us=0.5,
    )(place, att, att, w_mine, w_other, tokens, tokens, routes, routes, gain, w_router, after)


def grad_dispatch_kernel(rank_ref, gate_ref, cot_ref, g_ref):
    local_experts = g_ref.shape[0]
    rows = cot_ref.shape[0] // 2
    for half in range(2):
        hits = hits_of(rank_ref[half], local_experts)
        gate = gate_ref[half]
        slot_gate = jnp.concatenate(
            [jnp.sum(jnp.where(hit, gate[j : j + 1, :], 0.0), axis=1, keepdims=True) for j, hit in enumerate(hits)],
            axis=0,
        )
        grads = (dot(chosen_of(hits), cot_ref[half * rows : (half + 1) * rows, :]) * slot_gate).astype(bf16)
        for j in range(local_experts):
            g_ref[j, half] = grads[j * CAPACITY : (j + 1) * CAPACITY]


def grad_dispatch(rank, gate, cotangents, local_experts):
    members, _, rows = rank.shape
    width = cotangents.shape[1]
    small = pl.BlockSpec((2, 8, rows), lambda j: (j, 0, 0))
    return call(
        grad_dispatch_kernel,
        (members // 2,),
        0,
        [small, small, pl.BlockSpec((2 * rows, width), lambda j: (j, 0))],
        pl.BlockSpec((local_experts, 2, CAPACITY, width), lambda j: (0, j, 0, 0)),
        struct((local_experts, members, CAPACITY, width), bf16),
        us=0.5,
    )(rank, gate, cotangents)


def expert_kernel(
    x_ref, gate_ref, w_gate_ref, w_up_ref, w_down_ref, forth_ref, active_ref, factor_ref, silu_ref
):
    gate_pre = dot(x_ref[0], w_gate_ref[0])
    up_pre = dot(x_ref[0], w_up_ref[0])
    sig = 1.0 / (1.0 + jnp.exp(-gate_pre))
    silu = gate_pre * sig
    silu_ref[0] = silu
    factor_ref[0] = up_pre * sig * (1.0 + gate_pre * (1.0 - sig))
    active_ref[0] = (silu * up_pre).astype(bf16)
    produced = dot_nt(active_ref[0], w_down_ref[0]).astype(bf16).astype(f32)
    forth_ref[0] = (produced * gate_ref[0, :, 0:1]).astype(bf16)


def run_experts(x, slot_gate, w_gate, w_up, w_down):
    count, slots, width = x.shape
    hidden = w_gate.shape[2]

    def per_expert(*shape):
        return pl.BlockSpec((1,) + shape, lambda e: (e, 0, 0))

    return call(
        expert_kernel,
        (count,),
        0,
        [per_expert(slots, width), per_expert(slots, LANES)] + [per_expert(width, hidden)] * 3,
        [per_expert(slots, width)] + [per_expert(slots, hidden)] * 3,
        [
            struct((count, slots, width), bf16),
            struct((count, slots, hidden), bf16),
            struct((count, slots, hidden), f32),
            struct((count, slots, hidden), f32),
        ],
        us=0.5,
    )(x, slot_gate, w_gate, w_up, w_down)


def expert_back_kernel(place_ref, *refs, fast):
    x_ref, g_ref, active_ref, factor_ref, silu_ref = refs[:5]
    w_gate_ref, w_up_ref, w_down_ref, back_ref, dots_ref = refs[5:10]
    grads, (gate_low_ref, up_low_ref) = refs[10:-2], refs[-2:]
    slots, width = g_ref.shape[1], g_ref.shape[2]
    chunk = 256
    active_grad = dot(g_ref[0], w_down_ref[0])
    gate_low_ref[...] = (active_grad * factor_ref[0]).astype(bf16)
    up_low_ref[...] = (active_grad * silu_ref[0]).astype(bf16)
    dots = jnp.sum(active_ref[0].astype(f32) * active_grad, axis=1, keepdims=True)
    dots_ref[0] = jnp.broadcast_to(dots, (slots, LANES))
    back_ref[0] = (dot_nt(gate_low_ref[...], w_gate_ref[0]) + dot_nt(up_low_ref[...], w_up_ref[0])).astype(bf16)

    def products(cols):
        x = x_ref[0, :, cols]
        yield 0, dot_tn(x, gate_low_ref[...]).astype(bf16)
        yield 1, dot_tn(x, up_low_ref[...]).astype(bf16)
        yield 2, dot_tn(g_ref[0, :, cols], active_ref[0]).astype(bf16)

    if fast:
        write_shards(place_ref, grads, products, width)
    else:

        def whole_columns(index, carry):
            cols = pl.ds(pl.multiple_of(index * chunk, chunk), chunk)
            for which, product in products(cols):
                grads[which][0, cols, :] = product
            return carry

        lax.fori_loop(0, width // chunk, whole_columns, 0)


def write_shards(place_ref, outs, products, width):
    send_a, keep_a, send_b, keep_b = outs
    x_bit, y_bit = place_ref[3], place_ref[4]
    shard = width // 4
    for dy in range(2):
        for dx in range(2):
            x, y = x_bit ^ dx, y_bit ^ dy
            cols = pl.ds(pl.multiple_of((y * 2 + x) * shard, shard), shard)
            for which, product in products(cols):
                side = product.shape[1] // 2
                (send_a if dx else keep_a)[0, which, y] = product[:, :side]
                (send_b if dy else keep_b)[0, which, x] = product[:, side:]


def run_experts_back(place, x, g, active, factor, silu, w_gate, w_up, w_down, first, count, fast):
    slots, width = g.shape[1], g.shape[2]
    hidden = w_gate.shape[2]

    def taken(*shape):
        return pl.BlockSpec((1,) + shape, lambda e, p: (e + first, 0, 0))

    def given(*shape):
        zeros = (0,) * len(shape)
        return pl.BlockSpec((1,) + shape, lambda e, p: (e,) + zeros)

    if fast:
        grad_shapes = [(3, 2, width // 4, hidden // 2)] * 4
    else:
        grad_shapes = [(width, hidden)] * 3
    return call(
        lambda *refs: expert_back_kernel(*refs, fast=fast),
        (count,),
        1,
        [taken(slots, width)] * 2 + [taken(slots, hidden)] * 3 + [taken(width, hidden)] * 3,
        [given(slots, width), given(slots, LANES)] + [given(*shape) for shape in grad_shapes],
        [struct((count, slots, width), bf16), struct((count, slots, LANES), f32)]
        + [struct((count,) + shape, bf16) for shape in grad_shapes],
        scratch=[pltpu.VMEM((slots, hidden), bf16)] * 2,
        us=0.5,
    )(place, x, g, active, factor, silu, w_gate, w_up, w_down)


DOT_LANES = 2 * LANES


def combine_kernel(place_ref, rank_ref, *refs, pieces, with_dots, mine):
    parts, rest = refs[:pieces], refs[pieces:]
    rows = rank_ref.shape[2]
    local_experts = sum(part.shape[0] for part in parts)
    hits = hits_of(rank_ref[0], local_experts)
    gathered = jnp.concatenate([part[j, 0] for part in parts for j in range(part.shape[0])], axis=0)
    summed = dot_tn(chosen_of(hits), gathered)
    out_ref = rest[-1]
    if mine:
        arrived_ref = rest[-2]
        summed = summed + arrived_ref[0, 0:rows, :].astype(f32)
    out_ref[0, 0:rows, :] = summed.astype(bf16)
    if with_dots:
        column = [part[j, 0][:, 0:1] for part in rest[:pieces] for j in range(part.shape[0])]
        scattered = [
            jnp.sum(jnp.where(hit, value, 0.0), axis=0, keepdims=True) for hit, value in zip(hits, column)
        ]
        scattered.append(jnp.zeros((DOT_ROWS - local_experts, rows), f32))
        scattered = jnp.concatenate(scattered, axis=0)
        upper = scattered.astype(bf16)
        out_ref[0, rows:, :] = jnp.zeros((DOT_ROWS, out_ref.shape[2]), bf16)
        out_ref[0, rows:, 0:rows] = upper
        out_ref[0, rows:, DOT_LANES : DOT_LANES + rows] = (scattered - upper.astype(f32)).astype(bf16)
        if mine:
            out_ref[0, rows:, 2 * DOT_LANES : 4 * DOT_LANES] = arrived_ref[0, rows:, 0 : 2 * DOT_LANES]


def combine(place, rank, parts, dots=None, arrived=None):
    mine = arrived is not None
    rows, width = rank.shape[2], parts[0].shape[-1]
    out_rows = rows + (DOT_ROWS if dots else 0)

    def member(step, p):
        return (p[0] if mine else 1 - p[0]) * COLS + step

    def slots_of(array):
        return pl.BlockSpec((array.shape[0], 1) + array.shape[2:], lambda j, p: (0, member(j, p), 0, 0))

    inputs = [
        part.reshape(part.shape[0], 2 * COLS, CAPACITY, part.shape[-1]) for part in list(parts) + list(dots or [])
    ]
    in_specs = [pl.BlockSpec((1, 8, rows), lambda j, p: (member(j, p), 0, 0))] + [slots_of(item) for item in inputs]
    by_chip = pl.BlockSpec((1, out_rows, width), lambda j, p: (j, 0, 0))
    if mine:
        inputs.append(arrived)
        in_specs.append(by_chip)
    return call(
        lambda *refs: combine_kernel(*refs, pieces=len(parts), with_dots=bool(dots), mine=mine),
        (COLS,),
        1,
        in_specs,
        by_chip,
        struct((COLS, out_rows, width), bf16),
        us=0.5,
    )(place, rank, *inputs)


def split_dot(dimension_numbers, values, exact):
    upper = values.astype(bf16)
    lower = (values - upper.astype(f32)).astype(bf16)
    return lax.dot_general(
        upper, exact, dimension_numbers, preferred_element_type=f32
    ) + lax.dot_general(lower, exact, dimension_numbers, preferred_element_type=f32)


EXTRA_SLOTS = 6


def middle_back_kernel(
    place_ref, sums_ref, gates_ref, middle_ref, cot_ref, gain_ref, w_router_ref, w_mine_ref, w_other_ref,
    grad_ref, branch_ref, attended_ref, extra_ref
):
    rows = middle_ref.shape[0]
    tail = sums_ref[:, rows : rows + 8, 0 : 4 * DOT_LANES].astype(f32)
    mine = tail[:, :, 0:rows] + tail[:, :, DOT_LANES : DOT_LANES + rows]
    other = tail[:, :, 2 * DOT_LANES : 2 * DOT_LANES + rows] + tail[:, :, 3 * DOT_LANES : 3 * DOT_LANES + rows]
    first_row = place_ref[0] == 0
    dots = jnp.concatenate([jnp.where(first_row, mine, other), jnp.where(first_row, other, mine)], axis=0)
    dots = dots.reshape(dots.shape[0] * 8, rows)
    gates = gates_ref[...]
    logit_grad = dots - gates * jnp.sum(dots, axis=0, keepdims=True)
    middle = middle_ref[...]
    inverse = lax.rsqrt(jnp.mean(middle * middle, axis=1, keepdims=True) + epsilon)
    unit = middle * inverse
    gain = gain_ref[...]
    grad = sums_ref[0, 0:rows].astype(f32)
    for index in range(1, sums_ref.shape[0]):
        grad = grad + sums_ref[index, 0:rows].astype(f32)
    grad = grad + split_dot(TN, logit_grad, w_router_ref[...])
    gain_grad = jnp.sum(grad * unit, axis=0, keepdims=True)
    scaled = grad * gain
    middle_grad = cot_ref[...].astype(f32) + inverse * (
        scaled - unit * jnp.mean(scaled * unit, axis=1, keepdims=True)
    )
    grad_ref[...] = middle_grad
    branch_grad = middle_grad.astype(bf16)
    branch_ref[0:rows, :] = branch_grad
    extra_ref[...] = jnp.zeros_like(extra_ref)
    for index in range(logit_grad.shape[0] // 8):
        first, lane = index // EXTRA_SLOTS * 8, index % EXTRA_SLOTS * DOT_LANES
        extra_ref[first : first + 8, lane : lane + rows] = logit_grad[index * 8 : index * 8 + 8]
    upper = gain_grad.astype(bf16).astype(f32)
    extra_ref[13:14, :] = upper
    extra_ref[14:15, :] = gain_grad - upper
    branch_ref[rows:, :] = extra_ref[...].astype(bf16)
    for which, ref in enumerate((w_mine_ref, w_other_ref)):
        line = place_ref[0] if which == 0 else 1 - place_ref[0]
        for col in range(ref.shape[0]):
            product = dot_nt(branch_grad, ref[col])
            member = line * COLS + col
            attended_ref[member, :, 0:LANES] = product[:, 0:LANES].astype(bf16)
            attended_ref[member, :, LANES : LANES + HEAD_DIM] = product[:, LANES:].astype(bf16)
            attended_ref[member, :, LANES + HEAD_DIM :] = jnp.zeros((product.shape[0], HEAD_DIM), bf16)


def middle_back(place, sums, gates, middle, cotangent, gain, w_router, w_mine, w_other):
    rows, width = middle.shape
    members = 2 * COLS
    args = (sums, gates, middle, cotangent, gain, w_router, w_mine, w_other)
    return call(
        middle_back_kernel,
        (1,),
        1,
        [whole(item.shape) for item in args],
        [whole((rows, width)), whole((rows + DOT_ROWS, width)), whole((members, rows, 2 * LANES))],
        [
            struct((rows, width), f32),
            struct((rows + DOT_ROWS, width), bf16),
            struct((members, rows, 2 * LANES), bf16),
        ],
        scratch=[pltpu.VMEM((DOT_ROWS, width), f32)],
        us=0.5,
    )(place, *args)


def input_grad_kernel(
    place_ref, grads_mine_ref, grads_other_ref, mine_a_ref, mine_b_ref, other_a_ref, other_b_ref,
    tok_ref, middle_grad_ref, gain_ref, out_ref, sum_ref
):
    step = pl.program_id(0)
    first = place_ref[4] == 0

    def weights(a_ref, b_ref):
        a = jnp.concatenate([a_ref[index, 0] for index in range(a_ref.shape[0])], axis=0)
        b = jnp.concatenate([b_ref[index, 0] for index in range(b_ref.shape[0])], axis=0)
        upper, lower = jnp.where(first, a, b), jnp.where(first, b, a)
        return jnp.concatenate([upper, lower, lower[lower.shape[0] - HEAD_DIM :]], axis=0)

    part = dot(grads_mine_ref[0], weights(mine_a_ref, mine_b_ref))
    part = part + dot(grads_other_ref[0], weights(other_a_ref, other_b_ref))

    @pl.when(step == 0)
    def _():
        sum_ref[...] = part

    @pl.when(step > 0)
    def _():
        sum_ref[...] += part

    @pl.when(step == pl.num_programs(0) - 1)
    def _():
        resid = tok_ref[...].astype(f32)
        inverse = lax.rsqrt(jnp.mean(resid * resid, axis=1, keepdims=True) + epsilon)
        unit = resid * inverse
        scaled = sum_ref[...] * gain_ref[...]
        out_ref[...] = middle_grad_ref[...] + inverse * (
            scaled - unit * jnp.mean(scaled * unit, axis=1, keepdims=True)
        )


def input_grad(place, grads, weights, tokens, middle_grad, gain):
    rows, width = tokens.shape
    lanes = grads.shape[2]
    w_shape = (weights[0].shape[0], 1) + weights[0].shape[2:]
    return call(
        input_grad_kernel,
        (COLS,),
        1,
        [
            pl.BlockSpec((1, rows, lanes), lambda c, p: (p[0] * COLS + c, 0, 0)),
            pl.BlockSpec((1, rows, lanes), lambda c, p: ((1 - p[0]) * COLS + c, 0, 0)),
        ]
        + [pl.BlockSpec(w_shape, lambda c, p: (0, c, 0, 0))] * 4
        + [whole((rows, width)), whole((rows, width)), whole((1, width))],
        whole((rows, width)),
        struct((rows, width), f32),
        scratch=[pltpu.VMEM((rows, width), f32)],
        us=0.5,
    )(place, grads, grads, *weights, tokens, middle_grad, gain)


def own_weights_kernel(normed_ref, projected_ref, w_ref, gain_ref, out_ref, gain_grad_ref, sum_ref):
    step = pl.program_id(0)

    @pl.when(step == 0)
    def _():
        sum_ref[...] = jnp.zeros_like(sum_ref)

    sum_ref[...] += dot_tn(normed_ref[...], projected_ref[...])

    @pl.when(step == pl.num_programs(0) - 1)
    def _():
        total = sum_ref[...]
        out_ref[...] = total.astype(bf16)
        by_weight = jnp.sum(total * w_ref[...].astype(f32), axis=1, keepdims=True)
        gain_grad_ref[...] = jnp.broadcast_to(by_weight / gain_ref[...], gain_grad_ref.shape)


def own_weights(normed, projected, w_natural, gain):
    total, width = normed.shape
    lanes = projected.shape[1]
    rows = 512
    return call(
        own_weights_kernel,
        (total // rows,),
        0,
        [
            pl.BlockSpec((rows, width), lambda j: (j, 0)),
            pl.BlockSpec((rows, lanes), lambda j: (j, 0)),
            whole((width, lanes)),
            whole((width, 1)),
        ],
        [whole((width, lanes)), whole((width, 8))],
        [struct((width, lanes), bf16), struct((width, 8), f32)],
        scratch=[pltpu.VMEM((width, lanes), f32)],
        us=0.5,
    )(normed, projected, w_natural, gain)


def out_weights_kernel(place_ref, branch_ref, att_ref, normed_ref, own_ref, *refs, fast, local_experts):
    outs, small_ref, (sum_ref, gain_sum_ref) = refs[:-3], refs[-3], refs[-2:]
    step = pl.program_id(0)
    rows = att_ref.shape[0] // 2
    block = rows + DOT_ROWS

    @pl.when(step == 0)
    def _():
        sum_ref[...] = jnp.zeros_like(sum_ref)
        small_ref[...] = jnp.zeros_like(small_ref)
        gain_sum_ref[...] = jnp.zeros_like(gain_sum_ref)

    branch = jnp.concatenate([branch_ref[0:rows, :], branch_ref[block : block + rows, :]], axis=0)
    sum_ref[...] += dot_tn(branch, att_ref[...])
    for which in range(2):
        tail = branch_ref[which * block + rows : (which + 1) * block, :].astype(f32)
        slots = []
        for index in range(small_ref.shape[0] // 8):
            first, lane = index // EXTRA_SLOTS * 8, index % EXTRA_SLOTS * DOT_LANES
            slots.append(tail[first : first + 8, lane : lane + rows])
        logit_grad = jnp.concatenate(slots, axis=0)
        real = lax.broadcasted_iota(jnp.int32, logit_grad.shape, 0) % 8 < local_experts
        logit_grad = jnp.where(real, logit_grad, 0.0).astype(bf16)
        small_ref[...] += dot(logit_grad, normed_ref[which * rows : (which + 1) * rows, :])
        gain_sum_ref[...] += tail[8:16, :]

    @pl.when(step == pl.num_programs(0) - 1)
    def _():
        small_ref[7:8, :] = gain_sum_ref[5:6, :] + gain_sum_ref[6:7, :]

        def products(cols):
            own = own_ref[cols, 0 : 2 * LANES]
            out_one = sum_ref[cols, 0:LANES].astype(bf16)
            out_two = sum_ref[cols, LANES:]
            low = lane_of(out_two.shape) < HEAD_DIM
            tail = jnp.where(low, out_two, own_ref[cols, 2 * LANES :].astype(f32)).astype(bf16)
            yield 0, jnp.concatenate([own, out_one, tail], axis=1)

        if fast:
            write_shards(place_ref, outs, products, own_ref.shape[0])
        else:
            outs[0][...] = next(products(slice(0, own_ref.shape[0])))[1]


def out_weights(place, branch, attended, normed, own, padded, local_experts, fast):
    total, width = normed.shape
    rows = total // COLS
    blocks = branch.shape[0] // COLS
    if fast:
        shapes = [(1, 1, 2, width // 4, 2 * LANES)] * 4
    else:
        shapes = [(width, 4 * LANES)]
    return call(
        lambda *refs: out_weights_kernel(*refs, fast=fast, local_experts=local_experts),
        (COLS,),
        1,
        [
            pl.BlockSpec((blocks, width), lambda j, p: (j, 0)),
            pl.BlockSpec((rows, 2 * LANES), lambda j, p: (j, 0)),
            pl.BlockSpec((rows, width), lambda j, p: (j, 0)),
            whole(own.shape),
        ],
        [whole(shape) for shape in shapes] + [whole((padded, width))],
        [struct(shape, bf16) for shape in shapes] + [struct((padded, width), f32)],
        scratch=[pltpu.VMEM((width, 2 * LANES), f32), pltpu.VMEM((8, width), f32)],
        us=0.5,
    )(place, branch, attended, normed, own)


def first_sum_kernel(place_ref, keep_a_ref, got_a_ref, keep_b_ref, got_b_ref, *rest):
    send_a_ref, held_a_ref, send_b_ref, held_b_ref = rest[-4:]
    x_bit, y_bit = place_ref[3], place_ref[4]
    for bit, keep, got, send, held in (
        (y_bit, keep_a_ref, got_a_ref, send_a_ref, held_a_ref),
        (x_bit, keep_b_ref, got_b_ref, send_b_ref, held_b_ref),
    ):
        for kind in range(keep.shape[1]):
            held[0, kind] = (keep[0, kind, bit].astype(f32) + got[0, kind, bit].astype(f32)).astype(bf16)
            send[0, kind] = (keep[0, kind, 1 - bit].astype(f32) + got[0, kind, 1 - bit].astype(f32)).astype(bf16)


def first_sum(place, chunk, first=0, total=None, before=None):
    count, kinds, _, rows, cols = chunk[0].shape
    taken = pl.BlockSpec((1, kinds, 2, rows, cols), lambda e, p: (e, 0, 0, 0, 0))
    given = pl.BlockSpec((1, kinds, rows, cols), lambda e, p: (e + first, 0, 0, 0))
    extra = list(before) if before else []
    return call(
        first_sum_kernel,
        (count,),
        1,
        [taken] * 4 + [pl.BlockSpec(memory_space=pl.ANY)] * len(extra),
        [given] * 4,
        [struct((total or count, kinds, rows, cols), bf16)] * 4,
        us=0.5,
        aliases={5 + i: i for i in range(len(extra))},
    )(place, *chunk, *extra)


def last_sum_kernel(held_a_ref, got_a_ref, held_b_ref, got_b_ref, *rest):
    outs = rest[-3:]
    side = held_a_ref.shape[3]
    for which, out in enumerate(outs):
        out[0, :, :side] = held_a_ref[0, which].astype(f32) + got_a_ref[0, which].astype(f32)
        out[0, :, side:] = held_b_ref[0, which].astype(f32) + got_b_ref[0, which].astype(f32)


def last_sum(held_a, got_a, held_b, got_b, first, total, before):
    count, kinds, rows, cols = held_a.shape
    taken = pl.BlockSpec((1, kinds, rows, cols), lambda e: (e, 0, 0, 0))
    given = pl.BlockSpec((1, rows, 2 * cols), lambda e: (e + first, 0, 0))
    extra = list(before) if before else []
    return call(
        last_sum_kernel,
        (count,),
        0,
        [taken] * 4 + [pl.BlockSpec(memory_space=pl.ANY)] * len(extra),
        [given] * 3,
        [struct((total, rows, 2 * cols), f32)] * 3,
        us=0.5,
        aliases={4 + i: i for i in range(len(extra))},
    )(held_a, got_a, held_b, got_b, *extra)


def last_weights_kernel(held_a_ref, got_a_ref, held_b_ref, got_b_ref, query_ref, key_ref, value_ref, out_ref):
    left = held_a_ref[0, 0].astype(f32) + got_a_ref[0, 0].astype(f32)
    right = held_b_ref[0, 0].astype(f32) + got_b_ref[0, 0].astype(f32)
    cut = query_ref.shape[1]
    query_ref[...] = left[:, :cut]
    key_ref[...] = left[:, cut:]
    out_ref[...] = right[:, :cut]
    value_ref[...] = right[:, cut:]


def last_weights(parts, widths):
    rows = parts[0].shape[2]
    shapes = [(rows, width) for width in widths]
    return call(
        last_weights_kernel,
        (1,),
        0,
        [whole(part.shape) for part in parts],
        [whole(shape) for shape in shapes],
        [struct(shape, f32) for shape in shapes],
        us=0.5,
    )(*parts)


SWAP = [(0, 1), (1, 0)]


def after(value, *events):
    return lax.optimization_barrier((value,) + events)[0]


def gather_group(block):
    return lax.all_gather(block, ("row", "col"), axis=0, tiled=True)


def line_pieces(value):
    parts = [value]
    for distance in range(1, COLS):
        parts.insert(0, lax.ppermute(value, "col", [(i, (i + distance) % COLS) for i in range(COLS)]))
    return parts


def in_line_order(parts):
    parts = jnp.stack(parts + parts)
    return lax.dynamic_slice_in_dim(parts, COLS - 1 - lax.axis_index("col"), COLS, axis=0)


def flip(value, axis, bit, size):
    return lax.ppermute(value, axis, [(i, i ^ (1 << bit)) for i in range(size)])


def bits_of(size):
    return size.bit_length() - 1


def own_bit(axis, bit):
    return (lax.axis_index(axis) >> bit) & 1


def joined(mine, got, own):
    return jnp.where(own == 0, jnp.concatenate([mine, got]), jnp.concatenate([got, mine]))


def cube_step(value, axis, bit, size):
    return joined(value, flip(value, axis, bit, size), own_bit(axis, bit))


def lines_first(value):
    return jnp.transpose(value, (1, 0, 2, 3)).reshape(value.shape[1], value.shape[0] * value.shape[2], value.shape[3])


def cube_gather(value, axis, size):
    value = value[None]
    for bit in range(bits_of(size)):
        value = cube_step(value, axis, bit, size)
    return value


def sum_dp(value, sizes):
    for bit in range(bits_of(sizes["dp"])):
        value = value + flip(value, "dp", bit, sizes["dp"])
    return value


def reduce_over_dp(value, size):
    count = bits_of(size)
    value = value.reshape(value.shape[:1] + (2,) * count + value.shape[2:])
    current = value
    for bit in range(count - 1, -1, -1):
        own = own_bit("dp", bit)
        keep = lax.dynamic_index_in_dim(current, own, 1, keepdims=False)
        send = lax.dynamic_index_in_dim(current, 1 - own, 1, keepdims=False).astype(bf16)
        current = keep.astype(f32) + flip(send, "dp", bit, size).astype(f32)
    return current


def start_move(run, size):
    return flip(run[0], "dp", 0, size), flip(run[2], "dp", 1, size)


def second_move(sums, size):
    send_a, held_a, send_b, held_b = sums
    return held_a, flip(send_a, "dp", 1, size), held_b, flip(send_b, "dp", 0, size)


def layer(sizes):
    n_dp, n_row, n_col = sizes["dp"], sizes["row"], sizes["col"]
    members = n_row * n_col
    fast = n_dp == 4
    assert n_row == 2 and n_col == COLS and n_dp & (n_dp - 1) == 0

    def local(
        tokens, cotangent, routes, lengths, gain_attn, w_query, w_key, w_value, w_out,
        gain_moe, w_router, w_gate, w_up, w_down,
    ):
        rows, width = tokens.shape
        group = rows * members
        local_experts = w_gate.shape[0]
        row, col, dp = lax.axis_index("row"), lax.axis_index("col"), lax.axis_index("dp")
        place = jnp.stack([row, col, row * n_col + col, dp & 1, (dp >> 1) & 1]).astype(jnp.int32)
        gain_one = gain_attn.astype(f32)[None]
        gain_two = gain_moe.astype(f32)[None]

        tok_all = gather_group(tokens)
        w_in = jnp.concatenate([w_query.T, w_key.T, w_value.T], axis=0)
        out_share, in_share = rows // n_dp, w_in.shape[0] // n_dp
        shares = jnp.concatenate(
            [
                lax.dynamic_slice(w_out.T, (dp * out_share, 0), (out_share, width)),
                lax.dynamic_slice(w_in, (dp * in_share, 0), (in_share, width)),
                jnp.pad(routes.T.astype(bf16).reshape(1, TOP * rows), ((0, 7), (0, width - TOP * rows))),
            ],
            axis=0,
        )
        w_stack = jnp.concatenate([w_query.T, w_key.T, w_value.T, w_value.T], axis=0)
        w_natural = jnp.concatenate([w_query, w_key, w_value, w_value], axis=1)

        ends = jnp.cumsum(lengths[0])
        starts = ends - lengths[0]
        position = jnp.arange(group, dtype=jnp.int32)
        segment = jnp.sum((position[:, None] >= ends[None, :]).astype(jnp.int32), axis=1)
        member = segment[:, None] == jnp.arange(starts.shape[0], dtype=jnp.int32)[None, :]
        start = jnp.sum(jnp.where(member, starts[None, :], 0), axis=1).astype(jnp.int32)
        frequency = rope_base ** (-2.0 * jnp.arange(HEAD_DIM // 2, dtype=f32) / HEAD_DIM)
        angle = (position - start).astype(f32)[:, None] * frequency[None, :]
        cosine = jnp.tile(jnp.cos(angle), (1, 4))
        sine = jnp.tile(jnp.sin(angle), (1, 4))

        w_router_rows = w_router.T.reshape(members, local_experts, width)
        w_router_rows = jnp.pad(w_router_rows, ((0, 0), (0, 8 - local_experts), (0, 0)))
        w_router_rows = w_router_rows.reshape(members * 8, width)
        start_row = jnp.broadcast_to(start[None, :], (8, group))
        start = start[:, None]
        gain_column = gain_attn.astype(f32)[:, None]
        ready = (place, gain_one, gain_two, w_stack, w_natural, cosine, sine, w_router_rows, start, start_row, gain_column)
        shares, place, gain_one, gain_two, w_stack, w_natural, cosine, sine, w_router_rows, start, start_row, gain_column = (
            lax.optimization_barrier((shares,) + ready)
        )
        shares = line_pieces(after(shares, tok_all, cosine))

        query, key, value, normed_one = project(tok_all, gain_one, w_stack, cosine, sine)
        packed, attended, totals = attend(query, key, value, start)
        att_flat = gather_group(packed)
        att_all = att_flat.reshape((n_row, n_col) + packed.shape)
        shares = in_line_order(after(shares, packed))
        route_rows = shares[:, out_share + in_share]
        w_out_mine, in_part = shares[None, :, :out_share], shares[None, :, out_share : out_share + in_share]
        for bit in range(bits_of(n_dp)):
            w_out_mine = cube_step(w_out_mine, "dp", bit, n_dp)
        in_part = cube_step(in_part, "dp", 0, n_dp)
        w_out_mine = lines_first(w_out_mine)
        w_out_other = lax.ppermute(after(w_out_mine, in_part), "row", SWAP)
        route_rows = cube_gather(route_rows, "row", n_row)[:, :, : TOP * rows].reshape(members, TOP, rows)
        cot_all = gather_group(after(cotangent, w_out_other))
        x, slot_gate, rank, gate, normed_two, middle, gates = middle_and_dispatch(
            place, att_all, w_out_mine, w_out_other, tok_all, route_rows, gain_two, w_router_rows, local_experts
        )
        slots = members * CAPACITY
        x = x.reshape(local_experts, slots, width)
        slot_gate = slot_gate.reshape(local_experts, slots, LANES)
        rank, gate = rank.reshape(members, 8, rows), gate.reshape(members, 8, rows)
        forth, active, factor, silu = run_experts(x, slot_gate, w_gate, w_up, w_down)
        for bit in range(1, bits_of(n_dp) - 1):
            in_part = cube_step(in_part, "dp", bit, n_dp)
        last_bit = bits_of(n_dp) - 1
        in_got = after(flip(in_part, "dp", last_bit, n_dp), forth)
        forth_other = combine(place, after(rank, in_got), [forth])
        arrived = lax.ppermute(forth_other, "row", SWAP)
        g = grad_dispatch(after(rank, forth_other), gate, cot_all, local_experts)
        g = g.reshape(local_experts, slots, width)
        cuts = [0, 2, 4, local_experts]

        def backward(which, x):
            first, last = cuts[which], cuts[which + 1]
            return run_experts_back(place, x, g, active, factor, silu, w_gate, w_up, w_down, first, last - first, fast)

        runs = [backward(0, x)]
        forth_mine = combine(place, rank, [forth], arrived=after(arrived, runs[0][1]))
        forth_sums = lax.all_to_all(forth_mine, "col", 0, 0, tiled=True)
        runs.append(backward(1, after(x, forth_mine)))
        runs.append(backward(2, after(x, runs[1][1])))
        moved = [start_move(run[2:], n_dp) for run in runs] if fast else []
        back_parts, dot_parts = [run[0] for run in runs], [run[1] for run in runs]
        back_other = combine(place, after(rank, *moved[0]) if fast else rank, back_parts, dot_parts)
        arrived = lax.ppermute(back_other, "row", SWAP)
        back_mine = combine(place, rank, back_parts, dot_parts, arrived)
        back_mine = after(back_mine, forth_sums)
        back_sums = lax.all_to_all(back_mine, "col", 0, 0, tiled=True)

        if fast:
            w_in_parts = [in_part, in_got]
        else:
            own = own_bit("dp", last_bit)
            w_in_rows = lines_first(joined(in_part, in_got, own))[None]
            half = w_in_rows.shape[2] // 2
            upper, lower = w_in_rows[:, :, :half], w_in_rows[:, :, half:]
            w_in_parts = [jnp.where(place[4] == 0, upper, lower), jnp.where(place[4] == 0, lower, upper)]
        if fast:

            def chunk_of(which, event):
                keep_a, keep_b = after((runs[which][3], runs[which][5]), event)
                return keep_a, moved[which][0], keep_b, moved[which][1]

            sums = first_sum(place, chunk_of(0, back_mine), cuts[0], cuts[2])
            gate_middle = (sums[1],) + moved[1]
        else:
            gate_middle = ()
        w_in_parts += [lax.ppermute(after(part, back_mine), "row", SWAP) for part in w_in_parts]

        middle_grad, branch_grad, attended_grad = middle_back(
            place, back_sums, gates, middle, cotangent, after(gain_two, *w_in_parts[2:], *gate_middle),
            w_router_rows, w_out_mine, w_out_other,
        )
        if fast:
            sums = first_sum(place, chunk_of(1, branch_grad), cuts[1], cuts[2], sums)
            started = [second_move(sums, n_dp)]
        attended_grad = lax.all_to_all(attended_grad, ("row", "col"), 0, 0, tiled=True)
        if fast:
            attended_grad = after(attended_grad, sums[1])
        branch_all = gather_group(after(branch_grad, attended_grad))

        attended_grad = attended_grad.reshape(group, 2 * LANES)
        projected_grad = attend_back(query, key, value, attended_grad, totals, start_row, cosine, sine)
        projected_all = lax.all_to_all(
            projected_grad.reshape(members, rows, 3 * LANES), ("row", "col"), 0, 0, tiled=True
        )
        own_grads, gain_part = own_weights(
            after(normed_one, *moved[2]) if fast else normed_one,
            projected_grad, w_natural, gain_column,
        )
        if fast:
            started.append(second_move(first_sum(place, chunk_of(2, own_grads)), n_dp))
            normed_two = after(normed_two, started[1][0])
        *w_parts, small = out_weights(
            place, branch_all, attended, normed_two.reshape(group, width), own_grads,
            members * 8, local_experts, fast,
        )
        gain_rows = gather_group(after(gain_part, small)[:, 0].reshape(8, width // 8)).reshape(members, width)
        gain_attn_grad = jnp.sum(gain_rows, axis=0, keepdims=True)
        expert_grads = None
        if fast:
            w_moved = start_move(w_parts, n_dp)
            held_a, got_a, held_b, got_b = started[0]
            held_a, held_b = after((held_a, held_b), small)
            expert_grads = last_sum(held_a, got_a, held_b, got_b, 0, local_experts, None)
        else:
            cut = w_parts[0].reshape(1, n_dp, width // n_dp, w_parts[0].shape[1])
            w_sum = reduce_over_dp(cut, n_dp)[0]

        mixed = (middle + jnp.sum(after(forth_sums, projected_grad).astype(f32), axis=0)).astype(bf16)

        used = small.reshape(members, 8, width)[:, :local_experts].reshape(members * local_experts, width)
        both = jnp.concatenate([used, small[7:8], gain_attn_grad], axis=0)
        both = sum_dp(both, sizes)
        w_router_grad = both[: members * local_experts].T
        gain_moe_grad, gain_attn_grad = both[members * local_experts], both[members * local_experts + 1]

        tokens_grad = input_grad(
            place, projected_all, w_in_parts, tokens, middle_grad, after(gain_one, w_parts[0])
        )

        local_q, local_k = w_query.shape[1], w_key.shape[1]
        if fast:
            expert_grads = last_sum(*started[1], cuts[2], local_experts, expert_grads)
            w_sums = second_move(
                first_sum(place, (w_parts[1], w_moved[0], w_parts[3], w_moved[1])), n_dp
            )
            w_query_grad, w_key_grad, w_value_grad, w_out_grad = last_weights(
                w_sums, (local_q, local_k, local_k, local_q)
            )
        else:
            expert_grads = []
            for which in range(3):
                parts = [run[2 + which] for run in runs]
                parts = [part.reshape(part.shape[0], n_dp, width // n_dp, part.shape[2]) for part in parts]
                expert_grads.append(jnp.concatenate([reduce_over_dp(part, n_dp) for part in parts], axis=0))
            cut = local_q + local_k
            w_query_grad, w_key_grad = w_sum[:, :local_q], w_sum[:, local_q:cut]
            w_out_grad, w_value_grad = w_sum[:, cut : cut + local_q], w_sum[:, cut + local_q :]
        w_gate_grad, w_up_grad, w_down_grad = expert_grads
        return (
            mixed, tokens_grad, gain_attn_grad, w_query_grad, w_key_grad, w_value_grad, w_out_grad,
            gain_moe_grad, w_router_grad, w_gate_grad, w_up_grad, w_down_grad,
        )

    return local


def solution(mesh):
    return jax.shard_map(
        layer(dict(mesh.shape)),
        mesh=mesh,
        in_specs=(
            P(("dp", "row", "col"), None),
            P(("dp", "row", "col"), None),
            P(("dp", "row", "col"), None),
            P("dp", None),
            P(),
            P(None, ("row", "col")),
            P(None, ("row", "col")),
            P(None, ("row", "col")),
            P(None, ("row", "col")),
            P(),
            P(),
            P(("row", "col"), None, None),
            P(("row", "col"), None, None),
            P(("row", "col"), None, None),
        ),
        out_specs=(
            P(("dp", "row", "col"), None),
            P(("dp", "row", "col"), None),
            P(),
            P("dp", ("row", "col")),
            P("dp", ("row", "col")),
            P("dp", ("row", "col")),
            P("dp", ("row", "col")),
            P(),
            P(),
            P(("row", "col"), "dp", None),
            P(("row", "col"), "dp", None),
            P(("row", "col"), "dp", None),
        ),
        check_vma=False,
    )
```

```python
import math

import jax
import jax.numpy as jnp
import numpy as np
from jax import lax
from jax.experimental import pallas as pl
from jax.experimental.pallas import tpu as pltpu
from jax.sharding import PartitionSpec as P

HEAD_DIM = 64
EXPERTS = 40
TOP = 8
CAPACITY = 64
COLS = 4
LANES = 128
QUERY_BLOCK = 256
DOT_ROWS = 16

epsilon = 1e-06
rope_base = 10000.0
masked_score = -1e30
f32 = jnp.float32
bf16 = jnp.bfloat16
VMEM_LIMIT = 56 * 1024 * 1024

NT = (((1,), (1,)), ((), ()))
TN = (((0,), (0,)), ((), ()))


def dot(a, b):
    return jnp.dot(a, b, preferred_element_type=f32)


def dot_nt(a, b):
    return lax.dot_general(a, b, NT, preferred_element_type=f32)


def dot_tn(a, b):
    return lax.dot_general(a, b, TN, preferred_element_type=f32)


def lane_of(shape):
    return lax.broadcasted_iota(jnp.int32, shape, len(shape) - 1)


def call(
    kernel, grid, prefetch, in_specs, out_specs, out_shape, scratch=(), us=1.0, aliases=None
):
    return pl.pallas_call(
        kernel,
        grid_spec=pltpu.PrefetchScalarGridSpec(
            num_scalar_prefetch=prefetch,
            grid=grid,
            in_specs=in_specs,
            out_specs=out_specs,
            scratch_shapes=list(scratch),
        ),
        out_shape=out_shape,
        input_output_aliases=aliases or {},
        compiler_params=pltpu.CompilerParams(
            vmem_limit_bytes=VMEM_LIMIT, dimension_semantics=("arbitrary",) * len(grid)
        ),
        cost_estimate=pl.CostEstimate(
            flops=int(us * 1.1e9), bytes_accessed=int(us * 3.6e6), transcendentals=0
        ),
    )


def whole(shape):
    zeros = (0,) * len(shape)
    return pl.BlockSpec(shape, lambda *_: zeros)


def struct(shape, dtype):
    return jax.ShapeDtypeStruct(shape, dtype)


def turn_within_heads(values, sign):
    lane = lane_of(values.shape) % HEAD_DIM
    ahead = pltpu.roll(values, LANES - HEAD_DIM // 2, 1)
    behind = pltpu.roll(values, HEAD_DIM // 2, 1)
    return jnp.where(lane < HEAD_DIM // 2, -sign * ahead, sign * behind)


def project_kernel(
    tok_ref, gain_ref, w_ref, cos_ref, sin_ref, query_ref, key_ref, value_ref, normed_ref
):
    resid = tok_ref[...].astype(f32)
    inverse = lax.rsqrt(jnp.mean(resid * resid, axis=1, keepdims=True) + epsilon)
    normed = (resid * inverse * gain_ref[...]).astype(bf16)
    normed_ref[...] = normed
    raw = dot_nt(normed, w_ref[...])
    cosine, sine = cos_ref[...], sin_ref[...]

    def rot(values):
        return (values * cosine + turn_within_heads(values, 1.0) * sine).astype(bf16).astype(f32)

    first = rot(raw[:, :LANES])
    second = rot(raw[:, LANES : 2 * LANES])
    low = lane_of(first.shape) < HEAD_DIM
    scale = 1.0 / math.sqrt(HEAD_DIM)
    query_ref[0] = jnp.where(low, first * scale, 0.0).astype(bf16)
    query_ref[1] = jnp.where(low, 0.0, first * scale).astype(bf16)
    query_ref[2] = jnp.where(low, second * scale, 0.0).astype(bf16)
    key_ref[...] = jnp.where(low, pltpu.roll(second, HEAD_DIM, 1), second).astype(bf16)
    value_ref[...] = raw[:, 2 * LANES :].astype(bf16)


def project(tokens, gain, w_stack, cosine, sine):
    total, width = tokens.shape
    rows = 512
    lanes = pl.BlockSpec((rows, LANES), lambda j: (j, 0))
    wide = pl.BlockSpec((rows, width), lambda j: (j, 0))
    return call(
        project_kernel,
        (total // rows,),
        0,
        [wide, whole((1, width)), whole(w_stack.shape), lanes, lanes],
        [pl.BlockSpec((3, rows, LANES), lambda j: (0, j, 0)), lanes, lanes, wide],
        [
            struct((3, total, LANES), bf16),
            struct((total, LANES), bf16),
            struct((total, LANES), bf16),
            struct((total, width), bf16),
        ],
        us=0.5,
    )(tokens, gain, w_stack, cosine, sine)


def attend_kernel(query_ref, key_ref, value_ref, start_ref, packed_ref, plain_ref, total_ref, out_ref):
    blocks = query_ref.shape[1] // QUERY_BLOCK
    block = pl.program_id(0)
    for index in range(blocks):

        @pl.when(block == index)
        def _(index=index):
            rows = pl.ds(index * QUERY_BLOCK, QUERY_BLOCK)
            span = (index + 1) * QUERY_BLOCK
            row = index * QUERY_BLOCK + lax.broadcasted_iota(jnp.int32, (QUERY_BLOCK, span), 0)
            column = lane_of((QUERY_BLOCK, span))
            allowed = (column <= row) & (column >= start_ref[rows, :])

            def head(number, carry):
                scores = dot_nt(query_ref[number, rows, :], key_ref[0:span, :])
                scores = jnp.where(allowed, scores, masked_score)
                peak = jnp.max(scores, axis=1, keepdims=True)
                weights = jnp.exp(scores - peak)
                summed = jnp.sum(weights, axis=1, keepdims=True)
                probs = (weights * (1.0 / summed)).astype(bf16)
                out_ref[number] = dot(probs, value_ref[0:span, :])
                total = jnp.broadcast_to(peak + jnp.log(summed), (QUERY_BLOCK, LANES))
                total_ref[number, :, rows] = jnp.transpose(total)[0:8, :]
                return carry

            lax.fori_loop(0, 3, head, 0)
            low = lane_of((QUERY_BLOCK, LANES)) < HEAD_DIM
            one, two, three = out_ref[0], out_ref[1], out_ref[2]
            pair = jnp.where(low, one, two).astype(bf16)
            plain_ref[rows, 0:LANES] = pair
            plain_ref[rows, LANES : 2 * LANES] = jnp.where(low, three, 0.0).astype(bf16)
            if index < blocks // 2:
                packed_ref[rows, 0:LANES] = pair
                packed_ref[rows, LANES : 2 * LANES] = three.astype(bf16)
            else:
                back = pl.ds((index - blocks // 2) * QUERY_BLOCK, QUERY_BLOCK)
                before = packed_ref[back, LANES : 2 * LANES].astype(f32)
                packed_ref[back, LANES : 2 * LANES] = jnp.where(low, before, one).astype(bf16)
                packed_ref[back, 2 * LANES : 3 * LANES] = jnp.where(low, two, three).astype(bf16)


def attend(query, key, value, start):
    total = key.shape[0]
    return call(
        attend_kernel,
        (total // QUERY_BLOCK,),
        0,
        [whole(query.shape), whole(key.shape), whole(value.shape), whole(start.shape)],
        [whole((total // 2, 3 * LANES)), whole((total, 2 * LANES)), whole((3, 8, total))],
        [
            struct((total // 2, 3 * LANES), bf16),
            struct((total, 2 * LANES), bf16),
            struct((3, 8, total), f32),
        ],
        scratch=[pltpu.VMEM((3, QUERY_BLOCK, LANES), f32)],
        us=0.5,
    )(query, key, value, start)


def attend_back_kernel(
    query_ref, key_ref, value_ref, grad_ref, total_ref, start_ref, cos_ref, sin_ref, normed_ref, w_ref, gain_ref,
    blocks_ref, own_ref, out_ref, query_grad_ref, key_grad_ref, value_grad_ref, own_sum_ref
):
    blocks = query_ref.shape[1] // QUERY_BLOCK
    block = pl.program_id(0)
    scale = 1.0 / math.sqrt(HEAD_DIM)

    @pl.when(block == 0)
    def _():
        key_grad_ref[...] = jnp.zeros_like(key_grad_ref)
        value_grad_ref[...] = jnp.zeros_like(value_grad_ref)

    def back(values, cosine, sine):
        return values * cosine + turn_within_heads(values * sine, -1.0)

    for index in range(blocks):

        @pl.when(block == index)
        def _(index=index):
            rows = pl.ds(index * QUERY_BLOCK, QUERY_BLOCK)
            span = (index + 1) * QUERY_BLOCK
            row = index * QUERY_BLOCK + lane_of((span, QUERY_BLOCK))
            column = lax.broadcasted_iota(jnp.int32, (span, QUERY_BLOCK), 0)
            allowed = (column <= row) & (column >= start_ref[0:1, rows])
            low = lane_of((QUERY_BLOCK, LANES)) < HEAD_DIM

            def head(number, carry):
                query = query_ref[number, rows, :]
                tile = pl.multiple_of((number // 2) * LANES, LANES)
                upstream = grad_ref[rows, pl.ds(tile, LANES)].astype(f32)
                keep = low == (number != 1)
                upstream = jnp.where(keep, upstream, 0.0).astype(bf16)
                scores = dot_nt(key_ref[0:span, :], query)
                probs = jnp.exp(scores - total_ref[number, 0:1, rows])
                probs = jnp.where(allowed, probs, 0.0)
                prob_grad = dot_nt(value_ref[0:span, :], upstream)
                row_dot = jnp.sum(probs * prob_grad, axis=0, keepdims=True)
                score_grad = (probs * (prob_grad - row_dot)).astype(bf16)
                key_grad_ref[0:span, :] += dot(score_grad, query)
                value_grad_ref[0:span, :] += dot(probs.astype(bf16), upstream)
                query_grad_ref[number] = dot_tn(score_grad, key_ref[0:span, :]) * scale
                return carry

            lax.fori_loop(0, 3, head, 0)
            cosine, sine = cos_ref[rows, :], sin_ref[rows, :]
            pair = jnp.where(low, query_grad_ref[0], query_grad_ref[1])
            out_ref[rows, 0:LANES] = back(pair, cosine, sine).astype(bf16)
            out_ref[rows, LANES : 2 * LANES] = back(query_grad_ref[2], cosine, sine).astype(bf16)

    @pl.when(block == blocks - 1)
    def _():
        low = lane_of(key_grad_ref.shape) < HEAD_DIM
        key_grad = key_grad_ref[...]
        key_grad = key_grad + pltpu.roll(key_grad, HEAD_DIM, 1)
        key_grad = back(key_grad, cos_ref[...], sin_ref[...])
        before = out_ref[:, LANES : 2 * LANES].astype(f32)
        out_ref[:, LANES : 2 * LANES] = jnp.where(low, before, key_grad).astype(bf16)
        value_grad = value_grad_ref[...]
        value_grad = value_grad + pltpu.roll(value_grad, HEAD_DIM, 1)
        out_ref[:, 2 * LANES : 3 * LANES] = jnp.where(low, 0.0, value_grad).astype(bf16)
        chunk = 512
        own_sum_ref[...] = jnp.zeros_like(own_sum_ref)

        def add(index, carry):
            part = pl.ds(pl.multiple_of(index * chunk, chunk), chunk)
            own_sum_ref[...] += dot_tn(normed_ref[part, :], out_ref[part, :])
            return carry

        lax.fori_loop(0, out_ref.shape[0] // chunk, add, 0)
        own = own_sum_ref[...]
        own_ref[...] = own.astype(bf16)
        share = jnp.sum(own * w_ref[...].astype(f32), axis=1, keepdims=True) / gain_ref[...]
        share = jnp.transpose(jnp.broadcast_to(share, (share.shape[0], LANES)))[0:8, :]
        width = blocks_ref.shape[2]
        row = lax.broadcasted_iota(jnp.int32, (8, width), 0)
        terms = jnp.zeros((8, width), f32)
        for index in range(share.shape[1] // width):
            piece = share[:, index * width : (index + 1) * width]
            upper = piece.astype(bf16).astype(f32)
            terms = jnp.where(row == index, upper, jnp.where(row == index + 4, piece - upper, terms))
        terms = jnp.concatenate([terms, jnp.zeros((8, width), f32)], axis=0).astype(bf16)
        rows = blocks_ref.shape[1] - DOT_ROWS
        for index in range(blocks_ref.shape[0]):
            blocks_ref[index, 0:rows, :] = out_ref[index * rows : (index + 1) * rows, :]
            blocks_ref[index, rows:, :] = terms


def attend_back(query, key, value, grad, totals, start, cosine, sine, normed, w_natural, gain):
    total = key.shape[0]
    members = 2 * COLS
    rows = total // members + DOT_ROWS
    args = (query, key, value, grad, totals, start, cosine, sine, normed, w_natural, gain)
    return call(
        attend_back_kernel,
        (total // QUERY_BLOCK,),
        0,
        [whole(item.shape) for item in args],
        [whole((members, rows, 3 * LANES)), whole(w_natural.shape)],
        [struct((members, rows, 3 * LANES), bf16), struct(w_natural.shape, bf16)],
        scratch=[
            pltpu.VMEM((total, 3 * LANES), bf16),
            pltpu.VMEM((3, QUERY_BLOCK, LANES), f32),
            pltpu.VMEM((total, LANES), f32),
            pltpu.VMEM((total, LANES), f32),
            pltpu.VMEM(w_natural.shape, f32),
        ],
        us=0.5,
    )(*args)


def branch_operand(refs):
    rows = refs.shape[2]
    low = lane_of((rows, LANES)) < HEAD_DIM
    pairs, thirds = [], []
    for member in range(refs.shape[1]):
        one = refs[0, member, :, 0:LANES]
        mid = refs[0, member, :, LANES : 2 * LANES].astype(f32)
        end = refs[0, member, :, 2 * LANES : 3 * LANES].astype(f32)
        mid_turned = pltpu.roll(mid, HEAD_DIM, 1)
        end_turned = pltpu.roll(end, HEAD_DIM, 1)
        late = jnp.where(low, mid_turned, end_turned).astype(bf16)
        pairs.append(jnp.concatenate([one, late], axis=0))
        thirds.append((mid, end_turned))
    for member in range(0, refs.shape[1], 2):
        tops = []
        for which in range(2):
            left, right = thirds[member][which], thirds[member + 1][which]
            tops.append(jnp.where(low, left, pltpu.roll(right, HEAD_DIM, 1)).astype(bf16))
        pairs.append(jnp.concatenate(tops, axis=0))
    return jnp.concatenate(pairs, axis=1)


def branch_weights(ref):
    right = [ref[source, 0:LANES] for source in range(ref.shape[0])]
    return jnp.concatenate(right + [ref[source, LANES:] for source in range(ref.shape[0])], axis=0)


def hits_of(rank, local_experts):
    place = lax.broadcasted_iota(jnp.int32, (CAPACITY, rank.shape[1]), 0).astype(f32)
    return [place == rank[j : j + 1, :] for j in range(local_experts)]


def chosen_of(hits):
    return jnp.concatenate([jnp.where(hit, 1.0, 0.0).astype(bf16) for hit in hits], axis=0)


def middle_kernel(
    place_ref, att_mine_ref, att_other_ref, w_mine_ref, w_other_ref, tok_a_ref, tok_b_ref, routes_a_ref, routes_b_ref,
    gain_ref, w_router_ref, after_ref,
    x_ref, slot_gate_ref, rank_ref, gate_ref, normed_ref, middle_ref, gates_own_ref, gates_ref, ranks_ref
):
    step = pl.program_id(0)
    member = place_ref[2]
    cols = pl.num_programs(0)
    rows = tok_a_ref.shape[0]
    local_experts = x_ref.shape[0]
    branch = dot(branch_operand(att_mine_ref), branch_weights(w_mine_ref))
    branch = branch + dot(branch_operand(att_other_ref), branch_weights(w_other_ref))
    for half in range(2):
        tok_ref, routes_ref = ((tok_a_ref, routes_a_ref), (tok_b_ref, routes_b_ref))[half]
        middle = tok_ref[...].astype(f32) + branch[half * rows : (half + 1) * rows]
        inverse = lax.rsqrt(jnp.mean(middle * middle, axis=1, keepdims=True) + epsilon)
        normed = (middle * inverse * gain_ref[...]).astype(bf16)
        normed_ref[half, 0] = normed
        logits = dot_nt(w_router_ref[...], normed)
        padded = logits.shape[0]
        slot = lax.broadcasted_iota(jnp.int32, (padded, rows), 0)
        expert = (slot // 8) * local_experts + slot % 8
        expert = jnp.where(slot % 8 < local_experts, expert, -1).astype(f32)
        routes = routes_ref[0].astype(f32)
        named = expert == routes[0:1, 0:rows]
        for k in range(1, TOP):
            named = named | (expert == routes[k : k + 1, 0:rows])
        peak = jnp.max(jnp.where(named, logits, masked_score), axis=0, keepdims=True)
        weights = jnp.where(named, jnp.exp(logits - peak), 0.0)
        gates = weights / jnp.sum(weights, axis=0, keepdims=True)
        gates_ref[...] = gates
        ranks_ref[...] = jnp.where(named, dot(named.astype(f32).astype(bf16), after_ref[...]), -1.0)
        here = pl.ds(pl.multiple_of(member * 8, 8), 8)
        gate, rank = gates_ref[here, :], ranks_ref[here, :]
        rank_ref[half, 0] = rank
        gate_ref[half, 0] = gate
        hits = hits_of(rank, local_experts)
        slot_gate = jnp.concatenate(
            [jnp.sum(jnp.where(hit, gate[j : j + 1, :], 0.0), axis=1, keepdims=True) for j, hit in enumerate(hits)],
            axis=0,
        )
        chosen = chosen_of(hits)
        picked = dot(chosen, normed).astype(bf16)
        spread = jnp.broadcast_to(slot_gate, (slot_gate.shape[0], LANES))
        for j in range(local_experts):
            part = slice(j * CAPACITY, (j + 1) * CAPACITY)
            x_ref[j, half, 0] = picked[part]
            slot_gate_ref[j, half, 0] = spread[part]

        @pl.when(member == half * cols + step)
        def _(middle=middle, gates=gates):
            middle_ref[...] = middle
            gates_own_ref[...] = gates


def middle_and_dispatch(place, att, w_mine, w_other, tokens, routes, gain, w_router, local_experts):
    width = tokens.shape[1]
    half = COLS
    rows = tokens.shape[0] // (2 * half)
    padded = w_router.shape[0]
    after = jnp.asarray(np.triu(np.ones((rows, rows), np.float32), 1), bf16)
    slot_shape = (local_experts, 2, half, CAPACITY)
    early = pl.BlockSpec((rows, width), lambda i, p: (i, 0))
    late = pl.BlockSpec((rows, width), lambda i, p: (i + half, 0))
    routes_shape = (1,) + routes.shape[1:]
    return call(
        middle_kernel,
        (half,),
        1,
        [
            pl.BlockSpec((1, half, rows, 3 * LANES), lambda i, p: (p[0], 0, i, 0)),
            pl.BlockSpec((1, half, rows, 3 * LANES), lambda i, p: (1 - p[0], 0, i, 0)),
            whole(w_mine.shape),
            whole(w_other.shape),
            early,
            late,
            pl.BlockSpec(routes_shape, lambda i, p: (i, 0, 0)),
            pl.BlockSpec(routes_shape, lambda i, p: (i + half, 0, 0)),
            whole((1, width)),
            whole(w_router.shape),
            whole((rows, rows)),
        ],
        [
            pl.BlockSpec((local_experts, 2, 1, CAPACITY, width), lambda i, p: (0, 0, i, 0, 0)),
            pl.BlockSpec((local_experts, 2, 1, CAPACITY, LANES), lambda i, p: (0, 0, i, 0, 0)),
            pl.BlockSpec((2, 1, 8, rows), lambda i, p: (0, i, 0, 0)),
            pl.BlockSpec((2, 1, 8, rows), lambda i, p: (0, i, 0, 0)),
            pl.BlockSpec((2, 1, rows, width), lambda i, p: (0, i, 0, 0)),
            whole((rows, width)),
            whole((padded, rows)),
        ],
        [
            struct(slot_shape + (width,), bf16),
            struct(slot_shape + (LANES,), f32),
            struct((2, half, 8, rows), f32),
            struct((2, half, 8, rows), f32),
            struct((2, half, rows, width), bf16),
            struct((rows, width), f32),
            struct((padded, rows), f32),
        ],
        scratch=[pltpu.VMEM((padded, rows), f32), pltpu.VMEM((padded, rows), f32)],
        us=0.5,
    )(place, att, att, w_mine, w_other, tokens, tokens, routes, routes, gain, w_router, after)


def grad_dispatch_kernel(rank_ref, gate_ref, cot_ref, g_ref):
    local_experts = g_ref.shape[0]
    rows = cot_ref.shape[0] // 2
    for half in range(2):
        hits = hits_of(rank_ref[half], local_experts)
        gate = gate_ref[half]
        slot_gate = jnp.concatenate(
            [jnp.sum(jnp.where(hit, gate[j : j + 1, :], 0.0), axis=1, keepdims=True) for j, hit in enumerate(hits)],
            axis=0,
        )
        grads = (dot(chosen_of(hits), cot_ref[half * rows : (half + 1) * rows, :]) * slot_gate).astype(bf16)
        for j in range(local_experts):
            g_ref[j, half] = grads[j * CAPACITY : (j + 1) * CAPACITY]


def grad_dispatch(rank, gate, cotangents, local_experts):
    members, _, rows = rank.shape
    width = cotangents.shape[1]
    small = pl.BlockSpec((2, 8, rows), lambda j: (j, 0, 0))
    return call(
        grad_dispatch_kernel,
        (members // 2,),
        0,
        [small, small, pl.BlockSpec((2 * rows, width), lambda j: (j, 0))],
        pl.BlockSpec((local_experts, 2, CAPACITY, width), lambda j: (0, j, 0, 0)),
        struct((local_experts, members, CAPACITY, width), bf16),
        us=0.5,
    )(rank, gate, cotangents)


def expert_kernel(
    x_ref, gate_ref, w_gate_ref, w_up_ref, w_down_ref, forth_ref, active_ref, factor_ref, silu_ref
):
    gate_pre = dot(x_ref[0], w_gate_ref[0])
    up_pre = dot(x_ref[0], w_up_ref[0])
    sig = 1.0 / (1.0 + jnp.exp(-gate_pre))
    silu = gate_pre * sig
    silu_ref[0] = silu
    factor_ref[0] = up_pre * sig * (1.0 + gate_pre * (1.0 - sig))
    active_ref[0] = (silu * up_pre).astype(bf16)
    produced = dot_nt(active_ref[0], w_down_ref[0]).astype(bf16).astype(f32)
    forth_ref[0] = (produced * gate_ref[0, :, 0:1]).astype(bf16)


def run_experts(x, slot_gate, w_gate, w_up, w_down):
    count, slots, width = x.shape
    hidden = w_gate.shape[2]

    def per_expert(*shape):
        return pl.BlockSpec((1,) + shape, lambda e: (e, 0, 0))

    return call(
        expert_kernel,
        (count,),
        0,
        [per_expert(slots, width), per_expert(slots, LANES)] + [per_expert(width, hidden)] * 3,
        [per_expert(slots, width)] + [per_expert(slots, hidden)] * 3,
        [
            struct((count, slots, width), bf16),
            struct((count, slots, hidden), bf16),
            struct((count, slots, hidden), f32),
            struct((count, slots, hidden), f32),
        ],
        us=0.5,
    )(x, slot_gate, w_gate, w_up, w_down)


def expert_back_kernel(place_ref, *refs, fast):
    x_ref, g_ref, active_ref, factor_ref, silu_ref = refs[:5]
    w_gate_ref, w_up_ref, w_down_ref, back_ref, dots_ref = refs[5:10]
    grads, (gate_low_ref, up_low_ref) = refs[10:-2], refs[-2:]
    slots, width = g_ref.shape[1], g_ref.shape[2]
    chunk = 256
    active_grad = dot(g_ref[0], w_down_ref[0])
    gate_low_ref[...] = (active_grad * factor_ref[0]).astype(bf16)
    up_low_ref[...] = (active_grad * silu_ref[0]).astype(bf16)
    dots = jnp.sum(active_ref[0].astype(f32) * active_grad, axis=1, keepdims=True)
    dots_ref[0] = jnp.broadcast_to(dots, (slots, LANES))
    back_ref[0] = (dot_nt(gate_low_ref[...], w_gate_ref[0]) + dot_nt(up_low_ref[...], w_up_ref[0])).astype(bf16)

    def products(cols):
        x = x_ref[0, :, cols]
        yield 0, dot_tn(x, gate_low_ref[...]).astype(bf16)
        yield 1, dot_tn(x, up_low_ref[...]).astype(bf16)
        yield 2, dot_tn(g_ref[0, :, cols], active_ref[0]).astype(bf16)

    if fast:
        write_shards(place_ref, grads, products, width)
    else:

        def whole_columns(index, carry):
            cols = pl.ds(pl.multiple_of(index * chunk, chunk), chunk)
            for which, product in products(cols):
                grads[which][0, cols, :] = product
            return carry

        lax.fori_loop(0, width // chunk, whole_columns, 0)


def write_shards(place_ref, outs, products, width):
    send_a, keep_a, send_b, keep_b = outs
    x_bit, y_bit = place_ref[3], place_ref[4]
    shard = width // 4
    for dy in range(2):
        for dx in range(2):
            x, y = x_bit ^ dx, y_bit ^ dy
            cols = pl.ds(pl.multiple_of((y * 2 + x) * shard, shard), shard)
            for which, product in products(cols):
                side = product.shape[1] // 2
                (send_a if dx else keep_a)[0, which, y] = product[:, :side]
                (send_b if dy else keep_b)[0, which, x] = product[:, side:]


def run_experts_back(place, x, g, active, factor, silu, w_gate, w_up, w_down, first, count, fast):
    slots, width = g.shape[1], g.shape[2]
    hidden = w_gate.shape[2]

    def taken(*shape):
        return pl.BlockSpec((1,) + shape, lambda e, p: (e + first, 0, 0))

    def given(*shape):
        zeros = (0,) * len(shape)
        return pl.BlockSpec((1,) + shape, lambda e, p: (e,) + zeros)

    if fast:
        grad_shapes = [(3, 2, width // 4, hidden // 2)] * 4
    else:
        grad_shapes = [(width, hidden)] * 3
    return call(
        lambda *refs: expert_back_kernel(*refs, fast=fast),
        (count,),
        1,
        [taken(slots, width)] * 2 + [taken(slots, hidden)] * 3 + [taken(width, hidden)] * 3,
        [given(slots, width), given(slots, LANES)] + [given(*shape) for shape in grad_shapes],
        [struct((count, slots, width), bf16), struct((count, slots, LANES), f32)]
        + [struct((count,) + shape, bf16) for shape in grad_shapes],
        scratch=[pltpu.VMEM((slots, hidden), bf16)] * 2,
        us=0.5,
    )(place, x, g, active, factor, silu, w_gate, w_up, w_down)


DOT_LANES = 2 * LANES


def combine_kernel(place_ref, rank_ref, *refs, pieces, with_dots, mine):
    parts, rest = refs[:pieces], refs[pieces:]
    rows = rank_ref.shape[2]
    local_experts = sum(part.shape[0] for part in parts)
    hits = hits_of(rank_ref[0], local_experts)
    gathered = jnp.concatenate([part[j, 0] for part in parts for j in range(part.shape[0])], axis=0)
    summed = dot_tn(chosen_of(hits), gathered)
    out_ref = rest[-1]
    if mine:
        arrived_ref = rest[-2]
        summed = summed + arrived_ref[0, 0:rows, :].astype(f32)
    out_ref[0, 0:rows, :] = summed.astype(bf16)
    if with_dots:
        column = [part[j, 0][:, 0:1] for part in rest[:pieces] for j in range(part.shape[0])]
        scattered = [
            jnp.sum(jnp.where(hit, value, 0.0), axis=0, keepdims=True) for hit, value in zip(hits, column)
        ]
        scattered.append(jnp.zeros((DOT_ROWS - local_experts, rows), f32))
        scattered = jnp.concatenate(scattered, axis=0)
        upper = scattered.astype(bf16)
        out_ref[0, rows:, :] = jnp.zeros((DOT_ROWS, out_ref.shape[2]), bf16)
        out_ref[0, rows:, 0:rows] = upper
        out_ref[0, rows:, DOT_LANES : DOT_LANES + rows] = (scattered - upper.astype(f32)).astype(bf16)
        if mine:
            out_ref[0, rows:, 2 * DOT_LANES : 4 * DOT_LANES] = arrived_ref[0, rows:, 0 : 2 * DOT_LANES]


def combine(place, rank, parts, dots=None, arrived=None):
    mine = arrived is not None
    rows, width = rank.shape[2], parts[0].shape[-1]
    out_rows = rows + (DOT_ROWS if dots else 0)

    def member(step, p):
        return (p[0] if mine else 1 - p[0]) * COLS + step

    def slots_of(array):
        return pl.BlockSpec((array.shape[0], 1) + array.shape[2:], lambda j, p: (0, member(j, p), 0, 0))

    inputs = [
        part.reshape(part.shape[0], 2 * COLS, CAPACITY, part.shape[-1]) for part in list(parts) + list(dots or [])
    ]
    in_specs = [pl.BlockSpec((1, 8, rows), lambda j, p: (member(j, p), 0, 0))] + [slots_of(item) for item in inputs]
    by_chip = pl.BlockSpec((1, out_rows, width), lambda j, p: (j, 0, 0))
    if mine:
        inputs.append(arrived)
        in_specs.append(by_chip)
    return call(
        lambda *refs: combine_kernel(*refs, pieces=len(parts), with_dots=bool(dots), mine=mine),
        (COLS,),
        1,
        in_specs,
        by_chip,
        struct((COLS, out_rows, width), bf16),
        us=0.5,
    )(place, rank, *inputs)


def split_dot(dimension_numbers, values, exact):
    upper = values.astype(bf16)
    lower = (values - upper.astype(f32)).astype(bf16)
    return lax.dot_general(
        upper, exact, dimension_numbers, preferred_element_type=f32
    ) + lax.dot_general(lower, exact, dimension_numbers, preferred_element_type=f32)


EXTRA_SLOTS = 6


def middle_back_kernel(
    place_ref, sums_ref, gates_ref, middle_ref, cot_ref, gain_ref, w_router_ref, w_mine_ref, w_other_ref,
    grad_ref, branch_ref, attended_ref, extra_ref
):
    rows = middle_ref.shape[0]
    tail = sums_ref[:, rows : rows + 8, 0 : 4 * DOT_LANES].astype(f32)
    mine = tail[:, :, 0:rows] + tail[:, :, DOT_LANES : DOT_LANES + rows]
    other = tail[:, :, 2 * DOT_LANES : 2 * DOT_LANES + rows] + tail[:, :, 3 * DOT_LANES : 3 * DOT_LANES + rows]
    first_row = place_ref[0] == 0
    dots = jnp.concatenate([jnp.where(first_row, mine, other), jnp.where(first_row, other, mine)], axis=0)
    dots = dots.reshape(dots.shape[0] * 8, rows)
    gates = gates_ref[...]
    logit_grad = dots - gates * jnp.sum(dots, axis=0, keepdims=True)
    middle = middle_ref[...]
    inverse = lax.rsqrt(jnp.mean(middle * middle, axis=1, keepdims=True) + epsilon)
    unit = middle * inverse
    gain = gain_ref[...]
    grad = sums_ref[0, 0:rows].astype(f32)
    for index in range(1, sums_ref.shape[0]):
        grad = grad + sums_ref[index, 0:rows].astype(f32)
    grad = grad + split_dot(TN, logit_grad, w_router_ref[...])
    gain_grad = jnp.sum(grad * unit, axis=0, keepdims=True)
    scaled = grad * gain
    middle_grad = cot_ref[...].astype(f32) + inverse * (
        scaled - unit * jnp.mean(scaled * unit, axis=1, keepdims=True)
    )
    grad_ref[...] = middle_grad
    branch_grad = middle_grad.astype(bf16)
    branch_ref[0:rows, :] = branch_grad
    extra_ref[...] = jnp.zeros_like(extra_ref)
    for index in range(logit_grad.shape[0] // 8):
        first, lane = index // EXTRA_SLOTS * 8, index % EXTRA_SLOTS * DOT_LANES
        extra_ref[first : first + 8, lane : lane + rows] = logit_grad[index * 8 : index * 8 + 8]
    upper = gain_grad.astype(bf16).astype(f32)
    extra_ref[13:14, :] = upper
    extra_ref[14:15, :] = gain_grad - upper
    branch_ref[rows:, :] = extra_ref[...].astype(bf16)
    for which, ref in enumerate((w_mine_ref, w_other_ref)):
        line = place_ref[0] if which == 0 else 1 - place_ref[0]
        for col in range(ref.shape[0]):
            product = dot_nt(branch_grad, ref[col])
            member = line * COLS + col
            attended_ref[member, :, 0:LANES] = product[:, 0:LANES].astype(bf16)
            attended_ref[member, :, LANES : LANES + HEAD_DIM] = product[:, LANES:].astype(bf16)
            attended_ref[member, :, LANES + HEAD_DIM :] = jnp.zeros((product.shape[0], HEAD_DIM), bf16)


def middle_back(place, sums, gates, middle, cotangent, gain, w_router, w_mine, w_other):
    rows, width = middle.shape
    members = 2 * COLS
    args = (sums, gates, middle, cotangent, gain, w_router, w_mine, w_other)
    return call(
        middle_back_kernel,
        (1,),
        1,
        [whole(item.shape) for item in args],
        [whole((rows, width)), whole((rows + DOT_ROWS, width)), whole((members, rows, 2 * LANES))],
        [
            struct((rows, width), f32),
            struct((rows + DOT_ROWS, width), bf16),
            struct((members, rows, 2 * LANES), bf16),
        ],
        scratch=[pltpu.VMEM((DOT_ROWS, width), f32)],
        us=0.5,
    )(place, *args)


def input_grad_kernel(
    place_ref, grads_mine_ref, grads_other_ref, mine_a_ref, mine_b_ref, other_a_ref, other_b_ref,
    tok_ref, middle_grad_ref, gain_ref, out_ref, share_ref, sum_ref
):
    step = pl.program_id(0)
    first = place_ref[4] == 0

    def weights(a_ref, b_ref):
        a = jnp.concatenate([a_ref[index, 0] for index in range(a_ref.shape[0])], axis=0)
        b = jnp.concatenate([b_ref[index, 0] for index in range(b_ref.shape[0])], axis=0)
        upper, lower = jnp.where(first, a, b), jnp.where(first, b, a)
        return jnp.concatenate([upper, lower, lower[lower.shape[0] - HEAD_DIM :]], axis=0)

    rows = tok_ref.shape[0]
    part = dot(grads_mine_ref[0, 0:rows, :], weights(mine_a_ref, mine_b_ref))
    part = part + dot(grads_other_ref[0, 0:rows, :], weights(other_a_ref, other_b_ref))
    share = grads_mine_ref[0, rows:, :].astype(f32)[0:8] + grads_other_ref[0, rows:, :].astype(f32)[0:8]

    @pl.when(step == 0)
    def _():
        sum_ref[...] = part
        share_ref[...] = share

    @pl.when(step > 0)
    def _():
        sum_ref[...] += part
        share_ref[...] += share

    @pl.when(step == pl.num_programs(0) - 1)
    def _():
        resid = tok_ref[...].astype(f32)
        inverse = lax.rsqrt(jnp.mean(resid * resid, axis=1, keepdims=True) + epsilon)
        unit = resid * inverse
        scaled = sum_ref[...] * gain_ref[...]
        out_ref[...] = middle_grad_ref[...] + inverse * (
            scaled - unit * jnp.mean(scaled * unit, axis=1, keepdims=True)
        )


def input_grad(place, grads, weights, tokens, middle_grad, gain):
    rows, width = tokens.shape
    lanes = grads.shape[2]
    w_shape = (weights[0].shape[0], 1) + weights[0].shape[2:]
    return call(
        input_grad_kernel,
        (COLS,),
        1,
        [
            pl.BlockSpec((1, rows + DOT_ROWS, lanes), lambda c, p: (p[0] * COLS + c, 0, 0)),
            pl.BlockSpec((1, rows + DOT_ROWS, lanes), lambda c, p: ((1 - p[0]) * COLS + c, 0, 0)),
        ]
        + [pl.BlockSpec(w_shape, lambda c, p: (0, c, 0, 0))] * 4
        + [whole((rows, width)), whole((rows, width)), whole((1, width))],
        [whole((rows, width)), whole((8, lanes))],
        [struct((rows, width), f32), struct((8, lanes), f32)],
        scratch=[pltpu.VMEM((rows, width), f32)],
        us=0.5,
    )(place, grads, grads, *weights, tokens, middle_grad, gain)


def out_weights_kernel(place_ref, branch_ref, att_ref, normed_ref, own_ref, *refs, fast, local_experts):
    outs, small_ref, (sum_ref, gain_sum_ref) = refs[:-3], refs[-3], refs[-2:]
    step = pl.program_id(0)
    rows = att_ref.shape[0] // 2
    block = rows + DOT_ROWS

    @pl.when(step == 0)
    def _():
        sum_ref[...] = jnp.zeros_like(sum_ref)
        small_ref[...] = jnp.zeros_like(small_ref)
        gain_sum_ref[...] = jnp.zeros_like(gain_sum_ref)

    branch = jnp.concatenate([branch_ref[0:rows, :], branch_ref[block : block + rows, :]], axis=0)
    sum_ref[...] += dot_tn(branch, att_ref[...])
    for which in range(2):
        tail = branch_ref[which * block + rows : (which + 1) * block, :].astype(f32)
        slots = []
        for index in range(small_ref.shape[0] // 8):
            first, lane = index // EXTRA_SLOTS * 8, index % EXTRA_SLOTS * DOT_LANES
            slots.append(tail[first : first + 8, lane : lane + rows])
        logit_grad = jnp.concatenate(slots, axis=0)
        real = lax.broadcasted_iota(jnp.int32, logit_grad.shape, 0) % 8 < local_experts
        logit_grad = jnp.where(real, logit_grad, 0.0).astype(bf16)
        small_ref[...] += dot(logit_grad, normed_ref[which * rows : (which + 1) * rows, :])
        gain_sum_ref[...] += tail[8:16, :]

    @pl.when(step == pl.num_programs(0) - 1)
    def _():
        small_ref[7:8, :] = gain_sum_ref[5:6, :] + gain_sum_ref[6:7, :]

        def products(cols):
            own = own_ref[cols, 0 : 2 * LANES]
            out_one = sum_ref[cols, 0:LANES].astype(bf16)
            out_two = sum_ref[cols, LANES:]
            low = lane_of(out_two.shape) < HEAD_DIM
            tail = jnp.where(low, out_two, own_ref[cols, 2 * LANES :].astype(f32)).astype(bf16)
            yield 0, jnp.concatenate([own, out_one, tail], axis=1)

        if fast:
            write_shards(place_ref, outs, products, own_ref.shape[0])
        else:
            outs[0][...] = next(products(slice(0, own_ref.shape[0])))[1]


def out_weights(place, branch, attended, normed, own, padded, local_experts, fast):
    total, width = normed.shape
    rows = total // COLS
    blocks = branch.shape[0] // COLS
    if fast:
        shapes = [(1, 1, 2, width // 4, 2 * LANES)] * 4
    else:
        shapes = [(width, 4 * LANES)]
    return call(
        lambda *refs: out_weights_kernel(*refs, fast=fast, local_experts=local_experts),
        (COLS,),
        1,
        [
            pl.BlockSpec((blocks, width), lambda j, p: (j, 0)),
            pl.BlockSpec((rows, 2 * LANES), lambda j, p: (j, 0)),
            pl.BlockSpec((rows, width), lambda j, p: (j, 0)),
            whole(own.shape),
        ],
        [whole(shape) for shape in shapes] + [whole((padded, width))],
        [struct(shape, bf16) for shape in shapes] + [struct((padded, width), f32)],
        scratch=[pltpu.VMEM((width, 2 * LANES), f32), pltpu.VMEM((8, width), f32)],
        us=0.5,
    )(place, branch, attended, normed, own)


def first_sum_kernel(place_ref, keep_a_ref, got_a_ref, keep_b_ref, got_b_ref, *rest):
    send_a_ref, held_a_ref, send_b_ref, held_b_ref = rest[-4:]
    x_bit, y_bit = place_ref[3], place_ref[4]
    for bit, keep, got, send, held in (
        (y_bit, keep_a_ref, got_a_ref, send_a_ref, held_a_ref),
        (x_bit, keep_b_ref, got_b_ref, send_b_ref, held_b_ref),
    ):
        for kind in range(keep.shape[1]):
            held[0, kind] = (keep[0, kind, bit].astype(f32) + got[0, kind, bit].astype(f32)).astype(bf16)
            send[0, kind] = (keep[0, kind, 1 - bit].astype(f32) + got[0, kind, 1 - bit].astype(f32)).astype(bf16)


def first_sum(place, chunk, first=0, total=None, before=None):
    count, kinds, _, rows, cols = chunk[0].shape
    taken = pl.BlockSpec((1, kinds, 2, rows, cols), lambda e, p: (e, 0, 0, 0, 0))
    given = pl.BlockSpec((1, kinds, rows, cols), lambda e, p: (e + first, 0, 0, 0))
    extra = list(before) if before else []
    return call(
        first_sum_kernel,
        (count,),
        1,
        [taken] * 4 + [pl.BlockSpec(memory_space=pl.ANY)] * len(extra),
        [given] * 4,
        [struct((total or count, kinds, rows, cols), bf16)] * 4,
        us=0.5,
        aliases={5 + i: i for i in range(len(extra))},
    )(place, *chunk, *extra)


def last_sum_kernel(held_a_ref, got_a_ref, held_b_ref, got_b_ref, *rest):
    outs = rest[-3:]
    side = held_a_ref.shape[3]
    for which, out in enumerate(outs):
        out[0, :, :side] = held_a_ref[0, which].astype(f32) + got_a_ref[0, which].astype(f32)
        out[0, :, side:] = held_b_ref[0, which].astype(f32) + got_b_ref[0, which].astype(f32)


def last_sum(held_a, got_a, held_b, got_b, first, total, before):
    count, kinds, rows, cols = held_a.shape
    taken = pl.BlockSpec((1, kinds, rows, cols), lambda e: (e, 0, 0, 0))
    given = pl.BlockSpec((1, rows, 2 * cols), lambda e: (e + first, 0, 0))
    extra = list(before) if before else []
    return call(
        last_sum_kernel,
        (count,),
        0,
        [taken] * 4 + [pl.BlockSpec(memory_space=pl.ANY)] * len(extra),
        [given] * 3,
        [struct((total, rows, 2 * cols), f32)] * 3,
        us=0.5,
        aliases={4 + i: i for i in range(len(extra))},
    )(held_a, got_a, held_b, got_b, *extra)


def last_weights_kernel(held_a_ref, got_a_ref, held_b_ref, got_b_ref, query_ref, key_ref, value_ref, out_ref):
    left = held_a_ref[0, 0].astype(f32) + got_a_ref[0, 0].astype(f32)
    right = held_b_ref[0, 0].astype(f32) + got_b_ref[0, 0].astype(f32)
    cut = query_ref.shape[1]
    query_ref[...] = left[:, :cut]
    key_ref[...] = left[:, cut:]
    out_ref[...] = right[:, :cut]
    value_ref[...] = right[:, cut:]


def last_weights(parts, widths):
    rows = parts[0].shape[2]
    shapes = [(rows, width) for width in widths]
    return call(
        last_weights_kernel,
        (1,),
        0,
        [whole(part.shape) for part in parts],
        [whole(shape) for shape in shapes],
        [struct(shape, f32) for shape in shapes],
        us=0.5,
    )(*parts)


SWAP = [(0, 1), (1, 0)]


def after(value, *events):
    return lax.optimization_barrier((value,) + events)[0]


def gather_group(block):
    return lax.all_gather(block, ("row", "col"), axis=0, tiled=True)


def line_pieces(value):
    parts = [value]
    for distance in range(1, COLS):
        parts.insert(0, lax.ppermute(value, "col", [(i, (i + distance) % COLS) for i in range(COLS)]))
    return parts


def in_line_order(parts):
    parts = jnp.stack(parts + parts)
    return lax.dynamic_slice_in_dim(parts, COLS - 1 - lax.axis_index("col"), COLS, axis=0)


def flip(value, axis, bit, size):
    return lax.ppermute(value, axis, [(i, i ^ (1 << bit)) for i in range(size)])


def bits_of(size):
    return size.bit_length() - 1


def own_bit(axis, bit):
    return (lax.axis_index(axis) >> bit) & 1


def joined(mine, got, own):
    return jnp.where(own == 0, jnp.concatenate([mine, got]), jnp.concatenate([got, mine]))


def cube_step(value, axis, bit, size):
    return joined(value, flip(value, axis, bit, size), own_bit(axis, bit))


def lines_first(value):
    return jnp.transpose(value, (1, 0, 2, 3)).reshape(value.shape[1], value.shape[0] * value.shape[2], value.shape[3])


def cube_gather(value, axis, size):
    value = value[None]
    for bit in range(bits_of(size)):
        value = cube_step(value, axis, bit, size)
    return value


def sum_dp(value, sizes):
    for bit in range(bits_of(sizes["dp"])):
        value = value + flip(value, "dp", bit, sizes["dp"])
    return value


def reduce_over_dp(value, size):
    count = bits_of(size)
    value = value.reshape(value.shape[:1] + (2,) * count + value.shape[2:])
    current = value
    for bit in range(count - 1, -1, -1):
        own = own_bit("dp", bit)
        keep = lax.dynamic_index_in_dim(current, own, 1, keepdims=False)
        send = lax.dynamic_index_in_dim(current, 1 - own, 1, keepdims=False).astype(bf16)
        current = keep.astype(f32) + flip(send, "dp", bit, size).astype(f32)
    return current


def start_move(run, size):
    return flip(run[0], "dp", 0, size), flip(run[2], "dp", 1, size)


def second_move(sums, size):
    send_a, held_a, send_b, held_b = sums
    return held_a, flip(send_a, "dp", 1, size), held_b, flip(send_b, "dp", 0, size)


def layer(sizes):
    n_dp, n_row, n_col = sizes["dp"], sizes["row"], sizes["col"]
    members = n_row * n_col
    fast = n_dp == 4
    assert n_row == 2 and n_col == COLS and n_dp & (n_dp - 1) == 0

    def local(
        tokens, cotangent, routes, lengths, gain_attn, w_query, w_key, w_value, w_out,
        gain_moe, w_router, w_gate, w_up, w_down,
    ):
        rows, width = tokens.shape
        group = rows * members
        local_experts = w_gate.shape[0]
        row, col, dp = lax.axis_index("row"), lax.axis_index("col"), lax.axis_index("dp")
        place = jnp.stack([row, col, row * n_col + col, dp & 1, (dp >> 1) & 1]).astype(jnp.int32)
        gain_one = gain_attn.astype(f32)[None]
        gain_two = gain_moe.astype(f32)[None]

        tok_all = gather_group(tokens)
        w_in = jnp.concatenate([w_query.T, w_key.T, w_value.T], axis=0)
        out_share, in_share = rows // n_dp, w_in.shape[0] // n_dp
        shares = jnp.concatenate(
            [
                lax.dynamic_slice(w_out.T, (dp * out_share, 0), (out_share, width)),
                lax.dynamic_slice(w_in, (dp * in_share, 0), (in_share, width)),
                jnp.pad(routes.T.astype(bf16).reshape(1, TOP * rows), ((0, 7), (0, width - TOP * rows))),
            ],
            axis=0,
        )
        w_stack = jnp.concatenate([w_query.T, w_key.T, w_value.T, w_value.T], axis=0)
        w_natural = jnp.concatenate([w_query, w_key, w_value, w_value], axis=1)

        ends = jnp.cumsum(lengths[0])
        starts = ends - lengths[0]
        position = jnp.arange(group, dtype=jnp.int32)
        segment = jnp.sum((position[:, None] >= ends[None, :]).astype(jnp.int32), axis=1)
        member = segment[:, None] == jnp.arange(starts.shape[0], dtype=jnp.int32)[None, :]
        start = jnp.sum(jnp.where(member, starts[None, :], 0), axis=1).astype(jnp.int32)
        frequency = rope_base ** (-2.0 * jnp.arange(HEAD_DIM // 2, dtype=f32) / HEAD_DIM)
        angle = (position - start).astype(f32)[:, None] * frequency[None, :]
        cosine = jnp.tile(jnp.cos(angle), (1, 4))
        sine = jnp.tile(jnp.sin(angle), (1, 4))

        w_router_rows = w_router.T.reshape(members, local_experts, width)
        w_router_rows = jnp.pad(w_router_rows, ((0, 0), (0, 8 - local_experts), (0, 0)))
        w_router_rows = w_router_rows.reshape(members * 8, width)
        start_row = jnp.broadcast_to(start[None, :], (8, group))
        start = start[:, None]
        gain_column = gain_attn.astype(f32)[:, None]
        ready = (place, gain_one, gain_two, w_stack, w_natural, cosine, sine, w_router_rows, start, start_row, gain_column)
        shares, place, gain_one, gain_two, w_stack, w_natural, cosine, sine, w_router_rows, start, start_row, gain_column = (
            lax.optimization_barrier((shares,) + ready)
        )
        shares = line_pieces(after(shares, tok_all, cosine))

        query, key, value, normed_one = project(tok_all, gain_one, w_stack, cosine, sine)
        packed, attended, totals = attend(query, key, value, start)
        att_flat = gather_group(packed)
        att_all = att_flat.reshape((n_row, n_col) + packed.shape)
        shares = in_line_order(after(shares, packed))
        route_rows = shares[:, out_share + in_share]
        w_out_mine, in_part = shares[None, :, :out_share], shares[None, :, out_share : out_share + in_share]
        for bit in range(bits_of(n_dp)):
            w_out_mine = cube_step(w_out_mine, "dp", bit, n_dp)
        in_part = cube_step(in_part, "dp", 0, n_dp)
        w_out_mine = lines_first(w_out_mine)
        w_out_other = lax.ppermute(after(w_out_mine, in_part), "row", SWAP)
        route_rows = cube_gather(route_rows, "row", n_row)[:, :, : TOP * rows].reshape(members, TOP, rows)
        cot_all = gather_group(after(cotangent, w_out_other))
        x, slot_gate, rank, gate, normed_two, middle, gates = middle_and_dispatch(
            place, att_all, w_out_mine, w_out_other, tok_all, route_rows, gain_two, w_router_rows, local_experts
        )
        slots = members * CAPACITY
        x = x.reshape(local_experts, slots, width)
        slot_gate = slot_gate.reshape(local_experts, slots, LANES)
        rank, gate = rank.reshape(members, 8, rows), gate.reshape(members, 8, rows)
        forth, active, factor, silu = run_experts(x, slot_gate, w_gate, w_up, w_down)
        for bit in range(1, bits_of(n_dp) - 1):
            in_part = cube_step(in_part, "dp", bit, n_dp)
        last_bit = bits_of(n_dp) - 1
        in_got = after(flip(in_part, "dp", last_bit, n_dp), forth)
        forth_other = combine(place, after(rank, in_got), [forth])
        arrived = lax.ppermute(forth_other, "row", SWAP)
        g = grad_dispatch(after(rank, forth_other), gate, cot_all, local_experts)
        g = g.reshape(local_experts, slots, width)
        cuts = [0, 2, 4, local_experts]

        def backward(which, x):
            first, last = cuts[which], cuts[which + 1]
            return run_experts_back(place, x, g, active, factor, silu, w_gate, w_up, w_down, first, last - first, fast)

        runs = [backward(0, x)]
        forth_mine = combine(place, rank, [forth], arrived=after(arrived, runs[0][1]))
        forth_sums = lax.all_to_all(forth_mine, "col", 0, 0, tiled=True)
        runs.append(backward(1, after(x, forth_mine)))
        runs.append(backward(2, after(x, runs[1][1])))
        moved = [start_move(run[2:], n_dp) for run in runs] if fast else []
        back_parts, dot_parts = [run[0] for run in runs], [run[1] for run in runs]
        back_other = combine(place, after(rank, *moved[0]) if fast else rank, back_parts, dot_parts)
        arrived = lax.ppermute(back_other, "row", SWAP)
        back_mine = combine(place, rank, back_parts, dot_parts, arrived)
        back_mine = after(back_mine, forth_sums)
        back_sums = lax.all_to_all(back_mine, "col", 0, 0, tiled=True)

        if fast:
            w_in_parts = [in_part, in_got]
        else:
            own = own_bit("dp", last_bit)
            w_in_rows = lines_first(joined(in_part, in_got, own))[None]
            half = w_in_rows.shape[2] // 2
            upper, lower = w_in_rows[:, :, :half], w_in_rows[:, :, half:]
            w_in_parts = [jnp.where(place[4] == 0, upper, lower), jnp.where(place[4] == 0, lower, upper)]
        if fast:

            def chunk_of(which, *events):
                keep_a, keep_b = after((runs[which][3], runs[which][5]), *events)
                return keep_a, moved[which][0], keep_b, moved[which][1]

            sums = first_sum(place, chunk_of(0, back_mine), cuts[0], cuts[2])
            gate_middle = (sums[1],) + moved[1]
        else:
            gate_middle = ()
        w_in_parts += [lax.ppermute(after(part, back_mine), "row", SWAP) for part in w_in_parts]

        middle_grad, branch_grad, attended_grad = middle_back(
            place, back_sums, gates, middle, cotangent, after(gain_two, *w_in_parts[2:], *gate_middle),
            w_router_rows, w_out_mine, w_out_other,
        )
        if fast:
            sums = first_sum(place, chunk_of(1, branch_grad), cuts[1], cuts[2], sums)
            started = [second_move(sums, n_dp)]
        attended_grad = lax.all_to_all(attended_grad, ("row", "col"), 0, 0, tiled=True)
        if fast:
            attended_grad = after(attended_grad, sums[1])
        branch_all = gather_group(after(branch_grad, attended_grad))

        attended_grad = attended_grad.reshape(group, 2 * LANES)
        if fast:
            attended_grad = after(attended_grad, *moved[2])
        projected_grad, own_grads = attend_back(
            query, key, value, attended_grad, totals, start_row, cosine, sine, normed_one, w_natural, gain_column
        )
        projected_all = lax.all_to_all(projected_grad, ("row", "col"), 0, 0, tiled=True)
        if fast:
            started.append(second_move(first_sum(place, chunk_of(2, own_grads, started[0][1], started[0][3])), n_dp))
            normed_two = after(normed_two, started[1][1], started[1][3])
        *w_parts, small = out_weights(
            place, branch_all, attended, normed_two.reshape(group, width), own_grads,
            members * 8, local_experts, fast,
        )
        expert_grads = None
        if fast:
            w_moved = start_move(w_parts, n_dp)
            held_a, got_a, held_b, got_b = started[0]
            held_a, held_b = after((held_a, held_b), small)
            expert_grads = last_sum(held_a, got_a, held_b, got_b, 0, local_experts, None)
        else:
            cut = w_parts[0].reshape(1, n_dp, width // n_dp, w_parts[0].shape[1])
            w_sum = reduce_over_dp(cut, n_dp)[0]

        mixed = (middle + jnp.sum(after(forth_sums, projected_grad).astype(f32), axis=0)).astype(bf16)

        used = small.reshape(members, 8, width)[:, :local_experts].reshape(members * local_experts, width)
        both = sum_dp(jnp.concatenate([used, small[7:8]], axis=0), sizes)
        w_router_grad = both[: members * local_experts].T
        gain_moe_grad = both[members * local_experts]

        tokens_grad, share = input_grad(
            place, projected_all, w_in_parts, tokens, middle_grad, after(gain_one, w_parts[0])
        )
        gain_attn_grad = sum_dp((share[0:4] + share[4:8]).reshape(8, width // 8), sizes).reshape(width)

        local_q, local_k = w_query.shape[1], w_key.shape[1]
        if fast:
            expert_grads = last_sum(*started[1], cuts[2], local_experts, expert_grads)
            w_sums = second_move(
                first_sum(place, (w_parts[1], w_moved[0], w_parts[3], w_moved[1])), n_dp
            )
            w_query_grad, w_key_grad, w_value_grad, w_out_grad = last_weights(
                w_sums, (local_q, local_k, local_k, local_q)
            )
        else:
            expert_grads = []
            for which in range(3):
                parts = [run[2 + which] for run in runs]
                parts = [part.reshape(part.shape[0], n_dp, width // n_dp, part.shape[2]) for part in parts]
                expert_grads.append(jnp.concatenate([reduce_over_dp(part, n_dp) for part in parts], axis=0))
            cut = local_q + local_k
            w_query_grad, w_key_grad = w_sum[:, :local_q], w_sum[:, local_q:cut]
            w_out_grad, w_value_grad = w_sum[:, cut : cut + local_q], w_sum[:, cut + local_q :]
        w_gate_grad, w_up_grad, w_down_grad = expert_grads
        return (
            mixed, tokens_grad, gain_attn_grad, w_query_grad, w_key_grad, w_value_grad, w_out_grad,
            gain_moe_grad, w_router_grad, w_gate_grad, w_up_grad, w_down_grad,
        )

    return local


def solution(mesh):
    return jax.shard_map(
        layer(dict(mesh.shape)),
        mesh=mesh,
        in_specs=(
            P(("dp", "row", "col"), None),
            P(("dp", "row", "col"), None),
            P(("dp", "row", "col"), None),
            P("dp", None),
            P(),
            P(None, ("row", "col")),
            P(None, ("row", "col")),
            P(None, ("row", "col")),
            P(None, ("row", "col")),
            P(),
            P(),
            P(("row", "col"), None, None),
            P(("row", "col"), None, None),
            P(("row", "col"), None, None),
        ),
        out_specs=(
            P(("dp", "row", "col"), None),
            P(("dp", "row", "col"), None),
            P(),
            P("dp", ("row", "col")),
            P("dp", ("row", "col")),
            P("dp", ("row", "col")),
            P("dp", ("row", "col")),
            P(),
            P(),
            P(("row", "col"), "dp", None),
            P(("row", "col"), "dp", None),
            P(("row", "col"), "dp", None),
        ),
        check_vma=False,
    )
```

```python
import math

import jax
import jax.numpy as jnp
import numpy as np
from jax import lax
from jax.experimental import pallas as pl
from jax.experimental.pallas import tpu as pltpu
from jax.sharding import PartitionSpec as P

HEAD_DIM = 64
EXPERTS = 40
TOP = 8
CAPACITY = 64
COLS = 4
LANES = 128
QUERY_BLOCK = 256
DOT_ROWS = 16

epsilon = 1e-06
rope_base = 10000.0
masked_score = -1e30
f32 = jnp.float32
bf16 = jnp.bfloat16
VMEM_LIMIT = 56 * 1024 * 1024

NT = (((1,), (1,)), ((), ()))
TN = (((0,), (0,)), ((), ()))


def dot(a, b):
    return jnp.dot(a, b, preferred_element_type=f32)


def dot_nt(a, b):
    return lax.dot_general(a, b, NT, preferred_element_type=f32)


def dot_tn(a, b):
    return lax.dot_general(a, b, TN, preferred_element_type=f32)


def lane_of(shape):
    return lax.broadcasted_iota(jnp.int32, shape, len(shape) - 1)


def call(
    kernel, grid, prefetch, in_specs, out_specs, out_shape, scratch=(), us=1.0, aliases=None
):
    return pl.pallas_call(
        kernel,
        grid_spec=pltpu.PrefetchScalarGridSpec(
            num_scalar_prefetch=prefetch,
            grid=grid,
            in_specs=in_specs,
            out_specs=out_specs,
            scratch_shapes=list(scratch),
        ),
        out_shape=out_shape,
        input_output_aliases=aliases or {},
        compiler_params=pltpu.CompilerParams(
            vmem_limit_bytes=VMEM_LIMIT, dimension_semantics=("arbitrary",) * len(grid)
        ),
        cost_estimate=pl.CostEstimate(
            flops=int(us * 1.1e9), bytes_accessed=int(us * 3.6e6), transcendentals=0
        ),
    )


def whole(shape):
    zeros = (0,) * len(shape)
    return pl.BlockSpec(shape, lambda *_: zeros)


def struct(shape, dtype):
    return jax.ShapeDtypeStruct(shape, dtype)


def turn_within_heads(values, sign):
    lane = lane_of(values.shape) % HEAD_DIM
    ahead = pltpu.roll(values, LANES - HEAD_DIM // 2, 1)
    behind = pltpu.roll(values, HEAD_DIM // 2, 1)
    return jnp.where(lane < HEAD_DIM // 2, -sign * ahead, sign * behind)


def project_kernel(
    tok_ref, gain_ref, w_ref, cos_ref, sin_ref, query_ref, key_ref, value_ref, normed_ref
):
    resid = tok_ref[...].astype(f32)
    inverse = lax.rsqrt(jnp.mean(resid * resid, axis=1, keepdims=True) + epsilon)
    normed = (resid * inverse * gain_ref[...]).astype(bf16)
    normed_ref[...] = normed
    raw = dot_nt(normed, w_ref[...])
    cosine, sine = cos_ref[...], sin_ref[...]

    def rot(values):
        return (values * cosine + turn_within_heads(values, 1.0) * sine).astype(bf16).astype(f32)

    first = rot(raw[:, :LANES])
    second = rot(raw[:, LANES : 2 * LANES])
    low = lane_of(first.shape) < HEAD_DIM
    scale = 1.0 / math.sqrt(HEAD_DIM)
    query_ref[0] = jnp.where(low, first * scale, 0.0).astype(bf16)
    query_ref[1] = jnp.where(low, 0.0, first * scale).astype(bf16)
    query_ref[2] = jnp.where(low, second * scale, 0.0).astype(bf16)
    key_ref[...] = jnp.where(low, pltpu.roll(second, HEAD_DIM, 1), second).astype(bf16)
    value_ref[...] = raw[:, 2 * LANES :].astype(bf16)


def project(tokens, gain, w_stack, cosine, sine):
    total, width = tokens.shape
    rows = 512
    lanes = pl.BlockSpec((rows, LANES), lambda j: (j, 0))
    wide = pl.BlockSpec((rows, width), lambda j: (j, 0))
    return call(
        project_kernel,
        (total // rows,),
        0,
        [wide, whole((1, width)), whole(w_stack.shape), lanes, lanes],
        [pl.BlockSpec((3, rows, LANES), lambda j: (0, j, 0)), lanes, lanes, wide],
        [
            struct((3, total, LANES), bf16),
            struct((total, LANES), bf16),
            struct((total, LANES), bf16),
            struct((total, width), bf16),
        ],
        us=0.5,
    )(tokens, gain, w_stack, cosine, sine)


def attend_kernel(query_ref, key_ref, value_ref, start_ref, packed_ref, plain_ref, total_ref, out_ref):
    blocks = query_ref.shape[1] // QUERY_BLOCK
    block = pl.program_id(0)
    for index in range(blocks):

        @pl.when(block == index)
        def _(index=index):
            rows = pl.ds(index * QUERY_BLOCK, QUERY_BLOCK)
            span = (index + 1) * QUERY_BLOCK
            row = index * QUERY_BLOCK + lax.broadcasted_iota(jnp.int32, (QUERY_BLOCK, span), 0)
            column = lane_of((QUERY_BLOCK, span))
            allowed = (column <= row) & (column >= start_ref[rows, :])

            def head(number, carry):
                scores = dot_nt(query_ref[number, rows, :], key_ref[0:span, :])
                scores = jnp.where(allowed, scores, masked_score)
                peak = jnp.max(scores, axis=1, keepdims=True)
                weights = jnp.exp(scores - peak)
                summed = jnp.sum(weights, axis=1, keepdims=True)
                probs = (weights * (1.0 / summed)).astype(bf16)
                out_ref[number] = dot(probs, value_ref[0:span, :])
                total = jnp.broadcast_to(peak + jnp.log(summed), (QUERY_BLOCK, LANES))
                total_ref[number, :, rows] = jnp.transpose(total)[0:8, :]
                return carry

            lax.fori_loop(0, 3, head, 0)
            low = lane_of((QUERY_BLOCK, LANES)) < HEAD_DIM
            one, two, three = out_ref[0], out_ref[1], out_ref[2]
            pair = jnp.where(low, one, two).astype(bf16)
            plain_ref[rows, 0:LANES] = pair
            plain_ref[rows, LANES : 2 * LANES] = jnp.where(low, three, 0.0).astype(bf16)
            if index < blocks // 2:
                packed_ref[rows, 0:LANES] = pair
                packed_ref[rows, LANES : 2 * LANES] = three.astype(bf16)
            else:
                back = pl.ds((index - blocks // 2) * QUERY_BLOCK, QUERY_BLOCK)
                before = packed_ref[back, LANES : 2 * LANES].astype(f32)
                packed_ref[back, LANES : 2 * LANES] = jnp.where(low, before, one).astype(bf16)
                packed_ref[back, 2 * LANES : 3 * LANES] = jnp.where(low, two, three).astype(bf16)


def attend(query, key, value, start):
    total = key.shape[0]
    return call(
        attend_kernel,
        (total // QUERY_BLOCK,),
        0,
        [whole(query.shape), whole(key.shape), whole(value.shape), whole(start.shape)],
        [whole((total // 2, 3 * LANES)), whole((total, 2 * LANES)), whole((3, 8, total))],
        [
            struct((total // 2, 3 * LANES), bf16),
            struct((total, 2 * LANES), bf16),
            struct((3, 8, total), f32),
        ],
        scratch=[pltpu.VMEM((3, QUERY_BLOCK, LANES), f32)],
        us=0.5,
    )(query, key, value, start)


def attend_back_kernel(
    query_ref, key_ref, value_ref, grad_ref, total_ref, start_ref, cos_ref, sin_ref, normed_ref, w_ref, gain_ref,
    blocks_ref, own_ref, out_ref, query_grad_ref, key_grad_ref, value_grad_ref, own_sum_ref
):
    blocks = query_ref.shape[1] // QUERY_BLOCK
    block = pl.program_id(0)
    scale = 1.0 / math.sqrt(HEAD_DIM)

    @pl.when(block == 0)
    def _():
        key_grad_ref[...] = jnp.zeros_like(key_grad_ref)
        value_grad_ref[...] = jnp.zeros_like(value_grad_ref)

    def back(values, cosine, sine):
        return values * cosine + turn_within_heads(values * sine, -1.0)

    for index in range(blocks):

        @pl.when(block == index)
        def _(index=index):
            rows = pl.ds(index * QUERY_BLOCK, QUERY_BLOCK)
            span = (index + 1) * QUERY_BLOCK
            row = index * QUERY_BLOCK + lane_of((span, QUERY_BLOCK))
            column = lax.broadcasted_iota(jnp.int32, (span, QUERY_BLOCK), 0)
            allowed = (column <= row) & (column >= start_ref[0:1, rows])
            low = lane_of((QUERY_BLOCK, LANES)) < HEAD_DIM

            def head(number, carry):
                query = query_ref[number, rows, :]
                tile = pl.multiple_of((number // 2) * LANES, LANES)
                upstream = grad_ref[rows, pl.ds(tile, LANES)].astype(f32)
                keep = low == (number != 1)
                upstream = jnp.where(keep, upstream, 0.0).astype(bf16)
                scores = dot_nt(key_ref[0:span, :], query)
                probs = jnp.exp(scores - total_ref[number, 0:1, rows])
                probs = jnp.where(allowed, probs, 0.0)
                prob_grad = dot_nt(value_ref[0:span, :], upstream)
                row_dot = jnp.sum(probs * prob_grad, axis=0, keepdims=True)
                score_grad = (probs * (prob_grad - row_dot)).astype(bf16)
                key_grad_ref[0:span, :] += dot(score_grad, query)
                value_grad_ref[0:span, :] += dot(probs.astype(bf16), upstream)
                query_grad_ref[number] = dot_tn(score_grad, key_ref[0:span, :]) * scale
                return carry

            lax.fori_loop(0, 3, head, 0)
            cosine, sine = cos_ref[rows, :], sin_ref[rows, :]
            pair = jnp.where(low, query_grad_ref[0], query_grad_ref[1])
            out_ref[rows, 0:LANES] = back(pair, cosine, sine).astype(bf16)
            out_ref[rows, LANES : 2 * LANES] = back(query_grad_ref[2], cosine, sine).astype(bf16)

    @pl.when(block == blocks - 1)
    def _():
        low = lane_of(key_grad_ref.shape) < HEAD_DIM
        key_grad = key_grad_ref[...]
        key_grad = key_grad + pltpu.roll(key_grad, HEAD_DIM, 1)
        key_grad = back(key_grad, cos_ref[...], sin_ref[...])
        before = out_ref[:, LANES : 2 * LANES].astype(f32)
        out_ref[:, LANES : 2 * LANES] = jnp.where(low, before, key_grad).astype(bf16)
        value_grad = value_grad_ref[...]
        value_grad = value_grad + pltpu.roll(value_grad, HEAD_DIM, 1)
        out_ref[:, 2 * LANES : 3 * LANES] = jnp.where(low, 0.0, value_grad).astype(bf16)
        chunk = 512
        own_sum_ref[...] = jnp.zeros_like(own_sum_ref)

        def add(index, carry):
            part = pl.ds(pl.multiple_of(index * chunk, chunk), chunk)
            own_sum_ref[...] += dot_tn(normed_ref[part, :], out_ref[part, :])
            return carry

        lax.fori_loop(0, out_ref.shape[0] // chunk, add, 0)
        own = own_sum_ref[...]
        own_ref[...] = own.astype(bf16)
        share = jnp.sum(own * w_ref[...].astype(f32), axis=1, keepdims=True) / gain_ref[...]
        share = jnp.transpose(jnp.broadcast_to(share, (share.shape[0], LANES)))[0:8, :]
        width = blocks_ref.shape[2]
        row = lax.broadcasted_iota(jnp.int32, (8, width), 0)
        terms = jnp.zeros((8, width), f32)
        for index in range(share.shape[1] // width):
            piece = share[:, index * width : (index + 1) * width]
            upper = piece.astype(bf16).astype(f32)
            terms = jnp.where(row == index, upper, jnp.where(row == index + 4, piece - upper, terms))
        terms = jnp.concatenate([terms, jnp.zeros((8, width), f32)], axis=0).astype(bf16)
        rows = blocks_ref.shape[1] - DOT_ROWS
        for index in range(blocks_ref.shape[0]):
            blocks_ref[index, 0:rows, :] = out_ref[index * rows : (index + 1) * rows, :]
            blocks_ref[index, rows:, :] = terms


def attend_back(query, key, value, grad, totals, start, cosine, sine, normed, w_natural, gain):
    total = key.shape[0]
    members = 2 * COLS
    rows = total // members + DOT_ROWS
    args = (query, key, value, grad, totals, start, cosine, sine, normed, w_natural, gain)
    return call(
        attend_back_kernel,
        (total // QUERY_BLOCK,),
        0,
        [whole(item.shape) for item in args],
        [whole((members, rows, 3 * LANES)), whole(w_natural.shape)],
        [struct((members, rows, 3 * LANES), bf16), struct(w_natural.shape, bf16)],
        scratch=[
            pltpu.VMEM((total, 3 * LANES), bf16),
            pltpu.VMEM((3, QUERY_BLOCK, LANES), f32),
            pltpu.VMEM((total, LANES), f32),
            pltpu.VMEM((total, LANES), f32),
            pltpu.VMEM(w_natural.shape, f32),
        ],
        us=0.5,
    )(*args)


def branch_operand(refs):
    rows = refs.shape[2]
    low = lane_of((rows, LANES)) < HEAD_DIM
    pairs, thirds = [], []
    for member in range(refs.shape[1]):
        one = refs[0, member, :, 0:LANES]
        mid = refs[0, member, :, LANES : 2 * LANES].astype(f32)
        end = refs[0, member, :, 2 * LANES : 3 * LANES].astype(f32)
        mid_turned = pltpu.roll(mid, HEAD_DIM, 1)
        end_turned = pltpu.roll(end, HEAD_DIM, 1)
        late = jnp.where(low, mid_turned, end_turned).astype(bf16)
        pairs.append(jnp.concatenate([one, late], axis=0))
        thirds.append((mid, end_turned))
    for member in range(0, refs.shape[1], 2):
        tops = []
        for which in range(2):
            left, right = thirds[member][which], thirds[member + 1][which]
            tops.append(jnp.where(low, left, pltpu.roll(right, HEAD_DIM, 1)).astype(bf16))
        pairs.append(jnp.concatenate(tops, axis=0))
    return jnp.concatenate(pairs, axis=1)


def branch_weights(ref):
    right = [ref[source, 0:LANES] for source in range(ref.shape[0])]
    return jnp.concatenate(right + [ref[source, LANES:] for source in range(ref.shape[0])], axis=0)


def hits_of(rank, local_experts):
    place = lax.broadcasted_iota(jnp.int32, (CAPACITY, rank.shape[1]), 0).astype(f32)
    return [place == rank[j : j + 1, :] for j in range(local_experts)]


def chosen_of(hits):
    return jnp.concatenate([jnp.where(hit, 1.0, 0.0).astype(bf16) for hit in hits], axis=0)


def middle_kernel(
    place_ref, att_mine_ref, att_other_ref, w_mine_ref, w_other_ref, tok_a_ref, tok_b_ref, routes_a_ref, routes_b_ref,
    gain_ref, w_router_ref, after_ref,
    x_ref, slot_gate_ref, rank_ref, gate_ref, normed_ref, middle_ref, gates_own_ref, gates_ref, ranks_ref
):
    step = pl.program_id(0)
    member = place_ref[2]
    cols = pl.num_programs(0)
    rows = tok_a_ref.shape[0]
    local_experts = x_ref.shape[0]
    branch = dot(branch_operand(att_mine_ref), branch_weights(w_mine_ref))
    branch = branch + dot(branch_operand(att_other_ref), branch_weights(w_other_ref))
    for half in range(2):
        tok_ref, routes_ref = ((tok_a_ref, routes_a_ref), (tok_b_ref, routes_b_ref))[half]
        middle = tok_ref[...].astype(f32) + branch[half * rows : (half + 1) * rows]
        inverse = lax.rsqrt(jnp.mean(middle * middle, axis=1, keepdims=True) + epsilon)
        normed = (middle * inverse * gain_ref[...]).astype(bf16)
        normed_ref[half, 0] = normed
        logits = dot_nt(w_router_ref[...], normed)
        padded = logits.shape[0]
        slot = lax.broadcasted_iota(jnp.int32, (padded, rows), 0)
        expert = (slot // 8) * local_experts + slot % 8
        expert = jnp.where(slot % 8 < local_experts, expert, -1).astype(f32)
        routes = routes_ref[0].astype(f32)
        named = expert == routes[0:1, 0:rows]
        for k in range(1, TOP):
            named = named | (expert == routes[k : k + 1, 0:rows])
        peak = jnp.max(jnp.where(named, logits, masked_score), axis=0, keepdims=True)
        weights = jnp.where(named, jnp.exp(logits - peak), 0.0)
        gates = weights / jnp.sum(weights, axis=0, keepdims=True)
        gates_ref[...] = gates
        ranks_ref[...] = jnp.where(named, dot(named.astype(f32).astype(bf16), after_ref[...]), -1.0)
        here = pl.ds(pl.multiple_of(member * 8, 8), 8)
        gate, rank = gates_ref[here, :], ranks_ref[here, :]
        rank_ref[half, 0] = rank
        gate_ref[half, 0] = gate
        hits = hits_of(rank, local_experts)
        slot_gate = jnp.concatenate(
            [jnp.sum(jnp.where(hit, gate[j : j + 1, :], 0.0), axis=1, keepdims=True) for j, hit in enumerate(hits)],
            axis=0,
        )
        chosen = chosen_of(hits)
        picked = dot(chosen, normed).astype(bf16)
        spread = jnp.broadcast_to(slot_gate, (slot_gate.shape[0], LANES))
        for j in range(local_experts):
            part = slice(j * CAPACITY, (j + 1) * CAPACITY)
            x_ref[j, half, 0] = picked[part]
            slot_gate_ref[j, half, 0] = spread[part]

        @pl.when(member == half * cols + step)
        def _(middle=middle, gates=gates):
            middle_ref[...] = middle
            gates_own_ref[...] = gates


def middle_and_dispatch(place, att, w_mine, w_other, tokens, routes, gain, w_router, local_experts):
    width = tokens.shape[1]
    half = COLS
    rows = tokens.shape[0] // (2 * half)
    padded = w_router.shape[0]
    after = jnp.asarray(np.triu(np.ones((rows, rows), np.float32), 1), bf16)
    slot_shape = (local_experts, 2, half, CAPACITY)
    early = pl.BlockSpec((rows, width), lambda i, p: (i, 0))
    late = pl.BlockSpec((rows, width), lambda i, p: (i + half, 0))
    routes_shape = (1,) + routes.shape[1:]
    return call(
        middle_kernel,
        (half,),
        1,
        [
            pl.BlockSpec((1, half, rows, 3 * LANES), lambda i, p: (p[0], 0, i, 0)),
            pl.BlockSpec((1, half, rows, 3 * LANES), lambda i, p: (1 - p[0], 0, i, 0)),
            whole(w_mine.shape),
            whole(w_other.shape),
            early,
            late,
            pl.BlockSpec(routes_shape, lambda i, p: (i, 0, 0)),
            pl.BlockSpec(routes_shape, lambda i, p: (i + half, 0, 0)),
            whole((1, width)),
            whole(w_router.shape),
            whole((rows, rows)),
        ],
        [
            pl.BlockSpec((local_experts, 2, 1, CAPACITY, width), lambda i, p: (0, 0, i, 0, 0)),
            pl.BlockSpec((local_experts, 2, 1, CAPACITY, LANES), lambda i, p: (0, 0, i, 0, 0)),
            pl.BlockSpec((2, 1, 8, rows), lambda i, p: (0, i, 0, 0)),
            pl.BlockSpec((2, 1, 8, rows), lambda i, p: (0, i, 0, 0)),
            pl.BlockSpec((2, 1, rows, width), lambda i, p: (0, i, 0, 0)),
            whole((rows, width)),
            whole((padded, rows)),
        ],
        [
            struct(slot_shape + (width,), bf16),
            struct(slot_shape + (LANES,), f32),
            struct((2, half, 8, rows), f32),
            struct((2, half, 8, rows), f32),
            struct((2, half, rows, width), bf16),
            struct((rows, width), f32),
            struct((padded, rows), f32),
        ],
        scratch=[pltpu.VMEM((padded, rows), f32), pltpu.VMEM((padded, rows), f32)],
        us=0.5,
    )(place, att, att, w_mine, w_other, tokens, tokens, routes, routes, gain, w_router, after)


def grad_dispatch_kernel(rank_ref, gate_ref, cot_ref, g_ref):
    local_experts = g_ref.shape[0]
    rows = cot_ref.shape[0] // 2
    for half in range(2):
        hits = hits_of(rank_ref[half], local_experts)
        gate = gate_ref[half]
        slot_gate = jnp.concatenate(
            [jnp.sum(jnp.where(hit, gate[j : j + 1, :], 0.0), axis=1, keepdims=True) for j, hit in enumerate(hits)],
            axis=0,
        )
        grads = (dot(chosen_of(hits), cot_ref[half * rows : (half + 1) * rows, :]) * slot_gate).astype(bf16)
        for j in range(local_experts):
            g_ref[j, half] = grads[j * CAPACITY : (j + 1) * CAPACITY]


def grad_dispatch(rank, gate, cotangents, local_experts):
    members, _, rows = rank.shape
    width = cotangents.shape[1]
    small = pl.BlockSpec((2, 8, rows), lambda j: (j, 0, 0))
    return call(
        grad_dispatch_kernel,
        (members // 2,),
        0,
        [small, small, pl.BlockSpec((2 * rows, width), lambda j: (j, 0))],
        pl.BlockSpec((local_experts, 2, CAPACITY, width), lambda j: (0, j, 0, 0)),
        struct((local_experts, members, CAPACITY, width), bf16),
        us=0.5,
    )(rank, gate, cotangents)


def expert_kernel(
    x_ref, gate_ref, w_gate_ref, w_up_ref, w_down_ref, forth_ref, active_ref, factor_ref, silu_ref
):
    gate_pre = dot(x_ref[0], w_gate_ref[0])
    up_pre = dot(x_ref[0], w_up_ref[0])
    sig = 1.0 / (1.0 + jnp.exp(-gate_pre))
    silu = gate_pre * sig
    silu_ref[0] = silu
    factor_ref[0] = up_pre * sig * (1.0 + gate_pre * (1.0 - sig))
    active_ref[0] = (silu * up_pre).astype(bf16)
    produced = dot_nt(active_ref[0], w_down_ref[0]).astype(bf16).astype(f32)
    forth_ref[0] = (produced * gate_ref[0, :, 0:1]).astype(bf16)


def run_experts(x, slot_gate, w_gate, w_up, w_down):
    count, slots, width = x.shape
    hidden = w_gate.shape[2]

    def per_expert(*shape):
        return pl.BlockSpec((1,) + shape, lambda e: (e, 0, 0))

    return call(
        expert_kernel,
        (count,),
        0,
        [per_expert(slots, width), per_expert(slots, LANES)] + [per_expert(width, hidden)] * 3,
        [per_expert(slots, width)] + [per_expert(slots, hidden)] * 3,
        [
            struct((count, slots, width), bf16),
            struct((count, slots, hidden), bf16),
            struct((count, slots, hidden), f32),
            struct((count, slots, hidden), f32),
        ],
        us=0.5,
    )(x, slot_gate, w_gate, w_up, w_down)


def expert_back_kernel(place_ref, *refs, fast):
    x_ref, g_ref, active_ref, factor_ref, silu_ref = refs[:5]
    w_gate_ref, w_up_ref, w_down_ref, back_ref, dots_ref = refs[5:10]
    grads, (gate_low_ref, up_low_ref) = refs[10:-2], refs[-2:]
    slots, width = g_ref.shape[1], g_ref.shape[2]
    chunk = 256
    active_grad = dot(g_ref[0], w_down_ref[0])
    gate_low_ref[...] = (active_grad * factor_ref[0]).astype(bf16)
    up_low_ref[...] = (active_grad * silu_ref[0]).astype(bf16)
    dots = jnp.sum(active_ref[0].astype(f32) * active_grad, axis=1, keepdims=True)
    dots_ref[0] = jnp.broadcast_to(dots, (slots, LANES))
    back_ref[0] = (dot_nt(gate_low_ref[...], w_gate_ref[0]) + dot_nt(up_low_ref[...], w_up_ref[0])).astype(bf16)

    def products(cols):
        x = x_ref[0, :, cols]
        yield 0, dot_tn(x, gate_low_ref[...]).astype(bf16)
        yield 1, dot_tn(x, up_low_ref[...]).astype(bf16)
        yield 2, dot_tn(g_ref[0, :, cols], active_ref[0]).astype(bf16)

    if fast:
        write_shards(place_ref, grads, products, width)
    else:

        def whole_columns(index, carry):
            cols = pl.ds(pl.multiple_of(index * chunk, chunk), chunk)
            for which, product in products(cols):
                grads[which][0, cols, :] = product
            return carry

        lax.fori_loop(0, width // chunk, whole_columns, 0)


def write_shards(place_ref, outs, products, width):
    send_a, keep_a, send_b, keep_b = outs
    x_bit, y_bit = place_ref[3], place_ref[4]
    shard = width // 4
    for dy in range(2):
        for dx in range(2):
            x, y = x_bit ^ dx, y_bit ^ dy
            cols = pl.ds(pl.multiple_of((y * 2 + x) * shard, shard), shard)
            for which, product in products(cols):
                side = product.shape[1] // 2
                (send_a if dx else keep_a)[0, which, y] = product[:, :side]
                (send_b if dy else keep_b)[0, which, x] = product[:, side:]


def run_experts_back(place, x, g, active, factor, silu, w_gate, w_up, w_down, first, count, fast):
    slots, width = g.shape[1], g.shape[2]
    hidden = w_gate.shape[2]

    def taken(*shape):
        return pl.BlockSpec((1,) + shape, lambda e, p: (e + first, 0, 0))

    def given(*shape):
        zeros = (0,) * len(shape)
        return pl.BlockSpec((1,) + shape, lambda e, p: (e,) + zeros)

    if fast:
        grad_shapes = [(3, 2, width // 4, hidden // 2)] * 4
    else:
        grad_shapes = [(width, hidden)] * 3
    return call(
        lambda *refs: expert_back_kernel(*refs, fast=fast),
        (count,),
        1,
        [taken(slots, width)] * 2 + [taken(slots, hidden)] * 3 + [taken(width, hidden)] * 3,
        [given(slots, width), given(slots, LANES)] + [given(*shape) for shape in grad_shapes],
        [struct((count, slots, width), bf16), struct((count, slots, LANES), f32)]
        + [struct((count,) + shape, bf16) for shape in grad_shapes],
        scratch=[pltpu.VMEM((slots, hidden), bf16)] * 2,
        us=0.5,
    )(place, x, g, active, factor, silu, w_gate, w_up, w_down)


DOT_LANES = 2 * LANES


def combine_kernel(place_ref, rank_ref, *refs, pieces, with_dots, mine):
    parts, rest = refs[:pieces], refs[pieces:]
    rows = rank_ref.shape[2]
    local_experts = sum(part.shape[0] for part in parts)
    hits = hits_of(rank_ref[0], local_experts)
    gathered = jnp.concatenate([part[j, 0] for part in parts for j in range(part.shape[0])], axis=0)
    summed = dot_tn(chosen_of(hits), gathered)
    out_ref = rest[-1]
    if mine:
        arrived_ref = rest[-2]
        summed = summed + arrived_ref[0, 0:rows, :].astype(f32)
    out_ref[0, 0:rows, :] = summed.astype(bf16)
    if with_dots:
        column = [part[j, 0][:, 0:1] for part in rest[:pieces] for j in range(part.shape[0])]
        scattered = [
            jnp.sum(jnp.where(hit, value, 0.0), axis=0, keepdims=True) for hit, value in zip(hits, column)
        ]
        scattered.append(jnp.zeros((DOT_ROWS - local_experts, rows), f32))
        scattered = jnp.concatenate(scattered, axis=0)
        upper = scattered.astype(bf16)
        out_ref[0, rows:, :] = jnp.zeros((DOT_ROWS, out_ref.shape[2]), bf16)
        out_ref[0, rows:, 0:rows] = upper
        out_ref[0, rows:, DOT_LANES : DOT_LANES + rows] = (scattered - upper.astype(f32)).astype(bf16)
        if mine:
            out_ref[0, rows:, 2 * DOT_LANES : 4 * DOT_LANES] = arrived_ref[0, rows:, 0 : 2 * DOT_LANES]


def combine(place, rank, parts, dots=None, arrived=None):
    mine = arrived is not None
    rows, width = rank.shape[2], parts[0].shape[-1]
    out_rows = rows + (DOT_ROWS if dots else 0)

    def member(step, p):
        return (p[0] if mine else 1 - p[0]) * COLS + step

    def slots_of(array):
        return pl.BlockSpec((array.shape[0], 1) + array.shape[2:], lambda j, p: (0, member(j, p), 0, 0))

    inputs = [
        part.reshape(part.shape[0], 2 * COLS, CAPACITY, part.shape[-1]) for part in list(parts) + list(dots or [])
    ]
    in_specs = [pl.BlockSpec((1, 8, rows), lambda j, p: (member(j, p), 0, 0))] + [slots_of(item) for item in inputs]
    by_chip = pl.BlockSpec((1, out_rows, width), lambda j, p: (j, 0, 0))
    if mine:
        inputs.append(arrived)
        in_specs.append(by_chip)
    return call(
        lambda *refs: combine_kernel(*refs, pieces=len(parts), with_dots=bool(dots), mine=mine),
        (COLS,),
        1,
        in_specs,
        by_chip,
        struct((COLS, out_rows, width), bf16),
        us=0.5,
    )(place, rank, *inputs)


def split_dot(dimension_numbers, values, exact):
    upper = values.astype(bf16)
    lower = (values - upper.astype(f32)).astype(bf16)
    return lax.dot_general(
        upper, exact, dimension_numbers, preferred_element_type=f32
    ) + lax.dot_general(lower, exact, dimension_numbers, preferred_element_type=f32)


EXTRA_SLOTS = 6


def middle_back_kernel(
    place_ref, sums_ref, gates_ref, middle_ref, cot_ref, gain_ref, w_router_ref, w_mine_ref, w_other_ref,
    grad_ref, branch_ref, attended_ref, extra_ref
):
    rows = middle_ref.shape[0]
    tail = sums_ref[:, rows : rows + 8, 0 : 4 * DOT_LANES].astype(f32)
    mine = tail[:, :, 0:rows] + tail[:, :, DOT_LANES : DOT_LANES + rows]
    other = tail[:, :, 2 * DOT_LANES : 2 * DOT_LANES + rows] + tail[:, :, 3 * DOT_LANES : 3 * DOT_LANES + rows]
    first_row = place_ref[0] == 0
    dots = jnp.concatenate([jnp.where(first_row, mine, other), jnp.where(first_row, other, mine)], axis=0)
    dots = dots.reshape(dots.shape[0] * 8, rows)
    gates = gates_ref[...]
    logit_grad = dots - gates * jnp.sum(dots, axis=0, keepdims=True)
    middle = middle_ref[...]
    inverse = lax.rsqrt(jnp.mean(middle * middle, axis=1, keepdims=True) + epsilon)
    unit = middle * inverse
    gain = gain_ref[...]
    grad = sums_ref[0, 0:rows].astype(f32)
    for index in range(1, sums_ref.shape[0]):
        grad = grad + sums_ref[index, 0:rows].astype(f32)
    grad = grad + split_dot(TN, logit_grad, w_router_ref[...])
    gain_grad = jnp.sum(grad * unit, axis=0, keepdims=True)
    scaled = grad * gain
    middle_grad = cot_ref[...].astype(f32) + inverse * (
        scaled - unit * jnp.mean(scaled * unit, axis=1, keepdims=True)
    )
    grad_ref[...] = middle_grad
    branch_grad = middle_grad.astype(bf16)
    branch_ref[0:rows, :] = branch_grad
    extra_ref[...] = jnp.zeros_like(extra_ref)
    for index in range(logit_grad.shape[0] // 8):
        first, lane = index // EXTRA_SLOTS * 8, index % EXTRA_SLOTS * DOT_LANES
        extra_ref[first : first + 8, lane : lane + rows] = logit_grad[index * 8 : index * 8 + 8]
    upper = gain_grad.astype(bf16).astype(f32)
    extra_ref[13:14, :] = upper
    extra_ref[14:15, :] = gain_grad - upper
    branch_ref[rows:, :] = extra_ref[...].astype(bf16)
    for which, ref in enumerate((w_mine_ref, w_other_ref)):
        line = place_ref[0] if which == 0 else 1 - place_ref[0]
        for col in range(ref.shape[0]):
            product = dot_nt(branch_grad, ref[col])
            member = line * COLS + col
            attended_ref[member, :, 0:LANES] = product[:, 0:LANES].astype(bf16)
            attended_ref[member, :, LANES : LANES + HEAD_DIM] = product[:, LANES:].astype(bf16)
            attended_ref[member, :, LANES + HEAD_DIM :] = jnp.zeros((product.shape[0], HEAD_DIM), bf16)


def middle_back(place, sums, gates, middle, cotangent, gain, w_router, w_mine, w_other):
    rows, width = middle.shape
    members = 2 * COLS
    args = (sums, gates, middle, cotangent, gain, w_router, w_mine, w_other)
    return call(
        middle_back_kernel,
        (1,),
        1,
        [whole(item.shape) for item in args],
        [whole((rows, width)), whole((rows + DOT_ROWS, width)), whole((members, rows, 2 * LANES))],
        [
            struct((rows, width), f32),
            struct((rows + DOT_ROWS, width), bf16),
            struct((members, rows, 2 * LANES), bf16),
        ],
        scratch=[pltpu.VMEM((DOT_ROWS, width), f32)],
        us=0.5,
    )(place, *args)


def input_grad_kernel(
    place_ref, grads_mine_ref, grads_other_ref, mine_a_ref, mine_b_ref, other_a_ref, other_b_ref,
    tok_ref, middle_grad_ref, gain_ref, out_ref, share_ref, sum_ref
):
    step = pl.program_id(0)
    first = place_ref[4] == 0

    def weights(a_ref, b_ref):
        a = jnp.concatenate([a_ref[index, 0] for index in range(a_ref.shape[0])], axis=0)
        b = jnp.concatenate([b_ref[index, 0] for index in range(b_ref.shape[0])], axis=0)
        upper, lower = jnp.where(first, a, b), jnp.where(first, b, a)
        return jnp.concatenate([upper, lower, lower[lower.shape[0] - HEAD_DIM :]], axis=0)

    rows = tok_ref.shape[0]
    part = dot(grads_mine_ref[0, 0:rows, :], weights(mine_a_ref, mine_b_ref))
    part = part + dot(grads_other_ref[0, 0:rows, :], weights(other_a_ref, other_b_ref))
    share = grads_mine_ref[0, rows:, :].astype(f32)[0:8] + grads_other_ref[0, rows:, :].astype(f32)[0:8]

    @pl.when(step == 0)
    def _():
        sum_ref[...] = part
        share_ref[...] = share

    @pl.when(step > 0)
    def _():
        sum_ref[...] += part
        share_ref[...] += share

    @pl.when(step == pl.num_programs(0) - 1)
    def _():
        resid = tok_ref[...].astype(f32)
        inverse = lax.rsqrt(jnp.mean(resid * resid, axis=1, keepdims=True) + epsilon)
        unit = resid * inverse
        scaled = sum_ref[...] * gain_ref[...]
        out_ref[...] = middle_grad_ref[...] + inverse * (
            scaled - unit * jnp.mean(scaled * unit, axis=1, keepdims=True)
        )


def input_grad(place, grads, weights, tokens, middle_grad, gain):
    rows, width = tokens.shape
    lanes = grads.shape[2]
    w_shape = (weights[0].shape[0], 1) + weights[0].shape[2:]
    return call(
        input_grad_kernel,
        (COLS,),
        1,
        [
            pl.BlockSpec((1, rows + DOT_ROWS, lanes), lambda c, p: (p[0] * COLS + c, 0, 0)),
            pl.BlockSpec((1, rows + DOT_ROWS, lanes), lambda c, p: ((1 - p[0]) * COLS + c, 0, 0)),
        ]
        + [pl.BlockSpec(w_shape, lambda c, p: (0, c, 0, 0))] * 4
        + [whole((rows, width)), whole((rows, width)), whole((1, width))],
        [whole((rows, width)), whole((8, lanes))],
        [struct((rows, width), f32), struct((8, lanes), f32)],
        scratch=[pltpu.VMEM((rows, width), f32)],
        us=0.5,
    )(place, grads, grads, *weights, tokens, middle_grad, gain)


def out_weights_kernel(place_ref, branch_ref, att_ref, normed_ref, own_ref, *refs, fast, local_experts):
    outs, small_ref, (sum_ref, gain_sum_ref) = refs[:-3], refs[-3], refs[-2:]
    step = pl.program_id(0)
    rows = att_ref.shape[0] // 2
    block = rows + DOT_ROWS

    @pl.when(step == 0)
    def _():
        sum_ref[...] = jnp.zeros_like(sum_ref)
        small_ref[...] = jnp.zeros_like(small_ref)
        gain_sum_ref[...] = jnp.zeros_like(gain_sum_ref)

    branch = jnp.concatenate([branch_ref[0:rows, :], branch_ref[block : block + rows, :]], axis=0)
    sum_ref[...] += dot_tn(branch, att_ref[...])
    for which in range(2):
        tail = branch_ref[which * block + rows : (which + 1) * block, :].astype(f32)
        slots = []
        for index in range(small_ref.shape[0] // 8):
            first, lane = index // EXTRA_SLOTS * 8, index % EXTRA_SLOTS * DOT_LANES
            slots.append(tail[first : first + 8, lane : lane + rows])
        logit_grad = jnp.concatenate(slots, axis=0)
        real = lax.broadcasted_iota(jnp.int32, logit_grad.shape, 0) % 8 < local_experts
        logit_grad = jnp.where(real, logit_grad, 0.0).astype(bf16)
        small_ref[...] += dot(logit_grad, normed_ref[which * rows : (which + 1) * rows, :])
        gain_sum_ref[...] += tail[8:16, :]

    @pl.when(step == pl.num_programs(0) - 1)
    def _():
        small_ref[7:8, :] = gain_sum_ref[5:6, :] + gain_sum_ref[6:7, :]

        def products(cols):
            own = own_ref[cols, 0 : 2 * LANES]
            out_one = sum_ref[cols, 0:LANES].astype(bf16)
            out_two = sum_ref[cols, LANES:]
            low = lane_of(out_two.shape) < HEAD_DIM
            tail = jnp.where(low, out_two, own_ref[cols, 2 * LANES :].astype(f32)).astype(bf16)
            yield 0, jnp.concatenate([own, out_one, tail], axis=1)

        if fast:
            write_shards(place_ref, outs, products, own_ref.shape[0])
        else:
            outs[0][...] = next(products(slice(0, own_ref.shape[0])))[1]


def out_weights(place, branch, attended, normed, own, padded, local_experts, fast):
    total, width = normed.shape
    rows = total // COLS
    blocks = branch.shape[0] // COLS
    if fast:
        shapes = [(1, 1, 2, width // 4, 2 * LANES)] * 4
    else:
        shapes = [(width, 4 * LANES)]
    return call(
        lambda *refs: out_weights_kernel(*refs, fast=fast, local_experts=local_experts),
        (COLS,),
        1,
        [
            pl.BlockSpec((blocks, width), lambda j, p: (j, 0)),
            pl.BlockSpec((rows, 2 * LANES), lambda j, p: (j, 0)),
            pl.BlockSpec((rows, width), lambda j, p: (j, 0)),
            whole(own.shape),
        ],
        [whole(shape) for shape in shapes] + [whole((padded, width))],
        [struct(shape, bf16) for shape in shapes] + [struct((padded, width), f32)],
        scratch=[pltpu.VMEM((width, 2 * LANES), f32), pltpu.VMEM((8, width), f32)],
        us=0.5,
    )(place, branch, attended, normed, own)


def first_sum_kernel(place_ref, keep_a_ref, got_a_ref, keep_b_ref, got_b_ref, *rest):
    send_a_ref, held_a_ref, send_b_ref, held_b_ref = rest[-4:]
    x_bit, y_bit = place_ref[3], place_ref[4]
    for bit, keep, got, send, held in (
        (y_bit, keep_a_ref, got_a_ref, send_a_ref, held_a_ref),
        (x_bit, keep_b_ref, got_b_ref, send_b_ref, held_b_ref),
    ):
        for kind in range(keep.shape[1]):
            held[0, kind] = (keep[0, kind, bit].astype(f32) + got[0, kind, bit].astype(f32)).astype(bf16)
            send[0, kind] = (keep[0, kind, 1 - bit].astype(f32) + got[0, kind, 1 - bit].astype(f32)).astype(bf16)


def first_sum(place, chunk, first=0, total=None, before=None):
    count, kinds, _, rows, cols = chunk[0].shape
    taken = pl.BlockSpec((1, kinds, 2, rows, cols), lambda e, p: (e, 0, 0, 0, 0))
    given = pl.BlockSpec((1, kinds, rows, cols), lambda e, p: (e + first, 0, 0, 0))
    extra = list(before) if before else []
    return call(
        first_sum_kernel,
        (count,),
        1,
        [taken] * 4 + [pl.BlockSpec(memory_space=pl.ANY)] * len(extra),
        [given] * 4,
        [struct((total or count, kinds, rows, cols), bf16)] * 4,
        us=0.5,
        aliases={5 + i: i for i in range(len(extra))},
    )(place, *chunk, *extra)


def last_sum_kernel(held_a_ref, got_a_ref, held_b_ref, got_b_ref, *rest):
    outs = rest[-3:]
    side = held_a_ref.shape[3]
    for which, out in enumerate(outs):
        out[0, :, :side] = held_a_ref[0, which].astype(f32) + got_a_ref[0, which].astype(f32)
        out[0, :, side:] = held_b_ref[0, which].astype(f32) + got_b_ref[0, which].astype(f32)


def last_sum(held_a, got_a, held_b, got_b, first, total, before):
    count, kinds, rows, cols = held_a.shape
    taken = pl.BlockSpec((1, kinds, rows, cols), lambda e: (e, 0, 0, 0))
    given = pl.BlockSpec((1, rows, 2 * cols), lambda e: (e + first, 0, 0))
    extra = list(before) if before else []
    return call(
        last_sum_kernel,
        (count,),
        0,
        [taken] * 4 + [pl.BlockSpec(memory_space=pl.ANY)] * len(extra),
        [given] * 3,
        [struct((total, rows, 2 * cols), f32)] * 3,
        us=0.5,
        aliases={4 + i: i for i in range(len(extra))},
    )(held_a, got_a, held_b, got_b, *extra)


def last_weights_kernel(held_a_ref, got_a_ref, held_b_ref, got_b_ref, query_ref, key_ref, value_ref, out_ref):
    left = held_a_ref[0, 0].astype(f32) + got_a_ref[0, 0].astype(f32)
    right = held_b_ref[0, 0].astype(f32) + got_b_ref[0, 0].astype(f32)
    cut = query_ref.shape[1]
    query_ref[...] = left[:, :cut]
    key_ref[...] = left[:, cut:]
    out_ref[...] = right[:, :cut]
    value_ref[...] = right[:, cut:]


def last_weights(parts, widths):
    rows = parts[0].shape[2]
    shapes = [(rows, width) for width in widths]
    return call(
        last_weights_kernel,
        (1,),
        0,
        [whole(part.shape) for part in parts],
        [whole(shape) for shape in shapes],
        [struct(shape, f32) for shape in shapes],
        us=0.5,
    )(*parts)


SWAP = [(0, 1), (1, 0)]


def after(value, *events):
    return lax.optimization_barrier((value,) + events)[0]


def gather_group(block):
    return lax.all_gather(block, ("row", "col"), axis=0, tiled=True)


def line_pieces(value):
    parts = [value]
    for distance in range(1, COLS):
        parts.insert(0, lax.ppermute(value, "col", [(i, (i + distance) % COLS) for i in range(COLS)]))
    return parts


def in_line_order(parts):
    parts = jnp.stack(parts + parts)
    return lax.dynamic_slice_in_dim(parts, COLS - 1 - lax.axis_index("col"), COLS, axis=0)


def flip(value, axis, bit, size):
    return lax.ppermute(value, axis, [(i, i ^ (1 << bit)) for i in range(size)])


def bits_of(size):
    return size.bit_length() - 1


def own_bit(axis, bit):
    return (lax.axis_index(axis) >> bit) & 1


def joined(mine, got, own):
    return jnp.where(own == 0, jnp.concatenate([mine, got]), jnp.concatenate([got, mine]))


def cube_step(value, axis, bit, size):
    return joined(value, flip(value, axis, bit, size), own_bit(axis, bit))


def lines_first(value):
    return jnp.transpose(value, (1, 0, 2, 3)).reshape(value.shape[1], value.shape[0] * value.shape[2], value.shape[3])


def cube_gather(value, axis, size):
    value = value[None]
    for bit in range(bits_of(size)):
        value = cube_step(value, axis, bit, size)
    return value


def sum_dp(value, sizes):
    for bit in range(bits_of(sizes["dp"])):
        value = value + flip(value, "dp", bit, sizes["dp"])
    return value


def reduce_over_dp(value, size):
    count = bits_of(size)
    value = value.reshape(value.shape[:1] + (2,) * count + value.shape[2:])
    current = value
    for bit in range(count - 1, -1, -1):
        own = own_bit("dp", bit)
        keep = lax.dynamic_index_in_dim(current, own, 1, keepdims=False)
        send = lax.dynamic_index_in_dim(current, 1 - own, 1, keepdims=False).astype(bf16)
        current = keep.astype(f32) + flip(send, "dp", bit, size).astype(f32)
    return current


def start_move(run, size):
    return flip(run[0], "dp", 0, size), flip(run[2], "dp", 1, size)


def second_move(sums, size):
    send_a, held_a, send_b, held_b = sums
    return held_a, flip(send_a, "dp", 1, size), held_b, flip(send_b, "dp", 0, size)


def layer(sizes):
    n_dp, n_row, n_col = sizes["dp"], sizes["row"], sizes["col"]
    members = n_row * n_col
    fast = n_dp == 4
    assert n_row == 2 and n_col == COLS and n_dp & (n_dp - 1) == 0

    def local(
        tokens, cotangent, routes, lengths, gain_attn, w_query, w_key, w_value, w_out,
        gain_moe, w_router, w_gate, w_up, w_down,
    ):
        rows, width = tokens.shape
        group = rows * members
        local_experts = w_gate.shape[0]
        row, col, dp = lax.axis_index("row"), lax.axis_index("col"), lax.axis_index("dp")
        place = jnp.stack([row, col, row * n_col + col, dp & 1, (dp >> 1) & 1]).astype(jnp.int32)
        gain_one = gain_attn.astype(f32)[None]
        gain_two = gain_moe.astype(f32)[None]

        tok_all = gather_group(tokens)
        w_in = jnp.concatenate([w_query.T, w_key.T, w_value.T], axis=0)
        out_share, in_share = rows // n_dp, w_in.shape[0] // n_dp
        shares = jnp.concatenate(
            [
                lax.dynamic_slice(w_out.T, (dp * out_share, 0), (out_share, width)),
                lax.dynamic_slice(w_in, (dp * in_share, 0), (in_share, width)),
                jnp.pad(routes.T.astype(bf16).reshape(1, TOP * rows), ((0, 7), (0, width - TOP * rows))),
            ],
            axis=0,
        )
        w_stack = jnp.concatenate([w_query.T, w_key.T, w_value.T, w_value.T], axis=0)
        w_natural = jnp.concatenate([w_query, w_key, w_value, w_value], axis=1)

        ends = jnp.cumsum(lengths[0])
        starts = ends - lengths[0]
        position = jnp.arange(group, dtype=jnp.int32)
        segment = jnp.sum((position[:, None] >= ends[None, :]).astype(jnp.int32), axis=1)
        member = segment[:, None] == jnp.arange(starts.shape[0], dtype=jnp.int32)[None, :]
        start = jnp.sum(jnp.where(member, starts[None, :], 0), axis=1).astype(jnp.int32)
        frequency = rope_base ** (-2.0 * jnp.arange(HEAD_DIM // 2, dtype=f32) / HEAD_DIM)
        angle = (position - start).astype(f32)[:, None] * frequency[None, :]
        cosine = jnp.tile(jnp.cos(angle), (1, 4))
        sine = jnp.tile(jnp.sin(angle), (1, 4))

        w_router_rows = w_router.T.reshape(members, local_experts, width)
        w_router_rows = jnp.pad(w_router_rows, ((0, 0), (0, 8 - local_experts), (0, 0)))
        w_router_rows = w_router_rows.reshape(members * 8, width)
        start_row = jnp.broadcast_to(start[None, :], (8, group))
        start = start[:, None]
        gain_column = gain_attn.astype(f32)[:, None]
        ready = (place, gain_one, gain_two, w_stack, w_natural, cosine, sine, w_router_rows, start, start_row, gain_column)
        shares, place, gain_one, gain_two, w_stack, w_natural, cosine, sine, w_router_rows, start, start_row, gain_column = (
            lax.optimization_barrier((shares,) + ready)
        )
        shares = line_pieces(after(shares, tok_all, cosine))

        query, key, value, normed_one = project(tok_all, gain_one, w_stack, cosine, sine)
        packed, attended, totals = attend(query, key, value, start)
        att_flat = gather_group(packed)
        att_all = att_flat.reshape((n_row, n_col) + packed.shape)
        shares = in_line_order(after(shares, packed))
        route_rows = shares[:, out_share + in_share]
        w_out_mine, in_part = shares[None, :, :out_share], shares[None, :, out_share : out_share + in_share]
        for bit in range(bits_of(n_dp)):
            w_out_mine = cube_step(w_out_mine, "dp", bit, n_dp)
        in_part = cube_step(in_part, "dp", 0, n_dp)
        w_out_mine = lines_first(w_out_mine)
        w_out_other = lax.ppermute(after(w_out_mine, in_part), "row", SWAP)
        route_rows = cube_gather(route_rows, "row", n_row)[:, :, : TOP * rows].reshape(members, TOP, rows)
        cot_all = gather_group(after(cotangent, w_out_other))
        x, slot_gate, rank, gate, normed_two, middle, gates = middle_and_dispatch(
            place, att_all, w_out_mine, w_out_other, tok_all, route_rows, gain_two, w_router_rows, local_experts
        )
        slots = members * CAPACITY
        x = x.reshape(local_experts, slots, width)
        slot_gate = slot_gate.reshape(local_experts, slots, LANES)
        rank, gate = rank.reshape(members, 8, rows), gate.reshape(members, 8, rows)
        forth, active, factor, silu = run_experts(x, slot_gate, w_gate, w_up, w_down)
        for bit in range(1, bits_of(n_dp) - 1):
            in_part = cube_step(in_part, "dp", bit, n_dp)
        last_bit = bits_of(n_dp) - 1
        in_got = after(flip(in_part, "dp", last_bit, n_dp), forth)
        forth_other = combine(place, after(rank, in_got), [forth])
        arrived = lax.ppermute(forth_other, "row", SWAP)
        g = grad_dispatch(after(rank, forth_other), gate, cot_all, local_experts)
        g = g.reshape(local_experts, slots, width)
        cuts = [0, 2, 4, local_experts]

        def backward(which, x):
            first, last = cuts[which], cuts[which + 1]
            return run_experts_back(place, x, g, active, factor, silu, w_gate, w_up, w_down, first, last - first, fast)

        runs = [backward(0, x)]
        forth_mine = combine(place, rank, [forth], arrived=after(arrived, runs[0][1]))
        forth_sums = lax.all_to_all(forth_mine, "col", 0, 0, tiled=True)
        runs.append(backward(1, after(x, forth_mine)))
        runs.append(backward(2, after(x, runs[1][1])))
        moved = [start_move(run[2:], n_dp) for run in runs] if fast else []
        back_parts, dot_parts = [run[0] for run in runs], [run[1] for run in runs]
        back_other = combine(place, after(rank, *moved[0]) if fast else rank, back_parts, dot_parts)
        arrived = lax.ppermute(back_other, "row", SWAP)
        back_mine = combine(place, rank, back_parts, dot_parts, arrived)
        back_mine = after(back_mine, forth_sums)
        back_sums = lax.all_to_all(back_mine, "col", 0, 0, tiled=True)

        if fast:
            w_in_parts = [in_part, in_got]
        else:
            own = own_bit("dp", last_bit)
            w_in_rows = lines_first(joined(in_part, in_got, own))[None]
            half = w_in_rows.shape[2] // 2
            upper, lower = w_in_rows[:, :, :half], w_in_rows[:, :, half:]
            w_in_parts = [jnp.where(place[4] == 0, upper, lower), jnp.where(place[4] == 0, lower, upper)]
        if fast:

            def chunk_of(which, *events):
                keep_a, keep_b = after((runs[which][3], runs[which][5]), *events)
                return keep_a, moved[which][0], keep_b, moved[which][1]

            sums = first_sum(place, chunk_of(0, back_mine), cuts[0], cuts[2])
            gate_middle = (sums[1],) + moved[1]
        else:
            gate_middle = ()
        w_in_parts += [lax.ppermute(after(part, back_mine), "row", SWAP) for part in w_in_parts]

        middle_grad, branch_grad, attended_grad = middle_back(
            place, back_sums, gates, middle, cotangent, after(gain_two, *w_in_parts[2:], *gate_middle),
            w_router_rows, w_out_mine, w_out_other,
        )
        if fast:
            sums = first_sum(place, chunk_of(1, branch_grad), cuts[1], cuts[2], sums)
            started = [second_move(sums, n_dp)]
        attended_grad = lax.all_to_all(attended_grad, ("row", "col"), 0, 0, tiled=True)
        if fast:
            attended_grad = after(attended_grad, sums[1], *moved[2])
        branch_all = gather_group(after(branch_grad, attended_grad))

        attended_grad = attended_grad.reshape(group, 2 * LANES)
        projected_grad, own_grads = attend_back(
            query, key, value, attended_grad, totals, start_row, cosine, sine, normed_one, w_natural, gain_column
        )
        projected_all = lax.all_to_all(projected_grad, ("row", "col"), 0, 0, tiled=True)
        if fast:
            started.append(second_move(first_sum(place, chunk_of(2, own_grads, started[0][1], started[0][3])), n_dp))
            normed_two = after(normed_two, started[1][1], started[1][3])
        *w_parts, small = out_weights(
            place, branch_all, attended, normed_two.reshape(group, width), own_grads,
            members * 8, local_experts, fast,
        )
        expert_grads = None
        if fast:
            w_moved = start_move(w_parts, n_dp)
            held_a, got_a, held_b, got_b = started[0]
            held_a, held_b = after((held_a, held_b), small)
            expert_grads = last_sum(held_a, got_a, held_b, got_b, 0, local_experts, None)
        else:
            cut = w_parts[0].reshape(1, n_dp, width // n_dp, w_parts[0].shape[1])
            w_sum = reduce_over_dp(cut, n_dp)[0]

        mixed = (middle + jnp.sum(after(forth_sums, projected_grad).astype(f32), axis=0)).astype(bf16)

        used = small.reshape(members, 8, width)[:, :local_experts].reshape(members * local_experts, width)
        both = sum_dp(jnp.concatenate([used, small[7:8]], axis=0), sizes)
        w_router_grad = both[: members * local_experts].T
        gain_moe_grad = both[members * local_experts]

        tokens_grad, share = input_grad(
            place, projected_all, w_in_parts, tokens, middle_grad, after(gain_one, w_parts[0])
        )
        gain_attn_grad = sum_dp((share[0:4] + share[4:8]).reshape(8, width // 8), sizes).reshape(width)

        local_q, local_k = w_query.shape[1], w_key.shape[1]
        if fast:
            expert_grads = last_sum(*started[1], cuts[2], local_experts, expert_grads)
            w_sums = second_move(
                first_sum(place, (w_parts[1], w_moved[0], w_parts[3], w_moved[1])), n_dp
            )
            w_query_grad, w_key_grad, w_value_grad, w_out_grad = last_weights(
                w_sums, (local_q, local_k, local_k, local_q)
            )
        else:
            expert_grads = []
            for which in range(3):
                parts = [run[2 + which] for run in runs]
                parts = [part.reshape(part.shape[0], n_dp, width // n_dp, part.shape[2]) for part in parts]
                expert_grads.append(jnp.concatenate([reduce_over_dp(part, n_dp) for part in parts], axis=0))
            cut = local_q + local_k
            w_query_grad, w_key_grad = w_sum[:, :local_q], w_sum[:, local_q:cut]
            w_out_grad, w_value_grad = w_sum[:, cut : cut + local_q], w_sum[:, cut + local_q :]
        w_gate_grad, w_up_grad, w_down_grad = expert_grads
        return (
            mixed, tokens_grad, gain_attn_grad, w_query_grad, w_key_grad, w_value_grad, w_out_grad,
            gain_moe_grad, w_router_grad, w_gate_grad, w_up_grad, w_down_grad,
        )

    return local


def solution(mesh):
    return jax.shard_map(
        layer(dict(mesh.shape)),
        mesh=mesh,
        in_specs=(
            P(("dp", "row", "col"), None),
            P(("dp", "row", "col"), None),
            P(("dp", "row", "col"), None),
            P("dp", None),
            P(),
            P(None, ("row", "col")),
            P(None, ("row", "col")),
            P(None, ("row", "col")),
            P(None, ("row", "col")),
            P(),
            P(),
            P(("row", "col"), None, None),
            P(("row", "col"), None, None),
            P(("row", "col"), None, None),
        ),
        out_specs=(
            P(("dp", "row", "col"), None),
            P(("dp", "row", "col"), None),
            P(),
            P("dp", ("row", "col")),
            P("dp", ("row", "col")),
            P("dp", ("row", "col")),
            P("dp", ("row", "col")),
            P(),
            P(),
            P(("row", "col"), "dp", None),
            P(("row", "col"), "dp", None),
            P(("row", "col"), "dp", None),
        ),
        check_vma=False,
    )
```

```python
import math

import jax
import jax.numpy as jnp
import numpy as np
from jax import lax
from jax.experimental import pallas as pl
from jax.experimental.pallas import tpu as pltpu
from jax.sharding import PartitionSpec as P

HEAD_DIM = 64
EXPERTS = 40
TOP = 8
CAPACITY = 64
COLS = 4
LANES = 128
QUERY_BLOCK = 256
DOT_ROWS = 16

epsilon = 1e-06
rope_base = 10000.0
masked_score = -1e30
f32 = jnp.float32
bf16 = jnp.bfloat16
VMEM_LIMIT = 56 * 1024 * 1024

NT = (((1,), (1,)), ((), ()))
TN = (((0,), (0,)), ((), ()))


def dot(a, b):
    return jnp.dot(a, b, preferred_element_type=f32)


def dot_nt(a, b):
    return lax.dot_general(a, b, NT, preferred_element_type=f32)


def dot_tn(a, b):
    return lax.dot_general(a, b, TN, preferred_element_type=f32)


def lane_of(shape):
    return lax.broadcasted_iota(jnp.int32, shape, len(shape) - 1)


def call(
    kernel, grid, prefetch, in_specs, out_specs, out_shape, scratch=(), us=1.0, aliases=None
):
    return pl.pallas_call(
        kernel,
        grid_spec=pltpu.PrefetchScalarGridSpec(
            num_scalar_prefetch=prefetch,
            grid=grid,
            in_specs=in_specs,
            out_specs=out_specs,
            scratch_shapes=list(scratch),
        ),
        out_shape=out_shape,
        input_output_aliases=aliases or {},
        compiler_params=pltpu.CompilerParams(
            vmem_limit_bytes=VMEM_LIMIT, dimension_semantics=("arbitrary",) * len(grid)
        ),
        cost_estimate=pl.CostEstimate(
            flops=int(us * 1.1e9), bytes_accessed=int(us * 3.6e6), transcendentals=0
        ),
    )


def whole(shape):
    zeros = (0,) * len(shape)
    return pl.BlockSpec(shape, lambda *_: zeros)


def struct(shape, dtype):
    return jax.ShapeDtypeStruct(shape, dtype)


def turn_within_heads(values, sign):
    lane = lane_of(values.shape) % HEAD_DIM
    ahead = pltpu.roll(values, LANES - HEAD_DIM // 2, 1)
    behind = pltpu.roll(values, HEAD_DIM // 2, 1)
    return jnp.where(lane < HEAD_DIM // 2, -sign * ahead, sign * behind)


def project_kernel(
    tok_ref, gain_ref, w_ref, cos_ref, sin_ref, query_ref, key_ref, value_ref, normed_ref
):
    resid = tok_ref[...].astype(f32)
    inverse = lax.rsqrt(jnp.mean(resid * resid, axis=1, keepdims=True) + epsilon)
    normed = (resid * inverse * gain_ref[...]).astype(bf16)
    normed_ref[...] = normed
    raw = dot_nt(normed, w_ref[...])
    cosine, sine = cos_ref[...], sin_ref[...]

    def rot(values):
        return (values * cosine + turn_within_heads(values, 1.0) * sine).astype(bf16).astype(f32)

    first = rot(raw[:, :LANES])
    second = rot(raw[:, LANES : 2 * LANES])
    low = lane_of(first.shape) < HEAD_DIM
    scale = 1.0 / math.sqrt(HEAD_DIM)
    query_ref[0] = jnp.where(low, first * scale, 0.0).astype(bf16)
    query_ref[1] = jnp.where(low, 0.0, first * scale).astype(bf16)
    query_ref[2] = jnp.where(low, second * scale, 0.0).astype(bf16)
    key_ref[...] = jnp.where(low, pltpu.roll(second, HEAD_DIM, 1), second).astype(bf16)
    value_ref[...] = raw[:, 2 * LANES :].astype(bf16)


def project(tokens, gain, w_stack, cosine, sine):
    total, width = tokens.shape
    rows = 512
    lanes = pl.BlockSpec((rows, LANES), lambda j: (j, 0))
    wide = pl.BlockSpec((rows, width), lambda j: (j, 0))
    return call(
        project_kernel,
        (total // rows,),
        0,
        [wide, whole((1, width)), whole(w_stack.shape), lanes, lanes],
        [pl.BlockSpec((3, rows, LANES), lambda j: (0, j, 0)), lanes, lanes, wide],
        [
            struct((3, total, LANES), bf16),
            struct((total, LANES), bf16),
            struct((total, LANES), bf16),
            struct((total, width), bf16),
        ],
        us=0.5,
    )(tokens, gain, w_stack, cosine, sine)


def attend_kernel(query_ref, key_ref, value_ref, start_ref, packed_ref, plain_ref, total_ref, out_ref):
    blocks = query_ref.shape[1] // QUERY_BLOCK
    block = pl.program_id(0)
    for index in range(blocks):

        @pl.when(block == index)
        def _(index=index):
            rows = pl.ds(index * QUERY_BLOCK, QUERY_BLOCK)
            span = (index + 1) * QUERY_BLOCK
            row = index * QUERY_BLOCK + lax.broadcasted_iota(jnp.int32, (QUERY_BLOCK, span), 0)
            column = lane_of((QUERY_BLOCK, span))
            allowed = (column <= row) & (column >= start_ref[rows, :])

            def head(number, carry):
                scores = dot_nt(query_ref[number, rows, :], key_ref[0:span, :])
                scores = jnp.where(allowed, scores, masked_score)
                peak = jnp.max(scores, axis=1, keepdims=True)
                weights = jnp.exp(scores - peak)
                summed = jnp.sum(weights, axis=1, keepdims=True)
                probs = (weights * (1.0 / summed)).astype(bf16)
                out_ref[number] = dot(probs, value_ref[0:span, :])
                total = jnp.broadcast_to(peak + jnp.log(summed), (QUERY_BLOCK, LANES))
                total_ref[number, :, rows] = jnp.transpose(total)[0:8, :]
                return carry

            lax.fori_loop(0, 3, head, 0)
            low = lane_of((QUERY_BLOCK, LANES)) < HEAD_DIM
            one, two, three = out_ref[0], out_ref[1], out_ref[2]
            pair = jnp.where(low, one, two).astype(bf16)
            plain_ref[rows, 0:LANES] = pair
            plain_ref[rows, LANES : 2 * LANES] = jnp.where(low, three, 0.0).astype(bf16)
            if index < blocks // 2:
                packed_ref[rows, 0:LANES] = pair
                packed_ref[rows, LANES : 2 * LANES] = three.astype(bf16)
            else:
                back = pl.ds((index - blocks // 2) * QUERY_BLOCK, QUERY_BLOCK)
                before = packed_ref[back, LANES : 2 * LANES].astype(f32)
                packed_ref[back, LANES : 2 * LANES] = jnp.where(low, before, one).astype(bf16)
                packed_ref[back, 2 * LANES : 3 * LANES] = jnp.where(low, two, three).astype(bf16)


def attend(query, key, value, start):
    total = key.shape[0]
    return call(
        attend_kernel,
        (total // QUERY_BLOCK,),
        0,
        [whole(query.shape), whole(key.shape), whole(value.shape), whole(start.shape)],
        [whole((total // 2, 3 * LANES)), whole((total, 2 * LANES)), whole((3, 8, total))],
        [
            struct((total // 2, 3 * LANES), bf16),
            struct((total, 2 * LANES), bf16),
            struct((3, 8, total), f32),
        ],
        scratch=[pltpu.VMEM((3, QUERY_BLOCK, LANES), f32)],
        us=0.5,
    )(query, key, value, start)


def attend_back_kernel(
    query_ref, key_ref, value_ref, grad_ref, total_ref, start_ref, cos_ref, sin_ref, normed_ref, w_ref, gain_ref,
    blocks_ref, own_ref, out_ref, query_grad_ref, key_grad_ref, value_grad_ref, own_sum_ref
):
    blocks = query_ref.shape[1] // QUERY_BLOCK
    block = pl.program_id(0)
    scale = 1.0 / math.sqrt(HEAD_DIM)

    @pl.when(block == 0)
    def _():
        key_grad_ref[...] = jnp.zeros_like(key_grad_ref)
        value_grad_ref[...] = jnp.zeros_like(value_grad_ref)

    def back(values, cosine, sine):
        return values * cosine + turn_within_heads(values * sine, -1.0)

    for index in range(blocks):

        @pl.when(block == index)
        def _(index=index):
            rows = pl.ds(index * QUERY_BLOCK, QUERY_BLOCK)
            span = (index + 1) * QUERY_BLOCK
            row = index * QUERY_BLOCK + lane_of((span, QUERY_BLOCK))
            column = lax.broadcasted_iota(jnp.int32, (span, QUERY_BLOCK), 0)
            allowed = (column <= row) & (column >= start_ref[0:1, rows])
            low = lane_of((QUERY_BLOCK, LANES)) < HEAD_DIM

            def head(number, carry):
                query = query_ref[number, rows, :]
                tile = pl.multiple_of((number // 2) * LANES, LANES)
                upstream = grad_ref[rows, pl.ds(tile, LANES)].astype(f32)
                keep = low == (number != 1)
                upstream = jnp.where(keep, upstream, 0.0).astype(bf16)
                scores = dot_nt(key_ref[0:span, :], query)
                probs = jnp.exp(scores - total_ref[number, 0:1, rows])
                probs = jnp.where(allowed, probs, 0.0)
                prob_grad = dot_nt(value_ref[0:span, :], upstream)
                row_dot = jnp.sum(probs * prob_grad, axis=0, keepdims=True)
                score_grad = (probs * (prob_grad - row_dot)).astype(bf16)
                key_grad_ref[0:span, :] += dot(score_grad, query)
                value_grad_ref[0:span, :] += dot(probs.astype(bf16), upstream)
                query_grad_ref[number] = dot_tn(score_grad, key_ref[0:span, :]) * scale
                return carry

            lax.fori_loop(0, 3, head, 0)
            cosine, sine = cos_ref[rows, :], sin_ref[rows, :]
            pair = jnp.where(low, query_grad_ref[0], query_grad_ref[1])
            out_ref[rows, 0:LANES] = back(pair, cosine, sine).astype(bf16)
            out_ref[rows, LANES : 2 * LANES] = back(query_grad_ref[2], cosine, sine).astype(bf16)

    @pl.when(block == blocks - 1)
    def _():
        low = lane_of(key_grad_ref.shape) < HEAD_DIM
        key_grad = key_grad_ref[...]
        key_grad = key_grad + pltpu.roll(key_grad, HEAD_DIM, 1)
        key_grad = back(key_grad, cos_ref[...], sin_ref[...])
        before = out_ref[:, LANES : 2 * LANES].astype(f32)
        out_ref[:, LANES : 2 * LANES] = jnp.where(low, before, key_grad).astype(bf16)
        value_grad = value_grad_ref[...]
        value_grad = value_grad + pltpu.roll(value_grad, HEAD_DIM, 1)
        out_ref[:, 2 * LANES : 3 * LANES] = jnp.where(low, 0.0, value_grad).astype(bf16)
        chunk = 512
        own_sum_ref[...] = jnp.zeros_like(own_sum_ref)

        def add(index, carry):
            part = pl.ds(pl.multiple_of(index * chunk, chunk), chunk)
            own_sum_ref[...] += dot_tn(normed_ref[part, :], out_ref[part, :])
            return carry

        lax.fori_loop(0, out_ref.shape[0] // chunk, add, 0)
        own = own_sum_ref[...]
        own_ref[...] = own.astype(bf16)
        share = jnp.sum(own * w_ref[...].astype(f32), axis=1, keepdims=True) / gain_ref[...]
        share = jnp.transpose(jnp.broadcast_to(share, (share.shape[0], LANES)))[0:8, :]
        width = blocks_ref.shape[2]
        row = lax.broadcasted_iota(jnp.int32, (8, width), 0)
        terms = jnp.zeros((8, width), f32)
        for index in range(share.shape[1] // width):
            piece = share[:, index * width : (index + 1) * width]
            upper = piece.astype(bf16).astype(f32)
            terms = jnp.where(row == index, upper, jnp.where(row == index + 4, piece - upper, terms))
        terms = jnp.concatenate([terms, jnp.zeros((8, width), f32)], axis=0).astype(bf16)
        rows = blocks_ref.shape[1] - DOT_ROWS
        for index in range(blocks_ref.shape[0]):
            blocks_ref[index, 0:rows, :] = out_ref[index * rows : (index + 1) * rows, :]
            blocks_ref[index, rows:, :] = terms


def attend_back(query, key, value, grad, totals, start, cosine, sine, normed, w_natural, gain):
    total = key.shape[0]
    members = 2 * COLS
    rows = total // members + DOT_ROWS
    args = (query, key, value, grad, totals, start, cosine, sine, normed, w_natural, gain)
    return call(
        attend_back_kernel,
        (total // QUERY_BLOCK,),
        0,
        [whole(item.shape) for item in args],
        [whole((members, rows, 3 * LANES)), whole(w_natural.shape)],
        [struct((members, rows, 3 * LANES), bf16), struct(w_natural.shape, bf16)],
        scratch=[
            pltpu.VMEM((total, 3 * LANES), bf16),
            pltpu.VMEM((3, QUERY_BLOCK, LANES), f32),
            pltpu.VMEM((total, LANES), f32),
            pltpu.VMEM((total, LANES), f32),
            pltpu.VMEM(w_natural.shape, f32),
        ],
        us=0.5,
    )(*args)


def branch_operand(refs):
    rows = refs.shape[2]
    low = lane_of((rows, LANES)) < HEAD_DIM
    pairs, thirds = [], []
    for member in range(refs.shape[1]):
        one = refs[0, member, :, 0:LANES]
        mid = refs[0, member, :, LANES : 2 * LANES].astype(f32)
        end = refs[0, member, :, 2 * LANES : 3 * LANES].astype(f32)
        mid_turned = pltpu.roll(mid, HEAD_DIM, 1)
        end_turned = pltpu.roll(end, HEAD_DIM, 1)
        late = jnp.where(low, mid_turned, end_turned).astype(bf16)
        pairs.append(jnp.concatenate([one, late], axis=0))
        thirds.append((mid, end_turned))
    for member in range(0, refs.shape[1], 2):
        tops = []
        for which in range(2):
            left, right = thirds[member][which], thirds[member + 1][which]
            tops.append(jnp.where(low, left, pltpu.roll(right, HEAD_DIM, 1)).astype(bf16))
        pairs.append(jnp.concatenate(tops, axis=0))
    return jnp.concatenate(pairs, axis=1)


def branch_weights(ref):
    right = [ref[source, 0:LANES] for source in range(ref.shape[0])]
    return jnp.concatenate(right + [ref[source, LANES:] for source in range(ref.shape[0])], axis=0)


def hits_of(rank, local_experts):
    place = lax.broadcasted_iota(jnp.int32, (CAPACITY, rank.shape[1]), 0).astype(f32)
    return [place == rank[j : j + 1, :] for j in range(local_experts)]


def chosen_of(hits):
    return jnp.concatenate([jnp.where(hit, 1.0, 0.0).astype(bf16) for hit in hits], axis=0)


def middle_kernel(
    place_ref, att_mine_ref, att_other_ref, w_mine_ref, w_other_ref, tok_a_ref, tok_b_ref, routes_a_ref, routes_b_ref,
    gain_ref, w_router_ref, after_ref,
    x_ref, slot_gate_ref, rank_ref, gate_ref, normed_ref, middle_ref, gates_own_ref, gates_ref, ranks_ref
):
    step = pl.program_id(0)
    member = place_ref[2]
    cols = pl.num_programs(0)
    rows = tok_a_ref.shape[0]
    local_experts = x_ref.shape[0]
    branch = dot(branch_operand(att_mine_ref), branch_weights(w_mine_ref))
    branch = branch + dot(branch_operand(att_other_ref), branch_weights(w_other_ref))
    for half in range(2):
        tok_ref, routes_ref = ((tok_a_ref, routes_a_ref), (tok_b_ref, routes_b_ref))[half]
        middle = tok_ref[...].astype(f32) + branch[half * rows : (half + 1) * rows]
        inverse = lax.rsqrt(jnp.mean(middle * middle, axis=1, keepdims=True) + epsilon)
        normed = (middle * inverse * gain_ref[...]).astype(bf16)
        normed_ref[half, 0] = normed
        logits = dot_nt(w_router_ref[...], normed)
        padded = logits.shape[0]
        slot = lax.broadcasted_iota(jnp.int32, (padded, rows), 0)
        expert = (slot // 8) * local_experts + slot % 8
        expert = jnp.where(slot % 8 < local_experts, expert, -1).astype(f32)
        routes = routes_ref[0].astype(f32)
        named = expert == routes[0:1, 0:rows]
        for k in range(1, TOP):
            named = named | (expert == routes[k : k + 1, 0:rows])
        peak = jnp.max(jnp.where(named, logits, masked_score), axis=0, keepdims=True)
        weights = jnp.where(named, jnp.exp(logits - peak), 0.0)
        gates = weights / jnp.sum(weights, axis=0, keepdims=True)
        gates_ref[...] = gates
        ranks_ref[...] = jnp.where(named, dot(named.astype(f32).astype(bf16), after_ref[...]), -1.0)
        here = pl.ds(pl.multiple_of(member * 8, 8), 8)
        gate, rank = gates_ref[here, :], ranks_ref[here, :]
        rank_ref[half, 0] = rank
        gate_ref[half, 0] = gate
        hits = hits_of(rank, local_experts)
        slot_gate = jnp.concatenate(
            [jnp.sum(jnp.where(hit, gate[j : j + 1, :], 0.0), axis=1, keepdims=True) for j, hit in enumerate(hits)],
            axis=0,
        )
        chosen = chosen_of(hits)
        picked = dot(chosen, normed).astype(bf16)
        spread = jnp.broadcast_to(slot_gate, (slot_gate.shape[0], LANES))
        for j in range(local_experts):
            part = slice(j * CAPACITY, (j + 1) * CAPACITY)
            x_ref[j, half, 0] = picked[part]
            slot_gate_ref[j, half, 0] = spread[part]

        @pl.when(member == half * cols + step)
        def _(middle=middle, gates=gates):
            middle_ref[...] = middle
            gates_own_ref[...] = gates


def middle_and_dispatch(place, att, w_mine, w_other, tokens, routes, gain, w_router, local_experts):
    width = tokens.shape[1]
    half = COLS
    rows = tokens.shape[0] // (2 * half)
    padded = w_router.shape[0]
    after = jnp.asarray(np.triu(np.ones((rows, rows), np.float32), 1), bf16)
    slot_shape = (local_experts, 2, half, CAPACITY)
    early = pl.BlockSpec((rows, width), lambda i, p: (i, 0))
    late = pl.BlockSpec((rows, width), lambda i, p: (i + half, 0))
    routes_shape = (1,) + routes.shape[1:]
    return call(
        middle_kernel,
        (half,),
        1,
        [
            pl.BlockSpec((1, half, rows, 3 * LANES), lambda i, p: (p[0], 0, i, 0)),
            pl.BlockSpec((1, half, rows, 3 * LANES), lambda i, p: (1 - p[0], 0, i, 0)),
            whole(w_mine.shape),
            whole(w_other.shape),
            early,
            late,
            pl.BlockSpec(routes_shape, lambda i, p: (i, 0, 0)),
            pl.BlockSpec(routes_shape, lambda i, p: (i + half, 0, 0)),
            whole((1, width)),
            whole(w_router.shape),
            whole((rows, rows)),
        ],
        [
            pl.BlockSpec((local_experts, 2, 1, CAPACITY, width), lambda i, p: (0, 0, i, 0, 0)),
            pl.BlockSpec((local_experts, 2, 1, CAPACITY, LANES), lambda i, p: (0, 0, i, 0, 0)),
            pl.BlockSpec((2, 1, 8, rows), lambda i, p: (0, i, 0, 0)),
            pl.BlockSpec((2, 1, 8, rows), lambda i, p: (0, i, 0, 0)),
            pl.BlockSpec((2, 1, rows, width), lambda i, p: (0, i, 0, 0)),
            whole((rows, width)),
            whole((padded, rows)),
        ],
        [
            struct(slot_shape + (width,), bf16),
            struct(slot_shape + (LANES,), f32),
            struct((2, half, 8, rows), f32),
            struct((2, half, 8, rows), f32),
            struct((2, half, rows, width), bf16),
            struct((rows, width), f32),
            struct((padded, rows), f32),
        ],
        scratch=[pltpu.VMEM((padded, rows), f32), pltpu.VMEM((padded, rows), f32)],
        us=0.5,
    )(place, att, att, w_mine, w_other, tokens, tokens, routes, routes, gain, w_router, after)


def grad_dispatch_kernel(rank_ref, gate_ref, cot_ref, g_ref):
    local_experts = g_ref.shape[0]
    rows = cot_ref.shape[0] // 2
    for half in range(2):
        hits = hits_of(rank_ref[half], local_experts)
        gate = gate_ref[half]
        slot_gate = jnp.concatenate(
            [jnp.sum(jnp.where(hit, gate[j : j + 1, :], 0.0), axis=1, keepdims=True) for j, hit in enumerate(hits)],
            axis=0,
        )
        grads = (dot(chosen_of(hits), cot_ref[half * rows : (half + 1) * rows, :]) * slot_gate).astype(bf16)
        for j in range(local_experts):
            g_ref[j, half] = grads[j * CAPACITY : (j + 1) * CAPACITY]


def grad_dispatch(rank, gate, cotangents, local_experts):
    members, _, rows = rank.shape
    width = cotangents.shape[1]
    small = pl.BlockSpec((2, 8, rows), lambda j: (j, 0, 0))
    return call(
        grad_dispatch_kernel,
        (members // 2,),
        0,
        [small, small, pl.BlockSpec((2 * rows, width), lambda j: (j, 0))],
        pl.BlockSpec((local_experts, 2, CAPACITY, width), lambda j: (0, j, 0, 0)),
        struct((local_experts, members, CAPACITY, width), bf16),
        us=0.5,
    )(rank, gate, cotangents)


def expert_kernel(
    x_ref, gate_ref, w_gate_ref, w_up_ref, w_down_ref, forth_ref, active_ref, factor_ref, silu_ref
):
    gate_pre = dot(x_ref[0], w_gate_ref[0])
    up_pre = dot(x_ref[0], w_up_ref[0])
    sig = 1.0 / (1.0 + jnp.exp(-gate_pre))
    silu = gate_pre * sig
    silu_ref[0] = silu
    factor_ref[0] = up_pre * sig * (1.0 + gate_pre * (1.0 - sig))
    active_ref[0] = (silu * up_pre).astype(bf16)
    produced = dot_nt(active_ref[0], w_down_ref[0]).astype(bf16).astype(f32)
    forth_ref[0] = (produced * gate_ref[0, :, 0:1]).astype(bf16)


def run_experts(x, slot_gate, w_gate, w_up, w_down):
    count, slots, width = x.shape
    hidden = w_gate.shape[2]

    def per_expert(*shape):
        return pl.BlockSpec((1,) + shape, lambda e: (e, 0, 0))

    return call(
        expert_kernel,
        (count,),
        0,
        [per_expert(slots, width), per_expert(slots, LANES)] + [per_expert(width, hidden)] * 3,
        [per_expert(slots, width)] + [per_expert(slots, hidden)] * 3,
        [
            struct((count, slots, width), bf16),
            struct((count, slots, hidden), bf16),
            struct((count, slots, hidden), f32),
            struct((count, slots, hidden), f32),
        ],
        us=0.5,
    )(x, slot_gate, w_gate, w_up, w_down)


def expert_back_kernel(place_ref, *refs, fast):
    x_ref, g_ref, active_ref, factor_ref, silu_ref = refs[:5]
    w_gate_ref, w_up_ref, w_down_ref, back_ref, dots_ref = refs[5:10]
    grads, (gate_low_ref, up_low_ref) = refs[10:-2], refs[-2:]
    slots, width = g_ref.shape[1], g_ref.shape[2]
    chunk = 256
    active_grad = dot(g_ref[0], w_down_ref[0])
    gate_low_ref[...] = (active_grad * factor_ref[0]).astype(bf16)
    up_low_ref[...] = (active_grad * silu_ref[0]).astype(bf16)
    dots = jnp.sum(active_ref[0].astype(f32) * active_grad, axis=1, keepdims=True)
    dots_ref[0] = jnp.broadcast_to(dots, (slots, LANES))
    back_ref[0] = (dot_nt(gate_low_ref[...], w_gate_ref[0]) + dot_nt(up_low_ref[...], w_up_ref[0])).astype(bf16)

    def products(cols):
        x = x_ref[0, :, cols]
        yield 0, dot_tn(x, gate_low_ref[...]).astype(bf16)
        yield 1, dot_tn(x, up_low_ref[...]).astype(bf16)
        yield 2, dot_tn(g_ref[0, :, cols], active_ref[0]).astype(bf16)

    if fast:
        write_shards(place_ref, grads, products, width)
    else:

        def whole_columns(index, carry):
            cols = pl.ds(pl.multiple_of(index * chunk, chunk), chunk)
            for which, product in products(cols):
                grads[which][0, cols, :] = product
            return carry

        lax.fori_loop(0, width // chunk, whole_columns, 0)


def write_shards(place_ref, outs, products, width):
    send_a, keep_a, send_b, keep_b = outs
    x_bit, y_bit = place_ref[3], place_ref[4]
    shard = width // 4
    for dy in range(2):
        for dx in range(2):
            x, y = x_bit ^ dx, y_bit ^ dy
            cols = pl.ds(pl.multiple_of((y * 2 + x) * shard, shard), shard)
            for which, product in products(cols):
                side = product.shape[1] // 2
                (send_a if dx else keep_a)[0, which, y] = product[:, :side]
                (send_b if dy else keep_b)[0, which, x] = product[:, side:]


def run_experts_back(place, x, g, active, factor, silu, w_gate, w_up, w_down, first, count, fast):
    slots, width = g.shape[1], g.shape[2]
    hidden = w_gate.shape[2]

    def taken(*shape):
        return pl.BlockSpec((1,) + shape, lambda e, p: (e + first, 0, 0))

    def given(*shape):
        zeros = (0,) * len(shape)
        return pl.BlockSpec((1,) + shape, lambda e, p: (e,) + zeros)

    if fast:
        grad_shapes = [(3, 2, width // 4, hidden // 2)] * 4
    else:
        grad_shapes = [(width, hidden)] * 3
    return call(
        lambda *refs: expert_back_kernel(*refs, fast=fast),
        (count,),
        1,
        [taken(slots, width)] * 2 + [taken(slots, hidden)] * 3 + [taken(width, hidden)] * 3,
        [given(slots, width), given(slots, LANES)] + [given(*shape) for shape in grad_shapes],
        [struct((count, slots, width), bf16), struct((count, slots, LANES), f32)]
        + [struct((count,) + shape, bf16) for shape in grad_shapes],
        scratch=[pltpu.VMEM((slots, hidden), bf16)] * 2,
        us=0.5,
    )(place, x, g, active, factor, silu, w_gate, w_up, w_down)


DOT_LANES = 2 * LANES


def combine_kernel(place_ref, rank_ref, *refs, pieces, with_dots, mine):
    parts, rest = refs[:pieces], refs[pieces:]
    rows = rank_ref.shape[2]
    local_experts = sum(part.shape[0] for part in parts)
    hits = hits_of(rank_ref[0], local_experts)
    gathered = jnp.concatenate([part[j, 0] for part in parts for j in range(part.shape[0])], axis=0)
    summed = dot_tn(chosen_of(hits), gathered)
    out_ref = rest[-1]
    if mine:
        arrived_ref = rest[-2]
        summed = summed + arrived_ref[0, 0:rows, :].astype(f32)
    out_ref[0, 0:rows, :] = summed.astype(bf16)
    if with_dots:
        column = [part[j, 0][:, 0:1] for part in rest[:pieces] for j in range(part.shape[0])]
        scattered = [
            jnp.sum(jnp.where(hit, value, 0.0), axis=0, keepdims=True) for hit, value in zip(hits, column)
        ]
        scattered.append(jnp.zeros((DOT_ROWS - local_experts, rows), f32))
        scattered = jnp.concatenate(scattered, axis=0)
        upper = scattered.astype(bf16)
        out_ref[0, rows:, :] = jnp.zeros((DOT_ROWS, out_ref.shape[2]), bf16)
        out_ref[0, rows:, 0:rows] = upper
        out_ref[0, rows:, DOT_LANES : DOT_LANES + rows] = (scattered - upper.astype(f32)).astype(bf16)
        if mine:
            out_ref[0, rows:, 2 * DOT_LANES : 4 * DOT_LANES] = arrived_ref[0, rows:, 0 : 2 * DOT_LANES]


def combine(place, rank, parts, dots=None, arrived=None):
    mine = arrived is not None
    rows, width = rank.shape[2], parts[0].shape[-1]
    out_rows = rows + (DOT_ROWS if dots else 0)

    def member(step, p):
        return (p[0] if mine else 1 - p[0]) * COLS + step

    def slots_of(array):
        return pl.BlockSpec((array.shape[0], 1) + array.shape[2:], lambda j, p: (0, member(j, p), 0, 0))

    inputs = [
        part.reshape(part.shape[0], 2 * COLS, CAPACITY, part.shape[-1]) for part in list(parts) + list(dots or [])
    ]
    in_specs = [pl.BlockSpec((1, 8, rows), lambda j, p: (member(j, p), 0, 0))] + [slots_of(item) for item in inputs]
    by_chip = pl.BlockSpec((1, out_rows, width), lambda j, p: (j, 0, 0))
    if mine:
        inputs.append(arrived)
        in_specs.append(by_chip)
    return call(
        lambda *refs: combine_kernel(*refs, pieces=len(parts), with_dots=bool(dots), mine=mine),
        (COLS,),
        1,
        in_specs,
        by_chip,
        struct((COLS, out_rows, width), bf16),
        us=0.5,
    )(place, rank, *inputs)


def split_dot(dimension_numbers, values, exact):
    upper = values.astype(bf16)
    lower = (values - upper.astype(f32)).astype(bf16)
    return lax.dot_general(
        upper, exact, dimension_numbers, preferred_element_type=f32
    ) + lax.dot_general(lower, exact, dimension_numbers, preferred_element_type=f32)


EXTRA_SLOTS = 6


def middle_back_kernel(
    place_ref, sums_ref, gates_ref, middle_ref, cot_ref, gain_ref, w_router_ref, w_mine_ref, w_other_ref,
    grad_ref, branch_ref, attended_ref, extra_ref
):
    rows = middle_ref.shape[0]
    tail = sums_ref[:, rows : rows + 8, 0 : 4 * DOT_LANES].astype(f32)
    mine = tail[:, :, 0:rows] + tail[:, :, DOT_LANES : DOT_LANES + rows]
    other = tail[:, :, 2 * DOT_LANES : 2 * DOT_LANES + rows] + tail[:, :, 3 * DOT_LANES : 3 * DOT_LANES + rows]
    first_row = place_ref[0] == 0
    dots = jnp.concatenate([jnp.where(first_row, mine, other), jnp.where(first_row, other, mine)], axis=0)
    dots = dots.reshape(dots.shape[0] * 8, rows)
    gates = gates_ref[...]
    logit_grad = dots - gates * jnp.sum(dots, axis=0, keepdims=True)
    middle = middle_ref[...]
    inverse = lax.rsqrt(jnp.mean(middle * middle, axis=1, keepdims=True) + epsilon)
    unit = middle * inverse
    gain = gain_ref[...]
    grad = sums_ref[0, 0:rows].astype(f32)
    for index in range(1, sums_ref.shape[0]):
        grad = grad + sums_ref[index, 0:rows].astype(f32)
    grad = grad + split_dot(TN, logit_grad, w_router_ref[...])
    gain_grad = jnp.sum(grad * unit, axis=0, keepdims=True)
    scaled = grad * gain
    middle_grad = cot_ref[...].astype(f32) + inverse * (
        scaled - unit * jnp.mean(scaled * unit, axis=1, keepdims=True)
    )
    grad_ref[...] = middle_grad
    branch_grad = middle_grad.astype(bf16)
    branch_ref[0:rows, :] = branch_grad
    extra_ref[...] = jnp.zeros_like(extra_ref)
    for index in range(logit_grad.shape[0] // 8):
        first, lane = index // EXTRA_SLOTS * 8, index % EXTRA_SLOTS * DOT_LANES
        extra_ref[first : first + 8, lane : lane + rows] = logit_grad[index * 8 : index * 8 + 8]
    upper = gain_grad.astype(bf16).astype(f32)
    extra_ref[13:14, :] = upper
    extra_ref[14:15, :] = gain_grad - upper
    branch_ref[rows:, :] = extra_ref[...].astype(bf16)
    for which, ref in enumerate((w_mine_ref, w_other_ref)):
        line = place_ref[0] if which == 0 else 1 - place_ref[0]
        for col in range(ref.shape[0]):
            product = dot_nt(branch_grad, ref[col])
            member = line * COLS + col
            attended_ref[member, :, 0:LANES] = product[:, 0:LANES].astype(bf16)
            attended_ref[member, :, LANES : LANES + HEAD_DIM] = product[:, LANES:].astype(bf16)
            attended_ref[member, :, LANES + HEAD_DIM :] = jnp.zeros((product.shape[0], HEAD_DIM), bf16)


def middle_back(place, sums, gates, middle, cotangent, gain, w_router, w_mine, w_other):
    rows, width = middle.shape
    members = 2 * COLS
    args = (sums, gates, middle, cotangent, gain, w_router, w_mine, w_other)
    return call(
        middle_back_kernel,
        (1,),
        1,
        [whole(item.shape) for item in args],
        [whole((rows, width)), whole((rows + DOT_ROWS, width)), whole((members, rows, 2 * LANES))],
        [
            struct((rows, width), f32),
            struct((rows + DOT_ROWS, width), bf16),
            struct((members, rows, 2 * LANES), bf16),
        ],
        scratch=[pltpu.VMEM((DOT_ROWS, width), f32)],
        us=0.5,
    )(place, *args)


def input_grad_kernel(
    place_ref, grads_mine_ref, grads_other_ref, mine_a_ref, mine_b_ref, other_a_ref, other_b_ref,
    tok_ref, middle_grad_ref, gain_ref, out_ref, share_ref, sum_ref
):
    step = pl.program_id(0)
    first = place_ref[4] == 0

    def weights(a_ref, b_ref):
        a = jnp.concatenate([a_ref[index, 0] for index in range(a_ref.shape[0])], axis=0)
        b = jnp.concatenate([b_ref[index, 0] for index in range(b_ref.shape[0])], axis=0)
        upper, lower = jnp.where(first, a, b), jnp.where(first, b, a)
        return jnp.concatenate([upper, lower, lower[lower.shape[0] - HEAD_DIM :]], axis=0)

    rows = tok_ref.shape[0]
    part = dot(grads_mine_ref[0, 0:rows, :], weights(mine_a_ref, mine_b_ref))
    part = part + dot(grads_other_ref[0, 0:rows, :], weights(other_a_ref, other_b_ref))
    share = grads_mine_ref[0, rows:, :].astype(f32)[0:8] + grads_other_ref[0, rows:, :].astype(f32)[0:8]

    @pl.when(step == 0)
    def _():
        sum_ref[...] = part
        share_ref[...] = share

    @pl.when(step > 0)
    def _():
        sum_ref[...] += part
        share_ref[...] += share

    @pl.when(step == pl.num_programs(0) - 1)
    def _():
        resid = tok_ref[...].astype(f32)
        inverse = lax.rsqrt(jnp.mean(resid * resid, axis=1, keepdims=True) + epsilon)
        unit = resid * inverse
        scaled = sum_ref[...] * gain_ref[...]
        out_ref[...] = middle_grad_ref[...] + inverse * (
            scaled - unit * jnp.mean(scaled * unit, axis=1, keepdims=True)
        )


def input_grad(place, grads, weights, tokens, middle_grad, gain):
    rows, width = tokens.shape
    lanes = grads.shape[2]
    w_shape = (weights[0].shape[0], 1) + weights[0].shape[2:]
    return call(
        input_grad_kernel,
        (COLS,),
        1,
        [
            pl.BlockSpec((1, rows + DOT_ROWS, lanes), lambda c, p: (p[0] * COLS + c, 0, 0)),
            pl.BlockSpec((1, rows + DOT_ROWS, lanes), lambda c, p: ((1 - p[0]) * COLS + c, 0, 0)),
        ]
        + [pl.BlockSpec(w_shape, lambda c, p: (0, c, 0, 0))] * 4
        + [whole((rows, width)), whole((rows, width)), whole((1, width))],
        [whole((rows, width)), whole((8, lanes))],
        [struct((rows, width), f32), struct((8, lanes), f32)],
        scratch=[pltpu.VMEM((rows, width), f32)],
        us=0.5,
    )(place, grads, grads, *weights, tokens, middle_grad, gain)


def out_weights_kernel(place_ref, branch_ref, att_ref, normed_ref, own_ref, *refs, fast, local_experts):
    outs, small_ref, (sum_ref, gain_sum_ref) = refs[:-3], refs[-3], refs[-2:]
    step = pl.program_id(0)
    rows = att_ref.shape[0] // 2
    block = rows + DOT_ROWS

    @pl.when(step == 0)
    def _():
        sum_ref[...] = jnp.zeros_like(sum_ref)
        small_ref[...] = jnp.zeros_like(small_ref)
        gain_sum_ref[...] = jnp.zeros_like(gain_sum_ref)

    branch = jnp.concatenate([branch_ref[0:rows, :], branch_ref[block : block + rows, :]], axis=0)
    sum_ref[...] += dot_tn(branch, att_ref[...])
    for which in range(2):
        tail = branch_ref[which * block + rows : (which + 1) * block, :].astype(f32)
        slots = []
        for index in range(small_ref.shape[0] // 8):
            first, lane = index // EXTRA_SLOTS * 8, index % EXTRA_SLOTS * DOT_LANES
            slots.append(tail[first : first + 8, lane : lane + rows])
        logit_grad = jnp.concatenate(slots, axis=0)
        real = lax.broadcasted_iota(jnp.int32, logit_grad.shape, 0) % 8 < local_experts
        logit_grad = jnp.where(real, logit_grad, 0.0).astype(bf16)
        small_ref[...] += dot(logit_grad, normed_ref[which * rows : (which + 1) * rows, :])
        gain_sum_ref[...] += tail[8:16, :]

    @pl.when(step == pl.num_programs(0) - 1)
    def _():
        small_ref[7:8, :] = gain_sum_ref[5:6, :] + gain_sum_ref[6:7, :]

        def products(cols):
            own = own_ref[cols, 0 : 2 * LANES]
            out_one = sum_ref[cols, 0:LANES].astype(bf16)
            out_two = sum_ref[cols, LANES:]
            low = lane_of(out_two.shape) < HEAD_DIM
            tail = jnp.where(low, out_two, own_ref[cols, 2 * LANES :].astype(f32)).astype(bf16)
            yield 0, jnp.concatenate([own, out_one, tail], axis=1)

        if fast:
            write_shards(place_ref, outs, products, own_ref.shape[0])
        else:
            outs[0][...] = next(products(slice(0, own_ref.shape[0])))[1]


def out_weights(place, branch, attended, normed, own, padded, local_experts, fast):
    total, width = normed.shape
    rows = total // COLS
    blocks = branch.shape[0] // COLS
    if fast:
        shapes = [(1, 1, 2, width // 4, 2 * LANES)] * 4
    else:
        shapes = [(width, 4 * LANES)]
    return call(
        lambda *refs: out_weights_kernel(*refs, fast=fast, local_experts=local_experts),
        (COLS,),
        1,
        [
            pl.BlockSpec((blocks, width), lambda j, p: (j, 0)),
            pl.BlockSpec((rows, 2 * LANES), lambda j, p: (j, 0)),
            pl.BlockSpec((rows, width), lambda j, p: (j, 0)),
            whole(own.shape),
        ],
        [whole(shape) for shape in shapes] + [whole((padded, width))],
        [struct(shape, bf16) for shape in shapes] + [struct((padded, width), f32)],
        scratch=[pltpu.VMEM((width, 2 * LANES), f32), pltpu.VMEM((8, width), f32)],
        us=0.5,
    )(place, branch, attended, normed, own)


def first_sum_kernel(place_ref, keep_a_ref, got_a_ref, keep_b_ref, got_b_ref, *rest):
    send_a_ref, held_a_ref, send_b_ref, held_b_ref = rest[-4:]
    x_bit, y_bit = place_ref[3], place_ref[4]
    for bit, keep, got, send, held in (
        (y_bit, keep_a_ref, got_a_ref, send_a_ref, held_a_ref),
        (x_bit, keep_b_ref, got_b_ref, send_b_ref, held_b_ref),
    ):
        for kind in range(keep.shape[1]):
            held[0, kind] = (keep[0, kind, bit].astype(f32) + got[0, kind, bit].astype(f32)).astype(bf16)
            send[0, kind] = (keep[0, kind, 1 - bit].astype(f32) + got[0, kind, 1 - bit].astype(f32)).astype(bf16)


def first_sum(place, chunk, first=0, total=None, before=None):
    count, kinds, _, rows, cols = chunk[0].shape
    taken = pl.BlockSpec((1, kinds, 2, rows, cols), lambda e, p: (e, 0, 0, 0, 0))
    given = pl.BlockSpec((1, kinds, rows, cols), lambda e, p: (e + first, 0, 0, 0))
    extra = list(before) if before else []
    return call(
        first_sum_kernel,
        (count,),
        1,
        [taken] * 4 + [pl.BlockSpec(memory_space=pl.ANY)] * len(extra),
        [given] * 4,
        [struct((total or count, kinds, rows, cols), bf16)] * 4,
        us=0.5,
        aliases={5 + i: i for i in range(len(extra))},
    )(place, *chunk, *extra)


def last_sum_kernel(held_a_ref, got_a_ref, held_b_ref, got_b_ref, *rest):
    outs = rest[-3:]
    side = held_a_ref.shape[3]
    for which, out in enumerate(outs):
        out[0, :, :side] = held_a_ref[0, which].astype(f32) + got_a_ref[0, which].astype(f32)
        out[0, :, side:] = held_b_ref[0, which].astype(f32) + got_b_ref[0, which].astype(f32)


def last_sum(held_a, got_a, held_b, got_b, first, total, before):
    count, kinds, rows, cols = held_a.shape
    taken = pl.BlockSpec((1, kinds, rows, cols), lambda e: (e, 0, 0, 0))
    given = pl.BlockSpec((1, rows, 2 * cols), lambda e: (e + first, 0, 0))
    extra = list(before) if before else []
    return call(
        last_sum_kernel,
        (count,),
        0,
        [taken] * 4 + [pl.BlockSpec(memory_space=pl.ANY)] * len(extra),
        [given] * 3,
        [struct((total, rows, 2 * cols), f32)] * 3,
        us=0.5,
        aliases={4 + i: i for i in range(len(extra))},
    )(held_a, got_a, held_b, got_b, *extra)


def last_weights_kernel(held_a_ref, got_a_ref, held_b_ref, got_b_ref, query_ref, key_ref, value_ref, out_ref):
    left = jnp.transpose(held_a_ref[0, 0].astype(f32) + got_a_ref[0, 0].astype(f32))
    right = jnp.transpose(held_b_ref[0, 0].astype(f32) + got_b_ref[0, 0].astype(f32))
    cut = query_ref.shape[0]
    query_ref[...] = left[:cut]
    key_ref[...] = left[cut:]
    out_ref[...] = right[:cut]
    value_ref[...] = right[cut:]


def last_weights(parts, widths):
    rows = parts[0].shape[2]
    shapes = [(width, rows) for width in widths]
    return call(
        last_weights_kernel,
        (1,),
        0,
        [whole(part.shape) for part in parts],
        [whole(shape) for shape in shapes],
        [struct(shape, f32) for shape in shapes],
        us=0.5,
    )(*parts)


SWAP = [(0, 1), (1, 0)]


def after(value, *events):
    return lax.optimization_barrier((value,) + events)[0]


def gather_group(block):
    return lax.all_gather(block, ("row", "col"), axis=0, tiled=True)


def line_pieces(value):
    parts = [value]
    for distance in range(1, COLS):
        parts.insert(0, lax.ppermute(value, "col", [(i, (i + distance) % COLS) for i in range(COLS)]))
    return parts


def in_line_order(parts):
    parts = jnp.stack(parts + parts)
    return lax.dynamic_slice_in_dim(parts, COLS - 1 - lax.axis_index("col"), COLS, axis=0)


def flip(value, axis, bit, size):
    return lax.ppermute(value, axis, [(i, i ^ (1 << bit)) for i in range(size)])


def bits_of(size):
    return size.bit_length() - 1


def own_bit(axis, bit):
    return (lax.axis_index(axis) >> bit) & 1


def joined(mine, got, own):
    return jnp.where(own == 0, jnp.concatenate([mine, got]), jnp.concatenate([got, mine]))


def cube_step(value, axis, bit, size):
    return joined(value, flip(value, axis, bit, size), own_bit(axis, bit))


def lines_first(value):
    return jnp.transpose(value, (1, 0, 2, 3)).reshape(value.shape[1], value.shape[0] * value.shape[2], value.shape[3])


def cube_gather(value, axis, size):
    value = value[None]
    for bit in range(bits_of(size)):
        value = cube_step(value, axis, bit, size)
    return value


def sum_dp(value, sizes):
    for bit in range(bits_of(sizes["dp"])):
        value = value + flip(value, "dp", bit, sizes["dp"])
    return value


def reduce_over_dp(value, size):
    count = bits_of(size)
    value = value.reshape(value.shape[:1] + (2,) * count + value.shape[2:])
    current = value
    for bit in range(count - 1, -1, -1):
        own = own_bit("dp", bit)
        keep = lax.dynamic_index_in_dim(current, own, 1, keepdims=False)
        send = lax.dynamic_index_in_dim(current, 1 - own, 1, keepdims=False).astype(bf16)
        current = keep.astype(f32) + flip(send, "dp", bit, size).astype(f32)
    return current


def start_move(run, size):
    return flip(run[0], "dp", 0, size), flip(run[2], "dp", 1, size)


def second_move(sums, size):
    send_a, held_a, send_b, held_b = sums
    return held_a, flip(send_a, "dp", 1, size), held_b, flip(send_b, "dp", 0, size)


def layer(sizes):
    n_dp, n_row, n_col = sizes["dp"], sizes["row"], sizes["col"]
    members = n_row * n_col
    fast = n_dp == 4
    assert n_row == 2 and n_col == COLS and n_dp & (n_dp - 1) == 0

    def local(
        tokens, cotangent, routes, lengths, gain_attn, w_query, w_key, w_value, w_out,
        gain_moe, w_router, w_gate, w_up, w_down,
    ):
        rows, width = tokens.shape
        group = rows * members
        local_experts = w_gate.shape[0]
        row, col, dp = lax.axis_index("row"), lax.axis_index("col"), lax.axis_index("dp")
        place = jnp.stack([row, col, row * n_col + col, dp & 1, (dp >> 1) & 1]).astype(jnp.int32)
        gain_one = gain_attn.astype(f32)[None]
        gain_two = gain_moe.astype(f32)[None]

        tok_all = gather_group(tokens)
        w_in = jnp.concatenate([w_query.T, w_key.T, w_value.T], axis=0)
        out_share, in_share = rows // n_dp, w_in.shape[0] // n_dp
        shares = jnp.concatenate(
            [
                lax.dynamic_slice(w_out.T, (dp * out_share, 0), (out_share, width)),
                lax.dynamic_slice(w_in, (dp * in_share, 0), (in_share, width)),
                jnp.pad(routes.T.astype(bf16).reshape(1, TOP * rows), ((0, 7), (0, width - TOP * rows))),
            ],
            axis=0,
        )
        w_stack = jnp.concatenate([w_query.T, w_key.T, w_value.T, w_value.T], axis=0)
        w_natural = jnp.concatenate([w_query, w_key, w_value, w_value], axis=1)

        ends = jnp.cumsum(lengths[0])
        starts = ends - lengths[0]
        position = jnp.arange(group, dtype=jnp.int32)
        segment = jnp.sum((position[:, None] >= ends[None, :]).astype(jnp.int32), axis=1)
        member = segment[:, None] == jnp.arange(starts.shape[0], dtype=jnp.int32)[None, :]
        start = jnp.sum(jnp.where(member, starts[None, :], 0), axis=1).astype(jnp.int32)
        frequency = rope_base ** (-2.0 * jnp.arange(HEAD_DIM // 2, dtype=f32) / HEAD_DIM)
        angle = (position - start).astype(f32)[:, None] * frequency[None, :]
        cosine = jnp.tile(jnp.cos(angle), (1, 4))
        sine = jnp.tile(jnp.sin(angle), (1, 4))

        w_router_rows = w_router.T.reshape(members, local_experts, width)
        w_router_rows = jnp.pad(w_router_rows, ((0, 0), (0, 8 - local_experts), (0, 0)))
        w_router_rows = w_router_rows.reshape(members * 8, width)
        start_row = jnp.broadcast_to(start[None, :], (8, group))
        start = start[:, None]
        gain_column = gain_attn.astype(f32)[:, None]
        ready = (place, gain_one, gain_two, w_stack, w_natural, cosine, sine, w_router_rows, start, start_row, gain_column)
        shares, place, gain_one, gain_two, w_stack, w_natural, cosine, sine, w_router_rows, start, start_row, gain_column = (
            lax.optimization_barrier((shares,) + ready)
        )
        shares = line_pieces(after(shares, tok_all, cosine))

        query, key, value, normed_one = project(tok_all, gain_one, w_stack, cosine, sine)
        packed, attended, totals = attend(query, key, value, start)
        att_flat = gather_group(packed)
        att_all = att_flat.reshape((n_row, n_col) + packed.shape)
        shares = in_line_order(after(shares, packed))
        route_rows = shares[:, out_share + in_share]
        w_out_mine, in_part = shares[None, :, :out_share], shares[None, :, out_share : out_share + in_share]
        for bit in range(bits_of(n_dp)):
            w_out_mine = cube_step(w_out_mine, "dp", bit, n_dp)
        in_part = cube_step(in_part, "dp", 0, n_dp)
        w_out_mine = lines_first(w_out_mine)
        w_out_other = lax.ppermute(after(w_out_mine, in_part), "row", SWAP)
        route_rows = cube_gather(route_rows, "row", n_row)[:, :, : TOP * rows].reshape(members, TOP, rows)
        cot_all = gather_group(after(cotangent, w_out_other))
        x, slot_gate, rank, gate, normed_two, middle, gates = middle_and_dispatch(
            place, att_all, w_out_mine, w_out_other, tok_all, route_rows, gain_two, w_router_rows, local_experts
        )
        slots = members * CAPACITY
        x = x.reshape(local_experts, slots, width)
        slot_gate = slot_gate.reshape(local_experts, slots, LANES)
        rank, gate = rank.reshape(members, 8, rows), gate.reshape(members, 8, rows)
        forth, active, factor, silu = run_experts(x, slot_gate, w_gate, w_up, w_down)
        for bit in range(1, bits_of(n_dp) - 1):
            in_part = cube_step(in_part, "dp", bit, n_dp)
        last_bit = bits_of(n_dp) - 1
        in_got = after(flip(in_part, "dp", last_bit, n_dp), forth)
        forth_other = combine(place, after(rank, in_got), [forth])
        arrived = lax.ppermute(forth_other, "row", SWAP)
        g = grad_dispatch(after(rank, forth_other), gate, cot_all, local_experts)
        g = g.reshape(local_experts, slots, width)
        cuts = [0, 1, 3, local_experts]

        def backward(which, x):
            first, last = cuts[which], cuts[which + 1]
            return run_experts_back(place, x, g, active, factor, silu, w_gate, w_up, w_down, first, last - first, fast)

        forth_mine = combine(place, rank, [forth], arrived=after(arrived, g))
        forth_sums = lax.all_to_all(forth_mine, "col", 0, 0, tiled=True)
        runs = [backward(0, after(x, forth_mine))]
        runs.append(backward(1, after(x, runs[0][1])))
        runs.append(backward(2, after(x, runs[1][1])))
        moved = [start_move(run[2:], n_dp) for run in runs] if fast else []
        back_parts, dot_parts = [run[0] for run in runs], [run[1] for run in runs]
        back_other = combine(place, after(rank, *moved[0]) if fast else rank, back_parts, dot_parts)
        arrived = lax.ppermute(back_other, "row", SWAP)
        back_mine = combine(place, rank, back_parts, dot_parts, arrived)
        back_mine = after(back_mine, forth_sums)
        back_sums = lax.all_to_all(back_mine, "col", 0, 0, tiled=True)

        if fast:
            w_in_parts = [in_part, in_got]
        else:
            own = own_bit("dp", last_bit)
            w_in_rows = lines_first(joined(in_part, in_got, own))[None]
            half = w_in_rows.shape[2] // 2
            upper, lower = w_in_rows[:, :, :half], w_in_rows[:, :, half:]
            w_in_parts = [jnp.where(place[4] == 0, upper, lower), jnp.where(place[4] == 0, lower, upper)]
        if fast:

            def chunk_of(which, *events):
                keep_a, keep_b = after((runs[which][3], runs[which][5]), *events)
                return keep_a, moved[which][0], keep_b, moved[which][1]

            sums = first_sum(place, chunk_of(0, back_mine), cuts[0], cuts[2])
            gate_middle = (sums[1],) + moved[1]
        else:
            gate_middle = ()
        w_in_parts += [lax.ppermute(after(part, back_mine), "row", SWAP) for part in w_in_parts]

        mixed = (middle + jnp.sum(after(forth_sums, back_mine).astype(f32), axis=0)).astype(bf16)

        middle_grad, branch_grad, attended_grad = middle_back(
            place, back_sums, gates, middle, cotangent, after(gain_two, mixed, *w_in_parts[2:], *gate_middle),
            w_router_rows, w_out_mine, w_out_other,
        )
        if fast:
            sums = first_sum(place, chunk_of(1, branch_grad), cuts[1], cuts[2], sums)
            started = [second_move(sums, n_dp)]
        attended_grad = lax.all_to_all(attended_grad, ("row", "col"), 0, 0, tiled=True)
        if fast:
            attended_grad = after(attended_grad, sums[1])
        branch_all = gather_group(branch_grad)

        attended_grad = attended_grad.reshape(group, 2 * LANES)
        projected_grad, own_grads = attend_back(
            query, key, value, attended_grad, totals, start_row, cosine, sine, normed_one, w_natural, gain_column
        )
        projected_all = lax.all_to_all(projected_grad, ("row", "col"), 0, 0, tiled=True)
        if fast:
            started.append(second_move(first_sum(place, chunk_of(2, own_grads)), n_dp))
            normed_two = after(normed_two, started[1][0])
        arriving = (started[1][1], started[1][3]) if fast else ()
        *w_parts, small = out_weights(
            place, branch_all, attended, normed_two.reshape(group, width), own_grads,
            members * 8, local_experts, fast,
        )
        expert_grads = None
        if fast:
            w_moved = start_move(w_parts, n_dp)
            w_first = first_sum(place, (w_parts[1], w_moved[0], w_parts[3], w_moved[1]))
            w_sums = second_move(w_first, n_dp)
            held_a, got_a, held_b, got_b = started[0]
            held_a, held_b = after((held_a, held_b), w_first[1])
            expert_grads = last_sum(held_a, got_a, held_b, got_b, 0, local_experts, None)
        else:
            cut = w_parts[0].reshape(1, n_dp, width // n_dp, w_parts[0].shape[1])
            w_sum = reduce_over_dp(cut, n_dp)[0]


        used = small.reshape(members, 8, width)[:, :local_experts].reshape(members * local_experts, width)
        both = sum_dp(jnp.concatenate([used, small[7:8]], axis=0), sizes)
        w_router_grad = both[: members * local_experts].T
        gain_moe_grad = both[members * local_experts]

        tokens_grad, share = input_grad(
            place, projected_all, w_in_parts, tokens, middle_grad, after(gain_one, w_parts[0], *arriving)
        )
        gain_attn_grad = sum_dp((share[0:4] + share[4:8]).reshape(8, width // 8), sizes).reshape(width)

        local_q, local_k = w_query.shape[1], w_key.shape[1]
        if fast:
            expert_grads = last_sum(*started[1], cuts[2], local_experts, expert_grads)
            w_query_grad, w_key_grad, w_value_grad, w_out_grad = [
                item.T for item in last_weights(w_sums, (local_q, local_k, local_k, local_q))
            ]
        else:
            expert_grads = []
            for which in range(3):
                parts = [run[2 + which] for run in runs]
                parts = [part.reshape(part.shape[0], n_dp, width // n_dp, part.shape[2]) for part in parts]
                expert_grads.append(jnp.concatenate([reduce_over_dp(part, n_dp) for part in parts], axis=0))
            cut = local_q + local_k
            w_query_grad, w_key_grad = w_sum[:, :local_q], w_sum[:, local_q:cut]
            w_out_grad, w_value_grad = w_sum[:, cut : cut + local_q], w_sum[:, cut + local_q :]
        w_gate_grad, w_up_grad, w_down_grad = expert_grads
        return (
            mixed, tokens_grad, gain_attn_grad, w_query_grad, w_key_grad, w_value_grad, w_out_grad,
            gain_moe_grad, w_router_grad, w_gate_grad, w_up_grad, w_down_grad,
        )

    return local


def solution(mesh):
    return jax.shard_map(
        layer(dict(mesh.shape)),
        mesh=mesh,
        in_specs=(
            P(("dp", "row", "col"), None),
            P(("dp", "row", "col"), None),
            P(("dp", "row", "col"), None),
            P("dp", None),
            P(),
            P(None, ("row", "col")),
            P(None, ("row", "col")),
            P(None, ("row", "col")),
            P(None, ("row", "col")),
            P(),
            P(),
            P(("row", "col"), None, None),
            P(("row", "col"), None, None),
            P(("row", "col"), None, None),
        ),
        out_specs=(
            P(("dp", "row", "col"), None),
            P(("dp", "row", "col"), None),
            P(),
            P("dp", ("row", "col")),
            P("dp", ("row", "col")),
            P("dp", ("row", "col")),
            P("dp", ("row", "col")),
            P(),
            P(),
            P(("row", "col"), "dp", None),
            P(("row", "col"), "dp", None),
            P(("row", "col"), "dp", None),
        ),
        check_vma=False,
    )
```

```python
import math

import jax
import jax.numpy as jnp
import numpy as np
from jax import lax
from jax.experimental import pallas as pl
from jax.experimental.pallas import tpu as pltpu
from jax.sharding import PartitionSpec as P

HEAD_DIM = 64
EXPERTS = 40
TOP = 8
CAPACITY = 64
COLS = 4
LANES = 128
QUERY_BLOCK = 256
DOT_ROWS = 16

epsilon = 1e-06
rope_base = 10000.0
masked_score = -1e30
f32 = jnp.float32
bf16 = jnp.bfloat16
VMEM_LIMIT = 56 * 1024 * 1024

NT = (((1,), (1,)), ((), ()))
TN = (((0,), (0,)), ((), ()))


def dot(a, b):
    return jnp.dot(a, b, preferred_element_type=f32)


def dot_nt(a, b):
    return lax.dot_general(a, b, NT, preferred_element_type=f32)


def dot_tn(a, b):
    return lax.dot_general(a, b, TN, preferred_element_type=f32)


def lane_of(shape):
    return lax.broadcasted_iota(jnp.int32, shape, len(shape) - 1)


def call(
    kernel, grid, prefetch, in_specs, out_specs, out_shape, scratch=(), us=1.0, aliases=None
):
    return pl.pallas_call(
        kernel,
        grid_spec=pltpu.PrefetchScalarGridSpec(
            num_scalar_prefetch=prefetch,
            grid=grid,
            in_specs=in_specs,
            out_specs=out_specs,
            scratch_shapes=list(scratch),
        ),
        out_shape=out_shape,
        input_output_aliases=aliases or {},
        compiler_params=pltpu.CompilerParams(
            vmem_limit_bytes=VMEM_LIMIT, dimension_semantics=("arbitrary",) * len(grid)
        ),
        cost_estimate=pl.CostEstimate(
            flops=int(us * 1.1e9), bytes_accessed=int(us * 3.6e6), transcendentals=0
        ),
    )


def whole(shape):
    zeros = (0,) * len(shape)
    return pl.BlockSpec(shape, lambda *_: zeros)


def struct(shape, dtype):
    return jax.ShapeDtypeStruct(shape, dtype)


def turn_within_heads(values, sign):
    lane = lane_of(values.shape) % HEAD_DIM
    ahead = pltpu.roll(values, LANES - HEAD_DIM // 2, 1)
    behind = pltpu.roll(values, HEAD_DIM // 2, 1)
    return jnp.where(lane < HEAD_DIM // 2, -sign * ahead, sign * behind)


def project_kernel(
    tok_ref, gain_ref, w_ref, cos_ref, sin_ref, query_ref, key_ref, value_ref, normed_ref
):
    resid = tok_ref[...].astype(f32)
    inverse = lax.rsqrt(jnp.mean(resid * resid, axis=1, keepdims=True) + epsilon)
    normed = (resid * inverse * gain_ref[...]).astype(bf16)
    normed_ref[...] = normed
    raw = dot_nt(normed, w_ref[...])
    cosine, sine = cos_ref[...], sin_ref[...]

    def rot(values):
        return (values * cosine + turn_within_heads(values, 1.0) * sine).astype(bf16).astype(f32)

    first = rot(raw[:, :LANES])
    second = rot(raw[:, LANES : 2 * LANES])
    low = lane_of(first.shape) < HEAD_DIM
    scale = 1.0 / math.sqrt(HEAD_DIM)
    query_ref[0] = jnp.where(low, first * scale, 0.0).astype(bf16)
    query_ref[1] = jnp.where(low, 0.0, first * scale).astype(bf16)
    query_ref[2] = jnp.where(low, second * scale, 0.0).astype(bf16)
    key_ref[...] = jnp.where(low, pltpu.roll(second, HEAD_DIM, 1), second).astype(bf16)
    value_ref[...] = raw[:, 2 * LANES :].astype(bf16)


def project(tokens, gain, w_stack, cosine, sine):
    total, width = tokens.shape
    rows = 512
    lanes = pl.BlockSpec((rows, LANES), lambda j: (j, 0))
    wide = pl.BlockSpec((rows, width), lambda j: (j, 0))
    return call(
        project_kernel,
        (total // rows,),
        0,
        [wide, whole((1, width)), whole(w_stack.shape), lanes, lanes],
        [pl.BlockSpec((3, rows, LANES), lambda j: (0, j, 0)), lanes, lanes, wide],
        [
            struct((3, total, LANES), bf16),
            struct((total, LANES), bf16),
            struct((total, LANES), bf16),
            struct((total, width), bf16),
        ],
        us=0.5,
    )(tokens, gain, w_stack, cosine, sine)


def attend_kernel(query_ref, key_ref, value_ref, start_ref, packed_ref, plain_ref, total_ref, out_ref):
    blocks = query_ref.shape[1] // QUERY_BLOCK
    block = pl.program_id(0)
    for index in range(blocks):

        @pl.when(block == index)
        def _(index=index):
            rows = pl.ds(index * QUERY_BLOCK, QUERY_BLOCK)
            span = (index + 1) * QUERY_BLOCK
            row = index * QUERY_BLOCK + lax.broadcasted_iota(jnp.int32, (QUERY_BLOCK, span), 0)
            column = lane_of((QUERY_BLOCK, span))
            allowed = (column <= row) & (column >= start_ref[rows, :])

            def head(number, carry):
                scores = dot_nt(query_ref[number, rows, :], key_ref[0:span, :])
                scores = jnp.where(allowed, scores, masked_score)
                peak = jnp.max(scores, axis=1, keepdims=True)
                weights = jnp.exp(scores - peak)
                summed = jnp.sum(weights, axis=1, keepdims=True)
                probs = (weights * (1.0 / summed)).astype(bf16)
                out_ref[number] = dot(probs, value_ref[0:span, :])
                total = jnp.broadcast_to(peak + jnp.log(summed), (QUERY_BLOCK, LANES))
                total_ref[number, :, rows] = jnp.transpose(total)[0:8, :]
                return carry

            lax.fori_loop(0, 3, head, 0)
            low = lane_of((QUERY_BLOCK, LANES)) < HEAD_DIM
            one, two, three = out_ref[0], out_ref[1], out_ref[2]
            pair = jnp.where(low, one, two).astype(bf16)
            plain_ref[rows, 0:LANES] = pair
            plain_ref[rows, LANES : 2 * LANES] = jnp.where(low, three, 0.0).astype(bf16)
            if index < blocks // 2:
                packed_ref[rows, 0:LANES] = pair
                packed_ref[rows, LANES : 2 * LANES] = three.astype(bf16)
            else:
                back = pl.ds((index - blocks // 2) * QUERY_BLOCK, QUERY_BLOCK)
                before = packed_ref[back, LANES : 2 * LANES].astype(f32)
                packed_ref[back, LANES : 2 * LANES] = jnp.where(low, before, one).astype(bf16)
                packed_ref[back, 2 * LANES : 3 * LANES] = jnp.where(low, two, three).astype(bf16)


def attend(query, key, value, start):
    total = key.shape[0]
    return call(
        attend_kernel,
        (total // QUERY_BLOCK,),
        0,
        [whole(query.shape), whole(key.shape), whole(value.shape), whole(start.shape)],
        [whole((total // 2, 3 * LANES)), whole((total, 2 * LANES)), whole((3, 8, total))],
        [
            struct((total // 2, 3 * LANES), bf16),
            struct((total, 2 * LANES), bf16),
            struct((3, 8, total), f32),
        ],
        scratch=[pltpu.VMEM((3, QUERY_BLOCK, LANES), f32)],
        us=0.5,
    )(query, key, value, start)


def attend_back_kernel(
    query_ref, key_ref, value_ref, grad_ref, total_ref, start_ref, cos_ref, sin_ref, normed_ref, w_ref, gain_ref,
    blocks_ref, own_ref, out_ref, query_grad_ref, key_grad_ref, value_grad_ref, own_sum_ref
):
    blocks = query_ref.shape[1] // QUERY_BLOCK
    block = pl.program_id(0)
    scale = 1.0 / math.sqrt(HEAD_DIM)

    @pl.when(block == 0)
    def _():
        key_grad_ref[...] = jnp.zeros_like(key_grad_ref)
        value_grad_ref[...] = jnp.zeros_like(value_grad_ref)

    def back(values, cosine, sine):
        return values * cosine + turn_within_heads(values * sine, -1.0)

    for index in range(blocks):

        @pl.when(block == index)
        def _(index=index):
            rows = pl.ds(index * QUERY_BLOCK, QUERY_BLOCK)
            span = (index + 1) * QUERY_BLOCK
            row = index * QUERY_BLOCK + lane_of((span, QUERY_BLOCK))
            column = lax.broadcasted_iota(jnp.int32, (span, QUERY_BLOCK), 0)
            allowed = (column <= row) & (column >= start_ref[0:1, rows])
            low = lane_of((QUERY_BLOCK, LANES)) < HEAD_DIM

            def head(number, carry):
                query = query_ref[number, rows, :]
                tile = pl.multiple_of((number // 2) * LANES, LANES)
                upstream = grad_ref[rows, pl.ds(tile, LANES)].astype(f32)
                keep = low == (number != 1)
                upstream = jnp.where(keep, upstream, 0.0).astype(bf16)
                scores = dot_nt(key_ref[0:span, :], query)
                probs = jnp.exp(scores - total_ref[number, 0:1, rows])
                probs = jnp.where(allowed, probs, 0.0)
                prob_grad = dot_nt(value_ref[0:span, :], upstream)
                row_dot = jnp.sum(probs * prob_grad, axis=0, keepdims=True)
                score_grad = (probs * (prob_grad - row_dot)).astype(bf16)
                key_grad_ref[0:span, :] += dot(score_grad, query)
                value_grad_ref[0:span, :] += dot(probs.astype(bf16), upstream)
                query_grad_ref[number] = dot_tn(score_grad, key_ref[0:span, :]) * scale
                return carry

            lax.fori_loop(0, 3, head, 0)
            cosine, sine = cos_ref[rows, :], sin_ref[rows, :]
            pair = jnp.where(low, query_grad_ref[0], query_grad_ref[1])
            out_ref[rows, 0:LANES] = back(pair, cosine, sine).astype(bf16)
            out_ref[rows, LANES : 2 * LANES] = back(query_grad_ref[2], cosine, sine).astype(bf16)

    @pl.when(block == blocks - 1)
    def _():
        low = lane_of(key_grad_ref.shape) < HEAD_DIM
        key_grad = key_grad_ref[...]
        key_grad = key_grad + pltpu.roll(key_grad, HEAD_DIM, 1)
        key_grad = back(key_grad, cos_ref[...], sin_ref[...])
        before = out_ref[:, LANES : 2 * LANES].astype(f32)
        out_ref[:, LANES : 2 * LANES] = jnp.where(low, before, key_grad).astype(bf16)
        value_grad = value_grad_ref[...]
        value_grad = value_grad + pltpu.roll(value_grad, HEAD_DIM, 1)
        out_ref[:, 2 * LANES : 3 * LANES] = jnp.where(low, 0.0, value_grad).astype(bf16)
        chunk = 512
        own_sum_ref[...] = jnp.zeros_like(own_sum_ref)

        def add(index, carry):
            part = pl.ds(pl.multiple_of(index * chunk, chunk), chunk)
            own_sum_ref[...] += dot_tn(normed_ref[part, :], out_ref[part, :])
            return carry

        lax.fori_loop(0, out_ref.shape[0] // chunk, add, 0)
        own = own_sum_ref[...]
        own_ref[...] = own.astype(bf16)
        share = jnp.sum(own * w_ref[...].astype(f32), axis=1, keepdims=True) / gain_ref[...]
        share = jnp.transpose(jnp.broadcast_to(share, (share.shape[0], LANES)))[0:8, :]
        width = blocks_ref.shape[2]
        row = lax.broadcasted_iota(jnp.int32, (8, width), 0)
        terms = jnp.zeros((8, width), f32)
        for index in range(share.shape[1] // width):
            piece = share[:, index * width : (index + 1) * width]
            upper = piece.astype(bf16).astype(f32)
            terms = jnp.where(row == index, upper, jnp.where(row == index + 4, piece - upper, terms))
        terms = jnp.concatenate([terms, jnp.zeros((8, width), f32)], axis=0).astype(bf16)
        rows = blocks_ref.shape[1] - DOT_ROWS
        for index in range(blocks_ref.shape[0]):
            blocks_ref[index, 0:rows, :] = out_ref[index * rows : (index + 1) * rows, :]
            blocks_ref[index, rows:, :] = terms


def attend_back(query, key, value, grad, totals, start, cosine, sine, normed, w_natural, gain):
    total = key.shape[0]
    members = 2 * COLS
    rows = total // members + DOT_ROWS
    args = (query, key, value, grad, totals, start, cosine, sine, normed, w_natural, gain)
    return call(
        attend_back_kernel,
        (total // QUERY_BLOCK,),
        0,
        [whole(item.shape) for item in args],
        [whole((members, rows, 3 * LANES)), whole(w_natural.shape)],
        [struct((members, rows, 3 * LANES), bf16), struct(w_natural.shape, bf16)],
        scratch=[
            pltpu.VMEM((total, 3 * LANES), bf16),
            pltpu.VMEM((3, QUERY_BLOCK, LANES), f32),
            pltpu.VMEM((total, LANES), f32),
            pltpu.VMEM((total, LANES), f32),
            pltpu.VMEM(w_natural.shape, f32),
        ],
        us=0.5,
    )(*args)


def branch_operand(refs):
    rows = refs.shape[2]
    low = lane_of((rows, LANES)) < HEAD_DIM
    pairs, thirds = [], []
    for member in range(refs.shape[1]):
        one = refs[0, member, :, 0:LANES]
        mid = refs[0, member, :, LANES : 2 * LANES].astype(f32)
        end = refs[0, member, :, 2 * LANES : 3 * LANES].astype(f32)
        mid_turned = pltpu.roll(mid, HEAD_DIM, 1)
        end_turned = pltpu.roll(end, HEAD_DIM, 1)
        late = jnp.where(low, mid_turned, end_turned).astype(bf16)
        pairs.append(jnp.concatenate([one, late], axis=0))
        thirds.append((mid, end_turned))
    for member in range(0, refs.shape[1], 2):
        tops = []
        for which in range(2):
            left, right = thirds[member][which], thirds[member + 1][which]
            tops.append(jnp.where(low, left, pltpu.roll(right, HEAD_DIM, 1)).astype(bf16))
        pairs.append(jnp.concatenate(tops, axis=0))
    return jnp.concatenate(pairs, axis=1)


def branch_weights(ref):
    right = [ref[source, 0:LANES] for source in range(ref.shape[0])]
    return jnp.concatenate(right + [ref[source, LANES:] for source in range(ref.shape[0])], axis=0)


def hits_of(rank, local_experts):
    place = lax.broadcasted_iota(jnp.int32, (CAPACITY, rank.shape[1]), 0).astype(f32)
    return [place == rank[j : j + 1, :] for j in range(local_experts)]


def chosen_of(hits):
    return jnp.concatenate([jnp.where(hit, 1.0, 0.0).astype(bf16) for hit in hits], axis=0)


def middle_kernel(
    place_ref, att_mine_ref, att_other_ref, w_mine_ref, w_other_ref, tok_a_ref, tok_b_ref, routes_a_ref, routes_b_ref,
    gain_ref, w_router_ref, after_ref,
    x_ref, slot_gate_ref, rank_ref, gate_ref, normed_ref, middle_ref, gates_own_ref, gates_ref, ranks_ref
):
    step = pl.program_id(0)
    member = place_ref[2]
    cols = pl.num_programs(0)
    rows = tok_a_ref.shape[0]
    local_experts = x_ref.shape[0]
    branch = dot(branch_operand(att_mine_ref), branch_weights(w_mine_ref))
    branch = branch + dot(branch_operand(att_other_ref), branch_weights(w_other_ref))
    for half in range(2):
        tok_ref, routes_ref = ((tok_a_ref, routes_a_ref), (tok_b_ref, routes_b_ref))[half]
        middle = tok_ref[...].astype(f32) + branch[half * rows : (half + 1) * rows]
        inverse = lax.rsqrt(jnp.mean(middle * middle, axis=1, keepdims=True) + epsilon)
        normed = (middle * inverse * gain_ref[...]).astype(bf16)
        normed_ref[half, 0] = normed
        logits = dot_nt(w_router_ref[...], normed)
        padded = logits.shape[0]
        slot = lax.broadcasted_iota(jnp.int32, (padded, rows), 0)
        expert = (slot // 8) * local_experts + slot % 8
        expert = jnp.where(slot % 8 < local_experts, expert, -1).astype(f32)
        routes = routes_ref[0].astype(f32)
        named = expert == routes[0:1, 0:rows]
        for k in range(1, TOP):
            named = named | (expert == routes[k : k + 1, 0:rows])
        peak = jnp.max(jnp.where(named, logits, masked_score), axis=0, keepdims=True)
        weights = jnp.where(named, jnp.exp(logits - peak), 0.0)
        gates = weights / jnp.sum(weights, axis=0, keepdims=True)
        gates_ref[...] = gates
        ranks_ref[...] = jnp.where(named, dot(named.astype(f32).astype(bf16), after_ref[...]), -1.0)
        here = pl.ds(pl.multiple_of(member * 8, 8), 8)
        gate, rank = gates_ref[here, :], ranks_ref[here, :]
        rank_ref[half, 0] = rank
        gate_ref[half, 0] = gate
        hits = hits_of(rank, local_experts)
        slot_gate = jnp.concatenate(
            [jnp.sum(jnp.where(hit, gate[j : j + 1, :], 0.0), axis=1, keepdims=True) for j, hit in enumerate(hits)],
            axis=0,
        )
        chosen = chosen_of(hits)
        picked = dot(chosen, normed).astype(bf16)
        spread = jnp.broadcast_to(slot_gate, (slot_gate.shape[0], LANES))
        for j in range(local_experts):
            part = slice(j * CAPACITY, (j + 1) * CAPACITY)
            x_ref[j, half, 0] = picked[part]
            slot_gate_ref[j, half, 0] = spread[part]

        @pl.when(member == half * cols + step)
        def _(middle=middle, gates=gates):
            middle_ref[...] = middle
            gates_own_ref[...] = gates


def middle_and_dispatch(place, att, w_mine, w_other, tokens, routes, gain, w_router, local_experts):
    width = tokens.shape[1]
    half = COLS
    rows = tokens.shape[0] // (2 * half)
    padded = w_router.shape[0]
    after = jnp.asarray(np.triu(np.ones((rows, rows), np.float32), 1), bf16)
    slot_shape = (local_experts, 2, half, CAPACITY)
    early = pl.BlockSpec((rows, width), lambda i, p: (i, 0))
    late = pl.BlockSpec((rows, width), lambda i, p: (i + half, 0))
    routes_shape = (1,) + routes.shape[1:]
    return call(
        middle_kernel,
        (half,),
        1,
        [
            pl.BlockSpec((1, half, rows, 3 * LANES), lambda i, p: (p[0], 0, i, 0)),
            pl.BlockSpec((1, half, rows, 3 * LANES), lambda i, p: (1 - p[0], 0, i, 0)),
            whole(w_mine.shape),
            whole(w_other.shape),
            early,
            late,
            pl.BlockSpec(routes_shape, lambda i, p: (i, 0, 0)),
            pl.BlockSpec(routes_shape, lambda i, p: (i + half, 0, 0)),
            whole((1, width)),
            whole(w_router.shape),
            whole((rows, rows)),
        ],
        [
            pl.BlockSpec((local_experts, 2, 1, CAPACITY, width), lambda i, p: (0, 0, i, 0, 0)),
            pl.BlockSpec((local_experts, 2, 1, CAPACITY, LANES), lambda i, p: (0, 0, i, 0, 0)),
            pl.BlockSpec((2, 1, 8, rows), lambda i, p: (0, i, 0, 0)),
            pl.BlockSpec((2, 1, 8, rows), lambda i, p: (0, i, 0, 0)),
            pl.BlockSpec((2, 1, rows, width), lambda i, p: (0, i, 0, 0)),
            whole((rows, width)),
            whole((padded, rows)),
        ],
        [
            struct(slot_shape + (width,), bf16),
            struct(slot_shape + (LANES,), f32),
            struct((2, half, 8, rows), f32),
            struct((2, half, 8, rows), f32),
            struct((2, half, rows, width), bf16),
            struct((rows, width), f32),
            struct((padded, rows), f32),
        ],
        scratch=[pltpu.VMEM((padded, rows), f32), pltpu.VMEM((padded, rows), f32)],
        us=0.5,
    )(place, att, att, w_mine, w_other, tokens, tokens, routes, routes, gain, w_router, after)


def grad_dispatch_kernel(rank_ref, gate_ref, cot_ref, g_ref):
    local_experts = g_ref.shape[0]
    rows = cot_ref.shape[0] // 2
    for half in range(2):
        hits = hits_of(rank_ref[half], local_experts)
        gate = gate_ref[half]
        slot_gate = jnp.concatenate(
            [jnp.sum(jnp.where(hit, gate[j : j + 1, :], 0.0), axis=1, keepdims=True) for j, hit in enumerate(hits)],
            axis=0,
        )
        grads = (dot(chosen_of(hits), cot_ref[half * rows : (half + 1) * rows, :]) * slot_gate).astype(bf16)
        for j in range(local_experts):
            g_ref[j, half] = grads[j * CAPACITY : (j + 1) * CAPACITY]


def grad_dispatch(rank, gate, cotangents, local_experts):
    members, _, rows = rank.shape
    width = cotangents.shape[1]
    small = pl.BlockSpec((2, 8, rows), lambda j: (j, 0, 0))
    return call(
        grad_dispatch_kernel,
        (members // 2,),
        0,
        [small, small, pl.BlockSpec((2 * rows, width), lambda j: (j, 0))],
        pl.BlockSpec((local_experts, 2, CAPACITY, width), lambda j: (0, j, 0, 0)),
        struct((local_experts, members, CAPACITY, width), bf16),
        us=0.5,
    )(rank, gate, cotangents)


def expert_kernel(
    x_ref, gate_ref, w_gate_ref, w_up_ref, w_down_ref, forth_ref, active_ref, factor_ref, silu_ref
):
    gate_pre = dot(x_ref[0], w_gate_ref[0])
    up_pre = dot(x_ref[0], w_up_ref[0])
    sig = 1.0 / (1.0 + jnp.exp(-gate_pre))
    silu = gate_pre * sig
    silu_ref[0] = silu
    factor_ref[0] = up_pre * sig * (1.0 + gate_pre * (1.0 - sig))
    active_ref[0] = (silu * up_pre).astype(bf16)
    produced = dot_nt(active_ref[0], w_down_ref[0]).astype(bf16).astype(f32)
    forth_ref[0] = (produced * gate_ref[0, :, 0:1]).astype(bf16)


def run_experts(x, slot_gate, w_gate, w_up, w_down):
    count, slots, width = x.shape
    hidden = w_gate.shape[2]

    def per_expert(*shape):
        return pl.BlockSpec((1,) + shape, lambda e: (e, 0, 0))

    return call(
        expert_kernel,
        (count,),
        0,
        [per_expert(slots, width), per_expert(slots, LANES)] + [per_expert(width, hidden)] * 3,
        [per_expert(slots, width)] + [per_expert(slots, hidden)] * 3,
        [
            struct((count, slots, width), bf16),
            struct((count, slots, hidden), bf16),
            struct((count, slots, hidden), f32),
            struct((count, slots, hidden), f32),
        ],
        us=0.5,
    )(x, slot_gate, w_gate, w_up, w_down)


def expert_back_kernel(place_ref, *refs, fast):
    x_ref, g_ref, active_ref, factor_ref, silu_ref = refs[:5]
    w_gate_ref, w_up_ref, w_down_ref, back_ref, dots_ref = refs[5:10]
    grads, (gate_low_ref, up_low_ref) = refs[10:-2], refs[-2:]
    slots, width = g_ref.shape[1], g_ref.shape[2]
    chunk = 256
    active_grad = dot(g_ref[0], w_down_ref[0])
    gate_low_ref[...] = (active_grad * factor_ref[0]).astype(bf16)
    up_low_ref[...] = (active_grad * silu_ref[0]).astype(bf16)
    dots = jnp.sum(active_ref[0].astype(f32) * active_grad, axis=1, keepdims=True)
    dots_ref[0] = jnp.broadcast_to(dots, (slots, LANES))
    back_ref[0] = (dot_nt(gate_low_ref[...], w_gate_ref[0]) + dot_nt(up_low_ref[...], w_up_ref[0])).astype(bf16)

    def products(cols):
        x = x_ref[0, :, cols]
        yield 0, dot_tn(x, gate_low_ref[...]).astype(bf16)
        yield 1, dot_tn(x, up_low_ref[...]).astype(bf16)
        yield 2, dot_tn(g_ref[0, :, cols], active_ref[0]).astype(bf16)

    if fast:
        write_shards(place_ref, grads, products, width)
    else:

        def whole_columns(index, carry):
            cols = pl.ds(pl.multiple_of(index * chunk, chunk), chunk)
            for which, product in products(cols):
                grads[which][0, cols, :] = product
            return carry

        lax.fori_loop(0, width // chunk, whole_columns, 0)


def write_shards(place_ref, outs, products, width):
    send_a, keep_a, send_b, keep_b = outs
    x_bit, y_bit = place_ref[3], place_ref[4]
    shard = width // 4
    for dy in range(2):
        for dx in range(2):
            x, y = x_bit ^ dx, y_bit ^ dy
            cols = pl.ds(pl.multiple_of((y * 2 + x) * shard, shard), shard)
            for which, product in products(cols):
                side = product.shape[1] // 2
                (send_a if dx else keep_a)[0, which, y] = product[:, :side]
                (send_b if dy else keep_b)[0, which, x] = product[:, side:]


def run_experts_back(place, x, g, active, factor, silu, w_gate, w_up, w_down, first, count, fast):
    slots, width = g.shape[1], g.shape[2]
    hidden = w_gate.shape[2]

    def taken(*shape):
        return pl.BlockSpec((1,) + shape, lambda e, p: (e + first, 0, 0))

    def given(*shape):
        zeros = (0,) * len(shape)
        return pl.BlockSpec((1,) + shape, lambda e, p: (e,) + zeros)

    if fast:
        grad_shapes = [(3, 2, width // 4, hidden // 2)] * 4
    else:
        grad_shapes = [(width, hidden)] * 3
    return call(
        lambda *refs: expert_back_kernel(*refs, fast=fast),
        (count,),
        1,
        [taken(slots, width)] * 2 + [taken(slots, hidden)] * 3 + [taken(width, hidden)] * 3,
        [given(slots, width), given(slots, LANES)] + [given(*shape) for shape in grad_shapes],
        [struct((count, slots, width), bf16), struct((count, slots, LANES), f32)]
        + [struct((count,) + shape, bf16) for shape in grad_shapes],
        scratch=[pltpu.VMEM((slots, hidden), bf16)] * 2,
        us=0.5,
    )(place, x, g, active, factor, silu, w_gate, w_up, w_down)


DOT_LANES = 2 * LANES


def combine_kernel(place_ref, rank_ref, *refs, pieces, with_dots, mine):
    parts, rest = refs[:pieces], refs[pieces:]
    rows = rank_ref.shape[2]
    local_experts = sum(part.shape[0] for part in parts)
    hits = hits_of(rank_ref[0], local_experts)
    gathered = jnp.concatenate([part[j, 0] for part in parts for j in range(part.shape[0])], axis=0)
    summed = dot_tn(chosen_of(hits), gathered)
    out_ref = rest[-1]
    if mine:
        arrived_ref = rest[-2]
        summed = summed + arrived_ref[0, 0:rows, :].astype(f32)
    out_ref[0, 0:rows, :] = summed.astype(bf16)
    if with_dots:
        column = [part[j, 0][:, 0:1] for part in rest[:pieces] for j in range(part.shape[0])]
        scattered = [
            jnp.sum(jnp.where(hit, value, 0.0), axis=0, keepdims=True) for hit, value in zip(hits, column)
        ]
        scattered.append(jnp.zeros((DOT_ROWS - local_experts, rows), f32))
        scattered = jnp.concatenate(scattered, axis=0)
        upper = scattered.astype(bf16)
        out_ref[0, rows:, :] = jnp.zeros((DOT_ROWS, out_ref.shape[2]), bf16)
        out_ref[0, rows:, 0:rows] = upper
        out_ref[0, rows:, DOT_LANES : DOT_LANES + rows] = (scattered - upper.astype(f32)).astype(bf16)
        if mine:
            out_ref[0, rows:, 2 * DOT_LANES : 4 * DOT_LANES] = arrived_ref[0, rows:, 0 : 2 * DOT_LANES]


def combine(place, rank, parts, dots=None, arrived=None):
    mine = arrived is not None
    rows, width = rank.shape[2], parts[0].shape[-1]
    out_rows = rows + (DOT_ROWS if dots else 0)

    def member(step, p):
        return (p[0] if mine else 1 - p[0]) * COLS + step

    def slots_of(array):
        return pl.BlockSpec((array.shape[0], 1) + array.shape[2:], lambda j, p: (0, member(j, p), 0, 0))

    inputs = [
        part.reshape(part.shape[0], 2 * COLS, CAPACITY, part.shape[-1]) for part in list(parts) + list(dots or [])
    ]
    in_specs = [pl.BlockSpec((1, 8, rows), lambda j, p: (member(j, p), 0, 0))] + [slots_of(item) for item in inputs]
    by_chip = pl.BlockSpec((1, out_rows, width), lambda j, p: (j, 0, 0))
    if mine:
        inputs.append(arrived)
        in_specs.append(by_chip)
    return call(
        lambda *refs: combine_kernel(*refs, pieces=len(parts), with_dots=bool(dots), mine=mine),
        (COLS,),
        1,
        in_specs,
        by_chip,
        struct((COLS, out_rows, width), bf16),
        us=0.5,
    )(place, rank, *inputs)


def split_dot(dimension_numbers, values, exact):
    upper = values.astype(bf16)
    lower = (values - upper.astype(f32)).astype(bf16)
    return lax.dot_general(
        upper, exact, dimension_numbers, preferred_element_type=f32
    ) + lax.dot_general(lower, exact, dimension_numbers, preferred_element_type=f32)


EXTRA_SLOTS = 6


def middle_back_kernel(
    place_ref, sums_ref, gates_ref, middle_ref, cot_ref, gain_ref, w_router_ref, w_mine_ref, w_other_ref,
    grad_ref, branch_ref, attended_ref, extra_ref
):
    rows = middle_ref.shape[0]
    tail = sums_ref[:, rows : rows + 8, 0 : 4 * DOT_LANES].astype(f32)
    mine = tail[:, :, 0:rows] + tail[:, :, DOT_LANES : DOT_LANES + rows]
    other = tail[:, :, 2 * DOT_LANES : 2 * DOT_LANES + rows] + tail[:, :, 3 * DOT_LANES : 3 * DOT_LANES + rows]
    first_row = place_ref[0] == 0
    dots = jnp.concatenate([jnp.where(first_row, mine, other), jnp.where(first_row, other, mine)], axis=0)
    dots = dots.reshape(dots.shape[0] * 8, rows)
    gates = gates_ref[...]
    logit_grad = dots - gates * jnp.sum(dots, axis=0, keepdims=True)
    middle = middle_ref[...]
    inverse = lax.rsqrt(jnp.mean(middle * middle, axis=1, keepdims=True) + epsilon)
    unit = middle * inverse
    gain = gain_ref[...]
    grad = sums_ref[0, 0:rows].astype(f32)
    for index in range(1, sums_ref.shape[0]):
        grad = grad + sums_ref[index, 0:rows].astype(f32)
    grad = grad + split_dot(TN, logit_grad, w_router_ref[...])
    gain_grad = jnp.sum(grad * unit, axis=0, keepdims=True)
    scaled = grad * gain
    middle_grad = cot_ref[...].astype(f32) + inverse * (
        scaled - unit * jnp.mean(scaled * unit, axis=1, keepdims=True)
    )
    grad_ref[...] = middle_grad
    branch_grad = middle_grad.astype(bf16)
    branch_ref[0:rows, :] = branch_grad
    extra_ref[...] = jnp.zeros_like(extra_ref)
    for index in range(logit_grad.shape[0] // 8):
        first, lane = index // EXTRA_SLOTS * 8, index % EXTRA_SLOTS * DOT_LANES
        extra_ref[first : first + 8, lane : lane + rows] = logit_grad[index * 8 : index * 8 + 8]
    upper = gain_grad.astype(bf16).astype(f32)
    extra_ref[13:14, :] = upper
    extra_ref[14:15, :] = gain_grad - upper
    branch_ref[rows:, :] = extra_ref[...].astype(bf16)
    for which, ref in enumerate((w_mine_ref, w_other_ref)):
        line = place_ref[0] if which == 0 else 1 - place_ref[0]
        for col in range(ref.shape[0]):
            product = dot_nt(branch_grad, ref[col])
            member = line * COLS + col
            attended_ref[member, :, 0:LANES] = product[:, 0:LANES].astype(bf16)
            attended_ref[member, :, LANES : LANES + HEAD_DIM] = product[:, LANES:].astype(bf16)
            attended_ref[member, :, LANES + HEAD_DIM :] = jnp.zeros((product.shape[0], HEAD_DIM), bf16)


def middle_back(place, sums, gates, middle, cotangent, gain, w_router, w_mine, w_other):
    rows, width = middle.shape
    members = 2 * COLS
    args = (sums, gates, middle, cotangent, gain, w_router, w_mine, w_other)
    return call(
        middle_back_kernel,
        (1,),
        1,
        [whole(item.shape) for item in args],
        [whole((rows, width)), whole((rows + DOT_ROWS, width)), whole((members, rows, 2 * LANES))],
        [
            struct((rows, width), f32),
            struct((rows + DOT_ROWS, width), bf16),
            struct((members, rows, 2 * LANES), bf16),
        ],
        scratch=[pltpu.VMEM((DOT_ROWS, width), f32)],
        us=0.5,
    )(place, *args)


def input_grad_kernel(
    place_ref, grads_mine_ref, grads_other_ref, mine_a_ref, mine_b_ref, other_a_ref, other_b_ref,
    tok_ref, middle_grad_ref, gain_ref, out_ref, share_ref, sum_ref
):
    step = pl.program_id(0)
    first = place_ref[4] == 0

    def weights(a_ref, b_ref):
        a = jnp.concatenate([a_ref[index, 0] for index in range(a_ref.shape[0])], axis=0)
        b = jnp.concatenate([b_ref[index, 0] for index in range(b_ref.shape[0])], axis=0)
        upper, lower = jnp.where(first, a, b), jnp.where(first, b, a)
        return jnp.concatenate([upper, lower, lower[lower.shape[0] - HEAD_DIM :]], axis=0)

    rows = tok_ref.shape[0]
    part = dot(grads_mine_ref[0, 0:rows, :], weights(mine_a_ref, mine_b_ref))
    part = part + dot(grads_other_ref[0, 0:rows, :], weights(other_a_ref, other_b_ref))
    share = grads_mine_ref[0, rows:, :].astype(f32)[0:8] + grads_other_ref[0, rows:, :].astype(f32)[0:8]

    @pl.when(step == 0)
    def _():
        sum_ref[...] = part
        share_ref[...] = share

    @pl.when(step > 0)
    def _():
        sum_ref[...] += part
        share_ref[...] += share

    @pl.when(step == pl.num_programs(0) - 1)
    def _():
        resid = tok_ref[...].astype(f32)
        inverse = lax.rsqrt(jnp.mean(resid * resid, axis=1, keepdims=True) + epsilon)
        unit = resid * inverse
        scaled = sum_ref[...] * gain_ref[...]
        out_ref[...] = middle_grad_ref[...] + inverse * (
            scaled - unit * jnp.mean(scaled * unit, axis=1, keepdims=True)
        )


def input_grad(place, grads, weights, tokens, middle_grad, gain):
    rows, width = tokens.shape
    lanes = grads.shape[2]
    w_shape = (weights[0].shape[0], 1) + weights[0].shape[2:]
    return call(
        input_grad_kernel,
        (COLS,),
        1,
        [
            pl.BlockSpec((1, rows + DOT_ROWS, lanes), lambda c, p: (p[0] * COLS + c, 0, 0)),
            pl.BlockSpec((1, rows + DOT_ROWS, lanes), lambda c, p: ((1 - p[0]) * COLS + c, 0, 0)),
        ]
        + [pl.BlockSpec(w_shape, lambda c, p: (0, c, 0, 0))] * 4
        + [whole((rows, width)), whole((rows, width)), whole((1, width))],
        [whole((rows, width)), whole((8, lanes))],
        [struct((rows, width), f32), struct((8, lanes), f32)],
        scratch=[pltpu.VMEM((rows, width), f32)],
        us=0.5,
    )(place, grads, grads, *weights, tokens, middle_grad, gain)


def out_weights_kernel(place_ref, branch_ref, att_ref, normed_ref, own_ref, *refs, fast, local_experts):
    outs, small_ref, (sum_ref, gain_sum_ref) = refs[:-3], refs[-3], refs[-2:]
    step = pl.program_id(0)
    rows = att_ref.shape[0] // 2
    block = rows + DOT_ROWS

    @pl.when(step == 0)
    def _():
        sum_ref[...] = jnp.zeros_like(sum_ref)
        small_ref[...] = jnp.zeros_like(small_ref)
        gain_sum_ref[...] = jnp.zeros_like(gain_sum_ref)

    branch = jnp.concatenate([branch_ref[0:rows, :], branch_ref[block : block + rows, :]], axis=0)
    sum_ref[...] += dot_tn(branch, att_ref[...])
    for which in range(2):
        tail = branch_ref[which * block + rows : (which + 1) * block, :].astype(f32)
        slots = []
        for index in range(small_ref.shape[0] // 8):
            first, lane = index // EXTRA_SLOTS * 8, index % EXTRA_SLOTS * DOT_LANES
            slots.append(tail[first : first + 8, lane : lane + rows])
        logit_grad = jnp.concatenate(slots, axis=0)
        real = lax.broadcasted_iota(jnp.int32, logit_grad.shape, 0) % 8 < local_experts
        logit_grad = jnp.where(real, logit_grad, 0.0).astype(bf16)
        small_ref[...] += dot(logit_grad, normed_ref[which * rows : (which + 1) * rows, :])
        gain_sum_ref[...] += tail[8:16, :]

    @pl.when(step == pl.num_programs(0) - 1)
    def _():
        small_ref[7:8, :] = gain_sum_ref[5:6, :] + gain_sum_ref[6:7, :]

        def products(cols):
            own = own_ref[cols, 0 : 2 * LANES]
            out_one = sum_ref[cols, 0:LANES].astype(bf16)
            out_two = sum_ref[cols, LANES:]
            low = lane_of(out_two.shape) < HEAD_DIM
            tail = jnp.where(low, out_two, own_ref[cols, 2 * LANES :].astype(f32)).astype(bf16)
            yield 0, jnp.concatenate([own, out_one, tail], axis=1)

        if fast:
            write_shards(place_ref, outs, products, own_ref.shape[0])
        else:
            outs[0][...] = next(products(slice(0, own_ref.shape[0])))[1]


def out_weights(place, branch, attended, normed, own, padded, local_experts, fast):
    total, width = normed.shape
    rows = total // COLS
    blocks = branch.shape[0] // COLS
    if fast:
        shapes = [(1, 1, 2, width // 4, 2 * LANES)] * 4
    else:
        shapes = [(width, 4 * LANES)]
    return call(
        lambda *refs: out_weights_kernel(*refs, fast=fast, local_experts=local_experts),
        (COLS,),
        1,
        [
            pl.BlockSpec((blocks, width), lambda j, p: (j, 0)),
            pl.BlockSpec((rows, 2 * LANES), lambda j, p: (j, 0)),
            pl.BlockSpec((rows, width), lambda j, p: (j, 0)),
            whole(own.shape),
        ],
        [whole(shape) for shape in shapes] + [whole((padded, width))],
        [struct(shape, bf16) for shape in shapes] + [struct((padded, width), f32)],
        scratch=[pltpu.VMEM((width, 2 * LANES), f32), pltpu.VMEM((8, width), f32)],
        us=0.5,
    )(place, branch, attended, normed, own)


def first_sum_kernel(place_ref, keep_a_ref, got_a_ref, keep_b_ref, got_b_ref, *rest):
    send_a_ref, held_a_ref, send_b_ref, held_b_ref = rest[-4:]
    x_bit, y_bit = place_ref[3], place_ref[4]
    for bit, keep, got, send, held in (
        (y_bit, keep_a_ref, got_a_ref, send_a_ref, held_a_ref),
        (x_bit, keep_b_ref, got_b_ref, send_b_ref, held_b_ref),
    ):
        for kind in range(keep.shape[1]):
            held[0, kind] = (keep[0, kind, bit].astype(f32) + got[0, kind, bit].astype(f32)).astype(bf16)
            send[0, kind] = (keep[0, kind, 1 - bit].astype(f32) + got[0, kind, 1 - bit].astype(f32)).astype(bf16)


def first_sum(place, chunk, first=0, total=None, before=None):
    count, kinds, _, rows, cols = chunk[0].shape
    taken = pl.BlockSpec((1, kinds, 2, rows, cols), lambda e, p: (e, 0, 0, 0, 0))
    given = pl.BlockSpec((1, kinds, rows, cols), lambda e, p: (e + first, 0, 0, 0))
    extra = list(before) if before else []
    return call(
        first_sum_kernel,
        (count,),
        1,
        [taken] * 4 + [pl.BlockSpec(memory_space=pl.ANY)] * len(extra),
        [given] * 4,
        [struct((total or count, kinds, rows, cols), bf16)] * 4,
        us=0.5,
        aliases={5 + i: i for i in range(len(extra))},
    )(place, *chunk, *extra)


def last_sum_kernel(held_a_ref, got_a_ref, held_b_ref, got_b_ref, *rest):
    outs = rest[-3:]
    side = held_a_ref.shape[3]
    for which, out in enumerate(outs):
        out[0, :, :side] = held_a_ref[0, which].astype(f32) + got_a_ref[0, which].astype(f32)
        out[0, :, side:] = held_b_ref[0, which].astype(f32) + got_b_ref[0, which].astype(f32)


def last_sum(held_a, got_a, held_b, got_b, first, total, before):
    count, kinds, rows, cols = held_a.shape
    taken = pl.BlockSpec((1, kinds, rows, cols), lambda e: (e, 0, 0, 0))
    given = pl.BlockSpec((1, rows, 2 * cols), lambda e: (e + first, 0, 0))
    extra = list(before) if before else []
    return call(
        last_sum_kernel,
        (count,),
        0,
        [taken] * 4 + [pl.BlockSpec(memory_space=pl.ANY)] * len(extra),
        [given] * 3,
        [struct((total, rows, 2 * cols), f32)] * 3,
        us=0.5,
        aliases={4 + i: i for i in range(len(extra))},
    )(held_a, got_a, held_b, got_b, *extra)


def last_weights_kernel(held_a_ref, got_a_ref, held_b_ref, got_b_ref, query_ref, key_ref, value_ref, out_ref):
    left = jnp.transpose(held_a_ref[0, 0].astype(f32) + got_a_ref[0, 0].astype(f32))
    right = jnp.transpose(held_b_ref[0, 0].astype(f32) + got_b_ref[0, 0].astype(f32))
    cut = query_ref.shape[0]
    query_ref[...] = left[:cut]
    key_ref[...] = left[cut:]
    out_ref[...] = right[:cut]
    value_ref[...] = right[cut:]


def last_weights(parts, widths):
    rows = parts[0].shape[2]
    shapes = [(width, rows) for width in widths]
    return call(
        last_weights_kernel,
        (1,),
        0,
        [whole(part.shape) for part in parts],
        [whole(shape) for shape in shapes],
        [struct(shape, f32) for shape in shapes],
        us=0.5,
    )(*parts)


SWAP = [(0, 1), (1, 0)]


def after(value, *events):
    return lax.optimization_barrier((value,) + events)[0]


def gather_group(block):
    return lax.all_gather(block, ("row", "col"), axis=0, tiled=True)


def line_pieces(value):
    parts = [value]
    for distance in range(1, COLS):
        parts.insert(0, lax.ppermute(value, "col", [(i, (i + distance) % COLS) for i in range(COLS)]))
    return parts


def in_line_order(parts):
    parts = jnp.stack(parts + parts)
    return lax.dynamic_slice_in_dim(parts, COLS - 1 - lax.axis_index("col"), COLS, axis=0)


def flip(value, axis, bit, size):
    return lax.ppermute(value, axis, [(i, i ^ (1 << bit)) for i in range(size)])


def bits_of(size):
    return size.bit_length() - 1


def own_bit(axis, bit):
    return (lax.axis_index(axis) >> bit) & 1


def joined(mine, got, own):
    return jnp.where(own == 0, jnp.concatenate([mine, got]), jnp.concatenate([got, mine]))


def cube_step(value, axis, bit, size):
    return joined(value, flip(value, axis, bit, size), own_bit(axis, bit))


def lines_first(value):
    return jnp.transpose(value, (1, 0, 2, 3)).reshape(value.shape[1], value.shape[0] * value.shape[2], value.shape[3])


def cube_gather(value, axis, size):
    value = value[None]
    for bit in range(bits_of(size)):
        value = cube_step(value, axis, bit, size)
    return value


def sum_dp(value, sizes):
    for bit in range(bits_of(sizes["dp"])):
        value = value + flip(value, "dp", bit, sizes["dp"])
    return value


def reduce_over_dp(value, size):
    count = bits_of(size)
    value = value.reshape(value.shape[:1] + (2,) * count + value.shape[2:])
    current = value
    for bit in range(count - 1, -1, -1):
        own = own_bit("dp", bit)
        keep = lax.dynamic_index_in_dim(current, own, 1, keepdims=False)
        send = lax.dynamic_index_in_dim(current, 1 - own, 1, keepdims=False).astype(bf16)
        current = keep.astype(f32) + flip(send, "dp", bit, size).astype(f32)
    return current


def start_move(run, size):
    return flip(run[0], "dp", 0, size), flip(run[2], "dp", 1, size)


def second_move(sums, size):
    send_a, held_a, send_b, held_b = sums
    return held_a, flip(send_a, "dp", 1, size), held_b, flip(send_b, "dp", 0, size)


def layer(sizes):
    n_dp, n_row, n_col = sizes["dp"], sizes["row"], sizes["col"]
    members = n_row * n_col
    fast = n_dp == 4
    assert n_row == 2 and n_col == COLS and n_dp & (n_dp - 1) == 0

    def local(
        tokens, cotangent, routes, lengths, gain_attn, w_query, w_key, w_value, w_out,
        gain_moe, w_router, w_gate, w_up, w_down,
    ):
        rows, width = tokens.shape
        group = rows * members
        local_experts = w_gate.shape[0]
        row, col, dp = lax.axis_index("row"), lax.axis_index("col"), lax.axis_index("dp")
        place = jnp.stack([row, col, row * n_col + col, dp & 1, (dp >> 1) & 1]).astype(jnp.int32)
        gain_one = gain_attn.astype(f32)[None]
        gain_two = gain_moe.astype(f32)[None]

        tok_all = gather_group(tokens)
        w_in = jnp.concatenate([w_query.T, w_key.T, w_value.T], axis=0)
        out_share, in_share = rows // n_dp, w_in.shape[0] // n_dp
        shares = jnp.concatenate(
            [
                lax.dynamic_slice(w_out.T, (dp * out_share, 0), (out_share, width)),
                lax.dynamic_slice(w_in, (dp * in_share, 0), (in_share, width)),
                jnp.pad(routes.T.astype(bf16).reshape(1, TOP * rows), ((0, 7), (0, width - TOP * rows))),
            ],
            axis=0,
        )
        w_stack = jnp.concatenate([w_query.T, w_key.T, w_value.T, w_value.T], axis=0)
        w_natural = jnp.concatenate([w_query, w_key, w_value, w_value], axis=1)

        ends = jnp.cumsum(lengths[0])
        starts = ends - lengths[0]
        position = jnp.arange(group, dtype=jnp.int32)
        segment = jnp.sum((position[:, None] >= ends[None, :]).astype(jnp.int32), axis=1)
        member = segment[:, None] == jnp.arange(starts.shape[0], dtype=jnp.int32)[None, :]
        start = jnp.sum(jnp.where(member, starts[None, :], 0), axis=1).astype(jnp.int32)
        frequency = rope_base ** (-2.0 * jnp.arange(HEAD_DIM // 2, dtype=f32) / HEAD_DIM)
        angle = (position - start).astype(f32)[:, None] * frequency[None, :]
        cosine = jnp.tile(jnp.cos(angle), (1, 4))
        sine = jnp.tile(jnp.sin(angle), (1, 4))

        w_router_rows = w_router.T.reshape(members, local_experts, width)
        w_router_rows = jnp.pad(w_router_rows, ((0, 0), (0, 8 - local_experts), (0, 0)))
        w_router_rows = w_router_rows.reshape(members * 8, width)
        start_row = jnp.broadcast_to(start[None, :], (8, group))
        start = start[:, None]
        gain_column = gain_attn.astype(f32)[:, None]
        ready = (place, gain_one, gain_two, w_stack, w_natural, cosine, sine, w_router_rows, start, start_row, gain_column)
        shares, place, gain_one, gain_two, w_stack, w_natural, cosine, sine, w_router_rows, start, start_row, gain_column = (
            lax.optimization_barrier((shares,) + ready)
        )
        shares = line_pieces(after(shares, tok_all, cosine))

        query, key, value, normed_one = project(tok_all, gain_one, w_stack, cosine, sine)
        packed, attended, totals = attend(query, key, value, start)
        att_flat = gather_group(packed)
        att_all = att_flat.reshape((n_row, n_col) + packed.shape)
        shares = in_line_order(after(shares, packed))
        route_rows = shares[:, out_share + in_share]
        w_out_mine, in_part = shares[None, :, :out_share], shares[None, :, out_share : out_share + in_share]
        for bit in range(bits_of(n_dp)):
            w_out_mine = cube_step(w_out_mine, "dp", bit, n_dp)
        in_part = cube_step(in_part, "dp", 0, n_dp)
        w_out_mine = lines_first(w_out_mine)
        w_out_other = lax.ppermute(after(w_out_mine, in_part), "row", SWAP)
        route_rows = cube_gather(route_rows, "row", n_row)[:, :, : TOP * rows].reshape(members, TOP, rows)
        cot_all = gather_group(after(cotangent, w_out_other))
        x, slot_gate, rank, gate, normed_two, middle, gates = middle_and_dispatch(
            place, att_all, w_out_mine, w_out_other, tok_all, route_rows, gain_two, w_router_rows, local_experts
        )
        slots = members * CAPACITY
        x = x.reshape(local_experts, slots, width)
        slot_gate = slot_gate.reshape(local_experts, slots, LANES)
        rank, gate = rank.reshape(members, 8, rows), gate.reshape(members, 8, rows)
        forth, active, factor, silu = run_experts(x, slot_gate, w_gate, w_up, w_down)
        for bit in range(1, bits_of(n_dp) - 1):
            in_part = cube_step(in_part, "dp", bit, n_dp)
        last_bit = bits_of(n_dp) - 1
        in_got = after(flip(in_part, "dp", last_bit, n_dp), forth)
        forth_other = combine(place, after(rank, in_got), [forth])
        arrived = lax.ppermute(forth_other, "row", SWAP)
        g = grad_dispatch(after(rank, forth_other), gate, cot_all, local_experts)
        g = g.reshape(local_experts, slots, width)
        cuts = [0, 1, 3, local_experts]

        def backward(which, x):
            first, last = cuts[which], cuts[which + 1]
            return run_experts_back(place, x, g, active, factor, silu, w_gate, w_up, w_down, first, last - first, fast)

        runs = [backward(0, x)]
        forth_mine = combine(place, rank, [forth], arrived=after(arrived, runs[0][1]))
        forth_sums = lax.all_to_all(forth_mine, "col", 0, 0, tiled=True)
        runs.append(backward(1, after(x, forth_mine)))
        runs.append(backward(2, after(x, runs[1][1])))
        moved = [start_move(run[2:], n_dp) for run in runs] if fast else []
        back_parts, dot_parts = [run[0] for run in runs], [run[1] for run in runs]
        back_other = combine(place, after(rank, *moved[0]) if fast else rank, back_parts, dot_parts)
        arrived = lax.ppermute(back_other, "row", SWAP)
        back_mine = combine(place, rank, back_parts, dot_parts, arrived)
        back_mine = after(back_mine, forth_sums)
        back_sums = lax.all_to_all(back_mine, "col", 0, 0, tiled=True)

        if fast:
            w_in_parts = [in_part, in_got]
        else:
            own = own_bit("dp", last_bit)
            w_in_rows = lines_first(joined(in_part, in_got, own))[None]
            half = w_in_rows.shape[2] // 2
            upper, lower = w_in_rows[:, :, :half], w_in_rows[:, :, half:]
            w_in_parts = [jnp.where(place[4] == 0, upper, lower), jnp.where(place[4] == 0, lower, upper)]
        if fast:

            def chunk_of(which, *events):
                keep_a, keep_b = after((runs[which][3], runs[which][5]), *events)
                return keep_a, moved[which][0], keep_b, moved[which][1]

            sums = first_sum(place, chunk_of(0, back_mine), cuts[0], cuts[2])
            gate_middle = (sums[1],) + moved[1]
        else:
            gate_middle = ()
        w_in_parts += [lax.ppermute(after(part, back_mine), "row", SWAP) for part in w_in_parts]

        mixed = (middle + jnp.sum(after(forth_sums, back_mine).astype(f32), axis=0)).astype(bf16)

        middle_grad, branch_grad, attended_grad = middle_back(
            place, back_sums, gates, middle, cotangent, after(gain_two, mixed, *w_in_parts[2:], *gate_middle),
            w_router_rows, w_out_mine, w_out_other,
        )
        if fast:
            sums = first_sum(place, chunk_of(1, branch_grad), cuts[1], cuts[2], sums)
            started = [second_move(sums, n_dp)]
        attended_grad = lax.all_to_all(attended_grad, ("row", "col"), 0, 0, tiled=True)
        if fast:
            attended_grad = after(attended_grad, sums[1])
        branch_all = gather_group(branch_grad)

        attended_grad = attended_grad.reshape(group, 2 * LANES)
        projected_grad, own_grads = attend_back(
            query, key, value, attended_grad, totals, start_row, cosine, sine, normed_one, w_natural, gain_column
        )
        projected_all = lax.all_to_all(projected_grad, ("row", "col"), 0, 0, tiled=True)
        *w_parts, small = out_weights(
            place, branch_all, attended, normed_two.reshape(group, width), own_grads,
            members * 8, local_experts, fast,
        )
        arriving = ()
        if fast:
            w_moved = start_move(w_parts, n_dp)
            late = first_sum(place, chunk_of(2, small, started[0][1], started[0][3]))
            started.append(second_move(late, n_dp))
            w_first = first_sum(place, (w_parts[1], w_moved[0], w_parts[3], w_moved[1]))
            w_sums = second_move(w_first, n_dp)
            arriving = (w_first[1], started[1][0])
        else:
            cut = w_parts[0].reshape(1, n_dp, width // n_dp, w_parts[0].shape[1])
            w_sum = reduce_over_dp(cut, n_dp)[0]


        used = small.reshape(members, 8, width)[:, :local_experts].reshape(members * local_experts, width)
        both = sum_dp(jnp.concatenate([used, small[7:8]], axis=0), sizes)
        w_router_grad = both[: members * local_experts].T
        gain_moe_grad = both[members * local_experts]

        tokens_grad, share = input_grad(
            place, projected_all, w_in_parts, tokens, middle_grad, after(gain_one, w_parts[0], *arriving)
        )
        share = (share[0:4] + share[4:8]).reshape(8, width // 8)
        if fast:
            held_a, got_a, held_b, got_b = started[0]
            held_a, held_b = after((held_a, held_b), tokens_grad)
            expert_grads = last_sum(held_a, got_a, held_b, got_b, 0, local_experts, None)
            share = share + flip(share, "dp", 0, n_dp)
            held_a, got_a, held_b, got_b = started[1]
            held_a, held_b = after((held_a, held_b), share)
            expert_grads = last_sum(held_a, got_a, held_b, got_b, cuts[2], local_experts, expert_grads)
            gain_attn_grad = (share + flip(share, "dp", 1, n_dp)).reshape(width)
        else:
            gain_attn_grad = sum_dp(share, sizes).reshape(width)

        local_q, local_k = w_query.shape[1], w_key.shape[1]
        if fast:
            w_query_grad, w_key_grad, w_value_grad, w_out_grad = [
                item.T for item in last_weights(w_sums, (local_q, local_k, local_k, local_q))
            ]
        else:
            expert_grads = []
            for which in range(3):
                parts = [run[2 + which] for run in runs]
                parts = [part.reshape(part.shape[0], n_dp, width // n_dp, part.shape[2]) for part in parts]
                expert_grads.append(jnp.concatenate([reduce_over_dp(part, n_dp) for part in parts], axis=0))
            cut = local_q + local_k
            w_query_grad, w_key_grad = w_sum[:, :local_q], w_sum[:, local_q:cut]
            w_out_grad, w_value_grad = w_sum[:, cut : cut + local_q], w_sum[:, cut + local_q :]
        w_gate_grad, w_up_grad, w_down_grad = expert_grads
        return (
            mixed, tokens_grad, gain_attn_grad, w_query_grad, w_key_grad, w_value_grad, w_out_grad,
            gain_moe_grad, w_router_grad, w_gate_grad, w_up_grad, w_down_grad,
        )

    return local


def solution(mesh):
    return jax.shard_map(
        layer(dict(mesh.shape)),
        mesh=mesh,
        in_specs=(
            P(("dp", "row", "col"), None),
            P(("dp", "row", "col"), None),
            P(("dp", "row", "col"), None),
            P("dp", None),
            P(),
            P(None, ("row", "col")),
            P(None, ("row", "col")),
            P(None, ("row", "col")),
            P(None, ("row", "col")),
            P(),
            P(),
            P(("row", "col"), None, None),
            P(("row", "col"), None, None),
            P(("row", "col"), None, None),
        ),
        out_specs=(
            P(("dp", "row", "col"), None),
            P(("dp", "row", "col"), None),
            P(),
            P("dp", ("row", "col")),
            P("dp", ("row", "col")),
            P("dp", ("row", "col")),
            P("dp", ("row", "col")),
            P(),
            P(),
            P(("row", "col"), "dp", None),
            P(("row", "col"), "dp", None),
            P(("row", "col"), "dp", None),
        ),
        check_vma=False,
    )
```

```python
import math

import jax
import jax.numpy as jnp
import numpy as np
from jax import lax
from jax.experimental import pallas as pl
from jax.experimental.pallas import tpu as pltpu
from jax.sharding import PartitionSpec as P

HEAD_DIM = 64
EXPERTS = 40
TOP = 8
CAPACITY = 64
COLS = 4
LANES = 128
QUERY_BLOCK = 256
DOT_ROWS = 16

epsilon = 1e-06
rope_base = 10000.0
masked_score = -1e30
f32 = jnp.float32
bf16 = jnp.bfloat16
VMEM_LIMIT = 56 * 1024 * 1024

NT = (((1,), (1,)), ((), ()))
TN = (((0,), (0,)), ((), ()))


def dot(a, b):
    return jnp.dot(a, b, preferred_element_type=f32)


def dot_nt(a, b):
    return lax.dot_general(a, b, NT, preferred_element_type=f32)


def dot_tn(a, b):
    return lax.dot_general(a, b, TN, preferred_element_type=f32)


def lane_of(shape):
    return lax.broadcasted_iota(jnp.int32, shape, len(shape) - 1)


def call(
    kernel, grid, prefetch, in_specs, out_specs, out_shape, scratch=(), us=1.0, aliases=None
):
    return pl.pallas_call(
        kernel,
        grid_spec=pltpu.PrefetchScalarGridSpec(
            num_scalar_prefetch=prefetch,
            grid=grid,
            in_specs=in_specs,
            out_specs=out_specs,
            scratch_shapes=list(scratch),
        ),
        out_shape=out_shape,
        input_output_aliases=aliases or {},
        compiler_params=pltpu.CompilerParams(
            vmem_limit_bytes=VMEM_LIMIT, dimension_semantics=("arbitrary",) * len(grid)
        ),
        cost_estimate=pl.CostEstimate(
            flops=int(us * 1.1e9), bytes_accessed=int(us * 3.6e6), transcendentals=0
        ),
    )


def whole(shape):
    zeros = (0,) * len(shape)
    return pl.BlockSpec(shape, lambda *_: zeros)


def struct(shape, dtype):
    return jax.ShapeDtypeStruct(shape, dtype)


def turn_within_heads(values, sign):
    lane = lane_of(values.shape) % HEAD_DIM
    ahead = pltpu.roll(values, LANES - HEAD_DIM // 2, 1)
    behind = pltpu.roll(values, HEAD_DIM // 2, 1)
    return jnp.where(lane < HEAD_DIM // 2, -sign * ahead, sign * behind)


def project_kernel(
    tok_ref, gain_ref, w_ref, cos_ref, sin_ref, query_ref, key_ref, value_ref, normed_ref
):
    resid = tok_ref[...].astype(f32)
    inverse = lax.rsqrt(jnp.mean(resid * resid, axis=1, keepdims=True) + epsilon)
    normed = (resid * inverse * gain_ref[...]).astype(bf16)
    normed_ref[...] = normed
    raw = dot_nt(normed, w_ref[...])
    cosine, sine = cos_ref[...], sin_ref[...]

    def rot(values):
        return (values * cosine + turn_within_heads(values, 1.0) * sine).astype(bf16).astype(f32)

    first = rot(raw[:, :LANES])
    second = rot(raw[:, LANES : 2 * LANES])
    low = lane_of(first.shape) < HEAD_DIM
    scale = 1.0 / math.sqrt(HEAD_DIM)
    query_ref[0] = jnp.where(low, first * scale, 0.0).astype(bf16)
    query_ref[1] = jnp.where(low, 0.0, first * scale).astype(bf16)
    query_ref[2] = jnp.where(low, second * scale, 0.0).astype(bf16)
    key_ref[...] = jnp.where(low, pltpu.roll(second, HEAD_DIM, 1), second).astype(bf16)
    value_ref[...] = raw[:, 2 * LANES :].astype(bf16)


def project(tokens, gain, w_stack, cosine, sine):
    total, width = tokens.shape
    rows = 512
    lanes = pl.BlockSpec((rows, LANES), lambda j: (j, 0))
    wide = pl.BlockSpec((rows, width), lambda j: (j, 0))
    return call(
        project_kernel,
        (total // rows,),
        0,
        [wide, whole((1, width)), whole(w_stack.shape), lanes, lanes],
        [pl.BlockSpec((3, rows, LANES), lambda j: (0, j, 0)), lanes, lanes, wide],
        [
            struct((3, total, LANES), bf16),
            struct((total, LANES), bf16),
            struct((total, LANES), bf16),
            struct((total, width), bf16),
        ],
        us=0.5,
    )(tokens, gain, w_stack, cosine, sine)


def attend_kernel(query_ref, key_ref, value_ref, start_ref, packed_ref, plain_ref, total_ref, out_ref):
    blocks = query_ref.shape[1] // QUERY_BLOCK
    block = pl.program_id(0)
    for index in range(blocks):

        @pl.when(block == index)
        def _(index=index):
            rows = pl.ds(index * QUERY_BLOCK, QUERY_BLOCK)
            span = (index + 1) * QUERY_BLOCK
            row = index * QUERY_BLOCK + lax.broadcasted_iota(jnp.int32, (QUERY_BLOCK, span), 0)
            column = lane_of((QUERY_BLOCK, span))
            allowed = (column <= row) & (column >= start_ref[rows, :])

            def head(number, carry):
                scores = dot_nt(query_ref[number, rows, :], key_ref[0:span, :])
                scores = jnp.where(allowed, scores, masked_score)
                peak = jnp.max(scores, axis=1, keepdims=True)
                weights = jnp.exp(scores - peak)
                summed = jnp.sum(weights, axis=1, keepdims=True)
                probs = (weights * (1.0 / summed)).astype(bf16)
                out_ref[number] = dot(probs, value_ref[0:span, :])
                total = jnp.broadcast_to(peak + jnp.log(summed), (QUERY_BLOCK, LANES))
                total_ref[number, :, rows] = jnp.transpose(total)[0:8, :]
                return carry

            lax.fori_loop(0, 3, head, 0)
            low = lane_of((QUERY_BLOCK, LANES)) < HEAD_DIM
            one, two, three = out_ref[0], out_ref[1], out_ref[2]
            pair = jnp.where(low, one, two).astype(bf16)
            plain_ref[rows, 0:LANES] = pair
            plain_ref[rows, LANES : 2 * LANES] = jnp.where(low, three, 0.0).astype(bf16)
            if index < blocks // 2:
                packed_ref[rows, 0:LANES] = pair
                packed_ref[rows, LANES : 2 * LANES] = three.astype(bf16)
            else:
                back = pl.ds((index - blocks // 2) * QUERY_BLOCK, QUERY_BLOCK)
                before = packed_ref[back, LANES : 2 * LANES].astype(f32)
                packed_ref[back, LANES : 2 * LANES] = jnp.where(low, before, one).astype(bf16)
                packed_ref[back, 2 * LANES : 3 * LANES] = jnp.where(low, two, three).astype(bf16)


def attend(query, key, value, start):
    total = key.shape[0]
    return call(
        attend_kernel,
        (total // QUERY_BLOCK,),
        0,
        [whole(query.shape), whole(key.shape), whole(value.shape), whole(start.shape)],
        [whole((total // 2, 3 * LANES)), whole((total, 2 * LANES)), whole((3, 8, total))],
        [
            struct((total // 2, 3 * LANES), bf16),
            struct((total, 2 * LANES), bf16),
            struct((3, 8, total), f32),
        ],
        scratch=[pltpu.VMEM((3, QUERY_BLOCK, LANES), f32)],
        us=0.5,
    )(query, key, value, start)


def attend_back_kernel(
    query_ref, key_ref, value_ref, grad_ref, total_ref, start_ref, cos_ref, sin_ref, normed_ref, w_ref, gain_ref,
    blocks_ref, own_ref, out_ref, query_grad_ref, key_grad_ref, value_grad_ref, own_sum_ref
):
    blocks = query_ref.shape[1] // QUERY_BLOCK
    block = pl.program_id(0)
    scale = 1.0 / math.sqrt(HEAD_DIM)

    @pl.when(block == 0)
    def _():
        key_grad_ref[...] = jnp.zeros_like(key_grad_ref)
        value_grad_ref[...] = jnp.zeros_like(value_grad_ref)

    def back(values, cosine, sine):
        return values * cosine + turn_within_heads(values * sine, -1.0)

    for index in range(blocks):

        @pl.when(block == index)
        def _(index=index):
            rows = pl.ds(index * QUERY_BLOCK, QUERY_BLOCK)
            span = (index + 1) * QUERY_BLOCK
            row = index * QUERY_BLOCK + lane_of((span, QUERY_BLOCK))
            column = lax.broadcasted_iota(jnp.int32, (span, QUERY_BLOCK), 0)
            allowed = (column <= row) & (column >= start_ref[0:1, rows])
            low = lane_of((QUERY_BLOCK, LANES)) < HEAD_DIM

            def head(number, carry):
                query = query_ref[number, rows, :]
                tile = pl.multiple_of((number // 2) * LANES, LANES)
                upstream = grad_ref[rows, pl.ds(tile, LANES)].astype(f32)
                keep = low == (number != 1)
                upstream = jnp.where(keep, upstream, 0.0).astype(bf16)
                scores = dot_nt(key_ref[0:span, :], query)
                probs = jnp.exp(scores - total_ref[number, 0:1, rows])
                probs = jnp.where(allowed, probs, 0.0)
                prob_grad = dot_nt(value_ref[0:span, :], upstream)
                row_dot = jnp.sum(probs * prob_grad, axis=0, keepdims=True)
                score_grad = (probs * (prob_grad - row_dot)).astype(bf16)
                key_grad_ref[0:span, :] += dot(score_grad, query)
                value_grad_ref[0:span, :] += dot(probs.astype(bf16), upstream)
                query_grad_ref[number] = dot_tn(score_grad, key_ref[0:span, :]) * scale
                return carry

            lax.fori_loop(0, 3, head, 0)
            cosine, sine = cos_ref[rows, :], sin_ref[rows, :]
            pair = jnp.where(low, query_grad_ref[0], query_grad_ref[1])
            out_ref[rows, 0:LANES] = back(pair, cosine, sine).astype(bf16)
            out_ref[rows, LANES : 2 * LANES] = back(query_grad_ref[2], cosine, sine).astype(bf16)

    @pl.when(block == blocks - 1)
    def _():
        low = lane_of(key_grad_ref.shape) < HEAD_DIM
        key_grad = key_grad_ref[...]
        key_grad = key_grad + pltpu.roll(key_grad, HEAD_DIM, 1)
        key_grad = back(key_grad, cos_ref[...], sin_ref[...])
        before = out_ref[:, LANES : 2 * LANES].astype(f32)
        out_ref[:, LANES : 2 * LANES] = jnp.where(low, before, key_grad).astype(bf16)
        value_grad = value_grad_ref[...]
        value_grad = value_grad + pltpu.roll(value_grad, HEAD_DIM, 1)
        out_ref[:, 2 * LANES : 3 * LANES] = jnp.where(low, 0.0, value_grad).astype(bf16)
        chunk = 512
        own_sum_ref[...] = jnp.zeros_like(own_sum_ref)

        def add(index, carry):
            part = pl.ds(pl.multiple_of(index * chunk, chunk), chunk)
            own_sum_ref[...] += dot_tn(normed_ref[part, :], out_ref[part, :])
            return carry

        lax.fori_loop(0, out_ref.shape[0] // chunk, add, 0)
        own = own_sum_ref[...]
        own_ref[...] = own.astype(bf16)
        share = jnp.sum(own * w_ref[...].astype(f32), axis=1, keepdims=True) / gain_ref[...]
        share = jnp.transpose(jnp.broadcast_to(share, (share.shape[0], LANES)))[0:8, :]
        width = blocks_ref.shape[2]
        row = lax.broadcasted_iota(jnp.int32, (8, width), 0)
        terms = jnp.zeros((8, width), f32)
        for index in range(share.shape[1] // width):
            piece = share[:, index * width : (index + 1) * width]
            upper = piece.astype(bf16).astype(f32)
            terms = jnp.where(row == index, upper, jnp.where(row == index + 4, piece - upper, terms))
        terms = jnp.concatenate([terms, jnp.zeros((8, width), f32)], axis=0).astype(bf16)
        rows = blocks_ref.shape[1] - DOT_ROWS
        for index in range(blocks_ref.shape[0]):
            blocks_ref[index, 0:rows, :] = out_ref[index * rows : (index + 1) * rows, :]
            blocks_ref[index, rows:, :] = terms


def attend_back(query, key, value, grad, totals, start, cosine, sine, normed, w_natural, gain):
    total = key.shape[0]
    members = 2 * COLS
    rows = total // members + DOT_ROWS
    args = (query, key, value, grad, totals, start, cosine, sine, normed, w_natural, gain)
    return call(
        attend_back_kernel,
        (total // QUERY_BLOCK,),
        0,
        [whole(item.shape) for item in args],
        [whole((members, rows, 3 * LANES)), whole(w_natural.shape)],
        [struct((members, rows, 3 * LANES), bf16), struct(w_natural.shape, bf16)],
        scratch=[
            pltpu.VMEM((total, 3 * LANES), bf16),
            pltpu.VMEM((3, QUERY_BLOCK, LANES), f32),
            pltpu.VMEM((total, LANES), f32),
            pltpu.VMEM((total, LANES), f32),
            pltpu.VMEM(w_natural.shape, f32),
        ],
        us=0.5,
    )(*args)


def branch_operand(refs):
    rows = refs.shape[2]
    low = lane_of((rows, LANES)) < HEAD_DIM
    pairs, thirds = [], []
    for member in range(refs.shape[1]):
        one = refs[0, member, :, 0:LANES]
        mid = refs[0, member, :, LANES : 2 * LANES].astype(f32)
        end = refs[0, member, :, 2 * LANES : 3 * LANES].astype(f32)
        mid_turned = pltpu.roll(mid, HEAD_DIM, 1)
        end_turned = pltpu.roll(end, HEAD_DIM, 1)
        late = jnp.where(low, mid_turned, end_turned).astype(bf16)
        pairs.append(jnp.concatenate([one, late], axis=0))
        thirds.append((mid, end_turned))
    for member in range(0, refs.shape[1], 2):
        tops = []
        for which in range(2):
            left, right = thirds[member][which], thirds[member + 1][which]
            tops.append(jnp.where(low, left, pltpu.roll(right, HEAD_DIM, 1)).astype(bf16))
        pairs.append(jnp.concatenate(tops, axis=0))
    return jnp.concatenate(pairs, axis=1)


def branch_weights(ref):
    right = [ref[source, 0:LANES] for source in range(ref.shape[0])]
    return jnp.concatenate(right + [ref[source, LANES:] for source in range(ref.shape[0])], axis=0)


def hits_of(rank, local_experts):
    place = lax.broadcasted_iota(jnp.int32, (CAPACITY, rank.shape[1]), 0).astype(f32)
    return [place == rank[j : j + 1, :] for j in range(local_experts)]


def chosen_of(hits):
    return jnp.concatenate([jnp.where(hit, 1.0, 0.0).astype(bf16) for hit in hits], axis=0)


def middle_kernel(
    place_ref, att_mine_ref, att_other_ref, w_mine_ref, w_other_ref, tok_a_ref, tok_b_ref, routes_a_ref, routes_b_ref,
    gain_ref, w_router_ref, after_ref,
    x_ref, slot_gate_ref, rank_ref, gate_ref, normed_ref, middle_ref, gates_own_ref, gates_ref, ranks_ref
):
    step = pl.program_id(0)
    member = place_ref[2]
    cols = pl.num_programs(0)
    rows = tok_a_ref.shape[0]
    local_experts = x_ref.shape[0]
    branch = dot(branch_operand(att_mine_ref), branch_weights(w_mine_ref))
    branch = branch + dot(branch_operand(att_other_ref), branch_weights(w_other_ref))
    for half in range(2):
        tok_ref, routes_ref = ((tok_a_ref, routes_a_ref), (tok_b_ref, routes_b_ref))[half]
        middle = tok_ref[...].astype(f32) + branch[half * rows : (half + 1) * rows]
        inverse = lax.rsqrt(jnp.mean(middle * middle, axis=1, keepdims=True) + epsilon)
        normed = (middle * inverse * gain_ref[...]).astype(bf16)
        normed_ref[half, 0] = normed
        logits = dot_nt(w_router_ref[...], normed)
        padded = logits.shape[0]
        slot = lax.broadcasted_iota(jnp.int32, (padded, rows), 0)
        expert = (slot // 8) * local_experts + slot % 8
        expert = jnp.where(slot % 8 < local_experts, expert, -1).astype(f32)
        routes = routes_ref[0].astype(f32)
        named = expert == routes[0:1, 0:rows]
        for k in range(1, TOP):
            named = named | (expert == routes[k : k + 1, 0:rows])
        peak = jnp.max(jnp.where(named, logits, masked_score), axis=0, keepdims=True)
        weights = jnp.where(named, jnp.exp(logits - peak), 0.0)
        gates = weights / jnp.sum(weights, axis=0, keepdims=True)
        gates_ref[...] = gates
        ranks_ref[...] = jnp.where(named, dot(named.astype(f32).astype(bf16), after_ref[...]), -1.0)
        here = pl.ds(pl.multiple_of(member * 8, 8), 8)
        gate, rank = gates_ref[here, :], ranks_ref[here, :]
        rank_ref[half, 0] = rank
        gate_ref[half, 0] = gate
        hits = hits_of(rank, local_experts)
        slot_gate = jnp.concatenate(
            [jnp.sum(jnp.where(hit, gate[j : j + 1, :], 0.0), axis=1, keepdims=True) for j, hit in enumerate(hits)],
            axis=0,
        )
        chosen = chosen_of(hits)
        picked = dot(chosen, normed).astype(bf16)
        spread = jnp.broadcast_to(slot_gate, (slot_gate.shape[0], LANES))
        for j in range(local_experts):
            part = slice(j * CAPACITY, (j + 1) * CAPACITY)
            x_ref[j, half, 0] = picked[part]
            slot_gate_ref[j, half, 0] = spread[part]

        @pl.when(member == half * cols + step)
        def _(middle=middle, gates=gates):
            middle_ref[...] = middle
            gates_own_ref[...] = gates


def middle_and_dispatch(place, att, w_mine, w_other, tokens, routes, gain, w_router, local_experts):
    width = tokens.shape[1]
    half = COLS
    rows = tokens.shape[0] // (2 * half)
    padded = w_router.shape[0]
    after = jnp.asarray(np.triu(np.ones((rows, rows), np.float32), 1), bf16)
    slot_shape = (local_experts, 2, half, CAPACITY)
    early = pl.BlockSpec((rows, width), lambda i, p: (i, 0))
    late = pl.BlockSpec((rows, width), lambda i, p: (i + half, 0))
    routes_shape = (1,) + routes.shape[1:]
    return call(
        middle_kernel,
        (half,),
        1,
        [
            pl.BlockSpec((1, half, rows, 3 * LANES), lambda i, p: (p[0], 0, i, 0)),
            pl.BlockSpec((1, half, rows, 3 * LANES), lambda i, p: (1 - p[0], 0, i, 0)),
            whole(w_mine.shape),
            whole(w_other.shape),
            early,
            late,
            pl.BlockSpec(routes_shape, lambda i, p: (i, 0, 0)),
            pl.BlockSpec(routes_shape, lambda i, p: (i + half, 0, 0)),
            whole((1, width)),
            whole(w_router.shape),
            whole((rows, rows)),
        ],
        [
            pl.BlockSpec((local_experts, 2, 1, CAPACITY, width), lambda i, p: (0, 0, i, 0, 0)),
            pl.BlockSpec((local_experts, 2, 1, CAPACITY, LANES), lambda i, p: (0, 0, i, 0, 0)),
            pl.BlockSpec((2, 1, 8, rows), lambda i, p: (0, i, 0, 0)),
            pl.BlockSpec((2, 1, 8, rows), lambda i, p: (0, i, 0, 0)),
            pl.BlockSpec((2, 1, rows, width), lambda i, p: (0, i, 0, 0)),
            whole((rows, width)),
            whole((padded, rows)),
        ],
        [
            struct(slot_shape + (width,), bf16),
            struct(slot_shape + (LANES,), f32),
            struct((2, half, 8, rows), f32),
            struct((2, half, 8, rows), f32),
            struct((2, half, rows, width), bf16),
            struct((rows, width), f32),
            struct((padded, rows), f32),
        ],
        scratch=[pltpu.VMEM((padded, rows), f32), pltpu.VMEM((padded, rows), f32)],
        us=0.5,
    )(place, att, att, w_mine, w_other, tokens, tokens, routes, routes, gain, w_router, after)


def grad_dispatch_kernel(rank_ref, gate_ref, cot_ref, g_ref):
    local_experts = g_ref.shape[0]
    rows = cot_ref.shape[0] // 2
    for half in range(2):
        hits = hits_of(rank_ref[half], local_experts)
        gate = gate_ref[half]
        slot_gate = jnp.concatenate(
            [jnp.sum(jnp.where(hit, gate[j : j + 1, :], 0.0), axis=1, keepdims=True) for j, hit in enumerate(hits)],
            axis=0,
        )
        grads = (dot(chosen_of(hits), cot_ref[half * rows : (half + 1) * rows, :]) * slot_gate).astype(bf16)
        for j in range(local_experts):
            g_ref[j, half] = grads[j * CAPACITY : (j + 1) * CAPACITY]


def grad_dispatch(rank, gate, cotangents, local_experts):
    members, _, rows = rank.shape
    width = cotangents.shape[1]
    small = pl.BlockSpec((2, 8, rows), lambda j: (j, 0, 0))
    return call(
        grad_dispatch_kernel,
        (members // 2,),
        0,
        [small, small, pl.BlockSpec((2 * rows, width), lambda j: (j, 0))],
        pl.BlockSpec((local_experts, 2, CAPACITY, width), lambda j: (0, j, 0, 0)),
        struct((local_experts, members, CAPACITY, width), bf16),
        us=0.5,
    )(rank, gate, cotangents)


def expert_kernel(
    x_ref, gate_ref, w_gate_ref, w_up_ref, w_down_ref, forth_ref, active_ref, factor_ref, silu_ref
):
    gate_pre = dot(x_ref[0], w_gate_ref[0])
    up_pre = dot(x_ref[0], w_up_ref[0])
    sig = 1.0 / (1.0 + jnp.exp(-gate_pre))
    silu = gate_pre * sig
    silu_ref[0] = silu
    factor_ref[0] = up_pre * sig * (1.0 + gate_pre * (1.0 - sig))
    active_ref[0] = (silu * up_pre).astype(bf16)
    produced = dot_nt(active_ref[0], w_down_ref[0]).astype(bf16).astype(f32)
    forth_ref[0] = (produced * gate_ref[0, :, 0:1]).astype(bf16)


def run_experts(x, slot_gate, w_gate, w_up, w_down):
    count, slots, width = x.shape
    hidden = w_gate.shape[2]

    def per_expert(*shape):
        return pl.BlockSpec((1,) + shape, lambda e: (e, 0, 0))

    return call(
        expert_kernel,
        (count,),
        0,
        [per_expert(slots, width), per_expert(slots, LANES)] + [per_expert(width, hidden)] * 3,
        [per_expert(slots, width)] + [per_expert(slots, hidden)] * 3,
        [
            struct((count, slots, width), bf16),
            struct((count, slots, hidden), bf16),
            struct((count, slots, hidden), f32),
            struct((count, slots, hidden), f32),
        ],
        us=0.5,
    )(x, slot_gate, w_gate, w_up, w_down)


def expert_back_kernel(place_ref, *refs, fast):
    x_ref, g_ref, active_ref, factor_ref, silu_ref = refs[:5]
    w_gate_ref, w_up_ref, w_down_ref, back_ref, dots_ref = refs[5:10]
    grads, (gate_low_ref, up_low_ref) = refs[10:-2], refs[-2:]
    slots, width = g_ref.shape[1], g_ref.shape[2]
    chunk = 256
    active_grad = dot(g_ref[0], w_down_ref[0])
    gate_low_ref[...] = (active_grad * factor_ref[0]).astype(bf16)
    up_low_ref[...] = (active_grad * silu_ref[0]).astype(bf16)
    dots = jnp.sum(active_ref[0].astype(f32) * active_grad, axis=1, keepdims=True)
    dots_ref[0] = jnp.broadcast_to(dots, (slots, LANES))
    back_ref[0] = (dot_nt(gate_low_ref[...], w_gate_ref[0]) + dot_nt(up_low_ref[...], w_up_ref[0])).astype(bf16)

    def products(cols):
        x = x_ref[0, :, cols]
        yield 0, dot_tn(x, gate_low_ref[...]).astype(bf16)
        yield 1, dot_tn(x, up_low_ref[...]).astype(bf16)
        yield 2, dot_tn(g_ref[0, :, cols], active_ref[0]).astype(bf16)

    if fast:
        write_shards(place_ref, grads, products, width)
    else:

        def whole_columns(index, carry):
            cols = pl.ds(pl.multiple_of(index * chunk, chunk), chunk)
            for which, product in products(cols):
                grads[which][0, cols, :] = product
            return carry

        lax.fori_loop(0, width // chunk, whole_columns, 0)


def write_shards(place_ref, outs, products, width):
    send_a, keep_a, send_b, keep_b = outs
    x_bit, y_bit = place_ref[3], place_ref[4]
    shard = width // 4
    for dy in range(2):
        for dx in range(2):
            x, y = x_bit ^ dx, y_bit ^ dy
            cols = pl.ds(pl.multiple_of((y * 2 + x) * shard, shard), shard)
            for which, product in products(cols):
                side = product.shape[1] // 2
                (send_a if dx else keep_a)[0, which, y] = product[:, :side]
                (send_b if dy else keep_b)[0, which, x] = product[:, side:]


def run_experts_back(place, x, g, active, factor, silu, w_gate, w_up, w_down, first, count, fast):
    slots, width = g.shape[1], g.shape[2]
    hidden = w_gate.shape[2]

    def taken(*shape):
        return pl.BlockSpec((1,) + shape, lambda e, p: (e + first, 0, 0))

    def given(*shape):
        zeros = (0,) * len(shape)
        return pl.BlockSpec((1,) + shape, lambda e, p: (e,) + zeros)

    if fast:
        grad_shapes = [(3, 2, width // 4, hidden // 2)] * 4
    else:
        grad_shapes = [(width, hidden)] * 3
    return call(
        lambda *refs: expert_back_kernel(*refs, fast=fast),
        (count,),
        1,
        [taken(slots, width)] * 2 + [taken(slots, hidden)] * 3 + [taken(width, hidden)] * 3,
        [given(slots, width), given(slots, LANES)] + [given(*shape) for shape in grad_shapes],
        [struct((count, slots, width), bf16), struct((count, slots, LANES), f32)]
        + [struct((count,) + shape, bf16) for shape in grad_shapes],
        scratch=[pltpu.VMEM((slots, hidden), bf16)] * 2,
        us=0.5,
    )(place, x, g, active, factor, silu, w_gate, w_up, w_down)


DOT_LANES = 2 * LANES


def combine_kernel(place_ref, rank_ref, *refs, pieces, with_dots, mine):
    parts, rest = refs[:pieces], refs[pieces:]
    rows = rank_ref.shape[2]
    local_experts = sum(part.shape[0] for part in parts)
    hits = hits_of(rank_ref[0], local_experts)
    gathered = jnp.concatenate([part[j, 0] for part in parts for j in range(part.shape[0])], axis=0)
    summed = dot_tn(chosen_of(hits), gathered)
    out_ref = rest[-1]
    if mine:
        arrived_ref = rest[-2]
        summed = summed + arrived_ref[0, 0:rows, :].astype(f32)
    out_ref[0, 0:rows, :] = summed.astype(bf16)
    if with_dots:
        column = [part[j, 0][:, 0:1] for part in rest[:pieces] for j in range(part.shape[0])]
        scattered = [
            jnp.sum(jnp.where(hit, value, 0.0), axis=0, keepdims=True) for hit, value in zip(hits, column)
        ]
        scattered.append(jnp.zeros((DOT_ROWS - local_experts, rows), f32))
        scattered = jnp.concatenate(scattered, axis=0)
        upper = scattered.astype(bf16)
        out_ref[0, rows:, :] = jnp.zeros((DOT_ROWS, out_ref.shape[2]), bf16)
        out_ref[0, rows:, 0:rows] = upper
        out_ref[0, rows:, DOT_LANES : DOT_LANES + rows] = (scattered - upper.astype(f32)).astype(bf16)
        if mine:
            out_ref[0, rows:, 2 * DOT_LANES : 4 * DOT_LANES] = arrived_ref[0, rows:, 0 : 2 * DOT_LANES]


def combine(place, rank, parts, dots=None, arrived=None):
    mine = arrived is not None
    rows, width = rank.shape[2], parts[0].shape[-1]
    out_rows = rows + (DOT_ROWS if dots else 0)

    def member(step, p):
        return (p[0] if mine else 1 - p[0]) * COLS + step

    def slots_of(array):
        return pl.BlockSpec((array.shape[0], 1) + array.shape[2:], lambda j, p: (0, member(j, p), 0, 0))

    inputs = [
        part.reshape(part.shape[0], 2 * COLS, CAPACITY, part.shape[-1]) for part in list(parts) + list(dots or [])
    ]
    in_specs = [pl.BlockSpec((1, 8, rows), lambda j, p: (member(j, p), 0, 0))] + [slots_of(item) for item in inputs]
    by_chip = pl.BlockSpec((1, out_rows, width), lambda j, p: (j, 0, 0))
    if mine:
        inputs.append(arrived)
        in_specs.append(by_chip)
    return call(
        lambda *refs: combine_kernel(*refs, pieces=len(parts), with_dots=bool(dots), mine=mine),
        (COLS,),
        1,
        in_specs,
        by_chip,
        struct((COLS, out_rows, width), bf16),
        us=0.5,
    )(place, rank, *inputs)


def split_dot(dimension_numbers, values, exact):
    upper = values.astype(bf16)
    lower = (values - upper.astype(f32)).astype(bf16)
    return lax.dot_general(
        upper, exact, dimension_numbers, preferred_element_type=f32
    ) + lax.dot_general(lower, exact, dimension_numbers, preferred_element_type=f32)


EXTRA_SLOTS = 6


def middle_back_kernel(
    place_ref, sums_ref, gates_ref, middle_ref, cot_ref, gain_ref, w_router_ref, w_mine_ref, w_other_ref,
    grad_ref, branch_ref, attended_ref, extra_ref
):
    rows = middle_ref.shape[0]
    tail = sums_ref[:, rows : rows + 8, 0 : 4 * DOT_LANES].astype(f32)
    mine = tail[:, :, 0:rows] + tail[:, :, DOT_LANES : DOT_LANES + rows]
    other = tail[:, :, 2 * DOT_LANES : 2 * DOT_LANES + rows] + tail[:, :, 3 * DOT_LANES : 3 * DOT_LANES + rows]
    first_row = place_ref[0] == 0
    dots = jnp.concatenate([jnp.where(first_row, mine, other), jnp.where(first_row, other, mine)], axis=0)
    dots = dots.reshape(dots.shape[0] * 8, rows)
    gates = gates_ref[...]
    logit_grad = dots - gates * jnp.sum(dots, axis=0, keepdims=True)
    middle = middle_ref[...]
    inverse = lax.rsqrt(jnp.mean(middle * middle, axis=1, keepdims=True) + epsilon)
    unit = middle * inverse
    gain = gain_ref[...]
    grad = sums_ref[0, 0:rows].astype(f32)
    for index in range(1, sums_ref.shape[0]):
        grad = grad + sums_ref[index, 0:rows].astype(f32)
    grad = grad + split_dot(TN, logit_grad, w_router_ref[...])
    gain_grad = jnp.sum(grad * unit, axis=0, keepdims=True)
    scaled = grad * gain
    middle_grad = cot_ref[...].astype(f32) + inverse * (
        scaled - unit * jnp.mean(scaled * unit, axis=1, keepdims=True)
    )
    grad_ref[...] = middle_grad
    branch_grad = middle_grad.astype(bf16)
    branch_ref[0:rows, :] = branch_grad
    extra_ref[...] = jnp.zeros_like(extra_ref)
    for index in range(logit_grad.shape[0] // 8):
        first, lane = index // EXTRA_SLOTS * 8, index % EXTRA_SLOTS * DOT_LANES
        extra_ref[first : first + 8, lane : lane + rows] = logit_grad[index * 8 : index * 8 + 8]
    upper = gain_grad.astype(bf16).astype(f32)
    extra_ref[13:14, :] = upper
    extra_ref[14:15, :] = gain_grad - upper
    branch_ref[rows:, :] = extra_ref[...].astype(bf16)
    for which, ref in enumerate((w_mine_ref, w_other_ref)):
        line = place_ref[0] if which == 0 else 1 - place_ref[0]
        for col in range(ref.shape[0]):
            product = dot_nt(branch_grad, ref[col])
            member = line * COLS + col
            attended_ref[member, :, 0:LANES] = product[:, 0:LANES].astype(bf16)
            attended_ref[member, :, LANES : LANES + HEAD_DIM] = product[:, LANES:].astype(bf16)
            attended_ref[member, :, LANES + HEAD_DIM :] = jnp.zeros((product.shape[0], HEAD_DIM), bf16)


def middle_back(place, sums, gates, middle, cotangent, gain, w_router, w_mine, w_other):
    rows, width = middle.shape
    members = 2 * COLS
    args = (sums, gates, middle, cotangent, gain, w_router, w_mine, w_other)
    return call(
        middle_back_kernel,
        (1,),
        1,
        [whole(item.shape) for item in args],
        [whole((rows, width)), whole((rows + DOT_ROWS, width)), whole((members, rows, 2 * LANES))],
        [
            struct((rows, width), f32),
            struct((rows + DOT_ROWS, width), bf16),
            struct((members, rows, 2 * LANES), bf16),
        ],
        scratch=[pltpu.VMEM((DOT_ROWS, width), f32)],
        us=0.5,
    )(place, *args)


def input_grad_kernel(
    place_ref, grads_mine_ref, grads_other_ref, mine_a_ref, mine_b_ref, other_a_ref, other_b_ref,
    tok_ref, middle_grad_ref, gain_ref, out_ref, share_ref, sum_ref
):
    step = pl.program_id(0)
    first = place_ref[4] == 0

    def weights(a_ref, b_ref):
        a = jnp.concatenate([a_ref[index, 0] for index in range(a_ref.shape[0])], axis=0)
        b = jnp.concatenate([b_ref[index, 0] for index in range(b_ref.shape[0])], axis=0)
        upper, lower = jnp.where(first, a, b), jnp.where(first, b, a)
        return jnp.concatenate([upper, lower, lower[lower.shape[0] - HEAD_DIM :]], axis=0)

    rows = tok_ref.shape[0]
    part = dot(grads_mine_ref[0, 0:rows, :], weights(mine_a_ref, mine_b_ref))
    part = part + dot(grads_other_ref[0, 0:rows, :], weights(other_a_ref, other_b_ref))
    share = grads_mine_ref[0, rows:, :].astype(f32)[0:8] + grads_other_ref[0, rows:, :].astype(f32)[0:8]

    @pl.when(step == 0)
    def _():
        sum_ref[...] = part
        share_ref[...] = share

    @pl.when(step > 0)
    def _():
        sum_ref[...] += part
        share_ref[...] += share

    @pl.when(step == pl.num_programs(0) - 1)
    def _():
        resid = tok_ref[...].astype(f32)
        inverse = lax.rsqrt(jnp.mean(resid * resid, axis=1, keepdims=True) + epsilon)
        unit = resid * inverse
        scaled = sum_ref[...] * gain_ref[...]
        out_ref[...] = middle_grad_ref[...] + inverse * (
            scaled - unit * jnp.mean(scaled * unit, axis=1, keepdims=True)
        )


def input_grad(place, grads, weights, tokens, middle_grad, gain):
    rows, width = tokens.shape
    lanes = grads.shape[2]
    w_shape = (weights[0].shape[0], 1) + weights[0].shape[2:]
    return call(
        input_grad_kernel,
        (COLS,),
        1,
        [
            pl.BlockSpec((1, rows + DOT_ROWS, lanes), lambda c, p: (p[0] * COLS + c, 0, 0)),
            pl.BlockSpec((1, rows + DOT_ROWS, lanes), lambda c, p: ((1 - p[0]) * COLS + c, 0, 0)),
        ]
        + [pl.BlockSpec(w_shape, lambda c, p: (0, c, 0, 0))] * 4
        + [whole((rows, width)), whole((rows, width)), whole((1, width))],
        [whole((rows, width)), whole((8, lanes))],
        [struct((rows, width), f32), struct((8, lanes), f32)],
        scratch=[pltpu.VMEM((rows, width), f32)],
        us=0.5,
    )(place, grads, grads, *weights, tokens, middle_grad, gain)


def out_weights_kernel(place_ref, branch_ref, att_ref, normed_ref, own_ref, *refs, fast, local_experts):
    outs, small_ref, (sum_ref, gain_sum_ref) = refs[:-3], refs[-3], refs[-2:]
    step = pl.program_id(0)
    rows = att_ref.shape[0] // 2
    block = rows + DOT_ROWS

    @pl.when(step == 0)
    def _():
        sum_ref[...] = jnp.zeros_like(sum_ref)
        small_ref[...] = jnp.zeros_like(small_ref)
        gain_sum_ref[...] = jnp.zeros_like(gain_sum_ref)

    branch = jnp.concatenate([branch_ref[0:rows, :], branch_ref[block : block + rows, :]], axis=0)
    sum_ref[...] += dot_tn(branch, att_ref[...])
    for which in range(2):
        tail = branch_ref[which * block + rows : (which + 1) * block, :].astype(f32)
        slots = []
        for index in range(small_ref.shape[0] // 8):
            first, lane = index // EXTRA_SLOTS * 8, index % EXTRA_SLOTS * DOT_LANES
            slots.append(tail[first : first + 8, lane : lane + rows])
        logit_grad = jnp.concatenate(slots, axis=0)
        real = lax.broadcasted_iota(jnp.int32, logit_grad.shape, 0) % 8 < local_experts
        logit_grad = jnp.where(real, logit_grad, 0.0).astype(bf16)
        small_ref[...] += dot(logit_grad, normed_ref[which * rows : (which + 1) * rows, :])
        gain_sum_ref[...] += tail[8:16, :]

    @pl.when(step == pl.num_programs(0) - 1)
    def _():
        small_ref[7:8, :] = gain_sum_ref[5:6, :] + gain_sum_ref[6:7, :]

        def products(cols):
            own = own_ref[cols, 0 : 2 * LANES]
            out_one = sum_ref[cols, 0:LANES].astype(bf16)
            out_two = sum_ref[cols, LANES:]
            low = lane_of(out_two.shape) < HEAD_DIM
            tail = jnp.where(low, out_two, own_ref[cols, 2 * LANES :].astype(f32)).astype(bf16)
            yield 0, jnp.concatenate([own, out_one, tail], axis=1)

        if fast:
            write_shards(place_ref, outs, products, own_ref.shape[0])
        else:
            outs[0][...] = next(products(slice(0, own_ref.shape[0])))[1]


def out_weights(place, branch, attended, normed, own, padded, local_experts, fast):
    total, width = normed.shape
    rows = total // COLS
    blocks = branch.shape[0] // COLS
    if fast:
        shapes = [(1, 1, 2, width // 4, 2 * LANES)] * 4
    else:
        shapes = [(width, 4 * LANES)]
    return call(
        lambda *refs: out_weights_kernel(*refs, fast=fast, local_experts=local_experts),
        (COLS,),
        1,
        [
            pl.BlockSpec((blocks, width), lambda j, p: (j, 0)),
            pl.BlockSpec((rows, 2 * LANES), lambda j, p: (j, 0)),
            pl.BlockSpec((rows, width), lambda j, p: (j, 0)),
            whole(own.shape),
        ],
        [whole(shape) for shape in shapes] + [whole((padded, width))],
        [struct(shape, bf16) for shape in shapes] + [struct((padded, width), f32)],
        scratch=[pltpu.VMEM((width, 2 * LANES), f32), pltpu.VMEM((8, width), f32)],
        us=0.5,
    )(place, branch, attended, normed, own)


def first_sum_kernel(place_ref, keep_a_ref, got_a_ref, keep_b_ref, got_b_ref, *rest):
    send_a_ref, held_a_ref, send_b_ref, held_b_ref = rest[-4:]
    x_bit, y_bit = place_ref[3], place_ref[4]
    for bit, keep, got, send, held in (
        (y_bit, keep_a_ref, got_a_ref, send_a_ref, held_a_ref),
        (x_bit, keep_b_ref, got_b_ref, send_b_ref, held_b_ref),
    ):
        for kind in range(keep.shape[1]):
            held[0, kind] = (keep[0, kind, bit].astype(f32) + got[0, kind, bit].astype(f32)).astype(bf16)
            send[0, kind] = (keep[0, kind, 1 - bit].astype(f32) + got[0, kind, 1 - bit].astype(f32)).astype(bf16)


def first_sum(place, chunk, first=0, total=None, before=None):
    count, kinds, _, rows, cols = chunk[0].shape
    taken = pl.BlockSpec((1, kinds, 2, rows, cols), lambda e, p: (e, 0, 0, 0, 0))
    given = pl.BlockSpec((1, kinds, rows, cols), lambda e, p: (e + first, 0, 0, 0))
    extra = list(before) if before else []
    return call(
        first_sum_kernel,
        (count,),
        1,
        [taken] * 4 + [pl.BlockSpec(memory_space=pl.ANY)] * len(extra),
        [given] * 4,
        [struct((total or count, kinds, rows, cols), bf16)] * 4,
        us=0.5,
        aliases={5 + i: i for i in range(len(extra))},
    )(place, *chunk, *extra)


def last_sum_kernel(held_a_ref, got_a_ref, held_b_ref, got_b_ref, *rest):
    outs = rest[-3:]
    side = held_a_ref.shape[3]
    for which, out in enumerate(outs):
        out[0, :, :side] = held_a_ref[0, which].astype(f32) + got_a_ref[0, which].astype(f32)
        out[0, :, side:] = held_b_ref[0, which].astype(f32) + got_b_ref[0, which].astype(f32)


def last_sum(held_a, got_a, held_b, got_b, first, total, before):
    count, kinds, rows, cols = held_a.shape
    taken = pl.BlockSpec((1, kinds, rows, cols), lambda e: (e, 0, 0, 0))
    given = pl.BlockSpec((1, rows, 2 * cols), lambda e: (e + first, 0, 0))
    extra = list(before) if before else []
    return call(
        last_sum_kernel,
        (count,),
        0,
        [taken] * 4 + [pl.BlockSpec(memory_space=pl.ANY)] * len(extra),
        [given] * 3,
        [struct((total, rows, 2 * cols), f32)] * 3,
        us=0.5,
        aliases={4 + i: i for i in range(len(extra))},
    )(held_a, got_a, held_b, got_b, *extra)


def last_weights_kernel(held_a_ref, got_a_ref, held_b_ref, got_b_ref, query_ref, key_ref, value_ref, out_ref):
    left = jnp.transpose(held_a_ref[0, 0].astype(f32) + got_a_ref[0, 0].astype(f32))
    right = jnp.transpose(held_b_ref[0, 0].astype(f32) + got_b_ref[0, 0].astype(f32))
    cut = query_ref.shape[0]
    query_ref[...] = left[:cut]
    key_ref[...] = left[cut:]
    out_ref[...] = right[:cut]
    value_ref[...] = right[cut:]


def last_weights(parts, widths):
    rows = parts[0].shape[2]
    shapes = [(width, rows) for width in widths]
    return call(
        last_weights_kernel,
        (1,),
        0,
        [whole(part.shape) for part in parts],
        [whole(shape) for shape in shapes],
        [struct(shape, f32) for shape in shapes],
        us=0.5,
    )(*parts)


SWAP = [(0, 1), (1, 0)]


def after(value, *events):
    return lax.optimization_barrier((value,) + events)[0]


def gather_group(block):
    return lax.all_gather(block, ("row", "col"), axis=0, tiled=True)


def line_pieces(value):
    parts = [value]
    for distance in range(1, COLS):
        parts.insert(0, lax.ppermute(value, "col", [(i, (i + distance) % COLS) for i in range(COLS)]))
    return parts


def in_line_order(parts):
    parts = jnp.stack(parts + parts)
    return lax.dynamic_slice_in_dim(parts, COLS - 1 - lax.axis_index("col"), COLS, axis=0)


def flip(value, axis, bit, size):
    return lax.ppermute(value, axis, [(i, i ^ (1 << bit)) for i in range(size)])


def bits_of(size):
    return size.bit_length() - 1


def own_bit(axis, bit):
    return (lax.axis_index(axis) >> bit) & 1


def joined(mine, got, own):
    return jnp.where(own == 0, jnp.concatenate([mine, got]), jnp.concatenate([got, mine]))


def cube_step(value, axis, bit, size):
    return joined(value, flip(value, axis, bit, size), own_bit(axis, bit))


def lines_first(value):
    return jnp.transpose(value, (1, 0, 2, 3)).reshape(value.shape[1], value.shape[0] * value.shape[2], value.shape[3])


def cube_gather(value, axis, size):
    value = value[None]
    for bit in range(bits_of(size)):
        value = cube_step(value, axis, bit, size)
    return value


def sum_dp(value, sizes):
    for bit in range(bits_of(sizes["dp"])):
        value = value + flip(value, "dp", bit, sizes["dp"])
    return value


def reduce_over_dp(value, size):
    count = bits_of(size)
    value = value.reshape(value.shape[:1] + (2,) * count + value.shape[2:])
    current = value
    for bit in range(count - 1, -1, -1):
        own = own_bit("dp", bit)
        keep = lax.dynamic_index_in_dim(current, own, 1, keepdims=False)
        send = lax.dynamic_index_in_dim(current, 1 - own, 1, keepdims=False).astype(bf16)
        current = keep.astype(f32) + flip(send, "dp", bit, size).astype(f32)
    return current


def start_move(run, size):
    return flip(run[0], "dp", 0, size), flip(run[2], "dp", 1, size)


def second_move(sums, size):
    send_a, held_a, send_b, held_b = sums
    return held_a, flip(send_a, "dp", 1, size), held_b, flip(send_b, "dp", 0, size)


def layer(sizes):
    n_dp, n_row, n_col = sizes["dp"], sizes["row"], sizes["col"]
    members = n_row * n_col
    fast = n_dp == 4
    assert n_row == 2 and n_col == COLS and n_dp & (n_dp - 1) == 0

    def local(
        tokens, cotangent, routes, lengths, gain_attn, w_query, w_key, w_value, w_out,
        gain_moe, w_router, w_gate, w_up, w_down,
    ):
        rows, width = tokens.shape
        group = rows * members
        local_experts = w_gate.shape[0]
        row, col, dp = lax.axis_index("row"), lax.axis_index("col"), lax.axis_index("dp")
        place = jnp.stack([row, col, row * n_col + col, dp & 1, (dp >> 1) & 1]).astype(jnp.int32)
        gain_one = gain_attn.astype(f32)[None]
        gain_two = gain_moe.astype(f32)[None]

        tok_all = gather_group(tokens)
        w_in = jnp.concatenate([w_query.T, w_key.T, w_value.T], axis=0)
        out_share, in_share = rows // n_dp, w_in.shape[0] // n_dp
        shares = jnp.concatenate(
            [
                lax.dynamic_slice(w_out.T, (dp * out_share, 0), (out_share, width)),
                lax.dynamic_slice(w_in, (dp * in_share, 0), (in_share, width)),
                jnp.pad(routes.T.astype(bf16).reshape(1, TOP * rows), ((0, 7), (0, width - TOP * rows))),
            ],
            axis=0,
        )
        w_stack = jnp.concatenate([w_query.T, w_key.T, w_value.T, w_value.T], axis=0)
        w_natural = jnp.concatenate([w_query, w_key, w_value, w_value], axis=1)

        ends = jnp.cumsum(lengths[0])
        starts = ends - lengths[0]
        position = jnp.arange(group, dtype=jnp.int32)
        segment = jnp.sum((position[:, None] >= ends[None, :]).astype(jnp.int32), axis=1)
        member = segment[:, None] == jnp.arange(starts.shape[0], dtype=jnp.int32)[None, :]
        start = jnp.sum(jnp.where(member, starts[None, :], 0), axis=1).astype(jnp.int32)
        frequency = rope_base ** (-2.0 * jnp.arange(HEAD_DIM // 2, dtype=f32) / HEAD_DIM)
        angle = (position - start).astype(f32)[:, None] * frequency[None, :]
        cosine = jnp.tile(jnp.cos(angle), (1, 4))
        sine = jnp.tile(jnp.sin(angle), (1, 4))

        w_router_rows = w_router.T.reshape(members, local_experts, width)
        w_router_rows = jnp.pad(w_router_rows, ((0, 0), (0, 8 - local_experts), (0, 0)))
        w_router_rows = w_router_rows.reshape(members * 8, width)
        start_row = jnp.broadcast_to(start[None, :], (8, group))
        start = start[:, None]
        gain_column = gain_attn.astype(f32)[:, None]
        ready = (place, gain_one, gain_two, w_stack, w_natural, cosine, sine, w_router_rows, start, start_row, gain_column)
        shares, place, gain_one, gain_two, w_stack, w_natural, cosine, sine, w_router_rows, start, start_row, gain_column = (
            lax.optimization_barrier((shares,) + ready)
        )
        shares = line_pieces(after(shares, tok_all, cosine))

        query, key, value, normed_one = project(tok_all, gain_one, w_stack, cosine, sine)
        packed, attended, totals = attend(query, key, value, start)
        att_flat = gather_group(packed)
        att_all = att_flat.reshape((n_row, n_col) + packed.shape)
        shares = in_line_order(after(shares, packed))
        route_rows = shares[:, out_share + in_share]
        w_out_mine, in_part = shares[None, :, :out_share], shares[None, :, out_share : out_share + in_share]
        for bit in range(bits_of(n_dp)):
            w_out_mine = cube_step(w_out_mine, "dp", bit, n_dp)
        in_part = cube_step(in_part, "dp", 0, n_dp)
        w_out_mine = lines_first(w_out_mine)
        w_out_other = lax.ppermute(after(w_out_mine, in_part), "row", SWAP)
        route_rows = cube_gather(route_rows, "row", n_row)[:, :, : TOP * rows].reshape(members, TOP, rows)
        cot_all = gather_group(after(cotangent, w_out_other))
        x, slot_gate, rank, gate, normed_two, middle, gates = middle_and_dispatch(
            place, att_all, w_out_mine, w_out_other, tok_all, route_rows, gain_two, w_router_rows, local_experts
        )
        slots = members * CAPACITY
        x = x.reshape(local_experts, slots, width)
        slot_gate = slot_gate.reshape(local_experts, slots, LANES)
        rank, gate = rank.reshape(members, 8, rows), gate.reshape(members, 8, rows)
        forth, active, factor, silu = run_experts(x, slot_gate, w_gate, w_up, w_down)
        for bit in range(1, bits_of(n_dp) - 1):
            in_part = cube_step(in_part, "dp", bit, n_dp)
        last_bit = bits_of(n_dp) - 1
        in_got = after(flip(in_part, "dp", last_bit, n_dp), forth)
        forth_other = combine(place, after(rank, in_got), [forth])
        arrived = lax.ppermute(forth_other, "row", SWAP)
        g = grad_dispatch(after(rank, forth_other), gate, cot_all, local_experts)
        g = g.reshape(local_experts, slots, width)
        cuts = [0, 1, 3, local_experts]

        def backward(which, x):
            first, last = cuts[which], cuts[which + 1]
            return run_experts_back(place, x, g, active, factor, silu, w_gate, w_up, w_down, first, last - first, fast)

        runs = [backward(0, x)]
        forth_mine = combine(place, rank, [forth], arrived=after(arrived, runs[0][1]))
        forth_sums = lax.all_to_all(forth_mine, "col", 0, 0, tiled=True)
        runs.append(backward(1, after(x, forth_mine)))
        runs.append(backward(2, after(x, runs[1][1])))
        moved = [start_move(run[2:], n_dp) for run in runs] if fast else []
        back_parts, dot_parts = [run[0] for run in runs], [run[1] for run in runs]
        back_other = combine(place, after(rank, *moved[0]) if fast else rank, back_parts, dot_parts)
        arrived = lax.ppermute(back_other, "row", SWAP)
        back_mine = combine(place, rank, back_parts, dot_parts, arrived)
        back_mine = after(back_mine, forth_sums)
        back_sums = lax.all_to_all(back_mine, "col", 0, 0, tiled=True)

        if fast:
            w_in_parts = [in_part, in_got]
        else:
            own = own_bit("dp", last_bit)
            w_in_rows = lines_first(joined(in_part, in_got, own))[None]
            half = w_in_rows.shape[2] // 2
            upper, lower = w_in_rows[:, :, :half], w_in_rows[:, :, half:]
            w_in_parts = [jnp.where(place[4] == 0, upper, lower), jnp.where(place[4] == 0, lower, upper)]
        if fast:

            def chunk_of(which, *events):
                keep_a, keep_b = after((runs[which][3], runs[which][5]), *events)
                return keep_a, moved[which][0], keep_b, moved[which][1]

            sums = first_sum(place, chunk_of(0, back_mine), cuts[0], cuts[2])
            gate_middle = (sums[1],) + moved[1]
        else:
            gate_middle = ()
        w_in_parts += [lax.ppermute(after(part, back_mine), "row", SWAP) for part in w_in_parts]

        middle_grad, branch_grad, attended_grad = middle_back(
            place, back_sums, gates, middle, cotangent, after(gain_two, *w_in_parts[2:], *gate_middle),
            w_router_rows, w_out_mine, w_out_other,
        )
        if fast:
            sums = first_sum(place, chunk_of(1, branch_grad), cuts[1], cuts[2], sums)
            started = [second_move(sums, n_dp)]
        attended_grad = lax.all_to_all(attended_grad, ("row", "col"), 0, 0, tiled=True)
        if fast:
            attended_grad = after(attended_grad, sums[1])
        branch_all = gather_group(branch_grad)

        attended_grad = attended_grad.reshape(group, 2 * LANES)
        projected_grad, own_grads = attend_back(
            query, key, value, attended_grad, totals, start_row, cosine, sine, normed_one, w_natural, gain_column
        )
        mixed = (middle + jnp.sum(after(forth_sums, own_grads).astype(f32), axis=0)).astype(bf16)
        projected_all = lax.all_to_all(projected_grad, ("row", "col"), 0, 0, tiled=True)
        *w_parts, small = out_weights(
            place, branch_all, attended, normed_two.reshape(group, width), own_grads,
            members * 8, local_experts, fast,
        )
        arriving = ()
        if fast:
            w_moved = start_move(w_parts, n_dp)
            late = first_sum(place, chunk_of(2, small, started[0][1], started[0][3]))
            started.append(second_move(late, n_dp))
            w_first = first_sum(place, (w_parts[1], w_moved[0], w_parts[3], w_moved[1]))
            w_sums = second_move(w_first, n_dp)
            arriving = (w_first[1], started[1][0])
        else:
            cut = w_parts[0].reshape(1, n_dp, width // n_dp, w_parts[0].shape[1])
            w_sum = reduce_over_dp(cut, n_dp)[0]


        used = small.reshape(members, 8, width)[:, :local_experts].reshape(members * local_experts, width)
        both = sum_dp(jnp.concatenate([used, small[7:8]], axis=0), sizes)
        w_router_grad = both[: members * local_experts].T
        gain_moe_grad = both[members * local_experts]

        tokens_grad, share = input_grad(
            place, projected_all, w_in_parts, tokens, middle_grad, after(gain_one, w_parts[0], *arriving)
        )
        share = (share[0:4] + share[4:8]).reshape(8, width // 8)
        if fast:
            held_a, got_a, held_b, got_b = started[0]
            held_a, held_b = after((held_a, held_b), tokens_grad)
            expert_grads = last_sum(held_a, got_a, held_b, got_b, 0, local_experts, None)
            share = share + after(flip(share, "dp", 0, n_dp), expert_grads[0])
            held_a, got_a, held_b, got_b = started[1]
            held_a, held_b = after((held_a, held_b), share, w_sums[1], w_sums[3])
            expert_grads = last_sum(held_a, got_a, held_b, got_b, cuts[2], local_experts, expert_grads)
            gain_attn_grad = share + after(flip(share, "dp", 1, n_dp), expert_grads[0])
            gain_attn_grad = gain_attn_grad.reshape(width)
        else:
            gain_attn_grad = sum_dp(share, sizes).reshape(width)

        local_q, local_k = w_query.shape[1], w_key.shape[1]
        if fast:
            w_query_grad, w_key_grad, w_value_grad, w_out_grad = [
                item.T for item in last_weights(w_sums, (local_q, local_k, local_k, local_q))
            ]
        else:
            expert_grads = []
            for which in range(3):
                parts = [run[2 + which] for run in runs]
                parts = [part.reshape(part.shape[0], n_dp, width // n_dp, part.shape[2]) for part in parts]
                expert_grads.append(jnp.concatenate([reduce_over_dp(part, n_dp) for part in parts], axis=0))
            cut = local_q + local_k
            w_query_grad, w_key_grad = w_sum[:, :local_q], w_sum[:, local_q:cut]
            w_out_grad, w_value_grad = w_sum[:, cut : cut + local_q], w_sum[:, cut + local_q :]
        w_gate_grad, w_up_grad, w_down_grad = expert_grads
        return (
            mixed, tokens_grad, gain_attn_grad, w_query_grad, w_key_grad, w_value_grad, w_out_grad,
            gain_moe_grad, w_router_grad, w_gate_grad, w_up_grad, w_down_grad,
        )

    return local


def solution(mesh):
    return jax.shard_map(
        layer(dict(mesh.shape)),
        mesh=mesh,
        in_specs=(
            P(("dp", "row", "col"), None),
            P(("dp", "row", "col"), None),
            P(("dp", "row", "col"), None),
            P("dp", None),
            P(),
            P(None, ("row", "col")),
            P(None, ("row", "col")),
            P(None, ("row", "col")),
            P(None, ("row", "col")),
            P(),
            P(),
            P(("row", "col"), None, None),
            P(("row", "col"), None, None),
            P(("row", "col"), None, None),
        ),
        out_specs=(
            P(("dp", "row", "col"), None),
            P(("dp", "row", "col"), None),
            P(),
            P("dp", ("row", "col")),
            P("dp", ("row", "col")),
            P("dp", ("row", "col")),
            P("dp", ("row", "col")),
            P(),
            P(),
            P(("row", "col"), "dp", None),
            P(("row", "col"), "dp", None),
            P(("row", "col"), "dp", None),
        ),
        check_vma=False,
    )
```

```python
import math

import jax
import jax.numpy as jnp
import numpy as np
from jax import lax
from jax.experimental import pallas as pl
from jax.experimental.pallas import tpu as pltpu
from jax.sharding import PartitionSpec as P

HEAD_DIM = 64
EXPERTS = 40
TOP = 8
CAPACITY = 64
COLS = 4
LANES = 128
QUERY_BLOCK = 256
DOT_ROWS = 16

epsilon = 1e-06
rope_base = 10000.0
masked_score = -1e30
f32 = jnp.float32
bf16 = jnp.bfloat16
VMEM_LIMIT = 56 * 1024 * 1024

NT = (((1,), (1,)), ((), ()))
TN = (((0,), (0,)), ((), ()))


def dot(a, b):
    return jnp.dot(a, b, preferred_element_type=f32)


def dot_nt(a, b):
    return lax.dot_general(a, b, NT, preferred_element_type=f32)


def dot_tn(a, b):
    return lax.dot_general(a, b, TN, preferred_element_type=f32)


def lane_of(shape):
    return lax.broadcasted_iota(jnp.int32, shape, len(shape) - 1)


def call(
    kernel, grid, prefetch, in_specs, out_specs, out_shape, scratch=(), us=1.0, aliases=None
):
    return pl.pallas_call(
        kernel,
        grid_spec=pltpu.PrefetchScalarGridSpec(
            num_scalar_prefetch=prefetch,
            grid=grid,
            in_specs=in_specs,
            out_specs=out_specs,
            scratch_shapes=list(scratch),
        ),
        out_shape=out_shape,
        input_output_aliases=aliases or {},
        compiler_params=pltpu.CompilerParams(
            vmem_limit_bytes=VMEM_LIMIT, dimension_semantics=("arbitrary",) * len(grid)
        ),
        cost_estimate=pl.CostEstimate(
            flops=int(us * 1.1e9), bytes_accessed=int(us * 3.6e6), transcendentals=0
        ),
    )


def whole(shape):
    zeros = (0,) * len(shape)
    return pl.BlockSpec(shape, lambda *_: zeros)


def struct(shape, dtype):
    return jax.ShapeDtypeStruct(shape, dtype)


def turn_within_heads(values, sign):
    lane = lane_of(values.shape) % HEAD_DIM
    ahead = pltpu.roll(values, LANES - HEAD_DIM // 2, 1)
    behind = pltpu.roll(values, HEAD_DIM // 2, 1)
    return jnp.where(lane < HEAD_DIM // 2, -sign * ahead, sign * behind)


def project_kernel(
    tok_ref, gain_ref, w_ref, cos_ref, sin_ref, query_ref, key_ref, value_ref, normed_ref
):
    resid = tok_ref[...].astype(f32)
    inverse = lax.rsqrt(jnp.mean(resid * resid, axis=1, keepdims=True) + epsilon)
    normed = (resid * inverse * gain_ref[...]).astype(bf16)
    normed_ref[...] = normed
    raw = dot_nt(normed, w_ref[...])
    cosine, sine = cos_ref[...], sin_ref[...]

    def rot(values):
        return (values * cosine + turn_within_heads(values, 1.0) * sine).astype(bf16).astype(f32)

    first = rot(raw[:, :LANES])
    second = rot(raw[:, LANES : 2 * LANES])
    low = lane_of(first.shape) < HEAD_DIM
    scale = 1.0 / math.sqrt(HEAD_DIM)
    query_ref[0] = jnp.where(low, first * scale, 0.0).astype(bf16)
    query_ref[1] = jnp.where(low, 0.0, first * scale).astype(bf16)
    query_ref[2] = jnp.where(low, second * scale, 0.0).astype(bf16)
    key_ref[...] = jnp.where(low, pltpu.roll(second, HEAD_DIM, 1), second).astype(bf16)
    value_ref[...] = raw[:, 2 * LANES :].astype(bf16)


def project(tokens, gain, w_stack, cosine, sine):
    total, width = tokens.shape
    rows = 512
    lanes = pl.BlockSpec((rows, LANES), lambda j: (j, 0))
    wide = pl.BlockSpec((rows, width), lambda j: (j, 0))
    return call(
        project_kernel,
        (total // rows,),
        0,
        [wide, whole((1, width)), whole(w_stack.shape), lanes, lanes],
        [pl.BlockSpec((3, rows, LANES), lambda j: (0, j, 0)), lanes, lanes, wide],
        [
            struct((3, total, LANES), bf16),
            struct((total, LANES), bf16),
            struct((total, LANES), bf16),
            struct((total, width), bf16),
        ],
        us=0.5,
    )(tokens, gain, w_stack, cosine, sine)


def attend_kernel(query_ref, key_ref, value_ref, start_ref, packed_ref, plain_ref, total_ref, out_ref):
    blocks = query_ref.shape[1] // QUERY_BLOCK
    block = pl.program_id(0)
    for index in range(blocks):

        @pl.when(block == index)
        def _(index=index):
            rows = pl.ds(index * QUERY_BLOCK, QUERY_BLOCK)
            span = (index + 1) * QUERY_BLOCK
            row = index * QUERY_BLOCK + lax.broadcasted_iota(jnp.int32, (QUERY_BLOCK, span), 0)
            column = lane_of((QUERY_BLOCK, span))
            allowed = (column <= row) & (column >= start_ref[rows, :])

            def head(number, carry):
                scores = dot_nt(query_ref[number, rows, :], key_ref[0:span, :])
                scores = jnp.where(allowed, scores, masked_score)
                peak = jnp.max(scores, axis=1, keepdims=True)
                weights = jnp.exp(scores - peak)
                summed = jnp.sum(weights, axis=1, keepdims=True)
                probs = (weights * (1.0 / summed)).astype(bf16)
                out_ref[number] = dot(probs, value_ref[0:span, :])
                total = jnp.broadcast_to(peak + jnp.log(summed), (QUERY_BLOCK, LANES))
                total_ref[number, :, rows] = jnp.transpose(total)[0:8, :]
                return carry

            for number in range(3):
                head(number, 0)
            low = lane_of((QUERY_BLOCK, LANES)) < HEAD_DIM
            one, two, three = out_ref[0], out_ref[1], out_ref[2]
            pair = jnp.where(low, one, two).astype(bf16)
            plain_ref[rows, 0:LANES] = pair
            plain_ref[rows, LANES : 2 * LANES] = jnp.where(low, three, 0.0).astype(bf16)
            if index < blocks // 2:
                packed_ref[rows, 0:LANES] = pair
                packed_ref[rows, LANES : 2 * LANES] = three.astype(bf16)
            else:
                back = pl.ds((index - blocks // 2) * QUERY_BLOCK, QUERY_BLOCK)
                before = packed_ref[back, LANES : 2 * LANES].astype(f32)
                packed_ref[back, LANES : 2 * LANES] = jnp.where(low, before, one).astype(bf16)
                packed_ref[back, 2 * LANES : 3 * LANES] = jnp.where(low, two, three).astype(bf16)


def attend(query, key, value, start):
    total = key.shape[0]
    return call(
        attend_kernel,
        (total // QUERY_BLOCK,),
        0,
        [whole(query.shape), whole(key.shape), whole(value.shape), whole(start.shape)],
        [whole((total // 2, 3 * LANES)), whole((total, 2 * LANES)), whole((3, 8, total))],
        [
            struct((total // 2, 3 * LANES), bf16),
            struct((total, 2 * LANES), bf16),
            struct((3, 8, total), f32),
        ],
        scratch=[pltpu.VMEM((3, QUERY_BLOCK, LANES), f32)],
        us=0.5,
    )(query, key, value, start)


def attend_back_kernel(
    query_ref, key_ref, value_ref, grad_ref, total_ref, start_ref, cos_ref, sin_ref, normed_ref, w_ref, gain_ref,
    blocks_ref, own_ref, out_ref, query_grad_ref, key_grad_ref, value_grad_ref, own_sum_ref
):
    blocks = query_ref.shape[1] // QUERY_BLOCK
    block = pl.program_id(0)
    scale = 1.0 / math.sqrt(HEAD_DIM)

    @pl.when(block == 0)
    def _():
        key_grad_ref[...] = jnp.zeros_like(key_grad_ref)
        value_grad_ref[...] = jnp.zeros_like(value_grad_ref)

    def back(values, cosine, sine):
        return values * cosine + turn_within_heads(values * sine, -1.0)

    for index in range(blocks):

        @pl.when(block == index)
        def _(index=index):
            rows = pl.ds(index * QUERY_BLOCK, QUERY_BLOCK)
            span = (index + 1) * QUERY_BLOCK
            row = index * QUERY_BLOCK + lane_of((span, QUERY_BLOCK))
            column = lax.broadcasted_iota(jnp.int32, (span, QUERY_BLOCK), 0)
            allowed = (column <= row) & (column >= start_ref[0:1, rows])
            low = lane_of((QUERY_BLOCK, LANES)) < HEAD_DIM

            def head(number, carry):
                query = query_ref[number, rows, :]
                tile = number // 2 * LANES
                upstream = grad_ref[rows, tile : tile + LANES].astype(f32)
                keep = low == (number != 1)
                upstream = jnp.where(keep, upstream, 0.0).astype(bf16)
                scores = dot_nt(key_ref[0:span, :], query)
                probs = jnp.exp(scores - total_ref[number, 0:1, rows])
                probs = jnp.where(allowed, probs, 0.0)
                prob_grad = dot_nt(value_ref[0:span, :], upstream)
                row_dot = jnp.sum(probs * prob_grad, axis=0, keepdims=True)
                score_grad = (probs * (prob_grad - row_dot)).astype(bf16)
                key_grad_ref[0:span, :] += dot(score_grad, query)
                value_grad_ref[0:span, :] += dot(probs.astype(bf16), upstream)
                query_grad_ref[number] = dot_tn(score_grad, key_ref[0:span, :]) * scale
                return carry

            for number in range(3):
                head(number, 0)
            cosine, sine = cos_ref[rows, :], sin_ref[rows, :]
            pair = jnp.where(low, query_grad_ref[0], query_grad_ref[1])
            out_ref[rows, 0:LANES] = back(pair, cosine, sine).astype(bf16)
            out_ref[rows, LANES : 2 * LANES] = back(query_grad_ref[2], cosine, sine).astype(bf16)

    @pl.when(block == blocks - 1)
    def _():
        low = lane_of(key_grad_ref.shape) < HEAD_DIM
        key_grad = key_grad_ref[...]
        key_grad = key_grad + pltpu.roll(key_grad, HEAD_DIM, 1)
        key_grad = back(key_grad, cos_ref[...], sin_ref[...])
        before = out_ref[:, LANES : 2 * LANES].astype(f32)
        out_ref[:, LANES : 2 * LANES] = jnp.where(low, before, key_grad).astype(bf16)
        value_grad = value_grad_ref[...]
        value_grad = value_grad + pltpu.roll(value_grad, HEAD_DIM, 1)
        out_ref[:, 2 * LANES : 3 * LANES] = jnp.where(low, 0.0, value_grad).astype(bf16)
        chunk = 512
        own_sum_ref[...] = jnp.zeros_like(own_sum_ref)

        def add(index, carry):
            part = pl.ds(pl.multiple_of(index * chunk, chunk), chunk)
            own_sum_ref[...] += dot_tn(normed_ref[part, :], out_ref[part, :])
            return carry

        lax.fori_loop(0, out_ref.shape[0] // chunk, add, 0)
        own = own_sum_ref[...]
        own_ref[...] = own.astype(bf16)
        share = jnp.sum(own * w_ref[...].astype(f32), axis=1, keepdims=True) / gain_ref[...]
        share = jnp.transpose(jnp.broadcast_to(share, (share.shape[0], LANES)))[0:8, :]
        width = blocks_ref.shape[2]
        row = lax.broadcasted_iota(jnp.int32, (8, width), 0)
        terms = jnp.zeros((8, width), f32)
        for index in range(share.shape[1] // width):
            piece = share[:, index * width : (index + 1) * width]
            upper = piece.astype(bf16).astype(f32)
            terms = jnp.where(row == index, upper, jnp.where(row == index + 4, piece - upper, terms))
        terms = jnp.concatenate([terms, jnp.zeros((8, width), f32)], axis=0).astype(bf16)
        rows = blocks_ref.shape[1] - DOT_ROWS
        for index in range(blocks_ref.shape[0]):
            blocks_ref[index, 0:rows, :] = out_ref[index * rows : (index + 1) * rows, :]
            blocks_ref[index, rows:, :] = terms


def attend_back(query, key, value, grad, totals, start, cosine, sine, normed, w_natural, gain):
    total = key.shape[0]
    members = 2 * COLS
    rows = total // members + DOT_ROWS
    args = (query, key, value, grad, totals, start, cosine, sine, normed, w_natural, gain)
    return call(
        attend_back_kernel,
        (total // QUERY_BLOCK,),
        0,
        [whole(item.shape) for item in args],
        [whole((members, rows, 3 * LANES)), whole(w_natural.shape)],
        [struct((members, rows, 3 * LANES), bf16), struct(w_natural.shape, bf16)],
        scratch=[
            pltpu.VMEM((total, 3 * LANES), bf16),
            pltpu.VMEM((3, QUERY_BLOCK, LANES), f32),
            pltpu.VMEM((total, LANES), f32),
            pltpu.VMEM((total, LANES), f32),
            pltpu.VMEM(w_natural.shape, f32),
        ],
        us=0.5,
    )(*args)


def branch_operand(refs):
    rows = refs.shape[2]
    low = lane_of((rows, LANES)) < HEAD_DIM
    pairs, thirds = [], []
    for member in range(refs.shape[1]):
        one = refs[0, member, :, 0:LANES]
        mid = refs[0, member, :, LANES : 2 * LANES].astype(f32)
        end = refs[0, member, :, 2 * LANES : 3 * LANES].astype(f32)
        mid_turned = pltpu.roll(mid, HEAD_DIM, 1)
        end_turned = pltpu.roll(end, HEAD_DIM, 1)
        late = jnp.where(low, mid_turned, end_turned).astype(bf16)
        pairs.append(jnp.concatenate([one, late], axis=0))
        thirds.append((mid, end_turned))
    for member in range(0, refs.shape[1], 2):
        tops = []
        for which in range(2):
            left, right = thirds[member][which], thirds[member + 1][which]
            tops.append(jnp.where(low, left, pltpu.roll(right, HEAD_DIM, 1)).astype(bf16))
        pairs.append(jnp.concatenate(tops, axis=0))
    return jnp.concatenate(pairs, axis=1)


def branch_weights(ref):
    right = [ref[source, 0:LANES] for source in range(ref.shape[0])]
    return jnp.concatenate(right + [ref[source, LANES:] for source in range(ref.shape[0])], axis=0)


def hits_of(rank, local_experts):
    place = lax.broadcasted_iota(jnp.int32, (CAPACITY, rank.shape[1]), 0).astype(f32)
    return [place == rank[j : j + 1, :] for j in range(local_experts)]


def chosen_of(hits):
    return jnp.concatenate([jnp.where(hit, 1.0, 0.0).astype(bf16) for hit in hits], axis=0)


def middle_kernel(
    place_ref, att_mine_ref, att_other_ref, w_mine_ref, w_other_ref, tok_a_ref, tok_b_ref, routes_a_ref, routes_b_ref,
    gain_ref, w_router_ref, after_ref,
    x_ref, slot_gate_ref, rank_ref, gate_ref, normed_ref, middle_ref, gates_own_ref, gates_ref, ranks_ref
):
    step = pl.program_id(0)
    member = place_ref[2]
    cols = pl.num_programs(0)
    rows = tok_a_ref.shape[0]
    local_experts = x_ref.shape[0]
    branch = dot(branch_operand(att_mine_ref), branch_weights(w_mine_ref))
    branch = branch + dot(branch_operand(att_other_ref), branch_weights(w_other_ref))
    for half in range(2):
        tok_ref, routes_ref = ((tok_a_ref, routes_a_ref), (tok_b_ref, routes_b_ref))[half]
        middle = tok_ref[...].astype(f32) + branch[half * rows : (half + 1) * rows]
        inverse = lax.rsqrt(jnp.mean(middle * middle, axis=1, keepdims=True) + epsilon)
        normed = (middle * inverse * gain_ref[...]).astype(bf16)
        normed_ref[half, 0] = normed
        logits = dot_nt(w_router_ref[...], normed)
        padded = logits.shape[0]
        slot = lax.broadcasted_iota(jnp.int32, (padded, rows), 0)
        expert = (slot // 8) * local_experts + slot % 8
        expert = jnp.where(slot % 8 < local_experts, expert, -1).astype(f32)
        routes = routes_ref[0].astype(f32)
        named = expert == routes[0:1, 0:rows]
        for k in range(1, TOP):
            named = named | (expert == routes[k : k + 1, 0:rows])
        peak = jnp.max(jnp.where(named, logits, masked_score), axis=0, keepdims=True)
        weights = jnp.where(named, jnp.exp(logits - peak), 0.0)
        gates = weights / jnp.sum(weights, axis=0, keepdims=True)
        gates_ref[...] = gates
        ranks_ref[...] = jnp.where(named, dot(named.astype(f32).astype(bf16), after_ref[...]), -1.0)
        here = pl.ds(pl.multiple_of(member * 8, 8), 8)
        gate, rank = gates_ref[here, :], ranks_ref[here, :]
        rank_ref[half, 0] = rank
        gate_ref[half, 0] = gate
        hits = hits_of(rank, local_experts)
        slot_gate = jnp.concatenate(
            [jnp.sum(jnp.where(hit, gate[j : j + 1, :], 0.0), axis=1, keepdims=True) for j, hit in enumerate(hits)],
            axis=0,
        )
        chosen = chosen_of(hits)
        picked = dot(chosen, normed).astype(bf16)
        spread = jnp.broadcast_to(slot_gate, (slot_gate.shape[0], LANES))
        for j in range(local_experts):
            part = slice(j * CAPACITY, (j + 1) * CAPACITY)
            x_ref[j, half, 0] = picked[part]
            slot_gate_ref[j, half, 0] = spread[part]

        @pl.when(member == half * cols + step)
        def _(middle=middle, gates=gates):
            middle_ref[...] = middle
            gates_own_ref[...] = gates


def middle_and_dispatch(place, att, w_mine, w_other, tokens, routes, gain, w_router, local_experts):
    width = tokens.shape[1]
    half = COLS
    rows = tokens.shape[0] // (2 * half)
    padded = w_router.shape[0]
    after = jnp.asarray(np.triu(np.ones((rows, rows), np.float32), 1), bf16)
    slot_shape = (local_experts, 2, half, CAPACITY)
    early = pl.BlockSpec((rows, width), lambda i, p: (i, 0))
    late = pl.BlockSpec((rows, width), lambda i, p: (i + half, 0))
    routes_shape = (1,) + routes.shape[1:]
    return call(
        middle_kernel,
        (half,),
        1,
        [
            pl.BlockSpec((1, half, rows, 3 * LANES), lambda i, p: (p[0], 0, i, 0)),
            pl.BlockSpec((1, half, rows, 3 * LANES), lambda i, p: (1 - p[0], 0, i, 0)),
            whole(w_mine.shape),
            whole(w_other.shape),
            early,
            late,
            pl.BlockSpec(routes_shape, lambda i, p: (i, 0, 0)),
            pl.BlockSpec(routes_shape, lambda i, p: (i + half, 0, 0)),
            whole((1, width)),
            whole(w_router.shape),
            whole((rows, rows)),
        ],
        [
            pl.BlockSpec((local_experts, 2, 1, CAPACITY, width), lambda i, p: (0, 0, i, 0, 0)),
            pl.BlockSpec((local_experts, 2, 1, CAPACITY, LANES), lambda i, p: (0, 0, i, 0, 0)),
            pl.BlockSpec((2, 1, 8, rows), lambda i, p: (0, i, 0, 0)),
            pl.BlockSpec((2, 1, 8, rows), lambda i, p: (0, i, 0, 0)),
            pl.BlockSpec((2, 1, rows, width), lambda i, p: (0, i, 0, 0)),
            whole((rows, width)),
            whole((padded, rows)),
        ],
        [
            struct(slot_shape + (width,), bf16),
            struct(slot_shape + (LANES,), f32),
            struct((2, half, 8, rows), f32),
            struct((2, half, 8, rows), f32),
            struct((2, half, rows, width), bf16),
            struct((rows, width), f32),
            struct((padded, rows), f32),
        ],
        scratch=[pltpu.VMEM((padded, rows), f32), pltpu.VMEM((padded, rows), f32)],
        us=0.5,
    )(place, att, att, w_mine, w_other, tokens, tokens, routes, routes, gain, w_router, after)


def grad_dispatch_kernel(rank_ref, gate_ref, cot_ref, g_ref):
    local_experts = g_ref.shape[0]
    rows = cot_ref.shape[0] // 2
    for half in range(2):
        hits = hits_of(rank_ref[half], local_experts)
        gate = gate_ref[half]
        slot_gate = jnp.concatenate(
            [jnp.sum(jnp.where(hit, gate[j : j + 1, :], 0.0), axis=1, keepdims=True) for j, hit in enumerate(hits)],
            axis=0,
        )
        grads = (dot(chosen_of(hits), cot_ref[half * rows : (half + 1) * rows, :]) * slot_gate).astype(bf16)
        for j in range(local_experts):
            g_ref[j, half] = grads[j * CAPACITY : (j + 1) * CAPACITY]


def grad_dispatch(rank, gate, cotangents, local_experts):
    members, _, rows = rank.shape
    width = cotangents.shape[1]
    small = pl.BlockSpec((2, 8, rows), lambda j: (j, 0, 0))
    return call(
        grad_dispatch_kernel,
        (members // 2,),
        0,
        [small, small, pl.BlockSpec((2 * rows, width), lambda j: (j, 0))],
        pl.BlockSpec((local_experts, 2, CAPACITY, width), lambda j: (0, j, 0, 0)),
        struct((local_experts, members, CAPACITY, width), bf16),
        us=0.5,
    )(rank, gate, cotangents)


def expert_kernel(
    x_ref, gate_ref, w_gate_ref, w_up_ref, w_down_ref, forth_ref, active_ref, factor_ref, silu_ref
):
    gate_pre = dot(x_ref[0], w_gate_ref[0])
    up_pre = dot(x_ref[0], w_up_ref[0])
    sig = 1.0 / (1.0 + jnp.exp(-gate_pre))
    silu = gate_pre * sig
    silu_ref[0] = silu
    factor_ref[0] = up_pre * sig * (1.0 + gate_pre * (1.0 - sig))
    active_ref[0] = (silu * up_pre).astype(bf16)
    produced = dot_nt(active_ref[0], w_down_ref[0]).astype(bf16).astype(f32)
    forth_ref[0] = (produced * gate_ref[0, :, 0:1]).astype(bf16)


def run_experts(x, slot_gate, w_gate, w_up, w_down):
    count, slots, width = x.shape
    hidden = w_gate.shape[2]

    def per_expert(*shape):
        return pl.BlockSpec((1,) + shape, lambda e: (e, 0, 0))

    return call(
        expert_kernel,
        (count,),
        0,
        [per_expert(slots, width), per_expert(slots, LANES)] + [per_expert(width, hidden)] * 3,
        [per_expert(slots, width)] + [per_expert(slots, hidden)] * 3,
        [
            struct((count, slots, width), bf16),
            struct((count, slots, hidden), bf16),
            struct((count, slots, hidden), f32),
            struct((count, slots, hidden), f32),
        ],
        us=0.5,
    )(x, slot_gate, w_gate, w_up, w_down)


def expert_back_kernel(place_ref, *refs, fast):
    x_ref, g_ref, active_ref, factor_ref, silu_ref = refs[:5]
    w_gate_ref, w_up_ref, w_down_ref, back_ref, dots_ref = refs[5:10]
    grads, (gate_low_ref, up_low_ref) = refs[10:-2], refs[-2:]
    slots, width = g_ref.shape[1], g_ref.shape[2]
    chunk = 256
    active_grad = dot(g_ref[0], w_down_ref[0])
    gate_low_ref[...] = (active_grad * factor_ref[0]).astype(bf16)
    up_low_ref[...] = (active_grad * silu_ref[0]).astype(bf16)
    dots = jnp.sum(active_ref[0].astype(f32) * active_grad, axis=1, keepdims=True)
    dots_ref[0] = jnp.broadcast_to(dots, (slots, LANES))
    back_ref[0] = (dot_nt(gate_low_ref[...], w_gate_ref[0]) + dot_nt(up_low_ref[...], w_up_ref[0])).astype(bf16)

    def products(cols):
        x = x_ref[0, :, cols]
        yield 0, dot_tn(x, gate_low_ref[...]).astype(bf16)
        yield 1, dot_tn(x, up_low_ref[...]).astype(bf16)
        yield 2, dot_tn(g_ref[0, :, cols], active_ref[0]).astype(bf16)

    if fast:
        write_shards(place_ref, grads, products, width)
    else:

        def whole_columns(index, carry):
            cols = pl.ds(pl.multiple_of(index * chunk, chunk), chunk)
            for which, product in products(cols):
                grads[which][0, cols, :] = product
            return carry

        lax.fori_loop(0, width // chunk, whole_columns, 0)


def write_shards(place_ref, outs, products, width):
    send_a, keep_a, send_b, keep_b = outs
    x_bit, y_bit = place_ref[3], place_ref[4]
    shard = width // 4
    for dy in range(2):
        for dx in range(2):
            x, y = x_bit ^ dx, y_bit ^ dy
            cols = pl.ds(pl.multiple_of((y * 2 + x) * shard, shard), shard)
            for which, product in products(cols):
                side = product.shape[1] // 2
                (send_a if dx else keep_a)[0, which, y] = product[:, :side]
                (send_b if dy else keep_b)[0, which, x] = product[:, side:]


def run_experts_back(place, x, g, active, factor, silu, w_gate, w_up, w_down, first, count, fast):
    slots, width = g.shape[1], g.shape[2]
    hidden = w_gate.shape[2]

    def taken(*shape):
        return pl.BlockSpec((1,) + shape, lambda e, p: (e + first, 0, 0))

    def given(*shape):
        zeros = (0,) * len(shape)
        return pl.BlockSpec((1,) + shape, lambda e, p: (e,) + zeros)

    if fast:
        grad_shapes = [(3, 2, width // 4, hidden // 2)] * 4
    else:
        grad_shapes = [(width, hidden)] * 3
    return call(
        lambda *refs: expert_back_kernel(*refs, fast=fast),
        (count,),
        1,
        [taken(slots, width)] * 2 + [taken(slots, hidden)] * 3 + [taken(width, hidden)] * 3,
        [given(slots, width), given(slots, LANES)] + [given(*shape) for shape in grad_shapes],
        [struct((count, slots, width), bf16), struct((count, slots, LANES), f32)]
        + [struct((count,) + shape, bf16) for shape in grad_shapes],
        scratch=[pltpu.VMEM((slots, hidden), bf16)] * 2,
        us=0.5,
    )(place, x, g, active, factor, silu, w_gate, w_up, w_down)


DOT_LANES = 2 * LANES


def combine_kernel(place_ref, rank_ref, *refs, pieces, with_dots, mine):
    parts, rest = refs[:pieces], refs[pieces:]
    rows = rank_ref.shape[2]
    local_experts = sum(part.shape[0] for part in parts)
    hits = hits_of(rank_ref[0], local_experts)
    gathered = jnp.concatenate([part[j, 0] for part in parts for j in range(part.shape[0])], axis=0)
    summed = dot_tn(chosen_of(hits), gathered)
    out_ref = rest[-1]
    if mine:
        arrived_ref = rest[-2]
        summed = summed + arrived_ref[0, 0:rows, :].astype(f32)
    out_ref[0, 0:rows, :] = summed.astype(bf16)
    if with_dots:
        column = [part[j, 0][:, 0:1] for part in rest[:pieces] for j in range(part.shape[0])]
        scattered = [
            jnp.sum(jnp.where(hit, value, 0.0), axis=0, keepdims=True) for hit, value in zip(hits, column)
        ]
        scattered.append(jnp.zeros((DOT_ROWS - local_experts, rows), f32))
        scattered = jnp.concatenate(scattered, axis=0)
        upper = scattered.astype(bf16)
        out_ref[0, rows:, :] = jnp.zeros((DOT_ROWS, out_ref.shape[2]), bf16)
        out_ref[0, rows:, 0:rows] = upper
        out_ref[0, rows:, DOT_LANES : DOT_LANES + rows] = (scattered - upper.astype(f32)).astype(bf16)
        if mine:
            out_ref[0, rows:, 2 * DOT_LANES : 4 * DOT_LANES] = arrived_ref[0, rows:, 0 : 2 * DOT_LANES]


def combine(place, rank, parts, dots=None, arrived=None):
    mine = arrived is not None
    rows, width = rank.shape[2], parts[0].shape[-1]
    out_rows = rows + (DOT_ROWS if dots else 0)

    def member(step, p):
        return (p[0] if mine else 1 - p[0]) * COLS + step

    def slots_of(array):
        return pl.BlockSpec((array.shape[0], 1) + array.shape[2:], lambda j, p: (0, member(j, p), 0, 0))

    inputs = [
        part.reshape(part.shape[0], 2 * COLS, CAPACITY, part.shape[-1]) for part in list(parts) + list(dots or [])
    ]
    in_specs = [pl.BlockSpec((1, 8, rows), lambda j, p: (member(j, p), 0, 0))] + [slots_of(item) for item in inputs]
    by_chip = pl.BlockSpec((1, out_rows, width), lambda j, p: (j, 0, 0))
    if mine:
        inputs.append(arrived)
        in_specs.append(by_chip)
    return call(
        lambda *refs: combine_kernel(*refs, pieces=len(parts), with_dots=bool(dots), mine=mine),
        (COLS,),
        1,
        in_specs,
        by_chip,
        struct((COLS, out_rows, width), bf16),
        us=0.5,
    )(place, rank, *inputs)


def split_dot(dimension_numbers, values, exact):
    upper = values.astype(bf16)
    lower = (values - upper.astype(f32)).astype(bf16)
    return lax.dot_general(
        upper, exact, dimension_numbers, preferred_element_type=f32
    ) + lax.dot_general(lower, exact, dimension_numbers, preferred_element_type=f32)


EXTRA_SLOTS = 6


def middle_back_kernel(
    place_ref, sums_ref, gates_ref, middle_ref, cot_ref, gain_ref, w_router_ref, w_mine_ref, w_other_ref,
    grad_ref, branch_ref, attended_ref, extra_ref
):
    rows = middle_ref.shape[0]
    tail = sums_ref[:, rows : rows + 8, 0 : 4 * DOT_LANES].astype(f32)
    mine = tail[:, :, 0:rows] + tail[:, :, DOT_LANES : DOT_LANES + rows]
    other = tail[:, :, 2 * DOT_LANES : 2 * DOT_LANES + rows] + tail[:, :, 3 * DOT_LANES : 3 * DOT_LANES + rows]
    first_row = place_ref[0] == 0
    dots = jnp.concatenate([jnp.where(first_row, mine, other), jnp.where(first_row, other, mine)], axis=0)
    dots = dots.reshape(dots.shape[0] * 8, rows)
    gates = gates_ref[...]
    logit_grad = dots - gates * jnp.sum(dots, axis=0, keepdims=True)
    middle = middle_ref[...]
    inverse = lax.rsqrt(jnp.mean(middle * middle, axis=1, keepdims=True) + epsilon)
    unit = middle * inverse
    gain = gain_ref[...]
    grad = sums_ref[0, 0:rows].astype(f32)
    for index in range(1, sums_ref.shape[0]):
        grad = grad + sums_ref[index, 0:rows].astype(f32)
    grad = grad + split_dot(TN, logit_grad, w_router_ref[...])
    gain_grad = jnp.sum(grad * unit, axis=0, keepdims=True)
    scaled = grad * gain
    middle_grad = cot_ref[...].astype(f32) + inverse * (
        scaled - unit * jnp.mean(scaled * unit, axis=1, keepdims=True)
    )
    grad_ref[...] = middle_grad
    branch_grad = middle_grad.astype(bf16)
    branch_ref[0:rows, :] = branch_grad
    extra_ref[...] = jnp.zeros_like(extra_ref)
    for index in range(logit_grad.shape[0] // 8):
        first, lane = index // EXTRA_SLOTS * 8, index % EXTRA_SLOTS * DOT_LANES
        extra_ref[first : first + 8, lane : lane + rows] = logit_grad[index * 8 : index * 8 + 8]
    upper = gain_grad.astype(bf16).astype(f32)
    extra_ref[13:14, :] = upper
    extra_ref[14:15, :] = gain_grad - upper
    branch_ref[rows:, :] = extra_ref[...].astype(bf16)
    for which, ref in enumerate((w_mine_ref, w_other_ref)):
        line = place_ref[0] if which == 0 else 1 - place_ref[0]
        for col in range(ref.shape[0]):
            product = dot_nt(branch_grad, ref[col])
            member = line * COLS + col
            attended_ref[member, :, 0:LANES] = product[:, 0:LANES].astype(bf16)
            attended_ref[member, :, LANES : LANES + HEAD_DIM] = product[:, LANES:].astype(bf16)
            attended_ref[member, :, LANES + HEAD_DIM :] = jnp.zeros((product.shape[0], HEAD_DIM), bf16)


def middle_back(place, sums, gates, middle, cotangent, gain, w_router, w_mine, w_other):
    rows, width = middle.shape
    members = 2 * COLS
    args = (sums, gates, middle, cotangent, gain, w_router, w_mine, w_other)
    return call(
        middle_back_kernel,
        (1,),
        1,
        [whole(item.shape) for item in args],
        [whole((rows, width)), whole((rows + DOT_ROWS, width)), whole((members, rows, 2 * LANES))],
        [
            struct((rows, width), f32),
            struct((rows + DOT_ROWS, width), bf16),
            struct((members, rows, 2 * LANES), bf16),
        ],
        scratch=[pltpu.VMEM((DOT_ROWS, width), f32)],
        us=0.5,
    )(place, *args)


def input_grad_kernel(
    place_ref, grads_mine_ref, grads_other_ref, mine_a_ref, mine_b_ref, other_a_ref, other_b_ref,
    tok_ref, middle_grad_ref, gain_ref, out_ref, share_ref, sum_ref
):
    step = pl.program_id(0)
    first = place_ref[4] == 0

    def weights(a_ref, b_ref):
        a = jnp.concatenate([a_ref[index, 0] for index in range(a_ref.shape[0])], axis=0)
        b = jnp.concatenate([b_ref[index, 0] for index in range(b_ref.shape[0])], axis=0)
        upper, lower = jnp.where(first, a, b), jnp.where(first, b, a)
        return jnp.concatenate([upper, lower, lower[lower.shape[0] - HEAD_DIM :]], axis=0)

    rows = tok_ref.shape[0]
    part = dot(grads_mine_ref[0, 0:rows, :], weights(mine_a_ref, mine_b_ref))
    part = part + dot(grads_other_ref[0, 0:rows, :], weights(other_a_ref, other_b_ref))
    share = grads_mine_ref[0, rows:, :].astype(f32)[0:8] + grads_other_ref[0, rows:, :].astype(f32)[0:8]

    @pl.when(step == 0)
    def _():
        sum_ref[...] = part
        share_ref[...] = share

    @pl.when(step > 0)
    def _():
        sum_ref[...] += part
        share_ref[...] += share

    @pl.when(step == pl.num_programs(0) - 1)
    def _():
        resid = tok_ref[...].astype(f32)
        inverse = lax.rsqrt(jnp.mean(resid * resid, axis=1, keepdims=True) + epsilon)
        unit = resid * inverse
        scaled = sum_ref[...] * gain_ref[...]
        out_ref[...] = middle_grad_ref[...] + inverse * (
            scaled - unit * jnp.mean(scaled * unit, axis=1, keepdims=True)
        )


def input_grad(place, grads, weights, tokens, middle_grad, gain):
    rows, width = tokens.shape
    lanes = grads.shape[2]
    w_shape = (weights[0].shape[0], 1) + weights[0].shape[2:]
    return call(
        input_grad_kernel,
        (COLS,),
        1,
        [
            pl.BlockSpec((1, rows + DOT_ROWS, lanes), lambda c, p: (p[0] * COLS + c, 0, 0)),
            pl.BlockSpec((1, rows + DOT_ROWS, lanes), lambda c, p: ((1 - p[0]) * COLS + c, 0, 0)),
        ]
        + [pl.BlockSpec(w_shape, lambda c, p: (0, c, 0, 0))] * 4
        + [whole((rows, width)), whole((rows, width)), whole((1, width))],
        [whole((rows, width)), whole((8, lanes))],
        [struct((rows, width), f32), struct((8, lanes), f32)],
        scratch=[pltpu.VMEM((rows, width), f32)],
        us=0.5,
    )(place, grads, grads, *weights, tokens, middle_grad, gain)


def out_weights_kernel(place_ref, branch_ref, att_ref, normed_ref, own_ref, *refs, fast, local_experts):
    outs, small_ref, (sum_ref, gain_sum_ref) = refs[:-3], refs[-3], refs[-2:]
    step = pl.program_id(0)
    rows = att_ref.shape[0] // 2
    block = rows + DOT_ROWS

    @pl.when(step == 0)
    def _():
        sum_ref[...] = jnp.zeros_like(sum_ref)
        small_ref[...] = jnp.zeros_like(small_ref)
        gain_sum_ref[...] = jnp.zeros_like(gain_sum_ref)

    branch = jnp.concatenate([branch_ref[0:rows, :], branch_ref[block : block + rows, :]], axis=0)
    sum_ref[...] += dot_tn(branch, att_ref[...])
    for which in range(2):
        tail = branch_ref[which * block + rows : (which + 1) * block, :].astype(f32)
        slots = []
        for index in range(small_ref.shape[0] // 8):
            first, lane = index // EXTRA_SLOTS * 8, index % EXTRA_SLOTS * DOT_LANES
            slots.append(tail[first : first + 8, lane : lane + rows])
        logit_grad = jnp.concatenate(slots, axis=0)
        real = lax.broadcasted_iota(jnp.int32, logit_grad.shape, 0) % 8 < local_experts
        logit_grad = jnp.where(real, logit_grad, 0.0).astype(bf16)
        small_ref[...] += dot(logit_grad, normed_ref[which * rows : (which + 1) * rows, :])
        gain_sum_ref[...] += tail[8:16, :]

    @pl.when(step == pl.num_programs(0) - 1)
    def _():
        small_ref[7:8, :] = gain_sum_ref[5:6, :] + gain_sum_ref[6:7, :]

        def products(cols):
            own = own_ref[cols, 0 : 2 * LANES]
            out_one = sum_ref[cols, 0:LANES].astype(bf16)
            out_two = sum_ref[cols, LANES:]
            low = lane_of(out_two.shape) < HEAD_DIM
            tail = jnp.where(low, out_two, own_ref[cols, 2 * LANES :].astype(f32)).astype(bf16)
            yield 0, jnp.concatenate([own, out_one, tail], axis=1)

        if fast:
            write_shards(place_ref, outs, products, own_ref.shape[0])
        else:
            outs[0][...] = next(products(slice(0, own_ref.shape[0])))[1]


def out_weights(place, branch, attended, normed, own, padded, local_experts, fast):
    total, width = normed.shape
    rows = total // COLS
    blocks = branch.shape[0] // COLS
    if fast:
        shapes = [(1, 1, 2, width // 4, 2 * LANES)] * 4
    else:
        shapes = [(width, 4 * LANES)]
    return call(
        lambda *refs: out_weights_kernel(*refs, fast=fast, local_experts=local_experts),
        (COLS,),
        1,
        [
            pl.BlockSpec((blocks, width), lambda j, p: (j, 0)),
            pl.BlockSpec((rows, 2 * LANES), lambda j, p: (j, 0)),
            pl.BlockSpec((rows, width), lambda j, p: (j, 0)),
            whole(own.shape),
        ],
        [whole(shape) for shape in shapes] + [whole((padded, width))],
        [struct(shape, bf16) for shape in shapes] + [struct((padded, width), f32)],
        scratch=[pltpu.VMEM((width, 2 * LANES), f32), pltpu.VMEM((8, width), f32)],
        us=0.5,
    )(place, branch, attended, normed, own)


def first_sum_kernel(place_ref, keep_a_ref, got_a_ref, keep_b_ref, got_b_ref, *rest):
    send_a_ref, held_a_ref, send_b_ref, held_b_ref = rest[-4:]
    x_bit, y_bit = place_ref[3], place_ref[4]
    for bit, keep, got, send, held in (
        (y_bit, keep_a_ref, got_a_ref, send_a_ref, held_a_ref),
        (x_bit, keep_b_ref, got_b_ref, send_b_ref, held_b_ref),
    ):
        for kind in range(keep.shape[1]):
            held[0, kind] = (keep[0, kind, bit].astype(f32) + got[0, kind, bit].astype(f32)).astype(bf16)
            send[0, kind] = (keep[0, kind, 1 - bit].astype(f32) + got[0, kind, 1 - bit].astype(f32)).astype(bf16)


def first_sum(place, chunk, first=0, total=None, before=None):
    count, kinds, _, rows, cols = chunk[0].shape
    taken = pl.BlockSpec((1, kinds, 2, rows, cols), lambda e, p: (e, 0, 0, 0, 0))
    given = pl.BlockSpec((1, kinds, rows, cols), lambda e, p: (e + first, 0, 0, 0))
    extra = list(before) if before else []
    return call(
        first_sum_kernel,
        (count,),
        1,
        [taken] * 4 + [pl.BlockSpec(memory_space=pl.ANY)] * len(extra),
        [given] * 4,
        [struct((total or count, kinds, rows, cols), bf16)] * 4,
        us=0.5,
        aliases={5 + i: i for i in range(len(extra))},
    )(place, *chunk, *extra)


def last_sum_kernel(held_a_ref, got_a_ref, held_b_ref, got_b_ref, *rest):
    outs = rest[-3:]
    side = held_a_ref.shape[3]
    for which, out in enumerate(outs):
        out[0, :, :side] = held_a_ref[0, which].astype(f32) + got_a_ref[0, which].astype(f32)
        out[0, :, side:] = held_b_ref[0, which].astype(f32) + got_b_ref[0, which].astype(f32)


def last_sum(held_a, got_a, held_b, got_b, first, total, before):
    count, kinds, rows, cols = held_a.shape
    taken = pl.BlockSpec((1, kinds, rows, cols), lambda e: (e, 0, 0, 0))
    given = pl.BlockSpec((1, rows, 2 * cols), lambda e: (e + first, 0, 0))
    extra = list(before) if before else []
    return call(
        last_sum_kernel,
        (count,),
        0,
        [taken] * 4 + [pl.BlockSpec(memory_space=pl.ANY)] * len(extra),
        [given] * 3,
        [struct((total, rows, 2 * cols), f32)] * 3,
        us=0.5,
        aliases={4 + i: i for i in range(len(extra))},
    )(held_a, got_a, held_b, got_b, *extra)


def last_weights_kernel(held_a_ref, got_a_ref, held_b_ref, got_b_ref, query_ref, key_ref, value_ref, out_ref):
    left = jnp.transpose(held_a_ref[0, 0].astype(f32) + got_a_ref[0, 0].astype(f32))
    right = jnp.transpose(held_b_ref[0, 0].astype(f32) + got_b_ref[0, 0].astype(f32))
    cut = query_ref.shape[0]
    query_ref[...] = left[:cut]
    key_ref[...] = left[cut:]
    out_ref[...] = right[:cut]
    value_ref[...] = right[cut:]


def last_weights(parts, widths):
    rows = parts[0].shape[2]
    shapes = [(width, rows) for width in widths]
    return call(
        last_weights_kernel,
        (1,),
        0,
        [whole(part.shape) for part in parts],
        [whole(shape) for shape in shapes],
        [struct(shape, f32) for shape in shapes],
        us=0.5,
    )(*parts)


SWAP = [(0, 1), (1, 0)]


def after(value, *events):
    return lax.optimization_barrier((value,) + events)[0]


def gather_group(block):
    return lax.all_gather(block, ("row", "col"), axis=0, tiled=True)


def line_pieces(value):
    parts = [value]
    for distance in range(1, COLS):
        parts.insert(0, lax.ppermute(value, "col", [(i, (i + distance) % COLS) for i in range(COLS)]))
    return parts


def in_line_order(parts):
    parts = jnp.stack(parts + parts)
    return lax.dynamic_slice_in_dim(parts, COLS - 1 - lax.axis_index("col"), COLS, axis=0)


def flip(value, axis, bit, size):
    return lax.ppermute(value, axis, [(i, i ^ (1 << bit)) for i in range(size)])


def bits_of(size):
    return size.bit_length() - 1


def own_bit(axis, bit):
    return (lax.axis_index(axis) >> bit) & 1


def joined(mine, got, own):
    return jnp.where(own == 0, jnp.concatenate([mine, got]), jnp.concatenate([got, mine]))


def cube_step(value, axis, bit, size):
    return joined(value, flip(value, axis, bit, size), own_bit(axis, bit))


def lines_first(value):
    return jnp.transpose(value, (1, 0, 2, 3)).reshape(value.shape[1], value.shape[0] * value.shape[2], value.shape[3])


def cube_gather(value, axis, size):
    value = value[None]
    for bit in range(bits_of(size)):
        value = cube_step(value, axis, bit, size)
    return value


def sum_dp(value, sizes):
    for bit in range(bits_of(sizes["dp"])):
        value = value + flip(value, "dp", bit, sizes["dp"])
    return value


def reduce_over_dp(value, size):
    count = bits_of(size)
    value = value.reshape(value.shape[:1] + (2,) * count + value.shape[2:])
    current = value
    for bit in range(count - 1, -1, -1):
        own = own_bit("dp", bit)
        keep = lax.dynamic_index_in_dim(current, own, 1, keepdims=False)
        send = lax.dynamic_index_in_dim(current, 1 - own, 1, keepdims=False).astype(bf16)
        current = keep.astype(f32) + flip(send, "dp", bit, size).astype(f32)
    return current


def start_move(run, size):
    return flip(run[0], "dp", 0, size), flip(run[2], "dp", 1, size)


def second_move(sums, size):
    send_a, held_a, send_b, held_b = sums
    return held_a, flip(send_a, "dp", 1, size), held_b, flip(send_b, "dp", 0, size)


def layer(sizes):
    n_dp, n_row, n_col = sizes["dp"], sizes["row"], sizes["col"]
    members = n_row * n_col
    fast = n_dp == 4
    assert n_row == 2 and n_col == COLS and n_dp & (n_dp - 1) == 0

    def local(
        tokens, cotangent, routes, lengths, gain_attn, w_query, w_key, w_value, w_out,
        gain_moe, w_router, w_gate, w_up, w_down,
    ):
        rows, width = tokens.shape
        group = rows * members
        local_experts = w_gate.shape[0]
        row, col, dp = lax.axis_index("row"), lax.axis_index("col"), lax.axis_index("dp")
        place = jnp.stack([row, col, row * n_col + col, dp & 1, (dp >> 1) & 1]).astype(jnp.int32)
        gain_one = gain_attn.astype(f32)[None]
        gain_two = gain_moe.astype(f32)[None]

        tok_all = gather_group(tokens)
        w_in = jnp.concatenate([w_query.T, w_key.T, w_value.T], axis=0)
        out_share, in_share = rows // n_dp, w_in.shape[0] // n_dp
        shares = jnp.concatenate(
            [
                lax.dynamic_slice(w_out.T, (dp * out_share, 0), (out_share, width)),
                lax.dynamic_slice(w_in, (dp * in_share, 0), (in_share, width)),
                jnp.pad(routes.T.astype(bf16).reshape(1, TOP * rows), ((0, 7), (0, width - TOP * rows))),
            ],
            axis=0,
        )
        w_stack = jnp.concatenate([w_query.T, w_key.T, w_value.T, w_value.T], axis=0)
        w_natural = jnp.concatenate([w_query, w_key, w_value, w_value], axis=1)

        ends = jnp.cumsum(lengths[0])
        starts = ends - lengths[0]
        position = jnp.arange(group, dtype=jnp.int32)
        segment = jnp.sum((position[:, None] >= ends[None, :]).astype(jnp.int32), axis=1)
        member = segment[:, None] == jnp.arange(starts.shape[0], dtype=jnp.int32)[None, :]
        start = jnp.sum(jnp.where(member, starts[None, :], 0), axis=1).astype(jnp.int32)
        frequency = rope_base ** (-2.0 * jnp.arange(HEAD_DIM // 2, dtype=f32) / HEAD_DIM)
        angle = (position - start).astype(f32)[:, None] * frequency[None, :]
        cosine = jnp.tile(jnp.cos(angle), (1, 4))
        sine = jnp.tile(jnp.sin(angle), (1, 4))

        w_router_rows = w_router.T.reshape(members, local_experts, width)
        w_router_rows = jnp.pad(w_router_rows, ((0, 0), (0, 8 - local_experts), (0, 0)))
        w_router_rows = w_router_rows.reshape(members * 8, width)
        start_row = jnp.broadcast_to(start[None, :], (8, group))
        start = start[:, None]
        gain_column = gain_attn.astype(f32)[:, None]
        ready = (place, gain_one, gain_two, w_stack, w_natural, cosine, sine, w_router_rows, start, start_row, gain_column)
        shares, place, gain_one, gain_two, w_stack, w_natural, cosine, sine, w_router_rows, start, start_row, gain_column = (
            lax.optimization_barrier((shares,) + ready)
        )
        shares = line_pieces(after(shares, tok_all, cosine))

        query, key, value, normed_one = project(tok_all, gain_one, w_stack, cosine, sine)
        packed, attended, totals = attend(query, key, value, start)
        att_flat = gather_group(packed)
        att_all = att_flat.reshape((n_row, n_col) + packed.shape)
        shares = in_line_order(after(shares, packed))
        route_rows = shares[:, out_share + in_share]
        w_out_mine, in_part = shares[None, :, :out_share], shares[None, :, out_share : out_share + in_share]
        for bit in range(bits_of(n_dp)):
            w_out_mine = cube_step(w_out_mine, "dp", bit, n_dp)
        in_part = cube_step(in_part, "dp", 0, n_dp)
        w_out_mine = lines_first(w_out_mine)
        w_out_other = lax.ppermute(after(w_out_mine, in_part), "row", SWAP)
        route_rows = cube_gather(route_rows, "row", n_row)[:, :, : TOP * rows].reshape(members, TOP, rows)
        cot_all = gather_group(after(cotangent, w_out_other))
        x, slot_gate, rank, gate, normed_two, middle, gates = middle_and_dispatch(
            place, att_all, w_out_mine, w_out_other, tok_all, route_rows, gain_two, w_router_rows, local_experts
        )
        slots = members * CAPACITY
        x = x.reshape(local_experts, slots, width)
        slot_gate = slot_gate.reshape(local_experts, slots, LANES)
        rank, gate = rank.reshape(members, 8, rows), gate.reshape(members, 8, rows)
        forth, active, factor, silu = run_experts(x, slot_gate, w_gate, w_up, w_down)
        for bit in range(1, bits_of(n_dp) - 1):
            in_part = cube_step(in_part, "dp", bit, n_dp)
        last_bit = bits_of(n_dp) - 1
        in_got = after(flip(in_part, "dp", last_bit, n_dp), forth)
        forth_other = combine(place, after(rank, in_got), [forth])
        arrived = lax.ppermute(forth_other, "row", SWAP)
        g = grad_dispatch(after(rank, forth_other), gate, cot_all, local_experts)
        g = g.reshape(local_experts, slots, width)
        cuts = [0, 1, 3, local_experts]

        def backward(which, x):
            first, last = cuts[which], cuts[which + 1]
            return run_experts_back(place, x, g, active, factor, silu, w_gate, w_up, w_down, first, last - first, fast)

        runs = [backward(0, x)]
        forth_mine = combine(place, rank, [forth], arrived=after(arrived, runs[0][1]))
        forth_sums = lax.all_to_all(forth_mine, "col", 0, 0, tiled=True)
        runs.append(backward(1, after(x, forth_mine)))
        runs.append(backward(2, after(x, runs[1][1])))
        moved = [start_move(run[2:], n_dp) for run in runs] if fast else []
        back_parts, dot_parts = [run[0] for run in runs], [run[1] for run in runs]
        back_other = combine(place, after(rank, *moved[0]) if fast else rank, back_parts, dot_parts)
        arrived = lax.ppermute(back_other, "row", SWAP)
        back_mine = combine(place, rank, back_parts, dot_parts, arrived)
        back_mine = after(back_mine, forth_sums)
        back_sums = lax.all_to_all(back_mine, "col", 0, 0, tiled=True)

        if fast:
            w_in_parts = [in_part, in_got]
        else:
            own = own_bit("dp", last_bit)
            w_in_rows = lines_first(joined(in_part, in_got, own))[None]
            half = w_in_rows.shape[2] // 2
            upper, lower = w_in_rows[:, :, :half], w_in_rows[:, :, half:]
            w_in_parts = [jnp.where(place[4] == 0, upper, lower), jnp.where(place[4] == 0, lower, upper)]
        if fast:

            def chunk_of(which, *events):
                keep_a, keep_b = after((runs[which][3], runs[which][5]), *events)
                return keep_a, moved[which][0], keep_b, moved[which][1]

            sums = first_sum(place, chunk_of(0, back_mine), cuts[0], cuts[2])
            gate_middle = (sums[1],) + moved[1]
        else:
            gate_middle = ()
        w_in_parts += [lax.ppermute(after(part, back_mine), "row", SWAP) for part in w_in_parts]

        middle_grad, branch_grad, attended_grad = middle_back(
            place, back_sums, gates, middle, cotangent, after(gain_two, *w_in_parts[2:], *gate_middle),
            w_router_rows, w_out_mine, w_out_other,
        )
        if fast:
            sums = first_sum(place, chunk_of(1, branch_grad), cuts[1], cuts[2], sums)
            started = [second_move(sums, n_dp)]
        attended_grad = lax.all_to_all(attended_grad, ("row", "col"), 0, 0, tiled=True)
        if fast:
            attended_grad = after(attended_grad, sums[1])
        branch_all = gather_group(branch_grad)

        attended_grad = attended_grad.reshape(group, 2 * LANES)
        projected_grad, own_grads = attend_back(
            query, key, value, attended_grad, totals, start_row, cosine, sine, normed_one, w_natural, gain_column
        )
        projected_all = lax.all_to_all(projected_grad, ("row", "col"), 0, 0, tiled=True)
        *w_parts, small = out_weights(
            place, branch_all, attended, normed_two.reshape(group, width), own_grads,
            members * 8, local_experts, fast,
        )
        arriving = ()
        if fast:
            w_moved = start_move(w_parts, n_dp)
            late = first_sum(place, chunk_of(2, small, started[0][1], started[0][3]))
            started.append(second_move(late, n_dp))
            w_first = first_sum(place, (w_parts[1], w_moved[0], w_parts[3], w_moved[1]))
            w_sums = second_move(w_first, n_dp)
            arriving = (w_first[1], started[1][0])
        else:
            cut = w_parts[0].reshape(1, n_dp, width // n_dp, w_parts[0].shape[1])
            w_sum = reduce_over_dp(cut, n_dp)[0]


        mixed = (middle + jnp.sum(after(forth_sums, small).astype(f32), axis=0)).astype(bf16)
        used = small.reshape(members, 8, width)[:, :local_experts].reshape(members * local_experts, width)
        both = sum_dp(jnp.concatenate([used, small[7:8]], axis=0), sizes)
        w_router_grad = both[: members * local_experts].T
        gain_moe_grad = both[members * local_experts]

        tokens_grad, share = input_grad(
            place, projected_all, w_in_parts, tokens, middle_grad, after(gain_one, w_parts[0], *arriving)
        )
        share = (share[0:4] + share[4:8]).reshape(8, width // 8)
        if fast:
            held_a, got_a, held_b, got_b = started[0]
            held_a, held_b = after((held_a, held_b), tokens_grad)
            expert_grads = last_sum(held_a, got_a, held_b, got_b, 0, local_experts, None)
            share = share + after(flip(share, "dp", 0, n_dp), expert_grads[0])
            held_a, got_a, held_b, got_b = started[1]
            held_a, held_b = after((held_a, held_b), share, w_sums[1], w_sums[3])
            expert_grads = last_sum(held_a, got_a, held_b, got_b, cuts[2], local_experts, expert_grads)
            gain_attn_grad = share + after(flip(share, "dp", 1, n_dp), expert_grads[0])
            gain_attn_grad = gain_attn_grad.reshape(width)
        else:
            gain_attn_grad = sum_dp(share, sizes).reshape(width)

        local_q, local_k = w_query.shape[1], w_key.shape[1]
        if fast:
            w_query_grad, w_key_grad, w_value_grad, w_out_grad = [
                item.T for item in last_weights(w_sums, (local_q, local_k, local_k, local_q))
            ]
        else:
            expert_grads = []
            for which in range(3):
                parts = [run[2 + which] for run in runs]
                parts = [part.reshape(part.shape[0], n_dp, width // n_dp, part.shape[2]) for part in parts]
                expert_grads.append(jnp.concatenate([reduce_over_dp(part, n_dp) for part in parts], axis=0))
            cut = local_q + local_k
            w_query_grad, w_key_grad = w_sum[:, :local_q], w_sum[:, local_q:cut]
            w_out_grad, w_value_grad = w_sum[:, cut : cut + local_q], w_sum[:, cut + local_q :]
        w_gate_grad, w_up_grad, w_down_grad = expert_grads
        return (
            mixed, tokens_grad, gain_attn_grad, w_query_grad, w_key_grad, w_value_grad, w_out_grad,
            gain_moe_grad, w_router_grad, w_gate_grad, w_up_grad, w_down_grad,
        )

    return local


def solution(mesh):
    return jax.shard_map(
        layer(dict(mesh.shape)),
        mesh=mesh,
        in_specs=(
            P(("dp", "row", "col"), None),
            P(("dp", "row", "col"), None),
            P(("dp", "row", "col"), None),
            P("dp", None),
            P(),
            P(None, ("row", "col")),
            P(None, ("row", "col")),
            P(None, ("row", "col")),
            P(None, ("row", "col")),
            P(),
            P(),
            P(("row", "col"), None, None),
            P(("row", "col"), None, None),
            P(("row", "col"), None, None),
        ),
        out_specs=(
            P(("dp", "row", "col"), None),
            P(("dp", "row", "col"), None),
            P(),
            P("dp", ("row", "col")),
            P("dp", ("row", "col")),
            P("dp", ("row", "col")),
            P("dp", ("row", "col")),
            P(),
            P(),
            P(("row", "col"), "dp", None),
            P(("row", "col"), "dp", None),
            P(("row", "col"), "dp", None),
        ),
        check_vma=False,
    )
```

```python
import math

import jax
import jax.numpy as jnp
import numpy as np
from jax import lax
from jax.experimental import pallas as pl
from jax.experimental.pallas import tpu as pltpu
from jax.sharding import PartitionSpec as P

HEAD_DIM = 64
EXPERTS = 40
TOP = 8
CAPACITY = 64
COLS = 4
LANES = 128
QUERY_BLOCK = 256
DOT_ROWS = 16

epsilon = 1e-06
rope_base = 10000.0
masked_score = -1e30
f32 = jnp.float32
bf16 = jnp.bfloat16
VMEM_LIMIT = 56 * 1024 * 1024

NT = (((1,), (1,)), ((), ()))
TN = (((0,), (0,)), ((), ()))


def dot(a, b):
    return jnp.dot(a, b, preferred_element_type=f32)


def dot_nt(a, b):
    return lax.dot_general(a, b, NT, preferred_element_type=f32)


def dot_tn(a, b):
    return lax.dot_general(a, b, TN, preferred_element_type=f32)


def lane_of(shape):
    return lax.broadcasted_iota(jnp.int32, shape, len(shape) - 1)


def call(
    kernel, grid, prefetch, in_specs, out_specs, out_shape, scratch=(), us=1.0, aliases=None
):
    return pl.pallas_call(
        kernel,
        grid_spec=pltpu.PrefetchScalarGridSpec(
            num_scalar_prefetch=prefetch,
            grid=grid,
            in_specs=in_specs,
            out_specs=out_specs,
            scratch_shapes=list(scratch),
        ),
        out_shape=out_shape,
        input_output_aliases=aliases or {},
        compiler_params=pltpu.CompilerParams(
            vmem_limit_bytes=VMEM_LIMIT, dimension_semantics=("arbitrary",) * len(grid)
        ),
        cost_estimate=pl.CostEstimate(
            flops=int(us * 1.1e9), bytes_accessed=int(us * 3.6e6), transcendentals=0
        ),
    )


def whole(shape):
    zeros = (0,) * len(shape)
    return pl.BlockSpec(shape, lambda *_: zeros)


def struct(shape, dtype):
    return jax.ShapeDtypeStruct(shape, dtype)


def turn_within_heads(values, sign):
    lane = lane_of(values.shape) % HEAD_DIM
    ahead = pltpu.roll(values, LANES - HEAD_DIM // 2, 1)
    behind = pltpu.roll(values, HEAD_DIM // 2, 1)
    return jnp.where(lane < HEAD_DIM // 2, -sign * ahead, sign * behind)


def project_kernel(
    tok_ref, gain_ref, w_ref, cos_ref, sin_ref, query_ref, key_ref, value_ref, normed_ref
):
    resid = tok_ref[...].astype(f32)
    inverse = lax.rsqrt(jnp.mean(resid * resid, axis=1, keepdims=True) + epsilon)
    normed = (resid * inverse * gain_ref[...]).astype(bf16)
    normed_ref[...] = normed
    raw = dot_nt(normed, w_ref[...])
    cosine, sine = cos_ref[...], sin_ref[...]

    def rot(values):
        return (values * cosine + turn_within_heads(values, 1.0) * sine).astype(bf16).astype(f32)

    first = rot(raw[:, :LANES])
    second = rot(raw[:, LANES : 2 * LANES])
    low = lane_of(first.shape) < HEAD_DIM
    scale = 1.0 / math.sqrt(HEAD_DIM)
    query_ref[0] = jnp.where(low, first * scale, 0.0).astype(bf16)
    query_ref[1] = jnp.where(low, 0.0, first * scale).astype(bf16)
    query_ref[2] = jnp.where(low, second * scale, 0.0).astype(bf16)
    key_ref[...] = jnp.where(low, pltpu.roll(second, HEAD_DIM, 1), second).astype(bf16)
    value_ref[...] = raw[:, 2 * LANES :].astype(bf16)


def project(tokens, gain, w_stack, cosine, sine):
    total, width = tokens.shape
    rows = 512
    lanes = pl.BlockSpec((rows, LANES), lambda j: (j, 0))
    wide = pl.BlockSpec((rows, width), lambda j: (j, 0))
    return call(
        project_kernel,
        (total // rows,),
        0,
        [wide, whole((1, width)), whole(w_stack.shape), lanes, lanes],
        [pl.BlockSpec((3, rows, LANES), lambda j: (0, j, 0)), lanes, lanes, wide],
        [
            struct((3, total, LANES), bf16),
            struct((total, LANES), bf16),
            struct((total, LANES), bf16),
            struct((total, width), bf16),
        ],
        us=0.5,
    )(tokens, gain, w_stack, cosine, sine)


def attend_kernel(query_ref, key_ref, value_ref, start_ref, packed_ref, plain_ref, total_ref, out_ref):
    blocks = query_ref.shape[1] // QUERY_BLOCK
    block = pl.program_id(0)
    for index in range(blocks):

        @pl.when(block == index)
        def _(index=index):
            rows = pl.ds(index * QUERY_BLOCK, QUERY_BLOCK)
            span = (index + 1) * QUERY_BLOCK
            row = index * QUERY_BLOCK + lax.broadcasted_iota(jnp.int32, (QUERY_BLOCK, span), 0)
            column = lane_of((QUERY_BLOCK, span))
            allowed = (column <= row) & (column >= start_ref[rows, :])

            def head(number, carry):
                scores = dot_nt(query_ref[number, rows, :], key_ref[0:span, :])
                scores = jnp.where(allowed, scores, masked_score)
                peak = jnp.max(scores, axis=1, keepdims=True)
                weights = jnp.exp(scores - peak)
                summed = jnp.sum(weights, axis=1, keepdims=True)
                probs = (weights * (1.0 / summed)).astype(bf16)
                out_ref[number] = dot(probs, value_ref[0:span, :])
                total = jnp.broadcast_to(peak + jnp.log(summed), (QUERY_BLOCK, LANES))
                total_ref[number, :, rows] = jnp.transpose(total)[0:8, :]
                return carry

            for number in range(3):
                head(number, 0)
            low = lane_of((QUERY_BLOCK, LANES)) < HEAD_DIM
            one, two, three = out_ref[0], out_ref[1], out_ref[2]
            pair = jnp.where(low, one, two).astype(bf16)
            plain_ref[rows, 0:LANES] = pair
            plain_ref[rows, LANES : 2 * LANES] = jnp.where(low, three, 0.0).astype(bf16)
            if index < blocks // 2:
                packed_ref[rows, 0:LANES] = pair
                packed_ref[rows, LANES : 2 * LANES] = three.astype(bf16)
            else:
                back = pl.ds((index - blocks // 2) * QUERY_BLOCK, QUERY_BLOCK)
                before = packed_ref[back, LANES : 2 * LANES].astype(f32)
                packed_ref[back, LANES : 2 * LANES] = jnp.where(low, before, one).astype(bf16)
                packed_ref[back, 2 * LANES : 3 * LANES] = jnp.where(low, two, three).astype(bf16)


def attend(query, key, value, start):
    total = key.shape[0]
    return call(
        attend_kernel,
        (total // QUERY_BLOCK,),
        0,
        [whole(query.shape), whole(key.shape), whole(value.shape), whole(start.shape)],
        [whole((total // 2, 3 * LANES)), whole((total, 2 * LANES)), whole((3, 8, total))],
        [
            struct((total // 2, 3 * LANES), bf16),
            struct((total, 2 * LANES), bf16),
            struct((3, 8, total), f32),
        ],
        scratch=[pltpu.VMEM((3, QUERY_BLOCK, LANES), f32)],
        us=0.5,
    )(query, key, value, start)


def attend_back_kernel(
    query_ref, key_ref, value_ref, grad_ref, total_ref, start_ref, cos_ref, sin_ref, normed_ref, w_ref, gain_ref,
    blocks_ref, own_ref, out_ref, query_grad_ref, key_grad_ref, value_grad_ref, own_sum_ref
):
    blocks = query_ref.shape[1] // QUERY_BLOCK
    block = pl.program_id(0)
    scale = 1.0 / math.sqrt(HEAD_DIM)

    @pl.when(block == 0)
    def _():
        key_grad_ref[...] = jnp.zeros_like(key_grad_ref)
        value_grad_ref[...] = jnp.zeros_like(value_grad_ref)

    def back(values, cosine, sine):
        return values * cosine + turn_within_heads(values * sine, -1.0)

    for index in range(blocks):

        @pl.when(block == index)
        def _(index=index):
            rows = pl.ds(index * QUERY_BLOCK, QUERY_BLOCK)
            span = (index + 1) * QUERY_BLOCK
            row = index * QUERY_BLOCK + lane_of((span, QUERY_BLOCK))
            column = lax.broadcasted_iota(jnp.int32, (span, QUERY_BLOCK), 0)
            allowed = (column <= row) & (column >= start_ref[0:1, rows])
            low = lane_of((QUERY_BLOCK, LANES)) < HEAD_DIM

            def head(number, carry):
                query = query_ref[number, rows, :]
                tile = number // 2 * LANES
                upstream = grad_ref[rows, tile : tile + LANES].astype(f32)
                keep = low == (number != 1)
                upstream = jnp.where(keep, upstream, 0.0).astype(bf16)
                scores = dot_nt(key_ref[0:span, :], query)
                probs = jnp.exp(scores - total_ref[number, 0:1, rows])
                probs = jnp.where(allowed, probs, 0.0)
                prob_grad = dot_nt(value_ref[0:span, :], upstream)
                row_dot = jnp.sum(probs * prob_grad, axis=0, keepdims=True)
                score_grad = (probs * (prob_grad - row_dot)).astype(bf16)
                key_grad_ref[0:span, :] += dot(score_grad, query)
                value_grad_ref[0:span, :] += dot(probs.astype(bf16), upstream)
                query_grad_ref[number] = dot_tn(score_grad, key_ref[0:span, :]) * scale
                return carry

            for number in range(3):
                head(number, 0)
            cosine, sine = cos_ref[rows, :], sin_ref[rows, :]
            pair = jnp.where(low, query_grad_ref[0], query_grad_ref[1])
            out_ref[rows, 0:LANES] = back(pair, cosine, sine).astype(bf16)
            out_ref[rows, LANES : 2 * LANES] = back(query_grad_ref[2], cosine, sine).astype(bf16)

    @pl.when(block == blocks - 1)
    def _():
        low = lane_of(key_grad_ref.shape) < HEAD_DIM
        key_grad = key_grad_ref[...]
        key_grad = key_grad + pltpu.roll(key_grad, HEAD_DIM, 1)
        key_grad = back(key_grad, cos_ref[...], sin_ref[...])
        before = out_ref[:, LANES : 2 * LANES].astype(f32)
        out_ref[:, LANES : 2 * LANES] = jnp.where(low, before, key_grad).astype(bf16)
        value_grad = value_grad_ref[...]
        value_grad = value_grad + pltpu.roll(value_grad, HEAD_DIM, 1)
        out_ref[:, 2 * LANES : 3 * LANES] = jnp.where(low, 0.0, value_grad).astype(bf16)
        chunk = 512
        own_sum_ref[...] = jnp.zeros_like(own_sum_ref)

        def add(index, carry):
            part = pl.ds(pl.multiple_of(index * chunk, chunk), chunk)
            own_sum_ref[...] += dot_tn(normed_ref[part, :], out_ref[part, :])
            return carry

        lax.fori_loop(0, out_ref.shape[0] // chunk, add, 0)
        own = own_sum_ref[...]
        own_ref[...] = own.astype(bf16)
        share = jnp.sum(own * w_ref[...].astype(f32), axis=1, keepdims=True) / gain_ref[...]
        share = jnp.transpose(jnp.broadcast_to(share, (share.shape[0], LANES)))[0:8, :]
        width = blocks_ref.shape[2]
        row = lax.broadcasted_iota(jnp.int32, (8, width), 0)
        terms = jnp.zeros((8, width), f32)
        for index in range(share.shape[1] // width):
            piece = share[:, index * width : (index + 1) * width]
            upper = piece.astype(bf16).astype(f32)
            terms = jnp.where(row == index, upper, jnp.where(row == index + 4, piece - upper, terms))
        terms = jnp.concatenate([terms, jnp.zeros((8, width), f32)], axis=0).astype(bf16)
        rows = blocks_ref.shape[1] - DOT_ROWS
        for index in range(blocks_ref.shape[0]):
            blocks_ref[index, 0:rows, :] = out_ref[index * rows : (index + 1) * rows, :]
            blocks_ref[index, rows:, :] = terms


def attend_back(query, key, value, grad, totals, start, cosine, sine, normed, w_natural, gain):
    total = key.shape[0]
    members = 2 * COLS
    rows = total // members + DOT_ROWS
    args = (query, key, value, grad, totals, start, cosine, sine, normed, w_natural, gain)
    return call(
        attend_back_kernel,
        (total // QUERY_BLOCK,),
        0,
        [whole(item.shape) for item in args],
        [whole((members, rows, 3 * LANES)), whole(w_natural.shape)],
        [struct((members, rows, 3 * LANES), bf16), struct(w_natural.shape, bf16)],
        scratch=[
            pltpu.VMEM((total, 3 * LANES), bf16),
            pltpu.VMEM((3, QUERY_BLOCK, LANES), f32),
            pltpu.VMEM((total, LANES), f32),
            pltpu.VMEM((total, LANES), f32),
            pltpu.VMEM(w_natural.shape, f32),
        ],
        us=0.5,
    )(*args)


def branch_operand(refs):
    rows = refs.shape[2]
    low = lane_of((rows, LANES)) < HEAD_DIM
    pairs, thirds = [], []
    for member in range(refs.shape[1]):
        one = refs[0, member, :, 0:LANES]
        mid = refs[0, member, :, LANES : 2 * LANES].astype(f32)
        end = refs[0, member, :, 2 * LANES : 3 * LANES].astype(f32)
        mid_turned = pltpu.roll(mid, HEAD_DIM, 1)
        end_turned = pltpu.roll(end, HEAD_DIM, 1)
        late = jnp.where(low, mid_turned, end_turned).astype(bf16)
        pairs.append(jnp.concatenate([one, late], axis=0))
        thirds.append((mid, end_turned))
    for member in range(0, refs.shape[1], 2):
        tops = []
        for which in range(2):
            left, right = thirds[member][which], thirds[member + 1][which]
            tops.append(jnp.where(low, left, pltpu.roll(right, HEAD_DIM, 1)).astype(bf16))
        pairs.append(jnp.concatenate(tops, axis=0))
    return jnp.concatenate(pairs, axis=1)


def branch_weights(ref):
    right = [ref[source, 0:LANES] for source in range(ref.shape[0])]
    return jnp.concatenate(right + [ref[source, LANES:] for source in range(ref.shape[0])], axis=0)


def hits_of(rank, local_experts):
    place = lax.broadcasted_iota(jnp.int32, (CAPACITY, rank.shape[1]), 0).astype(f32)
    return [place == rank[j : j + 1, :] for j in range(local_experts)]


def chosen_of(hits):
    return jnp.concatenate([jnp.where(hit, 1.0, 0.0).astype(bf16) for hit in hits], axis=0)


def middle_kernel(
    place_ref, att_mine_ref, att_other_ref, w_mine_ref, w_other_ref, tok_a_ref, tok_b_ref, routes_a_ref, routes_b_ref,
    gain_ref, w_router_ref, after_ref,
    x_ref, slot_gate_ref, rank_ref, gate_ref, normed_ref, middle_ref, gates_own_ref, gates_ref, ranks_ref
):
    step = pl.program_id(0)
    member = place_ref[2]
    cols = pl.num_programs(0)
    rows = tok_a_ref.shape[0]
    local_experts = x_ref.shape[0]
    branch = dot(branch_operand(att_mine_ref), branch_weights(w_mine_ref))
    branch = branch + dot(branch_operand(att_other_ref), branch_weights(w_other_ref))
    for half in range(2):
        tok_ref, routes_ref = ((tok_a_ref, routes_a_ref), (tok_b_ref, routes_b_ref))[half]
        middle = tok_ref[...].astype(f32) + branch[half * rows : (half + 1) * rows]
        inverse = lax.rsqrt(jnp.mean(middle * middle, axis=1, keepdims=True) + epsilon)
        normed = (middle * inverse * gain_ref[...]).astype(bf16)
        normed_ref[half, 0] = normed
        logits = dot_nt(w_router_ref[...], normed)
        padded = logits.shape[0]
        slot = lax.broadcasted_iota(jnp.int32, (padded, rows), 0)
        expert = (slot // 8) * local_experts + slot % 8
        expert = jnp.where(slot % 8 < local_experts, expert, -1).astype(f32)
        routes = routes_ref[0].astype(f32)
        named = expert == routes[0:1, 0:rows]
        for k in range(1, TOP):
            named = named | (expert == routes[k : k + 1, 0:rows])
        peak = jnp.max(jnp.where(named, logits, masked_score), axis=0, keepdims=True)
        weights = jnp.where(named, jnp.exp(logits - peak), 0.0)
        gates = weights / jnp.sum(weights, axis=0, keepdims=True)
        gates_ref[...] = gates
        ranks_ref[...] = jnp.where(named, dot(named.astype(f32).astype(bf16), after_ref[...]), -1.0)
        here = pl.ds(pl.multiple_of(member * 8, 8), 8)
        gate, rank = gates_ref[here, :], ranks_ref[here, :]
        rank_ref[half, 0] = rank
        gate_ref[half, 0] = gate
        hits = hits_of(rank, local_experts)
        slot_gate = jnp.concatenate(
            [jnp.sum(jnp.where(hit, gate[j : j + 1, :], 0.0), axis=1, keepdims=True) for j, hit in enumerate(hits)],
            axis=0,
        )
        chosen = chosen_of(hits)
        picked = dot(chosen, normed).astype(bf16)
        spread = jnp.broadcast_to(slot_gate, (slot_gate.shape[0], LANES))
        for j in range(local_experts):
            part = slice(j * CAPACITY, (j + 1) * CAPACITY)
            x_ref[j, half, 0] = picked[part]
            slot_gate_ref[j, half, 0] = spread[part]

        @pl.when(member == half * cols + step)
        def _(middle=middle, gates=gates):
            middle_ref[...] = middle
            gates_own_ref[...] = gates


def middle_and_dispatch(place, att, w_mine, w_other, tokens, routes, gain, w_router, local_experts):
    width = tokens.shape[1]
    half = COLS
    rows = tokens.shape[0] // (2 * half)
    padded = w_router.shape[0]
    after = jnp.asarray(np.triu(np.ones((rows, rows), np.float32), 1), bf16)
    slot_shape = (local_experts, 2, half, CAPACITY)
    early = pl.BlockSpec((rows, width), lambda i, p: (i, 0))
    late = pl.BlockSpec((rows, width), lambda i, p: (i + half, 0))
    routes_shape = (1,) + routes.shape[1:]
    return call(
        middle_kernel,
        (half,),
        1,
        [
            pl.BlockSpec((1, half, rows, 3 * LANES), lambda i, p: (p[0], 0, i, 0)),
            pl.BlockSpec((1, half, rows, 3 * LANES), lambda i, p: (1 - p[0], 0, i, 0)),
            whole(w_mine.shape),
            whole(w_other.shape),
            early,
            late,
            pl.BlockSpec(routes_shape, lambda i, p: (i, 0, 0)),
            pl.BlockSpec(routes_shape, lambda i, p: (i + half, 0, 0)),
            whole((1, width)),
            whole(w_router.shape),
            whole((rows, rows)),
        ],
        [
            pl.BlockSpec((local_experts, 2, 1, CAPACITY, width), lambda i, p: (0, 0, i, 0, 0)),
            pl.BlockSpec((local_experts, 2, 1, CAPACITY, LANES), lambda i, p: (0, 0, i, 0, 0)),
            pl.BlockSpec((2, 1, 8, rows), lambda i, p: (0, i, 0, 0)),
            pl.BlockSpec((2, 1, 8, rows), lambda i, p: (0, i, 0, 0)),
            pl.BlockSpec((2, 1, rows, width), lambda i, p: (0, i, 0, 0)),
            whole((rows, width)),
            whole((padded, rows)),
        ],
        [
            struct(slot_shape + (width,), bf16),
            struct(slot_shape + (LANES,), f32),
            struct((2, half, 8, rows), f32),
            struct((2, half, 8, rows), f32),
            struct((2, half, rows, width), bf16),
            struct((rows, width), f32),
            struct((padded, rows), f32),
        ],
        scratch=[pltpu.VMEM((padded, rows), f32), pltpu.VMEM((padded, rows), f32)],
        us=0.5,
    )(place, att, att, w_mine, w_other, tokens, tokens, routes, routes, gain, w_router, after)


def grad_dispatch_kernel(rank_ref, gate_ref, cot_ref, g_ref):
    local_experts = g_ref.shape[0]
    rows = cot_ref.shape[0] // 2
    for half in range(2):
        hits = hits_of(rank_ref[half], local_experts)
        gate = gate_ref[half]
        slot_gate = jnp.concatenate(
            [jnp.sum(jnp.where(hit, gate[j : j + 1, :], 0.0), axis=1, keepdims=True) for j, hit in enumerate(hits)],
            axis=0,
        )
        grads = (dot(chosen_of(hits), cot_ref[half * rows : (half + 1) * rows, :]) * slot_gate).astype(bf16)
        for j in range(local_experts):
            g_ref[j, half] = grads[j * CAPACITY : (j + 1) * CAPACITY]


def grad_dispatch(rank, gate, cotangents, local_experts):
    members, _, rows = rank.shape
    width = cotangents.shape[1]
    small = pl.BlockSpec((2, 8, rows), lambda j: (j, 0, 0))
    return call(
        grad_dispatch_kernel,
        (members // 2,),
        0,
        [small, small, pl.BlockSpec((2 * rows, width), lambda j: (j, 0))],
        pl.BlockSpec((local_experts, 2, CAPACITY, width), lambda j: (0, j, 0, 0)),
        struct((local_experts, members, CAPACITY, width), bf16),
        us=0.5,
    )(rank, gate, cotangents)


def expert_kernel(
    x_ref, gate_ref, w_gate_ref, w_up_ref, w_down_ref, forth_ref, active_ref, factor_ref, silu_ref
):
    gate_pre = dot(x_ref[0], w_gate_ref[0])
    up_pre = dot(x_ref[0], w_up_ref[0])
    sig = 1.0 / (1.0 + jnp.exp(-gate_pre))
    silu = gate_pre * sig
    silu_ref[0] = silu
    factor_ref[0] = up_pre * sig * (1.0 + gate_pre * (1.0 - sig))
    active_ref[0] = (silu * up_pre).astype(bf16)
    produced = dot_nt(active_ref[0], w_down_ref[0]).astype(bf16).astype(f32)
    forth_ref[0] = (produced * gate_ref[0, :, 0:1]).astype(bf16)


def run_experts(x, slot_gate, w_gate, w_up, w_down):
    count, slots, width = x.shape
    hidden = w_gate.shape[2]

    def per_expert(*shape):
        return pl.BlockSpec((1,) + shape, lambda e: (e, 0, 0))

    return call(
        expert_kernel,
        (count,),
        0,
        [per_expert(slots, width), per_expert(slots, LANES)] + [per_expert(width, hidden)] * 3,
        [per_expert(slots, width)] + [per_expert(slots, hidden)] * 3,
        [
            struct((count, slots, width), bf16),
            struct((count, slots, hidden), bf16),
            struct((count, slots, hidden), f32),
            struct((count, slots, hidden), f32),
        ],
        us=0.5,
    )(x, slot_gate, w_gate, w_up, w_down)


def expert_back_kernel(place_ref, *refs, fast):
    x_ref, g_ref, active_ref, factor_ref, silu_ref = refs[:5]
    w_gate_ref, w_up_ref, w_down_ref, back_ref, dots_ref = refs[5:10]
    grads, (gate_low_ref, up_low_ref) = refs[10:-2], refs[-2:]
    slots, width = g_ref.shape[1], g_ref.shape[2]
    chunk = 256
    active_grad = dot(g_ref[0], w_down_ref[0])
    gate_low_ref[...] = (active_grad * factor_ref[0]).astype(bf16)
    up_low_ref[...] = (active_grad * silu_ref[0]).astype(bf16)
    dots = jnp.sum(active_ref[0].astype(f32) * active_grad, axis=1, keepdims=True)
    dots_ref[0] = jnp.broadcast_to(dots, (slots, LANES))
    back_ref[0] = (dot_nt(gate_low_ref[...], w_gate_ref[0]) + dot_nt(up_low_ref[...], w_up_ref[0])).astype(bf16)

    def products(cols):
        x = x_ref[0, :, cols]
        yield 0, dot_tn(x, gate_low_ref[...]).astype(bf16)
        yield 1, dot_tn(x, up_low_ref[...]).astype(bf16)
        yield 2, dot_tn(g_ref[0, :, cols], active_ref[0]).astype(bf16)

    if fast:
        write_shards(place_ref, grads, products, width)
    else:

        def whole_columns(index, carry):
            cols = pl.ds(pl.multiple_of(index * chunk, chunk), chunk)
            for which, product in products(cols):
                grads[which][0, cols, :] = product
            return carry

        lax.fori_loop(0, width // chunk, whole_columns, 0)


def write_shards(place_ref, outs, products, width):
    send_a, keep_a, send_b, keep_b = outs
    x_bit, y_bit = place_ref[3], place_ref[4]
    shard = width // 4
    for dy in range(2):
        for dx in range(2):
            x, y = x_bit ^ dx, y_bit ^ dy
            cols = pl.ds(pl.multiple_of((y * 2 + x) * shard, shard), shard)
            for which, product in products(cols):
                side = product.shape[1] // 2
                (send_a if dx else keep_a)[0, which, y] = product[:, :side]
                (send_b if dy else keep_b)[0, which, x] = product[:, side:]


def run_experts_back(place, x, g, active, factor, silu, w_gate, w_up, w_down, first, count, fast):
    slots, width = g.shape[1], g.shape[2]
    hidden = w_gate.shape[2]

    def taken(*shape):
        return pl.BlockSpec((1,) + shape, lambda e, p: (e + first, 0, 0))

    def given(*shape):
        zeros = (0,) * len(shape)
        return pl.BlockSpec((1,) + shape, lambda e, p: (e,) + zeros)

    if fast:
        grad_shapes = [(3, 2, width // 4, hidden // 2)] * 4
    else:
        grad_shapes = [(width, hidden)] * 3
    return call(
        lambda *refs: expert_back_kernel(*refs, fast=fast),
        (count,),
        1,
        [taken(slots, width)] * 2 + [taken(slots, hidden)] * 3 + [taken(width, hidden)] * 3,
        [given(slots, width), given(slots, LANES)] + [given(*shape) for shape in grad_shapes],
        [struct((count, slots, width), bf16), struct((count, slots, LANES), f32)]
        + [struct((count,) + shape, bf16) for shape in grad_shapes],
        scratch=[pltpu.VMEM((slots, hidden), bf16)] * 2,
        us=0.5,
    )(place, x, g, active, factor, silu, w_gate, w_up, w_down)


DOT_LANES = 2 * LANES


def combine_kernel(place_ref, rank_ref, *refs, pieces, with_dots, mine):
    parts, rest = refs[:pieces], refs[pieces:]
    rows = rank_ref.shape[2]
    local_experts = sum(part.shape[0] for part in parts)
    hits = hits_of(rank_ref[0], local_experts)
    gathered = jnp.concatenate([part[j, 0] for part in parts for j in range(part.shape[0])], axis=0)
    summed = dot_tn(chosen_of(hits), gathered)
    out_ref = rest[-1]
    if mine:
        arrived_ref = rest[-2]
        summed = summed + arrived_ref[0, 0:rows, :].astype(f32)
    out_ref[0, 0:rows, :] = summed.astype(bf16)
    if with_dots:
        column = [part[j, 0][:, 0:1] for part in rest[:pieces] for j in range(part.shape[0])]
        scattered = [
            jnp.sum(jnp.where(hit, value, 0.0), axis=0, keepdims=True) for hit, value in zip(hits, column)
        ]
        scattered.append(jnp.zeros((DOT_ROWS - local_experts, rows), f32))
        scattered = jnp.concatenate(scattered, axis=0)
        upper = scattered.astype(bf16)
        out_ref[0, rows:, :] = jnp.zeros((DOT_ROWS, out_ref.shape[2]), bf16)
        out_ref[0, rows:, 0:rows] = upper
        out_ref[0, rows:, DOT_LANES : DOT_LANES + rows] = (scattered - upper.astype(f32)).astype(bf16)
        if mine:
            out_ref[0, rows:, 2 * DOT_LANES : 4 * DOT_LANES] = arrived_ref[0, rows:, 0 : 2 * DOT_LANES]


def combine(place, rank, parts, dots=None, arrived=None):
    mine = arrived is not None
    rows, width = rank.shape[2], parts[0].shape[-1]
    out_rows = rows + (DOT_ROWS if dots else 0)

    def member(step, p):
        return (p[0] if mine else 1 - p[0]) * COLS + step

    def slots_of(array):
        return pl.BlockSpec((array.shape[0], 1) + array.shape[2:], lambda j, p: (0, member(j, p), 0, 0))

    inputs = [
        part.reshape(part.shape[0], 2 * COLS, CAPACITY, part.shape[-1]) for part in list(parts) + list(dots or [])
    ]
    in_specs = [pl.BlockSpec((1, 8, rows), lambda j, p: (member(j, p), 0, 0))] + [slots_of(item) for item in inputs]
    by_chip = pl.BlockSpec((1, out_rows, width), lambda j, p: (j, 0, 0))
    if mine:
        inputs.append(arrived)
        in_specs.append(by_chip)
    return call(
        lambda *refs: combine_kernel(*refs, pieces=len(parts), with_dots=bool(dots), mine=mine),
        (COLS,),
        1,
        in_specs,
        by_chip,
        struct((COLS, out_rows, width), bf16),
        us=0.5,
    )(place, rank, *inputs)


def split_dot(dimension_numbers, values, exact):
    upper = values.astype(bf16)
    lower = (values - upper.astype(f32)).astype(bf16)
    return lax.dot_general(
        upper, exact, dimension_numbers, preferred_element_type=f32
    ) + lax.dot_general(lower, exact, dimension_numbers, preferred_element_type=f32)


EXTRA_SLOTS = 6


def middle_back_kernel(
    place_ref, sums_ref, gates_ref, middle_ref, cot_ref, gain_ref, w_router_ref, w_mine_ref, w_other_ref,
    grad_ref, branch_ref, attended_ref, extra_ref
):
    rows = middle_ref.shape[0]
    tail = sums_ref[:, rows : rows + 8, 0 : 4 * DOT_LANES].astype(f32)
    mine = tail[:, :, 0:rows] + tail[:, :, DOT_LANES : DOT_LANES + rows]
    other = tail[:, :, 2 * DOT_LANES : 2 * DOT_LANES + rows] + tail[:, :, 3 * DOT_LANES : 3 * DOT_LANES + rows]
    first_row = place_ref[0] == 0
    dots = jnp.concatenate([jnp.where(first_row, mine, other), jnp.where(first_row, other, mine)], axis=0)
    dots = dots.reshape(dots.shape[0] * 8, rows)
    gates = gates_ref[...]
    logit_grad = dots - gates * jnp.sum(dots, axis=0, keepdims=True)
    middle = middle_ref[...]
    inverse = lax.rsqrt(jnp.mean(middle * middle, axis=1, keepdims=True) + epsilon)
    unit = middle * inverse
    gain = gain_ref[...]
    grad = sums_ref[0, 0:rows].astype(f32)
    for index in range(1, sums_ref.shape[0]):
        grad = grad + sums_ref[index, 0:rows].astype(f32)
    grad = grad + split_dot(TN, logit_grad, w_router_ref[...])
    gain_grad = jnp.sum(grad * unit, axis=0, keepdims=True)
    scaled = grad * gain
    middle_grad = cot_ref[...].astype(f32) + inverse * (
        scaled - unit * jnp.mean(scaled * unit, axis=1, keepdims=True)
    )
    grad_ref[...] = middle_grad
    branch_grad = middle_grad.astype(bf16)
    branch_ref[0:rows, :] = branch_grad
    extra_ref[...] = jnp.zeros_like(extra_ref)
    for index in range(logit_grad.shape[0] // 8):
        first, lane = index // EXTRA_SLOTS * 8, index % EXTRA_SLOTS * DOT_LANES
        extra_ref[first : first + 8, lane : lane + rows] = logit_grad[index * 8 : index * 8 + 8]
    upper = gain_grad.astype(bf16).astype(f32)
    extra_ref[13:14, :] = upper
    extra_ref[14:15, :] = gain_grad - upper
    branch_ref[rows:, :] = extra_ref[...].astype(bf16)
    for which, ref in enumerate((w_mine_ref, w_other_ref)):
        line = place_ref[0] if which == 0 else 1 - place_ref[0]
        for col in range(ref.shape[0]):
            product = dot_nt(branch_grad, ref[col])
            member = line * COLS + col
            attended_ref[member, :, 0:LANES] = product[:, 0:LANES].astype(bf16)
            attended_ref[member, :, LANES : LANES + HEAD_DIM] = product[:, LANES:].astype(bf16)
            attended_ref[member, :, LANES + HEAD_DIM :] = jnp.zeros((product.shape[0], HEAD_DIM), bf16)


def middle_back(place, sums, gates, middle, cotangent, gain, w_router, w_mine, w_other):
    rows, width = middle.shape
    members = 2 * COLS
    args = (sums, gates, middle, cotangent, gain, w_router, w_mine, w_other)
    return call(
        middle_back_kernel,
        (1,),
        1,
        [whole(item.shape) for item in args],
        [whole((rows, width)), whole((rows + DOT_ROWS, width)), whole((members, rows, 2 * LANES))],
        [
            struct((rows, width), f32),
            struct((rows + DOT_ROWS, width), bf16),
            struct((members, rows, 2 * LANES), bf16),
        ],
        scratch=[pltpu.VMEM((DOT_ROWS, width), f32)],
        us=0.5,
    )(place, *args)


def input_grad_kernel(
    place_ref, grads_mine_ref, grads_other_ref, mine_a_ref, mine_b_ref, other_a_ref, other_b_ref,
    tok_ref, middle_grad_ref, gain_ref, out_ref, share_ref, sum_ref
):
    step = pl.program_id(0)
    first = place_ref[4] == 0

    def weights(a_ref, b_ref):
        a = jnp.concatenate([a_ref[index, 0] for index in range(a_ref.shape[0])], axis=0)
        b = jnp.concatenate([b_ref[index, 0] for index in range(b_ref.shape[0])], axis=0)
        upper, lower = jnp.where(first, a, b), jnp.where(first, b, a)
        return jnp.concatenate([upper, lower, lower[lower.shape[0] - HEAD_DIM :]], axis=0)

    rows = tok_ref.shape[0]
    part = dot(grads_mine_ref[0, 0:rows, :], weights(mine_a_ref, mine_b_ref))
    part = part + dot(grads_other_ref[0, 0:rows, :], weights(other_a_ref, other_b_ref))
    share = grads_mine_ref[0, rows:, :].astype(f32)[0:8] + grads_other_ref[0, rows:, :].astype(f32)[0:8]

    @pl.when(step == 0)
    def _():
        sum_ref[...] = part
        share_ref[...] = share

    @pl.when(step > 0)
    def _():
        sum_ref[...] += part
        share_ref[...] += share

    @pl.when(step == pl.num_programs(0) - 1)
    def _():
        resid = tok_ref[...].astype(f32)
        inverse = lax.rsqrt(jnp.mean(resid * resid, axis=1, keepdims=True) + epsilon)
        unit = resid * inverse
        scaled = sum_ref[...] * gain_ref[...]
        out_ref[...] = middle_grad_ref[...] + inverse * (
            scaled - unit * jnp.mean(scaled * unit, axis=1, keepdims=True)
        )


def input_grad(place, grads, weights, tokens, middle_grad, gain):
    rows, width = tokens.shape
    lanes = grads.shape[2]
    w_shape = (weights[0].shape[0], 1) + weights[0].shape[2:]
    return call(
        input_grad_kernel,
        (COLS,),
        1,
        [
            pl.BlockSpec((1, rows + DOT_ROWS, lanes), lambda c, p: (p[0] * COLS + c, 0, 0)),
            pl.BlockSpec((1, rows + DOT_ROWS, lanes), lambda c, p: ((1 - p[0]) * COLS + c, 0, 0)),
        ]
        + [pl.BlockSpec(w_shape, lambda c, p: (0, c, 0, 0))] * 4
        + [whole((rows, width)), whole((rows, width)), whole((1, width))],
        [whole((rows, width)), whole((8, lanes))],
        [struct((rows, width), f32), struct((8, lanes), f32)],
        scratch=[pltpu.VMEM((rows, width), f32)],
        us=0.5,
    )(place, grads, grads, *weights, tokens, middle_grad, gain)


def out_weights_kernel(place_ref, branch_ref, att_ref, normed_ref, own_ref, *refs, fast, local_experts):
    outs, small_ref, (sum_ref, gain_sum_ref) = refs[:-3], refs[-3], refs[-2:]
    step = pl.program_id(0)
    rows = att_ref.shape[0] // 2
    block = rows + DOT_ROWS

    @pl.when(step == 0)
    def _():
        sum_ref[...] = jnp.zeros_like(sum_ref)
        small_ref[...] = jnp.zeros_like(small_ref)
        gain_sum_ref[...] = jnp.zeros_like(gain_sum_ref)

    branch = jnp.concatenate([branch_ref[0:rows, :], branch_ref[block : block + rows, :]], axis=0)
    sum_ref[...] += dot_tn(branch, att_ref[...])
    for which in range(2):
        tail = branch_ref[which * block + rows : (which + 1) * block, :].astype(f32)
        slots = []
        for index in range(small_ref.shape[0] // 8):
            first, lane = index // EXTRA_SLOTS * 8, index % EXTRA_SLOTS * DOT_LANES
            slots.append(tail[first : first + 8, lane : lane + rows])
        logit_grad = jnp.concatenate(slots, axis=0)
        real = lax.broadcasted_iota(jnp.int32, logit_grad.shape, 0) % 8 < local_experts
        logit_grad = jnp.where(real, logit_grad, 0.0).astype(bf16)
        small_ref[...] += dot(logit_grad, normed_ref[which * rows : (which + 1) * rows, :])
        gain_sum_ref[...] += tail[8:16, :]

    @pl.when(step == pl.num_programs(0) - 1)
    def _():
        small_ref[7:8, :] = gain_sum_ref[5:6, :] + gain_sum_ref[6:7, :]

        def products(cols):
            own = own_ref[cols, 0 : 2 * LANES]
            out_one = sum_ref[cols, 0:LANES].astype(bf16)
            out_two = sum_ref[cols, LANES:]
            low = lane_of(out_two.shape) < HEAD_DIM
            tail = jnp.where(low, out_two, own_ref[cols, 2 * LANES :].astype(f32)).astype(bf16)
            yield 0, jnp.concatenate([own, out_one, tail], axis=1)

        if fast:
            write_shards(place_ref, outs, products, own_ref.shape[0])
        else:
            outs[0][...] = next(products(slice(0, own_ref.shape[0])))[1]


def out_weights(place, branch, attended, normed, own, padded, local_experts, fast):
    total, width = normed.shape
    rows = total // COLS
    blocks = branch.shape[0] // COLS
    if fast:
        shapes = [(1, 1, 2, width // 4, 2 * LANES)] * 4
    else:
        shapes = [(width, 4 * LANES)]
    return call(
        lambda *refs: out_weights_kernel(*refs, fast=fast, local_experts=local_experts),
        (COLS,),
        1,
        [
            pl.BlockSpec((blocks, width), lambda j, p: (j, 0)),
            pl.BlockSpec((rows, 2 * LANES), lambda j, p: (j, 0)),
            pl.BlockSpec((rows, width), lambda j, p: (j, 0)),
            whole(own.shape),
        ],
        [whole(shape) for shape in shapes] + [whole((padded, width))],
        [struct(shape, bf16) for shape in shapes] + [struct((padded, width), f32)],
        scratch=[pltpu.VMEM((width, 2 * LANES), f32), pltpu.VMEM((8, width), f32)],
        us=0.5,
    )(place, branch, attended, normed, own)


def first_sum_kernel(place_ref, keep_a_ref, got_a_ref, keep_b_ref, got_b_ref, *rest):
    send_a_ref, held_a_ref, send_b_ref, held_b_ref = rest[-4:]
    x_bit, y_bit = place_ref[3], place_ref[4]
    for bit, keep, got, send, held in (
        (y_bit, keep_a_ref, got_a_ref, send_a_ref, held_a_ref),
        (x_bit, keep_b_ref, got_b_ref, send_b_ref, held_b_ref),
    ):
        for kind in range(keep.shape[1]):
            held[0, kind] = (keep[0, kind, bit].astype(f32) + got[0, kind, bit].astype(f32)).astype(bf16)
            send[0, kind] = (keep[0, kind, 1 - bit].astype(f32) + got[0, kind, 1 - bit].astype(f32)).astype(bf16)


def first_sum(place, chunk, first=0, total=None, before=None):
    count, kinds, _, rows, cols = chunk[0].shape
    taken = pl.BlockSpec((1, kinds, 2, rows, cols), lambda e, p: (e, 0, 0, 0, 0))
    given = pl.BlockSpec((1, kinds, rows, cols), lambda e, p: (e + first, 0, 0, 0))
    extra = list(before) if before else []
    return call(
        first_sum_kernel,
        (count,),
        1,
        [taken] * 4 + [pl.BlockSpec(memory_space=pl.ANY)] * len(extra),
        [given] * 4,
        [struct((total or count, kinds, rows, cols), bf16)] * 4,
        us=0.5,
        aliases={5 + i: i for i in range(len(extra))},
    )(place, *chunk, *extra)


def last_sum_kernel(held_a_ref, got_a_ref, held_b_ref, got_b_ref, *rest):
    outs = rest[-3:]
    side = held_a_ref.shape[3]
    for which, out in enumerate(outs):
        out[0, :, :side] = held_a_ref[0, which].astype(f32) + got_a_ref[0, which].astype(f32)
        out[0, :, side:] = held_b_ref[0, which].astype(f32) + got_b_ref[0, which].astype(f32)


def last_sum(held_a, got_a, held_b, got_b, first, total, before):
    count, kinds, rows, cols = held_a.shape
    taken = pl.BlockSpec((1, kinds, rows, cols), lambda e: (e, 0, 0, 0))
    given = pl.BlockSpec((1, rows, 2 * cols), lambda e: (e + first, 0, 0))
    extra = list(before) if before else []
    return call(
        last_sum_kernel,
        (count,),
        0,
        [taken] * 4 + [pl.BlockSpec(memory_space=pl.ANY)] * len(extra),
        [given] * 3,
        [struct((total, rows, 2 * cols), f32)] * 3,
        us=0.5,
        aliases={4 + i: i for i in range(len(extra))},
    )(held_a, got_a, held_b, got_b, *extra)


def last_weights_kernel(held_a_ref, got_a_ref, held_b_ref, got_b_ref, query_ref, key_ref, value_ref, out_ref):
    left = jnp.transpose(held_a_ref[0, 0].astype(f32) + got_a_ref[0, 0].astype(f32))
    right = jnp.transpose(held_b_ref[0, 0].astype(f32) + got_b_ref[0, 0].astype(f32))
    cut = query_ref.shape[0]
    query_ref[...] = left[:cut]
    key_ref[...] = left[cut:]
    out_ref[...] = right[:cut]
    value_ref[...] = right[cut:]


def last_weights(parts, widths):
    rows = parts[0].shape[2]
    shapes = [(width, rows) for width in widths]
    return call(
        last_weights_kernel,
        (1,),
        0,
        [whole(part.shape) for part in parts],
        [whole(shape) for shape in shapes],
        [struct(shape, f32) for shape in shapes],
        us=0.5,
    )(*parts)


SWAP = [(0, 1), (1, 0)]


def after(value, *events):
    return lax.optimization_barrier((value,) + events)[0]


def gather_group(block):
    return lax.all_gather(block, ("row", "col"), axis=0, tiled=True)


def line_pieces(value):
    parts = [value]
    for distance in range(1, COLS):
        parts.insert(0, lax.ppermute(value, "col", [(i, (i + distance) % COLS) for i in range(COLS)]))
    return parts


def in_line_order(parts):
    parts = jnp.stack(parts + parts)
    return lax.dynamic_slice_in_dim(parts, COLS - 1 - lax.axis_index("col"), COLS, axis=0)


def flip(value, axis, bit, size):
    return lax.ppermute(value, axis, [(i, i ^ (1 << bit)) for i in range(size)])


def bits_of(size):
    return size.bit_length() - 1


def own_bit(axis, bit):
    return (lax.axis_index(axis) >> bit) & 1


def joined(mine, got, own):
    return jnp.where(own == 0, jnp.concatenate([mine, got]), jnp.concatenate([got, mine]))


def cube_step(value, axis, bit, size):
    return joined(value, flip(value, axis, bit, size), own_bit(axis, bit))


def lines_first(value):
    return jnp.transpose(value, (1, 0, 2, 3)).reshape(value.shape[1], value.shape[0] * value.shape[2], value.shape[3])


def cube_gather(value, axis, size):
    value = value[None]
    for bit in range(bits_of(size)):
        value = cube_step(value, axis, bit, size)
    return value


def sum_dp(value, sizes):
    for bit in range(bits_of(sizes["dp"])):
        value = value + flip(value, "dp", bit, sizes["dp"])
    return value


def reduce_over_dp(value, size):
    count = bits_of(size)
    value = value.reshape(value.shape[:1] + (2,) * count + value.shape[2:])
    current = value
    for bit in range(count - 1, -1, -1):
        own = own_bit("dp", bit)
        keep = lax.dynamic_index_in_dim(current, own, 1, keepdims=False)
        send = lax.dynamic_index_in_dim(current, 1 - own, 1, keepdims=False).astype(bf16)
        current = keep.astype(f32) + flip(send, "dp", bit, size).astype(f32)
    return current


def start_move(run, size):
    return flip(run[0], "dp", 0, size), flip(run[2], "dp", 1, size)


def second_move(sums, size):
    send_a, held_a, send_b, held_b = sums
    return held_a, flip(send_a, "dp", 1, size), held_b, flip(send_b, "dp", 0, size)


def layer(sizes):
    n_dp, n_row, n_col = sizes["dp"], sizes["row"], sizes["col"]
    members = n_row * n_col
    fast = n_dp == 4
    assert n_row == 2 and n_col == COLS and n_dp & (n_dp - 1) == 0

    def local(
        tokens, cotangent, routes, lengths, gain_attn, w_query, w_key, w_value, w_out,
        gain_moe, w_router, w_gate, w_up, w_down,
    ):
        rows, width = tokens.shape
        group = rows * members
        local_experts = w_gate.shape[0]
        row, col, dp = lax.axis_index("row"), lax.axis_index("col"), lax.axis_index("dp")
        place = jnp.stack([row, col, row * n_col + col, dp & 1, (dp >> 1) & 1]).astype(jnp.int32)
        gain_one = gain_attn.astype(f32)[None]
        gain_two = gain_moe.astype(f32)[None]

        tok_all = gather_group(tokens)
        w_in = jnp.concatenate([w_query.T, w_key.T, w_value.T], axis=0)
        out_share, in_share = rows // n_dp, w_in.shape[0] // n_dp
        shares = jnp.concatenate(
            [
                lax.dynamic_slice(w_out.T, (dp * out_share, 0), (out_share, width)),
                lax.dynamic_slice(w_in, (dp * in_share, 0), (in_share, width)),
                jnp.pad(routes.T.astype(bf16).reshape(1, TOP * rows), ((0, 7), (0, width - TOP * rows))),
            ],
            axis=0,
        )
        w_stack = jnp.concatenate([w_query.T, w_key.T, w_value.T, w_value.T], axis=0)
        w_natural = jnp.concatenate([w_query, w_key, w_value, w_value], axis=1)

        ends = jnp.cumsum(lengths[0])
        starts = ends - lengths[0]
        position = jnp.arange(group, dtype=jnp.int32)
        segment = jnp.sum((position[:, None] >= ends[None, :]).astype(jnp.int32), axis=1)
        member = segment[:, None] == jnp.arange(starts.shape[0], dtype=jnp.int32)[None, :]
        start = jnp.sum(jnp.where(member, starts[None, :], 0), axis=1).astype(jnp.int32)
        frequency = rope_base ** (-2.0 * jnp.arange(HEAD_DIM // 2, dtype=f32) / HEAD_DIM)
        angle = (position - start).astype(f32)[:, None] * frequency[None, :]
        cosine = jnp.tile(jnp.cos(angle), (1, 4))
        sine = jnp.tile(jnp.sin(angle), (1, 4))

        w_router_rows = w_router.T.reshape(members, local_experts, width)
        w_router_rows = jnp.pad(w_router_rows, ((0, 0), (0, 8 - local_experts), (0, 0)))
        w_router_rows = w_router_rows.reshape(members * 8, width)
        start_row = jnp.broadcast_to(start[None, :], (8, group))
        start = start[:, None]
        gain_column = gain_attn.astype(f32)[:, None]
        ready = (place, gain_one, gain_two, w_stack, w_natural, cosine, sine, w_router_rows, start, start_row, gain_column)
        shares, place, gain_one, gain_two, w_stack, w_natural, cosine, sine, w_router_rows, start, start_row, gain_column = (
            lax.optimization_barrier((shares,) + ready)
        )
        shares = line_pieces(after(shares, tok_all, cosine))

        query, key, value, normed_one = project(tok_all, gain_one, w_stack, cosine, sine)
        packed, attended, totals = attend(query, key, value, start)
        att_flat = gather_group(packed)
        att_all = att_flat.reshape((n_row, n_col) + packed.shape)
        shares = in_line_order(after(shares, packed))
        route_rows = shares[:, out_share + in_share]
        w_out_mine, in_part = shares[None, :, :out_share], shares[None, :, out_share : out_share + in_share]
        for bit in range(bits_of(n_dp)):
            w_out_mine = cube_step(w_out_mine, "dp", bit, n_dp)
        in_part = cube_step(in_part, "dp", 0, n_dp)
        w_out_mine = lines_first(w_out_mine)
        route_rows = cube_gather(route_rows, "row", n_row)[:, :, : TOP * rows].reshape(members, TOP, rows)
        w_out_other = lax.ppermute(after(w_out_mine, in_part, route_rows), "row", SWAP)
        cot_all = gather_group(after(cotangent, w_out_other))
        x, slot_gate, rank, gate, normed_two, middle, gates = middle_and_dispatch(
            place, att_all, w_out_mine, w_out_other, tok_all, route_rows, gain_two, w_router_rows, local_experts
        )
        slots = members * CAPACITY
        x = x.reshape(local_experts, slots, width)
        slot_gate = slot_gate.reshape(local_experts, slots, LANES)
        rank, gate = rank.reshape(members, 8, rows), gate.reshape(members, 8, rows)
        forth, active, factor, silu = run_experts(x, slot_gate, w_gate, w_up, w_down)
        for bit in range(1, bits_of(n_dp) - 1):
            in_part = cube_step(in_part, "dp", bit, n_dp)
        last_bit = bits_of(n_dp) - 1
        in_got = after(flip(in_part, "dp", last_bit, n_dp), forth)
        forth_other = combine(place, after(rank, in_got), [forth])
        arrived = lax.ppermute(forth_other, "row", SWAP)
        g = grad_dispatch(after(rank, forth_other), gate, cot_all, local_experts)
        g = g.reshape(local_experts, slots, width)
        cuts = [0, 1, 3, local_experts]

        def backward(which, x):
            first, last = cuts[which], cuts[which + 1]
            return run_experts_back(place, x, g, active, factor, silu, w_gate, w_up, w_down, first, last - first, fast)

        runs = [backward(0, x)]
        forth_mine = combine(place, rank, [forth], arrived=after(arrived, runs[0][1]))
        forth_sums = lax.all_to_all(forth_mine, "col", 0, 0, tiled=True)
        runs.append(backward(1, after(x, forth_mine)))
        runs.append(backward(2, after(x, runs[1][1])))
        moved = [start_move(run[2:], n_dp) for run in runs] if fast else []
        back_parts, dot_parts = [run[0] for run in runs], [run[1] for run in runs]
        back_other = combine(place, after(rank, *moved[0]) if fast else rank, back_parts, dot_parts)
        arrived = lax.ppermute(back_other, "row", SWAP)
        back_mine = combine(place, rank, back_parts, dot_parts, arrived)
        back_mine = after(back_mine, forth_sums)
        back_sums = lax.all_to_all(back_mine, "col", 0, 0, tiled=True)

        if fast:
            w_in_parts = [in_part, in_got]
        else:
            own = own_bit("dp", last_bit)
            w_in_rows = lines_first(joined(in_part, in_got, own))[None]
            half = w_in_rows.shape[2] // 2
            upper, lower = w_in_rows[:, :, :half], w_in_rows[:, :, half:]
            w_in_parts = [jnp.where(place[4] == 0, upper, lower), jnp.where(place[4] == 0, lower, upper)]
        if fast:

            def chunk_of(which, *events):
                keep_a, keep_b = after((runs[which][3], runs[which][5]), *events)
                return keep_a, moved[which][0], keep_b, moved[which][1]

            sums = first_sum(place, chunk_of(0, back_mine), cuts[0], cuts[2])
            gate_middle = (sums[1],) + moved[1]
        else:
            gate_middle = ()
        w_in_parts += [lax.ppermute(after(part, back_mine), "row", SWAP) for part in w_in_parts]

        middle_grad, branch_grad, attended_grad = middle_back(
            place, back_sums, gates, middle, cotangent, after(gain_two, *w_in_parts[2:], *gate_middle),
            w_router_rows, w_out_mine, w_out_other,
        )
        if fast:
            sums = first_sum(place, chunk_of(1, branch_grad), cuts[1], cuts[2], sums)
            started = [second_move(sums, n_dp)]
        attended_grad = lax.all_to_all(attended_grad, ("row", "col"), 0, 0, tiled=True)
        if fast:
            attended_grad = after(attended_grad, sums[1])
        branch_all = gather_group(branch_grad)

        attended_grad = attended_grad.reshape(group, 2 * LANES)
        projected_grad, own_grads = attend_back(
            query, key, value, attended_grad, totals, start_row, cosine, sine, normed_one, w_natural, gain_column
        )
        projected_all = lax.all_to_all(projected_grad, ("row", "col"), 0, 0, tiled=True)
        *w_parts, small = out_weights(
            place, branch_all, attended, normed_two.reshape(group, width), own_grads,
            members * 8, local_experts, fast,
        )
        arriving = ()
        if fast:
            w_moved = start_move(w_parts, n_dp)
            late = first_sum(place, chunk_of(2, small, started[0][1], started[0][3]))
            started.append(second_move(late, n_dp))
            w_first = first_sum(place, (w_parts[1], w_moved[0], w_parts[3], w_moved[1]))
            w_sums = second_move(w_first, n_dp)
            arriving = (w_first[1], started[1][0])
        else:
            cut = w_parts[0].reshape(1, n_dp, width // n_dp, w_parts[0].shape[1])
            w_sum = reduce_over_dp(cut, n_dp)[0]


        mixed = (middle + jnp.sum(after(forth_sums, small).astype(f32), axis=0)).astype(bf16)
        used = small.reshape(members, 8, width)[:, :local_experts].reshape(members * local_experts, width)
        both = sum_dp(jnp.concatenate([used, small[7:8]], axis=0), sizes)
        w_router_grad = both[: members * local_experts].T
        gain_moe_grad = both[members * local_experts]

        tokens_grad, share = input_grad(
            place, projected_all, w_in_parts, tokens, middle_grad, after(gain_one, w_parts[0], *arriving)
        )
        share = (share[0:4] + share[4:8]).reshape(8, width // 8)
        if fast:
            held_a, got_a, held_b, got_b = started[0]
            held_a, held_b = after((held_a, held_b), tokens_grad)
            expert_grads = last_sum(held_a, got_a, held_b, got_b, 0, local_experts, None)
            share = share + after(flip(share, "dp", 0, n_dp), expert_grads[0])
            held_a, got_a, held_b, got_b = started[1]
            held_a, held_b = after((held_a, held_b), share, w_sums[1], w_sums[3])
            expert_grads = last_sum(held_a, got_a, held_b, got_b, cuts[2], local_experts, expert_grads)
            gain_attn_grad = share + after(flip(share, "dp", 1, n_dp), expert_grads[0])
            gain_attn_grad = gain_attn_grad.reshape(width)
        else:
            gain_attn_grad = sum_dp(share, sizes).reshape(width)

        local_q, local_k = w_query.shape[1], w_key.shape[1]
        if fast:
            w_query_grad, w_key_grad, w_value_grad, w_out_grad = [
                item.T for item in last_weights(w_sums, (local_q, local_k, local_k, local_q))
            ]
        else:
            expert_grads = []
            for which in range(3):
                parts = [run[2 + which] for run in runs]
                parts = [part.reshape(part.shape[0], n_dp, width // n_dp, part.shape[2]) for part in parts]
                expert_grads.append(jnp.concatenate([reduce_over_dp(part, n_dp) for part in parts], axis=0))
            cut = local_q + local_k
            w_query_grad, w_key_grad = w_sum[:, :local_q], w_sum[:, local_q:cut]
            w_out_grad, w_value_grad = w_sum[:, cut : cut + local_q], w_sum[:, cut + local_q :]
        w_gate_grad, w_up_grad, w_down_grad = expert_grads
        return (
            mixed, tokens_grad, gain_attn_grad, w_query_grad, w_key_grad, w_value_grad, w_out_grad,
            gain_moe_grad, w_router_grad, w_gate_grad, w_up_grad, w_down_grad,
        )

    return local


def solution(mesh):
    return jax.shard_map(
        layer(dict(mesh.shape)),
        mesh=mesh,
        in_specs=(
            P(("dp", "row", "col"), None),
            P(("dp", "row", "col"), None),
            P(("dp", "row", "col"), None),
            P("dp", None),
            P(),
            P(None, ("row", "col")),
            P(None, ("row", "col")),
            P(None, ("row", "col")),
            P(None, ("row", "col")),
            P(),
            P(),
            P(("row", "col"), None, None),
            P(("row", "col"), None, None),
            P(("row", "col"), None, None),
        ),
        out_specs=(
            P(("dp", "row", "col"), None),
            P(("dp", "row", "col"), None),
            P(),
            P("dp", ("row", "col")),
            P("dp", ("row", "col")),
            P("dp", ("row", "col")),
            P("dp", ("row", "col")),
            P(),
            P(),
            P(("row", "col"), "dp", None),
            P(("row", "col"), "dp", None),
            P(("row", "col"), "dp", None),
        ),
        check_vma=False,
    )
```
